32 devices in a mesh: ctx: 4 (over y, core), fsdp: 8 (over z, x).
Axes of the slice: x: 2, y: 2, z: 4, core: 2. Of those that a mesh axis runs over, the one named last changes fastest.
Arguments:
- hidden: bfloat16 [8, 1024, 2048], P('fsdp', 'ctx'), may hold values from -6 to 6
- cotangent: bfloat16 [8, 1024, 2048], P('fsdp', 'ctx'), may hold values from -6 to 6
- seq_lens: int32 [8], P('fsdp'), may hold values from 512 to 1024, as said below
- norm_gain: bfloat16 [2048], P('fsdp'), may hold values from 0.5 to 1.5
- in_weight: bfloat16 [2048, 8512], P('fsdp'), may hold values from -0.125 to 0.125
- conv_weight: bfloat16 [4, 4352], P(None, 'fsdp'), may hold values from -3 to 3
- conv_bias: bfloat16 [4352], P('fsdp'), may hold values from -3 to 3
- dt_bias: bfloat16 [64], P('fsdp'), may hold values from -6 to -4
- a_log: bfloat16 [64], P('fsdp'), may hold values from -3 to 1.59375
- d_skip: bfloat16 [64], P('fsdp'), may hold values from 0.5 to 4
- gate_gain: bfloat16 [4096], P('fsdp'), may hold values from 0.5 to 1.5
- out_weight: bfloat16 [4096, 2048], P('fsdp'), may hold values from -0.09375 to 0.09375
Outputs:
- layer_out: bfloat16 [8, 1024, 2048], P('fsdp', 'ctx')
- hidden_grad: bfloat16 [8, 1024, 2048], P('fsdp', 'ctx')
- norm_gain_grad: float32 [2048], P('fsdp')
- in_weight_grad: float32 [2048, 8512], P('fsdp')
- conv_weight_grad: float32 [4, 4352], P(None, 'fsdp')
- conv_bias_grad: float32 [4352], P('fsdp')
- dt_bias_grad: float32 [64], P('fsdp')
- a_log_grad: float32 [64], P('fsdp')
- d_skip_grad: float32 [64], P('fsdp')
- gate_gain_grad: float32 [4096], P('fsdp')
- out_weight_grad: float32 [4096, 2048], P('fsdp')
The draws below stay inside these ranges and needn't reach their ends.
Inputs may be any that keep to these rules, and one draw needn't show every extreme that they name: A sequence's first seq_lens tokens are valid, the rest padding; some sequence is full and some holds exactly 512 valid tokens.
All inputs are finite; a program needn't handle non-finite values.
Results may differ from the reference program's by a relative error of at most 0.015.
Values may be sent and summed in bfloat16 or wider, within the bound.
A program may use at most 224 MiB of HBM per device.

```python
import jax
import jax.numpy as jnp
from jax import lax

D = 2048
H = 64
P_SIZE = 64
N = 128
K = 4
BLOCK = 256
DI = 4096
CONVW = 4352
PROJ = 8512
SEQ = 1024
SEQS = 8


def draw_seq_lens(key, part):
    lengths = jax.random.randint(key, (SEQS,), SEQ // 2, SEQ + 1).astype(jnp.int32)
    lengths = lengths.at[0].set(SEQ)
    lengths = lengths.at[1].set(SEQ // 2)
    return lengths


def block_levels(stream_key, shape, shards, smallest, largest):
    factor_of = 1.0
    for dim, parts in shards:
        heights = jax.random.uniform(jax.random.fold_in(jax.random.fold_in(stream_key, 6), dim), (parts,), jnp.float32, smallest / len(shards), largest / len(shards))
        factor_of = factor_of * jnp.repeat(jnp.exp(heights), shape[dim] // parts).reshape((-1,) + (1,) * (len(shape) - 1 - dim))
    return factor_of


def normal_values(own_key, shape, deviation, most, cuts=(), kind=jnp.bfloat16):
    entries = jax.random.normal(own_key, shape, jnp.float32) * deviation
    if len(cuts) > 0:
        entries = block_levels(own_key, shape, cuts, -0.22, 0.18) * entries
    return jnp.clip(entries, min=-most, max=most).astype(kind)


def setup_inputs(seed: int = 0) -> dict:
    keys = jax.random.split(jax.random.key(seed), 13)
    return {
        "hidden": normal_values(keys[0], (SEQS, SEQ, D), 1.0, 6.0, ((0, 8), (1, 4))),
        "cotangent": normal_values(keys[1], (SEQS, SEQ, D), 1.0, 6.0, ((0, 8), (1, 4))),
        "seq_lens": draw_seq_lens(jax.random.fold_in(keys[12], 71), 0),
        "norm_gain": jnp.clip(0.5 + 1.0 * jax.random.uniform(keys[3], (D,), jnp.float32) ** block_levels(keys[3], (D,), ((0, 8),), -0.2, 0.2), 0.5, 1.5).astype(jnp.bfloat16),
        "in_weight": normal_values(keys[4], (D, PROJ), D ** -0.5, 0.125, ((0, 8),)),
        "conv_weight": normal_values(keys[5], (K, CONVW), K ** -0.5, 3.0, ((1, 8),)),
        "conv_bias": normal_values(keys[6], (CONVW,), 0.5, 3.0, ((0, 8),)),
        "dt_bias": jnp.clip(-6.0 + 2.0 * jax.random.uniform(keys[7], (H,), jnp.float32) ** block_levels(keys[7], (H,), ((0, 8),), -0.2, 0.2), -6.0, -4.0).astype(jnp.bfloat16),
        "a_log": jnp.clip(-3.0 + 4.59375 * jax.random.uniform(keys[8], (H,), jnp.float32) ** block_levels(keys[8], (H,), ((0, 8),), -0.2, 0.2), -3.0, 1.59375).astype(jnp.bfloat16),
        "d_skip": jnp.clip(0.5 + 3.5 * jax.random.uniform(keys[9], (H,), jnp.float32) ** block_levels(keys[9], (H,), ((0, 8),), -0.2, 0.2), 0.5, 4.0).astype(jnp.bfloat16),
        "gate_gain": jnp.clip(0.5 + 1.0 * jax.random.uniform(keys[10], (DI,), jnp.float32) ** block_levels(keys[10], (DI,), ((0, 8),), -0.2, 0.2), 0.5, 1.5).astype(jnp.bfloat16),
        "out_weight": normal_values(keys[11], (DI, D), DI ** -0.5, 0.09375, ((0, 8),)),
    }


epsilon_norm = 1e-05

@jax.custom_vjp
def low(v):
    return lax.optimization_barrier(v.astype(jnp.bfloat16)).astype(jnp.float32)

@jax.custom_vjp
def low_back(v):
    return v

def low_keep(v):
    return (low(v), None)

def low_pass(kept, grad):
    return (grad,)

def back_keep(v):
    return (v, None)

def back_low(kept, grad):
    return (low(grad),)
low.defvjp(low_keep, low_pass)
low_back.defvjp(back_keep, back_low)

def block_step(carried, pieces):
    values, b_rows, c_rows, decay_rate, step_size = pieces
    level = jnp.cumsum(decay_rate, axis=0)
    gram = jnp.dot(c_rows, b_rows.T, precision=lax.Precision.HIGHEST)
    across = level.T
    spread = jnp.exp(-jnp.abs(across[:, :, None] - across[:, None, :]))
    mixing = gram[None, :, :] * spread * step_size.T[:, None, :]
    inner = jnp.einsum('hts,shp->thp', mixing, values, precision=lax.Precision.HIGHEST)
    entering = jnp.exp(-level)[:, :, None] * jnp.einsum('tn,hpn->thp', c_rows, carried, precision=lax.Precision.HIGHEST)
    final = level[-1]
    weights = jnp.exp(level - final[None, :]) * step_size
    update = jnp.einsum('sh,shp,sn->hpn', weights, values, b_rows, precision=lax.Precision.HIGHEST)
    return (carried * jnp.exp(-final)[:, None, None] + update, inner + entering)

def mixer_forward(resid, valid, norm_gain, in_weight, conv_weight, conv_bias, dt_bias, a_log, d_skip, gate_gain, out_weight):
    normed = resid * lax.rsqrt(lax.optimization_barrier(jnp.mean(resid * resid, axis=-1, keepdims=True)) + epsilon_norm) * norm_gain
    normed = low(normed)
    projected = low_back(low(jnp.dot(normed, in_weight, precision=lax.Precision.HIGHEST)))
    gate_raw = projected[:, :DI]
    conv_in = projected[:, DI:DI + CONVW]
    step_raw = projected[:, DI + CONVW:]
    padded = jnp.concatenate([jnp.zeros((K - 1, CONVW), jnp.float32), conv_in], axis=0)
    convolved = conv_bias
    for offset in range(K):
        convolved = convolved + conv_weight[offset] * padded[offset:offset + SEQ]
    activated = low(jax.nn.silu(convolved))
    values = activated[:, :DI].reshape(SEQ, H, P_SIZE)
    b_rows = activated[:, DI:DI + N]
    c_rows = activated[:, DI + N:]
    step_size = jax.nn.softplus(step_raw + dt_bias) * valid[:, None]
    decay_rate = step_size * jnp.exp(a_log)
    count = SEQ // BLOCK
    blocks = (values.reshape(count, BLOCK, H, P_SIZE), b_rows.reshape(count, BLOCK, N), c_rows.reshape(count, BLOCK, N), decay_rate.reshape(count, BLOCK, H), step_size.reshape(count, BLOCK, H))
    _, outputs = lax.scan(jax.checkpoint(block_step), jnp.zeros((H, P_SIZE, N), jnp.float32), blocks)
    mixed_ssd = outputs.reshape(SEQ, H, P_SIZE) + d_skip[:, None] * values
    mixed_ssd = mixed_ssd.reshape(SEQ, DI)
    gated = mixed_ssd * jax.nn.silu(gate_raw)
    normed_gate = gated * lax.rsqrt(lax.optimization_barrier(jnp.mean(gated * gated, axis=-1, keepdims=True)) + epsilon_norm) * gate_gain
    normed_gate = low(normed_gate)
    mixed = low_back(jnp.dot(normed_gate, out_weight, precision=lax.Precision.HIGHEST))
    return resid + valid[:, None] * mixed

def reference(hidden, cotangent, seq_lens, norm_gain, in_weight, conv_weight, conv_bias, dt_bias, a_log, d_skip, gate_gain, out_weight):
    params = tuple((item.astype(jnp.float32) for item in (norm_gain, in_weight, conv_weight, conv_bias, dt_bias, a_log, d_skip, gate_gain, out_weight)))
    places = jnp.arange(SEQ, dtype=jnp.int32)

    def one_sequence(totals, item):
        resid, upstream, length = item
        valid = (places < length).astype(jnp.float32)

        def forward(resid_in, *weights):
            return mixer_forward(resid_in, valid, *weights)
        result, pullback = jax.vjp(forward, resid.astype(jnp.float32), *params)
        grads = pullback(upstream.astype(jnp.float32))
        totals = tuple((total + grad for total, grad in zip(totals, grads[1:])))
        return (totals, (result.astype(jnp.bfloat16), grads[0].astype(jnp.bfloat16)))
    zeros = tuple((jnp.zeros_like(item) for item in params))
    totals, (results, input_grads) = lax.scan(one_sequence, zeros, (hidden, cotangent, seq_lens))
    return (results, input_grads, totals[0], totals[1], totals[2], totals[3], totals[4], totals[5], totals[6], totals[7], totals[8])
```

```python
import functools

import jax
import jax.numpy as jnp
from jax import lax
from jax.experimental import pallas as pl
from jax.experimental.pallas import tpu as pltpu
from jax.sharding import PartitionSpec as P

HEAD = 64
STATE = 128
BLOCK = 256
LANES = 128
EPS = 1e-05
F32 = jnp.float32
BF16 = jnp.bfloat16


def mm(a, b, contract=((1,), (0,))):
    return lax.dot_general(a, b, (contract, ((), ())), preferred_element_type=F32)


def mm_exact(a, b, contract=((1,), (0,))):
    return lax.dot_general(
        a, b, (contract, ((), ())), precision=lax.Precision.HIGHEST, preferred_element_type=F32
    )


def iota2(shape, axis):
    return lax.broadcasted_iota(jnp.int32, shape, axis)


def levels(lam, step):
    tri = (iota2((BLOCK, BLOCK), 0) >= iota2((BLOCK, BLOCK), 1)).astype(F32)
    level = mm_exact(tri, lam)
    across = level.T
    last = level[BLOCK - 1 : BLOCK, :]
    weight = jnp.exp(level - last) * step
    return level, across, jnp.exp(-last), weight, jnp.exp(-level)


def pair_of(array, first, low_half):
    return jnp.where(low_half, array[:, first : first + 1], array[:, first + 1 : first + 2])


def spread(level, across, head):
    return jnp.exp(-jnp.abs(level[:, head : head + 1] - across[head : head + 1, :]))


def forward_kernel(heads, x_ref, b_ref, c_ref, lam_ref, step_ref, skip_ref, y_ref, kept_ref, state):
    @pl.when(pl.program_id(0) == 0)
    def _():
        state[...] = jnp.zeros_like(state)

    rows_b, rows_c = b_ref[...], c_ref[...]
    step = step_ref[...]
    gram = mm(rows_c, rows_b, ((1,), (1,)))
    level, across, last, weight, fade = levels(lam_ref[...], step)
    kept_ref[0] = state[...].astype(BF16)
    entering = mm(rows_c, state[...].astype(BF16))
    by_state = rows_b.T
    low_half = iota2((1, LANES), 1) < HEAD
    for first in range(0, heads, 2):
        lanes = slice(first * HEAD, (first + 2) * HEAD)
        x = x_ref[:, lanes].astype(F32)
        scaled = x * pair_of(step, first, low_half)
        total = pair_of(fade, first, low_half) * entering[:, lanes] + skip_ref[:, lanes] * x
        for head, keep in ((first, low_half), (first + 1, jnp.logical_not(low_half))):
            mixing = (gram * spread(level, across, head)).astype(BF16)
            total += mm(mixing, jnp.where(keep, scaled, 0.0).astype(BF16))
        y_ref[:, lanes] = total
        update = mm(by_state, (x * pair_of(weight, first, low_half)).astype(BF16))
        state[:, lanes] = state[:, lanes] * pair_of(last, first, low_half) + update


def scan_forward(x, rows_b, rows_c, lam, step, skip):
    tokens, width = x.shape
    heads = width // HEAD
    count = tokens // BLOCK
    by_block = lambda i: (i, 0)
    return pl.pallas_call(
        functools.partial(forward_kernel, heads),
        grid=(count,),
        in_specs=[
            pl.BlockSpec((BLOCK, width), by_block),
            pl.BlockSpec((BLOCK, STATE), by_block),
            pl.BlockSpec((BLOCK, STATE), by_block),
            pl.BlockSpec((BLOCK, LANES), by_block),
            pl.BlockSpec((BLOCK, LANES), by_block),
            pl.BlockSpec((1, width), lambda i: (0, 0)),
        ],
        out_specs=[
            pl.BlockSpec((BLOCK, width), by_block),
            pl.BlockSpec((1, STATE, width), lambda i: (i, 0, 0)),
        ],
        out_shape=[
            jax.ShapeDtypeStruct((tokens, width), F32),
            jax.ShapeDtypeStruct((count, STATE, width), BF16),
        ],
        scratch_shapes=[pltpu.VMEM((STATE, width), F32)],
        compiler_params=pltpu.CompilerParams(vmem_limit_bytes=32 * 1024 * 1024),
        cost_estimate=pl.CostEstimate(
            flops=2 * tokens * width * (2 * BLOCK + 2 * STATE),
            bytes_accessed=tokens * width * 6,
            transcendentals=tokens * heads * BLOCK,
        ),
        name="scan_forward",
    )(x, rows_b, rows_c, lam, step, skip)


def head_sums(product, chooser):
    high = product.astype(BF16)
    rest = (product - high.astype(F32)).astype(BF16)
    return mm(high, chooser) + mm(rest, chooser)


def backward_kernel(
    heads,
    x_ref,
    b_ref,
    c_ref,
    lam_ref,
    step_ref,
    skip_ref,
    grad_ref,
    kept_ref,
    dx_ref,
    db_ref,
    dc_ref,
    dstep_ref,
    dlam_ref,
    dskip_ref,
    back,
    mixed_grads,
    for_step,
    for_level,
    left,
    right,
    sums,
):
    @pl.when(pl.program_id(0) == 0)
    def _():
        back[...] = jnp.zeros_like(back)
        dskip_ref[...] = jnp.zeros_like(dskip_ref)

    rows_b, rows_c = b_ref[...], c_ref[...]
    step = step_ref[...]
    gram = mm(rows_c, rows_b, ((1,), (1,)))
    gram_t = mm(rows_b, rows_c, ((1,), (1,)))
    level, across, last, weight, fade = levels(lam_ref[...], step)
    step_across = step.T
    at_row, at_col = iota2((BLOCK, BLOCK), 0), iota2((BLOCK, BLOCK), 1)
    order = (at_row > at_col).astype(F32) - (at_row < at_col).astype(F32)
    low_half = iota2((1, LANES), 1) < HEAD
    lane = iota2((1, LANES), 1)
    by_state = rows_c.T
    kept = kept_ref[0]
    old_back = back[...].astype(BF16)
    entering = mm(rows_c, kept)
    leaving = mm(rows_b, old_back)
    at_last = jnp.sum(kept.astype(F32) * back[...], axis=0, keepdims=True)
    mixed_grads[...] = jnp.zeros_like(mixed_grads)
    left[...] = jnp.zeros_like(left)
    right[...] = jnp.zeros_like(right)
    sums[...] = jnp.zeros_like(sums)
    d_b = jnp.zeros((BLOCK, STATE), F32)
    d_c = jnp.zeros((BLOCK, STATE), F32)
    for first in range(0, heads, 2):
        lanes = slice(first * HEAD, (first + 2) * HEAD)
        x_low = x_ref[:, lanes]
        grad_low = grad_ref[:, lanes]
        x, grad = x_low.astype(F32), grad_low.astype(F32)
        through = jnp.zeros((BLOCK, LANES), F32)
        for head, keep in ((first, low_half), (first + 1, jnp.logical_not(low_half))):
            decay = spread(level, across, head)
            grad_own = jnp.where(keep, grad, 0.0).astype(BF16)
            pairs = mm(grad_own, x_low, ((1,), (1,)))
            through += mm((gram_t * decay).astype(BF16), grad_own)
            scaled = decay * pairs * step_across[head : head + 1, :]
            mixed_grads[...] += scaled
            ordered = gram * scaled * order
            left[...] = jnp.where(
                lane == head, jnp.sum(ordered, axis=1, keepdims=True), left[...]
            )
            right[head : head + 1, :] = jnp.sum(ordered, axis=0, keepdims=True)
        weight_pair = pair_of(weight, first, low_half)
        step_pair = pair_of(step, first, low_half)
        fade_pair = pair_of(fade, first, low_half)
        out_pair = pair_of(jnp.exp(level - level[BLOCK - 1 : BLOCK, :]), first, low_half)
        leave = leaving[:, lanes]
        dx_ref[:, lanes] = step_pair * through + weight_pair * leave + skip_ref[:, lanes] * grad
        for_step[:, lanes] = x * (through + out_pair * leave)
        weighted = weight_pair * x
        faded = fade_pair * grad
        for_level[:, lanes] = weighted * leave - faded * entering[:, lanes]
        sums[0:1, lanes] = jnp.sum(weighted * leave, axis=0, keepdims=True)
        dskip_ref[:, lanes] += jnp.sum(x * grad, axis=0, keepdims=True)
        faded_low = faded.astype(BF16)
        d_b += mm(weighted.astype(BF16), old_back[:, lanes], ((1,), (1,)))
        d_c += mm(faded_low, kept[:, lanes], ((1,), (1,)))
        back[:, lanes] = back[:, lanes] * pair_of(last, first, low_half) + mm(by_state, faded_low)
    all_pairs = mixed_grads[...]
    db_ref[...] = d_b + mm(all_pairs.T.astype(BF16), rows_c)
    dc_ref[...] = d_c + mm(all_pairs.astype(BF16), rows_b)
    width = x_ref.shape[1]
    chooser = (iota2((width, LANES), 0) // HEAD == iota2((width, LANES), 1)).astype(BF16)
    dstep_ref[...] = head_sums(for_step[...], chooser)
    sums[1:2, :] = at_last
    whole = head_sums(sums[...], chooser)
    d_level = head_sums(for_level[...], chooser) - left[...] + right[...].T
    final = -whole[0:1, :] - last * whole[1:2, :]
    d_level = d_level + jnp.where(iota2((BLOCK, 1), 0) == BLOCK - 1, final, 0.0)
    tri = (at_row <= at_col).astype(F32)
    dlam_ref[...] = mm_exact(tri, d_level)


def scan_backward(x, rows_b, rows_c, lam, step, skip, grad, kept):
    tokens, width = x.shape
    heads = width // HEAD
    count = tokens // BLOCK
    by_block = lambda i: (count - 1 - i, 0)
    return pl.pallas_call(
        functools.partial(backward_kernel, heads),
        grid=(count,),
        in_specs=[
            pl.BlockSpec((BLOCK, width), by_block),
            pl.BlockSpec((BLOCK, STATE), by_block),
            pl.BlockSpec((BLOCK, STATE), by_block),
            pl.BlockSpec((BLOCK, LANES), by_block),
            pl.BlockSpec((BLOCK, LANES), by_block),
            pl.BlockSpec((1, width), lambda i: (0, 0)),
            pl.BlockSpec((BLOCK, width), by_block),
            pl.BlockSpec((1, STATE, width), lambda i: (count - 1 - i, 0, 0)),
        ],
        out_specs=[
            pl.BlockSpec((BLOCK, width), by_block),
            pl.BlockSpec((BLOCK, STATE), by_block),
            pl.BlockSpec((BLOCK, STATE), by_block),
            pl.BlockSpec((BLOCK, LANES), by_block),
            pl.BlockSpec((BLOCK, LANES), by_block),
            pl.BlockSpec((1, width), lambda i: (0, 0)),
        ],
        out_shape=[
            jax.ShapeDtypeStruct((tokens, width), F32),
            jax.ShapeDtypeStruct((tokens, STATE), F32),
            jax.ShapeDtypeStruct((tokens, STATE), F32),
            jax.ShapeDtypeStruct((tokens, LANES), F32),
            jax.ShapeDtypeStruct((tokens, LANES), F32),
            jax.ShapeDtypeStruct((1, width), F32),
        ],
        scratch_shapes=[
            pltpu.VMEM((STATE, width), F32),
            pltpu.VMEM((BLOCK, BLOCK), F32),
            pltpu.VMEM((BLOCK, width), F32),
            pltpu.VMEM((BLOCK, width), F32),
            pltpu.VMEM((BLOCK, LANES), F32),
            pltpu.VMEM((LANES, BLOCK), F32),
            pltpu.VMEM((8, width), F32),
        ],
        compiler_params=pltpu.CompilerParams(vmem_limit_bytes=32 * 1024 * 1024),
        cost_estimate=pl.CostEstimate(
            flops=2 * tokens * width * (4 * BLOCK + 5 * STATE),
            bytes_accessed=tokens * width * 10,
            transcendentals=tokens * heads * BLOCK,
        ),
        name="scan_backward",
    )(x, rows_b, rows_c, lam, step, skip, grad, kept)


def conv_taps(array, taps, weight):
    tokens = array.shape[0]
    padded = jnp.pad(array, ((taps - 1, 0), (0, 0)))
    return sum(weight[k] * padded[k : k + tokens] for k in range(taps))


def silu_slope(v):
    s = jax.nn.sigmoid(v)
    return s * (1.0 + v * (1.0 - s))


def on_device(
    hidden,
    cotangent,
    seq_lens,
    norm_gain,
    in_weight,
    conv_weight,
    conv_bias,
    dt_bias,
    a_log,
    d_skip,
    gate_gain,
    out_weight,
):
    n_ctx, n_fsdp = lax.axis_size("ctx"), lax.axis_size("fsdp")
    me, shard = lax.axis_index("ctx"), lax.axis_index("fsdp")
    taps = conv_weight.shape[0]
    heads_all = dt_bias.shape[0] * n_fsdp
    inner = out_weight.shape[0] * n_fsdp
    heads, width = heads_all // n_ctx, inner // n_ctx
    model = hidden.shape[2]
    conv_width = width + 2 * STATE
    columns = width + conv_width + LANES
    x_at, bc_at, dt_at = inner, 2 * inner, 2 * inner + 2 * STATE

    small = (norm_gain, conv_weight.reshape(-1), conv_bias, dt_bias, a_log, d_skip, gate_gain)
    cuts = [0]
    for part in small:
        cuts.append(cuts[-1] + part.shape[0])
    packed = lax.all_gather(jnp.concatenate(small), "fsdp", axis=0)
    parts = [packed[:, cuts[i] : cuts[i + 1]] for i in range(len(small))]
    gain_norm = parts[0].reshape(-1).astype(F32)
    taps_all = jnp.moveaxis(parts[1].reshape(n_fsdp, taps, -1), 0, 1).reshape(taps, -1)
    bias_all = parts[2].reshape(-1)

    def own(vector, size):
        return lax.dynamic_slice_in_dim(vector, me * size, size, axis=-1)

    def own_channels(vector):
        return jnp.concatenate(
            [own(vector[..., :inner], width), vector[..., inner:]], axis=-1
        ).astype(F32)

    weight_conv, bias_conv = own_channels(taps_all), own_channels(bias_all)
    bias_step = own(parts[3].reshape(-1), heads).astype(F32)
    rate = jnp.exp(own(parts[4].reshape(-1), heads).astype(F32))
    skip = own(parts[5].reshape(-1), heads).astype(F32)
    gain_gate = own(parts[6].reshape(-1), width).astype(F32)

    resid_low = lax.all_gather(hidden[0], "ctx", axis=0, tiled=True)
    own_columns = jnp.concatenate(
        [
            lax.dynamic_slice_in_dim(in_weight, me * width, width, axis=1),
            lax.dynamic_slice_in_dim(in_weight, x_at + me * width, width, axis=1),
            in_weight[:, bc_at:dt_at],
            lax.dynamic_slice_in_dim(in_weight, dt_at + me * heads, heads, axis=1),
            jnp.zeros((in_weight.shape[0], LANES - heads), BF16),
        ],
        axis=1,
    )
    weight_in = lax.all_gather(own_columns, "fsdp", axis=0, tiled=True)
    upstream = lax.all_gather(cotangent[0], "ctx", axis=0, tiled=True)
    piece = out_weight.shape[0] // n_ctx
    there = [(c * n_fsdp + f, f * n_ctx + c) for c in range(n_ctx) for f in range(n_fsdp)]
    back_again = [(b, a) for a, b in there]
    own_rows = lax.ppermute(
        lax.dynamic_slice_in_dim(out_weight, me * piece, piece, axis=0), ("ctx", "fsdp"), there
    )
    weight_out = lax.all_gather(own_rows, "fsdp", axis=0, tiled=True)

    tokens = resid_low.shape[0]
    valid = (jnp.arange(tokens, dtype=jnp.int32) < seq_lens[0]).astype(F32)[:, None]
    resid = resid_low.astype(F32)
    scale_in = lax.rsqrt(jnp.mean(resid * resid, axis=1, keepdims=True) + EPS)
    normed = (resid * scale_in * gain_norm).astype(BF16)
    projected = mm(normed, weight_in).astype(BF16)
    gate_raw = projected[:, :width].astype(F32)
    conv_in = projected[:, width : width + conv_width].astype(F32)
    step_raw = projected[:, width + conv_width : width + conv_width + heads].astype(F32)

    convolved = bias_conv + conv_taps(conv_in, taps, weight_conv)
    activated = jax.nn.silu(convolved).astype(BF16)
    values = activated[:, :width]
    rows_b = activated[:, width : width + STATE]
    rows_c = activated[:, width + STATE :]
    step = jax.nn.softplus(step_raw + bias_step) * valid
    lam = step * rate
    in_lanes = lambda a: jnp.pad(a, ((0, 0), (0, LANES - heads)))
    step_lanes, lam_lanes = in_lanes(step), in_lanes(lam)
    skip_wide = jnp.repeat(skip, HEAD)[None, :]
    mixed_ssd, kept = scan_forward(values, rows_b, rows_c, lam_lanes, step_lanes, skip_wide)

    gate = jax.nn.silu(gate_raw)
    gated = mixed_ssd * gate
    d_mixed = upstream * valid.astype(BF16)
    d_yn = mm(d_mixed, weight_out, ((1,), (1,)))
    d_gain = gain_gate * d_yn
    stats = jnp.stack([jnp.sum(gated * gated, axis=1), jnp.sum(gated * d_gain, axis=1)])
    stats = lax.psum(stats, "ctx") / inner
    scale_gate = lax.rsqrt(stats[0] + EPS)[:, None]
    normed_gate = (gated * scale_gate * gain_gate).astype(BF16)
    mixed = lax.psum_scatter(
        mm(normed_gate, weight_out).astype(BF16), "ctx", scatter_dimension=0, tiled=True
    )
    own_tokens = lambda a: lax.dynamic_slice_in_dim(a, me * hidden.shape[1], hidden.shape[1], axis=0)
    layer_out = (hidden[0].astype(F32) + own_tokens(valid) * mixed.astype(F32)).astype(BF16)

    grad_out = mm(normed_gate, d_mixed, ((0,), (0,))).astype(BF16)
    grad_out = lax.psum_scatter(grad_out, "fsdp", scatter_dimension=0, tiled=True)
    grad_gain_gate = jnp.sum(d_yn * gated * scale_gate, axis=0)
    d_gated = scale_gate * d_gain - gated * (scale_gate**3 * stats[1][:, None])
    d_ssd = (d_gated * gate).astype(BF16)
    d_gate_raw = d_gated * mixed_ssd * silu_slope(gate_raw)

    d_x, d_b, d_c, d_step, d_lam, d_skip_lanes = scan_backward(
        values, rows_b, rows_c, lam_lanes, step_lanes, skip_wide, d_ssd, kept
    )
    d_step, d_lam = d_step[:, :heads], d_lam[:, :heads]
    grad_skip = jnp.sum(d_skip_lanes.reshape(heads, HEAD), axis=1)
    d_raw = valid * (d_step + d_lam * rate) * jax.nn.sigmoid(step_raw + bias_step)
    grad_bias_step = jnp.sum(d_raw, axis=0)
    grad_log = jnp.sum(d_lam * lam, axis=0)
    d_conv = jnp.concatenate([d_x, d_b, d_c], axis=1) * silu_slope(convolved)
    grad_bias_conv = jnp.sum(d_conv, axis=0)
    padded_in = jnp.pad(conv_in, ((taps - 1, 0), (0, 0)))
    grad_taps = jnp.stack(
        [jnp.sum(d_conv * padded_in[k : k + tokens], axis=0) for k in range(taps)]
    )
    padded_back = jnp.pad(d_conv, ((0, taps - 1), (0, 0)))
    d_conv_in = sum(
        weight_conv[k] * padded_back[taps - 1 - k : taps - 1 - k + tokens] for k in range(taps)
    )
    d_projected = jnp.concatenate([d_gate_raw, d_conv_in, in_lanes(d_raw)], axis=1).astype(BF16)
    grad_in = mm(normed, d_projected, ((0,), (0,))).astype(BF16)
    grad_in = lax.psum_scatter(grad_in, "fsdp", scatter_dimension=0, tiled=True)
    d_normed = mm(d_projected, weight_in, ((1,), (1,))).astype(BF16)
    d_normed = lax.psum_scatter(d_normed, "ctx", scatter_dimension=0, tiled=True).astype(F32)

    resid_own = hidden[0].astype(F32)
    scale_own = own_tokens(scale_in)
    f = gain_norm * d_normed
    d_resid = scale_own * f - resid_own * scale_own**3 * jnp.mean(
        resid_own * f, axis=1, keepdims=True
    )
    hidden_grad = (cotangent[0].astype(F32) + d_resid).astype(BF16)
    grad_gain_norm = jnp.sum(d_normed * resid_own * scale_own, axis=0)

    def placed(value, total):
        start = me * value.shape[-1]
        return lax.dynamic_update_slice_in_dim(
            jnp.zeros(value.shape[:-1] + (total,), F32), value, start, axis=-1
        )

    def placed_channels(value):
        return jnp.concatenate([placed(value[..., :width], inner), value[..., width:]], axis=-1)

    small_grads = (
        grad_gain_norm,
        placed_channels(grad_taps).reshape(-1),
        placed_channels(grad_bias_conv),
        placed(grad_bias_step, heads_all),
        placed(grad_log, heads_all),
        placed(grad_skip, heads_all),
        placed(grad_gain_gate, inner),
    )
    flat = lax.psum(jnp.concatenate(small_grads), ("ctx", "fsdp"))
    outs, at = [], 0
    for value in small_grads:
        outs.append(flat[at : at + value.shape[0]])
        at += value.shape[0]

    def own_shard(vector):
        size = vector.shape[-1] // n_fsdp
        return lax.dynamic_slice_in_dim(vector, shard * size, size, axis=-1)

    conv_total = inner + 2 * STATE
    pieces = lax.all_gather(grad_in, "ctx", axis=0).astype(F32)
    in_order = lambda a: jnp.moveaxis(a, 0, 1).reshape(a.shape[1], -1)
    grad_in_weight = jnp.concatenate(
        [
            in_order(pieces[:, :, :width]),
            in_order(pieces[:, :, width : 2 * width]),
            jnp.sum(pieces[:, :, 2 * width : width + conv_width], axis=0),
            in_order(pieces[:, :, width + conv_width : width + conv_width + heads]),
        ],
        axis=1,
    )
    grad_out = lax.ppermute(grad_out, ("ctx", "fsdp"), back_again)
    grad_out_weight = lax.all_gather(grad_out, "ctx", axis=0, tiled=True).astype(F32)
    return (
        layer_out[None],
        hidden_grad[None],
        own_shard(outs[0]),
        grad_in_weight,
        own_shard(outs[1].reshape(taps, conv_total)),
        own_shard(outs[2]),
        own_shard(outs[3]),
        own_shard(outs[4]),
        own_shard(outs[5]),
        own_shard(outs[6]),
        grad_out_weight,
    )


def solution(mesh):
    tokens, rows, flat = P("fsdp", "ctx", None), P("fsdp", None), P("fsdp")
    taps = P(None, "fsdp")
    return jax.shard_map(
        on_device,
        mesh=mesh,
        in_specs=(tokens, tokens, flat, flat, rows, taps, flat, flat, flat, flat, flat, rows),
        out_specs=(tokens, tokens, flat, rows, taps, flat, flat, flat, flat, flat, rows),
        check_vma=False,
    )
```

```python
import functools

import jax
import jax.numpy as jnp
from jax import lax
from jax.experimental import pallas as pl
from jax.experimental.pallas import tpu as pltpu
from jax.sharding import PartitionSpec as P

HEAD = 64
STATE = 128
BLOCK = 256
LANES = 128
EPS = 1e-05
F32 = jnp.float32
BF16 = jnp.bfloat16


def mm(a, b, contract=((1,), (0,))):
    return lax.dot_general(a, b, (contract, ((), ())), preferred_element_type=F32)


def mm_exact(a, b, contract=((1,), (0,))):
    return lax.dot_general(
        a, b, (contract, ((), ())), precision=lax.Precision.HIGHEST, preferred_element_type=F32
    )


def iota2(shape, axis):
    return lax.broadcasted_iota(jnp.int32, shape, axis)


def levels(lam, step):
    tri = (iota2((BLOCK, BLOCK), 0) >= iota2((BLOCK, BLOCK), 1)).astype(F32)
    level = mm_exact(tri, lam)
    across = level.T
    last = level[BLOCK - 1 : BLOCK, :]
    weight = jnp.exp(level - last) * step
    return level, across, jnp.exp(-last), weight, jnp.exp(-level)


def pair_of(array, first, low_half):
    return jnp.where(low_half, array[:, first : first + 1], array[:, first + 1 : first + 2])


def spread(level, across, head):
    return jnp.exp(-jnp.abs(level[:, head : head + 1] - across[head : head + 1, :]))


def forward_kernel(heads, x_ref, b_ref, c_ref, lam_ref, step_ref, skip_ref, y_ref, kept_ref, state):
    @pl.when(pl.program_id(0) == 0)
    def _():
        state[...] = jnp.zeros_like(state)

    rows_b, rows_c = b_ref[...], c_ref[...]
    step = step_ref[...]
    gram = mm(rows_c, rows_b, ((1,), (1,)))
    level, across, last, weight, fade = levels(lam_ref[...], step)
    kept_ref[0] = state[...].astype(BF16)
    entering = mm(rows_c, state[...].astype(BF16))
    by_state = rows_b.T
    low_half = iota2((1, LANES), 1) < HEAD
    for first in range(0, heads, 2):
        lanes = slice(first * HEAD, (first + 2) * HEAD)
        x = x_ref[:, lanes].astype(F32)
        scaled = x * pair_of(step, first, low_half)
        total = pair_of(fade, first, low_half) * entering[:, lanes] + skip_ref[:, lanes] * x
        for head, keep in ((first, low_half), (first + 1, jnp.logical_not(low_half))):
            mixing = (gram * spread(level, across, head)).astype(BF16)
            total += mm(mixing, jnp.where(keep, scaled, 0.0).astype(BF16))
        y_ref[:, lanes] = total
        update = mm(by_state, (x * pair_of(weight, first, low_half)).astype(BF16))
        state[:, lanes] = state[:, lanes] * pair_of(last, first, low_half) + update


def scan_forward(x, rows_b, rows_c, lam, step, skip):
    tokens, width = x.shape
    heads = width // HEAD
    count = tokens // BLOCK
    by_block = lambda i: (i, 0)
    return pl.pallas_call(
        functools.partial(forward_kernel, heads),
        grid=(count,),
        in_specs=[
            pl.BlockSpec((BLOCK, width), by_block),
            pl.BlockSpec((BLOCK, STATE), by_block),
            pl.BlockSpec((BLOCK, STATE), by_block),
            pl.BlockSpec((BLOCK, LANES), by_block),
            pl.BlockSpec((BLOCK, LANES), by_block),
            pl.BlockSpec((1, width), lambda i: (0, 0)),
        ],
        out_specs=[
            pl.BlockSpec((BLOCK, width), by_block),
            pl.BlockSpec((1, STATE, width), lambda i: (i, 0, 0)),
        ],
        out_shape=[
            jax.ShapeDtypeStruct((tokens, width), F32),
            jax.ShapeDtypeStruct((count, STATE, width), BF16),
        ],
        scratch_shapes=[pltpu.VMEM((STATE, width), F32)],
        compiler_params=pltpu.CompilerParams(vmem_limit_bytes=32 * 1024 * 1024),
        cost_estimate=pl.CostEstimate(
            flops=2 * tokens * width * (2 * BLOCK + 2 * STATE),
            bytes_accessed=tokens * width * 6,
            transcendentals=tokens * heads * BLOCK,
        ),
        name="scan_forward",
    )(x, rows_b, rows_c, lam, step, skip)


def head_sums(product, chooser):
    high = product.astype(BF16)
    rest = (product - high.astype(F32)).astype(BF16)
    return mm(high, chooser) + mm(rest, chooser)


def backward_kernel(
    heads,
    x_ref,
    b_ref,
    c_ref,
    lam_ref,
    step_ref,
    skip_ref,
    grad_ref,
    kept_ref,
    dx_ref,
    db_ref,
    dc_ref,
    dstep_ref,
    dlam_ref,
    dskip_ref,
    back,
    mixed_grads,
    for_step,
    for_level,
    left,
    right,
    sums,
):
    @pl.when(pl.program_id(0) == 0)
    def _():
        back[...] = jnp.zeros_like(back)
        dskip_ref[...] = jnp.zeros_like(dskip_ref)

    rows_b, rows_c = b_ref[...], c_ref[...]
    step = step_ref[...]
    gram = mm(rows_c, rows_b, ((1,), (1,)))
    gram_t = mm(rows_b, rows_c, ((1,), (1,)))
    level, across, last, weight, fade = levels(lam_ref[...], step)
    step_across = step.T
    at_row, at_col = iota2((BLOCK, BLOCK), 0), iota2((BLOCK, BLOCK), 1)
    order = (at_row > at_col).astype(F32) - (at_row < at_col).astype(F32)
    low_half = iota2((1, LANES), 1) < HEAD
    lane = iota2((1, LANES), 1)
    by_state = rows_c.T
    kept = kept_ref[0]
    old_back = back[...].astype(BF16)
    entering = mm(rows_c, kept)
    leaving = mm(rows_b, old_back)
    at_last = jnp.sum(kept.astype(F32) * back[...], axis=0, keepdims=True)
    mixed_grads[...] = jnp.zeros_like(mixed_grads)
    left[...] = jnp.zeros_like(left)
    right[...] = jnp.zeros_like(right)
    sums[...] = jnp.zeros_like(sums)
    d_b = jnp.zeros((BLOCK, STATE), F32)
    d_c = jnp.zeros((BLOCK, STATE), F32)
    for first in range(0, heads, 2):
        lanes = slice(first * HEAD, (first + 2) * HEAD)
        x_low = x_ref[:, lanes]
        grad_low = grad_ref[:, lanes]
        x, grad = x_low.astype(F32), grad_low.astype(F32)
        through = jnp.zeros((BLOCK, LANES), F32)
        for head, keep in ((first, low_half), (first + 1, jnp.logical_not(low_half))):
            decay = spread(level, across, head)
            grad_own = jnp.where(keep, grad, 0.0).astype(BF16)
            pairs = mm(grad_own, x_low, ((1,), (1,)))
            through += mm((gram_t * decay).astype(BF16), grad_own)
            scaled = decay * pairs * step_across[head : head + 1, :]
            mixed_grads[...] += scaled
            ordered = gram * scaled * order
            left[...] = jnp.where(
                lane == head, jnp.sum(ordered, axis=1, keepdims=True), left[...]
            )
            right[head : head + 1, :] = jnp.sum(ordered, axis=0, keepdims=True)
        weight_pair = pair_of(weight, first, low_half)
        step_pair = pair_of(step, first, low_half)
        fade_pair = pair_of(fade, first, low_half)
        out_pair = pair_of(jnp.exp(level - level[BLOCK - 1 : BLOCK, :]), first, low_half)
        leave = leaving[:, lanes]
        dx_ref[:, lanes] = step_pair * through + weight_pair * leave + skip_ref[:, lanes] * grad
        for_step[:, lanes] = x * (through + out_pair * leave)
        weighted = weight_pair * x
        faded = fade_pair * grad
        for_level[:, lanes] = weighted * leave - faded * entering[:, lanes]
        sums[0:1, lanes] = jnp.sum(weighted * leave, axis=0, keepdims=True)
        dskip_ref[:, lanes] += jnp.sum(x * grad, axis=0, keepdims=True)
        faded_low = faded.astype(BF16)
        d_b += mm(weighted.astype(BF16), old_back[:, lanes], ((1,), (1,)))
        d_c += mm(faded_low, kept[:, lanes], ((1,), (1,)))
        back[:, lanes] = back[:, lanes] * pair_of(last, first, low_half) + mm(by_state, faded_low)
    all_pairs = mixed_grads[...]
    db_ref[...] = d_b + mm(all_pairs.T.astype(BF16), rows_c)
    dc_ref[...] = d_c + mm(all_pairs.astype(BF16), rows_b)
    width = x_ref.shape[1]
    chooser = (iota2((width, LANES), 0) // HEAD == iota2((width, LANES), 1)).astype(BF16)
    dstep_ref[...] = head_sums(for_step[...], chooser)
    sums[1:2, :] = at_last
    whole = head_sums(sums[...], chooser)
    d_level = head_sums(for_level[...], chooser) - left[...] + right[...].T
    final = -whole[0:1, :] - last * whole[1:2, :]
    d_level = d_level + jnp.where(iota2((BLOCK, 1), 0) == BLOCK - 1, final, 0.0)
    tri = (at_row <= at_col).astype(F32)
    dlam_ref[...] = mm_exact(tri, d_level)


def scan_backward(x, rows_b, rows_c, lam, step, skip, grad, kept):
    tokens, width = x.shape
    heads = width // HEAD
    count = tokens // BLOCK
    by_block = lambda i: (count - 1 - i, 0)
    return pl.pallas_call(
        functools.partial(backward_kernel, heads),
        grid=(count,),
        in_specs=[
            pl.BlockSpec((BLOCK, width), by_block),
            pl.BlockSpec((BLOCK, STATE), by_block),
            pl.BlockSpec((BLOCK, STATE), by_block),
            pl.BlockSpec((BLOCK, LANES), by_block),
            pl.BlockSpec((BLOCK, LANES), by_block),
            pl.BlockSpec((1, width), lambda i: (0, 0)),
            pl.BlockSpec((BLOCK, width), by_block),
            pl.BlockSpec((1, STATE, width), lambda i: (count - 1 - i, 0, 0)),
        ],
        out_specs=[
            pl.BlockSpec((BLOCK, width), by_block),
            pl.BlockSpec((BLOCK, STATE), by_block),
            pl.BlockSpec((BLOCK, STATE), by_block),
            pl.BlockSpec((BLOCK, LANES), by_block),
            pl.BlockSpec((BLOCK, LANES), by_block),
            pl.BlockSpec((1, width), lambda i: (0, 0)),
        ],
        out_shape=[
            jax.ShapeDtypeStruct((tokens, width), F32),
            jax.ShapeDtypeStruct((tokens, STATE), F32),
            jax.ShapeDtypeStruct((tokens, STATE), F32),
            jax.ShapeDtypeStruct((tokens, LANES), F32),
            jax.ShapeDtypeStruct((tokens, LANES), F32),
            jax.ShapeDtypeStruct((1, width), F32),
        ],
        scratch_shapes=[
            pltpu.VMEM((STATE, width), F32),
            pltpu.VMEM((BLOCK, BLOCK), F32),
            pltpu.VMEM((BLOCK, width), F32),
            pltpu.VMEM((BLOCK, width), F32),
            pltpu.VMEM((BLOCK, LANES), F32),
            pltpu.VMEM((LANES, BLOCK), F32),
            pltpu.VMEM((8, width), F32),
        ],
        compiler_params=pltpu.CompilerParams(vmem_limit_bytes=32 * 1024 * 1024),
        cost_estimate=pl.CostEstimate(
            flops=2 * tokens * width * (4 * BLOCK + 5 * STATE),
            bytes_accessed=tokens * width * 10,
            transcendentals=tokens * heads * BLOCK,
        ),
        name="scan_backward",
    )(x, rows_b, rows_c, lam, step, skip, grad, kept)


MESH = pl.DeviceIdType.MESH


def ring_place(index, half):
    a, b = index // 2, index % 2
    return a + b * (2 * half - 1 - 2 * a)


def ring_index(place, half):
    b = place // half
    return 2 * (place + b * (2 * half - 1 - 2 * place)) + b


class Ring:
    def __init__(self, n):
        self.n, self.half = n, n // 2
        self.me, self.shard = lax.axis_index("ctx"), lax.axis_index("fsdp")
        self.place = ring_place(self.shard, self.half)

    def at(self, steps):
        return ring_index(lax.rem(self.place + steps + 2 * self.n, self.n), self.half)

    def neighbour(self, way):
        return (self.me, self.at(1 if way == 0 else -1))


def gather_kernel(
    n,
    n_ctx,
    hidden,
    cotangent,
    in_weight,
    shared,
    out_weight,
    hidden_all,
    cotangent_all,
    w_x,
    w_s,
    w_z,
    w_o,
    local_sem,
    ring_send,
    ring_recv,
    ctx_send,
    ctx_recv,
    piece_send,
    piece_recv,
):
    ring = Ring(n)
    me, shard = ring.me, ring.shard
    width = w_x.shape[2]
    inner = width * n_ctx
    row = me // 2
    other_core = (me + 1 - 2 * (me % 2), shard)
    other_row = (me + 2 - 4 * row, shard)
    piece = w_o.shape[1]
    sent_as = shard * n_ctx + me
    piece_to = (sent_as // n, sent_as % n)
    held_as = me * n + shard
    piece_from = (held_as % n_ctx, held_as // n_ctx)
    moves = sent_as != held_as

    barrier = pltpu.get_barrier_semaphore()
    for device in (other_core, other_row, ring.neighbour(0), ring.neighbour(1)):
        pl.semaphore_signal(barrier, inc=1, device_id=device, device_id_type=MESH)

    @pl.when(moves)
    def _():
        for device in (piece_to, piece_from):
            pl.semaphore_signal(barrier, inc=1, device_id=device, device_id_type=MESH)
        pl.semaphore_wait(barrier, 6)

    @pl.when(jnp.logical_not(moves))
    def _():
        pl.semaphore_wait(barrier, 4)

    def remote(source, target, send, recv, device):
        return pltpu.make_async_remote_copy(
            src_ref=source,
            dst_ref=target,
            send_sem=send,
            recv_sem=recv,
            device_id=device,
            device_id_type=MESH,
        )

    own_x = in_weight.at[:, pl.ds(pl.multiple_of(inner + me * width, LANES), width)]
    own_z = in_weight.at[:, pl.ds(pl.multiple_of(me * width, LANES), width)]
    half = width // 2
    quarter = w_o.shape[2] // 4
    rows, more = w_x.shape[1] // 2, w_s.shape[1] // 2
    by_rows = lambda a, way, count, first, size: a.at[
        pl.ds(way * count, count), pl.ds(first, size)
    ]
    x_part = lambda sub: lambda a, way: by_rows(a, way, rows, sub * half, half)
    s_part = lambda a, way: by_rows(a, way, more, 0, a.shape[1])
    o_part = lambda sub: lambda a, way: a.at[:, pl.ds((2 * way + sub) * quarter, quarter)]
    phases = (
        ((w_s, shared, s_part), (w_x, own_x, x_part(0)), (w_x, own_x, x_part(1))),
        ((w_z, own_z, x_part(0)), (w_z, own_z, x_part(1))),
        ((w_o, None, o_part(0)), (w_o, None, o_part(1))),
    )
    numbered, count = [], 0
    for phase in phases:
        numbered.append([(count + i,) + stream for i, stream in enumerate(phase)])
        count += len(phase)

    def hop(stream, way, step):
        number, whole, own, part = stream
        index = ring.at(-step if way == 0 else step)
        source = whole.at[index]
        if own is not None and isinstance(step, int) and step == 0:
            source = own
        return remote(
            part(source, way),
            part(whole.at[index], way),
            ring_send.at[number, way],
            ring_recv.at[number, way, step],
            ring.neighbour(way),
        )

    def arrives(stream, way, step):
        number, whole, own, part = stream
        index = ring.at(-step - 1 if way == 0 else step + 1)
        landed = part(whole.at[index], way)
        return remote(
            landed, landed, ring_send.at[number, way], ring_recv.at[number, way, step],
            ring.neighbour(way),
        )

    def start_phase(number):
        for stream in numbered[number]:
            for way in (0, 1):
                hop(stream, way, 0).start()

    to_row = lambda i, a, whole: remote(
        a, whole.at[me], ctx_send.at[i, 0], ctx_recv.at[i, 0], other_row
    )
    to_core = lambda i, a, whole: remote(
        a, whole.at[me], ctx_send.at[i, 1], ctx_recv.at[i, 1], other_core
    )
    beyond = other_row[0]
    pass_on = lambda i, whole: remote(
        whole.at[beyond], whole.at[beyond], ctx_send.at[i, 2], ctx_recv.at[i, 2], other_core
    )

    to_row(0, hidden, hidden_all).start()
    start_phase(0)
    to_core(0, hidden, hidden_all).start()
    own_piece = out_weight.at[pl.ds(me * piece, piece)]
    send_piece = remote(own_piece, w_o.at[piece_to[1]], piece_send, piece_recv, piece_to)
    keep_piece = pltpu.make_async_copy(own_piece, w_o.at[shard], local_sem.at[5])

    @pl.when(moves)
    def _():
        send_piece.start()

    @pl.when(jnp.logical_not(moves))
    def _():
        keep_piece.start()

    locals_ = [
        pltpu.make_async_copy(source, target, local_sem.at[i])
        for i, (source, target) in enumerate(
            (
                (hidden, hidden_all.at[me]),
                (cotangent, cotangent_all.at[me]),
                (own_x, w_x.at[shard]),
                (own_z, w_z.at[shard]),
                (shared, w_s.at[shard]),
            )
        )
    ]
    for copy in locals_:
        copy.start()

    def finish_ctx(i, a, whole):
        to_row(i, a, whole).wait_recv()
        pass_on(i, whole).start()

    def close_ctx(i, a, whole):
        to_row(i, a, whole).wait_send()
        to_core(i, a, whole).wait()
        pass_on(i, whole).wait()

    def run_phase(number, after):
        def body(step, carry):
            for stream in numbered[number]:
                for way in (0, 1):
                    arrives(stream, way, step).wait_recv()
                    hop(stream, way, step).wait_send()
                    hop(stream, way, step + 1).start()
            return carry

        lax.fori_loop(0, n - 2, body, 0)
        after()
        for stream in numbered[number]:
            for way in (0, 1):
                arrives(stream, way, n - 2).wait_recv()
                hop(stream, way, n - 2).wait_send()

    def after_first():
        finish_ctx(0, hidden, hidden_all)
        to_row(1, cotangent, cotangent_all).start()
        to_core(1, cotangent, cotangent_all).start()
        start_phase(1)

    def after_second():
        @pl.when(moves)
        def _():
            send_piece.wait()

        @pl.when(jnp.logical_not(moves))
        def _():
            keep_piece.wait()

        finish_ctx(1, cotangent, cotangent_all)
        start_phase(2)

    def after_third():
        close_ctx(0, hidden, hidden_all)
        close_ctx(1, cotangent, cotangent_all)
        for copy in locals_:
            copy.wait()

    run_phase(0, after_first)
    run_phase(1, after_second)
    run_phase(2, after_third)


def gather_all(n, n_ctx, hidden, cotangent, in_weight, shared, out_weight):
    tokens, model = hidden.shape
    width = out_weight.shape[0] * n // n_ctx
    rows = in_weight.shape[0]
    any_space = pl.BlockSpec(memory_space=pl.ANY)
    low = lambda *shape: jax.ShapeDtypeStruct(shape, BF16)
    return pl.pallas_call(
        functools.partial(gather_kernel, n, n_ctx),
        in_specs=[any_space] * 5,
        out_specs=[any_space] * 6,
        out_shape=[
            low(n_ctx, tokens, model),
            low(n_ctx, tokens, model),
            low(n, rows, width),
            low(n, shared.shape[0], shared.shape[1]),
            low(n, rows, width),
            low(n, width // n, model),
        ],
        scratch_shapes=[
            pltpu.SemaphoreType.DMA((6,)),
            pltpu.SemaphoreType.DMA((7, 2)),
            pltpu.SemaphoreType.DMA((7, 2, n - 1)),
            pltpu.SemaphoreType.DMA((2, 3)),
            pltpu.SemaphoreType.DMA((2, 3)),
            pltpu.SemaphoreType.DMA,
            pltpu.SemaphoreType.DMA,
        ],
        compiler_params=pltpu.CompilerParams(collective_id=0, has_side_effects=True),
        name="gather_all",
    )(hidden, cotangent, in_weight, shared, out_weight)


def conv_taps(array, taps, weight):
    tokens = array.shape[0]
    padded = jnp.pad(array, ((taps - 1, 0), (0, 0)))
    return sum(weight[k] * padded[k : k + tokens] for k in range(taps))


def silu_slope(v):
    s = jax.nn.sigmoid(v)
    return s * (1.0 + v * (1.0 - s))


def on_device(
    hidden,
    cotangent,
    seq_lens,
    norm_gain,
    in_weight,
    conv_weight,
    conv_bias,
    dt_bias,
    a_log,
    d_skip,
    gate_gain,
    out_weight,
):
    n_ctx, n_fsdp = lax.axis_size("ctx"), lax.axis_size("fsdp")
    me, shard = lax.axis_index("ctx"), lax.axis_index("fsdp")
    taps = conv_weight.shape[0]
    heads_all = dt_bias.shape[0] * n_fsdp
    inner = out_weight.shape[0] * n_fsdp
    heads, width = heads_all // n_ctx, inner // n_ctx
    model, rows = hidden.shape[2], in_weight.shape[0]
    both = 2 * STATE
    shared_width = -(-(both + heads_all) // LANES) * LANES

    small = (norm_gain, conv_weight.reshape(-1), conv_bias, dt_bias, a_log, d_skip, gate_gain)
    cuts = [0]
    for part in small:
        cuts.append(cuts[-1] + part.shape[0])
    small_rows = -(-cuts[-1] // (32 * shared_width)) * 32
    fill = small_rows * shared_width - cuts[-1]
    shared = jnp.concatenate(
        [
            jnp.pad(in_weight[:, 2 * inner :], ((0, 0), (0, shared_width - both - heads_all))),
            jnp.concatenate(small + (jnp.zeros((fill,), BF16),)).reshape(small_rows, shared_width),
        ],
        axis=0,
    )
    resid_low, upstream, w_x, w_s, w_z, w_o = gather_all(
        n_fsdp, n_ctx, hidden[0], cotangent[0], in_weight, shared, out_weight
    )
    resid_low, upstream = resid_low.reshape(-1, model), upstream.reshape(-1, model)
    w_x, w_z, w_o = w_x.reshape(-1, width), w_z.reshape(-1, width), w_o.reshape(-1, model)
    packed = w_s[:, rows:, :].reshape(n_fsdp, -1)
    w_s = w_s[:, :rows, :].reshape(-1, shared_width)
    parts = [packed[:, cuts[i] : cuts[i + 1]] for i in range(len(small))]
    gain_norm = parts[0].reshape(-1).astype(F32)
    taps_all = jnp.moveaxis(parts[1].reshape(n_fsdp, taps, -1), 0, 1).reshape(taps, -1).astype(F32)
    bias_all = parts[2].reshape(-1).astype(F32)

    def own(vector, size):
        return lax.dynamic_slice_in_dim(vector, me * size, size, axis=-1)

    taps_x, taps_s = own(taps_all[:, :inner], width), taps_all[:, inner:]
    bias_x, bias_s = own(bias_all[:inner], width), bias_all[inner:]
    bias_step = own(parts[3].reshape(-1), heads).astype(F32)
    rate = jnp.exp(own(parts[4].reshape(-1), heads).astype(F32))
    skip = own(parts[5].reshape(-1), heads).astype(F32)
    gain_gate = own(parts[6].reshape(-1), width).astype(F32)

    tokens = resid_low.shape[0]
    valid = (jnp.arange(tokens, dtype=jnp.int32) < seq_lens[0]).astype(F32)[:, None]
    resid = resid_low.astype(F32)
    scale_in = lax.rsqrt(jnp.mean(resid * resid, axis=1, keepdims=True) + EPS)
    normed = (resid * scale_in * gain_norm).astype(BF16)
    gate_raw = mm(normed, w_z).astype(BF16).astype(F32)
    conv_in_x = mm(normed, w_x).astype(BF16).astype(F32)
    projected_s = mm(normed, w_s).astype(BF16).astype(F32)
    conv_in_s = projected_s[:, :both]
    step_raw = own(projected_s[:, both : both + heads_all], heads)

    convolved_x = bias_x + conv_taps(conv_in_x, taps, taps_x)
    convolved_s = bias_s + conv_taps(conv_in_s, taps, taps_s)
    values = jax.nn.silu(convolved_x).astype(BF16)
    activated_s = jax.nn.silu(convolved_s).astype(BF16)
    rows_b, rows_c = activated_s[:, :STATE], activated_s[:, STATE:]
    step = jax.nn.softplus(step_raw + bias_step) * valid
    lam = step * rate
    in_lanes = lambda a: jnp.pad(a, ((0, 0), (0, LANES - heads)))
    step_lanes, lam_lanes = in_lanes(step), in_lanes(lam)
    skip_wide = jnp.repeat(skip, HEAD)[None, :]
    mixed_ssd, kept = scan_forward(values, rows_b, rows_c, lam_lanes, step_lanes, skip_wide)

    gate = jax.nn.silu(gate_raw)
    gated = mixed_ssd * gate
    d_mixed = upstream * valid.astype(BF16)
    d_yn = mm(d_mixed, w_o, ((1,), (1,)))
    d_gain = gain_gate * d_yn
    stats = jnp.stack([jnp.sum(gated * gated, axis=1), jnp.sum(gated * d_gain, axis=1)])
    stats = lax.psum(stats, "ctx") / inner
    scale_gate = lax.rsqrt(stats[0] + EPS)[:, None]
    normed_gate = (gated * scale_gate * gain_gate).astype(BF16)
    mixed = lax.psum_scatter(
        mm(normed_gate, w_o).astype(BF16), "ctx", scatter_dimension=0, tiled=True
    )
    own_tokens = lambda a: lax.dynamic_slice_in_dim(a, me * hidden.shape[1], hidden.shape[1], axis=0)
    layer_out = (hidden[0].astype(F32) + own_tokens(valid) * mixed.astype(F32)).astype(BF16)

    grad_out = mm(normed_gate, d_mixed, ((0,), (0,))).astype(BF16)
    grad_out = lax.psum_scatter(grad_out, "fsdp", scatter_dimension=0, tiled=True)
    grad_gain_gate = jnp.sum(d_yn * gated * scale_gate, axis=0)
    d_gated = scale_gate * d_gain - gated * (scale_gate**3 * stats[1][:, None])
    d_ssd = (d_gated * gate).astype(BF16)
    d_gate_raw = d_gated * mixed_ssd * silu_slope(gate_raw)

    d_x, d_b, d_c, d_step, d_lam, d_skip_lanes = scan_backward(
        values, rows_b, rows_c, lam_lanes, step_lanes, skip_wide, d_ssd, kept
    )
    d_step, d_lam = d_step[:, :heads], d_lam[:, :heads]
    grad_skip = jnp.sum(d_skip_lanes.reshape(heads, HEAD), axis=1)
    d_raw = valid * (d_step + d_lam * rate) * jax.nn.sigmoid(step_raw + bias_step)
    grad_bias_step = jnp.sum(d_raw, axis=0)
    grad_log = jnp.sum(d_lam * lam, axis=0)
    def conv_back(d_active, convolved, conv_in, weight):
        d_conv = d_active * silu_slope(convolved)
        padded_in = jnp.pad(conv_in, ((taps - 1, 0), (0, 0)))
        grad_taps = jnp.stack(
            [jnp.sum(d_conv * padded_in[k : k + tokens], axis=0) for k in range(taps)]
        )
        padded = jnp.pad(d_conv, ((0, taps - 1), (0, 0)))
        d_in = sum(weight[k] * padded[taps - 1 - k : taps - 1 - k + tokens] for k in range(taps))
        return d_in.astype(BF16), grad_taps, jnp.sum(d_conv, axis=0)

    d_in_x, grad_taps_x, grad_bias_x = conv_back(d_x, convolved_x, conv_in_x, taps_x)
    d_in_s, grad_taps_s, grad_bias_s = conv_back(
        jnp.concatenate([d_b, d_c], axis=1), convolved_s, conv_in_s, taps_s
    )
    d_raw_all = lax.dynamic_update_slice_in_dim(
        jnp.zeros((tokens, shared_width - both), BF16), d_raw.astype(BF16), me * heads, axis=1
    )
    d_in_s = jnp.concatenate([d_in_s, d_raw_all], axis=1)
    d_in_z = d_gate_raw.astype(BF16)
    grad_in = jnp.concatenate(
        [mm(normed, d, ((0,), (0,))).astype(BF16) for d in (d_in_z, d_in_x, d_in_s)], axis=1
    )
    grad_in = lax.psum_scatter(grad_in, "fsdp", scatter_dimension=0, tiled=True)
    d_normed = (
        mm(d_in_z, w_z, ((1,), (1,)))
        + mm(d_in_x, w_x, ((1,), (1,)))
        + mm(d_in_s, w_s, ((1,), (1,)))
    ).astype(BF16)
    d_normed = lax.psum_scatter(d_normed, "ctx", scatter_dimension=0, tiled=True).astype(F32)

    resid_own = hidden[0].astype(F32)
    scale_own = own_tokens(scale_in)
    f = gain_norm * d_normed
    d_resid = scale_own * f - resid_own * scale_own**3 * jnp.mean(
        resid_own * f, axis=1, keepdims=True
    )
    hidden_grad = (cotangent[0].astype(F32) + d_resid).astype(BF16)
    grad_gain_norm = jnp.sum(d_normed * resid_own * scale_own, axis=0)

    def placed(value, total):
        start = me * value.shape[-1]
        return lax.dynamic_update_slice_in_dim(
            jnp.zeros(value.shape[:-1] + (total,), F32), value, start, axis=-1
        )

    small_grads = (
        grad_gain_norm,
        jnp.concatenate([placed(grad_taps_x, inner), grad_taps_s], axis=1).reshape(-1),
        jnp.concatenate([placed(grad_bias_x, inner), grad_bias_s]),
        placed(grad_bias_step, heads_all),
        placed(grad_log, heads_all),
        placed(grad_skip, heads_all),
        placed(grad_gain_gate, inner),
    )
    flat = lax.psum(jnp.concatenate(small_grads), ("ctx", "fsdp"))
    outs, at = [], 0
    for value in small_grads:
        outs.append(flat[at : at + value.shape[0]])
        at += value.shape[0]

    def own_shard(vector):
        size = vector.shape[-1] // n_fsdp
        return lax.dynamic_slice_in_dim(vector, shard * size, size, axis=-1)

    conv_total = inner + both
    pieces = lax.all_gather(grad_in, "ctx", axis=0).astype(F32)
    in_order = lambda a: jnp.moveaxis(a, 0, 1).reshape(a.shape[1], -1)
    grad_in_weight = jnp.concatenate(
        [
            in_order(pieces[:, :, :width]),
            in_order(pieces[:, :, width : 2 * width]),
            jnp.sum(pieces[:, :, 2 * width : 2 * width + both + heads_all], axis=0),
        ],
        axis=1,
    )
    back_again = [(f * n_ctx + c, c * n_fsdp + f) for c in range(n_ctx) for f in range(n_fsdp)]
    grad_out = lax.ppermute(grad_out, ("ctx", "fsdp"), back_again)
    grad_out_weight = lax.all_gather(grad_out, "ctx", axis=0, tiled=True).astype(F32)
    return (
        layer_out[None],
        hidden_grad[None],
        own_shard(outs[0]),
        grad_in_weight,
        own_shard(outs[1].reshape(taps, conv_total)),
        own_shard(outs[2]),
        own_shard(outs[3]),
        own_shard(outs[4]),
        own_shard(outs[5]),
        own_shard(outs[6]),
        grad_out_weight,
    )


def solution(mesh):
    tokens, rows, flat = P("fsdp", "ctx", None), P("fsdp", None), P("fsdp")
    taps = P(None, "fsdp")
    return jax.shard_map(
        on_device,
        mesh=mesh,
        in_specs=(tokens, tokens, flat, flat, rows, taps, flat, flat, flat, flat, flat, rows),
        out_specs=(tokens, tokens, flat, rows, taps, flat, flat, flat, flat, flat, rows),
        check_vma=False,
    )
```

```python
import functools

import jax
import jax.numpy as jnp
from jax import lax
from jax.experimental import pallas as pl
from jax.experimental.pallas import tpu as pltpu
from jax.sharding import PartitionSpec as P

HEAD = 64
STATE = 128
BLOCK = 256
LANES = 128
EPS = 1e-05
F32 = jnp.float32
BF16 = jnp.bfloat16


def mm(a, b, contract=((1,), (0,))):
    return lax.dot_general(a, b, (contract, ((), ())), preferred_element_type=F32)


def mm_exact(a, b, contract=((1,), (0,))):
    return lax.dot_general(
        a, b, (contract, ((), ())), precision=lax.Precision.HIGHEST, preferred_element_type=F32
    )


def iota2(shape, axis):
    return lax.broadcasted_iota(jnp.int32, shape, axis)


def levels(lam, step):
    tri = (iota2((BLOCK, BLOCK), 0) >= iota2((BLOCK, BLOCK), 1)).astype(F32)
    level = mm_exact(tri, lam)
    across = level.T
    last = level[BLOCK - 1 : BLOCK, :]
    weight = jnp.exp(level - last) * step
    return level, across, jnp.exp(-last), weight, jnp.exp(-level)


def pair_of(array, first, low_half):
    return jnp.where(low_half, array[:, first : first + 1], array[:, first + 1 : first + 2])


def spread(level, across, head):
    return jnp.exp(-jnp.abs(level[:, head : head + 1] - across[head : head + 1, :]))


def forward_kernel(heads, x_ref, b_ref, c_ref, lam_ref, step_ref, skip_ref, y_ref, kept_ref, state):
    @pl.when(pl.program_id(0) == 0)
    def _():
        state[...] = jnp.zeros_like(state)

    rows_b, rows_c = b_ref[...], c_ref[...]
    step = step_ref[...]
    gram = mm(rows_c, rows_b, ((1,), (1,)))
    level, across, last, weight, fade = levels(lam_ref[...], step)
    kept_ref[0] = state[...].astype(BF16)
    entering = mm(rows_c, state[...].astype(BF16))
    by_state = rows_b.T
    low_half = iota2((1, LANES), 1) < HEAD
    for first in range(0, heads, 2):
        lanes = slice(first * HEAD, (first + 2) * HEAD)
        x = x_ref[:, lanes].astype(F32)
        scaled = x * pair_of(step, first, low_half)
        total = pair_of(fade, first, low_half) * entering[:, lanes] + skip_ref[:, lanes] * x
        for head, keep in ((first, low_half), (first + 1, jnp.logical_not(low_half))):
            mixing = (gram * spread(level, across, head)).astype(BF16)
            total += mm(mixing, jnp.where(keep, scaled, 0.0).astype(BF16))
        y_ref[:, lanes] = total
        update = mm(by_state, (x * pair_of(weight, first, low_half)).astype(BF16))
        state[:, lanes] = state[:, lanes] * pair_of(last, first, low_half) + update


def scan_forward(x, rows_b, rows_c, lam, step, skip):
    tokens, width = x.shape
    heads = width // HEAD
    count = tokens // BLOCK
    by_block = lambda i: (i, 0)
    return pl.pallas_call(
        functools.partial(forward_kernel, heads),
        grid=(count,),
        in_specs=[
            pl.BlockSpec((BLOCK, width), by_block),
            pl.BlockSpec((BLOCK, STATE), by_block),
            pl.BlockSpec((BLOCK, STATE), by_block),
            pl.BlockSpec((BLOCK, LANES), by_block),
            pl.BlockSpec((BLOCK, LANES), by_block),
            pl.BlockSpec((1, width), lambda i: (0, 0)),
        ],
        out_specs=[
            pl.BlockSpec((BLOCK, width), by_block),
            pl.BlockSpec((1, STATE, width), lambda i: (i, 0, 0)),
        ],
        out_shape=[
            jax.ShapeDtypeStruct((tokens, width), F32),
            jax.ShapeDtypeStruct((count, STATE, width), BF16),
        ],
        scratch_shapes=[pltpu.VMEM((STATE, width), F32)],
        compiler_params=pltpu.CompilerParams(vmem_limit_bytes=32 * 1024 * 1024),
        cost_estimate=pl.CostEstimate(
            flops=2 * tokens * width * (2 * BLOCK + 2 * STATE),
            bytes_accessed=tokens * width * 6,
            transcendentals=tokens * heads * BLOCK,
        ),
        name="scan_forward",
    )(x, rows_b, rows_c, lam, step, skip)


def head_sums(product, chooser):
    high = product.astype(BF16)
    rest = (product - high.astype(F32)).astype(BF16)
    return mm(high, chooser) + mm(rest, chooser)


def backward_kernel(
    heads,
    x_ref,
    b_ref,
    c_ref,
    lam_ref,
    step_ref,
    skip_ref,
    grad_ref,
    kept_ref,
    dx_ref,
    db_ref,
    dc_ref,
    dstep_ref,
    dlam_ref,
    dskip_ref,
    back,
    mixed_grads,
    for_step,
    for_level,
    left,
    right,
    sums,
):
    @pl.when(pl.program_id(0) == 0)
    def _():
        back[...] = jnp.zeros_like(back)
        dskip_ref[...] = jnp.zeros_like(dskip_ref)

    rows_b, rows_c = b_ref[...], c_ref[...]
    step = step_ref[...]
    gram = mm(rows_c, rows_b, ((1,), (1,)))
    gram_t = mm(rows_b, rows_c, ((1,), (1,)))
    level, across, last, weight, fade = levels(lam_ref[...], step)
    step_across = step.T
    at_row, at_col = iota2((BLOCK, BLOCK), 0), iota2((BLOCK, BLOCK), 1)
    order = (at_row > at_col).astype(F32) - (at_row < at_col).astype(F32)
    low_half = iota2((1, LANES), 1) < HEAD
    lane = iota2((1, LANES), 1)
    by_state = rows_c.T
    kept = kept_ref[0]
    old_back = back[...].astype(BF16)
    entering = mm(rows_c, kept)
    leaving = mm(rows_b, old_back)
    at_last = jnp.sum(kept.astype(F32) * back[...], axis=0, keepdims=True)
    mixed_grads[...] = jnp.zeros_like(mixed_grads)
    left[...] = jnp.zeros_like(left)
    right[...] = jnp.zeros_like(right)
    sums[...] = jnp.zeros_like(sums)
    d_b = jnp.zeros((BLOCK, STATE), F32)
    d_c = jnp.zeros((BLOCK, STATE), F32)
    for first in range(0, heads, 2):
        lanes = slice(first * HEAD, (first + 2) * HEAD)
        x_low = x_ref[:, lanes]
        grad_low = grad_ref[:, lanes]
        x, grad = x_low.astype(F32), grad_low.astype(F32)
        through = jnp.zeros((BLOCK, LANES), F32)
        for head, keep in ((first, low_half), (first + 1, jnp.logical_not(low_half))):
            decay = spread(level, across, head)
            grad_own = jnp.where(keep, grad, 0.0).astype(BF16)
            pairs = mm(grad_own, x_low, ((1,), (1,)))
            through += mm((gram_t * decay).astype(BF16), grad_own)
            scaled = decay * pairs * step_across[head : head + 1, :]
            mixed_grads[...] += scaled
            ordered = gram * scaled * order
            left[...] = jnp.where(
                lane == head, jnp.sum(ordered, axis=1, keepdims=True), left[...]
            )
            right[head : head + 1, :] = jnp.sum(ordered, axis=0, keepdims=True)
        weight_pair = pair_of(weight, first, low_half)
        step_pair = pair_of(step, first, low_half)
        fade_pair = pair_of(fade, first, low_half)
        out_pair = pair_of(jnp.exp(level - level[BLOCK - 1 : BLOCK, :]), first, low_half)
        leave = leaving[:, lanes]
        dx_ref[:, lanes] = step_pair * through + weight_pair * leave + skip_ref[:, lanes] * grad
        for_step[:, lanes] = x * (through + out_pair * leave)
        weighted = weight_pair * x
        faded = fade_pair * grad
        for_level[:, lanes] = weighted * leave - faded * entering[:, lanes]
        sums[0:1, lanes] = jnp.sum(weighted * leave, axis=0, keepdims=True)
        dskip_ref[:, lanes] += jnp.sum(x * grad, axis=0, keepdims=True)
        faded_low = faded.astype(BF16)
        d_b += mm(weighted.astype(BF16), old_back[:, lanes], ((1,), (1,)))
        d_c += mm(faded_low, kept[:, lanes], ((1,), (1,)))
        back[:, lanes] = back[:, lanes] * pair_of(last, first, low_half) + mm(by_state, faded_low)
    all_pairs = mixed_grads[...]
    db_ref[...] = d_b + mm(all_pairs.T.astype(BF16), rows_c)
    dc_ref[...] = d_c + mm(all_pairs.astype(BF16), rows_b)
    width = x_ref.shape[1]
    chooser = (iota2((width, LANES), 0) // HEAD == iota2((width, LANES), 1)).astype(BF16)
    dstep_ref[...] = head_sums(for_step[...], chooser)
    sums[1:2, :] = at_last
    whole = head_sums(sums[...], chooser)
    d_level = head_sums(for_level[...], chooser) - left[...] + right[...].T
    final = -whole[0:1, :] - last * whole[1:2, :]
    d_level = d_level + jnp.where(iota2((BLOCK, 1), 0) == BLOCK - 1, final, 0.0)
    tri = (at_row <= at_col).astype(F32)
    dlam_ref[...] = mm_exact(tri, d_level)


def scan_backward(x, rows_b, rows_c, lam, step, skip, grad, kept):
    tokens, width = x.shape
    heads = width // HEAD
    count = tokens // BLOCK
    by_block = lambda i: (count - 1 - i, 0)
    return pl.pallas_call(
        functools.partial(backward_kernel, heads),
        grid=(count,),
        in_specs=[
            pl.BlockSpec((BLOCK, width), by_block),
            pl.BlockSpec((BLOCK, STATE), by_block),
            pl.BlockSpec((BLOCK, STATE), by_block),
            pl.BlockSpec((BLOCK, LANES), by_block),
            pl.BlockSpec((BLOCK, LANES), by_block),
            pl.BlockSpec((1, width), lambda i: (0, 0)),
            pl.BlockSpec((BLOCK, width), by_block),
            pl.BlockSpec((1, STATE, width), lambda i: (count - 1 - i, 0, 0)),
        ],
        out_specs=[
            pl.BlockSpec((BLOCK, width), by_block),
            pl.BlockSpec((BLOCK, STATE), by_block),
            pl.BlockSpec((BLOCK, STATE), by_block),
            pl.BlockSpec((BLOCK, LANES), by_block),
            pl.BlockSpec((BLOCK, LANES), by_block),
            pl.BlockSpec((1, width), lambda i: (0, 0)),
        ],
        out_shape=[
            jax.ShapeDtypeStruct((tokens, width), F32),
            jax.ShapeDtypeStruct((tokens, STATE), F32),
            jax.ShapeDtypeStruct((tokens, STATE), F32),
            jax.ShapeDtypeStruct((tokens, LANES), F32),
            jax.ShapeDtypeStruct((tokens, LANES), F32),
            jax.ShapeDtypeStruct((1, width), F32),
        ],
        scratch_shapes=[
            pltpu.VMEM((STATE, width), F32),
            pltpu.VMEM((BLOCK, BLOCK), F32),
            pltpu.VMEM((BLOCK, width), F32),
            pltpu.VMEM((BLOCK, width), F32),
            pltpu.VMEM((BLOCK, LANES), F32),
            pltpu.VMEM((LANES, BLOCK), F32),
            pltpu.VMEM((8, width), F32),
        ],
        compiler_params=pltpu.CompilerParams(vmem_limit_bytes=32 * 1024 * 1024),
        cost_estimate=pl.CostEstimate(
            flops=2 * tokens * width * (4 * BLOCK + 5 * STATE),
            bytes_accessed=tokens * width * 10,
            transcendentals=tokens * heads * BLOCK,
        ),
        name="scan_backward",
    )(x, rows_b, rows_c, lam, step, skip, grad, kept)


MESH = pl.DeviceIdType.MESH


def ring_place(index, half):
    a, b = index // 2, index % 2
    return a + b * (2 * half - 1 - 2 * a)


def ring_index(place, half):
    b = place // half
    return 2 * (place + b * (2 * half - 1 - 2 * place)) + b


class Ring:
    def __init__(self, n):
        self.n, self.half = n, n // 2
        self.me, self.shard = lax.axis_index("ctx"), lax.axis_index("fsdp")
        self.place = ring_place(self.shard, self.half)

    def at(self, steps):
        return ring_index(lax.rem(self.place + steps + 2 * self.n, self.n), self.half)

    def neighbour(self, way):
        return (self.me, self.at(1 if way == 0 else -1))


def gather_kernel(
    n,
    n_ctx,
    hidden,
    cotangent,
    in_weight,
    shared,
    out_weight,
    hidden_all,
    cotangent_all,
    w_x,
    w_s,
    w_z,
    w_o,
    local_sem,
    ring_send,
    ring_recv,
    ctx_send,
    ctx_recv,
    piece_send,
    piece_recv,
):
    ring = Ring(n)
    me, shard = ring.me, ring.shard
    width = w_x.shape[2]
    inner = width * n_ctx
    row = me // 2
    other_core = (me + 1 - 2 * (me % 2), shard)
    other_row = (me + 2 - 4 * row, shard)
    piece = w_o.shape[1]
    sent_as = shard * n_ctx + me
    piece_to = (sent_as // n, sent_as % n)
    held_as = me * n + shard
    piece_from = (held_as % n_ctx, held_as // n_ctx)
    moves = sent_as != held_as

    barrier = pltpu.get_barrier_semaphore()
    for device in (other_core, other_row, ring.neighbour(0), ring.neighbour(1)):
        pl.semaphore_signal(barrier, inc=1, device_id=device, device_id_type=MESH)

    @pl.when(moves)
    def _():
        for device in (piece_to, piece_from):
            pl.semaphore_signal(barrier, inc=1, device_id=device, device_id_type=MESH)
        pl.semaphore_wait(barrier, 6)

    @pl.when(jnp.logical_not(moves))
    def _():
        pl.semaphore_wait(barrier, 4)

    def remote(source, target, send, recv, device):
        return pltpu.make_async_remote_copy(
            src_ref=source,
            dst_ref=target,
            send_sem=send,
            recv_sem=recv,
            device_id=device,
            device_id_type=MESH,
        )

    own_x = in_weight.at[:, pl.ds(pl.multiple_of(inner + me * width, LANES), width)]
    own_z = in_weight.at[:, pl.ds(pl.multiple_of(me * width, LANES), width)]
    half = width // 2
    quarter = w_o.shape[2] // 4
    rows, more = w_x.shape[1] // 2, w_s.shape[1] // 2
    by_rows = lambda a, way, count, first, size: a.at[
        pl.ds(way * count, count), pl.ds(first, size)
    ]
    x_part = lambda sub: lambda a, way: by_rows(a, way, rows, sub * half, half)
    s_part = lambda a, way: by_rows(a, way, more, 0, a.shape[1])
    o_part = lambda sub: lambda a, way: a.at[:, pl.ds((2 * way + sub) * quarter, quarter)]
    phases = (
        ((w_s, shared, s_part), (w_x, own_x, x_part(0)), (w_x, own_x, x_part(1))),
        ((w_z, own_z, x_part(0)), (w_z, own_z, x_part(1))),
        ((w_o, None, o_part(0)), (w_o, None, o_part(1))),
    )
    numbered, count = [], 0
    for phase in phases:
        numbered.append([(count + i,) + stream for i, stream in enumerate(phase)])
        count += len(phase)

    def hop(stream, way, step):
        number, whole, own, part = stream
        index = ring.at(-step if way == 0 else step)
        source = whole.at[index]
        if own is not None and isinstance(step, int) and step == 0:
            source = own
        return remote(
            part(source, way),
            part(whole.at[index], way),
            ring_send.at[number, way],
            ring_recv.at[number, way, step],
            ring.neighbour(way),
        )

    def arrives(stream, way, step):
        number, whole, own, part = stream
        index = ring.at(-step - 1 if way == 0 else step + 1)
        landed = part(whole.at[index], way)
        return remote(
            landed, landed, ring_send.at[number, way], ring_recv.at[number, way, step],
            ring.neighbour(way),
        )

    def start_phase(number):
        for stream in numbered[number]:
            for way in (0, 1):
                hop(stream, way, 0).start()

    to_row = lambda i, a, whole: remote(
        a, whole.at[me], ctx_send.at[i, 0], ctx_recv.at[i, 0], other_row
    )
    to_core = lambda i, a, whole: remote(
        a, whole.at[me], ctx_send.at[i, 1], ctx_recv.at[i, 1], other_core
    )
    beyond = other_row[0]
    pass_on = lambda i, whole: remote(
        whole.at[beyond], whole.at[beyond], ctx_send.at[i, 2], ctx_recv.at[i, 2], other_core
    )

    to_row(0, hidden, hidden_all).start()
    start_phase(0)
    to_core(0, hidden, hidden_all).start()
    own_piece = out_weight.at[pl.ds(me * piece, piece)]
    send_piece = remote(own_piece, w_o.at[piece_to[1]], piece_send, piece_recv, piece_to)
    keep_piece = pltpu.make_async_copy(own_piece, w_o.at[shard], local_sem.at[5])

    @pl.when(moves)
    def _():
        send_piece.start()

    @pl.when(jnp.logical_not(moves))
    def _():
        keep_piece.start()

    locals_ = [
        pltpu.make_async_copy(source, target, local_sem.at[i])
        for i, (source, target) in enumerate(
            (
                (hidden, hidden_all.at[me]),
                (cotangent, cotangent_all.at[me]),
                (own_x, w_x.at[shard]),
                (own_z, w_z.at[shard]),
                (shared, w_s.at[shard]),
            )
        )
    ]
    for copy in locals_:
        copy.start()

    def finish_ctx(i, a, whole):
        to_row(i, a, whole).wait_recv()
        pass_on(i, whole).start()

    def close_ctx(i, a, whole):
        to_row(i, a, whole).wait_send()
        to_core(i, a, whole).wait()
        pass_on(i, whole).wait()

    def run_phase(number, after):
        def body(step, carry):
            for stream in numbered[number]:
                for way in (0, 1):
                    arrives(stream, way, step).wait_recv()
                    hop(stream, way, step).wait_send()
                    hop(stream, way, step + 1).start()
            return carry

        lax.fori_loop(0, n - 2, body, 0)
        after()
        for stream in numbered[number]:
            for way in (0, 1):
                arrives(stream, way, n - 2).wait_recv()
                hop(stream, way, n - 2).wait_send()

    def after_first():
        finish_ctx(0, hidden, hidden_all)
        to_row(1, cotangent, cotangent_all).start()
        to_core(1, cotangent, cotangent_all).start()
        start_phase(1)

    def after_second():
        @pl.when(moves)
        def _():
            send_piece.wait()

        @pl.when(jnp.logical_not(moves))
        def _():
            keep_piece.wait()

        finish_ctx(1, cotangent, cotangent_all)
        start_phase(2)

    def after_third():
        close_ctx(0, hidden, hidden_all)
        close_ctx(1, cotangent, cotangent_all)
        for copy in locals_:
            copy.wait()

    run_phase(0, after_first)
    run_phase(1, after_second)
    run_phase(2, after_third)


def gather_all(n, n_ctx, hidden, cotangent, in_weight, shared, out_weight):
    tokens, model = hidden.shape
    width = out_weight.shape[0] * n // n_ctx
    rows = in_weight.shape[0]
    any_space = pl.BlockSpec(memory_space=pl.ANY)
    low = lambda *shape: jax.ShapeDtypeStruct(shape, BF16)
    return pl.pallas_call(
        functools.partial(gather_kernel, n, n_ctx),
        in_specs=[any_space] * 5,
        out_specs=[any_space] * 6,
        out_shape=[
            low(n_ctx, tokens, model),
            low(n_ctx, tokens, model),
            low(n, rows, width),
            low(n, shared.shape[0], shared.shape[1]),
            low(n, rows, width),
            low(n, width // n, model),
        ],
        scratch_shapes=[
            pltpu.SemaphoreType.DMA((6,)),
            pltpu.SemaphoreType.DMA((7, 2)),
            pltpu.SemaphoreType.DMA((7, 2, n - 1)),
            pltpu.SemaphoreType.DMA((2, 3)),
            pltpu.SemaphoreType.DMA((2, 3)),
            pltpu.SemaphoreType.DMA,
            pltpu.SemaphoreType.DMA,
        ],
        compiler_params=pltpu.CompilerParams(collective_id=0, has_side_effects=True),
        name="gather_all",
    )(hidden, cotangent, in_weight, shared, out_weight)


def reduce_kernel(
    n,
    n_ctx,
    normed_t,
    gate_t,
    d_mixed,
    d_z,
    d_x,
    d_s,
    mixed_parts,
    normed_parts,
    small,
    hidden,
    cotangent,
    gain,
    g_z,
    g_x,
    g_s,
    g_o,
    layer_out,
    hidden_grad,
    small_out,
    v_normed_t,
    v_gate_t,
    v_d_mixed,
    v_d_z,
    v_d_x,
    v_d_s,
    slot_o,
    slot_z,
    slot_x,
    slot_s,
    first_o,
    first_z,
    first_x,
    first_s,
    done_o,
    done_z,
    done_x,
    done_s,
    moved,
    mine,
    from_core,
    from_row,
    v_hidden,
    v_cotangent,
    v_gain,
    v_out,
    v_grad,
    small_all,
    small_ctx,
    load_sem,
    store_sem,
    ring_send,
    ring_recv,
    ctx_send,
    ctx_recv,
    own_sem,
    piece_send,
    piece_recv,
    part_send,
    part_recv,
    small_send,
    small_recv,
    small_ctx_send,
    small_ctx_recv,
):
    ring = Ring(n)
    me, shard = ring.me, ring.shard
    row = me // 2
    core = me % 2
    core_at = me + 1 - 2 * core
    row_at = me + 2 - 4 * row
    both_at = row_at + 1 - 2 * core
    other_core, other_row, other_both = (core_at, shard), (row_at, shard), (both_at, shard)
    held_as = me * n + shard
    piece_to = (held_as % n_ctx, held_as // n_ctx)
    sent_as = shard * n_ctx + me
    piece_from = (sent_as // n, sent_as % n)
    moves = sent_as != held_as

    barrier = pltpu.get_barrier_semaphore()

    def greet(device):
        pl.semaphore_signal(barrier, inc=1, device_id=device, device_id_type=MESH)

    def peer(offset):
        return (me, lax.rem(shard + offset, n))

    for device in (other_core, other_row, other_both):
        greet(device)
    lax.fori_loop(1, n, lambda j, carry: (greet(peer(j)), carry)[1], 0)

    loads = [
        pltpu.make_async_copy(source, target, load_sem.at[i])
        for i, (source, target) in enumerate(
            (
                (gate_t, v_gate_t),
                (d_mixed, v_d_mixed),
                (mixed_parts.at[row_at], mine.at[0, 1]),
                (normed_parts.at[row_at], mine.at[1, 1]),
                (normed_t, v_normed_t),
                (d_z, v_d_z),
                (mixed_parts.at[me], mine.at[0, 0]),
                (normed_parts.at[me], mine.at[1, 0]),
                (hidden, v_hidden),
                (cotangent, v_cotangent),
                (gain, v_gain),
                (small, small_all.at[shard, pl.ds(0, small.shape[0])]),
                (d_x, v_d_x),
                (d_s, v_d_s),
            )
        )
    ]
    for copy in loads:
        copy.start()

    @pl.when(moves)
    def _():
        greet(piece_to)
        greet(piece_from)
        pl.semaphore_wait(barrier, n + 4)

    @pl.when(jnp.logical_not(moves))
    def _():
        pl.semaphore_wait(barrier, n + 2)

    def remote(source, target, send, recv, device):
        return pltpu.make_async_remote_copy(
            src_ref=source,
            dst_ref=target,
            send_sem=send,
            recv_sem=recv,
            device_id=device,
            device_id_type=MESH,
        )

    def to_core(i, which):
        source = (mixed_parts, normed_parts)[i].at[(core_at, both_at)[which]]
        return remote(
            source, from_core.at[i, which], part_send.at[i, which], part_recv.at[i, which], other_core
        )

    def to_row(i):
        return remote(
            mine.at[i, 1], from_row.at[i], part_send.at[i, 2], part_recv.at[i, 2], other_row
        )

    for which in (1, 0):
        for i in (0, 1):
            to_core(i, which).start()

    rows, piece = v_normed_t.shape[0] // (2 * n), done_o.shape[0]
    half = v_d_z.shape[1] // 2
    quarter = v_d_mixed.shape[1] // 4

    def in_stream(number, right, first, size, slots, stage, done):
        def own(index, way):
            left = v_normed_t[pl.ds(pl.multiple_of((2 * index + way) * rows, 16), rows), :]
            return mm(left, right[:, first : first + size])

        return (
            number,
            own,
            lambda way, step: slots.at[step, way, :, pl.ds(first, size)],
            lambda way: stage.at[way, :, pl.ds(first, size)],
            lambda way: done.at[pl.ds(way * rows, rows), pl.ds(first, size)],
        )

    def out_stream(number, sub):
        def own(index, way):
            left = v_gate_t[pl.ds(pl.multiple_of(index * piece, 16), piece), :]
            at = (2 * way + sub) * quarter
            return mm(left, v_d_mixed[:, at : at + quarter])

        return (
            number,
            own,
            lambda way, step: slot_o.at[step, way, :, pl.ds(sub * quarter, quarter)],
            lambda way: first_o.at[way, :, pl.ds(sub * quarter, quarter)],
            lambda way: done_o.at[:, pl.ds((2 * way + sub) * quarter, quarter)],
        )

    phases = (
        (out_stream(0, 0), out_stream(1, 1)),
        (
            in_stream(2, v_d_z, 0, half, slot_z, first_z, done_z),
            in_stream(3, v_d_z, half, half, slot_z, first_z, done_z),
        ),
        (
            in_stream(4, v_d_s, 0, v_d_s.shape[1], slot_s, first_s, done_s),
            in_stream(5, v_d_x, 0, half, slot_x, first_x, done_x),
            in_stream(6, v_d_x, half, half, slot_x, first_x, done_x),
        ),
    )

    def hop(stream, way, step, source):
        number, own, slot, stage, done = stream
        return remote(
            source,
            slot(way, step),
            ring_send.at[number, way],
            ring_recv.at[number, way, step],
            ring.neighbour(way),
        )

    def start_phase(number):
        for stream in phases[number]:
            for way in (0, 1):
                stage = stream[3](way)
                stage[...] = stream[1](ring.at(-1 if way == 0 else 1), way).astype(BF16)
                hop(stream, way, 0, stage).start()

    def arrived(stream, way, step):
        number, own, slot, stage, done = stream
        partial = own(ring.at(-step - 2 if way == 0 else step + 2), way)
        hop(stream, way, step, stage(way)).wait()
        return slot(way, step)[...].astype(F32) + partial

    def run_phase(number, after):
        def body(step, carry):
            for stream in phases[number]:
                for way in (0, 1):
                    total = arrived(stream, way, step)
                    place = stream[2](way, step)
                    place[...] = total.astype(BF16)
                    hop(stream, way, step + 1, place).start()
            return carry

        lax.fori_loop(0, n - 2, body, 0)
        after()
        for stream in phases[number]:
            for way in (0, 1):
                done = stream[4](way)
                done[...] = arrived(stream, way, n - 2).astype(BF16)

    ctx_pairs = ((moved, g_o), (done_z, g_z), (done_x, g_x), (done_s, g_s))

    def share(i, kind):
        source, whole = ctx_pairs[i]
        if kind == 2:
            source, at = whole.at[row_at], row_at
        else:
            at = me
        device = other_row if kind == 0 else other_core
        return remote(source, whole.at[at], ctx_send.at[i, kind], ctx_recv.at[i, kind], device)

    def keep(i):
        source, whole = ctx_pairs[i]
        return pltpu.make_async_copy(source, whole.at[me], own_sem.at[i])

    def start_share(i):
        share(i, 0).start()
        share(i, 1).start()
        keep(i).start()

    def pass_share(i):
        share(i, 0).wait_recv()
        share(i, 2).start()

    def close_share(i):
        share(i, 0).wait_send()
        share(i, 1).wait()
        share(i, 2).wait()
        keep(i).wait()

    send_piece = remote(done_o, moved, piece_send, piece_recv, piece_to)
    keep_piece = pltpu.make_async_copy(done_o, moved, piece_send)

    def move_piece(wait):
        @pl.when(moves)
        def _():
            send_piece.wait() if wait else send_piece.start()

        @pl.when(jnp.logical_not(moves))
        def _():
            keep_piece.wait() if wait else keep_piece.start()

    def small_to(offset):
        return remote(
            small_all.at[shard],
            small_all.at[shard],
            small_send.at[offset - 1],
            small_recv.at[offset - 1],
            peer(offset),
        )

    def small_share(i):
        return remote(
            small_ctx.at[me],
            small_ctx.at[me],
            small_ctx_send.at[i],
            small_ctx_recv.at[i],
            (other_core, other_row, other_both)[i],
        )

    store_layer = pltpu.make_async_copy(v_out, layer_out, store_sem.at[0])
    store_grad = pltpu.make_async_copy(v_grad, hidden_grad, store_sem.at[1])
    store_small = pltpu.make_async_copy(small_ctx, small_out, store_sem.at[2])

    def sum_rows():
        for i in (0, 1):
            to_core(i, 1).wait()
            mine[i, 1] = (mine[i, 1].astype(F32) + from_core[i, 1].astype(F32)).astype(BF16)
            to_row(i).start()

    def whole_sum(i):
        to_core(i, 0).wait()
        to_row(i).wait()
        return (
            mine[i, 0].astype(F32) + from_core[i, 0].astype(F32) + from_row[i].astype(F32)
        )

    def finish_tokens():
        resid = v_hidden[...].astype(F32)
        v_out[...] = (resid + whole_sum(0)).astype(BF16)
        store_layer.start()
        scale = lax.rsqrt(jnp.mean(resid * resid, axis=1, keepdims=True) + EPS)
        d_normed = whole_sum(1)
        f = v_gain[...] * d_normed
        slope = scale**3 * jnp.mean(resid * f, axis=1, keepdims=True)
        v_grad[...] = (v_cotangent[...].astype(F32) + scale * f - resid * slope).astype(BF16)
        store_grad.start()
        by_model = jnp.sum(d_normed * resid * scale, axis=0, keepdims=True)
        base = small.shape[0]
        for j in range(by_model.shape[1] // LANES):
            small_all[shard, base + j : base + j + 1, :] = by_model[
                :, j * LANES : (j + 1) * LANES
            ]
        lax.fori_loop(1, n, lambda j, carry: (small_to(j).start(), carry)[1], 0)

    def sum_small():
        lax.fori_loop(1, n, lambda j, carry: (small_to(j).wait(), carry)[1], 0)
        small_ctx[me] = jnp.sum(small_all[...], axis=0)
        for i in range(3):
            small_share(i).start()

    loads[0].wait()
    loads[1].wait()
    start_phase(0)
    for copy in loads[2:]:
        copy.wait()
    sum_rows()

    def after_first():
        start_phase(1)

    def after_second():
        start_phase(2)
        move_piece(True)
        start_share(0)
        finish_tokens()

    def after_third():
        pass_share(0)
        pass_share(1)
        sum_small()

    run_phase(0, after_first)
    move_piece(False)
    run_phase(1, after_second)
    start_share(1)
    run_phase(2, after_third)
    start_share(2)
    start_share(3)
    for i in range(3):
        small_share(i).wait()
    store_small.start()
    pass_share(2)
    pass_share(3)
    for i in range(4):
        close_share(i)
    store_layer.wait()
    store_grad.wait()
    store_small.wait()


def reduce_all(
    n, n_ctx, normed_t, gate_t, d_mixed, d_z, d_x, d_s, mixed_parts, normed_parts, small, hidden, cotangent, gain
):
    model, tokens = normed_t.shape
    width, shared_width = d_z.shape[1], d_s.shape[1]
    rows, piece, own = model // n, width // n, hidden.shape[0]
    small_rows = small.shape[0] + model // LANES
    any_space = pl.BlockSpec(memory_space=pl.ANY)
    dma = pltpu.SemaphoreType.DMA
    low = lambda *shape: jax.ShapeDtypeStruct(shape, BF16)
    v_low = lambda *shape: pltpu.VMEM(shape, BF16)
    v_full = lambda *shape: pltpu.VMEM(shape, F32)
    return pl.pallas_call(
        functools.partial(reduce_kernel, n, n_ctx),
        in_specs=[any_space] * 12,
        out_specs=[any_space] * 7,
        out_shape=[
            low(n_ctx, rows, width),
            low(n_ctx, rows, width),
            low(n_ctx, rows, shared_width),
            low(n_ctx, piece, model),
            low(own, model),
            low(own, model),
            jax.ShapeDtypeStruct((n_ctx, small_rows, LANES), F32),
        ],
        scratch_shapes=[
            v_low(model, tokens),
            v_low(width, tokens),
            v_low(tokens, model),
            v_low(tokens, width),
            v_low(tokens, width),
            v_low(tokens, shared_width),
            v_low(n - 1, 2, piece, model // 2),
            v_low(n - 1, 2, rows // 2, width),
            v_low(n - 1, 2, rows // 2, width),
            v_low(n - 1, 2, rows // 2, shared_width),
            v_low(2, piece, model // 2),
            v_low(2, rows // 2, width),
            v_low(2, rows // 2, width),
            v_low(2, rows // 2, shared_width),
            v_low(piece, model),
            v_low(rows, width),
            v_low(rows, width),
            v_low(rows, shared_width),
            v_low(piece, model),
            v_low(2, 2, own, model),
            v_low(2, 2, own, model),
            v_low(2, own, model),
            v_low(own, model),
            v_low(own, model),
            v_full(1, model),
            v_low(own, model),
            v_low(own, model),
            v_full(n, small_rows, LANES),
            v_full(n_ctx, small_rows, LANES),
            dma((14,)),
            dma((3,)),
            dma((7, 2)),
            dma((7, 2, n - 1)),
            dma((4, 3)),
            dma((4, 3)),
            dma((4,)),
            dma,
            dma,
            dma((2, 3)),
            dma((2, 3)),
            dma((n - 1,)),
            dma((n - 1,)),
            dma((3,)),
            dma((3,)),
        ],
        compiler_params=pltpu.CompilerParams(
            collective_id=1, has_side_effects=True, vmem_limit_bytes=58 * 1024 * 1024
        ),
        name="reduce_all",
    )(
        normed_t, gate_t, d_mixed, d_z, d_x, d_s, mixed_parts, normed_parts, small, hidden, cotangent, gain
    )


def assemble_kernel(width, both_heads, z_ref, x_ref, s_ref, o_ref, in_ref, out_ref):
    n_ctx = z_ref.shape[0]
    for c in range(n_ctx):
        in_ref[:, c * width : (c + 1) * width] = z_ref[c].astype(F32)
        in_ref[:, (n_ctx + c) * width : (n_ctx + c + 1) * width] = x_ref[c].astype(F32)
    total = s_ref[0].astype(F32)
    for c in range(1, n_ctx):
        total += s_ref[c].astype(F32)
    in_ref[:, 2 * n_ctx * width :] = total[:, :both_heads]
    out_ref[...] = o_ref[...].astype(F32)


def assemble(g_z, g_x, g_s, g_o, both_heads):
    n_ctx, rows, width = g_z.shape
    shared_width, model = g_s.shape[2], g_o.shape[2]
    g_o = g_o.reshape(-1, model)
    steps = 4 if rows >= 64 and g_o.shape[0] >= 64 else 1
    tile, tile_o = rows // steps, g_o.shape[0] // steps
    columns = 2 * n_ctx * width + both_heads
    part = lambda size: pl.BlockSpec((n_ctx, tile, size), lambda i: (0, i, 0))
    return pl.pallas_call(
        functools.partial(assemble_kernel, width, both_heads),
        grid=(steps,),
        in_specs=[
            part(width),
            part(width),
            part(shared_width),
            pl.BlockSpec((tile_o, model), lambda i: (i, 0)),
        ],
        out_specs=[
            pl.BlockSpec((tile, columns), lambda i: (i, 0)),
            pl.BlockSpec((tile_o, model), lambda i: (i, 0)),
        ],
        out_shape=[
            jax.ShapeDtypeStruct((rows, columns), F32),
            jax.ShapeDtypeStruct(g_o.shape, F32),
        ],
        compiler_params=pltpu.CompilerParams(vmem_limit_bytes=32 * 1024 * 1024),
        name="assemble",
    )(g_z, g_x, g_s, g_o)


def conv_taps(array, taps, weight):
    tokens = array.shape[0]
    padded = jnp.pad(array, ((taps - 1, 0), (0, 0)))
    return sum(weight[k] * padded[k : k + tokens] for k in range(taps))


def silu_slope(v):
    s = jax.nn.sigmoid(v)
    return s * (1.0 + v * (1.0 - s))


def on_device(
    hidden,
    cotangent,
    seq_lens,
    norm_gain,
    in_weight,
    conv_weight,
    conv_bias,
    dt_bias,
    a_log,
    d_skip,
    gate_gain,
    out_weight,
):
    n_ctx, n_fsdp = lax.axis_size("ctx"), lax.axis_size("fsdp")
    me, shard = lax.axis_index("ctx"), lax.axis_index("fsdp")
    taps = conv_weight.shape[0]
    heads_all = dt_bias.shape[0] * n_fsdp
    inner = out_weight.shape[0] * n_fsdp
    heads, width = heads_all // n_ctx, inner // n_ctx
    model, rows = hidden.shape[2], in_weight.shape[0]
    both = 2 * STATE
    shared_width = -(-(both + heads_all) // LANES) * LANES

    small = (norm_gain, conv_weight.reshape(-1), conv_bias, dt_bias, a_log, d_skip, gate_gain)
    cuts = [0]
    for part in small:
        cuts.append(cuts[-1] + part.shape[0])
    small_rows = -(-cuts[-1] // (32 * shared_width)) * 32
    fill = small_rows * shared_width - cuts[-1]
    shared = jnp.concatenate(
        [
            jnp.pad(in_weight[:, 2 * inner :], ((0, 0), (0, shared_width - both - heads_all))),
            jnp.concatenate(small + (jnp.zeros((fill,), BF16),)).reshape(small_rows, shared_width),
        ],
        axis=0,
    )
    resid_low, upstream, w_x, w_s, w_z, w_o = gather_all(
        n_fsdp, n_ctx, hidden[0], cotangent[0], in_weight, shared, out_weight
    )
    resid_low, upstream = resid_low.reshape(-1, model), upstream.reshape(-1, model)
    w_x, w_z, w_o = w_x.reshape(-1, width), w_z.reshape(-1, width), w_o.reshape(-1, model)
    packed = w_s[:, rows:, :].reshape(n_fsdp, -1)
    w_s = w_s[:, :rows, :].reshape(-1, shared_width)
    parts = [packed[:, cuts[i] : cuts[i + 1]] for i in range(len(small))]
    gain_norm = parts[0].reshape(-1).astype(F32)
    taps_all = jnp.moveaxis(parts[1].reshape(n_fsdp, taps, -1), 0, 1).reshape(taps, -1).astype(F32)
    bias_all = parts[2].reshape(-1).astype(F32)

    def own(vector, size):
        return lax.dynamic_slice_in_dim(vector, me * size, size, axis=-1)

    taps_x, taps_s = own(taps_all[:, :inner], width), taps_all[:, inner:]
    bias_x, bias_s = own(bias_all[:inner], width), bias_all[inner:]
    bias_step = own(parts[3].reshape(-1), heads).astype(F32)
    rate = jnp.exp(own(parts[4].reshape(-1), heads).astype(F32))
    skip = own(parts[5].reshape(-1), heads).astype(F32)
    gain_gate = own(parts[6].reshape(-1), width).astype(F32)

    tokens = resid_low.shape[0]
    valid = (jnp.arange(tokens, dtype=jnp.int32) < seq_lens[0]).astype(F32)[:, None]
    resid = resid_low.astype(F32)
    scale_in = lax.rsqrt(jnp.mean(resid * resid, axis=1, keepdims=True) + EPS)
    normed = (resid * scale_in * gain_norm).astype(BF16)
    gate_raw = mm(normed, w_z).astype(BF16).astype(F32)
    conv_in_x = mm(normed, w_x).astype(BF16).astype(F32)
    projected_s = mm(normed, w_s).astype(BF16).astype(F32)
    conv_in_s = projected_s[:, :both]
    step_raw = own(projected_s[:, both : both + heads_all], heads)

    convolved_x = bias_x + conv_taps(conv_in_x, taps, taps_x)
    convolved_s = bias_s + conv_taps(conv_in_s, taps, taps_s)
    values = jax.nn.silu(convolved_x).astype(BF16)
    activated_s = jax.nn.silu(convolved_s).astype(BF16)
    rows_b, rows_c = activated_s[:, :STATE], activated_s[:, STATE:]
    step = jax.nn.softplus(step_raw + bias_step) * valid
    lam = step * rate
    in_lanes = lambda a: jnp.pad(a, ((0, 0), (0, LANES - heads)))
    step_lanes, lam_lanes = in_lanes(step), in_lanes(lam)
    skip_wide = jnp.repeat(skip, HEAD)[None, :]
    mixed_ssd, kept = scan_forward(values, rows_b, rows_c, lam_lanes, step_lanes, skip_wide)

    gate = jax.nn.silu(gate_raw)
    gated = mixed_ssd * gate
    d_mixed = upstream * valid.astype(BF16)
    d_yn = mm(d_mixed, w_o, ((1,), (1,)))
    d_gain = gain_gate * d_yn
    stats = jnp.stack([jnp.sum(gated * gated, axis=1), jnp.sum(gated * d_gain, axis=1)])
    stats = lax.psum(stats, "ctx") / inner
    scale_gate = lax.rsqrt(stats[0] + EPS)[:, None]
    normed_gate = (gated * scale_gate * gain_gate).astype(BF16)
    mixed = (valid * mm(normed_gate, w_o)).astype(BF16)
    grad_gain_gate = jnp.sum(d_yn * gated * scale_gate, axis=0)
    d_gated = scale_gate * d_gain - gated * (scale_gate**3 * stats[1][:, None])
    d_ssd = (d_gated * gate).astype(BF16)
    d_gate_raw = d_gated * mixed_ssd * silu_slope(gate_raw)

    d_x, d_b, d_c, d_step, d_lam, d_skip_lanes = scan_backward(
        values, rows_b, rows_c, lam_lanes, step_lanes, skip_wide, d_ssd, kept
    )
    d_step, d_lam = d_step[:, :heads], d_lam[:, :heads]
    grad_skip = jnp.sum(d_skip_lanes.reshape(heads, HEAD), axis=1)
    d_raw = valid * (d_step + d_lam * rate) * jax.nn.sigmoid(step_raw + bias_step)
    grad_bias_step = jnp.sum(d_raw, axis=0)
    grad_log = jnp.sum(d_lam * lam, axis=0)
    def conv_back(d_active, convolved, conv_in, weight):
        d_conv = d_active * silu_slope(convolved)
        padded_in = jnp.pad(conv_in, ((taps - 1, 0), (0, 0)))
        grad_taps = jnp.stack(
            [jnp.sum(d_conv * padded_in[k : k + tokens], axis=0) for k in range(taps)]
        )
        padded = jnp.pad(d_conv, ((0, taps - 1), (0, 0)))
        d_in = sum(weight[k] * padded[taps - 1 - k : taps - 1 - k + tokens] for k in range(taps))
        return d_in.astype(BF16), grad_taps, jnp.sum(d_conv, axis=0)

    d_in_x, grad_taps_x, grad_bias_x = conv_back(d_x, convolved_x, conv_in_x, taps_x)
    d_in_s, grad_taps_s, grad_bias_s = conv_back(
        jnp.concatenate([d_b, d_c], axis=1), convolved_s, conv_in_s, taps_s
    )
    d_raw_all = lax.dynamic_update_slice_in_dim(
        jnp.zeros((tokens, shared_width - both), BF16), d_raw.astype(BF16), me * heads, axis=1
    )
    d_in_s = jnp.concatenate([d_in_s, d_raw_all], axis=1)
    d_in_z = d_gate_raw.astype(BF16)
    d_normed = (
        mm(d_in_z, w_z, ((1,), (1,)))
        + mm(d_in_x, w_x, ((1,), (1,)))
        + mm(d_in_s, w_s, ((1,), (1,)))
    ).astype(BF16)
    small_grads = [grad_taps_x, grad_taps_s, grad_bias_x, grad_bias_s, grad_gain_gate]
    small_grads += [grad_bias_step, grad_log, grad_skip]
    sizes = [a.size for a in small_grads]
    small_count = -(-sum(sizes) // (8 * LANES)) * 8 * LANES
    flat = jnp.concatenate(
        [a.reshape(-1) for a in small_grads] + [jnp.zeros((small_count - sum(sizes),), F32)]
    )
    own = hidden.shape[1]
    g_z, g_x, g_s, g_o, layer_out, hidden_grad, small_sums = reduce_all(
        n_fsdp,
        n_ctx,
        normed.T,
        normed_gate.T,
        d_mixed,
        d_in_z,
        d_in_x,
        d_in_s,
        mixed.reshape(n_ctx, own, model),
        d_normed.reshape(n_ctx, own, model),
        flat.reshape(-1, LANES),
        hidden[0],
        cotangent[0],
        gain_norm[None, :],
    )
    grad_in_weight, grad_out_weight = assemble(g_z, g_x, g_s, g_o, both + heads_all)
    small_sums = small_sums.reshape(n_ctx, -1)
    ends = [sum(sizes[:i]) for i in range(len(sizes) + 1)]
    taps_x_sum, taps_s_sum, bias_x_sum, bias_s_sum, gate_sum, step_sum, log_sum, skip_sum = [
        small_sums[:, ends[i] : ends[i + 1]] for i in range(len(sizes))
    ]
    grad_gain_norm = jnp.sum(small_sums[:, small_count:], axis=0)
    by_tap = lambda a: jnp.moveaxis(a.reshape(n_ctx, taps, -1), 0, 1)

    def own_shard(vector):
        size = vector.shape[-1] // n_fsdp
        return lax.dynamic_slice_in_dim(vector, shard * size, size, axis=-1)

    return (
        layer_out[None],
        hidden_grad[None],
        own_shard(grad_gain_norm),
        grad_in_weight,
        own_shard(
            jnp.concatenate(
                [by_tap(taps_x_sum).reshape(taps, -1), jnp.sum(by_tap(taps_s_sum), axis=1)], axis=1
            )
        ),
        own_shard(jnp.concatenate([bias_x_sum.reshape(-1), jnp.sum(bias_s_sum, axis=0)])),
        own_shard(step_sum.reshape(-1)),
        own_shard(log_sum.reshape(-1)),
        own_shard(skip_sum.reshape(-1)),
        own_shard(gate_sum.reshape(-1)),
        grad_out_weight,
    )


def solution(mesh):
    tokens, rows, flat = P("fsdp", "ctx", None), P("fsdp", None), P("fsdp")
    taps = P(None, "fsdp")
    return jax.shard_map(
        on_device,
        mesh=mesh,
        in_specs=(tokens, tokens, flat, flat, rows, taps, flat, flat, flat, flat, flat, rows),
        out_specs=(tokens, tokens, flat, rows, taps, flat, flat, flat, flat, flat, rows),
        check_vma=False,
    )
```

```python
import functools

import jax
import jax.numpy as jnp
from jax import lax
from jax.experimental import pallas as pl
from jax.experimental.pallas import tpu as pltpu
from jax.sharding import PartitionSpec as P

HEAD = 64
STATE = 128
BLOCK = 256
LANES = 128
EPS = 1e-05
F32 = jnp.float32
BF16 = jnp.bfloat16


def mm(a, b, contract=((1,), (0,))):
    return lax.dot_general(a, b, (contract, ((), ())), preferred_element_type=F32)


def mm_exact(a, b, contract=((1,), (0,))):
    return lax.dot_general(
        a, b, (contract, ((), ())), precision=lax.Precision.HIGHEST, preferred_element_type=F32
    )


def iota2(shape, axis):
    return lax.broadcasted_iota(jnp.int32, shape, axis)


def levels(lam, step):
    tri = (iota2((BLOCK, BLOCK), 0) >= iota2((BLOCK, BLOCK), 1)).astype(F32)
    level = mm_exact(tri, lam)
    across = level.T
    last = level[BLOCK - 1 : BLOCK, :]
    weight = jnp.exp(level - last) * step
    return level, across, jnp.exp(-last), weight, jnp.exp(-level)


def pair_of(array, first, low_half):
    return jnp.where(low_half, array[:, first : first + 1], array[:, first + 1 : first + 2])


def spread(level, across, head):
    return jnp.exp(-jnp.abs(level[:, head : head + 1] - across[head : head + 1, :]))


def silu_and_slope(v):
    s = jax.nn.sigmoid(v)
    return v * s, s * (1.0 + v * (1.0 - s))


def own_lanes(array, me, heads, back=False):
    shift = me * heads if back else lax.rem(LANES - me * heads, LANES)
    return pltpu.roll(array, shift, 1)


def column_valid(length_ref, block):
    at = iota2((BLOCK, 1), 0) + block * BLOCK
    return (at < length_ref[0]).astype(F32)


def forward_kernel(
    heads,
    length_ref,
    px_ref,
    ps_ref,
    pz_ref,
    up_ref,
    w_o,
    taps_x_ref,
    taps_s_ref,
    gate_gain_ref,
    skip_ref,
    head_ref,
    x_ref,
    b_ref,
    c_ref,
    slope_x_ref,
    slope_s_ref,
    lam_ref,
    step_ref,
    chain_ref,
    kept_ref,
    y_ref,
    dyn_ref,
    stat_ref,
    state,
    before_x,
    before_s,
    v_o,
    load_sem,
):
    block = pl.program_id(0)
    load = pltpu.make_async_copy(w_o, v_o, load_sem)

    @pl.when(block == 0)
    def _():
        load.start()
        state[...] = jnp.zeros_like(state)
        before_x[...] = jnp.zeros_like(before_x)
        before_s[...] = jnp.zeros_like(before_s)

    valid = column_valid(length_ref, block)
    low_half = iota2((1, LANES), 1) < HEAD
    taps = taps_x_ref.shape[0] - 1

    def conv(current, before, weight):
        padded = jnp.concatenate([before, current], axis=0)
        total = weight[taps : taps + 1]
        for k in range(taps):
            first = 8 - (taps - 1) + k
            total = total + weight[k : k + 1] * padded[first : first + BLOCK]
        return silu_and_slope(total)

    shared = ps_ref[...].astype(F32)
    both = shared[:, : 2 * STATE]
    active, slope = conv(both, before_s[...], taps_s_ref[...])
    before_s[...] = both[BLOCK - 8 :]
    slope_s_ref[...] = slope.astype(BF16)
    rows_b, rows_c = active[:, :STATE].astype(BF16), active[:, STATE:].astype(BF16)
    b_ref[...] = rows_b
    c_ref[...] = rows_c
    raw = own_lanes(shared[:, 2 * STATE :], lax.axis_index("ctx"), heads)
    raw = raw + head_ref[0:1]
    own = iota2((1, LANES), 1) < heads
    step = jnp.where(own, valid * jax.nn.softplus(raw), 0.0)
    lam = step * head_ref[1:2]
    step_ref[...] = step
    lam_ref[...] = lam
    chain_ref[...] = jnp.where(own, valid * jax.nn.sigmoid(raw), 0.0)

    gram = mm(rows_c, rows_b, ((1,), (1,)))
    level, across, last, weight, fade = levels(lam, step)
    kept_ref[0] = state[...].astype(BF16)
    entering = mm(rows_c, state[...].astype(BF16))
    by_state = rows_b.T
    squares = jnp.zeros((BLOCK, LANES), F32)
    for first in range(0, heads, 2):
        lanes = slice(first * HEAD, (first + 2) * HEAD)
        current = px_ref[:, lanes].astype(F32)
        active, slope = conv(current, before_x[:, lanes], taps_x_ref[:, lanes])
        before_x[:, lanes] = current[BLOCK - 8 :]
        slope_x_ref[:, lanes] = slope.astype(BF16)
        x_low = active.astype(BF16)
        x_ref[:, lanes] = x_low
        x = x_low.astype(F32)
        scaled = x * pair_of(step, first, low_half)
        total = pair_of(fade, first, low_half) * entering[:, lanes] + skip_ref[:, lanes] * x
        for head, keep in ((first, low_half), (first + 1, jnp.logical_not(low_half))):
            mixing = (gram * spread(level, across, head)).astype(BF16)
            total += mm(mixing, jnp.where(keep, scaled, 0.0).astype(BF16))
        y_ref[:, lanes] = total
        update = mm(by_state, (x * pair_of(weight, first, low_half)).astype(BF16))
        state[:, lanes] = state[:, lanes] * pair_of(last, first, low_half) + update
        gated = total * jax.nn.silu(pz_ref[:, lanes].astype(F32))
        squares += gated * gated

    @pl.when(block == 0)
    def _():
        load.wait()

    d_yn = valid * mm(up_ref[0], v_o[...], ((1,), (1,)))
    dyn_ref[...] = d_yn
    gated = y_ref[...] * jax.nn.silu(pz_ref[...].astype(F32))
    terms = gate_gain_ref[...] * d_yn * gated
    square = jnp.sum(squares, axis=1, keepdims=True)
    along = jnp.sum(terms, axis=1, keepdims=True)
    lane = iota2((1, LANES), 1)
    both_sums = jnp.where(lane == 0, square, 0.0) + jnp.where(lane == 1, along, 0.0)
    stat_ref[...] = both_sums.T[0:8]


def scan_forward(length, px, ps, pz, upstream, w_o, taps_x, taps_s, gate_gain, skip, head):
    tokens, width = px.shape
    heads = width // HEAD
    count = tokens // BLOCK
    model = w_o.shape[1]
    by_block = lambda i: (i, 0)
    at_block = lambda size: pl.BlockSpec((BLOCK, size), by_block)
    whole = lambda a: pl.BlockSpec(a.shape, lambda i: (0, 0))
    low = lambda *shape: jax.ShapeDtypeStruct(shape, BF16)
    full = lambda *shape: jax.ShapeDtypeStruct(shape, F32)
    return pl.pallas_call(
        functools.partial(forward_kernel, heads),
        grid=(count,),
        in_specs=[
            pl.BlockSpec(memory_space=pltpu.SMEM),
            at_block(width),
            at_block(ps.shape[1]),
            at_block(width),
            pl.BlockSpec((1, BLOCK, model), lambda i: (i, 0, 0)),
            pl.BlockSpec(memory_space=pl.ANY),
            whole(taps_x),
            whole(taps_s),
            whole(gate_gain),
            whole(skip),
            whole(head),
        ],
        out_specs=[
            at_block(width),
            at_block(STATE),
            at_block(STATE),
            at_block(width),
            at_block(2 * STATE),
            at_block(LANES),
            at_block(LANES),
            at_block(LANES),
            pl.BlockSpec((1, STATE, width), lambda i: (i, 0, 0)),
            at_block(width),
            at_block(width),
            pl.BlockSpec((8, BLOCK), lambda i: (0, i)),
        ],
        out_shape=[
            low(tokens, width),
            low(tokens, STATE),
            low(tokens, STATE),
            low(tokens, width),
            low(tokens, 2 * STATE),
            full(tokens, LANES),
            full(tokens, LANES),
            full(tokens, LANES),
            low(count, STATE, width),
            full(tokens, width),
            full(tokens, width),
            full(8, tokens),
        ],
        scratch_shapes=[
            pltpu.VMEM((STATE, width), F32),
            pltpu.VMEM((8, width), F32),
            pltpu.VMEM((8, 2 * STATE), F32),
            pltpu.VMEM(w_o.shape, BF16),
            pltpu.SemaphoreType.DMA,
        ],
        compiler_params=pltpu.CompilerParams(vmem_limit_bytes=56 * 1024 * 1024),
        cost_estimate=pl.CostEstimate(
            flops=2 * tokens * width * (2 * BLOCK + 2 * STATE + model),
            bytes_accessed=tokens * width * 24,
            transcendentals=tokens * heads * BLOCK,
        ),
        name="scan_forward",
    )(length, px, ps, pz, upstream, w_o, taps_x, taps_s, gate_gain, skip, head)


def head_sums(product, chooser):
    high = product.astype(BF16)
    rest = (product - high.astype(F32)).astype(BF16)
    return mm(high, chooser) + mm(rest, chooser)


def backward_kernel(
    heads,
    channels,
    length_ref,
    px_ref,
    ps_ref,
    pz_ref,
    x_ref,
    b_ref,
    c_ref,
    slope_x_ref,
    slope_s_ref,
    lam_ref,
    step_ref,
    chain_ref,
    kept_ref,
    y_ref,
    dyn_ref,
    stat_ref,
    w_o,
    w_z,
    w_x,
    w_s,
    taps_x_ref,
    taps_s_ref,
    gate_gain_ref,
    skip_ref,
    head_ref,
    ynt_ref,
    mixed_ref,
    normed_ref,
    dz_ref,
    dx_ref,
    ds_ref,
    small_ref,
    back,
    mixed_grads,
    for_step,
    for_level,
    left,
    right,
    sums,
    after_x,
    after_s,
    v_y,
    v_o,
    v_z,
    v_x,
    v_s,
    load_sem,
):
    turn = pl.program_id(0)
    block = pl.num_programs(0) - 1 - turn
    loads = [
        pltpu.make_async_copy(source, target, load_sem.at[i])
        for i, (source, target) in enumerate(((w_o, v_o), (w_z, v_z), (w_x, v_x), (w_s, v_s)))
    ]

    @pl.when(turn == 0)
    def _():
        for copy in loads:
            copy.start()
        back[...] = jnp.zeros_like(back)
        small_ref[...] = jnp.zeros_like(small_ref)
        after_x[...] = jnp.zeros_like(after_x)
        after_s[...] = jnp.zeros_like(after_s)

    width = x_ref.shape[1]
    valid = column_valid(length_ref, block)
    columns = stat_ref[...].T
    scale = lax.rsqrt(columns[:, 0:1] / channels + EPS)
    slant = scale * scale * scale * columns[:, 1:2] / channels
    taps = taps_x_ref.shape[0] - 1

    rows_b, rows_c = b_ref[...], c_ref[...]
    step = step_ref[...]
    lam = lam_ref[...]
    gram = mm(rows_c, rows_b, ((1,), (1,)))
    gram_t = mm(rows_b, rows_c, ((1,), (1,)))
    level, across, last, weight, fade = levels(lam, step)
    out_decay = jnp.exp(level - level[BLOCK - 1 : BLOCK, :])
    step_across = step.T
    at_row, at_col = iota2((BLOCK, BLOCK), 0), iota2((BLOCK, BLOCK), 1)
    order = (at_row > at_col).astype(F32) - (at_row < at_col).astype(F32)
    low_half = iota2((1, LANES), 1) < HEAD
    lane = iota2((1, LANES), 1)
    by_state = rows_c.T
    kept = kept_ref[0]
    old_back = back[...].astype(BF16)
    entering = mm(rows_c, kept)
    leaving = mm(rows_b, old_back)
    at_last = jnp.sum(kept.astype(F32) * back[...], axis=0, keepdims=True)
    mixed_grads[...] = jnp.zeros_like(mixed_grads)
    left[...] = jnp.zeros_like(left)
    right[...] = jnp.zeros_like(right)
    sums[...] = jnp.zeros_like(sums)
    d_b = jnp.zeros((BLOCK, STATE), F32)
    d_c = jnp.zeros((BLOCK, STATE), F32)

    def conv_back(d_conv, after, current, weight):
        padded = jnp.concatenate([d_conv, after], axis=0)
        d_in = jnp.zeros_like(d_conv)
        grads = []
        for k in range(taps):
            moved = padded[taps - 1 - k : taps - 1 - k + BLOCK]
            d_in += weight[k : k + 1] * moved
            grads.append(jnp.sum(current * moved, axis=0, keepdims=True))
        grads.append(jnp.sum(d_conv, axis=0, keepdims=True))
        return d_in, jnp.concatenate(grads, axis=0)

    for first in range(0, heads, 2):
        lanes = slice(first * HEAD, (first + 2) * HEAD)
        x_low = x_ref[:, lanes]
        x = x_low.astype(F32)
        raw = pz_ref[:, lanes].astype(F32)
        gate, gate_slope = silu_and_slope(raw)
        mixed = y_ref[:, lanes]
        d_yn = dyn_ref[:, lanes]
        gain = gate_gain_ref[:, lanes]
        gated = mixed * gate
        v_y[:, lanes] = (valid * (gated * scale * gain)).astype(BF16)
        small_ref[taps + 1 : taps + 2, lanes] += jnp.sum(
            d_yn * (gated * scale), axis=0, keepdims=True
        )
        d_gated = scale * (gain * d_yn) - gated * slant
        dz_ref[:, lanes] = (d_gated * mixed * gate_slope).astype(BF16)
        grad_low = (d_gated * gate).astype(BF16)
        grad = grad_low.astype(F32)
        through = jnp.zeros((BLOCK, LANES), F32)
        for head, keep in ((first, low_half), (first + 1, jnp.logical_not(low_half))):
            decay = spread(level, across, head)
            grad_own = jnp.where(keep, grad, 0.0).astype(BF16)
            pairs = mm(grad_own, x_low, ((1,), (1,)))
            through += mm((gram_t * decay).astype(BF16), grad_own)
            scaled = decay * pairs * step_across[head : head + 1, :]
            mixed_grads[...] += scaled
            ordered = gram * scaled * order
            left[...] = jnp.where(
                lane == head, jnp.sum(ordered, axis=1, keepdims=True), left[...]
            )
            right[head : head + 1, :] = jnp.sum(ordered, axis=0, keepdims=True)
        weight_pair = pair_of(weight, first, low_half)
        step_pair = pair_of(step, first, low_half)
        fade_pair = pair_of(fade, first, low_half)
        out_pair = pair_of(out_decay, first, low_half)
        leave = leaving[:, lanes]
        d_x = step_pair * through + weight_pair * leave + skip_ref[:, lanes] * grad
        for_step[:, lanes] = x * (through + out_pair * leave)
        weighted = weight_pair * x
        faded = fade_pair * grad
        for_level[:, lanes] = weighted * leave - faded * entering[:, lanes]
        sums[0:1, lanes] = jnp.sum(weighted * leave, axis=0, keepdims=True)
        sums[2:3, lanes] = jnp.sum(x * grad, axis=0, keepdims=True)
        faded_low = faded.astype(BF16)
        d_b += mm(weighted.astype(BF16), old_back[:, lanes], ((1,), (1,)))
        d_c += mm(faded_low, kept[:, lanes], ((1,), (1,)))
        back[:, lanes] = back[:, lanes] * pair_of(last, first, low_half) + mm(by_state, faded_low)
        d_conv = d_x * slope_x_ref[:, lanes].astype(F32)
        d_in, grads = conv_back(
            d_conv, after_x[:, lanes], px_ref[:, lanes].astype(F32), taps_x_ref[:, lanes]
        )
        after_x[:, lanes] = d_conv[0:8]
        dx_ref[:, lanes] = d_in.astype(BF16)
        small_ref[0 : taps + 1, lanes] += grads

    all_pairs = mixed_grads[...]
    d_b = d_b + mm(all_pairs.T.astype(BF16), rows_c)
    d_c = d_c + mm(all_pairs.astype(BF16), rows_b)
    d_conv = jnp.concatenate([d_b, d_c], axis=1) * slope_s_ref[...].astype(F32)
    d_in, grads = conv_back(
        d_conv, after_s[...], ps_ref[:, : 2 * STATE].astype(F32), taps_s_ref[...]
    )
    after_s[...] = d_conv[0:8]
    ds_ref[:, : 2 * STATE] = d_in.astype(BF16)
    small_ref[0 : taps + 1, width:] += grads

    chooser = (iota2((width, LANES), 0) // HEAD == iota2((width, LANES), 1)).astype(BF16)
    d_step = head_sums(for_step[...], chooser)
    sums[1:2, :] = at_last
    total = head_sums(sums[...], chooser)
    d_level = head_sums(for_level[...], chooser) - left[...] + right[...].T
    final = -total[0:1, :] - last * total[1:2, :]
    d_level = d_level + jnp.where(iota2((BLOCK, 1), 0) == BLOCK - 1, final, 0.0)
    d_lam = mm_exact((at_row <= at_col).astype(F32), d_level)
    d_raw = (d_step + d_lam * head_ref[1:2]) * chain_ref[...]
    head_row = taps + 2
    small_ref[head_row : head_row + 1, 0:LANES] += jnp.sum(d_raw, axis=0, keepdims=True)
    small_ref[head_row : head_row + 1, LANES : 2 * LANES] += jnp.sum(
        d_lam * lam, axis=0, keepdims=True
    )
    small_ref[head_row : head_row + 1, 2 * LANES : 3 * LANES] += total[2:3, :]
    ds_ref[:, 2 * STATE :] = own_lanes(d_raw, lax.axis_index("ctx"), heads, True).astype(BF16)

    @pl.when(turn == 0)
    def _():
        for copy in loads:
            copy.wait()

    normed_gate = v_y[...]
    ynt_ref[...] = normed_gate.T
    mixed_ref[0] = mm(normed_gate, v_o[...]).astype(BF16)
    normed_ref[0] = (
        mm(dz_ref[...], v_z[...], ((1,), (1,)))
        + mm(dx_ref[...], v_x[...], ((1,), (1,)))
        + mm(ds_ref[...], v_s[...], ((1,), (1,)))
    ).astype(BF16)


def scan_backward(
    channels, length, px, ps, pz, kept_parts, stats, w_o, w_z, w_x, w_s, taps_x, taps_s, gate_gain, skip, head
):
    x, rows_b, rows_c, slope_x, slope_s, lam, step, chain, kept, y, d_yn = kept_parts
    tokens, width = px.shape
    heads = width // HEAD
    count = tokens // BLOCK
    model = w_o.shape[1]
    shared_width = ps.shape[1]
    taps = taps_x.shape[0] - 1
    by_block = lambda i: (count - 1 - i, 0)
    at_block = lambda size: pl.BlockSpec((BLOCK, size), by_block)
    whole = lambda a: pl.BlockSpec(a.shape, lambda i: (0, 0))
    any_space = pl.BlockSpec(memory_space=pl.ANY)
    low = lambda *shape: jax.ShapeDtypeStruct(shape, BF16)
    part = lambda a, b: pl.BlockSpec((1, a, b), lambda i: (count - 1 - i, 0, 0))
    small_shape = (8, width + 2 * STATE)
    return pl.pallas_call(
        functools.partial(backward_kernel, heads, channels),
        grid=(count,),
        in_specs=[
            pl.BlockSpec(memory_space=pltpu.SMEM),
            at_block(width),
            at_block(shared_width),
            at_block(width),
            at_block(width),
            at_block(STATE),
            at_block(STATE),
            at_block(width),
            at_block(2 * STATE),
            at_block(LANES),
            at_block(LANES),
            at_block(LANES),
            part(STATE, width),
            at_block(width),
            at_block(width),
            pl.BlockSpec((8, BLOCK), lambda i: (0, count - 1 - i)),
            any_space,
            any_space,
            any_space,
            any_space,
            whole(taps_x),
            whole(taps_s),
            whole(gate_gain),
            whole(skip),
            whole(head),
        ],
        out_specs=[
            pl.BlockSpec((width, BLOCK), lambda i: (0, count - 1 - i)),
            part(BLOCK, model),
            part(BLOCK, model),
            at_block(width),
            at_block(width),
            at_block(shared_width),
            pl.BlockSpec(small_shape, lambda i: (0, 0)),
        ],
        out_shape=[
            low(width, tokens),
            low(count, BLOCK, model),
            low(count, BLOCK, model),
            low(tokens, width),
            low(tokens, width),
            low(tokens, shared_width),
            jax.ShapeDtypeStruct(small_shape, F32),
        ],
        scratch_shapes=[
            pltpu.VMEM((STATE, width), F32),
            pltpu.VMEM((BLOCK, BLOCK), F32),
            pltpu.VMEM((BLOCK, width), F32),
            pltpu.VMEM((BLOCK, width), F32),
            pltpu.VMEM((BLOCK, LANES), F32),
            pltpu.VMEM((LANES, BLOCK), F32),
            pltpu.VMEM((8, width), F32),
            pltpu.VMEM((8, width), F32),
            pltpu.VMEM((8, 2 * STATE), F32),
            pltpu.VMEM((BLOCK, width), BF16),
            pltpu.VMEM(w_o.shape, BF16),
            pltpu.VMEM(w_z.shape, BF16),
            pltpu.VMEM(w_x.shape, BF16),
            pltpu.VMEM(w_s.shape, BF16),
            pltpu.SemaphoreType.DMA((4,)),
        ],
        compiler_params=pltpu.CompilerParams(vmem_limit_bytes=56 * 1024 * 1024),
        cost_estimate=pl.CostEstimate(
            flops=2 * tokens * width * (4 * BLOCK + 5 * STATE + 3 * model),
            bytes_accessed=tokens * width * 40,
            transcendentals=tokens * heads * BLOCK,
        ),
        name="scan_backward",
    )(
        length, px, ps, pz, x, rows_b, rows_c, slope_x, slope_s, lam, step, chain, kept, y, d_yn, stats, w_o, w_z, w_x, w_s, taps_x, taps_s, gate_gain, skip, head
    )


MESH = pl.DeviceIdType.MESH
SMALL_ROWS = 32


def ring_place(index, half):
    a, b = index // 2, index % 2
    return a + b * (2 * half - 1 - 2 * a)


def ring_index(place, half):
    b = place // half
    return 2 * (place + b * (2 * half - 1 - 2 * place)) + b


class Ring:
    def __init__(self, n):
        self.n, self.half = n, n // 2
        self.me, self.shard = lax.axis_index("ctx"), lax.axis_index("fsdp")
        self.place = ring_place(self.shard, self.half)

    def at(self, steps):
        return ring_index(lax.rem(self.place + steps + 2 * self.n, self.n), self.half)

    def neighbour(self, way):
        return (self.me, self.at(1 if way == 0 else -1))


def remote(source, target, send, recv, device):
    return pltpu.make_async_remote_copy(
        src_ref=source,
        dst_ref=target,
        send_sem=send,
        recv_sem=recv,
        device_id=device,
        device_id_type=MESH,
    )


def gather_kernel(
    n,
    n_ctx,
    hidden,
    cotangent,
    in_weight_t,
    small,
    out_weight,
    cotangent_all,
    w_x,
    w_s,
    w_z,
    w_o,
    small_out,
    proj_x,
    proj_s,
    proj_z,
    normed_t,
    v_hidden,
    v_normed,
    v_x,
    v_s,
    v_z,
    v_small,
    raw_x,
    raw_s,
    raw_z,
    out_x,
    out_s,
    out_z,
    out_t,
    v_gain,
    load_sem,
    local_sem,
    store_sem,
    ring_send,
    ring_recv,
    ctx_send,
    ctx_recv,
    piece_send,
    piece_recv,
):
    ring = Ring(n)
    me, shard = ring.me, ring.shard
    width, model = v_x.shape[1], v_x.shape[0]
    inner = width * n_ctx
    r = model // n
    shared = in_weight_t.shape[0] - 2 * inner
    row = me // 2
    other_core = (me + 1 - 2 * (me % 2), shard)
    other_row = (me + 2 - 4 * row, shard)
    piece = w_o.shape[1]
    sent_as = shard * n_ctx + me
    piece_to = (sent_as // n, sent_as % n)
    held_as = me * n + shard
    piece_from = (held_as % n_ctx, held_as // n_ctx)
    moves = sent_as != held_as

    barrier = pltpu.get_barrier_semaphore()
    for device in (other_core, other_row, ring.neighbour(0), ring.neighbour(1)):
        pl.semaphore_signal(barrier, inc=1, device_id=device, device_id_type=MESH)

    loads = [
        pltpu.make_async_copy(source, target, load_sem.at[i])
        for i, (source, target) in enumerate(
            (
                (in_weight_t.at[pl.ds(pl.multiple_of(inner + me * width, width), width)], raw_x),
                (in_weight_t.at[pl.ds(2 * inner, shared)], raw_s.at[pl.ds(0, shared)]),
                (small, v_small.at[shard]),
                (hidden, v_hidden.at[me]),
                (in_weight_t.at[pl.ds(pl.multiple_of(me * width, width), width)], raw_z),
            )
        )
    ]
    for copy in loads:
        copy.start()

    @pl.when(moves)
    def _():
        for device in (piece_to, piece_from):
            pl.semaphore_signal(barrier, inc=1, device_id=device, device_id_type=MESH)
        pl.semaphore_wait(barrier, 6)

    @pl.when(jnp.logical_not(moves))
    def _():
        pl.semaphore_wait(barrier, 4)

    half, quarter = width // 2, w_o.shape[2] // 4
    rows = r // 2
    both_rows = lambda index, way: pl.ds(pl.multiple_of((2 * index + way) * rows, 16), rows)
    x_part = lambda a, sub: lambda index, way: a.at[both_rows(index, way), pl.ds(sub * half, half)]
    s_part = lambda index, way: v_s.at[both_rows(index, way)]
    small_part = lambda index, way: v_small.at[index, pl.ds(way * SMALL_ROWS // 2, SMALL_ROWS // 2)]
    o_part = lambda sub: lambda index, way: w_o.at[
        index, :, pl.ds((2 * way + sub) * quarter, quarter)
    ]
    phases = (
        ((0, small_part), (1, s_part), (2, x_part(v_x, 0)), (3, x_part(v_x, 1))),
        ((4, x_part(v_z, 0)), (5, x_part(v_z, 1))),
        ((6, o_part(0)), (7, o_part(1))),
    )

    def hop(stream, way, step):
        number, part = stream
        place = part(ring.at(-step if way == 0 else step), way)
        return remote(
            place, place, ring_send.at[number, way], ring_recv.at[number, way, step],
            ring.neighbour(way),
        )

    def arrives(stream, way, step):
        number, part = stream
        landed = part(ring.at(-step - 1 if way == 0 else step + 1), way)
        return remote(
            landed, landed, ring_send.at[number, way], ring_recv.at[number, way, step],
            ring.neighbour(way),
        )

    def start_stream(stream):
        for way in (0, 1):
            hop(stream, way, 0).start()

    def to_row(i, a, whole):
        return remote(a, whole.at[me], ctx_send.at[i, 0], ctx_recv.at[i, 0], other_row)

    def to_core(i, a, whole):
        return remote(a, whole.at[me], ctx_send.at[i, 1], ctx_recv.at[i, 1], other_core)

    def pass_on(i, whole):
        beyond = whole.at[other_row[0]]
        return remote(beyond, beyond, ctx_send.at[i, 2], ctx_recv.at[i, 2], other_core)

    to_row(0, hidden, v_hidden).start()
    to_core(0, hidden, v_hidden).start()
    own_rows = pl.ds(pl.multiple_of(shard * r, 16), r)
    loads[2].wait()
    start_stream(phases[0][0])
    loads[0].wait()
    v_x[own_rows, :] = raw_x[...].T
    start_stream(phases[0][2])
    start_stream(phases[0][3])
    loads[1].wait()
    raw_s[shared:, :] = jnp.zeros((raw_s.shape[0] - shared, r), BF16)
    v_s[own_rows, :] = raw_s[...].T
    start_stream(phases[0][1])
    own_piece = out_weight.at[pl.ds(pl.multiple_of(me * piece, 16), piece)]
    send_piece = remote(own_piece, w_o.at[piece_to[1]], piece_send, piece_recv, piece_to)
    keep_piece = pltpu.make_async_copy(own_piece, w_o.at[shard], piece_send)

    def move_piece(wait):
        @pl.when(moves)
        def _():
            send_piece.wait() if wait else send_piece.start()

        @pl.when(jnp.logical_not(moves))
        def _():
            keep_piece.wait() if wait else keep_piece.start()

    keep_cotangent = pltpu.make_async_copy(cotangent, cotangent_all.at[me], local_sem)
    keep_cotangent.start()
    loads[3].wait()
    loads[4].wait()
    v_z[own_rows, :] = raw_z[...].T

    def run_phase(number, work, after):
        def body(step, carry):
            for stream in phases[number]:
                for way in (0, 1):
                    arrives(stream, way, step).wait_recv()
                    hop(stream, way, step).wait_send()
                    hop(stream, way, step + 1).start()
            if work is not None:

                @pl.when(step < n_ctx)
                def _():
                    work(step)

            return carry

        lax.fori_loop(0, n - 2, body, 0)
        after()
        for stream in phases[number]:
            for way in (0, 1):
                arrives(stream, way, n - 2).wait_recv()
                hop(stream, way, n - 2).wait_send()

    tokens = v_hidden.shape[1]

    def project_first(chunk):
        at = pl.ds(pl.multiple_of(chunk * tokens, tokens), tokens)
        resid = v_hidden[chunk].astype(F32)
        scale = lax.rsqrt(jnp.mean(resid * resid, axis=1, keepdims=True) + EPS)
        normed = (resid * scale * v_gain[...]).astype(BF16)
        v_normed[at, :] = normed
        out_x[at, :] = mm(normed, v_x[...]).astype(BF16)
        out_s[at, :] = mm(normed, v_s[...]).astype(BF16)

    def project_gate(chunk):
        at = pl.ds(pl.multiple_of(chunk * tokens, tokens), tokens)
        normed = v_normed[at, :]
        out_z[at, :] = mm(normed, v_z[...]).astype(BF16)
        out_t[chunk] = normed.T

    stores = [
        pltpu.make_async_copy(source, target, store_sem.at[i])
        for i, (source, target) in enumerate(
            (
                (v_x, w_x),
                (v_s, w_s),
                (v_small, small_out),
                (out_x, proj_x),
                (out_s, proj_s),
                (v_z, w_z),
                (out_z, proj_z),
                (out_t, normed_t),
            )
        )
    ]

    def after_first():
        for stream in phases[1]:
            start_stream(stream)
        to_row(0, hidden, v_hidden).wait_recv()
        pass_on(0, v_hidden).start()
        move_piece(False)
        to_row(1, cotangent, cotangent_all).start()
        to_core(1, cotangent, cotangent_all).start()
        to_row(0, hidden, v_hidden).wait_send()
        to_core(0, hidden, v_hidden).wait()
        pass_on(0, v_hidden).wait()

    def after_second():
        move_piece(True)
        for stream in phases[2]:
            start_stream(stream)
        to_row(1, cotangent, cotangent_all).wait_recv()
        pass_on(1, cotangent_all).start()

    def after_third():
        to_row(1, cotangent, cotangent_all).wait_send()
        to_core(1, cotangent, cotangent_all).wait()
        pass_on(1, cotangent_all).wait()
        keep_cotangent.wait()

    run_phase(0, None, after_first)
    for f in range(n):
        v_gain[:, f * r : (f + 1) * r] = v_small[f, 0:1, 0:r].astype(F32)
    for copy in stores[0:3]:
        copy.start()
    run_phase(1, project_first, after_second)
    for copy in stores[3:6]:
        copy.start()
    run_phase(2, project_gate, after_third)
    for copy in stores[6:]:
        copy.start()
    for copy in stores:
        copy.wait()


def gather_all(n, n_ctx, hidden, cotangent, in_weight_t, small, out_weight, shared_width):
    own, model = hidden.shape
    tokens = own * n_ctx
    width = out_weight.shape[0] * n // n_ctx
    rows = in_weight_t.shape[1]
    any_space = pl.BlockSpec(memory_space=pl.ANY)
    low = lambda *shape: jax.ShapeDtypeStruct(shape, BF16)
    v_low = lambda *shape: pltpu.VMEM(shape, BF16)
    dma = pltpu.SemaphoreType.DMA
    return pl.pallas_call(
        functools.partial(gather_kernel, n, n_ctx),
        in_specs=[any_space] * 5,
        out_specs=[any_space] * 10,
        out_shape=[
            low(n_ctx, own, model),
            low(model, width),
            low(model, shared_width),
            low(model, width),
            low(n, width // n, model),
            low(n, small.shape[0], small.shape[1]),
            low(tokens, width),
            low(tokens, shared_width),
            low(tokens, width),
            low(n_ctx, model, own),
        ],
        scratch_shapes=[
            v_low(n_ctx, own, model),
            v_low(tokens, model),
            v_low(model, width),
            v_low(model, shared_width),
            v_low(model, width),
            v_low(n, small.shape[0], small.shape[1]),
            v_low(width, rows),
            v_low(shared_width, rows),
            v_low(width, rows),
            v_low(tokens, width),
            v_low(tokens, shared_width),
            v_low(tokens, width),
            v_low(n_ctx, model, own),
            pltpu.VMEM((1, model), F32),
            dma((5,)),
            dma,
            dma((8,)),
            dma((8, 2)),
            dma((8, 2, n - 1)),
            dma((2, 3)),
            dma((2, 3)),
            dma,
            dma,
        ],
        compiler_params=pltpu.CompilerParams(
            collective_id=0, has_side_effects=True, vmem_limit_bytes=56 * 1024 * 1024
        ),
        name="gather_all",
    )(hidden, cotangent, in_weight_t, small, out_weight)


def reduce_kernel(
    n,
    n_ctx,
    normed_t,
    gate_t,
    upstream,
    d_z,
    d_x,
    d_s,
    mixed_parts,
    normed_parts,
    small,
    hidden,
    cotangent,
    gain,
    g_z,
    g_x,
    g_s,
    g_o,
    layer_out,
    hidden_grad,
    small_out,
    v_normed_t,
    v_gate_t,
    v_upstream,
    v_d_z,
    v_d_x,
    v_d_s,
    slot_o,
    slot_z,
    slot_x,
    slot_s,
    first_o,
    first_z,
    first_x,
    first_s,
    done_o,
    done_z,
    done_x,
    done_s,
    moved,
    mine,
    from_core,
    from_row,
    v_hidden,
    v_cotangent,
    v_gain,
    v_out,
    v_grad,
    small_all,
    small_ctx,
    load_sem,
    store_sem,
    ring_send,
    ring_recv,
    ctx_send,
    ctx_recv,
    own_sem,
    piece_send,
    piece_recv,
    part_send,
    part_recv,
    small_send,
    small_recv,
    small_ctx_send,
    small_ctx_recv,
):
    ring = Ring(n)
    me, shard = ring.me, ring.shard
    row = me // 2
    core = me % 2
    core_at = me + 1 - 2 * core
    row_at = me + 2 - 4 * row
    both_at = row_at + 1 - 2 * core
    other_core, other_row, other_both = (core_at, shard), (row_at, shard), (both_at, shard)
    held_as = me * n + shard
    piece_to = (held_as % n_ctx, held_as // n_ctx)
    sent_as = shard * n_ctx + me
    piece_from = (sent_as // n, sent_as % n)
    moves = sent_as != held_as

    barrier = pltpu.get_barrier_semaphore()

    def greet(device):
        pl.semaphore_signal(barrier, inc=1, device_id=device, device_id_type=MESH)

    def peer(offset):
        return (me, lax.rem(shard + offset, n))

    for device in (other_core, other_row, other_both):
        greet(device)
    lax.fori_loop(1, n, lambda j, carry: (greet(peer(j)), carry)[1], 0)

    own = hidden.shape[0]
    loads = [
        pltpu.make_async_copy(source, target, load_sem.at[i])
        for i, (source, target) in enumerate(
            (
                (gate_t, v_gate_t),
                *((upstream.at[c], v_upstream.at[pl.ds(c * own, own)]) for c in range(n_ctx)),
                (mixed_parts.at[row_at], mine.at[0, 1]),
                (normed_parts.at[row_at], mine.at[1, 1]),
                *((normed_t.at[c], v_normed_t.at[:, pl.ds(c * own, own)]) for c in range(n_ctx)),
                (d_z, v_d_z),
                (mixed_parts.at[me], mine.at[0, 0]),
                (normed_parts.at[me], mine.at[1, 0]),
                (hidden, v_hidden),
                (cotangent, v_cotangent),
                (gain, v_gain),
                (small, small_all.at[shard, pl.ds(0, small.shape[0])]),
                (d_x, v_d_x),
                (d_s, v_d_s),
            )
        )
    ]
    for copy in loads:
        copy.start()

    @pl.when(moves)
    def _():
        greet(piece_to)
        greet(piece_from)
        pl.semaphore_wait(barrier, n + 4)

    @pl.when(jnp.logical_not(moves))
    def _():
        pl.semaphore_wait(barrier, n + 2)

    def to_core(i, which):
        source = (mixed_parts, normed_parts)[i].at[(core_at, both_at)[which]]
        return remote(
            source, from_core.at[i, which], part_send.at[i, which], part_recv.at[i, which], other_core
        )

    def to_row(i):
        return remote(
            mine.at[i, 1], from_row.at[i], part_send.at[i, 2], part_recv.at[i, 2], other_row
        )

    for which in (1, 0):
        for i in (0, 1):
            to_core(i, which).start()

    rows, piece = v_normed_t.shape[0] // (2 * n), done_o.shape[0]
    half = v_d_z.shape[1] // 2
    quarter = v_upstream.shape[1] // 4

    def in_stream(number, right, first, size, slots, stage, done):
        def own(index, way):
            left = v_normed_t[pl.ds(pl.multiple_of((2 * index + way) * rows, 16), rows), :]
            return mm(left, right[:, first : first + size])

        return (
            number,
            own,
            lambda way, step: slots.at[step, way, :, pl.ds(first, size)],
            lambda way: stage.at[way, :, pl.ds(first, size)],
            lambda way: done.at[pl.ds(first, size), pl.ds(way * rows, rows)],
            True,
        )

    def out_stream(number, sub):
        def own(index, way):
            left = v_gate_t[pl.ds(pl.multiple_of(index * piece, 16), piece), :]
            at = (2 * way + sub) * quarter
            return mm(left, v_upstream[:, at : at + quarter])

        return (
            number,
            own,
            lambda way, step: slot_o.at[step, way, :, pl.ds(sub * quarter, quarter)],
            lambda way: first_o.at[way, :, pl.ds(sub * quarter, quarter)],
            lambda way: done_o.at[:, pl.ds((2 * way + sub) * quarter, quarter)],
            False,
        )

    phases = (
        (out_stream(0, 0), out_stream(1, 1)),
        (
            in_stream(2, v_d_z, 0, half, slot_z, first_z, done_z),
            in_stream(3, v_d_z, half, half, slot_z, first_z, done_z),
        ),
        (
            in_stream(4, v_d_s, 0, v_d_s.shape[1], slot_s, first_s, done_s),
            in_stream(5, v_d_x, 0, half, slot_x, first_x, done_x),
            in_stream(6, v_d_x, half, half, slot_x, first_x, done_x),
        ),
    )

    def hop(stream, way, step, source):
        number, own, slot, stage, done, turned = stream
        return remote(
            source,
            slot(way, step),
            ring_send.at[number, way],
            ring_recv.at[number, way, step],
            ring.neighbour(way),
        )

    def start_phase(number):
        for stream in phases[number]:
            for way in (0, 1):
                stage = stream[3](way)
                stage[...] = stream[1](ring.at(-1 if way == 0 else 1), way).astype(BF16)
                hop(stream, way, 0, stage).start()

    def arrived(stream, way, step):
        number, own, slot, stage, done, turned = stream
        partial = own(ring.at(-step - 2 if way == 0 else step + 2), way)
        hop(stream, way, step, stage(way)).wait()
        return slot(way, step)[...].astype(F32) + partial

    def run_phase(number, after):
        def body(step, carry):
            for stream in phases[number]:
                for way in (0, 1):
                    total = arrived(stream, way, step)
                    place = stream[2](way, step)
                    place[...] = total.astype(BF16)
                    hop(stream, way, step + 1, place).start()
            return carry

        lax.fori_loop(0, n - 2, body, 0)
        after()
        for stream in phases[number]:
            for way in (0, 1):
                done, total = stream[4](way), arrived(stream, way, n - 2)
                done[...] = (total.T if stream[5] else total).astype(BF16)

    ctx_pairs = ((moved, g_o), (done_z, g_z), (done_x, g_x), (done_s, g_s))

    def share(i, kind):
        source, whole = ctx_pairs[i]
        if kind == 2:
            source, at = whole.at[row_at], row_at
        else:
            at = me
        device = other_row if kind == 0 else other_core
        return remote(source, whole.at[at], ctx_send.at[i, kind], ctx_recv.at[i, kind], device)

    def keep(i):
        source, whole = ctx_pairs[i]
        return pltpu.make_async_copy(source, whole.at[me], own_sem.at[i])

    def start_share(i):
        share(i, 0).start()
        share(i, 1).start()
        keep(i).start()

    def pass_share(i):
        share(i, 0).wait_recv()
        share(i, 2).start()

    def close_share(i):
        share(i, 0).wait_send()
        share(i, 1).wait()
        share(i, 2).wait()
        keep(i).wait()

    send_piece = remote(done_o, moved, piece_send, piece_recv, piece_to)
    keep_piece = pltpu.make_async_copy(done_o, moved, piece_send)

    def move_piece(wait):
        @pl.when(moves)
        def _():
            send_piece.wait() if wait else send_piece.start()

        @pl.when(jnp.logical_not(moves))
        def _():
            keep_piece.wait() if wait else keep_piece.start()

    def small_to(offset):
        return remote(
            small_all.at[shard],
            small_all.at[shard],
            small_send.at[offset - 1],
            small_recv.at[offset - 1],
            peer(offset),
        )

    def small_share(i):
        return remote(
            small_ctx.at[me],
            small_ctx.at[me],
            small_ctx_send.at[i],
            small_ctx_recv.at[i],
            (other_core, other_row, other_both)[i],
        )

    store_layer = pltpu.make_async_copy(v_out, layer_out, store_sem.at[0])
    store_grad = pltpu.make_async_copy(v_grad, hidden_grad, store_sem.at[1])
    store_small = pltpu.make_async_copy(small_ctx, small_out, store_sem.at[2])

    def sum_rows():
        for i in (0, 1):
            to_core(i, 1).wait()
            mine[i, 1] = (mine[i, 1].astype(F32) + from_core[i, 1].astype(F32)).astype(BF16)
            to_row(i).start()

    def whole_sum(i):
        to_core(i, 0).wait()
        to_row(i).wait()
        return (
            mine[i, 0].astype(F32) + from_core[i, 0].astype(F32) + from_row[i].astype(F32)
        )

    def finish_tokens():
        resid = v_hidden[...].astype(F32)
        v_out[...] = (resid + whole_sum(0)).astype(BF16)
        store_layer.start()
        scale = lax.rsqrt(jnp.mean(resid * resid, axis=1, keepdims=True) + EPS)
        d_normed = whole_sum(1)
        f = v_gain[...] * d_normed
        slope = scale**3 * jnp.mean(resid * f, axis=1, keepdims=True)
        v_grad[...] = (v_cotangent[...].astype(F32) + scale * f - resid * slope).astype(BF16)
        store_grad.start()
        by_model = jnp.sum(d_normed * resid * scale, axis=0, keepdims=True)
        base, size = small.shape[0], d_z.shape[1]
        small_all[shard, base:, :] = jnp.zeros((small_all.shape[1] - base, small.shape[1]), F32)
        for j in range(by_model.shape[1] // size):
            small_all[shard, base + j : base + j + 1, 0:size] = by_model[
                :, j * size : (j + 1) * size
            ]
        lax.fori_loop(1, n, lambda j, carry: (small_to(j).start(), carry)[1], 0)

    def sum_small():
        lax.fori_loop(1, n, lambda j, carry: (small_to(j).wait(), carry)[1], 0)
        small_ctx[me] = jnp.sum(small_all[...], axis=0)
        for i in range(3):
            small_share(i).start()

    for copy in loads[: 1 + n_ctx]:
        copy.wait()
    start_phase(0)
    for copy in loads[1 + n_ctx :]:
        copy.wait()
    sum_rows()

    def after_first():
        start_phase(1)

    def after_second():
        start_phase(2)
        move_piece(True)
        start_share(0)
        finish_tokens()

    def after_third():
        pass_share(0)
        pass_share(1)
        sum_small()

    run_phase(0, after_first)
    move_piece(False)
    run_phase(1, after_second)
    start_share(1)
    run_phase(2, after_third)
    start_share(2)
    start_share(3)
    for i in range(3):
        small_share(i).wait()
    store_small.start()
    pass_share(2)
    pass_share(3)
    for i in range(4):
        close_share(i)
    store_layer.wait()
    store_grad.wait()
    store_small.wait()


def reduce_all(
    n, n_ctx, normed_t, gate_t, upstream, d_z, d_x, d_s, mixed_parts, normed_parts, small, hidden, cotangent, gain
):
    model, tokens = normed_t.shape[1], d_z.shape[0]
    width, shared_width = d_z.shape[1], d_s.shape[1]
    rows, piece, own = model // n, width // n, hidden.shape[0]
    small_rows, small_width = small.shape[0] + 8, small.shape[1]
    any_space = pl.BlockSpec(memory_space=pl.ANY)
    dma = pltpu.SemaphoreType.DMA
    low = lambda *shape: jax.ShapeDtypeStruct(shape, BF16)
    v_low = lambda *shape: pltpu.VMEM(shape, BF16)
    v_full = lambda *shape: pltpu.VMEM(shape, F32)
    return pl.pallas_call(
        functools.partial(reduce_kernel, n, n_ctx),
        in_specs=[any_space] * 12,
        out_specs=[any_space] * 7,
        out_shape=[
            low(n_ctx, width, rows),
            low(n_ctx, width, rows),
            low(n_ctx, shared_width, rows),
            low(n_ctx, piece, model),
            low(own, model),
            low(own, model),
            jax.ShapeDtypeStruct((n_ctx, small_rows, small_width), F32),
        ],
        scratch_shapes=[
            v_low(model, tokens),
            v_low(width, tokens),
            v_low(tokens, model),
            v_low(tokens, width),
            v_low(tokens, width),
            v_low(tokens, shared_width),
            v_low(n - 1, 2, piece, model // 2),
            v_low(n - 1, 2, rows // 2, width),
            v_low(n - 1, 2, rows // 2, width),
            v_low(n - 1, 2, rows // 2, shared_width),
            v_low(2, piece, model // 2),
            v_low(2, rows // 2, width),
            v_low(2, rows // 2, width),
            v_low(2, rows // 2, shared_width),
            v_low(piece, model),
            v_low(width, rows),
            v_low(width, rows),
            v_low(shared_width, rows),
            v_low(piece, model),
            v_low(2, 2, own, model),
            v_low(2, 2, own, model),
            v_low(2, own, model),
            v_low(own, model),
            v_low(own, model),
            v_full(1, model),
            v_low(own, model),
            v_low(own, model),
            v_full(n, small_rows, small_width),
            v_full(n_ctx, small_rows, small_width),
            dma((12 + 2 * n_ctx,)),
            dma((3,)),
            dma((7, 2)),
            dma((7, 2, n - 1)),
            dma((4, 3)),
            dma((4, 3)),
            dma((4,)),
            dma,
            dma,
            dma((2, 3)),
            dma((2, 3)),
            dma((n - 1,)),
            dma((n - 1,)),
            dma((3,)),
            dma((3,)),
        ],
        compiler_params=pltpu.CompilerParams(
            collective_id=1, has_side_effects=True, vmem_limit_bytes=58 * 1024 * 1024
        ),
        name="reduce_all",
    )(
        normed_t, gate_t, upstream, d_z, d_x, d_s, mixed_parts, normed_parts, small, hidden, cotangent, gain
    )


def assemble_kernel(n_ctx, z_ref, x_ref, s_ref, out_ref):
    place = pl.program_id(0)

    @pl.when(place < n_ctx)
    def _():
        out_ref[...] = z_ref[0].astype(F32)

    @pl.when(jnp.logical_and(place >= n_ctx, place < 2 * n_ctx))
    def _():
        out_ref[...] = x_ref[0].astype(F32)

    @pl.when(place == 2 * n_ctx)
    def _():
        total = s_ref[0].astype(F32)
        for c in range(1, n_ctx):
            total += s_ref[c].astype(F32)
        out_ref[0 : total.shape[0], :] = total


def assemble(g_z, g_x, g_s, columns):
    n_ctx, width, rows = g_z.shape
    return pl.pallas_call(
        functools.partial(assemble_kernel, n_ctx),
        grid=(2 * n_ctx + 1,),
        in_specs=[
            pl.BlockSpec((1, width, rows), lambda i: (jnp.minimum(i, n_ctx - 1), 0, 0)),
            pl.BlockSpec((1, width, rows), lambda i: (jnp.clip(i - n_ctx, 0, n_ctx - 1), 0, 0)),
            pl.BlockSpec(g_s.shape, lambda i: (0, 0, 0)),
        ],
        out_specs=pl.BlockSpec((width, rows), lambda i: (i, 0)),
        out_shape=jax.ShapeDtypeStruct((columns, rows), F32),
        compiler_params=pltpu.CompilerParams(vmem_limit_bytes=58 * 1024 * 1024),
        name="assemble",
    )(g_z, g_x, g_s)


def on_device(
    hidden,
    cotangent,
    seq_lens,
    norm_gain,
    in_weight,
    conv_weight,
    conv_bias,
    dt_bias,
    a_log,
    d_skip,
    gate_gain,
    out_weight,
):
    n_ctx, n_fsdp = lax.axis_size("ctx"), lax.axis_size("fsdp")
    me, shard = lax.axis_index("ctx"), lax.axis_index("fsdp")
    taps = conv_weight.shape[0]
    heads_all = dt_bias.shape[0] * n_fsdp
    inner = out_weight.shape[0] * n_fsdp
    heads, width = heads_all // n_ctx, inner // n_ctx
    model = hidden.shape[2]
    both = 2 * STATE
    shared_width = -(-(both + heads_all) // LANES) * LANES

    per_head = jnp.concatenate([dt_bias, a_log, d_skip])
    lines = [norm_gain[None], conv_weight, conv_bias[None], gate_gain[None], per_head[None]]
    longest = -(-max(a.shape[1] for a in lines) // LANES) * LANES
    small = jnp.concatenate([jnp.pad(a, ((0, 0), (0, longest - a.shape[1]))) for a in lines])
    small = jnp.pad(small, ((0, SMALL_ROWS - small.shape[0]), (0, 0)))
    upstream, w_x, w_s, w_z, w_o, small_all, proj_x, proj_s, proj_z, normed_t = gather_all(
        n_fsdp, n_ctx, hidden[0], cotangent[0], in_weight.T, small, out_weight, shared_width
    )
    w_o = w_o.reshape(-1, model)

    def line(first, count, size):
        rows = small_all[:, first : first + count, :size]
        return jnp.moveaxis(rows, 0, 1).reshape(count, -1).astype(F32)

    def own(lines, size):
        return lax.dynamic_slice_in_dim(lines, me * size, size, axis=1)

    gain_norm = line(0, 1, norm_gain.shape[0])
    conv_lines = line(1, taps + 1, conv_bias.shape[0])
    taps_x, taps_s = own(conv_lines[:, :inner], width), conv_lines[:, inner:]
    gain_gate = own(line(taps + 2, 1, gate_gain.shape[0]), width)
    each = small_all[:, taps + 3, : per_head.shape[0]].reshape(n_fsdp, 3, -1)
    each = own(jnp.moveaxis(each, 0, 1).reshape(3, -1).astype(F32), heads)
    head = jnp.pad(jnp.stack([each[0], jnp.exp(each[1])]), ((0, 0), (0, LANES - heads)))
    skip = jnp.repeat(each[2], HEAD)[None]

    *kept_parts, stats = scan_forward(
        seq_lens, proj_x, proj_s, proj_z, upstream, w_o, taps_x, taps_s, gain_gate, skip, head
    )
    stats = lax.psum(stats, "ctx")
    gate_t, mixed_parts, normed_parts, d_z, d_x, d_s, small_grads = scan_backward(
        inner, seq_lens, proj_x, proj_s, proj_z, kept_parts, stats, w_o, w_z, w_x, w_s, taps_x, taps_s, gain_gate, skip, head
    )
    g_z, g_x, g_s, g_o, layer_out, hidden_grad, sums = reduce_all(
        n_fsdp, n_ctx, normed_t, gate_t, upstream, d_z, d_x, d_s, mixed_parts, normed_parts, small_grads, hidden[0], cotangent[0], gain_norm
    )
    grad_in_weight = assemble(g_z, g_x, g_s, 2 * inner + both + heads_all).T
    grad_out_weight = g_o.reshape(-1, model).astype(F32)

    def shard_of(lines):
        size = lines.shape[1] // n_fsdp
        return lax.dynamic_slice_in_dim(lines, shard * size, size, axis=1)

    in_order = lambda a: jnp.moveaxis(a, 0, 1).reshape(a.shape[1], -1)
    conv_sums = shard_of(
        jnp.concatenate(
            [
                in_order(sums[:, : taps + 1, :width]),
                jnp.sum(sums[:, : taps + 1, width:], axis=0),
            ],
            axis=1,
        )
    )
    gate_sums = shard_of(in_order(sums[:, taps + 1 : taps + 2, :width]))
    head_sums_all = sums[:, taps + 2, : 3 * LANES].reshape(n_ctx, 3, LANES)[:, :, :heads]
    head_grads = shard_of(in_order(head_sums_all))
    norm_sums = jnp.sum(sums[:, 8 : 8 + model // width, :width], axis=0).reshape(1, -1)
    return (
        layer_out[None],
        hidden_grad[None],
        shard_of(norm_sums)[0],
        grad_in_weight,
        conv_sums[:taps],
        conv_sums[taps],
        head_grads[0],
        head_grads[1],
        head_grads[2],
        gate_sums[0],
        grad_out_weight,
    )


def solution(mesh):
    tokens, rows, flat = P("fsdp", "ctx", None), P("fsdp", None), P("fsdp")
    taps = P(None, "fsdp")
    return jax.shard_map(
        on_device,
        mesh=mesh,
        in_specs=(tokens, tokens, flat, flat, rows, taps, flat, flat, flat, flat, flat, rows),
        out_specs=(tokens, tokens, flat, rows, taps, flat, flat, flat, flat, flat, rows),
        check_vma=False,
    )
```

```python
import functools

import jax
import jax.numpy as jnp
from jax import lax
from jax.experimental import pallas as pl
from jax.experimental.pallas import tpu as pltpu
from jax.sharding import PartitionSpec as P

HEAD = 64
STATE = 128
BLOCK = 256
LANES = 128
EPS = 1e-05
F32 = jnp.float32
BF16 = jnp.bfloat16


def mm(a, b, contract=((1,), (0,))):
    return lax.dot_general(a, b, (contract, ((), ())), preferred_element_type=F32)


def mm_exact(a, b, contract=((1,), (0,))):
    return lax.dot_general(
        a, b, (contract, ((), ())), precision=lax.Precision.HIGHEST, preferred_element_type=F32
    )


def iota2(shape, axis):
    return lax.broadcasted_iota(jnp.int32, shape, axis)


def levels(lam, step):
    tri = (iota2((BLOCK, BLOCK), 0) >= iota2((BLOCK, BLOCK), 1)).astype(F32)
    level = mm_exact(tri, lam)
    across = level.T
    last = level[BLOCK - 1 : BLOCK, :]
    weight = jnp.exp(level - last) * step
    return level, across, jnp.exp(-last), weight, jnp.exp(-level)


def pair_of(array, first, low_half):
    return jnp.where(low_half, array[:, first : first + 1], array[:, first + 1 : first + 2])


def spread(level, across, head):
    return jnp.exp(-jnp.abs(level[:, head : head + 1] - across[head : head + 1, :]))


def silu_and_slope(v):
    s = jax.nn.sigmoid(v)
    return v * s, s * (1.0 + v * (1.0 - s))


def chosen_heads(me, heads, unit, n_ctx, turned=False):
    here, there = iota2((LANES, LANES), 1), iota2((LANES, LANES), 0)
    if turned:
        here, there = there, here
    head = (here // unit * n_ctx + me) * unit + here % unit
    return jnp.where(jnp.logical_and(there == head, here < heads), 1.0, 0.0).astype(BF16)


def column_valid(length_ref, block):
    at = iota2((BLOCK, 1), 0) + block * BLOCK
    return (at < length_ref[0]).astype(F32)


def forward_kernel(
    heads,
    unit,
    n_ctx,
    length_ref,
    px_ref,
    ps_ref,
    pz_ref,
    up_ref,
    w_o,
    taps_x_ref,
    taps_s_ref,
    gate_gain_ref,
    skip_ref,
    head_ref,
    x_ref,
    b_ref,
    c_ref,
    slope_x_ref,
    slope_s_ref,
    lam_ref,
    step_ref,
    chain_ref,
    kept_ref,
    y_ref,
    dyn_ref,
    stat_ref,
    state,
    before_x,
    before_s,
    v_o,
    load_sem,
):
    block = pl.program_id(0)
    load = pltpu.make_async_copy(w_o, v_o, load_sem)

    @pl.when(block == 0)
    def _():
        load.start()
        state[...] = jnp.zeros_like(state)
        before_x[...] = jnp.zeros_like(before_x)
        before_s[...] = jnp.zeros_like(before_s)

    valid = column_valid(length_ref, block)
    low_half = iota2((1, LANES), 1) < HEAD
    taps = taps_x_ref.shape[0] - 1

    def conv(current, before, weight):
        padded = jnp.concatenate([before, current], axis=0)
        total = weight[taps : taps + 1]
        for k in range(taps):
            first = 8 - (taps - 1) + k
            total = total + weight[k : k + 1] * padded[first : first + BLOCK]
        return silu_and_slope(total)

    shared = ps_ref[...].astype(F32)
    both = shared[:, : 2 * STATE]
    active, slope = conv(both, before_s[...], taps_s_ref[...])
    before_s[...] = both[BLOCK - 8 :]
    slope_s_ref[...] = slope.astype(BF16)
    rows_b, rows_c = active[:, :STATE].astype(BF16), active[:, STATE:].astype(BF16)
    b_ref[...] = rows_b
    c_ref[...] = rows_c
    chosen = chosen_heads(lax.axis_index("ctx"), heads, unit, n_ctx)
    raw = mm(ps_ref[:, 2 * STATE :], chosen)
    raw = raw + head_ref[0:1]
    own = iota2((1, LANES), 1) < heads
    step = jnp.where(own, valid * jax.nn.softplus(raw), 0.0)
    lam = step * head_ref[1:2]
    step_ref[...] = step
    lam_ref[...] = lam
    chain_ref[...] = jnp.where(own, valid * jax.nn.sigmoid(raw), 0.0)

    gram = mm(rows_c, rows_b, ((1,), (1,)))
    level, across, last, weight, fade = levels(lam, step)
    kept_ref[0] = state[...].astype(BF16)
    entering = mm(rows_c, state[...].astype(BF16))
    by_state = rows_b.T
    squares = jnp.zeros((BLOCK, LANES), F32)
    for first in range(0, heads, 2):
        lanes = slice(first * HEAD, (first + 2) * HEAD)
        current = px_ref[:, lanes].astype(F32)
        active, slope = conv(current, before_x[:, lanes], taps_x_ref[:, lanes])
        before_x[:, lanes] = current[BLOCK - 8 :]
        slope_x_ref[:, lanes] = slope.astype(BF16)
        x_low = active.astype(BF16)
        x_ref[:, lanes] = x_low
        x = x_low.astype(F32)
        scaled = x * pair_of(step, first, low_half)
        total = pair_of(fade, first, low_half) * entering[:, lanes] + skip_ref[:, lanes] * x
        for head, keep in ((first, low_half), (first + 1, jnp.logical_not(low_half))):
            mixing = (gram * spread(level, across, head)).astype(BF16)
            total += mm(mixing, jnp.where(keep, scaled, 0.0).astype(BF16))
        y_ref[:, lanes] = total
        update = mm(by_state, (x * pair_of(weight, first, low_half)).astype(BF16))
        state[:, lanes] = state[:, lanes] * pair_of(last, first, low_half) + update
        gated = total * jax.nn.silu(pz_ref[:, lanes].astype(F32))
        squares += gated * gated

    @pl.when(block == 0)
    def _():
        load.wait()

    d_yn = valid * mm(up_ref[0], v_o[...], ((1,), (1,)))
    dyn_ref[...] = d_yn
    gated = y_ref[...] * jax.nn.silu(pz_ref[...].astype(F32))
    terms = gate_gain_ref[...] * d_yn * gated
    square = jnp.sum(squares, axis=1, keepdims=True)
    along = jnp.sum(terms, axis=1, keepdims=True)
    lane = iota2((1, LANES), 1)
    both_sums = jnp.where(lane == 0, square, 0.0) + jnp.where(lane == 1, along, 0.0)
    stat_ref[...] = both_sums.T[0:8]


def scan_forward(unit, n_ctx, length, px, ps, pz, upstream, w_o, taps_x, taps_s, gate_gain, skip, head):
    tokens, width = px.shape
    heads = width // HEAD
    count = tokens // BLOCK
    model = w_o.shape[1]
    by_block = lambda i: (i, 0)
    at_block = lambda size: pl.BlockSpec((BLOCK, size), by_block)
    whole = lambda a: pl.BlockSpec(a.shape, lambda i: (0, 0))
    low = lambda *shape: jax.ShapeDtypeStruct(shape, BF16)
    full = lambda *shape: jax.ShapeDtypeStruct(shape, F32)
    return pl.pallas_call(
        functools.partial(forward_kernel, heads, unit, n_ctx),
        grid=(count,),
        in_specs=[
            pl.BlockSpec(memory_space=pltpu.SMEM),
            at_block(width),
            at_block(ps.shape[1]),
            at_block(width),
            pl.BlockSpec((1, BLOCK, model), lambda i: (i, 0, 0)),
            pl.BlockSpec(memory_space=pl.ANY),
            whole(taps_x),
            whole(taps_s),
            whole(gate_gain),
            whole(skip),
            whole(head),
        ],
        out_specs=[
            at_block(width),
            at_block(STATE),
            at_block(STATE),
            at_block(width),
            at_block(2 * STATE),
            at_block(LANES),
            at_block(LANES),
            at_block(LANES),
            pl.BlockSpec((1, STATE, width), lambda i: (i, 0, 0)),
            at_block(width),
            at_block(width),
            pl.BlockSpec((8, BLOCK), lambda i: (0, i)),
        ],
        out_shape=[
            low(tokens, width),
            low(tokens, STATE),
            low(tokens, STATE),
            low(tokens, width),
            low(tokens, 2 * STATE),
            full(tokens, LANES),
            full(tokens, LANES),
            full(tokens, LANES),
            low(count, STATE, width),
            full(tokens, width),
            full(tokens, width),
            full(8, tokens),
        ],
        scratch_shapes=[
            pltpu.VMEM((STATE, width), F32),
            pltpu.VMEM((8, width), F32),
            pltpu.VMEM((8, 2 * STATE), F32),
            pltpu.VMEM(w_o.shape, BF16),
            pltpu.SemaphoreType.DMA,
        ],
        compiler_params=pltpu.CompilerParams(vmem_limit_bytes=56 * 1024 * 1024),
        cost_estimate=pl.CostEstimate(
            flops=2 * tokens * width * (2 * BLOCK + 2 * STATE + model),
            bytes_accessed=tokens * width * 24,
            transcendentals=tokens * heads * BLOCK,
        ),
        name="scan_forward",
    )(length, px, ps, pz, upstream, w_o, taps_x, taps_s, gate_gain, skip, head)


def head_sums(product, chooser):
    high = product.astype(BF16)
    rest = (product - high.astype(F32)).astype(BF16)
    return mm(high, chooser) + mm(rest, chooser)


def backward_kernel(
    heads,
    unit,
    n_ctx,
    channels,
    length_ref,
    px_ref,
    ps_ref,
    pz_ref,
    x_ref,
    b_ref,
    c_ref,
    slope_x_ref,
    slope_s_ref,
    lam_ref,
    step_ref,
    chain_ref,
    kept_ref,
    y_ref,
    dyn_ref,
    stat_ref,
    w_o,
    w_z,
    w_x,
    w_s,
    taps_x_ref,
    taps_s_ref,
    gate_gain_ref,
    skip_ref,
    head_ref,
    ynt_ref,
    mixed_ref,
    normed_ref,
    dz_ref,
    dx_ref,
    ds_ref,
    small_ref,
    back,
    mixed_grads,
    for_step,
    for_level,
    left,
    right,
    sums,
    after_x,
    after_s,
    v_y,
    v_o,
    v_z,
    v_x,
    v_s,
    load_sem,
):
    turn = pl.program_id(0)
    block = pl.num_programs(0) - 1 - turn
    loads = [
        pltpu.make_async_copy(source, target, load_sem.at[i])
        for i, (source, target) in enumerate(((w_o, v_o), (w_z, v_z), (w_x, v_x), (w_s, v_s)))
    ]

    @pl.when(turn == 0)
    def _():
        for copy in loads:
            copy.start()
        back[...] = jnp.zeros_like(back)
        small_ref[...] = jnp.zeros_like(small_ref)
        after_x[...] = jnp.zeros_like(after_x)
        after_s[...] = jnp.zeros_like(after_s)

    width = x_ref.shape[1]
    valid = column_valid(length_ref, block)
    columns = stat_ref[...].T
    scale = lax.rsqrt(columns[:, 0:1] / channels + EPS)
    slant = scale * scale * scale * columns[:, 1:2] / channels
    taps = taps_x_ref.shape[0] - 1

    rows_b, rows_c = b_ref[...], c_ref[...]
    step = step_ref[...]
    lam = lam_ref[...]
    gram = mm(rows_c, rows_b, ((1,), (1,)))
    gram_t = mm(rows_b, rows_c, ((1,), (1,)))
    level, across, last, weight, fade = levels(lam, step)
    out_decay = jnp.exp(level - level[BLOCK - 1 : BLOCK, :])
    step_across = step.T
    at_row, at_col = iota2((BLOCK, BLOCK), 0), iota2((BLOCK, BLOCK), 1)
    order = (at_row > at_col).astype(F32) - (at_row < at_col).astype(F32)
    low_half = iota2((1, LANES), 1) < HEAD
    lane = iota2((1, LANES), 1)
    by_state = rows_c.T
    kept = kept_ref[0]
    old_back = back[...].astype(BF16)
    entering = mm(rows_c, kept)
    leaving = mm(rows_b, old_back)
    at_last = jnp.sum(kept.astype(F32) * back[...], axis=0, keepdims=True)
    mixed_grads[...] = jnp.zeros_like(mixed_grads)
    left[...] = jnp.zeros_like(left)
    right[...] = jnp.zeros_like(right)
    sums[...] = jnp.zeros_like(sums)
    d_b = jnp.zeros((BLOCK, STATE), F32)
    d_c = jnp.zeros((BLOCK, STATE), F32)

    def conv_back(d_conv, after, current, weight):
        padded = jnp.concatenate([d_conv, after], axis=0)
        d_in = jnp.zeros_like(d_conv)
        grads = []
        for k in range(taps):
            moved = padded[taps - 1 - k : taps - 1 - k + BLOCK]
            d_in += weight[k : k + 1] * moved
            grads.append(jnp.sum(current * moved, axis=0, keepdims=True))
        grads.append(jnp.sum(d_conv, axis=0, keepdims=True))
        return d_in, jnp.concatenate(grads, axis=0)

    for first in range(0, heads, 2):
        lanes = slice(first * HEAD, (first + 2) * HEAD)
        x_low = x_ref[:, lanes]
        x = x_low.astype(F32)
        raw = pz_ref[:, lanes].astype(F32)
        gate, gate_slope = silu_and_slope(raw)
        mixed = y_ref[:, lanes]
        d_yn = dyn_ref[:, lanes]
        gain = gate_gain_ref[:, lanes]
        gated = mixed * gate
        v_y[:, lanes] = (valid * (gated * scale * gain)).astype(BF16)
        small_ref[taps + 1 : taps + 2, lanes] += jnp.sum(
            d_yn * (gated * scale), axis=0, keepdims=True
        )
        d_gated = scale * (gain * d_yn) - gated * slant
        dz_ref[:, lanes] = (d_gated * mixed * gate_slope).astype(BF16)
        grad_low = (d_gated * gate).astype(BF16)
        grad = grad_low.astype(F32)
        through = jnp.zeros((BLOCK, LANES), F32)
        for head, keep in ((first, low_half), (first + 1, jnp.logical_not(low_half))):
            decay = spread(level, across, head)
            grad_own = jnp.where(keep, grad, 0.0).astype(BF16)
            pairs = mm(grad_own, x_low, ((1,), (1,)))
            through += mm((gram_t * decay).astype(BF16), grad_own)
            scaled = decay * pairs * step_across[head : head + 1, :]
            mixed_grads[...] += scaled
            ordered = gram * scaled * order
            left[...] = jnp.where(
                lane == head, jnp.sum(ordered, axis=1, keepdims=True), left[...]
            )
            right[head : head + 1, :] = jnp.sum(ordered, axis=0, keepdims=True)
        weight_pair = pair_of(weight, first, low_half)
        step_pair = pair_of(step, first, low_half)
        fade_pair = pair_of(fade, first, low_half)
        out_pair = pair_of(out_decay, first, low_half)
        leave = leaving[:, lanes]
        d_x = step_pair * through + weight_pair * leave + skip_ref[:, lanes] * grad
        for_step[:, lanes] = x * (through + out_pair * leave)
        weighted = weight_pair * x
        faded = fade_pair * grad
        for_level[:, lanes] = weighted * leave - faded * entering[:, lanes]
        sums[0:1, lanes] = jnp.sum(weighted * leave, axis=0, keepdims=True)
        sums[2:3, lanes] = jnp.sum(x * grad, axis=0, keepdims=True)
        faded_low = faded.astype(BF16)
        d_b += mm(weighted.astype(BF16), old_back[:, lanes], ((1,), (1,)))
        d_c += mm(faded_low, kept[:, lanes], ((1,), (1,)))
        back[:, lanes] = back[:, lanes] * pair_of(last, first, low_half) + mm(by_state, faded_low)
        d_conv = d_x * slope_x_ref[:, lanes].astype(F32)
        d_in, grads = conv_back(
            d_conv, after_x[:, lanes], px_ref[:, lanes].astype(F32), taps_x_ref[:, lanes]
        )
        after_x[:, lanes] = d_conv[0:8]
        dx_ref[:, lanes] = d_in.astype(BF16)
        small_ref[0 : taps + 1, lanes] += grads

    all_pairs = mixed_grads[...]
    d_b = d_b + mm(all_pairs.T.astype(BF16), rows_c)
    d_c = d_c + mm(all_pairs.astype(BF16), rows_b)
    d_conv = jnp.concatenate([d_b, d_c], axis=1) * slope_s_ref[...].astype(F32)
    d_in, grads = conv_back(
        d_conv, after_s[...], ps_ref[:, : 2 * STATE].astype(F32), taps_s_ref[...]
    )
    after_s[...] = d_conv[0:8]
    ds_ref[:, : 2 * STATE] = d_in.astype(BF16)
    small_ref[0 : taps + 1, width:] += grads

    chooser = (iota2((width, LANES), 0) // HEAD == iota2((width, LANES), 1)).astype(BF16)
    d_step = head_sums(for_step[...], chooser)
    sums[1:2, :] = at_last
    total = head_sums(sums[...], chooser)
    d_level = head_sums(for_level[...], chooser) - left[...] + right[...].T
    final = -total[0:1, :] - last * total[1:2, :]
    d_level = d_level + jnp.where(iota2((BLOCK, 1), 0) == BLOCK - 1, final, 0.0)
    d_lam = mm_exact((at_row <= at_col).astype(F32), d_level)
    d_raw = (d_step + d_lam * head_ref[1:2]) * chain_ref[...]
    head_row = taps + 2
    small_ref[head_row : head_row + 1, 0:LANES] += jnp.sum(d_raw, axis=0, keepdims=True)
    small_ref[head_row : head_row + 1, LANES : 2 * LANES] += jnp.sum(
        d_lam * lam, axis=0, keepdims=True
    )
    small_ref[head_row : head_row + 1, 2 * LANES : 3 * LANES] += total[2:3, :]
    chosen = chosen_heads(lax.axis_index("ctx"), heads, unit, n_ctx, True)
    ds_ref[:, 2 * STATE :] = mm(d_raw.astype(BF16), chosen).astype(BF16)

    @pl.when(turn == 0)
    def _():
        for copy in loads:
            copy.wait()

    normed_gate = v_y[...]
    ynt_ref[...] = normed_gate.T
    mixed_ref[0] = mm(normed_gate, v_o[...]).astype(BF16)
    normed_ref[0] = (
        mm(dz_ref[...], v_z[...], ((1,), (1,)))
        + mm(dx_ref[...], v_x[...], ((1,), (1,)))
        + mm(ds_ref[...], v_s[...], ((1,), (1,)))
    ).astype(BF16)


def scan_backward(
    unit, n_ctx, channels, length, px, ps, pz, kept_parts, stats, w_o, w_z, w_x, w_s, taps_x, taps_s, gate_gain, skip, head
):
    x, rows_b, rows_c, slope_x, slope_s, lam, step, chain, kept, y, d_yn = kept_parts
    tokens, width = px.shape
    heads = width // HEAD
    count = tokens // BLOCK
    model = w_o.shape[1]
    shared_width = ps.shape[1]
    taps = taps_x.shape[0] - 1
    by_block = lambda i: (count - 1 - i, 0)
    at_block = lambda size: pl.BlockSpec((BLOCK, size), by_block)
    whole = lambda a: pl.BlockSpec(a.shape, lambda i: (0, 0))
    any_space = pl.BlockSpec(memory_space=pl.ANY)
    low = lambda *shape: jax.ShapeDtypeStruct(shape, BF16)
    part = lambda a, b: pl.BlockSpec((1, a, b), lambda i: (count - 1 - i, 0, 0))
    small_shape = (8, width + 2 * STATE)
    return pl.pallas_call(
        functools.partial(backward_kernel, heads, unit, n_ctx, channels),
        grid=(count,),
        in_specs=[
            pl.BlockSpec(memory_space=pltpu.SMEM),
            at_block(width),
            at_block(shared_width),
            at_block(width),
            at_block(width),
            at_block(STATE),
            at_block(STATE),
            at_block(width),
            at_block(2 * STATE),
            at_block(LANES),
            at_block(LANES),
            at_block(LANES),
            part(STATE, width),
            at_block(width),
            at_block(width),
            pl.BlockSpec((8, BLOCK), lambda i: (0, count - 1 - i)),
            any_space,
            any_space,
            any_space,
            any_space,
            whole(taps_x),
            whole(taps_s),
            whole(gate_gain),
            whole(skip),
            whole(head),
        ],
        out_specs=[
            pl.BlockSpec((width, BLOCK), lambda i: (0, count - 1 - i)),
            part(BLOCK, model),
            part(BLOCK, model),
            at_block(width),
            at_block(width),
            at_block(shared_width),
            pl.BlockSpec(small_shape, lambda i: (0, 0)),
        ],
        out_shape=[
            low(width, tokens),
            low(count, BLOCK, model),
            low(count, BLOCK, model),
            low(tokens, width),
            low(tokens, width),
            low(tokens, shared_width),
            jax.ShapeDtypeStruct(small_shape, F32),
        ],
        scratch_shapes=[
            pltpu.VMEM((STATE, width), F32),
            pltpu.VMEM((BLOCK, BLOCK), F32),
            pltpu.VMEM((BLOCK, width), F32),
            pltpu.VMEM((BLOCK, width), F32),
            pltpu.VMEM((BLOCK, LANES), F32),
            pltpu.VMEM((LANES, BLOCK), F32),
            pltpu.VMEM((8, width), F32),
            pltpu.VMEM((8, width), F32),
            pltpu.VMEM((8, 2 * STATE), F32),
            pltpu.VMEM((BLOCK, width), BF16),
            pltpu.VMEM(w_o.shape, BF16),
            pltpu.VMEM(w_z.shape, BF16),
            pltpu.VMEM(w_x.shape, BF16),
            pltpu.VMEM(w_s.shape, BF16),
            pltpu.SemaphoreType.DMA((4,)),
        ],
        compiler_params=pltpu.CompilerParams(vmem_limit_bytes=56 * 1024 * 1024),
        cost_estimate=pl.CostEstimate(
            flops=2 * tokens * width * (4 * BLOCK + 5 * STATE + 3 * model),
            bytes_accessed=tokens * width * 40,
            transcendentals=tokens * heads * BLOCK,
        ),
        name="scan_backward",
    )(
        length, px, ps, pz, x, rows_b, rows_c, slope_x, slope_s, lam, step, chain, kept, y, d_yn, stats, w_o, w_z, w_x, w_s, taps_x, taps_s, gate_gain, skip, head
    )


MESH = pl.DeviceIdType.MESH
SMALL_ROWS = 32


def ring_place(index, half):
    a, b = index // 2, index % 2
    return a + b * (2 * half - 1 - 2 * a)


def ring_index(place, half):
    b = place // half
    return 2 * (place + b * (2 * half - 1 - 2 * place)) + b


class Ring:
    def __init__(self, n):
        self.n, self.half = n, n // 2
        self.me, self.shard = lax.axis_index("ctx"), lax.axis_index("fsdp")
        self.place = ring_place(self.shard, self.half)

    def at(self, steps):
        return ring_index(lax.rem(self.place + steps + 2 * self.n, self.n), self.half)

    def neighbour(self, way):
        return (self.me, self.at(1 if way == 0 else -1))


def remote(source, target, send, recv, device):
    return pltpu.make_async_remote_copy(
        src_ref=source,
        dst_ref=target,
        send_sem=send,
        recv_sem=recv,
        device_id=device,
        device_id_type=MESH,
    )


def gather_kernel(
    n,
    n_ctx,
    unit,
    direct,
    hidden,
    cotangent,
    in_weight_t,
    small,
    out_weight,
    cotangent_all,
    w_x,
    w_s,
    w_z,
    w_o,
    small_out,
    proj_x,
    proj_s,
    proj_z,
    normed_t,
    v_hidden,
    v_normed,
    v_x,
    v_s,
    v_z,
    v_small,
    raw_x,
    raw_s,
    raw_z,
    out_x,
    out_s,
    out_z,
    out_t,
    v_gain,
    load_sem,
    column_sem,
    local_sem,
    store_sem,
    ring_send,
    ring_recv,
    ctx_send,
    ctx_recv,
    piece_send,
    piece_recv,
):
    ring = Ring(n)
    me, shard = ring.me, ring.shard
    width, model = v_x.shape[1], v_x.shape[0]
    inner = width * n_ctx
    r = model // n
    shared = in_weight_t.shape[0] - 2 * inner
    row = me // 2
    other_core = (me + 1 - 2 * (me % 2), shard)
    other_row = (me + 2 - 4 * row, shard)
    piece = w_o.shape[1]
    piece_peer = (shard % n_ctx, shard // n_ctx * n_ctx + me)
    moves = shard % n_ctx != me

    barrier = pltpu.get_barrier_semaphore()
    for device in (other_core, other_row, ring.neighbour(0), ring.neighbour(1)):
        pl.semaphore_signal(barrier, inc=1, device_id=device, device_id_type=MESH)

    part = unit * HEAD

    def load_columns(base, target, sems):
        return [
            pltpu.make_async_copy(
                in_weight_t.at[pl.ds(pl.multiple_of(base + (a * n_ctx + me) * part, 16), part)],
                target.at[pl.ds(a * part, part)],
                sems.at[a],
            )
            for a in range(width // part)
        ]

    loads = [
        load_columns(inner, raw_x, column_sem.at[0]),
        [
            pltpu.make_async_copy(
                in_weight_t.at[pl.ds(2 * inner, shared)], raw_s.at[pl.ds(0, shared)], load_sem.at[0]
            )
        ],
        [pltpu.make_async_copy(small, v_small.at[shard], load_sem.at[1])],
        [pltpu.make_async_copy(hidden, v_hidden.at[me], load_sem.at[2])],
        load_columns(0, raw_z, column_sem.at[1]),
    ]
    for copies in loads:
        for copy in copies:
            copy.start()

    def loaded(i):
        for copy in loads[i]:
            copy.wait()

    if direct:
        pl.semaphore_wait(barrier, 4)
    else:

        @pl.when(moves)
        def _():
            pl.semaphore_signal(barrier, inc=1, device_id=piece_peer, device_id_type=MESH)
            pl.semaphore_wait(barrier, 5)

        @pl.when(jnp.logical_not(moves))
        def _():
            pl.semaphore_wait(barrier, 4)

    half, quarter = width // 2, w_o.shape[2] // 4
    rows = r // 2
    both_rows = lambda index, way: pl.ds(pl.multiple_of((2 * index + way) * rows, 16), rows)
    x_part = lambda a, sub: lambda index, way: a.at[both_rows(index, way), pl.ds(sub * half, half)]
    s_part = lambda index, way: v_s.at[both_rows(index, way)]
    small_part = lambda index, way: v_small.at[index, pl.ds(way * SMALL_ROWS // 2, SMALL_ROWS // 2)]
    o_part = lambda sub: lambda index, way: w_o.at[
        index, :, pl.ds((2 * way + sub) * quarter, quarter)
    ]
    phases = (
        ((0, small_part), (1, s_part), (2, x_part(v_x, 0)), (3, x_part(v_x, 1))),
        ((4, x_part(v_z, 0)), (5, x_part(v_z, 1))),
        ((6, o_part(0)), (7, o_part(1))),
    )

    def hop(stream, way, step):
        number, part = stream
        place = part(ring.at(-step if way == 0 else step), way)
        return remote(
            place, place, ring_send.at[number, way], ring_recv.at[number, way, step],
            ring.neighbour(way),
        )

    def arrives(stream, way, step):
        number, part = stream
        landed = part(ring.at(-step - 1 if way == 0 else step + 1), way)
        return remote(
            landed, landed, ring_send.at[number, way], ring_recv.at[number, way, step],
            ring.neighbour(way),
        )

    def start_stream(stream):
        for way in (0, 1):
            hop(stream, way, 0).start()

    def to_row(i, a, whole):
        return remote(a, whole.at[me], ctx_send.at[i, 0], ctx_recv.at[i, 0], other_row)

    def to_core(i, a, whole):
        return remote(a, whole.at[me], ctx_send.at[i, 1], ctx_recv.at[i, 1], other_core)

    def pass_on(i, whole):
        beyond = whole.at[other_row[0]]
        return remote(beyond, beyond, ctx_send.at[i, 2], ctx_recv.at[i, 2], other_core)

    to_row(0, hidden, v_hidden).start()
    to_core(0, hidden, v_hidden).start()
    own_rows = pl.ds(pl.multiple_of(shard * r, 16), r)
    loaded(2)
    start_stream(phases[0][0])
    loaded(0)
    v_x[own_rows, :] = raw_x[...].T
    start_stream(phases[0][2])
    start_stream(phases[0][3])
    loaded(1)
    raw_s[shared:, :] = jnp.zeros((raw_s.shape[0] - shared, r), BF16)
    v_s[own_rows, :] = raw_s[...].T
    start_stream(phases[0][1])
    own_piece = out_weight.at[pl.ds(pl.multiple_of(me * piece, 16), piece)]
    keep_piece = pltpu.make_async_copy(own_piece, w_o.at[shard], piece_send)

    def move_piece(wait):
        if direct:
            keep_piece.wait() if wait else keep_piece.start()
            return
        send_piece = remote(own_piece, w_o.at[piece_peer[1]], piece_send, piece_recv, piece_peer)

        @pl.when(moves)
        def _():
            send_piece.wait() if wait else send_piece.start()

        @pl.when(jnp.logical_not(moves))
        def _():
            keep_piece.wait() if wait else keep_piece.start()

    keep_cotangent = pltpu.make_async_copy(cotangent, cotangent_all.at[me], local_sem)
    keep_cotangent.start()
    loaded(3)
    loaded(4)
    v_z[own_rows, :] = raw_z[...].T

    def run_phase(number, work, after):
        def body(step, carry):
            for stream in phases[number]:
                for way in (0, 1):
                    arrives(stream, way, step).wait_recv()
                    hop(stream, way, step).wait_send()
                    hop(stream, way, step + 1).start()
            if work is not None:

                @pl.when(step < n_ctx)
                def _():
                    work(step)

            return carry

        lax.fori_loop(0, n - 2, body, 0)
        after()
        for stream in phases[number]:
            for way in (0, 1):
                arrives(stream, way, n - 2).wait_recv()
                hop(stream, way, n - 2).wait_send()

    tokens = v_hidden.shape[1]

    def project_first(chunk):
        at = pl.ds(pl.multiple_of(chunk * tokens, tokens), tokens)
        resid = v_hidden[chunk].astype(F32)
        scale = lax.rsqrt(jnp.mean(resid * resid, axis=1, keepdims=True) + EPS)
        normed = (resid * scale * v_gain[...]).astype(BF16)
        v_normed[at, :] = normed
        out_x[at, :] = mm(normed, v_x[...]).astype(BF16)
        out_s[at, :] = mm(normed, v_s[...]).astype(BF16)

    def project_gate(chunk):
        at = pl.ds(pl.multiple_of(chunk * tokens, tokens), tokens)
        normed = v_normed[at, :]
        out_z[at, :] = mm(normed, v_z[...]).astype(BF16)
        out_t[chunk] = normed.T

    stores = [
        pltpu.make_async_copy(source, target, store_sem.at[i])
        for i, (source, target) in enumerate(
            (
                (v_x, w_x),
                (v_s, w_s),
                (v_small, small_out),
                (out_x, proj_x),
                (out_s, proj_s),
                (v_z, w_z),
                (out_z, proj_z),
                (out_t, normed_t),
            )
        )
    ]

    def after_first():
        for stream in phases[1]:
            start_stream(stream)
        to_row(0, hidden, v_hidden).wait_recv()
        pass_on(0, v_hidden).start()
        move_piece(False)
        to_row(1, cotangent, cotangent_all).start()
        to_core(1, cotangent, cotangent_all).start()
        to_row(0, hidden, v_hidden).wait_send()
        to_core(0, hidden, v_hidden).wait()
        pass_on(0, v_hidden).wait()

    def after_second():
        move_piece(True)
        for stream in phases[2]:
            start_stream(stream)
        to_row(1, cotangent, cotangent_all).wait_recv()
        pass_on(1, cotangent_all).start()

    def after_third():
        to_row(1, cotangent, cotangent_all).wait_send()
        to_core(1, cotangent, cotangent_all).wait()
        pass_on(1, cotangent_all).wait()
        keep_cotangent.wait()

    run_phase(0, None, after_first)
    for f in range(n):
        v_gain[:, f * r : (f + 1) * r] = v_small[f, 0:1, 0:r].astype(F32)
    for copy in stores[0:3]:
        copy.start()
    run_phase(1, project_first, after_second)
    for copy in stores[3:6]:
        copy.start()
    run_phase(2, project_gate, after_third)
    for copy in stores[6:]:
        copy.start()
    for copy in stores:
        copy.wait()


def gather_all(n, n_ctx, unit, direct, hidden, cotangent, in_weight_t, small, out_weight, shared_width):
    own, model = hidden.shape
    tokens = own * n_ctx
    width = out_weight.shape[0] * n // n_ctx
    rows = in_weight_t.shape[1]
    any_space = pl.BlockSpec(memory_space=pl.ANY)
    low = lambda *shape: jax.ShapeDtypeStruct(shape, BF16)
    v_low = lambda *shape: pltpu.VMEM(shape, BF16)
    dma = pltpu.SemaphoreType.DMA
    return pl.pallas_call(
        functools.partial(gather_kernel, n, n_ctx, unit, direct),
        in_specs=[any_space] * 5,
        out_specs=[any_space] * 10,
        out_shape=[
            low(n_ctx, own, model),
            low(model, width),
            low(model, shared_width),
            low(model, width),
            low(n, width // n, model),
            low(n, small.shape[0], small.shape[1]),
            low(tokens, width),
            low(tokens, shared_width),
            low(tokens, width),
            low(n_ctx, model, own),
        ],
        scratch_shapes=[
            v_low(n_ctx, own, model),
            v_low(tokens, model),
            v_low(model, width),
            v_low(model, shared_width),
            v_low(model, width),
            v_low(n, small.shape[0], small.shape[1]),
            v_low(width, rows),
            v_low(shared_width, rows),
            v_low(width, rows),
            v_low(tokens, width),
            v_low(tokens, shared_width),
            v_low(tokens, width),
            v_low(n_ctx, model, own),
            pltpu.VMEM((1, model), F32),
            dma((3,)),
            dma((2, width // (unit * HEAD))),
            dma,
            dma((8,)),
            dma((8, 2)),
            dma((8, 2, n - 1)),
            dma((2, 3)),
            dma((2, 3)),
            dma,
            dma,
        ],
        compiler_params=pltpu.CompilerParams(
            collective_id=0, has_side_effects=True, vmem_limit_bytes=56 * 1024 * 1024
        ),
        name="gather_all",
    )(hidden, cotangent, in_weight_t, small, out_weight)


def reduce_kernel(
    n,
    n_ctx,
    direct,
    normed_t,
    gate_t,
    upstream,
    d_z,
    d_x,
    d_s,
    mixed_parts,
    normed_parts,
    small,
    hidden,
    cotangent,
    gain,
    g_z,
    g_x,
    g_s,
    g_o,
    layer_out,
    hidden_grad,
    small_out,
    v_normed_t,
    v_gate_t,
    v_upstream,
    v_d_z,
    v_d_x,
    v_d_s,
    slot_o,
    slot_z,
    slot_x,
    slot_s,
    first_o,
    first_z,
    first_x,
    first_s,
    done_o,
    done_z,
    done_x,
    done_s,
    moved,
    mine,
    from_core,
    from_row,
    v_hidden,
    v_cotangent,
    v_gain,
    v_out,
    v_grad,
    small_all,
    small_ctx,
    load_sem,
    store_sem,
    ring_send,
    ring_recv,
    ctx_send,
    ctx_recv,
    own_sem,
    piece_send,
    piece_recv,
    part_send,
    part_recv,
    small_send,
    small_recv,
    small_ctx_send,
    small_ctx_recv,
):
    ring = Ring(n)
    me, shard = ring.me, ring.shard
    row = me // 2
    core = me % 2
    core_at = me + 1 - 2 * core
    row_at = me + 2 - 4 * row
    both_at = row_at + 1 - 2 * core
    other_core, other_row, other_both = (core_at, shard), (row_at, shard), (both_at, shard)
    piece_peer = (shard % n_ctx, shard // n_ctx * n_ctx + me)
    moves = shard % n_ctx != me

    barrier = pltpu.get_barrier_semaphore()

    def greet(device):
        pl.semaphore_signal(barrier, inc=1, device_id=device, device_id_type=MESH)

    def peer(offset):
        return (me, lax.rem(shard + offset, n))

    for device in (other_core, other_row, other_both):
        greet(device)
    lax.fori_loop(1, n, lambda j, carry: (greet(peer(j)), carry)[1], 0)

    own = hidden.shape[0]
    loads = [
        pltpu.make_async_copy(source, target, load_sem.at[i])
        for i, (source, target) in enumerate(
            (
                (gate_t, v_gate_t),
                *((upstream.at[c], v_upstream.at[pl.ds(c * own, own)]) for c in range(n_ctx)),
                (mixed_parts.at[row_at], mine.at[0, 1]),
                (normed_parts.at[row_at], mine.at[1, 1]),
                *((normed_t.at[c], v_normed_t.at[:, pl.ds(c * own, own)]) for c in range(n_ctx)),
                (d_z, v_d_z),
                (mixed_parts.at[me], mine.at[0, 0]),
                (normed_parts.at[me], mine.at[1, 0]),
                (hidden, v_hidden),
                (cotangent, v_cotangent),
                (gain, v_gain),
                (small, small_all.at[shard, pl.ds(0, small.shape[0])]),
                (d_x, v_d_x),
                (d_s, v_d_s),
            )
        )
    ]
    for copy in loads:
        copy.start()

    if direct:
        pl.semaphore_wait(barrier, n + 2)
    else:

        @pl.when(moves)
        def _():
            greet(piece_peer)
            pl.semaphore_wait(barrier, n + 3)

        @pl.when(jnp.logical_not(moves))
        def _():
            pl.semaphore_wait(barrier, n + 2)

    def to_core(i, which):
        source = (mixed_parts, normed_parts)[i].at[(core_at, both_at)[which]]
        return remote(
            source, from_core.at[i, which], part_send.at[i, which], part_recv.at[i, which], other_core
        )

    def to_row(i):
        return remote(
            mine.at[i, 1], from_row.at[i], part_send.at[i, 2], part_recv.at[i, 2], other_row
        )

    for which in (1, 0):
        for i in (0, 1):
            to_core(i, which).start()

    rows, piece = v_normed_t.shape[0] // (2 * n), done_o.shape[0]
    half = v_d_z.shape[1] // 2
    quarter = v_upstream.shape[1] // 4

    def in_stream(number, right, first, size, slots, stage, done):
        def own(index, way):
            left = v_normed_t[pl.ds(pl.multiple_of((2 * index + way) * rows, 16), rows), :]
            return mm(left, right[:, first : first + size])

        return (
            number,
            own,
            lambda way, step: slots.at[step, way, :, pl.ds(first, size)],
            lambda way: stage.at[way, :, pl.ds(first, size)],
            lambda way: done.at[pl.ds(first, size), pl.ds(way * rows, rows)],
            True,
        )

    def out_stream(number, sub):
        def own(index, way):
            left = v_gate_t[pl.ds(pl.multiple_of(index * piece, 16), piece), :]
            at = (2 * way + sub) * quarter
            return mm(left, v_upstream[:, at : at + quarter])

        return (
            number,
            own,
            lambda way, step: slot_o.at[step, way, :, pl.ds(sub * quarter, quarter)],
            lambda way: first_o.at[way, :, pl.ds(sub * quarter, quarter)],
            lambda way: done_o.at[:, pl.ds((2 * way + sub) * quarter, quarter)],
            False,
        )

    phases = (
        (out_stream(0, 0), out_stream(1, 1)),
        (
            in_stream(2, v_d_z, 0, half, slot_z, first_z, done_z),
            in_stream(3, v_d_z, half, half, slot_z, first_z, done_z),
        ),
        (
            in_stream(4, v_d_s, 0, v_d_s.shape[1], slot_s, first_s, done_s),
            in_stream(5, v_d_x, 0, half, slot_x, first_x, done_x),
            in_stream(6, v_d_x, half, half, slot_x, first_x, done_x),
        ),
    )

    def hop(stream, way, step, source):
        number, own, slot, stage, done, turned = stream
        return remote(
            source,
            slot(way, step),
            ring_send.at[number, way],
            ring_recv.at[number, way, step],
            ring.neighbour(way),
        )

    def start_phase(number):
        for stream in phases[number]:
            for way in (0, 1):
                stage = stream[3](way)
                stage[...] = stream[1](ring.at(-1 if way == 0 else 1), way).astype(BF16)
                hop(stream, way, 0, stage).start()

    def arrived(stream, way, step):
        number, own, slot, stage, done, turned = stream
        partial = own(ring.at(-step - 2 if way == 0 else step + 2), way)
        hop(stream, way, step, stage(way)).wait()
        return slot(way, step)[...].astype(F32) + partial

    def run_phase(number, after):
        def body(step, carry):
            for stream in phases[number]:
                for way in (0, 1):
                    total = arrived(stream, way, step)
                    place = stream[2](way, step)
                    place[...] = total.astype(BF16)
                    hop(stream, way, step + 1, place).start()
            return carry

        lax.fori_loop(0, n - 2, body, 0)
        after()
        for stream in phases[number]:
            for way in (0, 1):
                done, total = stream[4](way), arrived(stream, way, n - 2)
                done[...] = (total.T if stream[5] else total).astype(BF16)

    ctx_pairs = ((done_o if direct else moved, g_o), (done_z, g_z), (done_x, g_x), (done_s, g_s))

    def share(i, kind):
        source, whole = ctx_pairs[i]
        if kind == 2:
            source, at = whole.at[row_at], row_at
        else:
            at = me
        device = other_row if kind == 0 else other_core
        return remote(source, whole.at[at], ctx_send.at[i, kind], ctx_recv.at[i, kind], device)

    def keep(i):
        source, whole = ctx_pairs[i]
        return pltpu.make_async_copy(source, whole.at[me], own_sem.at[i])

    def start_share(i):
        share(i, 0).start()
        share(i, 1).start()
        keep(i).start()

    def pass_share(i):
        share(i, 0).wait_recv()
        share(i, 2).start()

    def close_share(i):
        share(i, 0).wait_send()
        share(i, 1).wait()
        share(i, 2).wait()
        keep(i).wait()

    def move_piece(wait):
        if direct:
            return
        keep_piece = pltpu.make_async_copy(done_o, moved, piece_send)
        send_piece = remote(done_o, moved, piece_send, piece_recv, piece_peer)

        @pl.when(moves)
        def _():
            send_piece.wait() if wait else send_piece.start()

        @pl.when(jnp.logical_not(moves))
        def _():
            keep_piece.wait() if wait else keep_piece.start()

    def small_to(offset):
        return remote(
            small_all.at[shard],
            small_all.at[shard],
            small_send.at[offset - 1],
            small_recv.at[offset - 1],
            peer(offset),
        )

    def small_share(i):
        return remote(
            small_ctx.at[me],
            small_ctx.at[me],
            small_ctx_send.at[i],
            small_ctx_recv.at[i],
            (other_core, other_row, other_both)[i],
        )

    store_layer = pltpu.make_async_copy(v_out, layer_out, store_sem.at[0])
    store_grad = pltpu.make_async_copy(v_grad, hidden_grad, store_sem.at[1])
    store_small = pltpu.make_async_copy(small_ctx, small_out, store_sem.at[2])

    def sum_rows():
        for i in (0, 1):
            to_core(i, 1).wait()
            mine[i, 1] = (mine[i, 1].astype(F32) + from_core[i, 1].astype(F32)).astype(BF16)
            to_row(i).start()

    def whole_sum(i):
        to_core(i, 0).wait()
        to_row(i).wait()
        return (
            mine[i, 0].astype(F32) + from_core[i, 0].astype(F32) + from_row[i].astype(F32)
        )

    def finish_tokens():
        resid = v_hidden[...].astype(F32)
        v_out[...] = (resid + whole_sum(0)).astype(BF16)
        store_layer.start()
        scale = lax.rsqrt(jnp.mean(resid * resid, axis=1, keepdims=True) + EPS)
        d_normed = whole_sum(1)
        f = v_gain[...] * d_normed
        slope = scale**3 * jnp.mean(resid * f, axis=1, keepdims=True)
        v_grad[...] = (v_cotangent[...].astype(F32) + scale * f - resid * slope).astype(BF16)
        store_grad.start()
        by_model = jnp.sum(d_normed * resid * scale, axis=0, keepdims=True)
        base, size = small.shape[0], d_z.shape[1]
        small_all[shard, base:, :] = jnp.zeros((small_all.shape[1] - base, small.shape[1]), F32)
        for j in range(by_model.shape[1] // size):
            small_all[shard, base + j : base + j + 1, 0:size] = by_model[
                :, j * size : (j + 1) * size
            ]
        lax.fori_loop(1, n, lambda j, carry: (small_to(j).start(), carry)[1], 0)

    def sum_small():
        lax.fori_loop(1, n, lambda j, carry: (small_to(j).wait(), carry)[1], 0)
        small_ctx[me] = jnp.sum(small_all[...], axis=0)
        for i in range(3):
            small_share(i).start()

    for copy in loads[: 1 + n_ctx]:
        copy.wait()
    start_phase(0)
    for copy in loads[1 + n_ctx :]:
        copy.wait()
    sum_rows()

    def after_first():
        start_phase(1)

    def after_second():
        start_phase(2)
        move_piece(True)
        start_share(0)
        finish_tokens()

    def after_third():
        pass_share(0)
        pass_share(1)
        sum_small()

    run_phase(0, after_first)
    move_piece(False)
    run_phase(1, after_second)
    start_share(1)
    run_phase(2, after_third)
    start_share(2)
    start_share(3)
    for i in range(3):
        small_share(i).wait()
    store_small.start()
    pass_share(2)
    pass_share(3)
    for i in range(4):
        close_share(i)
    store_layer.wait()
    store_grad.wait()
    store_small.wait()


def reduce_all(
    n, n_ctx, direct, normed_t, gate_t, upstream, d_z, d_x, d_s, mixed_parts, normed_parts, small, hidden, cotangent, gain
):
    model, tokens = normed_t.shape[1], d_z.shape[0]
    width, shared_width = d_z.shape[1], d_s.shape[1]
    rows, piece, own = model // n, width // n, hidden.shape[0]
    small_rows, small_width = small.shape[0] + 8, small.shape[1]
    any_space = pl.BlockSpec(memory_space=pl.ANY)
    dma = pltpu.SemaphoreType.DMA
    low = lambda *shape: jax.ShapeDtypeStruct(shape, BF16)
    v_low = lambda *shape: pltpu.VMEM(shape, BF16)
    v_full = lambda *shape: pltpu.VMEM(shape, F32)
    return pl.pallas_call(
        functools.partial(reduce_kernel, n, n_ctx, direct),
        in_specs=[any_space] * 12,
        out_specs=[any_space] * 7,
        out_shape=[
            low(n_ctx, width, rows),
            low(n_ctx, width, rows),
            low(n_ctx, shared_width, rows),
            low(n_ctx, piece, model),
            low(own, model),
            low(own, model),
            jax.ShapeDtypeStruct((n_ctx, small_rows, small_width), F32),
        ],
        scratch_shapes=[
            v_low(model, tokens),
            v_low(width, tokens),
            v_low(tokens, model),
            v_low(tokens, width),
            v_low(tokens, width),
            v_low(tokens, shared_width),
            v_low(n - 1, 2, piece, model // 2),
            v_low(n - 1, 2, rows // 2, width),
            v_low(n - 1, 2, rows // 2, width),
            v_low(n - 1, 2, rows // 2, shared_width),
            v_low(2, piece, model // 2),
            v_low(2, rows // 2, width),
            v_low(2, rows // 2, width),
            v_low(2, rows // 2, shared_width),
            v_low(piece, model),
            v_low(width, rows),
            v_low(width, rows),
            v_low(shared_width, rows),
            v_low(piece, model),
            v_low(2, 2, own, model),
            v_low(2, 2, own, model),
            v_low(2, own, model),
            v_low(own, model),
            v_low(own, model),
            v_full(1, model),
            v_low(own, model),
            v_low(own, model),
            v_full(n, small_rows, small_width),
            v_full(n_ctx, small_rows, small_width),
            dma((12 + 2 * n_ctx,)),
            dma((3,)),
            dma((7, 2)),
            dma((7, 2, n - 1)),
            dma((4, 3)),
            dma((4, 3)),
            dma((4,)),
            dma,
            dma,
            dma((2, 3)),
            dma((2, 3)),
            dma((n - 1,)),
            dma((n - 1,)),
            dma((3,)),
            dma((3,)),
        ],
        compiler_params=pltpu.CompilerParams(
            collective_id=1, has_side_effects=True, vmem_limit_bytes=58 * 1024 * 1024
        ),
        name="reduce_all",
    )(
        normed_t, gate_t, upstream, d_z, d_x, d_s, mixed_parts, normed_parts, small, hidden, cotangent, gain
    )


def assemble_kernel(part, z_ref, x_ref, s_ref, out_ref):
    place = pl.program_id(0)
    n_ctx, size = z_ref.shape[0], z_ref.shape[1]

    def interleave(ref):
        for a in range(size // part):
            for c in range(n_ctx):
                out_ref[(a * n_ctx + c) * part : (a * n_ctx + c + 1) * part, :] = ref[
                    c, a * part : (a + 1) * part, :
                ].astype(F32)

    @pl.when(place < n_ctx)
    def _():
        interleave(z_ref)

    @pl.when(jnp.logical_and(place >= n_ctx, place < 2 * n_ctx))
    def _():
        interleave(x_ref)

    @pl.when(place == 2 * n_ctx)
    def _():
        total = s_ref[0].astype(F32)
        for c in range(1, n_ctx):
            total += s_ref[c].astype(F32)
        out_ref[0 : total.shape[0], :] = total


def assemble(part, g_z, g_x, g_s, columns):
    n_ctx, width, rows = g_z.shape
    block = (n_ctx, width // n_ctx, rows)
    return pl.pallas_call(
        functools.partial(assemble_kernel, part),
        grid=(2 * n_ctx + 1,),
        in_specs=[
            pl.BlockSpec(block, lambda i: (0, jnp.minimum(i, n_ctx - 1), 0)),
            pl.BlockSpec(block, lambda i: (0, jnp.clip(i - n_ctx, 0, n_ctx - 1), 0)),
            pl.BlockSpec(g_s.shape, lambda i: (0, 0, 0)),
        ],
        out_specs=pl.BlockSpec((width, rows), lambda i: (i, 0)),
        out_shape=jax.ShapeDtypeStruct((columns, rows), F32),
        compiler_params=pltpu.CompilerParams(vmem_limit_bytes=58 * 1024 * 1024),
        name="assemble",
    )(g_z, g_x, g_s)


def on_device(
    hidden,
    cotangent,
    seq_lens,
    norm_gain,
    in_weight,
    conv_weight,
    conv_bias,
    dt_bias,
    a_log,
    d_skip,
    gate_gain,
    out_weight,
):
    n_ctx, n_fsdp = lax.axis_size("ctx"), lax.axis_size("fsdp")
    me, shard = lax.axis_index("ctx"), lax.axis_index("fsdp")
    taps = conv_weight.shape[0]
    heads_all = dt_bias.shape[0] * n_fsdp
    inner = out_weight.shape[0] * n_fsdp
    heads, width = heads_all // n_ctx, inner // n_ctx
    model = hidden.shape[2]
    both = 2 * STATE
    held = dt_bias.shape[0]
    direct = held % n_ctx == 0
    unit = held // n_ctx if direct else 1
    part = unit * HEAD
    shared_width = -(-(both + heads_all) // LANES) * LANES

    per_head = jnp.concatenate([dt_bias, a_log, d_skip])
    lines = [norm_gain[None], conv_weight, conv_bias[None], gate_gain[None], per_head[None]]
    longest = -(-max(a.shape[1] for a in lines) // LANES) * LANES
    small = jnp.concatenate([jnp.pad(a, ((0, 0), (0, longest - a.shape[1]))) for a in lines])
    small = jnp.pad(small, ((0, SMALL_ROWS - small.shape[0]), (0, 0)))
    upstream, w_x, w_s, w_z, w_o, small_all, proj_x, proj_s, proj_z, normed_t = gather_all(
        n_fsdp, n_ctx, unit, direct, hidden[0], cotangent[0], in_weight.T, small, out_weight, shared_width
    )
    w_o = w_o.reshape(-1, model)

    def line(first, count, size):
        rows = small_all[:, first : first + count, :size]
        return jnp.moveaxis(rows, 0, 1).reshape(count, -1).astype(F32)

    def own(lines, size):
        by_part = lines.reshape(lines.shape[0], -1, n_ctx, size)
        return lax.dynamic_index_in_dim(by_part, me, 2, False).reshape(lines.shape[0], -1)

    gain_norm = line(0, 1, norm_gain.shape[0])
    conv_lines = line(1, taps + 1, conv_bias.shape[0])
    taps_x, taps_s = own(conv_lines[:, :inner], part), conv_lines[:, inner:]
    gain_gate = own(line(taps + 2, 1, gate_gain.shape[0]), part)
    each = small_all[:, taps + 3, : per_head.shape[0]].reshape(n_fsdp, 3, -1)
    each = own(jnp.moveaxis(each, 0, 1).reshape(3, -1).astype(F32), unit)
    head = jnp.pad(jnp.stack([each[0], jnp.exp(each[1])]), ((0, 0), (0, LANES - heads)))
    skip = jnp.repeat(each[2], HEAD)[None]

    *kept_parts, stats = scan_forward(
        unit, n_ctx, seq_lens, proj_x, proj_s, proj_z, upstream, w_o, taps_x, taps_s, gain_gate, skip, head
    )
    stats = lax.psum(stats, "ctx")
    gate_t, mixed_parts, normed_parts, d_z, d_x, d_s, small_grads = scan_backward(
        unit, n_ctx, inner, seq_lens, proj_x, proj_s, proj_z, kept_parts, stats, w_o, w_z, w_x, w_s, taps_x, taps_s, gain_gate, skip, head
    )
    g_z, g_x, g_s, g_o, layer_out, hidden_grad, sums = reduce_all(
        n_fsdp, n_ctx, direct, normed_t, gate_t, upstream, d_z, d_x, d_s, mixed_parts, normed_parts, small_grads, hidden[0], cotangent[0], gain_norm
    )
    grad_in_weight = assemble(part, g_z, g_x, g_s, 2 * inner + both + heads_all).T
    grad_out_weight = g_o.reshape(-1, model).astype(F32)

    def shard_of(lines):
        size = lines.shape[1] // n_fsdp
        return lax.dynamic_slice_in_dim(lines, shard * size, size, axis=1)

    def in_order(sums_of, size):
        lines = sums_of.shape[1]
        by_part = sums_of.reshape(n_ctx, lines, -1, size)
        return jnp.transpose(by_part, (1, 2, 0, 3)).reshape(lines, -1)

    conv_sums = shard_of(
        jnp.concatenate(
            [
                in_order(sums[:, : taps + 1, :width], part),
                jnp.sum(sums[:, : taps + 1, width:], axis=0),
            ],
            axis=1,
        )
    )
    gate_sums = shard_of(in_order(sums[:, taps + 1 : taps + 2, :width], part))
    head_sums_all = sums[:, taps + 2, : 3 * LANES].reshape(n_ctx, 3, LANES)[:, :, :heads]
    head_grads = shard_of(in_order(head_sums_all, unit))
    norm_sums = jnp.sum(sums[:, 8 : 8 + model // width, :width], axis=0).reshape(1, -1)
    return (
        layer_out[None],
        hidden_grad[None],
        shard_of(norm_sums)[0],
        grad_in_weight,
        conv_sums[:taps],
        conv_sums[taps],
        head_grads[0],
        head_grads[1],
        head_grads[2],
        gate_sums[0],
        grad_out_weight,
    )


def solution(mesh):
    tokens, rows, flat = P("fsdp", "ctx", None), P("fsdp", None), P("fsdp")
    taps = P(None, "fsdp")
    return jax.shard_map(
        on_device,
        mesh=mesh,
        in_specs=(tokens, tokens, flat, flat, rows, taps, flat, flat, flat, flat, flat, rows),
        out_specs=(tokens, tokens, flat, rows, taps, flat, flat, flat, flat, flat, rows),
        check_vma=False,
    )
```

```python
import functools

import jax
import jax.numpy as jnp
from jax import lax
from jax.experimental import pallas as pl
from jax.experimental.pallas import tpu as pltpu
from jax.sharding import PartitionSpec as P

HEAD = 64
STATE = 128
BLOCK = 256
LANES = 128
POINTS = 4
EPS = 1e-05
F32 = jnp.float32
BF16 = jnp.bfloat16


def mm(a, b, contract=((1,), (0,))):
    return lax.dot_general(a, b, (contract, ((), ())), preferred_element_type=F32)


def mm_exact(a, b, contract=((1,), (0,))):
    return lax.dot_general(
        a, b, (contract, ((), ())), precision=lax.Precision.HIGHEST, preferred_element_type=F32
    )


def iota2(shape, axis):
    return lax.broadcasted_iota(jnp.int32, shape, axis)


def levels(lam, step):
    tri = (iota2((BLOCK, BLOCK), 0) >= iota2((BLOCK, BLOCK), 1)).astype(F32)
    level = mm_exact(tri, lam)
    across = level.T
    last = level[BLOCK - 1 : BLOCK, :]
    weight = jnp.exp(level - last) * step
    return level, across, jnp.exp(-last), weight, jnp.exp(-level)


def pair_of(array, first, low_half):
    return jnp.where(low_half, array[:, first : first + 1], array[:, first + 1 : first + 2])


def spread(level, across, head):
    return jnp.exp(-jnp.abs(level[:, head : head + 1] - across[head : head + 1, :]))


def silu_and_slope(v):
    s = jax.nn.sigmoid(v)
    return v * s, s * (1.0 + v * (1.0 - s))


def chosen_heads(me, heads, unit, n_ctx, turned=False):
    here, there = iota2((LANES, LANES), 1), iota2((LANES, LANES), 0)
    if turned:
        here, there = there, here
    head = (here // unit * n_ctx + me) * unit + here % unit
    return jnp.where(jnp.logical_and(there == head, here < heads), 1.0, 0.0).astype(BF16)


def column_valid(length_ref, block):
    at = iota2((BLOCK, 1), 0) + block * BLOCK
    return (at < length_ref[0]).astype(F32)


def forward_kernel(
    heads,
    unit,
    n_ctx,
    length_ref,
    px_ref,
    ps_ref,
    pz_ref,
    up_ref,
    w_o,
    taps_x_ref,
    taps_s_ref,
    gate_gain_ref,
    skip_ref,
    head_ref,
    x_ref,
    b_ref,
    c_ref,
    slope_x_ref,
    slope_s_ref,
    lam_ref,
    step_ref,
    chain_ref,
    kept_ref,
    y_ref,
    dyn_ref,
    stat_ref,
    state,
    before_x,
    before_s,
    v_o,
    load_sem,
):
    block = pl.program_id(0)
    load = pltpu.make_async_copy(w_o, v_o, load_sem)

    @pl.when(block == 0)
    def _():
        load.start()
        state[...] = jnp.zeros_like(state)
        before_x[...] = jnp.zeros_like(before_x)
        before_s[...] = jnp.zeros_like(before_s)

    valid = column_valid(length_ref, block)
    low_half = iota2((1, LANES), 1) < HEAD
    taps = taps_x_ref.shape[0] - 1

    def conv(current, before, weight):
        padded = jnp.concatenate([before, current], axis=0)
        total = weight[taps : taps + 1]
        for k in range(taps):
            first = 8 - (taps - 1) + k
            total = total + weight[k : k + 1] * padded[first : first + BLOCK]
        return silu_and_slope(total)

    shared = ps_ref[...].astype(F32)
    both = shared[:, : 2 * STATE]
    active, slope = conv(both, before_s[...], taps_s_ref[...])
    before_s[...] = both[BLOCK - 8 :]
    slope_s_ref[...] = slope.astype(BF16)
    rows_b, rows_c = active[:, :STATE].astype(BF16), active[:, STATE:].astype(BF16)
    b_ref[...] = rows_b
    c_ref[...] = rows_c
    chosen = chosen_heads(lax.axis_index("ctx"), heads, unit, n_ctx)
    raw = mm(ps_ref[:, 2 * STATE :], chosen)
    raw = raw + head_ref[0:1]
    own = iota2((1, LANES), 1) < heads
    step = jnp.where(own, valid * jax.nn.softplus(raw), 0.0)
    lam = step * head_ref[1:2]
    step_ref[...] = step
    lam_ref[...] = lam
    chain_ref[...] = jnp.where(own, valid * jax.nn.sigmoid(raw), 0.0)

    gram = mm(rows_c, rows_b, ((1,), (1,)))
    level, across, last, weight, fade = levels(lam, step)
    kept_ref[0] = state[...].astype(BF16)
    entering = mm(rows_c, state[...].astype(BF16))
    by_state = rows_b.T
    squares = jnp.zeros((BLOCK, LANES), F32)
    for first in range(0, heads, 2):
        lanes = slice(first * HEAD, (first + 2) * HEAD)
        current = px_ref[:, lanes].astype(F32)
        active, slope = conv(current, before_x[:, lanes], taps_x_ref[:, lanes])
        before_x[:, lanes] = current[BLOCK - 8 :]
        slope_x_ref[:, lanes] = slope.astype(BF16)
        x_low = active.astype(BF16)
        x_ref[:, lanes] = x_low
        x = x_low.astype(F32)
        scaled = x * pair_of(step, first, low_half)
        total = pair_of(fade, first, low_half) * entering[:, lanes] + skip_ref[:, lanes] * x
        for head, keep in ((first, low_half), (first + 1, jnp.logical_not(low_half))):
            mixing = (gram * spread(level, across, head)).astype(BF16)
            total += mm(mixing, jnp.where(keep, scaled, 0.0).astype(BF16))
        y_ref[:, lanes] = total
        update = mm(by_state, (x * pair_of(weight, first, low_half)).astype(BF16))
        state[:, lanes] = state[:, lanes] * pair_of(last, first, low_half) + update
        gated = total * jax.nn.silu(pz_ref[:, lanes].astype(F32))
        squares += gated * gated

    @pl.when(block == 0)
    def _():
        load.wait()

    d_yn = valid * mm(up_ref[0], v_o[...], ((1,), (1,)))
    dyn_ref[...] = d_yn
    gated = y_ref[...] * jax.nn.silu(pz_ref[...].astype(F32))
    terms = gate_gain_ref[...] * d_yn * gated
    square = jnp.sum(squares, axis=1, keepdims=True)
    along = jnp.sum(terms, axis=1, keepdims=True)
    lane = iota2((1, LANES), 1)
    both_sums = jnp.where(lane == 0, square, 0.0) + jnp.where(lane == 1, along, 0.0)
    stat_ref[...] = both_sums.T[0:8]


def scan_forward(unit, n_ctx, length, px, ps, pz, upstream, w_o, taps_x, taps_s, gate_gain, skip, head):
    tokens, width = px.shape
    heads = width // HEAD
    count = tokens // BLOCK
    model = w_o.shape[1]
    by_block = lambda i: (i, 0)
    at_block = lambda size: pl.BlockSpec((BLOCK, size), by_block)
    whole = lambda a: pl.BlockSpec(a.shape, lambda i: (0, 0))
    low = lambda *shape: jax.ShapeDtypeStruct(shape, BF16)
    full = lambda *shape: jax.ShapeDtypeStruct(shape, F32)
    return pl.pallas_call(
        functools.partial(forward_kernel, heads, unit, n_ctx),
        grid=(count,),
        in_specs=[
            pl.BlockSpec(memory_space=pltpu.SMEM),
            at_block(width),
            at_block(ps.shape[1]),
            at_block(width),
            pl.BlockSpec((1, BLOCK, model), lambda i: (i, 0, 0)),
            pl.BlockSpec(memory_space=pl.ANY),
            whole(taps_x),
            whole(taps_s),
            whole(gate_gain),
            whole(skip),
            whole(head),
        ],
        out_specs=[
            at_block(width),
            at_block(STATE),
            at_block(STATE),
            at_block(width),
            at_block(2 * STATE),
            at_block(LANES),
            at_block(LANES),
            at_block(LANES),
            pl.BlockSpec((1, STATE, width), lambda i: (i, 0, 0)),
            at_block(width),
            at_block(width),
            pl.BlockSpec((8, BLOCK), lambda i: (0, i)),
        ],
        out_shape=[
            low(tokens, width),
            low(tokens, STATE),
            low(tokens, STATE),
            low(tokens, width),
            low(tokens, 2 * STATE),
            full(tokens, LANES),
            full(tokens, LANES),
            full(tokens, LANES),
            low(count, STATE, width),
            full(tokens, width),
            full(tokens, width),
            full(8, tokens),
        ],
        scratch_shapes=[
            pltpu.VMEM((STATE, width), F32),
            pltpu.VMEM((8, width), F32),
            pltpu.VMEM((8, 2 * STATE), F32),
            pltpu.VMEM(w_o.shape, BF16),
            pltpu.SemaphoreType.DMA,
        ],
        compiler_params=pltpu.CompilerParams(vmem_limit_bytes=56 * 1024 * 1024),
        cost_estimate=pl.CostEstimate(
            flops=2 * tokens * width * (2 * BLOCK + 2 * STATE + model),
            bytes_accessed=tokens * width * 24,
            transcendentals=tokens * heads * BLOCK,
        ),
        name="scan_forward",
    )(length, px, ps, pz, upstream, w_o, taps_x, taps_s, gate_gain, skip, head)


def head_sums(product, chooser):
    high = product.astype(BF16)
    rest = (product - high.astype(F32)).astype(BF16)
    return mm(high, chooser) + mm(rest, chooser)


MESH = pl.DeviceIdType.MESH
SMALL_ROWS = 32


def ring_place(index, half):
    a, b = index // 2, index % 2
    return a + b * (2 * half - 1 - 2 * a)


def ring_index(place, half):
    b = place // half
    return 2 * (place + b * (2 * half - 1 - 2 * place)) + b


class Ring:
    def __init__(self, n):
        self.n, self.half = n, n // 2
        self.me, self.shard = lax.axis_index("ctx"), lax.axis_index("fsdp")
        self.place = ring_place(self.shard, self.half)

    def at(self, steps):
        return ring_index(lax.rem(self.place + steps + 2 * self.n, self.n), self.half)

    def neighbour(self, way):
        return (self.me, self.at(1 if way == 0 else -1))


def remote(source, target, send, recv, device):
    return pltpu.make_async_remote_copy(
        src_ref=source,
        dst_ref=target,
        send_sem=send,
        recv_sem=recv,
        device_id=device,
        device_id_type=MESH,
    )


def greet(device):
    pl.semaphore_signal(pltpu.get_barrier_semaphore(), inc=1, device_id=device, device_id_type=MESH)


class Around:
    def __init__(self, me, shard):
        core, row = me % 2, me // 2
        self.me = me
        self.core_at = me + 1 - 2 * core
        self.row_at = me + 2 - 4 * row
        self.both_at = self.row_at + 1 - 2 * core
        self.core, self.row, self.both = (
            (at, shard) for at in (self.core_at, self.row_at, self.both_at)
        )
        self.all = (self.core, self.row, self.both)


class TokenSum:
    def __init__(self, around, parts, mine, from_core, from_row, send, recv):
        self.around, self.parts, self.mine = around, parts, mine
        self.from_core, self.from_row, self.send, self.recv = from_core, from_row, send, recv

    def loads(self):
        at = self.around
        return (
            (self.parts.at[at.row_at], self.mine.at[1]),
            (self.parts.at[at.me], self.mine.at[0]),
        )

    def to_core(self, which):
        at = self.around
        return remote(
            self.parts.at[(at.core_at, at.both_at)[which]],
            self.from_core.at[which],
            self.send.at[which],
            self.recv.at[which],
            at.core,
        )

    def to_row(self):
        return remote(
            self.mine.at[1], self.from_row, self.send.at[2], self.recv.at[2], self.around.row
        )

    def start(self):
        self.to_core(1).start()
        self.to_core(0).start()

    def pass_row(self):
        self.to_core(1).wait()
        total = self.mine[1].astype(F32) + self.from_core[1].astype(F32)
        self.mine[1] = total.astype(BF16)
        self.to_row().start()

    def total(self):
        self.to_core(0).wait()
        self.to_row().wait()
        return (
            self.mine[0].astype(F32) + self.from_core[0].astype(F32) + self.from_row[...].astype(F32)
        )


def gate_kernel(
    heads,
    channels,
    length_ref,
    stats,
    pz_ref,
    y_ref,
    dyn_ref,
    w_o,
    gate_gain_ref,
    ynt_ref,
    mixed_ref,
    dz_ref,
    dssd_ref,
    gain_ref,
    stat_all,
    columns,
    v_y,
    v_o,
    load_sem,
    stat_send,
    stat_recv,
):
    block = pl.program_id(0)
    me = lax.axis_index("ctx")
    around = Around(me, lax.axis_index("fsdp"))
    load = pltpu.make_async_copy(w_o, v_o, load_sem.at[0])

    @pl.when(block == 0)
    def _():
        for device in around.all:
            greet(device)
        load.start()
        own = pltpu.make_async_copy(stats, stat_all.at[me], load_sem.at[1])
        own.start()
        own.wait()
        pl.semaphore_wait(pltpu.get_barrier_semaphore(), 3)
        copies = [
            remote(stat_all.at[me], stat_all.at[me], stat_send.at[i], stat_recv.at[i], device)
            for i, device in enumerate(around.all)
        ]
        for copy in copies:
            copy.start()
        for copy in copies:
            copy.wait()
        total = jnp.sum(stat_all[...], axis=0)
        for i in range(total.shape[1] // BLOCK):
            columns[i] = total[:, i * BLOCK : (i + 1) * BLOCK].T
        gain_ref[...] = jnp.zeros_like(gain_ref)
        load.wait()

    valid = column_valid(length_ref, block)
    sums = columns[block]
    scale = lax.rsqrt(sums[:, 0:1] / channels + EPS)
    slant = scale * scale * scale * sums[:, 1:2] / channels
    for first in range(0, heads, 2):
        lanes = slice(first * HEAD, (first + 2) * HEAD)
        gate, gate_slope = silu_and_slope(pz_ref[:, lanes].astype(F32))
        mixed = y_ref[:, lanes]
        d_yn = dyn_ref[:, lanes]
        gain = gate_gain_ref[:, lanes]
        gated = mixed * gate
        scaled = gated * scale
        v_y[:, lanes] = (valid * (scaled * gain)).astype(BF16)
        gain_ref[0:1, lanes] += jnp.sum(d_yn * scaled, axis=0, keepdims=True)
        d_gated = scale * (gain * d_yn) - gated * slant
        dz_ref[:, lanes] = (d_gated * mixed * gate_slope).astype(BF16)
        dssd_ref[:, lanes] = (d_gated * gate).astype(BF16)
    normed_gate = v_y[...]
    ynt_ref[...] = normed_gate.T
    mixed_ref[0] = mm(normed_gate, v_o[...]).astype(BF16)


def gate_norm(channels, length, stats, pz, y, d_yn, w_o, gate_gain):
    tokens, width = pz.shape
    count, model = tokens // BLOCK, w_o.shape[1]
    n_ctx = channels // width
    at_block = lambda size: pl.BlockSpec((BLOCK, size), lambda i: (i, 0))
    any_space = pl.BlockSpec(memory_space=pl.ANY)
    low = lambda *shape: jax.ShapeDtypeStruct(shape, BF16)
    return pl.pallas_call(
        functools.partial(gate_kernel, width // HEAD, channels),
        grid=(count,),
        in_specs=[
            pl.BlockSpec(memory_space=pltpu.SMEM),
            any_space,
            at_block(width),
            at_block(width),
            at_block(width),
            any_space,
            pl.BlockSpec(gate_gain.shape, lambda i: (0, 0)),
        ],
        out_specs=[
            pl.BlockSpec((width, BLOCK), lambda i: (0, i)),
            pl.BlockSpec((1, BLOCK, model), lambda i: (i, 0, 0)),
            at_block(width),
            at_block(width),
            pl.BlockSpec((8, width), lambda i: (0, 0)),
        ],
        out_shape=[
            low(width, tokens),
            low(count, BLOCK, model),
            low(tokens, width),
            low(tokens, width),
            jax.ShapeDtypeStruct((8, width), F32),
        ],
        scratch_shapes=[
            pltpu.VMEM((n_ctx, 8, tokens), F32),
            pltpu.VMEM((count, BLOCK, 8), F32),
            pltpu.VMEM((BLOCK, width), BF16),
            pltpu.VMEM(w_o.shape, BF16),
            pltpu.SemaphoreType.DMA((2,)),
            pltpu.SemaphoreType.DMA((3,)),
            pltpu.SemaphoreType.DMA((3,)),
        ],
        compiler_params=pltpu.CompilerParams(
            collective_id=2, has_side_effects=True, vmem_limit_bytes=56 * 1024 * 1024
        ),
        name="gate_norm",
    )(length, stats, pz, y, d_yn, w_o, gate_gain)


def backward_kernel(
    heads,
    unit,
    n_ctx,
    n,
    px_ref,
    ps_ref,
    x_ref,
    b_ref,
    c_ref,
    slope_x_ref,
    slope_s_ref,
    lam_ref,
    step_ref,
    chain_ref,
    kept_ref,
    dssd_ref,
    w_z,
    w_x,
    w_s,
    gate_t,
    normed_t,
    upstream,
    d_z,
    mixed_parts,
    hidden,
    gain_grads_ref,
    taps_x_ref,
    taps_s_ref,
    skip_ref,
    head_ref,
    normed_ref,
    dx_ref,
    ds_ref,
    small_ref,
    shard_o,
    shard_z,
    layer_out,
    back,
    mixed_grads,
    for_step,
    for_level,
    left,
    right,
    sums,
    after_x,
    after_s,
    v_z,
    v_x,
    v_s,
    v_left,
    v_right,
    slots,
    stage,
    done_o,
    done_z,
    mine,
    from_core,
    from_row,
    v_hidden,
    load_sem,
    store_sem,
    ring_send,
    ring_recv,
    part_send,
    part_recv,
):
    turn = pl.program_id(0)
    turns = heads // 2 // POINTS
    block = pl.num_programs(0) - 1 - turn
    width, model = x_ref.shape[1], v_hidden.shape[1]
    own = hidden.shape[0]
    ring = Ring(n)
    around = Around(ring.me, ring.shard)
    piece, size = slots.shape[4], slots.shape[5]
    sum_mixed = TokenSum(around, mixed_parts, mine, from_core, from_row, part_send, part_recv)
    loads = [
        pltpu.make_async_copy(source, target, load_sem.at[i])
        for i, (source, target) in enumerate(
            (
                (gate_t, v_left.at[pl.ds(0, width)]),
                *((upstream.at[c], v_right.at[pl.ds(c * own, own), pl.ds(0, model)]) for c in range(n_ctx)),
                *((normed_t.at[c], v_left.at[pl.ds(width, model), pl.ds(c * own, own)]) for c in range(n_ctx)),
                (d_z, v_right.at[:, pl.ds(model, width)]),
                *sum_mixed.loads(),
                (hidden, v_hidden),
                (w_z, v_z),
                (w_x, v_x),
                (w_s, v_s),
            )
        )
    ]
    ring_loads = 2 + 2 * n_ctx

    def partial_sum(kind, way, sub, index):
        first = (1 - kind) * index * piece + kind * (width + (2 * index + way) * piece)
        at = (1 - kind) * (2 * way + sub) * size + kind * (model + sub * size)
        return mm(
            v_left[pl.ds(pl.multiple_of(first, 16), piece), :],
            v_right[:, pl.ds(pl.multiple_of(at, LANES), size)],
        )

    def hop(kind, way, sub, step, source):
        return remote(
            source,
            slots.at[kind, step, way, sub],
            ring_send.at[kind, way, sub],
            ring_recv.at[kind, way, sub, step],
            (ring.me, ring.at(1 - 2 * way)),
        )

    def streams(body):
        def one(e, carry):
            body(e // 4, e // 2 % 2, e % 2)
            return carry

        lax.fori_loop(0, 8, one, 0)

    def start_ring(kind, way, sub):
        place = stage.at[kind, way, sub]
        place[...] = partial_sum(kind, way, sub, ring.at(2 * way - 1)).astype(BF16)
        hop(kind, way, sub, 0, place).start()

    def ring_step(step):
        def body(kind, way, sub):
            index = ring.at((step + 2) * (2 * way - 1))
            partial = partial_sum(kind, way, sub, index)
            hop(kind, way, sub, step, stage.at[kind, way, sub]).wait()
            place = slots.at[kind, step, way, sub]
            total = place[...].astype(F32) + partial

            @pl.when(step < n - 2)
            def _():
                place[...] = total.astype(BF16)
                hop(kind, way, sub, step + 1, place).start()

            @pl.when(jnp.logical_and(step == n - 2, kind == 0))
            def _():
                at = pl.multiple_of((2 * way + sub) * size, LANES)
                done_o[:, pl.ds(at, size)] = total.astype(BF16)

            @pl.when(jnp.logical_and(step == n - 2, kind == 1))
            def _():
                done_z[way, pl.ds(pl.multiple_of(sub * size, 16), size), :] = total.T.astype(BF16)

        streams(body)

    def serve(point):
        at = turn * POINTS + point
        points = POINTS * n_ctx
        lax.fori_loop(
            at * (n - 1) // points,
            (at + 1) * (n - 1) // points,
            lambda step, carry: (ring_step(step), carry)[1],
            0,
        )

    @pl.when(turn == 0)
    def _():
        for device in around.all:
            greet(device)
        greet(ring.neighbour(0))
        greet(ring.neighbour(1))
        for copy in loads:
            copy.start()
        back[...] = jnp.zeros_like(back)
        small_ref[...] = jnp.zeros_like(small_ref)
        small_ref[taps_x_ref.shape[0] : taps_x_ref.shape[0] + 1, 0:width] = gain_grads_ref[0:1, :]
        after_x[...] = jnp.zeros_like(after_x)
        after_s[...] = jnp.zeros_like(after_s)
        pl.semaphore_wait(pltpu.get_barrier_semaphore(), 5)
        for copy in loads[:ring_loads]:
            copy.wait()
        streams(start_ring)
        sum_mixed.start()
        for copy in loads[ring_loads:]:
            copy.wait()

    @pl.when(turn == 1)
    def _():
        sum_mixed.pass_row()

    taps = taps_x_ref.shape[0] - 1

    rows_b, rows_c = b_ref[...], c_ref[...]
    step = step_ref[...]
    lam = lam_ref[...]
    gram = mm(rows_c, rows_b, ((1,), (1,)))
    gram_t = mm(rows_b, rows_c, ((1,), (1,)))
    level, across, last, weight, fade = levels(lam, step)
    out_decay = jnp.exp(level - level[BLOCK - 1 : BLOCK, :])
    step_across = step.T
    at_row, at_col = iota2((BLOCK, BLOCK), 0), iota2((BLOCK, BLOCK), 1)
    order = (at_row > at_col).astype(F32) - (at_row < at_col).astype(F32)
    low_half = iota2((1, LANES), 1) < HEAD
    lane = iota2((1, LANES), 1)
    by_state = rows_c.T
    kept = kept_ref[0]
    old_back = back[...].astype(BF16)
    entering = mm(rows_c, kept)
    leaving = mm(rows_b, old_back)
    at_last = jnp.sum(kept.astype(F32) * back[...], axis=0, keepdims=True)
    mixed_grads[...] = jnp.zeros_like(mixed_grads)
    left[...] = jnp.zeros_like(left)
    right[...] = jnp.zeros_like(right)
    sums[...] = jnp.zeros_like(sums)
    d_b = jnp.zeros((BLOCK, STATE), F32)
    d_c = jnp.zeros((BLOCK, STATE), F32)

    def conv_back(d_conv, after, current, weight):
        padded = jnp.concatenate([d_conv, after], axis=0)
        d_in = jnp.zeros_like(d_conv)
        grads = []
        for k in range(taps):
            moved = padded[taps - 1 - k : taps - 1 - k + BLOCK]
            d_in += weight[k : k + 1] * moved
            grads.append(jnp.sum(current * moved, axis=0, keepdims=True))
        grads.append(jnp.sum(d_conv, axis=0, keepdims=True))
        return d_in, jnp.concatenate(grads, axis=0)

    for first in range(0, heads, 2):
        lanes = slice(first * HEAD, (first + 2) * HEAD)
        x_low = x_ref[:, lanes]
        x = x_low.astype(F32)
        grad_low = dssd_ref[:, lanes]
        grad = grad_low.astype(F32)
        through = jnp.zeros((BLOCK, LANES), F32)
        for head, keep in ((first, low_half), (first + 1, jnp.logical_not(low_half))):
            decay = spread(level, across, head)
            grad_own = jnp.where(keep, grad, 0.0).astype(BF16)
            pairs = mm(grad_own, x_low, ((1,), (1,)))
            through += mm((gram_t * decay).astype(BF16), grad_own)
            scaled = decay * pairs * step_across[head : head + 1, :]
            mixed_grads[...] += scaled
            ordered = gram * scaled * order
            left[...] = jnp.where(
                lane == head, jnp.sum(ordered, axis=1, keepdims=True), left[...]
            )
            right[head : head + 1, :] = jnp.sum(ordered, axis=0, keepdims=True)
        weight_pair = pair_of(weight, first, low_half)
        step_pair = pair_of(step, first, low_half)
        fade_pair = pair_of(fade, first, low_half)
        out_pair = pair_of(out_decay, first, low_half)
        leave = leaving[:, lanes]
        d_x = step_pair * through + weight_pair * leave + skip_ref[:, lanes] * grad
        for_step[:, lanes] = x * (through + out_pair * leave)
        weighted = weight_pair * x
        faded = fade_pair * grad
        for_level[:, lanes] = weighted * leave - faded * entering[:, lanes]
        sums[0:1, lanes] = jnp.sum(weighted * leave, axis=0, keepdims=True)
        sums[2:3, lanes] = jnp.sum(x * grad, axis=0, keepdims=True)
        faded_low = faded.astype(BF16)
        d_b += mm(weighted.astype(BF16), old_back[:, lanes], ((1,), (1,)))
        d_c += mm(faded_low, kept[:, lanes], ((1,), (1,)))
        back[:, lanes] = back[:, lanes] * pair_of(last, first, low_half) + mm(by_state, faded_low)
        d_conv = d_x * slope_x_ref[:, lanes].astype(F32)
        d_in, grads = conv_back(
            d_conv, after_x[:, lanes], px_ref[:, lanes].astype(F32), taps_x_ref[:, lanes]
        )
        after_x[:, lanes] = d_conv[0:8]
        dx_ref[:, lanes] = d_in.astype(BF16)
        small_ref[0 : taps + 1, lanes] += grads
        if first // 2 % turns == turns - 1 and first // 2 // turns < POINTS - 1:
            serve(first // 2 // turns)

    all_pairs = mixed_grads[...]
    d_b = d_b + mm(all_pairs.T.astype(BF16), rows_c)
    d_c = d_c + mm(all_pairs.astype(BF16), rows_b)
    d_conv = jnp.concatenate([d_b, d_c], axis=1) * slope_s_ref[...].astype(F32)
    d_in, grads = conv_back(
        d_conv, after_s[...], ps_ref[:, : 2 * STATE].astype(F32), taps_s_ref[...]
    )
    after_s[...] = d_conv[0:8]
    ds_ref[:, : 2 * STATE] = d_in.astype(BF16)
    small_ref[0 : taps + 1, width:] += grads

    chooser = (iota2((width, LANES), 0) // HEAD == iota2((width, LANES), 1)).astype(BF16)
    d_step = head_sums(for_step[...], chooser)
    sums[1:2, :] = at_last
    total = head_sums(sums[...], chooser)
    d_level = head_sums(for_level[...], chooser) - left[...] + right[...].T
    final = -total[0:1, :] - last * total[1:2, :]
    d_level = d_level + jnp.where(iota2((BLOCK, 1), 0) == BLOCK - 1, final, 0.0)
    d_lam = mm_exact((at_row <= at_col).astype(F32), d_level)
    d_raw = (d_step + d_lam * head_ref[1:2]) * chain_ref[...]
    head_row = taps + 2
    small_ref[head_row : head_row + 1, 0:LANES] += jnp.sum(d_raw, axis=0, keepdims=True)
    small_ref[head_row : head_row + 1, LANES : 2 * LANES] += jnp.sum(
        d_lam * lam, axis=0, keepdims=True
    )
    small_ref[head_row : head_row + 1, 2 * LANES : 3 * LANES] += total[2:3, :]
    chosen = chosen_heads(lax.axis_index("ctx"), heads, unit, n_ctx, True)
    ds_ref[:, 2 * STATE :] = mm(d_raw.astype(BF16), chosen).astype(BF16)

    d_z_block = v_right[pl.ds(pl.multiple_of(block * BLOCK, BLOCK), BLOCK), model:]
    normed_ref[0] = (
        mm(d_z_block, v_z[...], ((1,), (1,)))
        + mm(dx_ref[...], v_x[...], ((1,), (1,)))
        + mm(ds_ref[...], v_s[...], ((1,), (1,)))
    ).astype(BF16)
    serve(POINTS - 1)

    @pl.when(turn == pl.num_programs(0) - 1)
    def _():
        stores = [
            pltpu.make_async_copy(source, target, store_sem.at[i])
            for i, (source, target) in enumerate(
                ((done_o, shard_o), (done_z, shard_z), (v_hidden, layer_out))
            )
        ]
        stores[0].start()
        stores[1].start()
        v_hidden[...] = (v_hidden[...].astype(F32) + sum_mixed.total()).astype(BF16)
        stores[2].start()
        for copy in stores:
            copy.wait()


def scan_backward(
    n, unit, n_ctx, px, ps, kept_parts, d_ssd, w_z, w_x, w_s, gate_t, normed_t, upstream, d_z, mixed_parts, hidden, gain_grads, taps_x, taps_s, skip, head
):
    x, rows_b, rows_c, slope_x, slope_s, lam, step, chain, kept = kept_parts
    tokens, width = px.shape
    heads = width // HEAD
    count = tokens // BLOCK
    own, model = hidden.shape
    shared_width = ps.shape[1]
    piece = width // n
    assert model == 2 * width and heads // 2 % POINTS == 0
    by_block = lambda i: (count - 1 - i, 0)
    at_block = lambda size: pl.BlockSpec((BLOCK, size), by_block)
    whole = lambda a: pl.BlockSpec(a.shape, lambda i: (0, 0))
    any_space = pl.BlockSpec(memory_space=pl.ANY)
    low = lambda *shape: jax.ShapeDtypeStruct(shape, BF16)
    v_low = lambda *shape: pltpu.VMEM(shape, BF16)
    v_full = lambda *shape: pltpu.VMEM(shape, F32)
    part = lambda a, b: pl.BlockSpec((1, a, b), lambda i: (count - 1 - i, 0, 0))
    small_shape = (8, width + 2 * STATE)
    dma = pltpu.SemaphoreType.DMA
    return pl.pallas_call(
        functools.partial(backward_kernel, heads, unit, n_ctx, n),
        grid=(count,),
        in_specs=[
            at_block(width),
            at_block(shared_width),
            at_block(width),
            at_block(STATE),
            at_block(STATE),
            at_block(width),
            at_block(2 * STATE),
            at_block(LANES),
            at_block(LANES),
            at_block(LANES),
            part(STATE, width),
            at_block(width),
        ]
        + [any_space] * 9
        + [whole(a) for a in (gain_grads, taps_x, taps_s, skip, head)],
        out_specs=[
            part(BLOCK, model),
            at_block(width),
            at_block(shared_width),
            pl.BlockSpec(small_shape, lambda i: (0, 0)),
            any_space,
            any_space,
            any_space,
        ],
        out_shape=[
            low(count, BLOCK, model),
            low(tokens, width),
            low(tokens, shared_width),
            jax.ShapeDtypeStruct(small_shape, F32),
            low(piece, model),
            low(2, width, piece),
            low(own, model),
        ],
        scratch_shapes=[
            v_full(STATE, width),
            v_full(BLOCK, BLOCK),
            v_full(BLOCK, width),
            v_full(BLOCK, width),
            v_full(BLOCK, LANES),
            v_full(LANES, BLOCK),
            v_full(8, width),
            v_full(8, width),
            v_full(8, 2 * STATE),
            v_low(*w_z.shape),
            v_low(*w_x.shape),
            v_low(*w_s.shape),
            v_low(width + model, tokens),
            v_low(tokens, model + width),
            v_low(2, n - 1, 2, 2, piece, width // 2),
            v_low(2, 2, 2, piece, width // 2),
            v_low(piece, model),
            v_low(2, width, piece),
            v_low(2, own, model),
            v_low(2, own, model),
            v_low(own, model),
            v_low(own, model),
            dma((8 + 2 * n_ctx,)),
            dma((3,)),
            dma((2, 2, 2)),
            dma((2, 2, 2, n - 1)),
            dma((3,)),
            dma((3,)),
        ],
        compiler_params=pltpu.CompilerParams(
            collective_id=3, has_side_effects=True, vmem_limit_bytes=59 * 1024 * 1024
        ),
        name="scan_backward",
    )(
        px, ps, x, rows_b, rows_c, slope_x, slope_s, lam, step, chain, kept, d_ssd, w_z, w_x, w_s, gate_t, normed_t, upstream, d_z, mixed_parts, hidden, gain_grads, taps_x, taps_s, skip, head
    )


def gather_kernel(
    n,
    n_ctx,
    unit,
    direct,
    hidden,
    cotangent,
    in_weight_t,
    small,
    out_weight,
    cotangent_all,
    w_x,
    w_s,
    w_z,
    w_o,
    small_out,
    proj_x,
    proj_s,
    proj_z,
    normed_t,
    v_hidden,
    v_normed,
    v_x,
    v_s,
    v_z,
    v_small,
    raw_x,
    raw_s,
    raw_z,
    out_x,
    out_s,
    out_z,
    out_t,
    v_gain,
    load_sem,
    column_sem,
    local_sem,
    store_sem,
    ring_send,
    ring_recv,
    ctx_send,
    ctx_recv,
    piece_send,
    piece_recv,
):
    ring = Ring(n)
    me, shard = ring.me, ring.shard
    width, model = v_x.shape[1], v_x.shape[0]
    inner = width * n_ctx
    r = model // n
    shared = in_weight_t.shape[0] - 2 * inner
    row = me // 2
    other_core = (me + 1 - 2 * (me % 2), shard)
    other_row = (me + 2 - 4 * row, shard)
    piece = w_o.shape[1]
    piece_peer = (shard % n_ctx, shard // n_ctx * n_ctx + me)
    moves = shard % n_ctx != me

    barrier = pltpu.get_barrier_semaphore()
    for device in (other_core, other_row, ring.neighbour(0), ring.neighbour(1)):
        pl.semaphore_signal(barrier, inc=1, device_id=device, device_id_type=MESH)

    part = unit * HEAD

    def load_columns(base, target, sems):
        return [
            pltpu.make_async_copy(
                in_weight_t.at[pl.ds(pl.multiple_of(base + (a * n_ctx + me) * part, 16), part)],
                target.at[pl.ds(a * part, part)],
                sems.at[a],
            )
            for a in range(width // part)
        ]

    loads = [
        load_columns(inner, raw_x, column_sem.at[0]),
        [
            pltpu.make_async_copy(
                in_weight_t.at[pl.ds(2 * inner, shared)], raw_s.at[pl.ds(0, shared)], load_sem.at[0]
            )
        ],
        [pltpu.make_async_copy(small, v_small.at[shard], load_sem.at[1])],
        [pltpu.make_async_copy(hidden, v_hidden.at[me], load_sem.at[2])],
        load_columns(0, raw_z, column_sem.at[1]),
    ]
    for copies in loads:
        for copy in copies:
            copy.start()

    def loaded(i):
        for copy in loads[i]:
            copy.wait()

    if direct:
        pl.semaphore_wait(barrier, 4)
    else:

        @pl.when(moves)
        def _():
            pl.semaphore_signal(barrier, inc=1, device_id=piece_peer, device_id_type=MESH)
            pl.semaphore_wait(barrier, 5)

        @pl.when(jnp.logical_not(moves))
        def _():
            pl.semaphore_wait(barrier, 4)

    half, quarter = width // 2, w_o.shape[2] // 4
    rows = r // 2
    both_rows = lambda index, way: pl.ds(pl.multiple_of((2 * index + way) * rows, 16), rows)
    x_part = lambda a, sub: lambda index, way: a.at[both_rows(index, way), pl.ds(sub * half, half)]
    s_part = lambda index, way: v_s.at[both_rows(index, way)]
    small_part = lambda index, way: v_small.at[index, pl.ds(way * SMALL_ROWS // 2, SMALL_ROWS // 2)]
    o_part = lambda sub: lambda index, way: w_o.at[
        index, :, pl.ds((2 * way + sub) * quarter, quarter)
    ]
    phases = (
        ((0, small_part), (1, s_part), (2, x_part(v_x, 0)), (3, x_part(v_x, 1))),
        ((4, x_part(v_z, 0)), (5, x_part(v_z, 1))),
        ((6, o_part(0)), (7, o_part(1))),
    )

    def hop(stream, way, step):
        number, part = stream
        place = part(ring.at(-step if way == 0 else step), way)
        return remote(
            place, place, ring_send.at[number, way], ring_recv.at[number, way, step],
            ring.neighbour(way),
        )

    def arrives(stream, way, step):
        number, part = stream
        landed = part(ring.at(-step - 1 if way == 0 else step + 1), way)
        return remote(
            landed, landed, ring_send.at[number, way], ring_recv.at[number, way, step],
            ring.neighbour(way),
        )

    def start_stream(stream):
        for way in (0, 1):
            hop(stream, way, 0).start()

    def to_row(i, a, whole):
        return remote(a, whole.at[me], ctx_send.at[i, 0], ctx_recv.at[i, 0], other_row)

    def to_core(i, a, whole):
        return remote(a, whole.at[me], ctx_send.at[i, 1], ctx_recv.at[i, 1], other_core)

    def pass_on(i, whole):
        beyond = whole.at[other_row[0]]
        return remote(beyond, beyond, ctx_send.at[i, 2], ctx_recv.at[i, 2], other_core)

    to_row(0, hidden, v_hidden).start()
    to_core(0, hidden, v_hidden).start()
    own_rows = pl.ds(pl.multiple_of(shard * r, 16), r)
    loaded(2)
    start_stream(phases[0][0])
    loaded(0)
    v_x[own_rows, :] = raw_x[...].T
    start_stream(phases[0][2])
    start_stream(phases[0][3])
    loaded(1)
    raw_s[shared:, :] = jnp.zeros((raw_s.shape[0] - shared, r), BF16)
    v_s[own_rows, :] = raw_s[...].T
    start_stream(phases[0][1])
    own_piece = out_weight.at[pl.ds(pl.multiple_of(me * piece, 16), piece)]
    keep_piece = pltpu.make_async_copy(own_piece, w_o.at[shard], piece_send)

    def move_piece(wait):
        if direct:
            keep_piece.wait() if wait else keep_piece.start()
            return
        send_piece = remote(own_piece, w_o.at[piece_peer[1]], piece_send, piece_recv, piece_peer)

        @pl.when(moves)
        def _():
            send_piece.wait() if wait else send_piece.start()

        @pl.when(jnp.logical_not(moves))
        def _():
            keep_piece.wait() if wait else keep_piece.start()

    keep_cotangent = pltpu.make_async_copy(cotangent, cotangent_all.at[me], local_sem)
    keep_cotangent.start()
    loaded(3)
    loaded(4)
    v_z[own_rows, :] = raw_z[...].T

    def run_phase(number, work, after):
        def body(step, carry):
            for stream in phases[number]:
                for way in (0, 1):
                    arrives(stream, way, step).wait_recv()
                    hop(stream, way, step).wait_send()
                    hop(stream, way, step + 1).start()
            if work is not None:

                @pl.when(step < n_ctx)
                def _():
                    work(step)

            return carry

        lax.fori_loop(0, n - 2, body, 0)
        after()
        for stream in phases[number]:
            for way in (0, 1):
                arrives(stream, way, n - 2).wait_recv()
                hop(stream, way, n - 2).wait_send()

    tokens = v_hidden.shape[1]

    def project_first(chunk):
        at = pl.ds(pl.multiple_of(chunk * tokens, tokens), tokens)
        resid = v_hidden[chunk].astype(F32)
        scale = lax.rsqrt(jnp.mean(resid * resid, axis=1, keepdims=True) + EPS)
        normed = (resid * scale * v_gain[...]).astype(BF16)
        v_normed[at, :] = normed
        out_x[at, :] = mm(normed, v_x[...]).astype(BF16)
        out_s[at, :] = mm(normed, v_s[...]).astype(BF16)

    def project_gate(chunk):
        at = pl.ds(pl.multiple_of(chunk * tokens, tokens), tokens)
        normed = v_normed[at, :]
        out_z[at, :] = mm(normed, v_z[...]).astype(BF16)
        out_t[chunk] = normed.T

    stores = [
        pltpu.make_async_copy(source, target, store_sem.at[i])
        for i, (source, target) in enumerate(
            (
                (v_x, w_x),
                (v_s, w_s),
                (v_small, small_out),
                (out_x, proj_x),
                (out_s, proj_s),
                (v_z, w_z),
                (out_z, proj_z),
                (out_t, normed_t),
            )
        )
    ]

    def after_first():
        for stream in phases[1]:
            start_stream(stream)
        to_row(0, hidden, v_hidden).wait_recv()
        pass_on(0, v_hidden).start()
        move_piece(False)
        to_row(1, cotangent, cotangent_all).start()
        to_core(1, cotangent, cotangent_all).start()
        to_row(0, hidden, v_hidden).wait_send()
        to_core(0, hidden, v_hidden).wait()
        pass_on(0, v_hidden).wait()

    def after_second():
        move_piece(True)
        for stream in phases[2]:
            start_stream(stream)
        to_row(1, cotangent, cotangent_all).wait_recv()
        pass_on(1, cotangent_all).start()

    def after_third():
        to_row(1, cotangent, cotangent_all).wait_send()
        to_core(1, cotangent, cotangent_all).wait()
        pass_on(1, cotangent_all).wait()
        keep_cotangent.wait()

    run_phase(0, None, after_first)
    for f in range(n):
        v_gain[:, f * r : (f + 1) * r] = v_small[f, 0:1, 0:r].astype(F32)
    for copy in stores[0:3]:
        copy.start()
    run_phase(1, project_first, after_second)
    for copy in stores[3:6]:
        copy.start()
    run_phase(2, project_gate, after_third)
    for copy in stores[6:]:
        copy.start()
    for copy in stores:
        copy.wait()


def gather_all(n, n_ctx, unit, direct, hidden, cotangent, in_weight_t, small, out_weight, shared_width):
    own, model = hidden.shape
    tokens = own * n_ctx
    width = out_weight.shape[0] * n // n_ctx
    rows = in_weight_t.shape[1]
    any_space = pl.BlockSpec(memory_space=pl.ANY)
    low = lambda *shape: jax.ShapeDtypeStruct(shape, BF16)
    v_low = lambda *shape: pltpu.VMEM(shape, BF16)
    dma = pltpu.SemaphoreType.DMA
    return pl.pallas_call(
        functools.partial(gather_kernel, n, n_ctx, unit, direct),
        in_specs=[any_space] * 5,
        out_specs=[any_space] * 10,
        out_shape=[
            low(n_ctx, own, model),
            low(model, width),
            low(model, shared_width),
            low(model, width),
            low(n, width // n, model),
            low(n, small.shape[0], small.shape[1]),
            low(tokens, width),
            low(tokens, shared_width),
            low(tokens, width),
            low(n_ctx, model, own),
        ],
        scratch_shapes=[
            v_low(n_ctx, own, model),
            v_low(tokens, model),
            v_low(model, width),
            v_low(model, shared_width),
            v_low(model, width),
            v_low(n, small.shape[0], small.shape[1]),
            v_low(width, rows),
            v_low(shared_width, rows),
            v_low(width, rows),
            v_low(tokens, width),
            v_low(tokens, shared_width),
            v_low(tokens, width),
            v_low(n_ctx, model, own),
            pltpu.VMEM((1, model), F32),
            dma((3,)),
            dma((2, width // (unit * HEAD))),
            dma,
            dma((8,)),
            dma((8, 2)),
            dma((8, 2, n - 1)),
            dma((2, 3)),
            dma((2, 3)),
            dma,
            dma,
        ],
        compiler_params=pltpu.CompilerParams(
            collective_id=0, has_side_effects=True, vmem_limit_bytes=56 * 1024 * 1024
        ),
        name="gather_all",
    )(hidden, cotangent, in_weight_t, small, out_weight)


def reduce_kernel(
    n,
    n_ctx,
    direct,
    normed_t,
    d_x,
    d_s,
    normed_parts,
    shard_o,
    shard_z,
    small,
    hidden,
    cotangent,
    gain,
    g_z,
    g_x,
    g_s,
    g_o,
    hidden_grad,
    small_out,
    v_normed_t,
    v_d_x,
    v_d_s,
    slot_x,
    slot_s,
    first_x,
    first_s,
    done_x,
    done_s,
    moved,
    mine,
    from_core,
    from_row,
    v_hidden,
    v_cotangent,
    v_gain,
    small_all,
    small_ctx,
    load_sem,
    store_sem,
    ring_send,
    ring_recv,
    ctx_send,
    ctx_recv,
    own_sem,
    piece_send,
    piece_recv,
    part_send,
    part_recv,
    small_send,
    small_recv,
    small_ctx_send,
    small_ctx_recv,
):
    ring = Ring(n)
    me, shard = ring.me, ring.shard
    around = Around(me, shard)
    piece_peer = (shard % n_ctx, shard // n_ctx * n_ctx + me)
    moves = shard % n_ctx != me
    barrier = pltpu.get_barrier_semaphore()

    def peer(offset):
        return (me, lax.rem(shard + offset, n))

    for device in around.all:
        greet(device)
    lax.fori_loop(1, n, lambda j, carry: (greet(peer(j)), carry)[1], 0)
    own = hidden.shape[0]
    sum_normed = TokenSum(around, normed_parts, mine, from_core, from_row, part_send, part_recv)
    loads = [
        pltpu.make_async_copy(source, target, load_sem.at[i])
        for i, (source, target) in enumerate(
            (
                *((normed_t.at[c], v_normed_t.at[:, pl.ds(c * own, own)]) for c in range(n_ctx)),
                (d_s, v_d_s),
                (d_x, v_d_x),
                *sum_normed.loads(),
                (hidden, v_hidden),
                (cotangent, v_cotangent),
                (gain, v_gain),
                (small, small_all.at[shard, pl.ds(0, small.shape[0])]),
            )
        )
    ]
    ring_loads = n_ctx + 2
    for copy in loads:
        copy.start()
    if direct:
        pl.semaphore_wait(barrier, n + 2)
    else:

        @pl.when(moves)
        def _():
            greet(piece_peer)
            pl.semaphore_wait(barrier, n + 3)

        @pl.when(jnp.logical_not(moves))
        def _():
            pl.semaphore_wait(barrier, n + 2)

    rows = v_normed_t.shape[0] // (2 * n)
    half = v_d_x.shape[1] // 2

    def in_stream(number, right, first, size, slots, stage, done):
        def partial(index, way):
            left = v_normed_t[pl.ds(pl.multiple_of((2 * index + way) * rows, 16), rows), :]
            return mm(left, right[:, first : first + size])

        return (
            number,
            partial,
            lambda way, step: slots.at[step, way, :, pl.ds(first, size)],
            lambda way: stage.at[way, :, pl.ds(first, size)],
            lambda way: done.at[pl.ds(first, size), pl.ds(way * rows, rows)],
        )

    streams = (
        in_stream(0, v_d_s, 0, v_d_s.shape[1], slot_s, first_s, done_s),
        in_stream(1, v_d_x, 0, half, slot_x, first_x, done_x),
        in_stream(2, v_d_x, half, half, slot_x, first_x, done_x),
    )

    def hop(stream, way, step, source):
        return remote(
            source,
            stream[2](way, step),
            ring_send.at[stream[0], way],
            ring_recv.at[stream[0], way, step],
            ring.neighbour(way),
        )

    def arrived(stream, way, step):
        partial = stream[1](ring.at(-step - 2 if way == 0 else step + 2), way)
        hop(stream, way, step, stream[3](way)).wait()
        return stream[2](way, step)[...].astype(F32) + partial

    ctx_pairs = ((shard_o if direct else moved, g_o), (shard_z, g_z), (done_x, g_x), (done_s, g_s))

    def share(i, kind):
        source, whole = ctx_pairs[i]
        at = me
        if kind == 2:
            source, at = whole.at[around.row_at], around.row_at
        device = around.row if kind == 0 else around.core
        return remote(source, whole.at[at], ctx_send.at[i, kind], ctx_recv.at[i, kind], device)

    def keep(i):
        source, whole = ctx_pairs[i]
        return pltpu.make_async_copy(source, whole.at[me], own_sem.at[i])

    def start_share(i):
        share(i, 0).start()
        share(i, 1).start()
        keep(i).start()

    def pass_share(i):
        share(i, 0).wait_recv()
        share(i, 2).start()

    def close_share(i):
        share(i, 0).wait_send()
        share(i, 1).wait()
        share(i, 2).wait()
        keep(i).wait()

    def move_piece(wait):
        if direct:
            return
        keep_piece = pltpu.make_async_copy(shard_o, moved, piece_send)
        send_piece = remote(shard_o, moved, piece_send, piece_recv, piece_peer)

        @pl.when(moves)
        def _():
            send_piece.wait() if wait else send_piece.start()

        @pl.when(jnp.logical_not(moves))
        def _():
            keep_piece.wait() if wait else keep_piece.start()

    def small_to(offset):
        return remote(
            small_all.at[shard],
            small_all.at[shard],
            small_send.at[offset - 1],
            small_recv.at[offset - 1],
            peer(offset),
        )

    def small_share(i):
        return remote(
            small_ctx.at[me], small_ctx.at[me], small_ctx_send.at[i], small_ctx_recv.at[i], around.all[i]
        )

    store_grad = pltpu.make_async_copy(v_cotangent, hidden_grad, store_sem.at[0])
    store_small = pltpu.make_async_copy(small_ctx, small_out, store_sem.at[1])

    def finish_tokens():
        resid = v_hidden[...].astype(F32)
        scale = lax.rsqrt(jnp.mean(resid * resid, axis=1, keepdims=True) + EPS)
        d_normed = sum_normed.total()
        f = v_gain[...] * d_normed
        slope = scale**3 * jnp.mean(resid * f, axis=1, keepdims=True)
        grad = v_cotangent[...].astype(F32) + scale * f - resid * slope
        v_cotangent[...] = grad.astype(BF16)
        store_grad.start()
        by_model = jnp.sum(d_normed * resid * scale, axis=0, keepdims=True)
        base, size = small.shape[0], d_x.shape[1]
        small_all[shard, base:, :] = jnp.zeros((small_all.shape[1] - base, small.shape[1]), F32)
        for j in range(by_model.shape[1] // size):
            small_all[shard, base + j : base + j + 1, 0:size] = by_model[
                :, j * size : (j + 1) * size
            ]
        lax.fori_loop(1, n, lambda j, carry: (small_to(j).start(), carry)[1], 0)

    def sum_small():
        lax.fori_loop(1, n, lambda j, carry: (small_to(j).wait(), carry)[1], 0)
        small_ctx[me] = jnp.sum(small_all[...], axis=0)
        for i in range(3):
            small_share(i).start()

    sum_normed.start()
    move_piece(False)
    for copy in loads[:ring_loads]:
        copy.wait()
    for stream in streams:
        for way in (0, 1):
            stage = stream[3](way)
            stage[...] = stream[1](ring.at(-1 if way == 0 else 1), way).astype(BF16)
            hop(stream, way, 0, stage).start()
    for copy in loads[ring_loads:]:
        copy.wait()
    sum_normed.pass_row()
    move_piece(True)
    start_share(0)
    start_share(1)

    def body(step, carry):
        for stream in streams:
            for way in (0, 1):
                total = arrived(stream, way, step)
                place = stream[2](way, step)
                place[...] = total.astype(BF16)
                hop(stream, way, step + 1, place).start()

        @pl.when(step == (n - 2) // 2)
        def _():
            finish_tokens()

        return carry

    lax.fori_loop(0, n - 2, body, 0)
    sum_small()
    pass_share(0)
    pass_share(1)
    for number in (1, 2, 0):
        for way in (0, 1):
            done = streams[number][4](way)
            done[...] = arrived(streams[number], way, n - 2).T.astype(BF16)
        if number == 2:
            start_share(2)
    start_share(3)
    for i in range(3):
        small_share(i).wait()
    store_small.start()
    pass_share(2)
    pass_share(3)
    for i in range(4):
        close_share(i)
    store_grad.wait()
    store_small.wait()


def reduce_all(
    n, n_ctx, direct, normed_t, d_x, d_s, normed_parts, shard_o, shard_z, small, hidden, cotangent, gain
):
    model, tokens = normed_t.shape[1], d_x.shape[0]
    width, shared_width = d_x.shape[1], d_s.shape[1]
    rows, piece, own = model // n, width // n, hidden.shape[0]
    small_rows, small_width = small.shape[0] + 8, small.shape[1]
    any_space = pl.BlockSpec(memory_space=pl.ANY)
    dma = pltpu.SemaphoreType.DMA
    low = lambda *shape: jax.ShapeDtypeStruct(shape, BF16)
    v_low = lambda *shape: pltpu.VMEM(shape, BF16)
    v_full = lambda *shape: pltpu.VMEM(shape, F32)
    return pl.pallas_call(
        functools.partial(reduce_kernel, n, n_ctx, direct),
        in_specs=[any_space] * 10,
        out_specs=[any_space] * 6,
        out_shape=[
            low(n_ctx, 2, width, rows // 2),
            low(n_ctx, width, rows),
            low(n_ctx, shared_width, rows),
            low(n_ctx, piece, model),
            low(own, model),
            jax.ShapeDtypeStruct((n_ctx, small_rows, small_width), F32),
        ],
        scratch_shapes=[
            v_low(model, tokens),
            v_low(tokens, width),
            v_low(tokens, shared_width),
            v_low(n - 1, 2, rows // 2, width),
            v_low(n - 1, 2, rows // 2, shared_width),
            v_low(2, rows // 2, width),
            v_low(2, rows // 2, shared_width),
            v_low(width, rows),
            v_low(shared_width, rows),
            v_low(piece, model),
            v_low(2, own, model),
            v_low(2, own, model),
            v_low(own, model),
            v_low(own, model),
            v_low(own, model),
            v_full(1, model),
            v_full(n, small_rows, small_width),
            v_full(n_ctx, small_rows, small_width),
            dma((8 + n_ctx,)),
            dma((2,)),
            dma((3, 2)),
            dma((3, 2, n - 1)),
            dma((4, 3)),
            dma((4, 3)),
            dma((4,)),
            dma,
            dma,
            dma((3,)),
            dma((3,)),
            dma((n - 1,)),
            dma((n - 1,)),
            dma((3,)),
            dma((3,)),
        ],
        compiler_params=pltpu.CompilerParams(
            collective_id=1, has_side_effects=True, vmem_limit_bytes=56 * 1024 * 1024
        ),
        name="reduce_all",
    )(
        normed_t, d_x, d_s, normed_parts, shard_o, shard_z, small, hidden, cotangent, gain
    )


def assemble_kernel(part, z_ref, x_ref, s_ref, out_ref):
    place = pl.program_id(0)
    n_ctx, size, half = x_ref.shape[0], x_ref.shape[1], z_ref.shape[3]

    def interleave(write):
        for a in range(size // part):
            for c in range(n_ctx):
                write(
                    slice((a * n_ctx + c) * part, (a * n_ctx + c + 1) * part),
                    c,
                    slice(a * part, (a + 1) * part),
                )

    def write_z(target, c, source):
        for way in (0, 1):
            out_ref[target, way * half : (way + 1) * half] = z_ref[c, way, source, :].astype(F32)

    def write_x(target, c, source):
        out_ref[target, :] = x_ref[c, source, :].astype(F32)

    @pl.when(place < n_ctx)
    def _():
        interleave(write_z)

    @pl.when(jnp.logical_and(place >= n_ctx, place < 2 * n_ctx))
    def _():
        interleave(write_x)

    @pl.when(place == 2 * n_ctx)
    def _():
        total = s_ref[0].astype(F32)
        for c in range(1, n_ctx):
            total += s_ref[c].astype(F32)
        out_ref[0 : total.shape[0], :] = total


def assemble(part, g_z, g_x, g_s, columns):
    n_ctx, width, rows = g_x.shape
    block = (n_ctx, width // n_ctx, rows)
    return pl.pallas_call(
        functools.partial(assemble_kernel, part),
        grid=(2 * n_ctx + 1,),
        in_specs=[
            pl.BlockSpec(
                (n_ctx, 2, width // n_ctx, rows // 2),
                lambda i: (0, 0, jnp.minimum(i, n_ctx - 1), 0),
            ),
            pl.BlockSpec(block, lambda i: (0, jnp.clip(i - n_ctx, 0, n_ctx - 1), 0)),
            pl.BlockSpec(g_s.shape, lambda i: (0, 0, 0)),
        ],
        out_specs=pl.BlockSpec((width, rows), lambda i: (i, 0)),
        out_shape=jax.ShapeDtypeStruct((columns, rows), F32),
        compiler_params=pltpu.CompilerParams(vmem_limit_bytes=58 * 1024 * 1024),
        name="assemble",
    )(g_z, g_x, g_s)


def on_device(
    hidden,
    cotangent,
    seq_lens,
    norm_gain,
    in_weight,
    conv_weight,
    conv_bias,
    dt_bias,
    a_log,
    d_skip,
    gate_gain,
    out_weight,
):
    n_ctx, n_fsdp = lax.axis_size("ctx"), lax.axis_size("fsdp")
    me, shard = lax.axis_index("ctx"), lax.axis_index("fsdp")
    taps = conv_weight.shape[0]
    heads_all = dt_bias.shape[0] * n_fsdp
    inner = out_weight.shape[0] * n_fsdp
    heads, width = heads_all // n_ctx, inner // n_ctx
    model = hidden.shape[2]
    both = 2 * STATE
    held = dt_bias.shape[0]
    direct = held % n_ctx == 0
    unit = held // n_ctx if direct else 1
    part = unit * HEAD
    shared_width = -(-(both + heads_all) // LANES) * LANES

    per_head = jnp.concatenate([dt_bias, a_log, d_skip])
    lines = [norm_gain[None], conv_weight, conv_bias[None], gate_gain[None], per_head[None]]
    longest = -(-max(a.shape[1] for a in lines) // LANES) * LANES
    small = jnp.concatenate([jnp.pad(a, ((0, 0), (0, longest - a.shape[1]))) for a in lines])
    small = jnp.pad(small, ((0, SMALL_ROWS - small.shape[0]), (0, 0)))
    upstream, w_x, w_s, w_z, w_o, small_all, proj_x, proj_s, proj_z, normed_t = gather_all(
        n_fsdp, n_ctx, unit, direct, hidden[0], cotangent[0], in_weight.T, small, out_weight, shared_width
    )
    w_o = w_o.reshape(-1, model)

    def line(first, count, size):
        rows = small_all[:, first : first + count, :size]
        return jnp.moveaxis(rows, 0, 1).reshape(count, -1).astype(F32)

    def own(lines, size):
        by_part = lines.reshape(lines.shape[0], -1, n_ctx, size)
        return lax.dynamic_index_in_dim(by_part, me, 2, False).reshape(lines.shape[0], -1)

    gain_norm = line(0, 1, norm_gain.shape[0])
    conv_lines = line(1, taps + 1, conv_bias.shape[0])
    taps_x, taps_s = own(conv_lines[:, :inner], part), conv_lines[:, inner:]
    gain_gate = own(line(taps + 2, 1, gate_gain.shape[0]), part)
    each = small_all[:, taps + 3, : per_head.shape[0]].reshape(n_fsdp, 3, -1)
    each = own(jnp.moveaxis(each, 0, 1).reshape(3, -1).astype(F32), unit)
    head = jnp.pad(jnp.stack([each[0], jnp.exp(each[1])]), ((0, 0), (0, LANES - heads)))
    skip = jnp.repeat(each[2], HEAD)[None]

    *kept_parts, y, d_yn, stats = scan_forward(
        unit, n_ctx, seq_lens, proj_x, proj_s, proj_z, upstream, w_o, taps_x, taps_s, gain_gate, skip, head
    )
    gate_t, mixed_parts, d_z, d_ssd, gain_grads = gate_norm(
        inner, seq_lens, stats, proj_z, y, d_yn, w_o, gain_gate
    )
    normed_parts, d_x, d_s, small_grads, shard_o, shard_z, layer_out = scan_backward(
        n_fsdp, unit, n_ctx, proj_x, proj_s, kept_parts, d_ssd, w_z, w_x, w_s, gate_t, normed_t, upstream, d_z, mixed_parts, hidden[0], gain_grads, taps_x, taps_s, skip, head
    )
    g_z, g_x, g_s, g_o, hidden_grad, sums = reduce_all(
        n_fsdp, n_ctx, direct, normed_t, d_x, d_s, normed_parts, shard_o, shard_z, small_grads, hidden[0], cotangent[0], gain_norm
    )
    grad_in_weight = assemble(part, g_z, g_x, g_s, 2 * inner + both + heads_all).T
    grad_out_weight = g_o.reshape(-1, model).astype(F32)

    def shard_of(lines):
        size = lines.shape[1] // n_fsdp
        return lax.dynamic_slice_in_dim(lines, shard * size, size, axis=1)

    def in_order(sums_of, size):
        lines = sums_of.shape[1]
        by_part = sums_of.reshape(n_ctx, lines, -1, size)
        return jnp.transpose(by_part, (1, 2, 0, 3)).reshape(lines, -1)

    conv_sums = shard_of(
        jnp.concatenate(
            [
                in_order(sums[:, : taps + 1, :width], part),
                jnp.sum(sums[:, : taps + 1, width:], axis=0),
            ],
            axis=1,
        )
    )
    gate_sums = shard_of(in_order(sums[:, taps + 1 : taps + 2, :width], part))
    head_sums_all = sums[:, taps + 2, : 3 * LANES].reshape(n_ctx, 3, LANES)[:, :, :heads]
    head_grads = shard_of(in_order(head_sums_all, unit))
    norm_sums = jnp.sum(sums[:, 8 : 8 + model // width, :width], axis=0).reshape(1, -1)
    return (
        layer_out[None],
        hidden_grad[None],
        shard_of(norm_sums)[0],
        grad_in_weight,
        conv_sums[:taps],
        conv_sums[taps],
        head_grads[0],
        head_grads[1],
        head_grads[2],
        gate_sums[0],
        grad_out_weight,
    )


def solution(mesh):
    tokens, rows, flat = P("fsdp", "ctx", None), P("fsdp", None), P("fsdp")
    taps = P(None, "fsdp")
    return jax.shard_map(
        on_device,
        mesh=mesh,
        in_specs=(tokens, tokens, flat, flat, rows, taps, flat, flat, flat, flat, flat, rows),
        out_specs=(tokens, tokens, flat, rows, taps, flat, flat, flat, flat, flat, rows),
        check_vma=False,
    )
```

```python
import functools

import jax
import jax.numpy as jnp
from jax import lax
from jax.experimental import pallas as pl
from jax.experimental.pallas import tpu as pltpu
from jax.sharding import PartitionSpec as P

HEAD = 64
STATE = 128
BLOCK = 256
LANES = 128
POINTS = 4
EPS = 1e-05
F32 = jnp.float32
BF16 = jnp.bfloat16


def mm(a, b, contract=((1,), (0,))):
    return lax.dot_general(a, b, (contract, ((), ())), preferred_element_type=F32)


def mm_exact(a, b, contract=((1,), (0,))):
    return lax.dot_general(
        a, b, (contract, ((), ())), precision=lax.Precision.HIGHEST, preferred_element_type=F32
    )


def iota2(shape, axis):
    return lax.broadcasted_iota(jnp.int32, shape, axis)


def levels(lam, step):
    tri = (iota2((BLOCK, BLOCK), 0) >= iota2((BLOCK, BLOCK), 1)).astype(F32)
    level = mm_exact(tri, lam)
    across = level.T
    last = level[BLOCK - 1 : BLOCK, :]
    weight = jnp.exp(level - last) * step
    return level, across, jnp.exp(-last), weight, jnp.exp(-level)


def pair_of(array, first, low_half):
    return jnp.where(low_half, array[:, first : first + 1], array[:, first + 1 : first + 2])


def spread(level, across, head):
    return jnp.exp(-jnp.abs(level[:, head : head + 1] - across[head : head + 1, :]))


def silu_and_slope(v):
    s = jax.nn.sigmoid(v)
    return v * s, s * (1.0 + v * (1.0 - s))


def chosen_heads(me, heads, unit, n_ctx, turned=False):
    here, there = iota2((LANES, LANES), 1), iota2((LANES, LANES), 0)
    if turned:
        here, there = there, here
    head = (here // unit * n_ctx + me) * unit + here % unit
    return jnp.where(jnp.logical_and(there == head, here < heads), 1.0, 0.0).astype(BF16)


def column_valid(length_ref, block):
    at = iota2((BLOCK, 1), 0) + block * BLOCK
    return (at < length_ref[0]).astype(F32)


def forward_kernel(
    heads,
    unit,
    n_ctx,
    length_ref,
    px_ref,
    ps_ref,
    pz_ref,
    up_ref,
    w_o,
    taps_x_ref,
    taps_s_ref,
    gate_gain_ref,
    skip_ref,
    head_ref,
    x_ref,
    b_ref,
    c_ref,
    slope_x_ref,
    slope_s_ref,
    lam_ref,
    step_ref,
    chain_ref,
    kept_ref,
    y_ref,
    dyn_ref,
    stat_ref,
    state,
    before_x,
    before_s,
    v_o,
    load_sem,
):
    block = pl.program_id(0)
    load = pltpu.make_async_copy(w_o, v_o, load_sem)

    @pl.when(block == 0)
    def _():
        load.start()
        state[...] = jnp.zeros_like(state)
        before_x[...] = jnp.zeros_like(before_x)
        before_s[...] = jnp.zeros_like(before_s)

    valid = column_valid(length_ref, block)
    low_half = iota2((1, LANES), 1) < HEAD
    taps = taps_x_ref.shape[0] - 1

    def conv(current, before, weight):
        padded = jnp.concatenate([before, current], axis=0)
        total = weight[taps : taps + 1]
        for k in range(taps):
            first = 8 - (taps - 1) + k
            total = total + weight[k : k + 1] * padded[first : first + BLOCK]
        return silu_and_slope(total)

    shared = ps_ref[...].astype(F32)
    both = shared[:, : 2 * STATE]
    active, slope = conv(both, before_s[...], taps_s_ref[...])
    before_s[...] = both[BLOCK - 8 :]
    slope_s_ref[...] = slope.astype(BF16)
    rows_b, rows_c = active[:, :STATE].astype(BF16), active[:, STATE:].astype(BF16)
    b_ref[...] = rows_b
    c_ref[...] = rows_c
    chosen = chosen_heads(lax.axis_index("ctx"), heads, unit, n_ctx)
    raw = mm(ps_ref[:, 2 * STATE :], chosen)
    raw = raw + head_ref[0:1]
    own = iota2((1, LANES), 1) < heads
    step = jnp.where(own, valid * jax.nn.softplus(raw), 0.0)
    lam = step * head_ref[1:2]
    step_ref[...] = step
    lam_ref[...] = lam
    chain_ref[...] = jnp.where(own, valid * jax.nn.sigmoid(raw), 0.0)

    gram = mm(rows_c, rows_b, ((1,), (1,)))
    level, across, last, weight, fade = levels(lam, step)
    kept_ref[0] = state[...].astype(BF16)
    entering = mm(rows_c, state[...].astype(BF16))
    by_state = rows_b.T
    squares = jnp.zeros((BLOCK, LANES), F32)
    for first in range(0, heads, 2):
        lanes = slice(first * HEAD, (first + 2) * HEAD)
        current = px_ref[:, lanes].astype(F32)
        active, slope = conv(current, before_x[:, lanes], taps_x_ref[:, lanes])
        before_x[:, lanes] = current[BLOCK - 8 :]
        slope_x_ref[:, lanes] = slope.astype(BF16)
        x_low = active.astype(BF16)
        x_ref[:, lanes] = x_low
        x = x_low.astype(F32)
        scaled = x * pair_of(step, first, low_half)
        total = pair_of(fade, first, low_half) * entering[:, lanes] + skip_ref[:, lanes] * x
        for head, keep in ((first, low_half), (first + 1, jnp.logical_not(low_half))):
            mixing = (gram * spread(level, across, head)).astype(BF16)
            total += mm(mixing, jnp.where(keep, scaled, 0.0).astype(BF16))
        y_ref[:, lanes] = total
        update = mm(by_state, (x * pair_of(weight, first, low_half)).astype(BF16))
        state[:, lanes] = state[:, lanes] * pair_of(last, first, low_half) + update
        gated = total * jax.nn.silu(pz_ref[:, lanes].astype(F32))
        squares += gated * gated

    @pl.when(block == 0)
    def _():
        load.wait()

    d_yn = valid * mm(up_ref[0], v_o[...], ((1,), (1,)))
    dyn_ref[...] = d_yn
    gated = y_ref[...] * jax.nn.silu(pz_ref[...].astype(F32))
    terms = gate_gain_ref[...] * d_yn * gated
    square = jnp.sum(squares, axis=1, keepdims=True)
    along = jnp.sum(terms, axis=1, keepdims=True)
    lane = iota2((1, LANES), 1)
    both_sums = jnp.where(lane == 0, square, 0.0) + jnp.where(lane == 1, along, 0.0)
    stat_ref[...] = both_sums.T[0:8]


def scan_forward(unit, n_ctx, length, px, ps, pz, upstream, w_o, taps_x, taps_s, gate_gain, skip, head):
    tokens, width = px.shape
    heads = width // HEAD
    count = tokens // BLOCK
    model = w_o.shape[1]
    by_block = lambda i: (i, 0)
    at_block = lambda size: pl.BlockSpec((BLOCK, size), by_block)
    whole = lambda a: pl.BlockSpec(a.shape, lambda i: (0, 0))
    low = lambda *shape: jax.ShapeDtypeStruct(shape, BF16)
    full = lambda *shape: jax.ShapeDtypeStruct(shape, F32)
    return pl.pallas_call(
        functools.partial(forward_kernel, heads, unit, n_ctx),
        grid=(count,),
        in_specs=[
            pl.BlockSpec(memory_space=pltpu.SMEM),
            at_block(width),
            at_block(ps.shape[1]),
            at_block(width),
            pl.BlockSpec((1, BLOCK, model), lambda i: (i, 0, 0)),
            pl.BlockSpec(memory_space=pl.ANY),
            whole(taps_x),
            whole(taps_s),
            whole(gate_gain),
            whole(skip),
            whole(head),
        ],
        out_specs=[
            at_block(width),
            at_block(STATE),
            at_block(STATE),
            at_block(width),
            at_block(2 * STATE),
            at_block(LANES),
            at_block(LANES),
            at_block(LANES),
            pl.BlockSpec((1, STATE, width), lambda i: (i, 0, 0)),
            at_block(width),
            at_block(width),
            pl.BlockSpec((8, BLOCK), lambda i: (0, i)),
        ],
        out_shape=[
            low(tokens, width),
            low(tokens, STATE),
            low(tokens, STATE),
            low(tokens, width),
            low(tokens, 2 * STATE),
            full(tokens, LANES),
            full(tokens, LANES),
            full(tokens, LANES),
            low(count, STATE, width),
            full(tokens, width),
            full(tokens, width),
            full(8, tokens),
        ],
        scratch_shapes=[
            pltpu.VMEM((STATE, width), F32),
            pltpu.VMEM((8, width), F32),
            pltpu.VMEM((8, 2 * STATE), F32),
            pltpu.VMEM(w_o.shape, BF16),
            pltpu.SemaphoreType.DMA,
        ],
        compiler_params=pltpu.CompilerParams(vmem_limit_bytes=56 * 1024 * 1024),
        cost_estimate=pl.CostEstimate(
            flops=2 * tokens * width * (2 * BLOCK + 2 * STATE + model),
            bytes_accessed=tokens * width * 24,
            transcendentals=tokens * heads * BLOCK,
        ),
        name="scan_forward",
    )(length, px, ps, pz, upstream, w_o, taps_x, taps_s, gate_gain, skip, head)


def head_sums(product, chooser):
    high = product.astype(BF16)
    rest = (product - high.astype(F32)).astype(BF16)
    return mm(high, chooser) + mm(rest, chooser)


MESH = pl.DeviceIdType.MESH
SMALL_ROWS = 32


def ring_place(index, half):
    a, b = index // 2, index % 2
    return a + b * (2 * half - 1 - 2 * a)


def ring_index(place, half):
    b = place // half
    return 2 * (place + b * (2 * half - 1 - 2 * place)) + b


class Ring:
    def __init__(self, n):
        self.n, self.half = n, n // 2
        self.me, self.shard = lax.axis_index("ctx"), lax.axis_index("fsdp")
        self.place = ring_place(self.shard, self.half)

    def at(self, steps):
        return ring_index(lax.rem(self.place + steps + 2 * self.n, self.n), self.half)

    def neighbour(self, way):
        return (self.me, self.at(1 if way == 0 else -1))


def remote(source, target, send, recv, device):
    return pltpu.make_async_remote_copy(
        src_ref=source,
        dst_ref=target,
        send_sem=send,
        recv_sem=recv,
        device_id=device,
        device_id_type=MESH,
    )


def greet(device):
    pl.semaphore_signal(pltpu.get_barrier_semaphore(), inc=1, device_id=device, device_id_type=MESH)


class Around:
    def __init__(self, me, shard):
        core, row = me % 2, me // 2
        self.me = me
        self.core_at = me + 1 - 2 * core
        self.row_at = me + 2 - 4 * row
        self.both_at = self.row_at + 1 - 2 * core
        self.core, self.row, self.both = (
            (at, shard) for at in (self.core_at, self.row_at, self.both_at)
        )
        self.all = (self.core, self.row, self.both)


class TokenSum:
    def __init__(self, around, parts, own_part, row_part, from_core, from_row, send, recv):
        self.around, self.parts, self.own_part, self.row_part = around, parts, own_part, row_part
        self.from_core, self.from_row, self.send, self.recv = from_core, from_row, send, recv

    def loads(self):
        at = self.around
        return (
            (self.parts.at[at.row_at], self.row_part),
            (self.parts.at[at.me], self.own_part),
        )

    def to_core(self, which):
        at = self.around
        return remote(
            self.parts.at[(at.core_at, at.both_at)[which]],
            self.from_core.at[which],
            self.send.at[which],
            self.recv.at[which],
            at.core,
        )

    def to_row(self):
        return remote(
            self.row_part, self.from_row, self.send.at[2], self.recv.at[2], self.around.row
        )

    def start(self):
        self.to_core(1).start()
        self.to_core(0).start()

    def pass_row(self):
        self.to_core(1).wait()
        total = self.row_part[...].astype(F32) + self.from_core[1].astype(F32)
        self.row_part[...] = total.astype(BF16)
        self.to_row().start()

    def total(self):
        self.to_core(0).wait()
        self.to_row().wait()
        return (
            self.own_part[...].astype(F32)
            + self.from_core[0].astype(F32)
            + self.from_row[...].astype(F32)
        )


class SmallSum:
    def __init__(self, n, around, whole, sums, send, recv, ctx_send, ctx_recv):
        self.n, self.around, self.whole, self.sums = n, around, whole, sums
        self.send, self.recv, self.ctx_send, self.ctx_recv = send, recv, ctx_send, ctx_recv
        self.shard = lax.axis_index("fsdp")

    def to_peer(self, offset):
        own = self.whole.at[self.shard]
        peer = (self.around.me, lax.rem(self.shard + offset, self.n))
        return remote(own, own, self.send.at[offset - 1], self.recv.at[offset - 1], peer)

    def to_ctx(self, i):
        own = self.sums.at[self.around.me]
        return remote(own, own, self.ctx_send.at[i], self.ctx_recv.at[i], self.around.all[i])

    def start(self):
        lax.fori_loop(1, self.n, lambda j, carry: (self.to_peer(j).start(), carry)[1], 0)

    def add(self):
        lax.fori_loop(1, self.n, lambda j, carry: (self.to_peer(j).wait(), carry)[1], 0)
        self.sums[self.around.me] = jnp.sum(self.whole[...], axis=0)
        for i in range(3):
            self.to_ctx(i).start()

    def finish(self):
        for i in range(3):
            self.to_ctx(i).wait()


def gate_kernel(
    heads,
    channels,
    length_ref,
    stats,
    pz_ref,
    y_ref,
    dyn_ref,
    w_o,
    gate_gain_ref,
    ynt_ref,
    mixed_ref,
    dz_ref,
    dssd_ref,
    gain_ref,
    stat_all,
    columns,
    v_y,
    v_o,
    load_sem,
    stat_send,
    stat_recv,
):
    block = pl.program_id(0)
    me = lax.axis_index("ctx")
    around = Around(me, lax.axis_index("fsdp"))
    load = pltpu.make_async_copy(w_o, v_o, load_sem.at[0])

    @pl.when(block == 0)
    def _():
        for device in around.all:
            greet(device)
        load.start()
        own = pltpu.make_async_copy(stats, stat_all.at[me], load_sem.at[1])
        own.start()
        own.wait()
        pl.semaphore_wait(pltpu.get_barrier_semaphore(), 3)
        copies = [
            remote(stat_all.at[me], stat_all.at[me], stat_send.at[i], stat_recv.at[i], device)
            for i, device in enumerate(around.all)
        ]
        for copy in copies:
            copy.start()
        for copy in copies:
            copy.wait()
        total = jnp.sum(stat_all[...], axis=0)
        for i in range(total.shape[1] // BLOCK):
            columns[i] = total[:, i * BLOCK : (i + 1) * BLOCK].T
        gain_ref[...] = jnp.zeros_like(gain_ref)
        load.wait()

    valid = column_valid(length_ref, block)
    sums = columns[block]
    scale = lax.rsqrt(sums[:, 0:1] / channels + EPS)
    slant = scale * scale * scale * sums[:, 1:2] / channels
    for first in range(0, heads, 2):
        lanes = slice(first * HEAD, (first + 2) * HEAD)
        gate, gate_slope = silu_and_slope(pz_ref[:, lanes].astype(F32))
        mixed = y_ref[:, lanes]
        d_yn = dyn_ref[:, lanes]
        gain = gate_gain_ref[:, lanes]
        gated = mixed * gate
        scaled = gated * scale
        v_y[:, lanes] = (valid * (scaled * gain)).astype(BF16)
        gain_ref[0:1, lanes] += jnp.sum(d_yn * scaled, axis=0, keepdims=True)
        d_gated = scale * (gain * d_yn) - gated * slant
        dz_ref[:, lanes] = (d_gated * mixed * gate_slope).astype(BF16)
        dssd_ref[:, lanes] = (d_gated * gate).astype(BF16)
    normed_gate = v_y[...]
    ynt_ref[...] = normed_gate.T
    mixed_ref[0] = mm(normed_gate, v_o[...]).astype(BF16)


def gate_norm(channels, length, stats, pz, y, d_yn, w_o, gate_gain):
    tokens, width = pz.shape
    count, model = tokens // BLOCK, w_o.shape[1]
    n_ctx = channels // width
    at_block = lambda size: pl.BlockSpec((BLOCK, size), lambda i: (i, 0))
    any_space = pl.BlockSpec(memory_space=pl.ANY)
    low = lambda *shape: jax.ShapeDtypeStruct(shape, BF16)
    return pl.pallas_call(
        functools.partial(gate_kernel, width // HEAD, channels),
        grid=(count,),
        in_specs=[
            pl.BlockSpec(memory_space=pltpu.SMEM),
            any_space,
            at_block(width),
            at_block(width),
            at_block(width),
            any_space,
            pl.BlockSpec(gate_gain.shape, lambda i: (0, 0)),
        ],
        out_specs=[
            pl.BlockSpec((width, BLOCK), lambda i: (0, i)),
            pl.BlockSpec((1, BLOCK, model), lambda i: (i, 0, 0)),
            at_block(width),
            at_block(width),
            pl.BlockSpec((8, width), lambda i: (0, 0)),
        ],
        out_shape=[
            low(width, tokens),
            low(count, BLOCK, model),
            low(tokens, width),
            low(tokens, width),
            jax.ShapeDtypeStruct((8, width), F32),
        ],
        scratch_shapes=[
            pltpu.VMEM((n_ctx, 8, tokens), F32),
            pltpu.VMEM((count, BLOCK, 8), F32),
            pltpu.VMEM((BLOCK, width), BF16),
            pltpu.VMEM(w_o.shape, BF16),
            pltpu.SemaphoreType.DMA((2,)),
            pltpu.SemaphoreType.DMA((3,)),
            pltpu.SemaphoreType.DMA((3,)),
        ],
        compiler_params=pltpu.CompilerParams(
            collective_id=2, has_side_effects=True, vmem_limit_bytes=56 * 1024 * 1024
        ),
        name="gate_norm",
    )(length, stats, pz, y, d_yn, w_o, gate_gain)


def backward_kernel(
    heads,
    unit,
    n_ctx,
    n,
    px_ref,
    ps_ref,
    x_ref,
    b_ref,
    c_ref,
    slope_x_ref,
    slope_s_ref,
    lam_ref,
    step_ref,
    chain_ref,
    kept_ref,
    dssd_ref,
    gate_t,
    normed_t,
    upstream,
    d_z,
    mixed_parts,
    hidden,
    gain_grads_ref,
    taps_x_ref,
    taps_s_ref,
    skip_ref,
    head_ref,
    dx_ref,
    ds_ref,
    small_ref,
    shard_o,
    shard_z,
    layer_out,
    back,
    mixed_grads,
    for_step,
    for_level,
    left,
    right,
    sums,
    after_x,
    after_s,
    v_left,
    v_right,
    products,
    slots,
    stage,
    done_o,
    done_z,
    mine,
    from_core,
    from_row,
    v_hidden,
    load_sem,
    store_sem,
    ring_send,
    ring_recv,
    part_send,
    part_recv,
):
    turn = pl.program_id(0)
    turns = heads // 2 // POINTS
    block = pl.num_programs(0) - 1 - turn
    width, model = x_ref.shape[1], v_hidden.shape[1]
    own = hidden.shape[0]
    ring = Ring(n)
    around = Around(ring.me, ring.shard)
    piece, size = slots.shape[4], slots.shape[5]
    sum_mixed = TokenSum(
        around, mixed_parts, mine.at[0], mine.at[1], from_core, from_row, part_send, part_recv
    )
    loads = [
        pltpu.make_async_copy(source, target, load_sem.at[i])
        for i, (source, target) in enumerate(
            (
                (gate_t, v_left.at[pl.ds(0, width)]),
                *((upstream.at[c], v_right.at[pl.ds(c * own, own), pl.ds(0, model)]) for c in range(n_ctx)),
                *((normed_t.at[c], v_left.at[pl.ds(width, model), pl.ds(c * own, own)]) for c in range(n_ctx)),
                (d_z, v_right.at[:, pl.ds(model, width)]),
                *sum_mixed.loads(),
                (hidden, v_hidden),
            )
        )
    ]
    ring_loads = 2 + 2 * n_ctx

    def partial_sum(kind, way, sub, index):
        first = (1 - kind) * index * piece + kind * (width + (2 * index + way) * piece)
        at = (1 - kind) * (2 * way + sub) * size + kind * (model + sub * size)
        return mm(
            v_left[pl.ds(pl.multiple_of(first, 16), piece), :],
            v_right[:, pl.ds(pl.multiple_of(at, LANES), size)],
        )

    def all_products():
        tile = max(2 * piece, BLOCK)
        shards = tile // (2 * piece)

        def out_rows(i, carry):
            rows = pl.ds(pl.multiple_of(i * BLOCK, BLOCK), BLOCK)
            left = v_left[rows, :]
            products[rows, 0:width] = mm(left, v_right[:, 0:width]).astype(BF16)
            products[rows, width:model] = mm(left, v_right[:, width:model]).astype(BF16)
            return carry

        def in_rows(i, carry):
            left = v_left[pl.ds(pl.multiple_of(width + i * tile, 16), tile), :]
            both = mm(left, v_right[:, model:]).astype(BF16)
            for j in range(shards):
                place = pl.ds(pl.multiple_of((i * shards + j) * piece, 16), piece)
                for way in (0, 1):
                    products[place, model + way * width : model + (way + 1) * width] = both[
                        (2 * j + way) * piece : (2 * j + way + 1) * piece
                    ]
            return carry

        lax.fori_loop(0, width // BLOCK, out_rows, 0)
        lax.fori_loop(0, model // tile, in_rows, 0)

    def product(kind, way, sub, index):
        at = pl.multiple_of(kind * model + way * width + sub * size, LANES)
        return products[pl.ds(pl.multiple_of(index * piece, 16), piece), pl.ds(at, size)]

    def hop(kind, way, sub, step, source):
        return remote(
            source,
            slots.at[kind, step, way, sub],
            ring_send.at[kind, way, sub],
            ring_recv.at[kind, way, sub, step],
            (ring.me, ring.at(1 - 2 * way)),
        )

    def streams(body):
        def one(e, carry):
            body(e // 4, e // 2 % 2, e % 2)
            return carry

        lax.fori_loop(0, 8, one, 0)

    def start_ring(kind, way, sub):
        place = stage.at[kind, way, sub]
        place[...] = partial_sum(kind, way, sub, ring.at(2 * way - 1)).astype(BF16)
        hop(kind, way, sub, 0, place).start()

    def ring_step(step):
        def body(kind, way, sub):
            index = ring.at((step + 2) * (2 * way - 1))
            hop(kind, way, sub, step, stage.at[kind, way, sub]).wait()
            place = slots.at[kind, step, way, sub]
            total = place[...].astype(F32) + product(kind, way, sub, index).astype(F32)

            @pl.when(step < n - 2)
            def _():
                place[...] = total.astype(BF16)
                hop(kind, way, sub, step + 1, place).start()

            @pl.when(jnp.logical_and(step == n - 2, kind == 0))
            def _():
                at = pl.multiple_of((2 * way + sub) * size, LANES)
                done_o[:, pl.ds(at, size)] = total.astype(BF16)

            @pl.when(jnp.logical_and(step == n - 2, kind == 1))
            def _():
                done_z[way, pl.ds(pl.multiple_of(sub * size, 16), size), :] = total.T.astype(BF16)

        streams(body)

    def serve(point):
        at = turn * POINTS + point
        points = POINTS * n_ctx
        lax.fori_loop(
            at * (n - 1) // points,
            (at + 1) * (n - 1) // points,
            lambda step, carry: (ring_step(step), carry)[1],
            0,
        )

    @pl.when(turn == 0)
    def _():
        for device in around.all:
            greet(device)
        greet(ring.neighbour(0))
        greet(ring.neighbour(1))
        for copy in loads:
            copy.start()
        back[...] = jnp.zeros_like(back)
        small_ref[...] = jnp.zeros_like(small_ref)
        small_ref[taps_x_ref.shape[0] : taps_x_ref.shape[0] + 1, 0:width] = gain_grads_ref[0:1, :]
        after_x[...] = jnp.zeros_like(after_x)
        after_s[...] = jnp.zeros_like(after_s)
        pl.semaphore_wait(pltpu.get_barrier_semaphore(), 5)
        for copy in loads[:ring_loads]:
            copy.wait()
        streams(start_ring)
        sum_mixed.start()
        all_products()
        for copy in loads[ring_loads:]:
            copy.wait()

    @pl.when(turn == 1)
    def _():
        sum_mixed.pass_row()

    taps = taps_x_ref.shape[0] - 1

    rows_b, rows_c = b_ref[...], c_ref[...]
    step = step_ref[...]
    lam = lam_ref[...]
    gram = mm(rows_c, rows_b, ((1,), (1,)))
    gram_t = mm(rows_b, rows_c, ((1,), (1,)))
    level, across, last, weight, fade = levels(lam, step)
    out_decay = jnp.exp(level - level[BLOCK - 1 : BLOCK, :])
    step_across = step.T
    at_row, at_col = iota2((BLOCK, BLOCK), 0), iota2((BLOCK, BLOCK), 1)
    order = (at_row > at_col).astype(F32) - (at_row < at_col).astype(F32)
    low_half = iota2((1, LANES), 1) < HEAD
    lane = iota2((1, LANES), 1)
    by_state = rows_c.T
    kept = kept_ref[0]
    old_back = back[...].astype(BF16)
    entering = mm(rows_c, kept)
    leaving = mm(rows_b, old_back)
    at_last = jnp.sum(kept.astype(F32) * back[...], axis=0, keepdims=True)
    mixed_grads[...] = jnp.zeros_like(mixed_grads)
    left[...] = jnp.zeros_like(left)
    right[...] = jnp.zeros_like(right)
    sums[...] = jnp.zeros_like(sums)
    d_b = jnp.zeros((BLOCK, STATE), F32)
    d_c = jnp.zeros((BLOCK, STATE), F32)

    def conv_back(d_conv, after, current, weight):
        padded = jnp.concatenate([d_conv, after], axis=0)
        d_in = jnp.zeros_like(d_conv)
        grads = []
        for k in range(taps):
            moved = padded[taps - 1 - k : taps - 1 - k + BLOCK]
            d_in += weight[k : k + 1] * moved
            grads.append(jnp.sum(current * moved, axis=0, keepdims=True))
        grads.append(jnp.sum(d_conv, axis=0, keepdims=True))
        return d_in, jnp.concatenate(grads, axis=0)

    for first in range(0, heads, 2):
        lanes = slice(first * HEAD, (first + 2) * HEAD)
        x_low = x_ref[:, lanes]
        x = x_low.astype(F32)
        grad_low = dssd_ref[:, lanes]
        grad = grad_low.astype(F32)
        through = jnp.zeros((BLOCK, LANES), F32)
        for head, keep in ((first, low_half), (first + 1, jnp.logical_not(low_half))):
            decay = spread(level, across, head)
            grad_own = jnp.where(keep, grad, 0.0).astype(BF16)
            pairs = mm(grad_own, x_low, ((1,), (1,)))
            through += mm((gram_t * decay).astype(BF16), grad_own)
            scaled = decay * pairs * step_across[head : head + 1, :]
            mixed_grads[...] += scaled
            ordered = gram * scaled * order
            left[...] = jnp.where(
                lane == head, jnp.sum(ordered, axis=1, keepdims=True), left[...]
            )
            right[head : head + 1, :] = jnp.sum(ordered, axis=0, keepdims=True)
        weight_pair = pair_of(weight, first, low_half)
        step_pair = pair_of(step, first, low_half)
        fade_pair = pair_of(fade, first, low_half)
        out_pair = pair_of(out_decay, first, low_half)
        leave = leaving[:, lanes]
        d_x = step_pair * through + weight_pair * leave + skip_ref[:, lanes] * grad
        for_step[:, lanes] = x * (through + out_pair * leave)
        weighted = weight_pair * x
        faded = fade_pair * grad
        for_level[:, lanes] = weighted * leave - faded * entering[:, lanes]
        sums[0:1, lanes] = jnp.sum(weighted * leave, axis=0, keepdims=True)
        sums[2:3, lanes] = jnp.sum(x * grad, axis=0, keepdims=True)
        faded_low = faded.astype(BF16)
        d_b += mm(weighted.astype(BF16), old_back[:, lanes], ((1,), (1,)))
        d_c += mm(faded_low, kept[:, lanes], ((1,), (1,)))
        back[:, lanes] = back[:, lanes] * pair_of(last, first, low_half) + mm(by_state, faded_low)
        d_conv = d_x * slope_x_ref[:, lanes].astype(F32)
        d_in, grads = conv_back(
            d_conv, after_x[:, lanes], px_ref[:, lanes].astype(F32), taps_x_ref[:, lanes]
        )
        after_x[:, lanes] = d_conv[0:8]
        dx_ref[:, lanes] = d_in.astype(BF16)
        small_ref[0 : taps + 1, lanes] += grads
        if first // 2 % turns == turns - 1 and first // 2 // turns < POINTS - 1:
            serve(first // 2 // turns)

    all_pairs = mixed_grads[...]
    d_b = d_b + mm(all_pairs.T.astype(BF16), rows_c)
    d_c = d_c + mm(all_pairs.astype(BF16), rows_b)
    d_conv = jnp.concatenate([d_b, d_c], axis=1) * slope_s_ref[...].astype(F32)
    d_in, grads = conv_back(
        d_conv, after_s[...], ps_ref[:, : 2 * STATE].astype(F32), taps_s_ref[...]
    )
    after_s[...] = d_conv[0:8]
    ds_ref[:, : 2 * STATE] = d_in.astype(BF16)
    small_ref[0 : taps + 1, width:] += grads

    chooser = (iota2((width, LANES), 0) // HEAD == iota2((width, LANES), 1)).astype(BF16)
    d_step = head_sums(for_step[...], chooser)
    sums[1:2, :] = at_last
    total = head_sums(sums[...], chooser)
    d_level = head_sums(for_level[...], chooser) - left[...] + right[...].T
    final = -total[0:1, :] - last * total[1:2, :]
    d_level = d_level + jnp.where(iota2((BLOCK, 1), 0) == BLOCK - 1, final, 0.0)
    d_lam = mm_exact((at_row <= at_col).astype(F32), d_level)
    d_raw = (d_step + d_lam * head_ref[1:2]) * chain_ref[...]
    head_row = taps + 2
    small_ref[head_row : head_row + 1, 0:LANES] += jnp.sum(d_raw, axis=0, keepdims=True)
    small_ref[head_row : head_row + 1, LANES : 2 * LANES] += jnp.sum(
        d_lam * lam, axis=0, keepdims=True
    )
    small_ref[head_row : head_row + 1, 2 * LANES : 3 * LANES] += total[2:3, :]
    chosen = chosen_heads(lax.axis_index("ctx"), heads, unit, n_ctx, True)
    ds_ref[:, 2 * STATE :] = mm(d_raw.astype(BF16), chosen).astype(BF16)

    serve(POINTS - 1)

    @pl.when(turn == pl.num_programs(0) - 1)
    def _():
        stores = [
            pltpu.make_async_copy(source, target, store_sem.at[i])
            for i, (source, target) in enumerate(
                ((done_o, shard_o), (done_z, shard_z), (v_hidden, layer_out))
            )
        ]
        stores[0].start()
        stores[1].start()
        v_hidden[...] = (v_hidden[...].astype(F32) + sum_mixed.total()).astype(BF16)
        stores[2].start()
        for copy in stores:
            copy.wait()


def scan_backward(
    n, unit, n_ctx, px, ps, kept_parts, d_ssd, gate_t, normed_t, upstream, d_z, mixed_parts, hidden, gain_grads, taps_x, taps_s, skip, head
):
    x, rows_b, rows_c, slope_x, slope_s, lam, step, chain, kept = kept_parts
    tokens, width = px.shape
    heads = width // HEAD
    count = tokens // BLOCK
    own, model = hidden.shape
    shared_width = ps.shape[1]
    piece = width // n
    assert model == 2 * width and heads // 2 % POINTS == 0
    by_block = lambda i: (count - 1 - i, 0)
    at_block = lambda size: pl.BlockSpec((BLOCK, size), by_block)
    whole = lambda a: pl.BlockSpec(a.shape, lambda i: (0, 0))
    any_space = pl.BlockSpec(memory_space=pl.ANY)
    low = lambda *shape: jax.ShapeDtypeStruct(shape, BF16)
    v_low = lambda *shape: pltpu.VMEM(shape, BF16)
    v_full = lambda *shape: pltpu.VMEM(shape, F32)
    part = lambda a, b: pl.BlockSpec((1, a, b), lambda i: (count - 1 - i, 0, 0))
    small_shape = (8, width + 2 * STATE)
    dma = pltpu.SemaphoreType.DMA
    return pl.pallas_call(
        functools.partial(backward_kernel, heads, unit, n_ctx, n),
        grid=(count,),
        in_specs=[
            at_block(width),
            at_block(shared_width),
            at_block(width),
            at_block(STATE),
            at_block(STATE),
            at_block(width),
            at_block(2 * STATE),
            at_block(LANES),
            at_block(LANES),
            at_block(LANES),
            part(STATE, width),
            at_block(width),
        ]
        + [any_space] * 6
        + [whole(a) for a in (gain_grads, taps_x, taps_s, skip, head)],
        out_specs=[
            at_block(width),
            at_block(shared_width),
            pl.BlockSpec(small_shape, lambda i: (0, 0)),
            any_space,
            any_space,
            any_space,
        ],
        out_shape=[
            low(tokens, width),
            low(tokens, shared_width),
            jax.ShapeDtypeStruct(small_shape, F32),
            low(piece, model),
            low(2, width, piece),
            low(own, model),
        ],
        scratch_shapes=[
            v_full(STATE, width),
            v_full(BLOCK, BLOCK),
            v_full(BLOCK, width),
            v_full(BLOCK, width),
            v_full(BLOCK, LANES),
            v_full(LANES, BLOCK),
            v_full(8, width),
            v_full(8, width),
            v_full(8, 2 * STATE),
            v_low(width + model, tokens),
            v_low(tokens, model + width),
            v_low(width, 2 * model),
            v_low(2, n - 1, 2, 2, piece, width // 2),
            v_low(2, 2, 2, piece, width // 2),
            v_low(piece, model),
            v_low(2, width, piece),
            v_low(2, own, model),
            v_low(2, own, model),
            v_low(own, model),
            v_low(own, model),
            dma((5 + 2 * n_ctx,)),
            dma((3,)),
            dma((2, 2, 2)),
            dma((2, 2, 2, n - 1)),
            dma((3,)),
            dma((3,)),
        ],
        compiler_params=pltpu.CompilerParams(
            collective_id=3, has_side_effects=True, vmem_limit_bytes=59 * 1024 * 1024
        ),
        name="scan_backward",
    )(
        px, ps, x, rows_b, rows_c, slope_x, slope_s, lam, step, chain, kept, d_ssd, gate_t, normed_t, upstream, d_z, mixed_parts, hidden, gain_grads, taps_x, taps_s, skip, head
    )


def gather_kernel(
    n,
    n_ctx,
    unit,
    direct,
    hidden,
    cotangent,
    in_weight_t,
    small,
    out_weight,
    cotangent_all,
    w_x,
    w_s,
    w_z,
    w_o,
    small_out,
    proj_x,
    proj_s,
    proj_z,
    normed_t,
    v_hidden,
    v_normed,
    v_x,
    v_s,
    v_z,
    v_small,
    raw_x,
    raw_s,
    raw_z,
    out_x,
    out_s,
    out_z,
    out_t,
    v_gain,
    load_sem,
    column_sem,
    local_sem,
    store_sem,
    ring_send,
    ring_recv,
    ctx_send,
    ctx_recv,
    piece_send,
    piece_recv,
):
    ring = Ring(n)
    me, shard = ring.me, ring.shard
    width, model = v_x.shape[1], v_x.shape[0]
    inner = width * n_ctx
    r = model // n
    shared = in_weight_t.shape[0] - 2 * inner
    row = me // 2
    other_core = (me + 1 - 2 * (me % 2), shard)
    other_row = (me + 2 - 4 * row, shard)
    piece = w_o.shape[1]
    piece_peer = (shard % n_ctx, shard // n_ctx * n_ctx + me)
    moves = shard % n_ctx != me

    barrier = pltpu.get_barrier_semaphore()
    for device in (other_core, other_row, ring.neighbour(0), ring.neighbour(1)):
        pl.semaphore_signal(barrier, inc=1, device_id=device, device_id_type=MESH)

    part = unit * HEAD

    def load_columns(base, target, sems):
        return [
            pltpu.make_async_copy(
                in_weight_t.at[pl.ds(pl.multiple_of(base + (a * n_ctx + me) * part, 16), part)],
                target.at[pl.ds(a * part, part)],
                sems.at[a],
            )
            for a in range(width // part)
        ]

    loads = [
        load_columns(inner, raw_x, column_sem.at[0]),
        [
            pltpu.make_async_copy(
                in_weight_t.at[pl.ds(2 * inner, shared)], raw_s.at[pl.ds(0, shared)], load_sem.at[0]
            )
        ],
        [pltpu.make_async_copy(small, v_small.at[shard], load_sem.at[1])],
        [pltpu.make_async_copy(hidden, v_hidden.at[me], load_sem.at[2])],
        load_columns(0, raw_z, column_sem.at[1]),
    ]
    for copies in loads:
        for copy in copies:
            copy.start()

    def loaded(i):
        for copy in loads[i]:
            copy.wait()

    if direct:
        pl.semaphore_wait(barrier, 4)
    else:

        @pl.when(moves)
        def _():
            pl.semaphore_signal(barrier, inc=1, device_id=piece_peer, device_id_type=MESH)
            pl.semaphore_wait(barrier, 5)

        @pl.when(jnp.logical_not(moves))
        def _():
            pl.semaphore_wait(barrier, 4)

    half, quarter = width // 2, w_o.shape[2] // 4
    rows = r // 2
    both_rows = lambda index, way: pl.ds(pl.multiple_of((2 * index + way) * rows, 16), rows)
    x_part = lambda a, sub: lambda index, way: a.at[both_rows(index, way), pl.ds(sub * half, half)]
    s_part = lambda index, way: v_s.at[both_rows(index, way)]
    small_part = lambda index, way: v_small.at[index, pl.ds(way * SMALL_ROWS // 2, SMALL_ROWS // 2)]
    o_part = lambda sub: lambda index, way: w_o.at[
        index, :, pl.ds((2 * way + sub) * quarter, quarter)
    ]
    phases = (
        ((0, small_part), (1, s_part), (2, x_part(v_x, 0)), (3, x_part(v_x, 1))),
        ((4, x_part(v_z, 0)), (5, x_part(v_z, 1))),
        ((6, o_part(0)), (7, o_part(1))),
    )

    def hop(stream, way, step):
        number, part = stream
        place = part(ring.at(-step if way == 0 else step), way)
        return remote(
            place, place, ring_send.at[number, way], ring_recv.at[number, way, step],
            ring.neighbour(way),
        )

    def arrives(stream, way, step):
        number, part = stream
        landed = part(ring.at(-step - 1 if way == 0 else step + 1), way)
        return remote(
            landed, landed, ring_send.at[number, way], ring_recv.at[number, way, step],
            ring.neighbour(way),
        )

    def start_stream(stream):
        for way in (0, 1):
            hop(stream, way, 0).start()

    def to_row(i, a, whole):
        return remote(a, whole.at[me], ctx_send.at[i, 0], ctx_recv.at[i, 0], other_row)

    def to_core(i, a, whole):
        return remote(a, whole.at[me], ctx_send.at[i, 1], ctx_recv.at[i, 1], other_core)

    def pass_on(i, whole):
        beyond = whole.at[other_row[0]]
        return remote(beyond, beyond, ctx_send.at[i, 2], ctx_recv.at[i, 2], other_core)

    to_row(0, hidden, v_hidden).start()
    to_core(0, hidden, v_hidden).start()
    own_rows = pl.ds(pl.multiple_of(shard * r, 16), r)
    loaded(2)
    start_stream(phases[0][0])
    loaded(0)
    v_x[own_rows, :] = raw_x[...].T
    start_stream(phases[0][2])
    start_stream(phases[0][3])
    loaded(1)
    raw_s[shared:, :] = jnp.zeros((raw_s.shape[0] - shared, r), BF16)
    v_s[own_rows, :] = raw_s[...].T
    start_stream(phases[0][1])
    own_piece = out_weight.at[pl.ds(pl.multiple_of(me * piece, 16), piece)]
    keep_piece = pltpu.make_async_copy(own_piece, w_o.at[shard], piece_send)

    def move_piece(wait):
        if direct:
            keep_piece.wait() if wait else keep_piece.start()
            return
        send_piece = remote(own_piece, w_o.at[piece_peer[1]], piece_send, piece_recv, piece_peer)

        @pl.when(moves)
        def _():
            send_piece.wait() if wait else send_piece.start()

        @pl.when(jnp.logical_not(moves))
        def _():
            keep_piece.wait() if wait else keep_piece.start()

    keep_cotangent = pltpu.make_async_copy(cotangent, cotangent_all.at[me], local_sem)
    keep_cotangent.start()
    loaded(3)
    loaded(4)
    v_z[own_rows, :] = raw_z[...].T

    def run_phase(number, work, after):
        def body(step, carry):
            for stream in phases[number]:
                for way in (0, 1):
                    arrives(stream, way, step).wait_recv()
                    hop(stream, way, step).wait_send()
                    hop(stream, way, step + 1).start()
            if work is not None:

                @pl.when(step < n_ctx)
                def _():
                    work(step)

            return carry

        lax.fori_loop(0, n - 2, body, 0)
        after()
        for stream in phases[number]:
            for way in (0, 1):
                arrives(stream, way, n - 2).wait_recv()
                hop(stream, way, n - 2).wait_send()

    tokens = v_hidden.shape[1]

    def project_first(chunk):
        at = pl.ds(pl.multiple_of(chunk * tokens, tokens), tokens)
        resid = v_hidden[chunk].astype(F32)
        scale = lax.rsqrt(jnp.mean(resid * resid, axis=1, keepdims=True) + EPS)
        normed = (resid * scale * v_gain[...]).astype(BF16)
        v_normed[at, :] = normed
        out_x[at, :] = mm(normed, v_x[...]).astype(BF16)
        out_s[at, :] = mm(normed, v_s[...]).astype(BF16)

    def project_gate(chunk):
        at = pl.ds(pl.multiple_of(chunk * tokens, tokens), tokens)
        normed = v_normed[at, :]
        out_z[at, :] = mm(normed, v_z[...]).astype(BF16)
        out_t[chunk] = normed.T

    stores = [
        pltpu.make_async_copy(source, target, store_sem.at[i])
        for i, (source, target) in enumerate(
            (
                (v_x, w_x),
                (v_s, w_s),
                (v_small, small_out),
                (out_x, proj_x),
                (out_s, proj_s),
                (v_z, w_z),
                (out_z, proj_z),
                (out_t, normed_t),
            )
        )
    ]

    def after_first():
        for stream in phases[1]:
            start_stream(stream)
        to_row(0, hidden, v_hidden).wait_recv()
        pass_on(0, v_hidden).start()
        move_piece(False)
        to_row(1, cotangent, cotangent_all).start()
        to_core(1, cotangent, cotangent_all).start()
        to_row(0, hidden, v_hidden).wait_send()
        to_core(0, hidden, v_hidden).wait()
        pass_on(0, v_hidden).wait()

    def after_second():
        move_piece(True)
        for stream in phases[2]:
            start_stream(stream)
        to_row(1, cotangent, cotangent_all).wait_recv()
        pass_on(1, cotangent_all).start()

    def after_third():
        to_row(1, cotangent, cotangent_all).wait_send()
        to_core(1, cotangent, cotangent_all).wait()
        pass_on(1, cotangent_all).wait()
        keep_cotangent.wait()

    run_phase(0, None, after_first)
    for f in range(n):
        v_gain[:, f * r : (f + 1) * r] = v_small[f, 0:1, 0:r].astype(F32)
    for copy in stores[0:3]:
        copy.start()
    run_phase(1, project_first, after_second)
    for copy in stores[3:6]:
        copy.start()
    run_phase(2, project_gate, after_third)
    for copy in stores[6:]:
        copy.start()
    for copy in stores:
        copy.wait()


def gather_all(n, n_ctx, unit, direct, hidden, cotangent, in_weight_t, small, out_weight, shared_width):
    own, model = hidden.shape
    tokens = own * n_ctx
    width = out_weight.shape[0] * n // n_ctx
    rows = in_weight_t.shape[1]
    any_space = pl.BlockSpec(memory_space=pl.ANY)
    low = lambda *shape: jax.ShapeDtypeStruct(shape, BF16)
    v_low = lambda *shape: pltpu.VMEM(shape, BF16)
    dma = pltpu.SemaphoreType.DMA
    return pl.pallas_call(
        functools.partial(gather_kernel, n, n_ctx, unit, direct),
        in_specs=[any_space] * 5,
        out_specs=[any_space] * 10,
        out_shape=[
            low(n_ctx, own, model),
            low(model, width),
            low(model, shared_width),
            low(model, width),
            low(n, width // n, model),
            low(n, small.shape[0], small.shape[1]),
            low(tokens, width),
            low(tokens, shared_width),
            low(tokens, width),
            low(n_ctx, model, own),
        ],
        scratch_shapes=[
            v_low(n_ctx, own, model),
            v_low(tokens, model),
            v_low(model, width),
            v_low(model, shared_width),
            v_low(model, width),
            v_low(n, small.shape[0], small.shape[1]),
            v_low(width, rows),
            v_low(shared_width, rows),
            v_low(width, rows),
            v_low(tokens, width),
            v_low(tokens, shared_width),
            v_low(tokens, width),
            v_low(n_ctx, model, own),
            pltpu.VMEM((1, model), F32),
            dma((3,)),
            dma((2, width // (unit * HEAD))),
            dma,
            dma((8,)),
            dma((8, 2)),
            dma((8, 2, n - 1)),
            dma((2, 3)),
            dma((2, 3)),
            dma,
            dma,
        ],
        compiler_params=pltpu.CompilerParams(
            collective_id=0, has_side_effects=True, vmem_limit_bytes=56 * 1024 * 1024
        ),
        name="gather_all",
    )(hidden, cotangent, in_weight_t, small, out_weight)


def reduce_kernel(
    n,
    n_ctx,
    direct,
    normed_t,
    d_z,
    d_x,
    d_s,
    w_z,
    w_x,
    w_s,
    shard_o,
    shard_z,
    small,
    hidden,
    cotangent,
    gain,
    g_z,
    g_x,
    g_s,
    g_o,
    hidden_grad,
    small_out,
    norm_out,
    v_normed_t,
    v_d_z,
    v_d_x,
    v_d_s,
    v_z,
    v_x,
    v_s,
    parts,
    partials,
    slots,
    stage,
    done,
    moved,
    from_core,
    from_row,
    v_hidden,
    v_cotangent,
    v_gain,
    small_all,
    small_ctx,
    norm_all,
    norm_ctx,
    load_sem,
    store_sem,
    ring_send,
    ring_recv,
    ctx_send,
    ctx_recv,
    own_sem,
    piece_send,
    piece_recv,
    part_send,
    part_recv,
    small_send,
    small_recv,
    small_ctx_send,
    small_ctx_recv,
):
    ring = Ring(n)
    me, shard = ring.me, ring.shard
    around = Around(me, shard)
    core, row = me % 2, me // 2
    piece_peer = (shard % n_ctx, shard // n_ctx * n_ctx + me)
    moves = shard % n_ctx != me
    barrier = pltpu.get_barrier_semaphore()
    for device in around.all:
        greet(device)
    lax.fori_loop(1, n, lambda j, carry: (greet((me, lax.rem(shard + j, n))), carry)[1], 0)
    own = hidden.shape[0]
    sum_normed = TokenSum(
        around, parts, parts.at[me], parts.at[around.row_at], from_core, from_row, part_send, part_recv
    )
    sum_small, sum_norm = (
        SmallSum(
            n, around, whole, sums, small_send.at[i], small_recv.at[i], small_ctx_send.at[i], small_ctx_recv.at[i]
        )
        for i, (whole, sums) in enumerate(((small_all, small_ctx), (norm_all, norm_ctx)))
    )
    loads = [
        pltpu.make_async_copy(source, target, load_sem.at[i])
        for i, (source, target) in enumerate(
            (
                *((normed_t.at[c], v_normed_t.at[:, pl.ds(c * own, own)]) for c in range(n_ctx)),
                (d_s, v_d_s),
                (d_x, v_d_x),
                (small, small_all.at[shard]),
                (d_z, v_d_z),
                (w_z, v_z),
                (w_x, v_x),
                (w_s, v_s),
                (hidden, v_hidden),
                (cotangent, v_cotangent),
                (gain, v_gain),
            )
        )
    ]
    ring_loads = n_ctx + 2
    for copy in loads:
        copy.start()
    if direct:
        pl.semaphore_wait(barrier, n + 2)
    else:

        @pl.when(moves)
        def _():
            greet(piece_peer)
            pl.semaphore_wait(barrier, n + 3)

        @pl.when(jnp.logical_not(moves))
        def _():
            pl.semaphore_wait(barrier, n + 2)

    rows = v_normed_t.shape[0] // (2 * n)
    half, last = v_d_x.shape[1] // 2, v_d_s.shape[1]
    streams = (
        (0, v_d_s, 0, last, 2 * half),
        (1, v_d_x, 0, half, 0),
        (2, v_d_x, half, half, half),
    )

    def compute_partials(step):
        for way in (0, 1):
            index = ring.at(-step - 2 if way == 0 else step + 2)
            left = v_normed_t[pl.ds(pl.multiple_of((2 * index + way) * rows, 16), rows), :]
            partials[way, :, 2 * half :] = mm(left, v_d_s[...])
            partials[way, :, 0 : 2 * half] = mm(left, v_d_x[...])

    def slot(stream, way, step):
        return slots.at[step, way, :, pl.ds(stream[4], stream[3])]

    def hop(stream, way, step, source):
        return remote(
            source,
            slot(stream, way, step),
            ring_send.at[stream[0], way],
            ring_recv.at[stream[0], way, step],
            ring.neighbour(way),
        )

    def first_part(stream, way):
        return stage.at[way, :, pl.ds(stream[4], stream[3])]

    def arrived(stream, way, step):
        hop(stream, way, step, first_part(stream, way)).wait()
        partial = partials[way, :, stream[4] : stream[4] + stream[3]]
        return slot(stream, way, step)[...].astype(F32) + partial

    done_of = lambda stream: done.at[pl.ds(stream[4], stream[3])]
    of_x = lambda c, first: g_x.at[c, pl.ds(first, half)]
    shares = (
        (shard_o if direct else moved, lambda c: g_o.at[c]),
        (shard_z, lambda c: g_z.at[c]),
        (done_of(streams[1]), lambda c: of_x(c, 0)),
        (done_of(streams[2]), lambda c: of_x(c, half)),
        (done_of(streams[0]), lambda c: g_s.at[c]),
    )

    def share(i, kind):
        source, whole = shares[i]
        at = me
        if kind == 2:
            source, at = whole(around.row_at), around.row_at
        device = around.row if kind == 0 else around.core
        return remote(source, whole(at), ctx_send.at[i, kind], ctx_recv.at[i, kind], device)

    def keep(i):
        return pltpu.make_async_copy(shares[i][0], shares[i][1](me), own_sem.at[i])

    def start_share(i):
        share(i, 0).start()
        share(i, 1).start()
        keep(i).start()

    def pass_share(i):
        share(i, 0).wait_recv()
        share(i, 2).start()

    def close_share(i):
        share(i, 0).wait_send()
        share(i, 1).wait()
        share(i, 2).wait()
        keep(i).wait()

    def move_piece(wait):
        if direct:
            return
        keep_piece = pltpu.make_async_copy(shard_o, moved, piece_send)
        send_piece = remote(shard_o, moved, piece_send, piece_recv, piece_peer)

        @pl.when(moves)
        def _():
            send_piece.wait() if wait else send_piece.start()

        @pl.when(jnp.logical_not(moves))
        def _():
            keep_piece.wait() if wait else keep_piece.start()

    def normed_part(i, carry):
        to_row = row + (1 - i % 2) * (1 - 2 * row)
        to_core = core + (1 - i // 2) * (1 - 2 * core)
        at = 2 * to_row + to_core
        tokens = pl.ds(pl.multiple_of(at * own, own), own)
        parts[at] = (
            mm(v_d_z[tokens, :], v_z[...], ((1,), (1,)))
            + mm(v_d_x[tokens, :], v_x[...], ((1,), (1,)))
            + mm(v_d_s[tokens, :], v_s[...], ((1,), (1,)))
        ).astype(BF16)
        return carry

    store_grad = pltpu.make_async_copy(v_cotangent, hidden_grad, store_sem.at[0])
    store_small = pltpu.make_async_copy(small_ctx, small_out, store_sem.at[1])
    store_norm = pltpu.make_async_copy(norm_ctx, norm_out, store_sem.at[2])

    def finish_tokens():
        resid = v_hidden[...].astype(F32)
        scale = lax.rsqrt(jnp.mean(resid * resid, axis=1, keepdims=True) + EPS)
        d_normed = sum_normed.total()
        f = v_gain[...] * d_normed
        slope = scale**3 * jnp.mean(resid * f, axis=1, keepdims=True)
        grad = v_cotangent[...].astype(F32) + scale * f - resid * slope
        v_cotangent[...] = grad.astype(BF16)
        store_grad.start()
        by_model = jnp.sum(d_normed * resid * scale, axis=0, keepdims=True)
        size = norm_all.shape[2]
        for j in range(norm_all.shape[1]):
            norm_all[shard, j : j + 1, :] = by_model[:, j * size : (j + 1) * size]
        sum_norm.start()

    move_piece(False)
    for copy in loads[:ring_loads]:
        copy.wait()
    compute_partials(-1)
    for way in (0, 1):
        stage[way] = partials[way].astype(BF16)
        for stream in streams:
            hop(stream, way, 0, first_part(stream, way)).start()
    compute_partials(0)
    for copy in loads[ring_loads:]:
        copy.wait()
    sum_small.start()
    move_piece(True)
    start_share(0)
    start_share(1)

    def body(step, carry):
        for stream in streams:
            for way in (0, 1):
                total = arrived(stream, way, step)
                place = slot(stream, way, step)
                place[...] = total.astype(BF16)
                hop(stream, way, step + 1, place).start()
        compute_partials(step + 1)

        @pl.when(step < 2)
        def _():
            lax.fori_loop(2 * step, 2 * step + 2, normed_part, 0)

        @pl.when(step == 0)
        def _():
            sum_normed.start()

        @pl.when(step == 1)
        def _():
            sum_normed.pass_row()

        @pl.when(step == n - 3)
        def _():
            finish_tokens()

        return carry

    lax.fori_loop(0, n - 2, body, 0)
    sum_small.add()
    pass_share(0)
    pass_share(1)
    for number, shared in ((0, 4), (1, 2), (2, 3)):
        place = done_of(streams[number])
        for way in (0, 1):
            total = arrived(streams[number], way, n - 2)
            place[:, way * rows : (way + 1) * rows] = total.T.astype(BF16)
        start_share(shared)
    sum_norm.add()
    sum_small.finish()
    store_small.start()
    for i in (4, 2, 3):
        pass_share(i)
    sum_norm.finish()
    store_norm.start()
    for i in range(5):
        close_share(i)
    store_grad.wait()
    store_small.wait()
    store_norm.wait()


def reduce_all(
    n, n_ctx, direct, normed_t, d_z, d_x, d_s, w_z, w_x, w_s, shard_o, shard_z, small, hidden, cotangent, gain
):
    model, tokens = normed_t.shape[1], d_x.shape[0]
    width, shared_width = d_x.shape[1], d_s.shape[1]
    rows, piece, own = model // n, width // n, hidden.shape[0]
    columns = width + shared_width
    any_space = pl.BlockSpec(memory_space=pl.ANY)
    dma = pltpu.SemaphoreType.DMA
    low = lambda *shape: jax.ShapeDtypeStruct(shape, BF16)
    v_low = lambda *shape: pltpu.VMEM(shape, BF16)
    v_full = lambda *shape: pltpu.VMEM(shape, F32)
    norm_shape = (8, model // 8)
    return pl.pallas_call(
        functools.partial(reduce_kernel, n, n_ctx, direct),
        in_specs=[any_space] * 13,
        out_specs=[any_space] * 7,
        out_shape=[
            low(n_ctx, 2, width, rows // 2),
            low(n_ctx, width, rows),
            low(n_ctx, shared_width, rows),
            low(n_ctx, piece, model),
            low(own, model),
            jax.ShapeDtypeStruct((n_ctx,) + small.shape, F32),
            jax.ShapeDtypeStruct((n_ctx,) + norm_shape, F32),
        ],
        scratch_shapes=[
            v_low(model, tokens),
            v_low(tokens, width),
            v_low(tokens, width),
            v_low(tokens, shared_width),
            v_low(*w_z.shape),
            v_low(*w_x.shape),
            v_low(*w_s.shape),
            v_low(n_ctx, own, model),
            v_full(2, rows // 2, columns),
            v_low(n - 1, 2, rows // 2, columns),
            v_low(2, rows // 2, columns),
            v_low(columns, rows),
            v_low(piece, model),
            v_low(2, own, model),
            v_low(own, model),
            v_low(own, model),
            v_low(own, model),
            v_full(1, model),
            v_full(n, *small.shape),
            v_full(n_ctx, *small.shape),
            v_full(n, *norm_shape),
            v_full(n_ctx, *norm_shape),
            dma((10 + n_ctx,)),
            dma((3,)),
            dma((3, 2)),
            dma((3, 2, n - 1)),
            dma((5, 3)),
            dma((5, 3)),
            dma((5,)),
            dma,
            dma,
            dma((3,)),
            dma((3,)),
            dma((2, n - 1)),
            dma((2, n - 1)),
            dma((2, 3)),
            dma((2, 3)),
        ],
        compiler_params=pltpu.CompilerParams(
            collective_id=1, has_side_effects=True, vmem_limit_bytes=58 * 1024 * 1024
        ),
        name="reduce_all",
    )(
        normed_t, d_z, d_x, d_s, w_z, w_x, w_s, shard_o, shard_z, small, hidden, cotangent, gain
    )


def assemble_kernel(part, z_ref, x_ref, s_ref, out_ref):
    place = pl.program_id(0)
    n_ctx, size, half = x_ref.shape[0], x_ref.shape[1], z_ref.shape[3]

    def interleave(write):
        for a in range(size // part):
            for c in range(n_ctx):
                write(
                    slice((a * n_ctx + c) * part, (a * n_ctx + c + 1) * part),
                    c,
                    slice(a * part, (a + 1) * part),
                )

    def write_z(target, c, source):
        for way in (0, 1):
            out_ref[target, way * half : (way + 1) * half] = z_ref[c, way, source, :].astype(F32)

    def write_x(target, c, source):
        out_ref[target, :] = x_ref[c, source, :].astype(F32)

    @pl.when(place < n_ctx)
    def _():
        interleave(write_z)

    @pl.when(jnp.logical_and(place >= n_ctx, place < 2 * n_ctx))
    def _():
        interleave(write_x)

    @pl.when(place == 2 * n_ctx)
    def _():
        total = s_ref[0].astype(F32)
        for c in range(1, n_ctx):
            total += s_ref[c].astype(F32)
        out_ref[0 : total.shape[0], :] = total


def assemble(part, g_z, g_x, g_s, columns):
    n_ctx, width, rows = g_x.shape
    block = (n_ctx, width // n_ctx, rows)
    return pl.pallas_call(
        functools.partial(assemble_kernel, part),
        grid=(2 * n_ctx + 1,),
        in_specs=[
            pl.BlockSpec(
                (n_ctx, 2, width // n_ctx, rows // 2),
                lambda i: (0, 0, jnp.minimum(i, n_ctx - 1), 0),
            ),
            pl.BlockSpec(block, lambda i: (0, jnp.clip(i - n_ctx, 0, n_ctx - 1), 0)),
            pl.BlockSpec(g_s.shape, lambda i: (0, 0, 0)),
        ],
        out_specs=pl.BlockSpec((width, rows), lambda i: (i, 0)),
        out_shape=jax.ShapeDtypeStruct((columns, rows), F32),
        compiler_params=pltpu.CompilerParams(vmem_limit_bytes=58 * 1024 * 1024),
        name="assemble",
    )(g_z, g_x, g_s)


def on_device(
    hidden,
    cotangent,
    seq_lens,
    norm_gain,
    in_weight,
    conv_weight,
    conv_bias,
    dt_bias,
    a_log,
    d_skip,
    gate_gain,
    out_weight,
):
    n_ctx, n_fsdp = lax.axis_size("ctx"), lax.axis_size("fsdp")
    me, shard = lax.axis_index("ctx"), lax.axis_index("fsdp")
    taps = conv_weight.shape[0]
    heads_all = dt_bias.shape[0] * n_fsdp
    inner = out_weight.shape[0] * n_fsdp
    heads, width = heads_all // n_ctx, inner // n_ctx
    model = hidden.shape[2]
    both = 2 * STATE
    held = dt_bias.shape[0]
    direct = held % n_ctx == 0
    unit = held // n_ctx if direct else 1
    part = unit * HEAD
    shared_width = -(-(both + heads_all) // LANES) * LANES

    per_head = jnp.concatenate([dt_bias, a_log, d_skip])
    lines = [norm_gain[None], conv_weight, conv_bias[None], gate_gain[None], per_head[None]]
    longest = -(-max(a.shape[1] for a in lines) // LANES) * LANES
    small = jnp.concatenate([jnp.pad(a, ((0, 0), (0, longest - a.shape[1]))) for a in lines])
    small = jnp.pad(small, ((0, SMALL_ROWS - small.shape[0]), (0, 0)))
    upstream, w_x, w_s, w_z, w_o, small_all, proj_x, proj_s, proj_z, normed_t = gather_all(
        n_fsdp, n_ctx, unit, direct, hidden[0], cotangent[0], in_weight.T, small, out_weight, shared_width
    )
    w_o = w_o.reshape(-1, model)

    def line(first, count, size):
        rows = small_all[:, first : first + count, :size]
        return jnp.moveaxis(rows, 0, 1).reshape(count, -1).astype(F32)

    def own(lines, size):
        by_part = lines.reshape(lines.shape[0], -1, n_ctx, size)
        return lax.dynamic_index_in_dim(by_part, me, 2, False).reshape(lines.shape[0], -1)

    gain_norm = line(0, 1, norm_gain.shape[0])
    conv_lines = line(1, taps + 1, conv_bias.shape[0])
    taps_x, taps_s = own(conv_lines[:, :inner], part), conv_lines[:, inner:]
    gain_gate = own(line(taps + 2, 1, gate_gain.shape[0]), part)
    each = small_all[:, taps + 3, : per_head.shape[0]].reshape(n_fsdp, 3, -1)
    each = own(jnp.moveaxis(each, 0, 1).reshape(3, -1).astype(F32), unit)
    head = jnp.pad(jnp.stack([each[0], jnp.exp(each[1])]), ((0, 0), (0, LANES - heads)))
    skip = jnp.repeat(each[2], HEAD)[None]

    *kept_parts, y, d_yn, stats = scan_forward(
        unit, n_ctx, seq_lens, proj_x, proj_s, proj_z, upstream, w_o, taps_x, taps_s, gain_gate, skip, head
    )
    gate_t, mixed_parts, d_z, d_ssd, gain_grads = gate_norm(
        inner, seq_lens, stats, proj_z, y, d_yn, w_o, gain_gate
    )
    d_x, d_s, small_grads, shard_o, shard_z, layer_out = scan_backward(
        n_fsdp, unit, n_ctx, proj_x, proj_s, kept_parts, d_ssd, gate_t, normed_t, upstream, d_z, mixed_parts, hidden[0], gain_grads, taps_x, taps_s, skip, head
    )
    g_z, g_x, g_s, g_o, hidden_grad, sums, norm_sums = reduce_all(
        n_fsdp, n_ctx, direct, normed_t, d_z, d_x, d_s, w_z, w_x, w_s, shard_o, shard_z, small_grads, hidden[0], cotangent[0], gain_norm
    )
    grad_in_weight = assemble(part, g_z, g_x, g_s, 2 * inner + both + heads_all).T
    grad_out_weight = g_o.reshape(-1, model).astype(F32)

    def shard_of(lines):
        size = lines.shape[1] // n_fsdp
        return lax.dynamic_slice_in_dim(lines, shard * size, size, axis=1)

    def in_order(sums_of, size):
        lines = sums_of.shape[1]
        by_part = sums_of.reshape(n_ctx, lines, -1, size)
        return jnp.transpose(by_part, (1, 2, 0, 3)).reshape(lines, -1)

    conv_sums = shard_of(
        jnp.concatenate(
            [
                in_order(sums[:, : taps + 1, :width], part),
                jnp.sum(sums[:, : taps + 1, width:], axis=0),
            ],
            axis=1,
        )
    )
    gate_sums = shard_of(in_order(sums[:, taps + 1 : taps + 2, :width], part))
    head_sums_all = sums[:, taps + 2, : 3 * LANES].reshape(n_ctx, 3, LANES)[:, :, :heads]
    head_grads = shard_of(in_order(head_sums_all, unit))
    norm_sums = jnp.sum(norm_sums, axis=0).reshape(1, -1)
    return (
        layer_out[None],
        hidden_grad[None],
        shard_of(norm_sums)[0],
        grad_in_weight,
        conv_sums[:taps],
        conv_sums[taps],
        head_grads[0],
        head_grads[1],
        head_grads[2],
        gate_sums[0],
        grad_out_weight,
    )


def solution(mesh):
    tokens, rows, flat = P("fsdp", "ctx", None), P("fsdp", None), P("fsdp")
    taps = P(None, "fsdp")
    return jax.shard_map(
        on_device,
        mesh=mesh,
        in_specs=(tokens, tokens, flat, flat, rows, taps, flat, flat, flat, flat, flat, rows),
        out_specs=(tokens, tokens, flat, rows, taps, flat, flat, flat, flat, flat, rows),
        check_vma=False,
    )
```

```python
import functools

import jax
import jax.numpy as jnp
from jax import lax
from jax.experimental import pallas as pl
from jax.experimental.pallas import tpu as pltpu
from jax.sharding import PartitionSpec as P

HEAD = 64
STATE = 128
BLOCK = 256
LANES = 128
POINTS = 4
EPS = 1e-05
F32 = jnp.float32
BF16 = jnp.bfloat16


def mm(a, b, contract=((1,), (0,))):
    return lax.dot_general(a, b, (contract, ((), ())), preferred_element_type=F32)


def mm_exact(a, b, contract=((1,), (0,))):
    return lax.dot_general(
        a, b, (contract, ((), ())), precision=lax.Precision.HIGHEST, preferred_element_type=F32
    )


def iota2(shape, axis):
    return lax.broadcasted_iota(jnp.int32, shape, axis)


def levels(lam, step):
    tri = (iota2((BLOCK, BLOCK), 0) >= iota2((BLOCK, BLOCK), 1)).astype(F32)
    level = mm_exact(tri, lam)
    across = level.T
    last = level[BLOCK - 1 : BLOCK, :]
    weight = jnp.exp(level - last) * step
    return level, across, jnp.exp(-last), weight, jnp.exp(-level)


def pair_of(array, first, low_half):
    return jnp.where(low_half, array[:, first : first + 1], array[:, first + 1 : first + 2])


def spread(level, across, head):
    return jnp.exp(-jnp.abs(level[:, head : head + 1] - across[head : head + 1, :]))


def silu_and_slope(v):
    s = jax.nn.sigmoid(v)
    return v * s, s * (1.0 + v * (1.0 - s))


def chosen_heads(me, heads, unit, n_ctx, turned=False):
    here, there = iota2((LANES, LANES), 1), iota2((LANES, LANES), 0)
    if turned:
        here, there = there, here
    head = (here // unit * n_ctx + me) * unit + here % unit
    return jnp.where(jnp.logical_and(there == head, here < heads), 1.0, 0.0).astype(BF16)


def column_valid(length_ref, block):
    at = iota2((BLOCK, 1), 0) + block * BLOCK
    return (at < length_ref[0]).astype(F32)


MESH = pl.DeviceIdType.MESH
SMALL_ROWS = 32


def ring_place(index, half):
    a, b = index // 2, index % 2
    return a + b * (2 * half - 1 - 2 * a)


def ring_index(place, half):
    b = place // half
    return 2 * (place + b * (2 * half - 1 - 2 * place)) + b


class Ring:
    def __init__(self, n):
        self.n, self.half = n, n // 2
        self.me, self.shard = lax.axis_index("ctx"), lax.axis_index("fsdp")
        self.place = ring_place(self.shard, self.half)

    def at(self, steps):
        return ring_index(lax.rem(self.place + steps + 2 * self.n, self.n), self.half)

    def neighbour(self, way):
        return (self.me, self.at(1 if way == 0 else -1))


def remote(source, target, send, recv, device):
    return pltpu.make_async_remote_copy(
        src_ref=source,
        dst_ref=target,
        send_sem=send,
        recv_sem=recv,
        device_id=device,
        device_id_type=MESH,
    )


def greet(device):
    pl.semaphore_signal(pltpu.get_barrier_semaphore(), inc=1, device_id=device, device_id_type=MESH)


class Around:
    def __init__(self, me, shard):
        core, row = me % 2, me // 2
        self.me = me
        self.core_at = me + 1 - 2 * core
        self.row_at = me + 2 - 4 * row
        self.both_at = self.row_at + 1 - 2 * core
        self.core, self.row, self.both = (
            (at, shard) for at in (self.core_at, self.row_at, self.both_at)
        )
        self.all = (self.core, self.row, self.both)


class TokenSum:
    def __init__(self, around, parts, own_part, row_part, from_core, from_row, send, recv):
        self.around, self.parts, self.own_part, self.row_part = around, parts, own_part, row_part
        self.from_core, self.from_row, self.send, self.recv = from_core, from_row, send, recv

    def loads(self):
        at = self.around
        return (
            (self.parts.at[at.row_at], self.row_part),
            (self.parts.at[at.me], self.own_part),
        )

    def to_core(self, which):
        at = self.around
        return remote(
            self.parts.at[(at.core_at, at.both_at)[which]],
            self.from_core.at[which],
            self.send.at[which],
            self.recv.at[which],
            at.core,
        )

    def to_row(self):
        return remote(
            self.row_part, self.from_row, self.send.at[2], self.recv.at[2], self.around.row
        )

    def start(self):
        self.to_core(1).start()
        self.to_core(0).start()

    def pass_row(self):
        self.to_core(1).wait()
        total = self.row_part[...].astype(F32) + self.from_core[1].astype(F32)
        self.row_part[...] = total.astype(BF16)
        self.to_row().start()

    def total(self):
        self.to_core(0).wait()
        self.to_row().wait()
        return (
            self.own_part[...].astype(F32)
            + self.from_core[0].astype(F32)
            + self.from_row[...].astype(F32)
        )


class SmallSum:
    def __init__(self, n, around, whole, sums, send, recv, ctx_send, ctx_recv):
        self.n, self.around, self.whole, self.sums = n, around, whole, sums
        self.send, self.recv, self.ctx_send, self.ctx_recv = send, recv, ctx_send, ctx_recv
        self.shard = lax.axis_index("fsdp")

    def to_peer(self, offset):
        own = self.whole.at[self.shard]
        peer = (self.around.me, lax.rem(self.shard + offset, self.n))
        return remote(own, own, self.send.at[offset - 1], self.recv.at[offset - 1], peer)

    def to_ctx(self, i):
        own = self.sums.at[self.around.me]
        return remote(own, own, self.ctx_send.at[i], self.ctx_recv.at[i], self.around.all[i])

    def start(self):
        lax.fori_loop(1, self.n, lambda j, carry: (self.to_peer(j).start(), carry)[1], 0)

    def add(self):
        lax.fori_loop(1, self.n, lambda j, carry: (self.to_peer(j).wait(), carry)[1], 0)
        self.sums[self.around.me] = jnp.sum(self.whole[...], axis=0)
        for i in range(3):
            self.to_ctx(i).start()

    def finish(self):
        for i in range(3):
            self.to_ctx(i).wait()


def forward_kernel(
    heads,
    unit,
    n_ctx,
    n,
    direct,
    length_ref,
    px_ref,
    ps_ref,
    normed_ref,
    out_weight,
    w_z,
    upstream,
    taps_x_ref,
    taps_s_ref,
    gate_gain_ref,
    skip_ref,
    head_ref,
    x_ref,
    b_ref,
    c_ref,
    slope_x_ref,
    slope_s_ref,
    lam_ref,
    step_ref,
    chain_ref,
    kept_ref,
    gain_ref,
    gate_t,
    mixed_parts,
    d_z,
    d_ssd,
    state,
    before_x,
    before_s,
    v_o,
    v_z,
    v_up,
    all_y,
    all_z,
    all_dyn,
    v_yt,
    v_mixed,
    v_dz,
    v_dssd,
    stat_all,
    columns,
    load_sem,
    store_sem,
    ring_send,
    ring_recv,
    piece_recv,
    stat_send,
    stat_recv,
):
    block = pl.program_id(0)
    blocks = pl.num_programs(0)
    ring = Ring(n)
    me, shard = ring.me, ring.shard
    around = Around(me, shard)
    width = px_ref.shape[1]
    channels = width * n_ctx
    piece, size = v_o.shape[0] // n, v_o.shape[1] // 4
    points = heads // 2 * n_ctx
    loads = [
        pltpu.make_async_copy(source, target, load_sem.at[i])
        for i, (source, target) in enumerate(((w_z, v_z), (upstream, v_up)))
    ]
    shard_rows = lambda index: pl.ds(pl.multiple_of(index * piece, 16), piece)
    own_piece = out_weight.at[pl.ds(pl.multiple_of(me * piece, 16), piece)]
    piece_peer = (shard % n_ctx, shard // n_ctx * n_ctx + me)
    moves = shard % n_ctx != me

    def hop(way, sub, step):
        at = pl.multiple_of((2 * way + sub) * size, LANES)
        place = v_o.at[shard_rows(ring.at(step * (2 * way - 1))), pl.ds(at, size)]
        return remote(
            place,
            place,
            ring_send.at[way, sub],
            ring_recv.at[way, sub, step],
            (me, ring.at(1 - 2 * way)),
        )

    def streams(body):
        lax.fori_loop(0, 4, lambda e, carry: (body(e // 2, e % 2), carry)[1], 0)

    def ring_step(step):
        def body(way, sub):
            hop(way, sub, step).wait()

            @pl.when(step < n - 2)
            def _():
                hop(way, sub, step + 1).start()

        streams(body)

    def serve(point):
        at = block * (heads // 2) + point
        lax.fori_loop(
            at * (n - 1) // points,
            (at + 1) * (n - 1) // points,
            lambda step, carry: (ring_step(step), carry)[1],
            0,
        )

    @pl.when(block == 0)
    def _():
        for device in around.all:
            greet(device)
        greet(ring.neighbour(0))
        greet(ring.neighbour(1))
        keep = pltpu.make_async_copy(own_piece, v_o.at[shard_rows(shard)], load_sem.at[2])
        if direct:
            keep.start()
            pl.semaphore_wait(pltpu.get_barrier_semaphore(), 5)
            keep.wait()
        else:
            send = remote(
                own_piece, v_o.at[shard_rows(piece_peer[1])], load_sem.at[2], piece_recv, piece_peer
            )

            @pl.when(moves)
            def _():
                greet(piece_peer)
                pl.semaphore_wait(pltpu.get_barrier_semaphore(), 6)
                send.start()
                send.wait()

            @pl.when(jnp.logical_not(moves))
            def _():
                pl.semaphore_wait(pltpu.get_barrier_semaphore(), 5)
                keep.start()
                keep.wait()

        streams(lambda way, sub: hop(way, sub, 0).start())
        for copy in loads:
            copy.start()
        state[...] = jnp.zeros_like(state)
        before_x[...] = jnp.zeros_like(before_x)
        before_s[...] = jnp.zeros_like(before_s)

    valid = column_valid(length_ref, block)
    low_half = iota2((1, LANES), 1) < HEAD
    taps = taps_x_ref.shape[0] - 1

    def conv(current, before, weight):
        padded = jnp.concatenate([before, current], axis=0)
        total = weight[taps : taps + 1]
        for k in range(taps):
            first = 8 - (taps - 1) + k
            total = total + weight[k : k + 1] * padded[first : first + BLOCK]
        return silu_and_slope(total)

    both = ps_ref[:, : 2 * STATE].astype(F32)
    active, slope = conv(both, before_s[...], taps_s_ref[...])
    before_s[...] = both[BLOCK - 8 :]
    slope_s_ref[...] = slope.astype(BF16)
    rows_b, rows_c = active[:, :STATE].astype(BF16), active[:, STATE:].astype(BF16)
    b_ref[...] = rows_b
    c_ref[...] = rows_c
    raw = mm(ps_ref[:, 2 * STATE :], chosen_heads(me, heads, unit, n_ctx)) + head_ref[0:1]
    own = iota2((1, LANES), 1) < heads
    step = jnp.where(own, valid * jax.nn.softplus(raw), 0.0)
    lam = step * head_ref[1:2]
    step_ref[...] = step
    lam_ref[...] = lam
    chain_ref[...] = jnp.where(own, valid * jax.nn.sigmoid(raw), 0.0)

    gram = mm(rows_c, rows_b, ((1,), (1,)))
    level, across, last, weight, fade = levels(lam, step)
    kept_ref[0] = state[...].astype(BF16)
    entering = mm(rows_c, state[...].astype(BF16))
    by_state = rows_b.T
    for first in range(0, heads, 2):
        lanes = slice(first * HEAD, (first + 2) * HEAD)
        current = px_ref[:, lanes].astype(F32)
        active, slope = conv(current, before_x[:, lanes], taps_x_ref[:, lanes])
        before_x[:, lanes] = current[BLOCK - 8 :]
        slope_x_ref[:, lanes] = slope.astype(BF16)
        x_low = active.astype(BF16)
        x_ref[:, lanes] = x_low
        x = x_low.astype(F32)
        scaled = x * pair_of(step, first, low_half)
        total = pair_of(fade, first, low_half) * entering[:, lanes] + skip_ref[:, lanes] * x
        for head, keep in ((first, low_half), (first + 1, jnp.logical_not(low_half))):
            mixing = (gram * spread(level, across, head)).astype(BF16)
            total += mm(mixing, jnp.where(keep, scaled, 0.0).astype(BF16))
        all_y[block, :, lanes] = total
        update = mm(by_state, (x * pair_of(weight, first, low_half)).astype(BF16))
        state[:, lanes] = state[:, lanes] * pair_of(last, first, low_half) + update
        if first + 2 < heads:
            serve(first // 2)

    @pl.when(block == 0)
    def _():
        loads[0].wait()

    all_z[block] = mm(normed_ref[...], v_z[...]).astype(BF16)
    serve(heads // 2 - 1)

    @pl.when(block == blocks - 1)
    def _():
        loads[1].wait()
        lane = iota2((1, LANES), 1)

        def sums_of(chunk, carry):
            d_yn = column_valid(length_ref, chunk) * mm(v_up[chunk], v_o[...], ((1,), (1,)))
            all_dyn[chunk] = d_yn
            gated = all_y[chunk] * jax.nn.silu(all_z[chunk].astype(F32))
            square = jnp.sum(gated * gated, axis=1, keepdims=True)
            along = jnp.sum(gate_gain_ref[...] * d_yn * gated, axis=1, keepdims=True)
            pair = jnp.where(lane == 0, square, 0.0) + jnp.where(lane == 1, along, 0.0)
            stat_all[me, chunk] = pair.T[0:8]
            return carry

        lax.fori_loop(0, blocks, sums_of, 0)
        own_stats = stat_all.at[me]
        copies = [
            remote(own_stats, own_stats, stat_send.at[i], stat_recv.at[i], device)
            for i, device in enumerate(around.all)
        ]
        for copy in copies:
            copy.start()
        gain_ref[...] = jnp.zeros_like(gain_ref)
        for copy in copies:
            copy.wait()
        total = jnp.sum(stat_all[...], axis=0)
        for i in range(n_ctx):
            columns[i] = total[i].T

        def stores(chunk):
            slot = chunk % 2
            rows = pl.ds(pl.multiple_of(chunk * BLOCK, BLOCK), BLOCK)
            return [
                pltpu.make_async_copy(source.at[slot], target, store_sem.at[slot, i])
                for i, (source, target) in enumerate(
                    (
                        (v_yt, gate_t.at[chunk]),
                        (v_mixed, mixed_parts.at[chunk]),
                        (v_dz, d_z.at[rows]),
                        (v_dssd, d_ssd.at[rows]),
                    )
                )
            ]

        def gate_part(chunk, carry):
            slot = chunk % 2

            @pl.when(chunk >= 2)
            def _():
                for copy in stores(chunk - 2):
                    copy.wait()

            sums = columns[chunk]
            scale = lax.rsqrt(sums[:, 0:1] / channels + EPS)
            slant = scale * scale * scale * sums[:, 1:2] / channels
            here = column_valid(length_ref, chunk)
            for first in range(0, heads, 2):
                lanes = slice(first * HEAD, (first + 2) * HEAD)
                gate, gate_slope = silu_and_slope(all_z[chunk, :, lanes].astype(F32))
                mixed = all_y[chunk, :, lanes]
                d_yn = all_dyn[chunk, :, lanes]
                gain = gate_gain_ref[:, lanes]
                gated = mixed * gate
                scaled = gated * scale
                all_z[chunk, :, lanes] = (here * (scaled * gain)).astype(BF16)
                gain_ref[0:1, lanes] += jnp.sum(d_yn * scaled, axis=0, keepdims=True)
                d_gated = scale * (gain * d_yn) - gated * slant
                v_dz[slot, :, lanes] = (d_gated * mixed * gate_slope).astype(BF16)
                v_dssd[slot, :, lanes] = (d_gated * gate).astype(BF16)
            normed_gate = all_z[chunk]
            v_yt[slot] = normed_gate.T
            v_mixed[slot] = mm(normed_gate, v_o[...]).astype(BF16)
            for copy in stores(chunk):
                copy.start()
            return carry

        lax.fori_loop(0, blocks, gate_part, 0)
        for chunk in (n_ctx - 2, n_ctx - 1):
            for copy in stores(chunk):
                copy.wait()


def scan_forward(
    n, direct, unit, n_ctx, length, px, ps, normed, out_weight, w_z, upstream, taps_x, taps_s, gate_gain, skip, head
):
    tokens, width = px.shape
    heads = width // HEAD
    count = tokens // BLOCK
    model = out_weight.shape[1]
    assert count == n_ctx
    by_block = lambda i: (i, 0)
    at_block = lambda size: pl.BlockSpec((BLOCK, size), by_block)
    whole = lambda a: pl.BlockSpec(a.shape, lambda i: (0, 0))
    any_space = pl.BlockSpec(memory_space=pl.ANY)
    low = lambda *shape: jax.ShapeDtypeStruct(shape, BF16)
    full = lambda *shape: jax.ShapeDtypeStruct(shape, F32)
    v_low = lambda *shape: pltpu.VMEM(shape, BF16)
    v_full = lambda *shape: pltpu.VMEM(shape, F32)
    dma = pltpu.SemaphoreType.DMA
    return pl.pallas_call(
        functools.partial(forward_kernel, heads, unit, n_ctx, n, direct),
        grid=(count,),
        in_specs=[
            pl.BlockSpec(memory_space=pltpu.SMEM),
            at_block(width),
            at_block(ps.shape[1]),
            at_block(model),
            any_space,
            any_space,
            any_space,
        ]
        + [whole(a) for a in (taps_x, taps_s, gate_gain, skip, head)],
        out_specs=[
            at_block(width),
            at_block(STATE),
            at_block(STATE),
            at_block(width),
            at_block(2 * STATE),
            at_block(LANES),
            at_block(LANES),
            at_block(LANES),
            pl.BlockSpec((1, STATE, width), lambda i: (i, 0, 0)),
            pl.BlockSpec((8, width), lambda i: (0, 0)),
            any_space,
            any_space,
            any_space,
            any_space,
        ],
        out_shape=[
            low(tokens, width),
            low(tokens, STATE),
            low(tokens, STATE),
            low(tokens, width),
            low(tokens, 2 * STATE),
            full(tokens, LANES),
            full(tokens, LANES),
            full(tokens, LANES),
            low(count, STATE, width),
            full(8, width),
            low(count, width, BLOCK),
            low(count, BLOCK, model),
            low(tokens, width),
            low(tokens, width),
        ],
        scratch_shapes=[
            v_full(STATE, width),
            v_full(8, width),
            v_full(8, 2 * STATE),
            v_low(width, model),
            v_low(*w_z.shape),
            v_low(count, BLOCK, model),
            v_full(count, BLOCK, width),
            v_low(count, BLOCK, width),
            v_full(count, BLOCK, width),
            v_low(2, width, BLOCK),
            v_low(2, BLOCK, model),
            v_low(2, BLOCK, width),
            v_low(2, BLOCK, width),
            v_full(n_ctx, count, 8, BLOCK),
            v_full(count, BLOCK, 8),
            dma((3,)),
            dma((2, 4)),
            dma((2, 2)),
            dma((2, 2, n - 1)),
            dma,
            dma((3,)),
            dma((3,)),
        ],
        compiler_params=pltpu.CompilerParams(
            collective_id=2, has_side_effects=True, vmem_limit_bytes=58 * 1024 * 1024
        ),
        name="scan_forward",
    )(length, px, ps, normed, out_weight, w_z, upstream, taps_x, taps_s, gate_gain, skip, head)


def head_sums(product, chooser):
    high = product.astype(BF16)
    rest = (product - high.astype(F32)).astype(BF16)
    return mm(high, chooser) + mm(rest, chooser)


def backward_kernel(
    heads,
    unit,
    n_ctx,
    n,
    px_ref,
    ps_ref,
    x_ref,
    b_ref,
    c_ref,
    slope_x_ref,
    slope_s_ref,
    lam_ref,
    step_ref,
    chain_ref,
    kept_ref,
    dssd_ref,
    gate_t,
    normed_t,
    upstream,
    d_z,
    mixed_parts,
    hidden,
    gain_grads_ref,
    taps_x_ref,
    taps_s_ref,
    skip_ref,
    head_ref,
    dx_ref,
    ds_ref,
    small_ref,
    shard_o,
    shard_z,
    layer_out,
    back,
    mixed_grads,
    for_step,
    for_level,
    left,
    right,
    sums,
    after_x,
    after_s,
    v_left,
    v_right,
    products,
    slots,
    stage,
    done_o,
    done_z,
    mine,
    from_core,
    from_row,
    v_hidden,
    load_sem,
    store_sem,
    ring_send,
    ring_recv,
    part_send,
    part_recv,
):
    turn = pl.program_id(0)
    turns = heads // 2 // POINTS
    block = pl.num_programs(0) - 1 - turn
    width, model = x_ref.shape[1], v_hidden.shape[1]
    own = hidden.shape[0]
    ring = Ring(n)
    around = Around(ring.me, ring.shard)
    piece, size = slots.shape[4], slots.shape[5]
    sum_mixed = TokenSum(
        around, mixed_parts, mine.at[0], mine.at[1], from_core, from_row, part_send, part_recv
    )
    loads = [
        pltpu.make_async_copy(source, target, load_sem.at[i])
        for i, (source, target) in enumerate(
            (
                *((gate_t.at[c], v_left.at[pl.ds(0, width), pl.ds(c * own, own)]) for c in range(n_ctx)),
                *((upstream.at[c], v_right.at[pl.ds(c * own, own), pl.ds(0, model)]) for c in range(n_ctx)),
                *((normed_t.at[c], v_left.at[pl.ds(width, model), pl.ds(c * own, own)]) for c in range(n_ctx)),
                (d_z, v_right.at[:, pl.ds(model, width)]),
                *sum_mixed.loads(),
                (hidden, v_hidden),
            )
        )
    ]
    ring_loads = 1 + 3 * n_ctx

    def partial_sum(kind, way, sub, index):
        first = (1 - kind) * index * piece + kind * (width + (2 * index + way) * piece)
        at = (1 - kind) * (2 * way + sub) * size + kind * (model + sub * size)
        return mm(
            v_left[pl.ds(pl.multiple_of(first, 16), piece), :],
            v_right[:, pl.ds(pl.multiple_of(at, LANES), size)],
        )

    def all_products():
        tile = max(2 * piece, BLOCK)
        shards = tile // (2 * piece)

        def out_rows(i, carry):
            rows = pl.ds(pl.multiple_of(i * BLOCK, BLOCK), BLOCK)
            left = v_left[rows, :]
            products[rows, 0:width] = mm(left, v_right[:, 0:width]).astype(BF16)
            products[rows, width:model] = mm(left, v_right[:, width:model]).astype(BF16)
            return carry

        def in_rows(i, carry):
            left = v_left[pl.ds(pl.multiple_of(width + i * tile, 16), tile), :]
            both = mm(left, v_right[:, model:]).astype(BF16)
            for j in range(shards):
                place = pl.ds(pl.multiple_of((i * shards + j) * piece, 16), piece)
                for way in (0, 1):
                    products[place, model + way * width : model + (way + 1) * width] = both[
                        (2 * j + way) * piece : (2 * j + way + 1) * piece
                    ]
            return carry

        lax.fori_loop(0, width // BLOCK, out_rows, 0)
        lax.fori_loop(0, model // tile, in_rows, 0)

    def product(kind, way, sub, index):
        at = pl.multiple_of(kind * model + way * width + sub * size, LANES)
        return products[pl.ds(pl.multiple_of(index * piece, 16), piece), pl.ds(at, size)]

    def hop(kind, way, sub, step, source):
        return remote(
            source,
            slots.at[kind, step, way, sub],
            ring_send.at[kind, way, sub],
            ring_recv.at[kind, way, sub, step],
            (ring.me, ring.at(1 - 2 * way)),
        )

    def streams(body):
        def one(e, carry):
            body(e // 4, e // 2 % 2, e % 2)
            return carry

        lax.fori_loop(0, 8, one, 0)

    def start_ring(kind, way, sub):
        place = stage.at[kind, way, sub]
        place[...] = partial_sum(kind, way, sub, ring.at(2 * way - 1)).astype(BF16)
        hop(kind, way, sub, 0, place).start()

    def ring_step(step):
        def body(kind, way, sub):
            index = ring.at((step + 2) * (2 * way - 1))
            hop(kind, way, sub, step, stage.at[kind, way, sub]).wait()
            place = slots.at[kind, step, way, sub]
            total = place[...].astype(F32) + product(kind, way, sub, index).astype(F32)

            @pl.when(step < n - 2)
            def _():
                place[...] = total.astype(BF16)
                hop(kind, way, sub, step + 1, place).start()

            @pl.when(jnp.logical_and(step == n - 2, kind == 0))
            def _():
                at = pl.multiple_of((2 * way + sub) * size, LANES)
                done_o[:, pl.ds(at, size)] = total.astype(BF16)

            @pl.when(jnp.logical_and(step == n - 2, kind == 1))
            def _():
                done_z[way, pl.ds(pl.multiple_of(sub * size, 16), size), :] = total.T.astype(BF16)

        streams(body)

    def serve(point):
        at = turn * POINTS + point
        points = POINTS * n_ctx
        lax.fori_loop(
            at * (n - 1) // points,
            (at + 1) * (n - 1) // points,
            lambda step, carry: (ring_step(step), carry)[1],
            0,
        )

    @pl.when(turn == 0)
    def _():
        for device in around.all:
            greet(device)
        greet(ring.neighbour(0))
        greet(ring.neighbour(1))
        for copy in loads:
            copy.start()
        back[...] = jnp.zeros_like(back)
        small_ref[...] = jnp.zeros_like(small_ref)
        small_ref[taps_x_ref.shape[0] : taps_x_ref.shape[0] + 1, 0:width] = gain_grads_ref[0:1, :]
        after_x[...] = jnp.zeros_like(after_x)
        after_s[...] = jnp.zeros_like(after_s)
        pl.semaphore_wait(pltpu.get_barrier_semaphore(), 5)
        for copy in loads[:ring_loads]:
            copy.wait()
        streams(start_ring)
        sum_mixed.start()
        all_products()
        for copy in loads[ring_loads:]:
            copy.wait()

    @pl.when(turn == 1)
    def _():
        sum_mixed.pass_row()

    taps = taps_x_ref.shape[0] - 1

    rows_b, rows_c = b_ref[...], c_ref[...]
    step = step_ref[...]
    lam = lam_ref[...]
    gram = mm(rows_c, rows_b, ((1,), (1,)))
    gram_t = mm(rows_b, rows_c, ((1,), (1,)))
    level, across, last, weight, fade = levels(lam, step)
    out_decay = jnp.exp(level - level[BLOCK - 1 : BLOCK, :])
    step_across = step.T
    at_row, at_col = iota2((BLOCK, BLOCK), 0), iota2((BLOCK, BLOCK), 1)
    order = (at_row > at_col).astype(F32) - (at_row < at_col).astype(F32)
    low_half = iota2((1, LANES), 1) < HEAD
    lane = iota2((1, LANES), 1)
    by_state = rows_c.T
    kept = kept_ref[0]
    old_back = back[...].astype(BF16)
    entering = mm(rows_c, kept)
    leaving = mm(rows_b, old_back)
    at_last = jnp.sum(kept.astype(F32) * back[...], axis=0, keepdims=True)
    mixed_grads[...] = jnp.zeros_like(mixed_grads)
    left[...] = jnp.zeros_like(left)
    right[...] = jnp.zeros_like(right)
    sums[...] = jnp.zeros_like(sums)
    d_b = jnp.zeros((BLOCK, STATE), F32)
    d_c = jnp.zeros((BLOCK, STATE), F32)

    def conv_back(d_conv, after, current, weight):
        padded = jnp.concatenate([d_conv, after], axis=0)
        d_in = jnp.zeros_like(d_conv)
        grads = []
        for k in range(taps):
            moved = padded[taps - 1 - k : taps - 1 - k + BLOCK]
            d_in += weight[k : k + 1] * moved
            grads.append(jnp.sum(current * moved, axis=0, keepdims=True))
        grads.append(jnp.sum(d_conv, axis=0, keepdims=True))
        return d_in, jnp.concatenate(grads, axis=0)

    for first in range(0, heads, 2):
        lanes = slice(first * HEAD, (first + 2) * HEAD)
        x_low = x_ref[:, lanes]
        x = x_low.astype(F32)
        grad_low = dssd_ref[:, lanes]
        grad = grad_low.astype(F32)
        through = jnp.zeros((BLOCK, LANES), F32)
        for head, keep in ((first, low_half), (first + 1, jnp.logical_not(low_half))):
            decay = spread(level, across, head)
            grad_own = jnp.where(keep, grad, 0.0).astype(BF16)
            pairs = mm(grad_own, x_low, ((1,), (1,)))
            through += mm((gram_t * decay).astype(BF16), grad_own)
            scaled = decay * pairs * step_across[head : head + 1, :]
            mixed_grads[...] += scaled
            ordered = gram * scaled * order
            left[...] = jnp.where(
                lane == head, jnp.sum(ordered, axis=1, keepdims=True), left[...]
            )
            right[head : head + 1, :] = jnp.sum(ordered, axis=0, keepdims=True)
        weight_pair = pair_of(weight, first, low_half)
        step_pair = pair_of(step, first, low_half)
        fade_pair = pair_of(fade, first, low_half)
        out_pair = pair_of(out_decay, first, low_half)
        leave = leaving[:, lanes]
        d_x = step_pair * through + weight_pair * leave + skip_ref[:, lanes] * grad
        for_step[:, lanes] = x * (through + out_pair * leave)
        weighted = weight_pair * x
        faded = fade_pair * grad
        for_level[:, lanes] = weighted * leave - faded * entering[:, lanes]
        sums[0:1, lanes] = jnp.sum(weighted * leave, axis=0, keepdims=True)
        sums[2:3, lanes] = jnp.sum(x * grad, axis=0, keepdims=True)
        faded_low = faded.astype(BF16)
        d_b += mm(weighted.astype(BF16), old_back[:, lanes], ((1,), (1,)))
        d_c += mm(faded_low, kept[:, lanes], ((1,), (1,)))
        back[:, lanes] = back[:, lanes] * pair_of(last, first, low_half) + mm(by_state, faded_low)
        d_conv = d_x * slope_x_ref[:, lanes].astype(F32)
        d_in, grads = conv_back(
            d_conv, after_x[:, lanes], px_ref[:, lanes].astype(F32), taps_x_ref[:, lanes]
        )
        after_x[:, lanes] = d_conv[0:8]
        dx_ref[:, lanes] = d_in.astype(BF16)
        small_ref[0 : taps + 1, lanes] += grads
        if first // 2 % turns == turns - 1 and first // 2 // turns < POINTS - 1:
            serve(first // 2 // turns)

    all_pairs = mixed_grads[...]
    d_b = d_b + mm(all_pairs.T.astype(BF16), rows_c)
    d_c = d_c + mm(all_pairs.astype(BF16), rows_b)
    d_conv = jnp.concatenate([d_b, d_c], axis=1) * slope_s_ref[...].astype(F32)
    d_in, grads = conv_back(
        d_conv, after_s[...], ps_ref[:, : 2 * STATE].astype(F32), taps_s_ref[...]
    )
    after_s[...] = d_conv[0:8]
    ds_ref[:, : 2 * STATE] = d_in.astype(BF16)
    small_ref[0 : taps + 1, width:] += grads

    chooser = (iota2((width, LANES), 0) // HEAD == iota2((width, LANES), 1)).astype(BF16)
    d_step = head_sums(for_step[...], chooser)
    sums[1:2, :] = at_last
    total = head_sums(sums[...], chooser)
    d_level = head_sums(for_level[...], chooser) - left[...] + right[...].T
    final = -total[0:1, :] - last * total[1:2, :]
    d_level = d_level + jnp.where(iota2((BLOCK, 1), 0) == BLOCK - 1, final, 0.0)
    d_lam = mm_exact((at_row <= at_col).astype(F32), d_level)
    d_raw = (d_step + d_lam * head_ref[1:2]) * chain_ref[...]
    head_row = taps + 2
    small_ref[head_row : head_row + 1, 0:LANES] += jnp.sum(d_raw, axis=0, keepdims=True)
    small_ref[head_row : head_row + 1, LANES : 2 * LANES] += jnp.sum(
        d_lam * lam, axis=0, keepdims=True
    )
    small_ref[head_row : head_row + 1, 2 * LANES : 3 * LANES] += total[2:3, :]
    chosen = chosen_heads(lax.axis_index("ctx"), heads, unit, n_ctx, True)
    ds_ref[:, 2 * STATE :] = mm(d_raw.astype(BF16), chosen).astype(BF16)

    serve(POINTS - 1)

    @pl.when(turn == pl.num_programs(0) - 1)
    def _():
        stores = [
            pltpu.make_async_copy(source, target, store_sem.at[i])
            for i, (source, target) in enumerate(
                ((done_o, shard_o), (done_z, shard_z), (v_hidden, layer_out))
            )
        ]
        stores[0].start()
        stores[1].start()
        v_hidden[...] = (v_hidden[...].astype(F32) + sum_mixed.total()).astype(BF16)
        stores[2].start()
        for copy in stores:
            copy.wait()


def scan_backward(
    n, unit, n_ctx, px, ps, kept_parts, d_ssd, gate_t, normed_t, upstream, d_z, mixed_parts, hidden, gain_grads, taps_x, taps_s, skip, head
):
    x, rows_b, rows_c, slope_x, slope_s, lam, step, chain, kept = kept_parts
    tokens, width = px.shape
    heads = width // HEAD
    count = tokens // BLOCK
    own, model = hidden.shape
    shared_width = ps.shape[1]
    piece = width // n
    assert model == 2 * width and heads // 2 % POINTS == 0
    by_block = lambda i: (count - 1 - i, 0)
    at_block = lambda size: pl.BlockSpec((BLOCK, size), by_block)
    whole = lambda a: pl.BlockSpec(a.shape, lambda i: (0, 0))
    any_space = pl.BlockSpec(memory_space=pl.ANY)
    low = lambda *shape: jax.ShapeDtypeStruct(shape, BF16)
    v_low = lambda *shape: pltpu.VMEM(shape, BF16)
    v_full = lambda *shape: pltpu.VMEM(shape, F32)
    part = lambda a, b: pl.BlockSpec((1, a, b), lambda i: (count - 1 - i, 0, 0))
    small_shape = (8, width + 2 * STATE)
    dma = pltpu.SemaphoreType.DMA
    return pl.pallas_call(
        functools.partial(backward_kernel, heads, unit, n_ctx, n),
        grid=(count,),
        in_specs=[
            at_block(width),
            at_block(shared_width),
            at_block(width),
            at_block(STATE),
            at_block(STATE),
            at_block(width),
            at_block(2 * STATE),
            at_block(LANES),
            at_block(LANES),
            at_block(LANES),
            part(STATE, width),
            at_block(width),
        ]
        + [any_space] * 6
        + [whole(a) for a in (gain_grads, taps_x, taps_s, skip, head)],
        out_specs=[
            at_block(width),
            at_block(shared_width),
            pl.BlockSpec(small_shape, lambda i: (0, 0)),
            any_space,
            any_space,
            any_space,
        ],
        out_shape=[
            low(tokens, width),
            low(tokens, shared_width),
            jax.ShapeDtypeStruct(small_shape, F32),
            low(piece, model),
            low(2, width, piece),
            low(own, model),
        ],
        scratch_shapes=[
            v_full(STATE, width),
            v_full(BLOCK, BLOCK),
            v_full(BLOCK, width),
            v_full(BLOCK, width),
            v_full(BLOCK, LANES),
            v_full(LANES, BLOCK),
            v_full(8, width),
            v_full(8, width),
            v_full(8, 2 * STATE),
            v_low(width + model, tokens),
            v_low(tokens, model + width),
            v_low(width, 2 * model),
            v_low(2, n - 1, 2, 2, piece, width // 2),
            v_low(2, 2, 2, piece, width // 2),
            v_low(piece, model),
            v_low(2, width, piece),
            v_low(2, own, model),
            v_low(2, own, model),
            v_low(own, model),
            v_low(own, model),
            dma((4 + 3 * n_ctx,)),
            dma((3,)),
            dma((2, 2, 2)),
            dma((2, 2, 2, n - 1)),
            dma((3,)),
            dma((3,)),
        ],
        compiler_params=pltpu.CompilerParams(
            collective_id=3, has_side_effects=True, vmem_limit_bytes=59 * 1024 * 1024
        ),
        name="scan_backward",
    )(
        px, ps, x, rows_b, rows_c, slope_x, slope_s, lam, step, chain, kept, d_ssd, gate_t, normed_t, upstream, d_z, mixed_parts, hidden, gain_grads, taps_x, taps_s, skip, head
    )


def gather_kernel(
    n,
    n_ctx,
    unit,
    hidden,
    cotangent,
    in_weight_t,
    small,
    cotangent_all,
    w_x,
    w_s,
    w_z,
    small_out,
    proj_x,
    proj_s,
    normed_out,
    normed_t,
    v_hidden,
    v_normed,
    v_x,
    v_s,
    own_z,
    v_small,
    raw_x,
    raw_s,
    raw_z,
    out_x,
    out_s,
    out_t,
    v_gain,
    load_sem,
    column_sem,
    local_sem,
    keep_sem,
    store_sem,
    ring_send,
    ring_recv,
    ctx_send,
    ctx_recv,
):
    ring = Ring(n)
    me, shard = ring.me, ring.shard
    width, model = v_x.shape[1], v_x.shape[0]
    inner = width * n_ctx
    r = model // n
    shared = in_weight_t.shape[0] - 2 * inner
    row = me // 2
    other_core = (me + 1 - 2 * (me % 2), shard)
    other_row = (me + 2 - 4 * row, shard)
    barrier = pltpu.get_barrier_semaphore()
    for device in (other_core, other_row, ring.neighbour(0), ring.neighbour(1)):
        pl.semaphore_signal(barrier, inc=1, device_id=device, device_id_type=MESH)

    part = unit * HEAD

    def load_columns(base, target, sems):
        return [
            pltpu.make_async_copy(
                in_weight_t.at[pl.ds(pl.multiple_of(base + (a * n_ctx + me) * part, 16), part)],
                target.at[pl.ds(a * part, part)],
                sems.at[a],
            )
            for a in range(width // part)
        ]

    loads = [
        load_columns(inner, raw_x, column_sem.at[0]),
        [
            pltpu.make_async_copy(
                in_weight_t.at[pl.ds(2 * inner, shared)], raw_s.at[pl.ds(0, shared)], load_sem.at[0]
            )
        ],
        [pltpu.make_async_copy(small, v_small.at[shard], load_sem.at[1])],
        [pltpu.make_async_copy(hidden, v_hidden.at[me], load_sem.at[2])],
        load_columns(0, raw_z, column_sem.at[1]),
    ]
    for copies in loads:
        for copy in copies:
            copy.start()

    def loaded(i):
        for copy in loads[i]:
            copy.wait()

    pl.semaphore_wait(barrier, 4)

    half = width // 2
    rows = r // 2
    both_rows = lambda index, way: pl.ds(pl.multiple_of((2 * index + way) * rows, 16), rows)
    x_part = lambda a, sub: lambda index, way: a.at[both_rows(index, way), pl.ds(sub * half, half)]
    s_part = lambda index, way: v_s.at[both_rows(index, way)]
    small_part = lambda index, way: v_small.at[index, pl.ds(way * SMALL_ROWS // 2, SMALL_ROWS // 2)]
    phases = (
        ((0, small_part), (1, s_part), (2, x_part(v_x, 0)), (3, x_part(v_x, 1))),
        ((4, x_part(w_z, 0)), (5, x_part(w_z, 1))),
    )

    def hop(stream, way, step):
        number, part = stream
        place = part(ring.at(-step if way == 0 else step), way)
        return remote(
            place, place, ring_send.at[number, way], ring_recv.at[number, way, step],
            ring.neighbour(way),
        )

    def arrives(stream, way, step):
        number, part = stream
        landed = part(ring.at(-step - 1 if way == 0 else step + 1), way)
        return remote(
            landed, landed, ring_send.at[number, way], ring_recv.at[number, way, step],
            ring.neighbour(way),
        )

    def start_stream(stream):
        for way in (0, 1):
            hop(stream, way, 0).start()

    def to_row(i, a, whole):
        return remote(a, whole.at[me], ctx_send.at[i, 0], ctx_recv.at[i, 0], other_row)

    def to_core(i, a, whole):
        return remote(a, whole.at[me], ctx_send.at[i, 1], ctx_recv.at[i, 1], other_core)

    def pass_on(i, whole):
        beyond = whole.at[other_row[0]]
        return remote(beyond, beyond, ctx_send.at[i, 2], ctx_recv.at[i, 2], other_core)

    to_row(0, hidden, v_hidden).start()
    to_core(0, hidden, v_hidden).start()
    own_rows = pl.ds(pl.multiple_of(shard * r, 16), r)
    loaded(2)
    start_stream(phases[0][0])
    loaded(0)
    v_x[own_rows, :] = raw_x[...].T
    start_stream(phases[0][2])
    start_stream(phases[0][3])
    loaded(1)
    raw_s[shared:, :] = jnp.zeros((raw_s.shape[0] - shared, r), BF16)
    v_s[own_rows, :] = raw_s[...].T
    start_stream(phases[0][1])
    keep_cotangent = pltpu.make_async_copy(cotangent, cotangent_all.at[me], local_sem)
    keep_cotangent.start()
    loaded(3)
    loaded(4)
    own_z[...] = raw_z[...].T
    keep_z = pltpu.make_async_copy(own_z, w_z.at[own_rows], keep_sem)
    keep_z.start()
    keep_z.wait()

    def run_phase(number, work, after):
        def body(step, carry):
            for stream in phases[number]:
                for way in (0, 1):
                    arrives(stream, way, step).wait_recv()
                    hop(stream, way, step).wait_send()
                    hop(stream, way, step + 1).start()
            if work is not None:

                @pl.when(step < n_ctx)
                def _():
                    work(step)

            return carry

        lax.fori_loop(0, n - 2, body, 0)
        after()
        for stream in phases[number]:
            for way in (0, 1):
                arrives(stream, way, n - 2).wait_recv()
                hop(stream, way, n - 2).wait_send()

    tokens = v_hidden.shape[1]

    def project_first(chunk):
        at = pl.ds(pl.multiple_of(chunk * tokens, tokens), tokens)
        resid = v_hidden[chunk].astype(F32)
        scale = lax.rsqrt(jnp.mean(resid * resid, axis=1, keepdims=True) + EPS)
        normed = (resid * scale * v_gain[...]).astype(BF16)
        v_normed[at, :] = normed
        out_x[at, :] = mm(normed, v_x[...]).astype(BF16)
        out_s[at, :] = mm(normed, v_s[...]).astype(BF16)
        out_t[chunk] = normed.T

    stores = [
        pltpu.make_async_copy(source, target, store_sem.at[i])
        for i, (source, target) in enumerate(
            (
                (v_x, w_x),
                (v_s, w_s),
                (v_small, small_out),
                (out_x, proj_x),
                (out_s, proj_s),
                (v_normed, normed_out),
                (out_t, normed_t),
            )
        )
    ]

    def after_first():
        for stream in phases[1]:
            start_stream(stream)
        to_row(0, hidden, v_hidden).wait_recv()
        pass_on(0, v_hidden).start()
        to_row(1, cotangent, cotangent_all).start()
        to_core(1, cotangent, cotangent_all).start()
        to_row(0, hidden, v_hidden).wait_send()
        to_core(0, hidden, v_hidden).wait()
        pass_on(0, v_hidden).wait()

    def after_second():
        to_row(1, cotangent, cotangent_all).wait_recv()
        pass_on(1, cotangent_all).start()
        for copy in stores[3:]:
            copy.start()

    run_phase(0, None, after_first)
    for f in range(n):
        v_gain[:, f * r : (f + 1) * r] = v_small[f, 0:1, 0:r].astype(F32)
    for copy in stores[0:3]:
        copy.start()
    run_phase(1, project_first, after_second)
    to_row(1, cotangent, cotangent_all).wait_send()
    to_core(1, cotangent, cotangent_all).wait()
    pass_on(1, cotangent_all).wait()
    keep_cotangent.wait()
    for copy in stores:
        copy.wait()


def gather_all(n, n_ctx, unit, width, hidden, cotangent, in_weight_t, small, shared_width):
    own, model = hidden.shape
    tokens = own * n_ctx
    rows = in_weight_t.shape[1]
    any_space = pl.BlockSpec(memory_space=pl.ANY)
    low = lambda *shape: jax.ShapeDtypeStruct(shape, BF16)
    v_low = lambda *shape: pltpu.VMEM(shape, BF16)
    dma = pltpu.SemaphoreType.DMA
    return pl.pallas_call(
        functools.partial(gather_kernel, n, n_ctx, unit),
        in_specs=[any_space] * 4,
        out_specs=[any_space] * 9,
        out_shape=[
            low(n_ctx, own, model),
            low(model, width),
            low(model, shared_width),
            low(model, width),
            low(n, small.shape[0], small.shape[1]),
            low(tokens, width),
            low(tokens, shared_width),
            low(tokens, model),
            low(n_ctx, model, own),
        ],
        scratch_shapes=[
            v_low(n_ctx, own, model),
            v_low(tokens, model),
            v_low(model, width),
            v_low(model, shared_width),
            v_low(rows, width),
            v_low(n, small.shape[0], small.shape[1]),
            v_low(width, rows),
            v_low(shared_width, rows),
            v_low(width, rows),
            v_low(tokens, width),
            v_low(tokens, shared_width),
            v_low(n_ctx, model, own),
            pltpu.VMEM((1, model), F32),
            dma((3,)),
            dma((2, width // (unit * HEAD))),
            dma,
            dma,
            dma((7,)),
            dma((6, 2)),
            dma((6, 2, n - 1)),
            dma((2, 3)),
            dma((2, 3)),
        ],
        compiler_params=pltpu.CompilerParams(
            collective_id=0, has_side_effects=True, vmem_limit_bytes=56 * 1024 * 1024
        ),
        name="gather_all",
    )(hidden, cotangent, in_weight_t, small)


def reduce_kernel(
    n,
    n_ctx,
    direct,
    normed_t,
    d_z,
    d_x,
    d_s,
    w_z,
    w_x,
    w_s,
    shard_o,
    shard_z,
    small,
    hidden,
    cotangent,
    gain,
    g_z,
    g_x,
    g_s,
    g_o,
    hidden_grad,
    small_out,
    norm_out,
    v_normed_t,
    v_d_z,
    v_d_x,
    v_d_s,
    v_z,
    v_x,
    v_s,
    parts,
    partials,
    slots,
    stage,
    done,
    moved,
    from_core,
    from_row,
    v_hidden,
    v_cotangent,
    v_gain,
    small_all,
    small_ctx,
    norm_all,
    norm_ctx,
    load_sem,
    store_sem,
    ring_send,
    ring_recv,
    ctx_send,
    ctx_recv,
    own_sem,
    piece_send,
    piece_recv,
    part_send,
    part_recv,
    small_send,
    small_recv,
    small_ctx_send,
    small_ctx_recv,
):
    ring = Ring(n)
    me, shard = ring.me, ring.shard
    around = Around(me, shard)
    core, row = me % 2, me // 2
    piece_peer = (shard % n_ctx, shard // n_ctx * n_ctx + me)
    moves = shard % n_ctx != me
    barrier = pltpu.get_barrier_semaphore()
    for device in around.all:
        greet(device)
    lax.fori_loop(1, n, lambda j, carry: (greet((me, lax.rem(shard + j, n))), carry)[1], 0)
    own = hidden.shape[0]
    sum_normed = TokenSum(
        around, parts, parts.at[me], parts.at[around.row_at], from_core, from_row, part_send, part_recv
    )
    sum_small, sum_norm = (
        SmallSum(
            n, around, whole, sums, small_send.at[i], small_recv.at[i], small_ctx_send.at[i], small_ctx_recv.at[i]
        )
        for i, (whole, sums) in enumerate(((small_all, small_ctx), (norm_all, norm_ctx)))
    )
    loads = [
        pltpu.make_async_copy(source, target, load_sem.at[i])
        for i, (source, target) in enumerate(
            (
                *((normed_t.at[c], v_normed_t.at[:, pl.ds(c * own, own)]) for c in range(n_ctx)),
                (d_s, v_d_s),
                (d_x, v_d_x),
                (small, small_all.at[shard]),
                (d_z, v_d_z),
                (w_z, v_z),
                (w_x, v_x),
                (w_s, v_s),
                (hidden, v_hidden),
                (cotangent, v_cotangent),
                (gain, v_gain),
            )
        )
    ]
    ring_loads = n_ctx + 2
    for copy in loads:
        copy.start()
    if direct:
        pl.semaphore_wait(barrier, n + 2)
    else:

        @pl.when(moves)
        def _():
            greet(piece_peer)
            pl.semaphore_wait(barrier, n + 3)

        @pl.when(jnp.logical_not(moves))
        def _():
            pl.semaphore_wait(barrier, n + 2)

    rows = v_normed_t.shape[0] // (2 * n)
    half, last = v_d_x.shape[1] // 2, v_d_s.shape[1]
    streams = (
        (0, v_d_s, 0, last, 2 * half),
        (1, v_d_x, 0, half, 0),
        (2, v_d_x, half, half, half),
    )

    def compute_partials(step):
        for way in (0, 1):
            index = ring.at(-step - 2 if way == 0 else step + 2)
            left = v_normed_t[pl.ds(pl.multiple_of((2 * index + way) * rows, 16), rows), :]
            partials[way, :, 2 * half :] = mm(left, v_d_s[...])
            partials[way, :, 0 : 2 * half] = mm(left, v_d_x[...])

    def slot(stream, way, step):
        return slots.at[step, way, :, pl.ds(stream[4], stream[3])]

    def hop(stream, way, step, source):
        return remote(
            source,
            slot(stream, way, step),
            ring_send.at[stream[0], way],
            ring_recv.at[stream[0], way, step],
            ring.neighbour(way),
        )

    def first_part(stream, way):
        return stage.at[way, :, pl.ds(stream[4], stream[3])]

    def arrived(stream, way, step):
        hop(stream, way, step, first_part(stream, way)).wait()
        partial = partials[way, :, stream[4] : stream[4] + stream[3]]
        return slot(stream, way, step)[...].astype(F32) + partial

    done_of = lambda stream: done.at[pl.ds(stream[4], stream[3])]
    of_x = lambda c, first: g_x.at[c, pl.ds(first, half)]
    shares = (
        (shard_o if direct else moved, lambda c: g_o.at[c]),
        (shard_z, lambda c: g_z.at[c]),
        (done_of(streams[1]), lambda c: of_x(c, 0)),
        (done_of(streams[2]), lambda c: of_x(c, half)),
        (done_of(streams[0]), lambda c: g_s.at[c]),
    )

    def share(i, kind):
        source, whole = shares[i]
        at = me
        if kind == 2:
            source, at = whole(around.row_at), around.row_at
        device = around.row if kind == 0 else around.core
        return remote(source, whole(at), ctx_send.at[i, kind], ctx_recv.at[i, kind], device)

    def keep(i):
        return pltpu.make_async_copy(shares[i][0], shares[i][1](me), own_sem.at[i])

    def start_share(i):
        share(i, 0).start()
        share(i, 1).start()
        keep(i).start()

    def pass_share(i):
        share(i, 0).wait_recv()
        share(i, 2).start()

    def close_share(i):
        share(i, 0).wait_send()
        share(i, 1).wait()
        share(i, 2).wait()
        keep(i).wait()

    def move_piece(wait):
        if direct:
            return
        keep_piece = pltpu.make_async_copy(shard_o, moved, piece_send)
        send_piece = remote(shard_o, moved, piece_send, piece_recv, piece_peer)

        @pl.when(moves)
        def _():
            send_piece.wait() if wait else send_piece.start()

        @pl.when(jnp.logical_not(moves))
        def _():
            keep_piece.wait() if wait else keep_piece.start()

    def normed_part(i, carry):
        to_row = row + (1 - i % 2) * (1 - 2 * row)
        to_core = core + (1 - i // 2) * (1 - 2 * core)
        at = 2 * to_row + to_core
        tokens = pl.ds(pl.multiple_of(at * own, own), own)
        parts[at] = (
            mm(v_d_z[tokens, :], v_z[...], ((1,), (1,)))
            + mm(v_d_x[tokens, :], v_x[...], ((1,), (1,)))
            + mm(v_d_s[tokens, :], v_s[...], ((1,), (1,)))
        ).astype(BF16)
        return carry

    store_grad = pltpu.make_async_copy(v_cotangent, hidden_grad, store_sem.at[0])
    store_small = pltpu.make_async_copy(small_ctx, small_out, store_sem.at[1])
    store_norm = pltpu.make_async_copy(norm_ctx, norm_out, store_sem.at[2])

    def finish_tokens():
        resid = v_hidden[...].astype(F32)
        scale = lax.rsqrt(jnp.mean(resid * resid, axis=1, keepdims=True) + EPS)
        d_normed = sum_normed.total()
        f = v_gain[...] * d_normed
        slope = scale**3 * jnp.mean(resid * f, axis=1, keepdims=True)
        grad = v_cotangent[...].astype(F32) + scale * f - resid * slope
        v_cotangent[...] = grad.astype(BF16)
        store_grad.start()
        by_model = jnp.sum(d_normed * resid * scale, axis=0, keepdims=True)
        size = norm_all.shape[2]
        for j in range(norm_all.shape[1]):
            norm_all[shard, j : j + 1, :] = by_model[:, j * size : (j + 1) * size]
        sum_norm.start()

    move_piece(False)
    for copy in loads[:ring_loads]:
        copy.wait()
    compute_partials(-1)
    for way in (0, 1):
        stage[way] = partials[way].astype(BF16)
        for stream in streams:
            hop(stream, way, 0, first_part(stream, way)).start()
    compute_partials(0)
    for copy in loads[ring_loads:]:
        copy.wait()
    sum_small.start()
    move_piece(True)
    start_share(0)
    start_share(1)

    def body(step, carry):
        for stream in streams:
            for way in (0, 1):
                total = arrived(stream, way, step)
                place = slot(stream, way, step)
                place[...] = total.astype(BF16)
                hop(stream, way, step + 1, place).start()
        compute_partials(step + 1)

        @pl.when(step < 2)
        def _():
            lax.fori_loop(2 * step, 2 * step + 2, normed_part, 0)

        @pl.when(step == 0)
        def _():
            sum_normed.start()

        @pl.when(step == 1)
        def _():
            sum_normed.pass_row()

        @pl.when(step == n - 3)
        def _():
            finish_tokens()

        return carry

    lax.fori_loop(0, n - 2, body, 0)
    sum_small.add()
    pass_share(0)
    pass_share(1)
    for number, shared in ((0, 4), (1, 2), (2, 3)):
        place = done_of(streams[number])
        for way in (0, 1):
            total = arrived(streams[number], way, n - 2)
            place[:, way * rows : (way + 1) * rows] = total.T.astype(BF16)
        start_share(shared)
    sum_norm.add()
    sum_small.finish()
    store_small.start()
    for i in (4, 2, 3):
        pass_share(i)
    sum_norm.finish()
    store_norm.start()
    for i in range(5):
        close_share(i)
    store_grad.wait()
    store_small.wait()
    store_norm.wait()


def reduce_all(
    n, n_ctx, direct, normed_t, d_z, d_x, d_s, w_z, w_x, w_s, shard_o, shard_z, small, hidden, cotangent, gain
):
    model, tokens = normed_t.shape[1], d_x.shape[0]
    width, shared_width = d_x.shape[1], d_s.shape[1]
    rows, piece, own = model // n, width // n, hidden.shape[0]
    columns = width + shared_width
    any_space = pl.BlockSpec(memory_space=pl.ANY)
    dma = pltpu.SemaphoreType.DMA
    low = lambda *shape: jax.ShapeDtypeStruct(shape, BF16)
    v_low = lambda *shape: pltpu.VMEM(shape, BF16)
    v_full = lambda *shape: pltpu.VMEM(shape, F32)
    norm_shape = (8, model // 8)
    return pl.pallas_call(
        functools.partial(reduce_kernel, n, n_ctx, direct),
        in_specs=[any_space] * 13,
        out_specs=[any_space] * 7,
        out_shape=[
            low(n_ctx, 2, width, rows // 2),
            low(n_ctx, width, rows),
            low(n_ctx, shared_width, rows),
            low(n_ctx, piece, model),
            low(own, model),
            jax.ShapeDtypeStruct((n_ctx,) + small.shape, F32),
            jax.ShapeDtypeStruct((n_ctx,) + norm_shape, F32),
        ],
        scratch_shapes=[
            v_low(model, tokens),
            v_low(tokens, width),
            v_low(tokens, width),
            v_low(tokens, shared_width),
            v_low(*w_z.shape),
            v_low(*w_x.shape),
            v_low(*w_s.shape),
            v_low(n_ctx, own, model),
            v_full(2, rows // 2, columns),
            v_low(n - 1, 2, rows // 2, columns),
            v_low(2, rows // 2, columns),
            v_low(columns, rows),
            v_low(piece, model),
            v_low(2, own, model),
            v_low(own, model),
            v_low(own, model),
            v_low(own, model),
            v_full(1, model),
            v_full(n, *small.shape),
            v_full(n_ctx, *small.shape),
            v_full(n, *norm_shape),
            v_full(n_ctx, *norm_shape),
            dma((10 + n_ctx,)),
            dma((3,)),
            dma((3, 2)),
            dma((3, 2, n - 1)),
            dma((5, 3)),
            dma((5, 3)),
            dma((5,)),
            dma,
            dma,
            dma((3,)),
            dma((3,)),
            dma((2, n - 1)),
            dma((2, n - 1)),
            dma((2, 3)),
            dma((2, 3)),
        ],
        compiler_params=pltpu.CompilerParams(
            collective_id=1, has_side_effects=True, vmem_limit_bytes=58 * 1024 * 1024
        ),
        name="reduce_all",
    )(
        normed_t, d_z, d_x, d_s, w_z, w_x, w_s, shard_o, shard_z, small, hidden, cotangent, gain
    )


def assemble_kernel(part, z_ref, x_ref, s_ref, out_ref):
    place = pl.program_id(0)
    n_ctx, size, half = x_ref.shape[0], x_ref.shape[1], z_ref.shape[3]

    def interleave(write):
        for a in range(size // part):
            for c in range(n_ctx):
                write(
                    slice((a * n_ctx + c) * part, (a * n_ctx + c + 1) * part),
                    c,
                    slice(a * part, (a + 1) * part),
                )

    def write_z(target, c, source):
        for way in (0, 1):
            out_ref[target, way * half : (way + 1) * half] = z_ref[c, way, source, :].astype(F32)

    def write_x(target, c, source):
        out_ref[target, :] = x_ref[c, source, :].astype(F32)

    @pl.when(place < n_ctx)
    def _():
        interleave(write_z)

    @pl.when(jnp.logical_and(place >= n_ctx, place < 2 * n_ctx))
    def _():
        interleave(write_x)

    @pl.when(place == 2 * n_ctx)
    def _():
        total = s_ref[0].astype(F32)
        for c in range(1, n_ctx):
            total += s_ref[c].astype(F32)
        out_ref[0 : total.shape[0], :] = total


def assemble(part, g_z, g_x, g_s, columns):
    n_ctx, width, rows = g_x.shape
    block = (n_ctx, width // n_ctx, rows)
    return pl.pallas_call(
        functools.partial(assemble_kernel, part),
        grid=(2 * n_ctx + 1,),
        in_specs=[
            pl.BlockSpec(
                (n_ctx, 2, width // n_ctx, rows // 2),
                lambda i: (0, 0, jnp.minimum(i, n_ctx - 1), 0),
            ),
            pl.BlockSpec(block, lambda i: (0, jnp.clip(i - n_ctx, 0, n_ctx - 1), 0)),
            pl.BlockSpec(g_s.shape, lambda i: (0, 0, 0)),
        ],
        out_specs=pl.BlockSpec((width, rows), lambda i: (i, 0)),
        out_shape=jax.ShapeDtypeStruct((columns, rows), F32),
        compiler_params=pltpu.CompilerParams(vmem_limit_bytes=58 * 1024 * 1024),
        name="assemble",
    )(g_z, g_x, g_s)


def on_device(
    hidden,
    cotangent,
    seq_lens,
    norm_gain,
    in_weight,
    conv_weight,
    conv_bias,
    dt_bias,
    a_log,
    d_skip,
    gate_gain,
    out_weight,
):
    n_ctx, n_fsdp = lax.axis_size("ctx"), lax.axis_size("fsdp")
    me, shard = lax.axis_index("ctx"), lax.axis_index("fsdp")
    taps = conv_weight.shape[0]
    heads_all = dt_bias.shape[0] * n_fsdp
    inner = out_weight.shape[0] * n_fsdp
    heads, width = heads_all // n_ctx, inner // n_ctx
    model = hidden.shape[2]
    both = 2 * STATE
    held = dt_bias.shape[0]
    direct = held % n_ctx == 0
    unit = held // n_ctx if direct else 1
    part = unit * HEAD
    shared_width = -(-(both + heads_all) // LANES) * LANES

    per_head = jnp.concatenate([dt_bias, a_log, d_skip])
    lines = [norm_gain[None], conv_weight, conv_bias[None], gate_gain[None], per_head[None]]
    longest = -(-max(a.shape[1] for a in lines) // LANES) * LANES
    small = jnp.concatenate([jnp.pad(a, ((0, 0), (0, longest - a.shape[1]))) for a in lines])
    small = jnp.pad(small, ((0, SMALL_ROWS - small.shape[0]), (0, 0)))
    upstream, w_x, w_s, w_z, small_all, proj_x, proj_s, normed, normed_t = gather_all(
        n_fsdp, n_ctx, unit, width, hidden[0], cotangent[0], in_weight.T, small, shared_width
    )

    def line(first, count, size):
        rows = small_all[:, first : first + count, :size]
        return jnp.moveaxis(rows, 0, 1).reshape(count, -1).astype(F32)

    def own(lines, size):
        by_part = lines.reshape(lines.shape[0], -1, n_ctx, size)
        return lax.dynamic_index_in_dim(by_part, me, 2, False).reshape(lines.shape[0], -1)

    gain_norm = line(0, 1, norm_gain.shape[0])
    conv_lines = line(1, taps + 1, conv_bias.shape[0])
    taps_x, taps_s = own(conv_lines[:, :inner], part), conv_lines[:, inner:]
    gain_gate = own(line(taps + 2, 1, gate_gain.shape[0]), part)
    each = small_all[:, taps + 3, : per_head.shape[0]].reshape(n_fsdp, 3, -1)
    each = own(jnp.moveaxis(each, 0, 1).reshape(3, -1).astype(F32), unit)
    head = jnp.pad(jnp.stack([each[0], jnp.exp(each[1])]), ((0, 0), (0, LANES - heads)))
    skip = jnp.repeat(each[2], HEAD)[None]

    *kept_parts, gain_grads, gate_t, mixed_parts, d_z, d_ssd = scan_forward(
        n_fsdp, direct, unit, n_ctx, seq_lens, proj_x, proj_s, normed, out_weight, w_z, upstream, taps_x, taps_s, gain_gate, skip, head
    )
    d_x, d_s, small_grads, shard_o, shard_z, layer_out = scan_backward(
        n_fsdp, unit, n_ctx, proj_x, proj_s, kept_parts, d_ssd, gate_t, normed_t, upstream, d_z, mixed_parts, hidden[0], gain_grads, taps_x, taps_s, skip, head
    )
    g_z, g_x, g_s, g_o, hidden_grad, sums, norm_sums = reduce_all(
        n_fsdp, n_ctx, direct, normed_t, d_z, d_x, d_s, w_z, w_x, w_s, shard_o, shard_z, small_grads, hidden[0], cotangent[0], gain_norm
    )
    grad_in_weight = assemble(part, g_z, g_x, g_s, 2 * inner + both + heads_all).T
    grad_out_weight = g_o.reshape(-1, model).astype(F32)

    def shard_of(lines):
        size = lines.shape[1] // n_fsdp
        return lax.dynamic_slice_in_dim(lines, shard * size, size, axis=1)

    def in_order(sums_of, size):
        lines = sums_of.shape[1]
        by_part = sums_of.reshape(n_ctx, lines, -1, size)
        return jnp.transpose(by_part, (1, 2, 0, 3)).reshape(lines, -1)

    conv_sums = shard_of(
        jnp.concatenate(
            [
                in_order(sums[:, : taps + 1, :width], part),
                jnp.sum(sums[:, : taps + 1, width:], axis=0),
            ],
            axis=1,
        )
    )
    gate_sums = shard_of(in_order(sums[:, taps + 1 : taps + 2, :width], part))
    head_sums_all = sums[:, taps + 2, : 3 * LANES].reshape(n_ctx, 3, LANES)[:, :, :heads]
    head_grads = shard_of(in_order(head_sums_all, unit))
    norm_sums = jnp.sum(norm_sums, axis=0).reshape(1, -1)
    return (
        layer_out[None],
        hidden_grad[None],
        shard_of(norm_sums)[0],
        grad_in_weight,
        conv_sums[:taps],
        conv_sums[taps],
        head_grads[0],
        head_grads[1],
        head_grads[2],
        gate_sums[0],
        grad_out_weight,
    )


def solution(mesh):
    tokens, rows, flat = P("fsdp", "ctx", None), P("fsdp", None), P("fsdp")
    taps = P(None, "fsdp")
    return jax.shard_map(
        on_device,
        mesh=mesh,
        in_specs=(tokens, tokens, flat, flat, rows, taps, flat, flat, flat, flat, flat, rows),
        out_specs=(tokens, tokens, flat, rows, taps, flat, flat, flat, flat, flat, rows),
        check_vma=False,
    )
```

```python
import functools

import jax
import jax.numpy as jnp
from jax import lax
from jax.experimental import pallas as pl
from jax.experimental.pallas import tpu as pltpu
from jax.sharding import PartitionSpec as P

HEAD = 64
STATE = 128
BLOCK = 256
LANES = 128
POINTS = 4
EPS = 1e-05
F32 = jnp.float32
BF16 = jnp.bfloat16


def mm(a, b, contract=((1,), (0,))):
    return lax.dot_general(a, b, (contract, ((), ())), preferred_element_type=F32)


def mm_exact(a, b, contract=((1,), (0,))):
    return lax.dot_general(
        a, b, (contract, ((), ())), precision=lax.Precision.HIGHEST, preferred_element_type=F32
    )


def iota2(shape, axis):
    return lax.broadcasted_iota(jnp.int32, shape, axis)


def levels(lam, step):
    tri = (iota2((BLOCK, BLOCK), 0) >= iota2((BLOCK, BLOCK), 1)).astype(F32)
    level = mm_exact(tri, lam)
    across = level.T
    last = level[BLOCK - 1 : BLOCK, :]
    weight = jnp.exp(level - last) * step
    return level, across, jnp.exp(-last), weight, jnp.exp(-level)


def pair_of(array, first, low_half):
    return jnp.where(low_half, array[:, first : first + 1], array[:, first + 1 : first + 2])


def spread(level, across, head):
    return jnp.exp(-jnp.abs(level[:, head : head + 1] - across[head : head + 1, :]))


def silu_and_slope(v):
    s = jax.nn.sigmoid(v)
    return v * s, s * (1.0 + v * (1.0 - s))


def chosen_heads(me, heads, unit, n_ctx, turned=False):
    here, there = iota2((LANES, LANES), 1), iota2((LANES, LANES), 0)
    if turned:
        here, there = there, here
    head = (here // unit * n_ctx + me) * unit + here % unit
    return jnp.where(jnp.logical_and(there == head, here < heads), 1.0, 0.0).astype(BF16)


class Lines:
    def __init__(self, ref, first, rows, at, size):
        self.ref, self.first, self.at, self.shape = ref, first, at, (rows, size)

    def __getitem__(self, index):
        rows = slice(self.first, self.first + self.shape[0])
        lanes = slice(0, self.shape[1]) if index is Ellipsis else index[1]
        return self.ref[rows, self.at + lanes.start : self.at + lanes.stop]


def parameters(par_ref, width):
    lines = par_ref.shape[0] - 3
    head = par_ref[lines + 2 : lines + 3, 0 : 2 * LANES]
    return (
        Lines(par_ref, 0, lines, 0, width),
        Lines(par_ref, 0, lines, width, 2 * STATE),
        Lines(par_ref, lines, 1, 0, width),
        Lines(par_ref, lines + 1, 1, 0, width),
        head[:, :LANES],
        head[:, LANES:],
    )


def column_valid(length_ref, block):
    at = iota2((BLOCK, 1), 0) + block * BLOCK
    return (at < length_ref[0]).astype(F32)


MESH = pl.DeviceIdType.MESH
SMALL_ROWS = 32


def ring_place(index, half):
    a, b = index // 2, index % 2
    return a + b * (2 * half - 1 - 2 * a)


def ring_index(place, half):
    b = place // half
    return 2 * (place + b * (2 * half - 1 - 2 * place)) + b


class Ring:
    def __init__(self, n):
        self.n, self.half = n, n // 2
        self.me, self.shard = lax.axis_index("ctx"), lax.axis_index("fsdp")
        self.place = ring_place(self.shard, self.half)

    def at(self, steps):
        return ring_index(lax.rem(self.place + steps + 2 * self.n, self.n), self.half)

    def neighbour(self, way):
        return (self.me, self.at(1 if way == 0 else -1))


def remote(source, target, send, recv, device):
    return pltpu.make_async_remote_copy(
        src_ref=source,
        dst_ref=target,
        send_sem=send,
        recv_sem=recv,
        device_id=device,
        device_id_type=MESH,
    )


def greet(device):
    pl.semaphore_signal(pltpu.get_barrier_semaphore(), inc=1, device_id=device, device_id_type=MESH)


class Around:
    def __init__(self, me, shard):
        core, row = me % 2, me // 2
        self.me = me
        self.core_at = me + 1 - 2 * core
        self.row_at = me + 2 - 4 * row
        self.both_at = self.row_at + 1 - 2 * core
        self.core, self.row, self.both = (
            (at, shard) for at in (self.core_at, self.row_at, self.both_at)
        )
        self.all = (self.core, self.row, self.both)


class TokenSum:
    def __init__(self, around, parts, own_part, row_part, from_core, from_row, send, recv):
        self.around, self.parts, self.own_part, self.row_part = around, parts, own_part, row_part
        self.from_core, self.from_row, self.send, self.recv = from_core, from_row, send, recv

    def loads(self):
        at = self.around
        return (
            (self.parts.at[at.row_at], self.row_part),
            (self.parts.at[at.me], self.own_part),
        )

    def to_core(self, which):
        at = self.around
        return remote(
            self.parts.at[(at.core_at, at.both_at)[which]],
            self.from_core.at[which],
            self.send.at[which],
            self.recv.at[which],
            at.core,
        )

    def to_row(self):
        return remote(
            self.row_part, self.from_row, self.send.at[2], self.recv.at[2], self.around.row
        )

    def start(self):
        self.to_core(1).start()
        self.to_core(0).start()

    def pass_row(self):
        self.to_core(1).wait()
        total = self.row_part[...].astype(F32) + self.from_core[1].astype(F32)
        self.row_part[...] = total.astype(BF16)
        self.to_row().start()

    def total(self):
        self.to_core(0).wait()
        self.to_row().wait()
        return (
            self.own_part[...].astype(F32)
            + self.from_core[0].astype(F32)
            + self.from_row[...].astype(F32)
        )


class SmallSum:
    def __init__(self, n, around, whole, sums, send, recv, ctx_send, ctx_recv):
        self.n, self.around, self.whole, self.sums = n, around, whole, sums
        self.send, self.recv, self.ctx_send, self.ctx_recv = send, recv, ctx_send, ctx_recv
        self.shard = lax.axis_index("fsdp")

    def to_peer(self, offset):
        own = self.whole.at[self.shard]
        peer = (self.around.me, lax.rem(self.shard + offset, self.n))
        return remote(own, own, self.send.at[offset - 1], self.recv.at[offset - 1], peer)

    def to_ctx(self, i):
        own = self.sums.at[self.around.me]
        return remote(own, own, self.ctx_send.at[i], self.ctx_recv.at[i], self.around.all[i])

    def start(self):
        lax.fori_loop(1, self.n, lambda j, carry: (self.to_peer(j).start(), carry)[1], 0)

    def add(self):
        lax.fori_loop(1, self.n, lambda j, carry: (self.to_peer(j).wait(), carry)[1], 0)
        self.sums[self.around.me] = jnp.sum(self.whole[...], axis=0)
        for i in range(3):
            self.to_ctx(i).start()

    def finish(self):
        for i in range(3):
            self.to_ctx(i).wait()


def forward_kernel(
    heads,
    unit,
    n_ctx,
    n,
    direct,
    length_ref,
    px_ref,
    ps_ref,
    normed_ref,
    out_weight,
    w_z,
    upstream,
    par_ref,
    x_ref,
    b_ref,
    c_ref,
    slope_x_ref,
    slope_s_ref,
    lam_ref,
    step_ref,
    chain_ref,
    kept_ref,
    gain_ref,
    gate_t,
    mixed_parts,
    d_z,
    d_ssd,
    state,
    before_x,
    before_s,
    v_o,
    v_z,
    v_up,
    all_y,
    all_z,
    all_dyn,
    v_yt,
    v_mixed,
    v_dz,
    v_dssd,
    stat_all,
    columns,
    load_sem,
    store_sem,
    ring_send,
    ring_recv,
    piece_recv,
    stat_send,
    stat_recv,
):
    block = pl.program_id(0)
    blocks = pl.num_programs(0)
    ring = Ring(n)
    me, shard = ring.me, ring.shard
    around = Around(me, shard)
    width = px_ref.shape[1]
    taps_x_ref, taps_s_ref, gate_gain_ref, skip_ref, bias_step, rate = parameters(par_ref, width)
    channels = width * n_ctx
    piece, size = v_o.shape[0] // n, v_o.shape[1] // 4
    points = heads // 2 * n_ctx
    loads = [
        pltpu.make_async_copy(source, target, load_sem.at[i])
        for i, (source, target) in enumerate(((w_z, v_z), (upstream, v_up)))
    ]
    shard_rows = lambda index: pl.ds(pl.multiple_of(index * piece, 16), piece)
    own_piece = out_weight.at[pl.ds(pl.multiple_of(me * piece, 16), piece)]
    piece_peer = (shard % n_ctx, shard // n_ctx * n_ctx + me)
    moves = shard % n_ctx != me

    def hop(way, sub, step):
        at = pl.multiple_of((2 * way + sub) * size, LANES)
        place = v_o.at[shard_rows(ring.at(step * (2 * way - 1))), pl.ds(at, size)]
        return remote(
            place,
            place,
            ring_send.at[way, sub],
            ring_recv.at[way, sub, step],
            (me, ring.at(1 - 2 * way)),
        )

    def streams(body):
        lax.fori_loop(0, 4, lambda e, carry: (body(e // 2, e % 2), carry)[1], 0)

    def ring_step(step):
        def body(way, sub):
            hop(way, sub, step).wait()

            @pl.when(step < n - 2)
            def _():
                hop(way, sub, step + 1).start()

        streams(body)

    def serve(point):
        at = block * (heads // 2) + point
        lax.fori_loop(
            at * (n - 1) // points,
            (at + 1) * (n - 1) // points,
            lambda step, carry: (ring_step(step), carry)[1],
            0,
        )

    @pl.when(block == 0)
    def _():
        for device in around.all:
            greet(device)
        greet(ring.neighbour(0))
        greet(ring.neighbour(1))
        keep = pltpu.make_async_copy(own_piece, v_o.at[shard_rows(shard)], load_sem.at[2])
        if direct:
            keep.start()
            pl.semaphore_wait(pltpu.get_barrier_semaphore(), 5)
            keep.wait()
        else:
            send = remote(
                own_piece, v_o.at[shard_rows(piece_peer[1])], load_sem.at[2], piece_recv, piece_peer
            )

            @pl.when(moves)
            def _():
                greet(piece_peer)
                pl.semaphore_wait(pltpu.get_barrier_semaphore(), 6)
                send.start()
                send.wait()

            @pl.when(jnp.logical_not(moves))
            def _():
                pl.semaphore_wait(pltpu.get_barrier_semaphore(), 5)
                keep.start()
                keep.wait()

        streams(lambda way, sub: hop(way, sub, 0).start())
        for copy in loads:
            copy.start()
        state[...] = jnp.zeros_like(state)
        before_x[...] = jnp.zeros_like(before_x)
        before_s[...] = jnp.zeros_like(before_s)

    valid = column_valid(length_ref, block)
    low_half = iota2((1, LANES), 1) < HEAD
    taps = taps_x_ref.shape[0] - 1

    def conv(current, before, weight):
        padded = jnp.concatenate([before, current], axis=0)
        total = weight[taps : taps + 1]
        for k in range(taps):
            first = 8 - (taps - 1) + k
            total = total + weight[k : k + 1] * padded[first : first + BLOCK]
        return silu_and_slope(total)

    both = jnp.concatenate([ps_ref[0], ps_ref[1]], axis=1).astype(F32)
    active, slope = conv(both, before_s[...], taps_s_ref[...])
    before_s[...] = both[BLOCK - 8 :]
    slope_s_ref[...] = slope.astype(BF16)
    rows_b, rows_c = active[:, :STATE].astype(BF16), active[:, STATE:].astype(BF16)
    b_ref[...] = rows_b
    c_ref[...] = rows_c
    raw = mm(ps_ref[2], chosen_heads(me, heads, unit, n_ctx)) + bias_step
    own = iota2((1, LANES), 1) < heads
    step = jnp.where(own, valid * jax.nn.softplus(raw), 0.0)
    lam = step * rate
    step_ref[...] = step
    lam_ref[...] = lam
    chain_ref[...] = jnp.where(own, valid * jax.nn.sigmoid(raw), 0.0)

    gram = mm(rows_c, rows_b, ((1,), (1,)))
    level, across, last, weight, fade = levels(lam, step)
    kept_ref[0] = state[...].astype(BF16)
    entering = mm(rows_c, state[...].astype(BF16))
    by_state = rows_b.T
    for first in range(0, heads, 2):
        lanes = slice(first * HEAD, (first + 2) * HEAD)
        current = px_ref[:, lanes].astype(F32)
        active, slope = conv(current, before_x[:, lanes], taps_x_ref[:, lanes])
        before_x[:, lanes] = current[BLOCK - 8 :]
        slope_x_ref[:, lanes] = slope.astype(BF16)
        x_low = active.astype(BF16)
        x_ref[:, lanes] = x_low
        x = x_low.astype(F32)
        scaled = x * pair_of(step, first, low_half)
        total = pair_of(fade, first, low_half) * entering[:, lanes] + skip_ref[:, lanes] * x
        for head, keep in ((first, low_half), (first + 1, jnp.logical_not(low_half))):
            mixing = (gram * spread(level, across, head)).astype(BF16)
            total += mm(mixing, jnp.where(keep, scaled, 0.0).astype(BF16))
        all_y[block, :, lanes] = total
        update = mm(by_state, (x * pair_of(weight, first, low_half)).astype(BF16))
        state[:, lanes] = state[:, lanes] * pair_of(last, first, low_half) + update
        if first + 2 < heads:
            serve(first // 2)

    @pl.when(block == 0)
    def _():
        loads[0].wait()

    all_z[block] = mm(normed_ref[...], v_z[...]).astype(BF16)
    serve(heads // 2 - 1)

    @pl.when(block == blocks - 1)
    def _():
        loads[1].wait()
        lane = iota2((1, LANES), 1)

        def sums_of(chunk, carry):
            d_yn = column_valid(length_ref, chunk) * mm(v_up[chunk], v_o[...], ((1,), (1,)))
            all_dyn[chunk] = d_yn
            gated = all_y[chunk] * jax.nn.silu(all_z[chunk].astype(F32))
            square = jnp.sum(gated * gated, axis=1, keepdims=True)
            along = jnp.sum(gate_gain_ref[...] * d_yn * gated, axis=1, keepdims=True)
            pair = jnp.where(lane == 0, square, 0.0) + jnp.where(lane == 1, along, 0.0)
            stat_all[me, chunk] = pair.T[0:8]
            return carry

        lax.fori_loop(0, blocks, sums_of, 0)
        own_stats = stat_all.at[me]
        copies = [
            remote(own_stats, own_stats, stat_send.at[i], stat_recv.at[i], device)
            for i, device in enumerate(around.all)
        ]
        for copy in copies:
            copy.start()
        gain_ref[...] = jnp.zeros_like(gain_ref)
        for copy in copies:
            copy.wait()
        total = jnp.sum(stat_all[...], axis=0)
        for i in range(n_ctx):
            columns[i] = total[i].T

        def stores(chunk):
            slot = chunk % 2
            rows = pl.ds(pl.multiple_of(chunk * BLOCK, BLOCK), BLOCK)
            return [
                pltpu.make_async_copy(source.at[slot], target, store_sem.at[slot, i])
                for i, (source, target) in enumerate(
                    (
                        (v_yt, gate_t.at[chunk]),
                        (v_mixed, mixed_parts.at[chunk]),
                        (v_dz, d_z.at[rows]),
                        (v_dssd, d_ssd.at[rows]),
                    )
                )
            ]

        def gate_part(chunk, carry):
            slot = chunk % 2

            @pl.when(chunk >= 2)
            def _():
                for copy in stores(chunk - 2):
                    copy.wait()

            sums = columns[chunk]
            scale = lax.rsqrt(sums[:, 0:1] / channels + EPS)
            slant = scale * scale * scale * sums[:, 1:2] / channels
            here = column_valid(length_ref, chunk)
            for first in range(0, heads, 2):
                lanes = slice(first * HEAD, (first + 2) * HEAD)
                gate, gate_slope = silu_and_slope(all_z[chunk, :, lanes].astype(F32))
                mixed = all_y[chunk, :, lanes]
                d_yn = all_dyn[chunk, :, lanes]
                gain = gate_gain_ref[:, lanes]
                gated = mixed * gate
                scaled = gated * scale
                all_z[chunk, :, lanes] = (here * (scaled * gain)).astype(BF16)
                gain_ref[0:1, lanes] += jnp.sum(d_yn * scaled, axis=0, keepdims=True)
                d_gated = scale * (gain * d_yn) - gated * slant
                v_dz[slot, :, lanes] = (d_gated * mixed * gate_slope).astype(BF16)
                v_dssd[slot, :, lanes] = (d_gated * gate).astype(BF16)
            normed_gate = all_z[chunk]
            v_yt[slot] = normed_gate.T
            v_mixed[slot] = mm(normed_gate, v_o[...]).astype(BF16)
            for copy in stores(chunk):
                copy.start()
            return carry

        lax.fori_loop(0, blocks, gate_part, 0)
        for chunk in (n_ctx - 2, n_ctx - 1):
            for copy in stores(chunk):
                copy.wait()


def scan_forward(
    n, direct, unit, n_ctx, length, px, ps, normed, out_weight, w_z, upstream, par
):
    tokens, width = px.shape
    heads = width // HEAD
    count = tokens // BLOCK
    model = out_weight.shape[1]
    assert count == n_ctx
    by_block = lambda i: (i, 0)
    at_block = lambda size: pl.BlockSpec((BLOCK, size), by_block)
    whole = lambda a: pl.BlockSpec(a.shape, lambda i: (0, 0))
    any_space = pl.BlockSpec(memory_space=pl.ANY)
    low = lambda *shape: jax.ShapeDtypeStruct(shape, BF16)
    full = lambda *shape: jax.ShapeDtypeStruct(shape, F32)
    v_low = lambda *shape: pltpu.VMEM(shape, BF16)
    v_full = lambda *shape: pltpu.VMEM(shape, F32)
    dma = pltpu.SemaphoreType.DMA
    return pl.pallas_call(
        functools.partial(forward_kernel, heads, unit, n_ctx, n, direct),
        grid=(count,),
        in_specs=[
            pl.BlockSpec(memory_space=pltpu.SMEM),
            at_block(width),
            pl.BlockSpec((n_ctx, BLOCK, LANES), lambda i: (0, i, 0)),
            at_block(model),
            any_space,
            any_space,
            any_space,
        ]
        + [whole(par)],
        out_specs=[
            at_block(width),
            at_block(STATE),
            at_block(STATE),
            at_block(width),
            at_block(2 * STATE),
            at_block(LANES),
            at_block(LANES),
            at_block(LANES),
            pl.BlockSpec((1, STATE, width), lambda i: (i, 0, 0)),
            pl.BlockSpec((8, width), lambda i: (0, 0)),
            any_space,
            any_space,
            any_space,
            any_space,
        ],
        out_shape=[
            low(tokens, width),
            low(tokens, STATE),
            low(tokens, STATE),
            low(tokens, width),
            low(tokens, 2 * STATE),
            full(tokens, LANES),
            full(tokens, LANES),
            full(tokens, LANES),
            low(count, STATE, width),
            full(8, width),
            low(count, width, BLOCK),
            low(count, BLOCK, model),
            low(tokens, width),
            low(tokens, width),
        ],
        scratch_shapes=[
            v_full(STATE, width),
            v_full(8, width),
            v_full(8, 2 * STATE),
            v_low(width, model),
            v_low(*w_z.shape),
            v_low(count, BLOCK, model),
            v_full(count, BLOCK, width),
            v_low(count, BLOCK, width),
            v_full(count, BLOCK, width),
            v_low(2, width, BLOCK),
            v_low(2, BLOCK, model),
            v_low(2, BLOCK, width),
            v_low(2, BLOCK, width),
            v_full(n_ctx, count, 8, BLOCK),
            v_full(count, BLOCK, 8),
            dma((3,)),
            dma((2, 4)),
            dma((2, 2)),
            dma((2, 2, n - 1)),
            dma,
            dma((3,)),
            dma((3,)),
        ],
        compiler_params=pltpu.CompilerParams(
            collective_id=2, has_side_effects=True, vmem_limit_bytes=58 * 1024 * 1024
        ),
        name="scan_forward",
    )(length, px, ps, normed, out_weight, w_z, upstream, par)


def head_sums(product, chooser):
    high = product.astype(BF16)
    rest = (product - high.astype(F32)).astype(BF16)
    return mm(high, chooser) + mm(rest, chooser)


def backward_kernel(
    heads,
    unit,
    n_ctx,
    n,
    px_ref,
    ps_ref,
    x_ref,
    b_ref,
    c_ref,
    slope_x_ref,
    slope_s_ref,
    lam_ref,
    step_ref,
    chain_ref,
    kept_ref,
    dssd_ref,
    gate_t,
    normed_t,
    upstream,
    d_z,
    mixed_parts,
    hidden,
    gain_grads_ref,
    par_ref,
    dx_ref,
    small_ref,
    d_s,
    shard_o,
    shard_z,
    layer_out,
    back,
    mixed_grads,
    for_step,
    for_level,
    left,
    right,
    sums,
    after_x,
    after_s,
    v_left,
    v_right,
    products,
    slots,
    stage,
    done_o,
    done_z,
    mine,
    from_core,
    from_row,
    shared_parts,
    shared_core,
    shared_row,
    v_hidden,
    load_sem,
    store_sem,
    ring_send,
    ring_recv,
    part_send,
    part_recv,
    shared_send,
    shared_recv,
):
    turn = pl.program_id(0)
    turns = heads // 2 // POINTS
    block = pl.num_programs(0) - 1 - turn
    width, model = x_ref.shape[1], v_hidden.shape[1]
    taps_x_ref, taps_s_ref, _, skip_ref, _, rate = parameters(par_ref, width)
    own = hidden.shape[0]
    ring = Ring(n)
    around = Around(ring.me, ring.shard)
    piece, size = slots.shape[4], slots.shape[5]
    sum_mixed = TokenSum(
        around, mixed_parts, mine.at[0], mine.at[1], from_core, from_row, part_send, part_recv
    )
    sum_shared = TokenSum(
        around,
        shared_parts,
        shared_parts.at[ring.me],
        shared_parts.at[around.row_at],
        shared_core,
        shared_row,
        shared_send,
        shared_recv,
    )
    loads = [
        pltpu.make_async_copy(source, target, load_sem.at[i])
        for i, (source, target) in enumerate(
            (
                *((gate_t.at[c], v_left.at[pl.ds(0, width), pl.ds(c * own, own)]) for c in range(n_ctx)),
                *((upstream.at[c], v_right.at[pl.ds(c * own, own), pl.ds(0, model)]) for c in range(n_ctx)),
                *((normed_t.at[c], v_left.at[pl.ds(width, model), pl.ds(c * own, own)]) for c in range(n_ctx)),
                (d_z, v_right.at[:, pl.ds(model, width)]),
                *sum_mixed.loads(),
                (hidden, v_hidden),
            )
        )
    ]
    ring_loads = 1 + 3 * n_ctx

    def partial_sum(kind, way, sub, index):
        first = (1 - kind) * index * piece + kind * (width + (2 * index + way) * piece)
        at = (1 - kind) * (2 * way + sub) * size + kind * (model + sub * size)
        return mm(
            v_left[pl.ds(pl.multiple_of(first, 16), piece), :],
            v_right[:, pl.ds(pl.multiple_of(at, LANES), size)],
        )

    def all_products():
        tile = max(2 * piece, BLOCK)
        shards = tile // (2 * piece)

        def out_rows(i, carry):
            rows = pl.ds(pl.multiple_of(i * BLOCK, BLOCK), BLOCK)
            left = v_left[rows, :]
            products[rows, 0:width] = mm(left, v_right[:, 0:width]).astype(BF16)
            products[rows, width:model] = mm(left, v_right[:, width:model]).astype(BF16)
            return carry

        def in_rows(i, carry):
            left = v_left[pl.ds(pl.multiple_of(width + i * tile, 16), tile), :]
            both = mm(left, v_right[:, model:]).astype(BF16)
            for j in range(shards):
                place = pl.ds(pl.multiple_of((i * shards + j) * piece, 16), piece)
                for way in (0, 1):
                    products[place, model + way * width : model + (way + 1) * width] = both[
                        (2 * j + way) * piece : (2 * j + way + 1) * piece
                    ]
            return carry

        lax.fori_loop(0, width // BLOCK, out_rows, 0)
        lax.fori_loop(0, model // tile, in_rows, 0)

    def product(kind, way, sub, index):
        at = pl.multiple_of(kind * model + way * width + sub * size, LANES)
        return products[pl.ds(pl.multiple_of(index * piece, 16), piece), pl.ds(at, size)]

    def hop(kind, way, sub, step, source):
        return remote(
            source,
            slots.at[kind, step, way, sub],
            ring_send.at[kind, way, sub],
            ring_recv.at[kind, way, sub, step],
            (ring.me, ring.at(1 - 2 * way)),
        )

    def streams(body):
        def one(e, carry):
            body(e // 4, e // 2 % 2, e % 2)
            return carry

        lax.fori_loop(0, 8, one, 0)

    def start_ring(kind, way, sub):
        place = stage.at[kind, way, sub]
        place[...] = partial_sum(kind, way, sub, ring.at(2 * way - 1)).astype(BF16)
        hop(kind, way, sub, 0, place).start()

    def ring_step(step):
        def body(kind, way, sub):
            index = ring.at((step + 2) * (2 * way - 1))
            hop(kind, way, sub, step, stage.at[kind, way, sub]).wait()
            place = slots.at[kind, step, way, sub]
            total = place[...].astype(F32) + product(kind, way, sub, index).astype(F32)

            @pl.when(step < n - 2)
            def _():
                place[...] = total.astype(BF16)
                hop(kind, way, sub, step + 1, place).start()

            @pl.when(jnp.logical_and(step == n - 2, kind == 0))
            def _():
                at = pl.multiple_of((2 * way + sub) * size, LANES)
                done_o[:, pl.ds(at, size)] = total.astype(BF16)

            @pl.when(jnp.logical_and(step == n - 2, kind == 1))
            def _():
                done_z[way, pl.ds(pl.multiple_of(sub * size, 16), size), :] = total.T.astype(BF16)

        streams(body)

    def serve(point):
        at = turn * POINTS + point
        points = POINTS * n_ctx
        lax.fori_loop(
            at * (n - 1) // points,
            (at + 1) * (n - 1) // points,
            lambda step, carry: (ring_step(step), carry)[1],
            0,
        )

    @pl.when(turn == 0)
    def _():
        for device in around.all:
            greet(device)
        greet(ring.neighbour(0))
        greet(ring.neighbour(1))
        for copy in loads:
            copy.start()
        for c in range(3, n_ctx):
            shared_parts[c] = jnp.zeros(shared_parts.shape[1:], BF16)
        back[...] = jnp.zeros_like(back)
        small_ref[...] = jnp.zeros_like(small_ref)
        small_ref[taps_x_ref.shape[0] : taps_x_ref.shape[0] + 1, 0:width] = gain_grads_ref[0:1, :]
        after_x[...] = jnp.zeros_like(after_x)
        after_s[...] = jnp.zeros_like(after_s)
        pl.semaphore_wait(pltpu.get_barrier_semaphore(), 5)
        for copy in loads[:ring_loads]:
            copy.wait()
        streams(start_ring)
        sum_mixed.start()
        all_products()
        for copy in loads[ring_loads:]:
            copy.wait()

    @pl.when(turn == 1)
    def _():
        sum_mixed.pass_row()

    taps = taps_x_ref.shape[0] - 1

    rows_b, rows_c = b_ref[...], c_ref[...]
    step = step_ref[...]
    lam = lam_ref[...]
    gram = mm(rows_c, rows_b, ((1,), (1,)))
    gram_t = mm(rows_b, rows_c, ((1,), (1,)))
    level, across, last, weight, fade = levels(lam, step)
    out_decay = jnp.exp(level - level[BLOCK - 1 : BLOCK, :])
    step_across = step.T
    at_row, at_col = iota2((BLOCK, BLOCK), 0), iota2((BLOCK, BLOCK), 1)
    order = (at_row > at_col).astype(F32) - (at_row < at_col).astype(F32)
    low_half = iota2((1, LANES), 1) < HEAD
    lane = iota2((1, LANES), 1)
    by_state = rows_c.T
    kept = kept_ref[0]
    old_back = back[...].astype(BF16)
    entering = mm(rows_c, kept)
    leaving = mm(rows_b, old_back)
    at_last = jnp.sum(kept.astype(F32) * back[...], axis=0, keepdims=True)
    mixed_grads[...] = jnp.zeros_like(mixed_grads)
    left[...] = jnp.zeros_like(left)
    right[...] = jnp.zeros_like(right)
    sums[...] = jnp.zeros_like(sums)
    d_b = jnp.zeros((BLOCK, STATE), F32)
    d_c = jnp.zeros((BLOCK, STATE), F32)

    def conv_back(d_conv, after, current, weight):
        padded = jnp.concatenate([d_conv, after], axis=0)
        d_in = jnp.zeros_like(d_conv)
        grads = []
        for k in range(taps):
            moved = padded[taps - 1 - k : taps - 1 - k + BLOCK]
            d_in += weight[k : k + 1] * moved
            grads.append(jnp.sum(current * moved, axis=0, keepdims=True))
        grads.append(jnp.sum(d_conv, axis=0, keepdims=True))
        return d_in, jnp.concatenate(grads, axis=0)

    for first in range(0, heads, 2):
        lanes = slice(first * HEAD, (first + 2) * HEAD)
        x_low = x_ref[:, lanes]
        x = x_low.astype(F32)
        grad_low = dssd_ref[:, lanes]
        grad = grad_low.astype(F32)
        through = jnp.zeros((BLOCK, LANES), F32)
        for head, keep in ((first, low_half), (first + 1, jnp.logical_not(low_half))):
            decay = spread(level, across, head)
            grad_own = jnp.where(keep, grad, 0.0).astype(BF16)
            pairs = mm(grad_own, x_low, ((1,), (1,)))
            through += mm((gram_t * decay).astype(BF16), grad_own)
            scaled = decay * pairs * step_across[head : head + 1, :]
            mixed_grads[...] += scaled
            ordered = gram * scaled * order
            left[...] = jnp.where(
                lane == head, jnp.sum(ordered, axis=1, keepdims=True), left[...]
            )
            right[head : head + 1, :] = jnp.sum(ordered, axis=0, keepdims=True)
        weight_pair = pair_of(weight, first, low_half)
        step_pair = pair_of(step, first, low_half)
        fade_pair = pair_of(fade, first, low_half)
        out_pair = pair_of(out_decay, first, low_half)
        leave = leaving[:, lanes]
        d_x = step_pair * through + weight_pair * leave + skip_ref[:, lanes] * grad
        for_step[:, lanes] = x * (through + out_pair * leave)
        weighted = weight_pair * x
        faded = fade_pair * grad
        for_level[:, lanes] = weighted * leave - faded * entering[:, lanes]
        sums[0:1, lanes] = jnp.sum(weighted * leave, axis=0, keepdims=True)
        sums[2:3, lanes] = jnp.sum(x * grad, axis=0, keepdims=True)
        faded_low = faded.astype(BF16)
        d_b += mm(weighted.astype(BF16), old_back[:, lanes], ((1,), (1,)))
        d_c += mm(faded_low, kept[:, lanes], ((1,), (1,)))
        back[:, lanes] = back[:, lanes] * pair_of(last, first, low_half) + mm(by_state, faded_low)
        d_conv = d_x * slope_x_ref[:, lanes].astype(F32)
        d_in, grads = conv_back(
            d_conv, after_x[:, lanes], px_ref[:, lanes].astype(F32), taps_x_ref[:, lanes]
        )
        after_x[:, lanes] = d_conv[0:8]
        dx_ref[:, lanes] = d_in.astype(BF16)
        small_ref[0 : taps + 1, lanes] += grads
        if first // 2 % turns == turns - 1 and first // 2 // turns < POINTS - 1:
            serve(first // 2 // turns)

    all_pairs = mixed_grads[...]
    d_b = d_b + mm(all_pairs.T.astype(BF16), rows_c)
    d_c = d_c + mm(all_pairs.astype(BF16), rows_b)
    both = jnp.concatenate([ps_ref[0], ps_ref[1]], axis=1).astype(F32)
    d_conv = jnp.concatenate([d_b, d_c], axis=1) * slope_s_ref[...].astype(F32)
    d_in, grads = conv_back(
        d_conv, after_s[...], both, taps_s_ref[...]
    )
    after_s[...] = d_conv[0:8]
    here = pl.ds(pl.multiple_of(block * BLOCK, BLOCK), BLOCK)
    shared_parts[0, here, :] = d_in[:, :STATE].astype(BF16)
    shared_parts[1, here, :] = d_in[:, STATE:].astype(BF16)
    small_ref[0 : taps + 1, width:] += grads

    chooser = (iota2((width, LANES), 0) // HEAD == iota2((width, LANES), 1)).astype(BF16)
    d_step = head_sums(for_step[...], chooser)
    sums[1:2, :] = at_last
    total = head_sums(sums[...], chooser)
    d_level = head_sums(for_level[...], chooser) - left[...] + right[...].T
    final = -total[0:1, :] - last * total[1:2, :]
    d_level = d_level + jnp.where(iota2((BLOCK, 1), 0) == BLOCK - 1, final, 0.0)
    d_lam = mm_exact((at_row <= at_col).astype(F32), d_level)
    d_raw = (d_step + d_lam * rate) * chain_ref[...]
    head_row = taps + 2
    small_ref[head_row : head_row + 1, 0:LANES] += jnp.sum(d_raw, axis=0, keepdims=True)
    small_ref[head_row : head_row + 1, LANES : 2 * LANES] += jnp.sum(
        d_lam * lam, axis=0, keepdims=True
    )
    small_ref[head_row : head_row + 1, 2 * LANES : 3 * LANES] += total[2:3, :]
    chosen = chosen_heads(lax.axis_index("ctx"), heads, unit, n_ctx, True)
    shared_parts[2, here, :] = mm(d_raw.astype(BF16), chosen).astype(BF16)

    @pl.when(turn == pl.num_programs(0) - 1)
    def _():
        sum_shared.start()
        sum_shared.pass_row()


    serve(POINTS - 1)

    @pl.when(turn == pl.num_programs(0) - 1)
    def _():
        stores = [
            pltpu.make_async_copy(source, target, store_sem.at[i])
            for i, (source, target) in enumerate(
                (
                    (done_o, shard_o),
                    (done_z, shard_z),
                    (v_hidden, layer_out),
                    (shared_parts.at[ring.me], d_s),
                )
            )
        ]
        stores[0].start()
        stores[1].start()
        v_hidden[...] = (v_hidden[...].astype(F32) + sum_mixed.total()).astype(BF16)
        stores[2].start()
        shared_parts[ring.me] = sum_shared.total().astype(BF16)
        stores[3].start()
        for copy in stores:
            copy.wait()


def scan_backward(
    n, unit, n_ctx, px, ps, kept_parts, d_ssd, gate_t, normed_t, upstream, d_z, mixed_parts, hidden, gain_grads, par
):
    x, rows_b, rows_c, slope_x, slope_s, lam, step, chain, kept = kept_parts
    tokens, width = px.shape
    heads = width // HEAD
    count = tokens // BLOCK
    own, model = hidden.shape
    piece = width // n
    assert model == 2 * width and heads // 2 % POINTS == 0
    by_block = lambda i: (count - 1 - i, 0)
    at_block = lambda size: pl.BlockSpec((BLOCK, size), by_block)
    whole = lambda a: pl.BlockSpec(a.shape, lambda i: (0, 0))
    any_space = pl.BlockSpec(memory_space=pl.ANY)
    low = lambda *shape: jax.ShapeDtypeStruct(shape, BF16)
    v_low = lambda *shape: pltpu.VMEM(shape, BF16)
    v_full = lambda *shape: pltpu.VMEM(shape, F32)
    part = lambda a, b: pl.BlockSpec((1, a, b), lambda i: (count - 1 - i, 0, 0))
    small_shape = (8, width + 2 * STATE)
    dma = pltpu.SemaphoreType.DMA
    return pl.pallas_call(
        functools.partial(backward_kernel, heads, unit, n_ctx, n),
        grid=(count,),
        in_specs=[
            at_block(width),
            pl.BlockSpec((n_ctx, BLOCK, LANES), lambda i: (0, count - 1 - i, 0)),
            at_block(width),
            at_block(STATE),
            at_block(STATE),
            at_block(width),
            at_block(2 * STATE),
            at_block(LANES),
            at_block(LANES),
            at_block(LANES),
            part(STATE, width),
            at_block(width),
        ]
        + [any_space] * 6
        + [whole(a) for a in (gain_grads, par)],
        out_specs=[
            at_block(width),
            pl.BlockSpec(small_shape, lambda i: (0, 0)),
            any_space,
            any_space,
            any_space,
            any_space,
        ],
        out_shape=[
            low(tokens, width),
            jax.ShapeDtypeStruct(small_shape, F32),
            low(tokens, LANES),
            low(piece, model),
            low(2, width, piece),
            low(own, model),
        ],
        scratch_shapes=[
            v_full(STATE, width),
            v_full(BLOCK, BLOCK),
            v_full(BLOCK, width),
            v_full(BLOCK, width),
            v_full(BLOCK, LANES),
            v_full(LANES, BLOCK),
            v_full(8, width),
            v_full(8, width),
            v_full(8, 2 * STATE),
            v_low(width + model, tokens),
            v_low(tokens, model + width),
            v_low(width, 2 * model),
            v_low(2, n - 1, 2, 2, piece, width // 2),
            v_low(2, 2, 2, piece, width // 2),
            v_low(piece, model),
            v_low(2, width, piece),
            v_low(2, own, model),
            v_low(2, own, model),
            v_low(own, model),
            v_low(n_ctx, tokens, LANES),
            v_low(2, tokens, LANES),
            v_low(tokens, LANES),
            v_low(own, model),
            dma((4 + 3 * n_ctx,)),
            dma((4,)),
            dma((2, 2, 2)),
            dma((2, 2, 2, n - 1)),
            dma((3,)),
            dma((3,)),
            dma((3,)),
            dma((3,)),
        ],
        compiler_params=pltpu.CompilerParams(
            collective_id=3, has_side_effects=True, vmem_limit_bytes=59 * 1024 * 1024
        ),
        name="scan_backward",
    )(
        px, ps, x, rows_b, rows_c, slope_x, slope_s, lam, step, chain, kept, d_ssd, gate_t, normed_t, upstream, d_z, mixed_parts, hidden, gain_grads, par
    )


def gather_kernel(
    n,
    n_ctx,
    unit,
    taps,
    sizes,
    hidden,
    cotangent,
    in_weight_t,
    small,
    cotangent_all,
    w_x,
    w_s,
    w_z,
    par_out,
    gain_out,
    proj_x,
    proj_s,
    normed_out,
    normed_t,
    v_hidden,
    v_normed,
    v_x,
    v_s,
    own_z,
    v_small,
    raw_x,
    raw_s,
    raw_z,
    out_x,
    out_s,
    out_t,
    v_gain,
    v_par,
    conv_lines,
    gate_line,
    head_lines,
    load_sem,
    shared_sem,
    column_sem,
    local_sem,
    keep_sem,
    store_sem,
    ring_send,
    ring_recv,
    ctx_send,
    ctx_recv,
):
    ring = Ring(n)
    me, shard = ring.me, ring.shard
    width, model = v_x.shape[1], v_x.shape[0]
    inner = width * n_ctx
    r = model // n
    shared = in_weight_t.shape[0] - 2 * inner
    row = me // 2
    other_core = (me + 1 - 2 * (me % 2), shard)
    other_row = (me + 2 - 4 * row, shard)
    barrier = pltpu.get_barrier_semaphore()
    for device in (other_core, other_row, ring.neighbour(0), ring.neighbour(1)):
        pl.semaphore_signal(barrier, inc=1, device_id=device, device_id_type=MESH)

    part = unit * HEAD

    def load_columns(base, target, sems):
        return [
            pltpu.make_async_copy(
                in_weight_t.at[pl.ds(pl.multiple_of(base + (a * n_ctx + me) * part, 16), part)],
                target.at[pl.ds(a * part, part)],
                sems.at[a],
            )
            for a in range(width // part)
        ]

    loads = [
        load_columns(inner, raw_x, column_sem.at[0]),
        [],
        [pltpu.make_async_copy(small, v_small.at[shard], load_sem.at[1])],
        [pltpu.make_async_copy(hidden, v_hidden.at[me], load_sem.at[2])],
        load_columns(0, raw_z, column_sem.at[1]),
    ]
    raw_s[...] = jnp.zeros_like(raw_s)

    def load_shared(wait):
        for j in (0, 1):
            first = me * LANES + j * HEAD

            @pl.when(first < shared)
            def _():
                copy = pltpu.make_async_copy(
                    in_weight_t.at[pl.ds(pl.multiple_of(2 * inner + first, HEAD), HEAD)],
                    raw_s.at[pl.ds(j * HEAD, HEAD)],
                    shared_sem.at[j],
                )
                copy.wait() if wait else copy.start()

    load_shared(False)
    for copies in loads:
        for copy in copies:
            copy.start()

    def loaded(i):
        for copy in loads[i]:
            copy.wait()

    pl.semaphore_wait(barrier, 4)

    half = width // 2
    rows = r // 2
    both_rows = lambda index, way: pl.ds(pl.multiple_of((2 * index + way) * rows, 16), rows)
    x_part = lambda a, sub: lambda index, way: a.at[both_rows(index, way), pl.ds(sub * half, half)]
    s_part = lambda index, way: v_s.at[both_rows(index, way)]
    small_part = lambda index, way: v_small.at[index, pl.ds(way * SMALL_ROWS // 2, SMALL_ROWS // 2)]
    phases = (
        ((0, small_part), (1, s_part), (2, x_part(v_x, 0)), (3, x_part(v_x, 1))),
        ((4, x_part(w_z, 0)), (5, x_part(w_z, 1))),
    )

    def hop(stream, way, step):
        number, part = stream
        place = part(ring.at(-step if way == 0 else step), way)
        return remote(
            place, place, ring_send.at[number, way], ring_recv.at[number, way, step],
            ring.neighbour(way),
        )

    def arrives(stream, way, step):
        number, part = stream
        landed = part(ring.at(-step - 1 if way == 0 else step + 1), way)
        return remote(
            landed, landed, ring_send.at[number, way], ring_recv.at[number, way, step],
            ring.neighbour(way),
        )

    def start_stream(stream):
        for way in (0, 1):
            hop(stream, way, 0).start()

    def to_row(i, a, whole):
        return remote(a, whole.at[me], ctx_send.at[i, 0], ctx_recv.at[i, 0], other_row)

    def to_core(i, a, whole):
        return remote(a, whole.at[me], ctx_send.at[i, 1], ctx_recv.at[i, 1], other_core)

    def pass_on(i, whole):
        beyond = whole.at[other_row[0]]
        return remote(beyond, beyond, ctx_send.at[i, 2], ctx_recv.at[i, 2], other_core)

    to_row(0, hidden, v_hidden).start()
    to_core(0, hidden, v_hidden).start()
    own_rows = pl.ds(pl.multiple_of(shard * r, 16), r)
    loaded(2)
    start_stream(phases[0][0])
    loaded(0)
    v_x[own_rows, :] = raw_x[...].T
    start_stream(phases[0][2])
    start_stream(phases[0][3])
    load_shared(True)
    v_s[own_rows, :] = raw_s[...].T
    start_stream(phases[0][1])
    keep_cotangent = pltpu.make_async_copy(cotangent, cotangent_all.at[me], local_sem)
    keep_cotangent.start()
    keep_shared = pltpu.make_async_copy(out_s, proj_s.at[me], shared_sem.at[2])
    loaded(3)
    loaded(4)
    own_z[...] = raw_z[...].T
    keep_z = pltpu.make_async_copy(own_z, w_z.at[own_rows], keep_sem)
    keep_z.start()
    keep_z.wait()

    def run_phase(number, work, after):
        def body(step, carry):
            for stream in phases[number]:
                for way in (0, 1):
                    arrives(stream, way, step).wait_recv()
                    hop(stream, way, step).wait_send()
                    hop(stream, way, step + 1).start()
            if work is not None:

                @pl.when(step < n_ctx)
                def _():
                    work(step)

                @pl.when(step == n_ctx - 1)
                def _():
                    to_row(2, out_s, proj_s).start()
                    to_core(2, out_s, proj_s).start()
                    keep_shared.start()

            return carry

        lax.fori_loop(0, n - 2, body, 0)
        after()
        for stream in phases[number]:
            for way in (0, 1):
                arrives(stream, way, n - 2).wait_recv()
                hop(stream, way, n - 2).wait_send()

    tokens = v_hidden.shape[1]

    def project_first(chunk):
        at = pl.ds(pl.multiple_of(chunk * tokens, tokens), tokens)
        resid = v_hidden[chunk].astype(F32)
        scale = lax.rsqrt(jnp.mean(resid * resid, axis=1, keepdims=True) + EPS)
        normed = (resid * scale * v_gain[...]).astype(BF16)
        v_normed[at, :] = normed
        out_x[at, :] = mm(normed, v_x[...]).astype(BF16)
        out_s[at, :] = mm(normed, v_s[...]).astype(BF16)
        out_t[chunk] = normed.T

    stores = [
        pltpu.make_async_copy(source, target, store_sem.at[i])
        for i, (source, target) in enumerate(
            (
                (v_x, w_x),
                (v_s, w_s),
                (v_par, par_out),
                (v_gain, gain_out),
                (out_x, proj_x),
                (v_normed, normed_out),
                (out_t, normed_t),
            )
        )
    ]

    def after_first():
        for stream in phases[1]:
            start_stream(stream)
        to_row(0, hidden, v_hidden).wait_recv()
        pass_on(0, v_hidden).start()
        to_row(1, cotangent, cotangent_all).start()
        to_core(1, cotangent, cotangent_all).start()
        to_row(0, hidden, v_hidden).wait_send()
        to_core(0, hidden, v_hidden).wait()
        pass_on(0, v_hidden).wait()

    def after_second():
        to_row(1, cotangent, cotangent_all).wait_recv()
        pass_on(1, cotangent_all).start()
        to_row(2, out_s, proj_s).wait_recv()
        pass_on(2, proj_s).start()
        for copy in stores[4:]:
            copy.start()

    run_phase(0, None, after_first)
    gain_size, conv_size, gate_size, held = sizes
    head_lines[...] = jnp.zeros_like(head_lines)
    for f in range(n):
        v_gain[:, f * r : (f + 1) * r] = v_small[f, 0:1, 0:r].astype(F32)
        conv_lines[0 : taps + 1, f * conv_size : (f + 1) * conv_size] = v_small[
            f, 1 : taps + 2, 0:conv_size
        ].astype(F32)
        gate_line[:, f * gate_size : (f + 1) * gate_size] = v_small[
            f, taps + 2 : taps + 3, 0:gate_size
        ].astype(F32)
        for k in range(3):
            head_lines[k : k + 1, f * held : (f + 1) * held] = v_small[
                f, taps + 3 : taps + 4, k * held : (k + 1) * held
            ].astype(F32)

    def own_part(line, a):
        at = (a * n_ctx + me) * part
        span = max(part, LANES)
        found = line[:, pl.ds(pl.multiple_of(at // LANES * LANES, LANES), span)]
        if part < LANES:
            found = pltpu.roll(found, lax.rem(LANES - at % LANES, LANES), 1)
        return found[:, 0:part]

    v_par[...] = jnp.zeros_like(v_par)
    for a in range(width // part):
        v_par[0 : taps + 1, a * part : (a + 1) * part] = own_part(conv_lines, a)[0 : taps + 1]
        v_par[taps + 1 : taps + 2, a * part : (a + 1) * part] = own_part(gate_line, a)
    v_par[0 : taps + 1, width:] = conv_lines[0 : taps + 1, inner:]
    lines = mm(head_lines[...].astype(BF16), chosen_heads(me, width // HEAD, unit, n_ctx))
    heads_row = taps + 3
    v_par[heads_row : heads_row + 1, 0:LANES] = lines[0:1]
    v_par[heads_row : heads_row + 1, LANES : 2 * LANES] = jnp.exp(lines[1:2])
    wide = (iota2((LANES, width), 1) // HEAD == iota2((LANES, width), 0)).astype(BF16)
    v_par[taps + 2 : taps + 3, 0:width] = mm(lines.astype(BF16), wide)[2:3]
    for copy in stores[0:4]:
        copy.start()
    run_phase(1, project_first, after_second)
    to_row(1, cotangent, cotangent_all).wait_send()
    to_core(1, cotangent, cotangent_all).wait()
    pass_on(1, cotangent_all).wait()
    keep_cotangent.wait()
    to_row(2, out_s, proj_s).wait_send()
    to_core(2, out_s, proj_s).wait()
    pass_on(2, proj_s).wait()
    keep_shared.wait()
    for copy in stores:
        copy.wait()


def gather_all(n, n_ctx, unit, taps, sizes, width, hidden, cotangent, in_weight_t, small):
    own, model = hidden.shape
    tokens = own * n_ctx
    rows = in_weight_t.shape[1]
    any_space = pl.BlockSpec(memory_space=pl.ANY)
    par_shape = (taps + 4, width + 2 * STATE)
    inner = width * n_ctx
    low = lambda *shape: jax.ShapeDtypeStruct(shape, BF16)
    v_low = lambda *shape: pltpu.VMEM(shape, BF16)
    dma = pltpu.SemaphoreType.DMA
    return pl.pallas_call(
        functools.partial(gather_kernel, n, n_ctx, unit, taps, sizes),
        in_specs=[any_space] * 4,
        out_specs=[any_space] * 10,
        out_shape=[
            low(n_ctx, own, model),
            low(model, width),
            low(model, LANES),
            low(model, width),
            jax.ShapeDtypeStruct(par_shape, F32),
            jax.ShapeDtypeStruct((1, model), F32),
            low(tokens, width),
            low(n_ctx, tokens, LANES),
            low(tokens, model),
            low(n_ctx, model, own),
        ],
        scratch_shapes=[
            v_low(n_ctx, own, model),
            v_low(tokens, model),
            v_low(model, width),
            v_low(model, LANES),
            v_low(rows, width),
            v_low(n, small.shape[0], small.shape[1]),
            v_low(width, rows),
            v_low(LANES, rows),
            v_low(width, rows),
            v_low(tokens, width),
            v_low(tokens, LANES),
            v_low(n_ctx, model, own),
            pltpu.VMEM((1, model), F32),
            pltpu.VMEM(par_shape, F32),
            pltpu.VMEM((8, inner + 2 * STATE), F32),
            pltpu.VMEM((1, inner), F32),
            pltpu.VMEM((8, LANES), F32),
            dma((3,)),
            dma((3,)),
            dma((2, width // (unit * HEAD))),
            dma,
            dma,
            dma((7,)),
            dma((6, 2)),
            dma((6, 2, n - 1)),
            dma((3, 3)),
            dma((3, 3)),
        ],
        compiler_params=pltpu.CompilerParams(
            collective_id=0, has_side_effects=True, vmem_limit_bytes=56 * 1024 * 1024
        ),
        name="gather_all",
    )(hidden, cotangent, in_weight_t, small)


def reduce_kernel(
    n,
    n_ctx,
    direct,
    normed_t,
    d_z,
    d_x,
    d_s,
    w_z,
    w_x,
    w_s,
    shard_o,
    shard_z,
    small,
    hidden,
    cotangent,
    gain,
    g_z,
    g_x,
    g_s,
    g_o,
    hidden_grad,
    small_out,
    norm_out,
    v_normed_t,
    v_d_z,
    v_d_x,
    v_d_s,
    v_z,
    v_x,
    v_s,
    parts,
    partials,
    slots,
    stage,
    done,
    moved,
    from_core,
    from_row,
    v_hidden,
    v_cotangent,
    v_gain,
    small_all,
    small_ctx,
    norm_all,
    norm_ctx,
    load_sem,
    store_sem,
    ring_send,
    ring_recv,
    ctx_send,
    ctx_recv,
    own_sem,
    piece_send,
    piece_recv,
    part_send,
    part_recv,
    small_send,
    small_recv,
    small_ctx_send,
    small_ctx_recv,
):
    ring = Ring(n)
    me, shard = ring.me, ring.shard
    around = Around(me, shard)
    core, row = me % 2, me // 2
    piece_peer = (shard % n_ctx, shard // n_ctx * n_ctx + me)
    moves = shard % n_ctx != me
    barrier = pltpu.get_barrier_semaphore()
    for device in around.all:
        greet(device)
    lax.fori_loop(1, n, lambda j, carry: (greet((me, lax.rem(shard + j, n))), carry)[1], 0)
    own = hidden.shape[0]
    sum_normed = TokenSum(
        around, parts, parts.at[me], parts.at[around.row_at], from_core, from_row, part_send, part_recv
    )
    sum_small, sum_norm = (
        SmallSum(
            n, around, whole, sums, small_send.at[i], small_recv.at[i], small_ctx_send.at[i], small_ctx_recv.at[i]
        )
        for i, (whole, sums) in enumerate(((small_all, small_ctx), (norm_all, norm_ctx)))
    )
    loads = [
        pltpu.make_async_copy(source, target, load_sem.at[i])
        for i, (source, target) in enumerate(
            (
                *((normed_t.at[c], v_normed_t.at[:, pl.ds(c * own, own)]) for c in range(n_ctx)),
                (d_s, v_d_s),
                (d_x, v_d_x),
                (small, small_all.at[shard]),
                (d_z, v_d_z),
                (w_z, v_z),
                (w_x, v_x),
                (w_s, v_s),
                (hidden, v_hidden),
                (cotangent, v_cotangent),
                (gain, v_gain),
            )
        )
    ]
    ring_loads = n_ctx + 2
    for copy in loads:
        copy.start()
    if direct:
        pl.semaphore_wait(barrier, n + 2)
    else:

        @pl.when(moves)
        def _():
            greet(piece_peer)
            pl.semaphore_wait(barrier, n + 3)

        @pl.when(jnp.logical_not(moves))
        def _():
            pl.semaphore_wait(barrier, n + 2)

    rows = v_normed_t.shape[0] // (2 * n)
    half, last = v_d_x.shape[1] // 2, v_d_s.shape[1]
    streams = (
        (0, v_d_s, 0, last, 2 * half),
        (1, v_d_x, 0, half, 0),
        (2, v_d_x, half, half, half),
    )

    def compute_partials(step):
        for way in (0, 1):
            index = ring.at(-step - 2 if way == 0 else step + 2)
            left = v_normed_t[pl.ds(pl.multiple_of((2 * index + way) * rows, 16), rows), :]
            partials[way, :, 2 * half :] = mm(left, v_d_s[...])
            partials[way, :, 0 : 2 * half] = mm(left, v_d_x[...])

    def slot(stream, way, step):
        return slots.at[step, way, :, pl.ds(stream[4], stream[3])]

    def hop(stream, way, step, source):
        return remote(
            source,
            slot(stream, way, step),
            ring_send.at[stream[0], way],
            ring_recv.at[stream[0], way, step],
            ring.neighbour(way),
        )

    def first_part(stream, way):
        return stage.at[way, :, pl.ds(stream[4], stream[3])]

    def arrived(stream, way, step):
        hop(stream, way, step, first_part(stream, way)).wait()
        partial = partials[way, :, stream[4] : stream[4] + stream[3]]
        return slot(stream, way, step)[...].astype(F32) + partial

    done_of = lambda stream: done.at[pl.ds(stream[4], stream[3])]
    of_x = lambda c, first: g_x.at[c, pl.ds(first, half)]
    shares = (
        (shard_o if direct else moved, lambda c: g_o.at[c]),
        (shard_z, lambda c: g_z.at[c]),
        (done_of(streams[1]), lambda c: of_x(c, 0)),
        (done_of(streams[2]), lambda c: of_x(c, half)),
        (done_of(streams[0]), lambda c: g_s.at[c]),
    )

    def share(i, kind):
        source, whole = shares[i]
        at = me
        if kind == 2:
            source, at = whole(around.row_at), around.row_at
        device = around.row if kind == 0 else around.core
        return remote(source, whole(at), ctx_send.at[i, kind], ctx_recv.at[i, kind], device)

    def keep(i):
        return pltpu.make_async_copy(shares[i][0], shares[i][1](me), own_sem.at[i])

    def start_share(i):
        share(i, 0).start()
        share(i, 1).start()
        keep(i).start()

    def pass_share(i):
        share(i, 0).wait_recv()
        share(i, 2).start()

    def close_share(i):
        share(i, 0).wait_send()
        share(i, 1).wait()
        share(i, 2).wait()
        keep(i).wait()

    def move_piece(wait):
        if direct:
            return
        keep_piece = pltpu.make_async_copy(shard_o, moved, piece_send)
        send_piece = remote(shard_o, moved, piece_send, piece_recv, piece_peer)

        @pl.when(moves)
        def _():
            send_piece.wait() if wait else send_piece.start()

        @pl.when(jnp.logical_not(moves))
        def _():
            keep_piece.wait() if wait else keep_piece.start()

    def normed_part(i, carry):
        to_row = row + (1 - i % 2) * (1 - 2 * row)
        to_core = core + (1 - i // 2) * (1 - 2 * core)
        at = 2 * to_row + to_core
        tokens = pl.ds(pl.multiple_of(at * own, own), own)
        parts[at] = (
            mm(v_d_z[tokens, :], v_z[...], ((1,), (1,)))
            + mm(v_d_x[tokens, :], v_x[...], ((1,), (1,)))
            + mm(v_d_s[tokens, :], v_s[...], ((1,), (1,)))
        ).astype(BF16)
        return carry

    store_grad = pltpu.make_async_copy(v_cotangent, hidden_grad, store_sem.at[0])
    store_small = pltpu.make_async_copy(small_ctx, small_out, store_sem.at[1])
    store_norm = pltpu.make_async_copy(norm_ctx, norm_out, store_sem.at[2])

    def finish_tokens():
        resid = v_hidden[...].astype(F32)
        scale = lax.rsqrt(jnp.mean(resid * resid, axis=1, keepdims=True) + EPS)
        d_normed = sum_normed.total()
        f = v_gain[...] * d_normed
        slope = scale**3 * jnp.mean(resid * f, axis=1, keepdims=True)
        grad = v_cotangent[...].astype(F32) + scale * f - resid * slope
        v_cotangent[...] = grad.astype(BF16)
        store_grad.start()
        by_model = jnp.sum(d_normed * resid * scale, axis=0, keepdims=True)
        size = norm_all.shape[2]
        for j in range(norm_all.shape[1]):
            norm_all[shard, j : j + 1, :] = by_model[:, j * size : (j + 1) * size]
        sum_norm.start()

    move_piece(False)
    for copy in loads[:ring_loads]:
        copy.wait()
    compute_partials(-1)
    for way in (0, 1):
        stage[way] = partials[way].astype(BF16)
        for stream in streams:
            hop(stream, way, 0, first_part(stream, way)).start()
    compute_partials(0)
    for copy in loads[ring_loads:]:
        copy.wait()
    sum_small.start()
    move_piece(True)
    start_share(0)
    start_share(1)

    def body(step, carry):
        for stream in streams:
            for way in (0, 1):
                total = arrived(stream, way, step)
                place = slot(stream, way, step)
                place[...] = total.astype(BF16)
                hop(stream, way, step + 1, place).start()
        compute_partials(step + 1)

        @pl.when(step < 2)
        def _():
            lax.fori_loop(2 * step, 2 * step + 2, normed_part, 0)

        @pl.when(step == 0)
        def _():
            sum_normed.start()

        @pl.when(step == 1)
        def _():
            sum_normed.pass_row()

        @pl.when(step == n - 3)
        def _():
            finish_tokens()

        return carry

    lax.fori_loop(0, n - 2, body, 0)
    sum_small.add()
    pass_share(0)
    pass_share(1)
    for number, shared in ((0, 4), (1, 2), (2, 3)):
        place = done_of(streams[number])
        for way in (0, 1):
            total = arrived(streams[number], way, n - 2)
            place[:, way * rows : (way + 1) * rows] = total.T.astype(BF16)
        start_share(shared)
    sum_norm.add()
    sum_small.finish()
    store_small.start()
    for i in (4, 2, 3):
        pass_share(i)
    sum_norm.finish()
    store_norm.start()
    for i in range(5):
        close_share(i)
    store_grad.wait()
    store_small.wait()
    store_norm.wait()


def reduce_all(
    n, n_ctx, direct, normed_t, d_z, d_x, d_s, w_z, w_x, w_s, shard_o, shard_z, small, hidden, cotangent, gain
):
    model, tokens = normed_t.shape[1], d_x.shape[0]
    width, shared_width = d_x.shape[1], d_s.shape[1]
    rows, piece, own = model // n, width // n, hidden.shape[0]
    columns = width + shared_width
    any_space = pl.BlockSpec(memory_space=pl.ANY)
    dma = pltpu.SemaphoreType.DMA
    low = lambda *shape: jax.ShapeDtypeStruct(shape, BF16)
    v_low = lambda *shape: pltpu.VMEM(shape, BF16)
    v_full = lambda *shape: pltpu.VMEM(shape, F32)
    norm_shape = (8, model // 8)
    return pl.pallas_call(
        functools.partial(reduce_kernel, n, n_ctx, direct),
        in_specs=[any_space] * 13,
        out_specs=[any_space] * 7,
        out_shape=[
            low(n_ctx, 2, width, rows // 2),
            low(n_ctx, width, rows),
            low(n_ctx, shared_width, rows),
            low(n_ctx, piece, model),
            low(own, model),
            jax.ShapeDtypeStruct((n_ctx,) + small.shape, F32),
            jax.ShapeDtypeStruct((n_ctx,) + norm_shape, F32),
        ],
        scratch_shapes=[
            v_low(model, tokens),
            v_low(tokens, width),
            v_low(tokens, width),
            v_low(tokens, shared_width),
            v_low(*w_z.shape),
            v_low(*w_x.shape),
            v_low(*w_s.shape),
            v_low(n_ctx, own, model),
            v_full(2, rows // 2, columns),
            v_low(n - 1, 2, rows // 2, columns),
            v_low(2, rows // 2, columns),
            v_low(columns, rows),
            v_low(piece, model),
            v_low(2, own, model),
            v_low(own, model),
            v_low(own, model),
            v_low(own, model),
            v_full(1, model),
            v_full(n, *small.shape),
            v_full(n_ctx, *small.shape),
            v_full(n, *norm_shape),
            v_full(n_ctx, *norm_shape),
            dma((10 + n_ctx,)),
            dma((3,)),
            dma((3, 2)),
            dma((3, 2, n - 1)),
            dma((5, 3)),
            dma((5, 3)),
            dma((5,)),
            dma,
            dma,
            dma((3,)),
            dma((3,)),
            dma((2, n - 1)),
            dma((2, n - 1)),
            dma((2, 3)),
            dma((2, 3)),
        ],
        compiler_params=pltpu.CompilerParams(
            collective_id=1, has_side_effects=True, vmem_limit_bytes=58 * 1024 * 1024
        ),
        name="reduce_all",
    )(
        normed_t, d_z, d_x, d_s, w_z, w_x, w_s, shard_o, shard_z, small, hidden, cotangent, gain
    )


def assemble_kernel(part, z_ref, x_ref, s_ref, o_ref, out_ref, rows_ref):
    place = pl.program_id(0)
    n_ctx, size, half = x_ref.shape[0], x_ref.shape[1], z_ref.shape[3]

    def interleave(write):
        for a in range(size // part):
            for c in range(n_ctx):
                write(
                    slice((a * n_ctx + c) * part, (a * n_ctx + c + 1) * part),
                    c,
                    slice(a * part, (a + 1) * part),
                )

    def write_z(target, c, source):
        for way in (0, 1):
            out_ref[target, way * half : (way + 1) * half] = z_ref[c, way, source, :].astype(F32)

    def write_x(target, c, source):
        out_ref[target, :] = x_ref[c, source, :].astype(F32)

    @pl.when(place < n_ctx)
    def _():
        interleave(write_z)

    @pl.when(jnp.logical_and(place >= n_ctx, place < 2 * n_ctx))
    def _():
        interleave(write_x)

    @pl.when(place == 2 * n_ctx)
    def _():
        for c in range(s_ref.shape[0]):
            out_ref[c * LANES : (c + 1) * LANES, :] = s_ref[c].astype(F32)

    @pl.when(place < 2 * n_ctx)
    def _():
        rows_ref[...] = o_ref[...].astype(F32)


def assemble(part, g_z, g_x, g_s, g_o, columns):
    n_ctx, width, rows = g_x.shape
    block = (n_ctx, width // n_ctx, rows)
    g_o = g_o.reshape(-1, g_o.shape[2])
    tile = max(g_o.shape[0] // (2 * n_ctx), 16)
    at_tile = lambda i: (jnp.minimum(i, g_o.shape[0] // tile - 1), 0)
    return pl.pallas_call(
        functools.partial(assemble_kernel, part),
        grid=(2 * n_ctx + 1,),
        in_specs=[
            pl.BlockSpec(
                (n_ctx, 2, width // n_ctx, rows // 2),
                lambda i: (0, 0, jnp.minimum(i, n_ctx - 1), 0),
            ),
            pl.BlockSpec(block, lambda i: (0, jnp.clip(i - n_ctx, 0, n_ctx - 1), 0)),
            pl.BlockSpec(g_s.shape, lambda i: (0, 0, 0)),
            pl.BlockSpec((tile, g_o.shape[1]), at_tile),
        ],
        out_specs=[
            pl.BlockSpec((width, rows), lambda i: (i, 0)),
            pl.BlockSpec((tile, g_o.shape[1]), at_tile),
        ],
        out_shape=[
            jax.ShapeDtypeStruct((columns, rows), F32),
            jax.ShapeDtypeStruct(g_o.shape, F32),
        ],
        compiler_params=pltpu.CompilerParams(vmem_limit_bytes=58 * 1024 * 1024),
        name="assemble",
    )(g_z, g_x, g_s, g_o)


def on_device(
    hidden,
    cotangent,
    seq_lens,
    norm_gain,
    in_weight,
    conv_weight,
    conv_bias,
    dt_bias,
    a_log,
    d_skip,
    gate_gain,
    out_weight,
):
    n_ctx, n_fsdp = lax.axis_size("ctx"), lax.axis_size("fsdp")
    me, shard = lax.axis_index("ctx"), lax.axis_index("fsdp")
    taps = conv_weight.shape[0]
    heads_all = dt_bias.shape[0] * n_fsdp
    inner = out_weight.shape[0] * n_fsdp
    heads, width = heads_all // n_ctx, inner // n_ctx
    model = hidden.shape[2]
    both = 2 * STATE
    held = dt_bias.shape[0]
    direct = held % n_ctx == 0
    unit = held // n_ctx if direct else 1
    part = unit * HEAD
    assert both + heads_all <= n_ctx * LANES and heads_all == HEAD

    per_head = jnp.concatenate([dt_bias, a_log, d_skip])
    lines = [norm_gain[None], conv_weight, conv_bias[None], gate_gain[None], per_head[None]]
    longest = -(-max(a.shape[1] for a in lines) // LANES) * LANES
    small = jnp.concatenate([jnp.pad(a, ((0, 0), (0, longest - a.shape[1]))) for a in lines])
    small = jnp.pad(small, ((0, SMALL_ROWS - small.shape[0]), (0, 0)))
    sizes = (norm_gain.shape[0], conv_bias.shape[0], gate_gain.shape[0], held)
    upstream, w_x, w_s, w_z, par, gain_norm, proj_x, proj_s, normed, normed_t = gather_all(
        n_fsdp, n_ctx, unit, taps, sizes, width, hidden[0], cotangent[0], in_weight.T, small
    )
    *kept_parts, gain_grads, gate_t, mixed_parts, d_z, d_ssd = scan_forward(
        n_fsdp, direct, unit, n_ctx, seq_lens, proj_x, proj_s, normed, out_weight, w_z, upstream, par
    )
    d_x, small_grads, d_s, shard_o, shard_z, layer_out = scan_backward(
        n_fsdp, unit, n_ctx, proj_x, proj_s, kept_parts, d_ssd, gate_t, normed_t, upstream, d_z, mixed_parts, hidden[0], gain_grads, par
    )
    g_z, g_x, g_s, g_o, hidden_grad, sums, norm_sums = reduce_all(
        n_fsdp, n_ctx, direct, normed_t, d_z, d_x, d_s, w_z, w_x, w_s, shard_o, shard_z, small_grads, hidden[0], cotangent[0], gain_norm
    )
    grad_in_weight, grad_out_weight = assemble(
        part, g_z, g_x, g_s, g_o, 2 * inner + both + heads_all
    )

    def shard_of(lines):
        size = lines.shape[1] // n_fsdp
        return lax.dynamic_slice_in_dim(lines, shard * size, size, axis=1)

    def in_order(sums_of, size):
        lines = sums_of.shape[1]
        by_part = sums_of.reshape(n_ctx, lines, -1, size)
        return jnp.transpose(by_part, (1, 2, 0, 3)).reshape(lines, -1)

    conv_sums = shard_of(
        jnp.concatenate(
            [
                in_order(sums[:, : taps + 1, :width], part),
                jnp.sum(sums[:, : taps + 1, width:], axis=0),
            ],
            axis=1,
        )
    )
    gate_sums = shard_of(in_order(sums[:, taps + 1 : taps + 2, :width], part))
    head_sums_all = sums[:, taps + 2, : 3 * LANES].reshape(n_ctx, 3, LANES)[:, :, :heads]
    head_grads = shard_of(in_order(head_sums_all, unit))
    norm_sums = jnp.sum(norm_sums, axis=0).reshape(1, -1)
    return (
        layer_out[None],
        hidden_grad[None],
        shard_of(norm_sums)[0],
        grad_in_weight.T,
        conv_sums[:taps],
        conv_sums[taps],
        head_grads[0],
        head_grads[1],
        head_grads[2],
        gate_sums[0],
        grad_out_weight,
    )


def solution(mesh):
    tokens, rows, flat = P("fsdp", "ctx", None), P("fsdp", None), P("fsdp")
    taps = P(None, "fsdp")
    return jax.shard_map(
        on_device,
        mesh=mesh,
        in_specs=(tokens, tokens, flat, flat, rows, taps, flat, flat, flat, flat, flat, rows),
        out_specs=(tokens, tokens, flat, rows, taps, flat, flat, flat, flat, flat, rows),
        check_vma=False,
    )
```

```python
import functools

import jax
import jax.numpy as jnp
from jax import lax
from jax.experimental import pallas as pl
from jax.experimental.pallas import tpu as pltpu
from jax.sharding import PartitionSpec as P

HEAD = 64
STATE = 128
BLOCK = 256
LANES = 128
POINTS = 4
EPS = 1e-05
F32 = jnp.float32
BF16 = jnp.bfloat16


def mm(a, b, contract=((1,), (0,))):
    return lax.dot_general(a, b, (contract, ((), ())), preferred_element_type=F32)


def mm_exact(a, b, contract=((1,), (0,))):
    return lax.dot_general(
        a, b, (contract, ((), ())), precision=lax.Precision.HIGHEST, preferred_element_type=F32
    )


def iota2(shape, axis):
    return lax.broadcasted_iota(jnp.int32, shape, axis)


def levels(lam, step):
    tri = (iota2((BLOCK, BLOCK), 0) >= iota2((BLOCK, BLOCK), 1)).astype(F32)
    level = mm_exact(tri, lam)
    across = level.T
    last = level[BLOCK - 1 : BLOCK, :]
    weight = jnp.exp(level - last) * step
    return level, across, jnp.exp(-last), weight, jnp.exp(-level)


def pair_of(array, first, low_half):
    return jnp.where(low_half, array[:, first : first + 1], array[:, first + 1 : first + 2])


def spread(level, across, head):
    return jnp.exp(-jnp.abs(level[:, head : head + 1] - across[head : head + 1, :]))


def silu_and_slope(v):
    s = jax.nn.sigmoid(v)
    return v * s, s * (1.0 + v * (1.0 - s))


def chosen_heads(me, heads, unit, n_ctx, turned=False):
    here, there = iota2((LANES, LANES), 1), iota2((LANES, LANES), 0)
    if turned:
        here, there = there, here
    head = (here // unit * n_ctx + me) * unit + here % unit
    return jnp.where(jnp.logical_and(there == head, here < heads), 1.0, 0.0).astype(BF16)


class Lines:
    def __init__(self, ref, first, rows, at, size):
        self.ref, self.first, self.at, self.shape = ref, first, at, (rows, size)

    def __getitem__(self, index):
        rows = slice(self.first, self.first + self.shape[0])
        lanes = slice(0, self.shape[1]) if index is Ellipsis else index[1]
        return self.ref[rows, self.at + lanes.start : self.at + lanes.stop]


def parameters(par_ref, width):
    lines = par_ref.shape[0] - 3
    head = par_ref[lines + 2 : lines + 3, 0 : 2 * LANES]
    return (
        Lines(par_ref, 0, lines, 0, width),
        Lines(par_ref, 0, lines, width, 2 * STATE),
        Lines(par_ref, lines, 1, 0, width),
        Lines(par_ref, lines + 1, 1, 0, width),
        head[:, :LANES],
        head[:, LANES:],
    )


def column_valid(length_ref, block):
    at = iota2((BLOCK, 1), 0) + block * BLOCK
    return (at < length_ref[0]).astype(F32)


MESH = pl.DeviceIdType.MESH
SMALL_ROWS = 32


def ring_place(index, half):
    a, b = index // 2, index % 2
    return a + b * (2 * half - 1 - 2 * a)


def ring_index(place, half):
    b = place // half
    return 2 * (place + b * (2 * half - 1 - 2 * place)) + b


class Ring:
    def __init__(self, n):
        self.n, self.half = n, n // 2
        self.me, self.shard = lax.axis_index("ctx"), lax.axis_index("fsdp")
        self.place = ring_place(self.shard, self.half)

    def at(self, steps):
        return ring_index(lax.rem(self.place + steps + 2 * self.n, self.n), self.half)

    def neighbour(self, way):
        return (self.me, self.at(1 if way == 0 else -1))


def remote(source, target, send, recv, device):
    return pltpu.make_async_remote_copy(
        src_ref=source,
        dst_ref=target,
        send_sem=send,
        recv_sem=recv,
        device_id=device,
        device_id_type=MESH,
    )


def greet(device):
    pl.semaphore_signal(pltpu.get_barrier_semaphore(), inc=1, device_id=device, device_id_type=MESH)


class Around:
    def __init__(self, me, shard):
        core, row = me % 2, me // 2
        self.me = me
        self.core_at = me + 1 - 2 * core
        self.row_at = me + 2 - 4 * row
        self.both_at = self.row_at + 1 - 2 * core
        self.core, self.row, self.both = (
            (at, shard) for at in (self.core_at, self.row_at, self.both_at)
        )
        self.all = (self.core, self.row, self.both)


class TokenSum:
    def __init__(self, around, parts, own_part, row_part, from_core, from_row, send, recv):
        self.around, self.parts, self.own_part, self.row_part = around, parts, own_part, row_part
        self.from_core, self.from_row, self.send, self.recv = from_core, from_row, send, recv

    def loads(self):
        at = self.around
        return (
            (self.parts.at[at.row_at], self.row_part),
            (self.parts.at[at.me], self.own_part),
        )

    def to_core(self, which):
        at = self.around
        return remote(
            self.parts.at[(at.core_at, at.both_at)[which]],
            self.from_core.at[which],
            self.send.at[which],
            self.recv.at[which],
            at.core,
        )

    def to_row(self):
        return remote(
            self.row_part, self.from_row, self.send.at[2], self.recv.at[2], self.around.row
        )

    def start(self):
        self.to_core(1).start()
        self.to_core(0).start()

    def pass_row(self):
        self.to_core(1).wait()
        total = self.row_part[...].astype(F32) + self.from_core[1].astype(F32)
        self.row_part[...] = total.astype(BF16)
        self.to_row().start()

    def total(self):
        self.to_core(0).wait()
        self.to_row().wait()
        return (
            self.own_part[...].astype(F32)
            + self.from_core[0].astype(F32)
            + self.from_row[...].astype(F32)
        )


class SmallSum:
    def __init__(self, n, around, whole, sums, send, recv, ctx_send, ctx_recv):
        self.n, self.around, self.whole, self.sums = n, around, whole, sums
        self.send, self.recv, self.ctx_send, self.ctx_recv = send, recv, ctx_send, ctx_recv
        self.shard = lax.axis_index("fsdp")

    def to_peer(self, offset):
        own = self.whole.at[self.shard]
        peer = (self.around.me, lax.rem(self.shard + offset, self.n))
        return remote(own, own, self.send.at[offset - 1], self.recv.at[offset - 1], peer)

    def to_ctx(self, i):
        own = self.sums.at[self.around.me]
        return remote(own, own, self.ctx_send.at[i], self.ctx_recv.at[i], self.around.all[i])

    def start(self):
        lax.fori_loop(1, self.n, lambda j, carry: (self.to_peer(j).start(), carry)[1], 0)

    def add(self):
        lax.fori_loop(1, self.n, lambda j, carry: (self.to_peer(j).wait(), carry)[1], 0)
        self.sums[self.around.me] = jnp.sum(self.whole[...], axis=0)
        for i in range(3):
            self.to_ctx(i).start()

    def finish(self):
        for i in range(3):
            self.to_ctx(i).wait()


def forward_kernel(
    heads,
    unit,
    n_ctx,
    n,
    direct,
    length_ref,
    px_ref,
    ps_ref,
    normed_ref,
    out_weight,
    w_z,
    upstream,
    par_ref,
    x_ref,
    b_ref,
    c_ref,
    slope_x_ref,
    slope_s_ref,
    lam_ref,
    step_ref,
    chain_ref,
    kept_ref,
    gain_ref,
    gate_t,
    mixed_parts,
    d_z,
    d_ssd,
    own_scale,
    state,
    before_x,
    before_s,
    v_o,
    v_z,
    v_up,
    all_y,
    all_z,
    all_dyn,
    all_g,
    v_yt,
    v_mixed,
    v_dz,
    v_dssd,
    v_scale,
    stat_all,
    columns,
    load_sem,
    store_sem,
    ring_send,
    ring_recv,
    piece_recv,
    stat_send,
    stat_recv,
):
    block = pl.program_id(0)
    blocks = pl.num_programs(0)
    ring = Ring(n)
    me, shard = ring.me, ring.shard
    around = Around(me, shard)
    width = px_ref.shape[1]
    taps_x_ref, taps_s_ref, gate_gain_ref, skip_ref, bias_step, rate = parameters(par_ref, width)
    channels = width * n_ctx
    piece, size = v_o.shape[0] // n, v_o.shape[1] // 4
    points = heads // 2 * n_ctx
    loads = [
        pltpu.make_async_copy(source, target, load_sem.at[i])
        for i, (source, target) in enumerate(((w_z, v_z), (upstream, v_up)))
    ]
    shard_rows = lambda index: pl.ds(pl.multiple_of(index * piece, 16), piece)
    own_piece = out_weight.at[pl.ds(pl.multiple_of(me * piece, 16), piece)]
    piece_peer = (shard % n_ctx, shard // n_ctx * n_ctx + me)
    moves = shard % n_ctx != me

    def hop(way, sub, step):
        at = pl.multiple_of((2 * way + sub) * size, LANES)
        place = v_o.at[shard_rows(ring.at(step * (2 * way - 1))), pl.ds(at, size)]
        return remote(
            place,
            place,
            ring_send.at[way, sub],
            ring_recv.at[way, sub, step],
            (me, ring.at(1 - 2 * way)),
        )

    def streams(body):
        lax.fori_loop(0, 4, lambda e, carry: (body(e // 2, e % 2), carry)[1], 0)

    def ring_step(step):
        def body(way, sub):
            hop(way, sub, step).wait()

            @pl.when(step < n - 2)
            def _():
                hop(way, sub, step + 1).start()

        streams(body)

    def serve(point):
        at = block * (heads // 2) + point
        lax.fori_loop(
            at * (n - 1) // points,
            (at + 1) * (n - 1) // points,
            lambda step, carry: (ring_step(step), carry)[1],
            0,
        )

    @pl.when(block == 0)
    def _():
        for device in around.all:
            greet(device)
        greet(ring.neighbour(0))
        greet(ring.neighbour(1))
        keep = pltpu.make_async_copy(own_piece, v_o.at[shard_rows(shard)], load_sem.at[2])
        if direct:
            keep.start()
            pl.semaphore_wait(pltpu.get_barrier_semaphore(), 5)
            keep.wait()
        else:
            send = remote(
                own_piece, v_o.at[shard_rows(piece_peer[1])], load_sem.at[2], piece_recv, piece_peer
            )

            @pl.when(moves)
            def _():
                greet(piece_peer)
                pl.semaphore_wait(pltpu.get_barrier_semaphore(), 6)
                send.start()
                send.wait()

            @pl.when(jnp.logical_not(moves))
            def _():
                pl.semaphore_wait(pltpu.get_barrier_semaphore(), 5)
                keep.start()
                keep.wait()

        streams(lambda way, sub: hop(way, sub, 0).start())
        for copy in loads:
            copy.start()
        state[...] = jnp.zeros_like(state)
        before_x[...] = jnp.zeros_like(before_x)
        before_s[...] = jnp.zeros_like(before_s)

    valid = column_valid(length_ref, block)
    low_half = iota2((1, LANES), 1) < HEAD
    taps = taps_x_ref.shape[0] - 1

    def conv(current, before, weight):
        padded = jnp.concatenate([before, current], axis=0)
        total = weight[taps : taps + 1]
        for k in range(taps):
            first = 8 - (taps - 1) + k
            total = total + weight[k : k + 1] * padded[first : first + BLOCK]
        return silu_and_slope(total)

    both = jnp.concatenate([ps_ref[0], ps_ref[1]], axis=1).astype(F32)
    active, slope = conv(both, before_s[...], taps_s_ref[...])
    before_s[...] = both[BLOCK - 8 :]
    slope_s_ref[...] = slope.astype(BF16)
    rows_b, rows_c = active[:, :STATE].astype(BF16), active[:, STATE:].astype(BF16)
    b_ref[...] = rows_b
    c_ref[...] = rows_c
    raw = mm(ps_ref[2], chosen_heads(me, heads, unit, n_ctx)) + bias_step
    own = iota2((1, LANES), 1) < heads
    step = jnp.where(own, valid * jax.nn.softplus(raw), 0.0)
    lam = step * rate
    step_ref[...] = step
    lam_ref[...] = lam
    chain_ref[...] = jnp.where(own, valid * jax.nn.sigmoid(raw), 0.0)

    gram = mm(rows_c, rows_b, ((1,), (1,)))
    level, across, last, weight, fade = levels(lam, step)
    kept_ref[0] = state[...].astype(BF16)
    entering = mm(rows_c, state[...].astype(BF16))
    by_state = rows_b.T
    for first in range(0, heads, 2):
        lanes = slice(first * HEAD, (first + 2) * HEAD)
        current = px_ref[:, lanes].astype(F32)
        active, slope = conv(current, before_x[:, lanes], taps_x_ref[:, lanes])
        before_x[:, lanes] = current[BLOCK - 8 :]
        slope_x_ref[:, lanes] = slope.astype(BF16)
        x_low = active.astype(BF16)
        x_ref[:, lanes] = x_low
        x = x_low.astype(F32)
        scaled = x * pair_of(step, first, low_half)
        total = pair_of(fade, first, low_half) * entering[:, lanes] + skip_ref[:, lanes] * x
        for head, keep in ((first, low_half), (first + 1, jnp.logical_not(low_half))):
            mixing = (gram * spread(level, across, head)).astype(BF16)
            total += mm(mixing, jnp.where(keep, scaled, 0.0).astype(BF16))
        all_y[block, :, lanes] = total
        update = mm(by_state, (x * pair_of(weight, first, low_half)).astype(BF16))
        state[:, lanes] = state[:, lanes] * pair_of(last, first, low_half) + update
        if first + 2 < heads:
            serve(first // 2)

    @pl.when(block == 0)
    def _():
        loads[0].wait()

    all_z[block] = mm(normed_ref[...], v_z[...]).astype(BF16)
    serve(heads // 2 - 1)

    @pl.when(block == blocks - 1)
    def _():
        loads[1].wait()
        lane = iota2((1, LANES), 1)

        def sums_of(chunk, carry):
            d_yn = column_valid(length_ref, chunk) * mm(v_up[chunk], v_o[...], ((1,), (1,)))
            all_dyn[chunk] = d_yn
            gated = all_y[chunk] * jax.nn.silu(all_z[chunk].astype(F32))
            square = jnp.sum(gated * gated, axis=1, keepdims=True)
            weighted = gate_gain_ref[...] * gated
            all_g[chunk] = weighted.astype(BF16)
            along = jnp.sum(weighted * d_yn, axis=1, keepdims=True)
            pair = jnp.where(lane == 0, square, 0.0) + jnp.where(lane == 1, along, 0.0)
            stat_all[me, chunk] = pair.T[0:8]
            return carry

        lax.fori_loop(0, blocks, sums_of, 0)
        own_stats = stat_all.at[me]
        copies = [
            remote(own_stats, own_stats, stat_send.at[i], stat_recv.at[i], device)
            for i, device in enumerate(around.all)
        ]
        for copy in copies:
            copy.start()
        gain_ref[...] = jnp.zeros_like(gain_ref)

        def store_mixed(chunk):
            slot = chunk % 2
            return pltpu.make_async_copy(
                v_mixed.at[slot], mixed_parts.at[chunk], store_sem.at[slot, 3]
            )

        def mixed_of(chunk, carry):
            @pl.when(chunk >= 2)
            def _():
                store_mixed(chunk - 2).wait()

            v_mixed[chunk % 2] = mm(all_g[chunk], v_o[...]).astype(BF16)
            store_mixed(chunk).start()
            return carry

        lax.fori_loop(0, blocks, mixed_of, 0)
        for copy in copies:
            copy.wait()
        total = jnp.sum(stat_all[...], axis=0)
        for i in range(n_ctx):
            columns[i] = total[i].T
        scale = lax.rsqrt(columns[me][:, 0:1] / channels + EPS) * column_valid(length_ref, me)
        v_scale[...] = jnp.broadcast_to(scale, v_scale.shape)
        store_scale = pltpu.make_async_copy(v_scale, own_scale, load_sem.at[2])
        store_scale.start()

        def stores(chunk):
            slot = chunk % 2
            rows = pl.ds(pl.multiple_of(chunk * BLOCK, BLOCK), BLOCK)
            return [
                pltpu.make_async_copy(source.at[slot], target, store_sem.at[slot, i])
                for i, (source, target) in enumerate(
                    (
                        (v_yt, gate_t.at[chunk]),
                        (v_dz, d_z.at[rows]),
                        (v_dssd, d_ssd.at[rows]),
                    )
                )
            ]

        def gate_part(chunk, carry):
            slot = chunk % 2

            @pl.when(chunk >= 2)
            def _():
                for copy in stores(chunk - 2):
                    copy.wait()

            sums = columns[chunk]
            scale = lax.rsqrt(sums[:, 0:1] / channels + EPS)
            slant = scale * scale * scale * sums[:, 1:2] / channels
            here = column_valid(length_ref, chunk)
            for first in range(0, heads, 2):
                lanes = slice(first * HEAD, (first + 2) * HEAD)
                gate, gate_slope = silu_and_slope(all_z[chunk, :, lanes].astype(F32))
                mixed = all_y[chunk, :, lanes]
                d_yn = all_dyn[chunk, :, lanes]
                gain = gate_gain_ref[:, lanes]
                gated = mixed * gate
                scaled = gated * scale
                all_z[chunk, :, lanes] = (here * (scaled * gain)).astype(BF16)
                gain_ref[0:1, lanes] += jnp.sum(d_yn * scaled, axis=0, keepdims=True)
                d_gated = scale * (gain * d_yn) - gated * slant
                v_dz[slot, :, lanes] = (d_gated * mixed * gate_slope).astype(BF16)
                v_dssd[slot, :, lanes] = (d_gated * gate).astype(BF16)
            v_yt[slot] = all_z[chunk].T
            for copy in stores(chunk):
                copy.start()
            return carry

        lax.fori_loop(0, blocks, gate_part, 0)
        for chunk in (n_ctx - 2, n_ctx - 1):
            for copy in stores(chunk):
                copy.wait()
            store_mixed(chunk).wait()
        store_scale.wait()


def scan_forward(
    n, direct, unit, n_ctx, length, px, ps, normed, out_weight, w_z, upstream, par
):
    tokens, width = px.shape
    heads = width // HEAD
    count = tokens // BLOCK
    model = out_weight.shape[1]
    assert count == n_ctx
    by_block = lambda i: (i, 0)
    at_block = lambda size: pl.BlockSpec((BLOCK, size), by_block)
    whole = lambda a: pl.BlockSpec(a.shape, lambda i: (0, 0))
    any_space = pl.BlockSpec(memory_space=pl.ANY)
    low = lambda *shape: jax.ShapeDtypeStruct(shape, BF16)
    full = lambda *shape: jax.ShapeDtypeStruct(shape, F32)
    v_low = lambda *shape: pltpu.VMEM(shape, BF16)
    v_full = lambda *shape: pltpu.VMEM(shape, F32)
    dma = pltpu.SemaphoreType.DMA
    return pl.pallas_call(
        functools.partial(forward_kernel, heads, unit, n_ctx, n, direct),
        grid=(count,),
        in_specs=[
            pl.BlockSpec(memory_space=pltpu.SMEM),
            at_block(width),
            pl.BlockSpec((n_ctx, BLOCK, LANES), lambda i: (0, i, 0)),
            at_block(model),
            any_space,
            any_space,
            any_space,
        ]
        + [whole(par)],
        out_specs=[
            at_block(width),
            at_block(STATE),
            at_block(STATE),
            at_block(width),
            at_block(2 * STATE),
            at_block(LANES),
            at_block(LANES),
            at_block(LANES),
            pl.BlockSpec((1, STATE, width), lambda i: (i, 0, 0)),
            pl.BlockSpec((8, width), lambda i: (0, 0)),
            any_space,
            any_space,
            any_space,
            any_space,
            any_space,
        ],
        out_shape=[
            low(tokens, width),
            low(tokens, STATE),
            low(tokens, STATE),
            low(tokens, width),
            low(tokens, 2 * STATE),
            full(tokens, LANES),
            full(tokens, LANES),
            full(tokens, LANES),
            low(count, STATE, width),
            full(8, width),
            low(count, width, BLOCK),
            low(count, BLOCK, model),
            low(tokens, width),
            low(tokens, width),
            full(BLOCK, LANES),
        ],
        scratch_shapes=[
            v_full(STATE, width),
            v_full(8, width),
            v_full(8, 2 * STATE),
            v_low(width, model),
            v_low(*w_z.shape),
            v_low(count, BLOCK, model),
            v_full(count, BLOCK, width),
            v_low(count, BLOCK, width),
            v_full(count, BLOCK, width),
            v_low(count, BLOCK, width),
            v_low(2, width, BLOCK),
            v_low(2, BLOCK, model),
            v_low(2, BLOCK, width),
            v_low(2, BLOCK, width),
            v_full(BLOCK, LANES),
            v_full(n_ctx, count, 8, BLOCK),
            v_full(count, BLOCK, 8),
            dma((3,)),
            dma((2, 4)),
            dma((2, 2)),
            dma((2, 2, n - 1)),
            dma,
            dma((3,)),
            dma((3,)),
        ],
        compiler_params=pltpu.CompilerParams(
            collective_id=2, has_side_effects=True, vmem_limit_bytes=58 * 1024 * 1024
        ),
        name="scan_forward",
    )(length, px, ps, normed, out_weight, w_z, upstream, par)


def head_sums(product, chooser):
    high = product.astype(BF16)
    rest = (product - high.astype(F32)).astype(BF16)
    return mm(high, chooser) + mm(rest, chooser)


def backward_kernel(
    heads,
    unit,
    n_ctx,
    n,
    px_ref,
    ps_ref,
    x_ref,
    b_ref,
    c_ref,
    slope_x_ref,
    slope_s_ref,
    lam_ref,
    step_ref,
    chain_ref,
    kept_ref,
    dssd_ref,
    gate_t,
    normed_t,
    upstream,
    d_z,
    mixed_parts,
    own_scale,
    hidden,
    gain_grads_ref,
    par_ref,
    dx_ref,
    small_ref,
    d_s,
    shard_o,
    g_z,
    first_x,
    layer_out,
    back,
    mixed_grads,
    for_step,
    for_level,
    left,
    right,
    sums,
    after_x,
    after_s,
    v_left,
    v_right,
    products,
    slots,
    stage,
    done_o,
    done_z,
    mine,
    from_core,
    from_row,
    shared_parts,
    shared_core,
    shared_row,
    v_hidden,
    v_scale,
    load_sem,
    store_sem,
    ring_send,
    ring_recv,
    part_send,
    part_recv,
    shared_send,
    shared_recv,
    ctx_send,
    ctx_recv,
):
    turn = pl.program_id(0)
    turns = heads // 2 // POINTS
    block = pl.num_programs(0) - 1 - turn
    width, model = x_ref.shape[1], v_hidden.shape[1]
    taps_x_ref, taps_s_ref, _, skip_ref, _, rate = parameters(par_ref, width)
    own = hidden.shape[0]
    ring = Ring(n)
    around = Around(ring.me, ring.shard)
    piece, size = slots.shape[4], slots.shape[5]
    sum_mixed = TokenSum(
        around, mixed_parts, mine.at[0], mine.at[1], from_core, from_row, part_send, part_recv
    )
    sum_shared = TokenSum(
        around,
        shared_parts,
        shared_parts.at[ring.me],
        shared_parts.at[around.row_at],
        shared_core,
        shared_row,
        shared_send,
        shared_recv,
    )
    loads = [
        pltpu.make_async_copy(source, target, load_sem.at[i])
        for i, (source, target) in enumerate(
            (
                (d_z, v_right.at[:, pl.ds(model, width)]),
                *((normed_t.at[c], v_left.at[pl.ds(width, model), pl.ds(c * own, own)]) for c in range(n_ctx)),
                *((upstream.at[c], v_right.at[pl.ds(c * own, own), pl.ds(0, model)]) for c in range(n_ctx)),
                *((gate_t.at[c], v_left.at[pl.ds(0, width), pl.ds(c * own, own)]) for c in range(n_ctx)),
                *sum_mixed.loads(),
                (hidden, v_hidden),
                (own_scale, v_scale),
            )
        )
    ]
    loads_z, loads_o = loads[: 1 + n_ctx], loads[1 + n_ctx : 1 + 3 * n_ctx]
    loads_rest = loads[1 + 3 * n_ctx :]

    def in_left(way, index):
        first = width + (2 * index + way) * piece
        return v_left[pl.ds(pl.multiple_of(first, 16), piece), :]

    def out_left(index):
        return v_left[pl.ds(pl.multiple_of(index * piece, 16), piece), :]

    def all_products():
        tile = max(2 * piece, BLOCK)
        shards = tile // (2 * piece)

        def out_rows(i, carry):
            rows = pl.ds(pl.multiple_of(i * BLOCK, BLOCK), BLOCK)
            left = v_left[rows, :]
            products[rows, 0:width] = mm(left, v_right[:, 0:width]).astype(BF16)
            products[rows, width:model] = mm(left, v_right[:, width:model]).astype(BF16)
            return carry

        def in_rows(i, carry):
            left = v_left[pl.ds(pl.multiple_of(width + i * tile, 16), tile), :]
            both = mm(left, v_right[:, model:]).astype(BF16)
            for j in range(shards):
                place = pl.ds(pl.multiple_of((i * shards + j) * piece, 16), piece)
                for way in (0, 1):
                    products[place, model + way * width : model + (way + 1) * width] = both[
                        (2 * j + way) * piece : (2 * j + way + 1) * piece
                    ]
            return carry

        lax.fori_loop(0, model // tile, in_rows, 0)
        lax.fori_loop(0, width // BLOCK, out_rows, 0)

    def product(kind, way, sub, index):
        at = pl.multiple_of(kind * model + way * width + sub * size, LANES)
        return products[pl.ds(pl.multiple_of(index * piece, 16), piece), pl.ds(at, size)]

    def hop(kind, way, sub, step, source):
        return remote(
            source,
            slots.at[kind, step, way, sub],
            ring_send.at[kind, way, sub],
            ring_recv.at[kind, way, sub, step],
            (ring.me, ring.at(1 - 2 * way)),
        )

    def start_ring(kind):
        for way in (0, 1):
            index = ring.at(2 * way - 1)
            if kind == 0:
                first = mm(out_left(index), v_right[:, way * width : (way + 1) * width])
            else:
                first = mm(in_left(way, index), v_right[:, model:])
            for sub in (0, 1):
                stage[kind, way, sub] = first[:, sub * size : (sub + 1) * size].astype(BF16)
                hop(kind, way, sub, 0, stage.at[kind, way, sub]).start()

    def share(i):
        source, at = (done_z, ring.me) if i < 2 else (g_z.at[around.row_at], around.row_at)
        device = around.row if i == 0 else around.core
        return remote(source, g_z.at[at], ctx_send.at[i], ctx_recv.at[i], device)

    keep_z = pltpu.make_async_copy(done_z, g_z.at[ring.me], store_sem.at[1])

    def ring_step(turn_of_ring):
        kind = 1 - turn_of_ring // (n - 1)
        step = turn_of_ring % (n - 1)

        def body(way, sub):
            index = ring.at((step + 2) * (2 * way - 1))
            hop(kind, way, sub, step, stage.at[kind, way, sub]).wait()
            place = slots.at[kind, step, way, sub]
            total = place[...].astype(F32) + product(kind, way, sub, index).astype(F32)

            @pl.when(step < n - 2)
            def _():
                place[...] = total.astype(BF16)
                hop(kind, way, sub, step + 1, place).start()

            @pl.when(jnp.logical_and(step == n - 2, kind == 0))
            def _():
                at = pl.multiple_of((2 * way + sub) * size, LANES)
                done_o[:, pl.ds(at, size)] = total.astype(BF16)

            @pl.when(jnp.logical_and(step == n - 2, kind == 1))
            def _():
                done_z[way, pl.ds(pl.multiple_of(sub * size, 16), size), :] = total.T.astype(BF16)

        lax.fori_loop(0, 4, lambda e, carry: (body(e // 2, e % 2), carry)[1], 0)

        @pl.when(turn_of_ring == n - 2)
        def _():
            share(0).start()
            share(1).start()
            keep_z.start()

    def serve(point):
        at = turn * POINTS + point
        points = POINTS * n_ctx
        lax.fori_loop(
            at * (2 * n - 2) // points,
            (at + 1) * (2 * n - 2) // points,
            lambda step, carry: (ring_step(step), carry)[1],
            0,
        )

    @pl.when(turn == 0)
    def _():
        for device in around.all:
            greet(device)
        greet(ring.neighbour(0))
        greet(ring.neighbour(1))
        for copy in loads:
            copy.start()
        for c in range(3, n_ctx):
            shared_parts[c] = jnp.zeros(shared_parts.shape[1:], BF16)
        back[...] = jnp.zeros_like(back)
        small_ref[...] = jnp.zeros_like(small_ref)
        small_ref[taps_x_ref.shape[0] : taps_x_ref.shape[0] + 1, 0:width] = gain_grads_ref[0:1, :]
        after_x[...] = jnp.zeros_like(after_x)
        after_s[...] = jnp.zeros_like(after_s)
        pl.semaphore_wait(pltpu.get_barrier_semaphore(), 5)
        for copy in loads_z:
            copy.wait()
        start_ring(1)
        for copy in loads_o:
            copy.wait()
        start_ring(0)
        sum_mixed.start()
        all_products()
        for copy in loads_rest:
            copy.wait()

    @pl.when(turn == 1)
    def _():
        sum_mixed.pass_row()

    taps = taps_x_ref.shape[0] - 1

    rows_b, rows_c = b_ref[...], c_ref[...]
    step = step_ref[...]
    lam = lam_ref[...]
    gram = mm(rows_c, rows_b, ((1,), (1,)))
    gram_t = mm(rows_b, rows_c, ((1,), (1,)))
    level, across, last, weight, fade = levels(lam, step)
    out_decay = jnp.exp(level - level[BLOCK - 1 : BLOCK, :])
    step_across = step.T
    at_row, at_col = iota2((BLOCK, BLOCK), 0), iota2((BLOCK, BLOCK), 1)
    order = (at_row > at_col).astype(F32) - (at_row < at_col).astype(F32)
    low_half = iota2((1, LANES), 1) < HEAD
    lane = iota2((1, LANES), 1)
    by_state = rows_c.T
    kept = kept_ref[0]
    old_back = back[...].astype(BF16)
    entering = mm(rows_c, kept)
    leaving = mm(rows_b, old_back)
    at_last = jnp.sum(kept.astype(F32) * back[...], axis=0, keepdims=True)
    mixed_grads[...] = jnp.zeros_like(mixed_grads)
    left[...] = jnp.zeros_like(left)
    right[...] = jnp.zeros_like(right)
    sums[...] = jnp.zeros_like(sums)
    d_b = jnp.zeros((BLOCK, STATE), F32)
    d_c = jnp.zeros((BLOCK, STATE), F32)

    def conv_back(d_conv, after, current, weight):
        padded = jnp.concatenate([d_conv, after], axis=0)
        d_in = jnp.zeros_like(d_conv)
        grads = []
        for k in range(taps):
            moved = padded[taps - 1 - k : taps - 1 - k + BLOCK]
            d_in += weight[k : k + 1] * moved
            grads.append(jnp.sum(current * moved, axis=0, keepdims=True))
        grads.append(jnp.sum(d_conv, axis=0, keepdims=True))
        return d_in, jnp.concatenate(grads, axis=0)

    for first in range(0, heads, 2):
        lanes = slice(first * HEAD, (first + 2) * HEAD)
        x_low = x_ref[:, lanes]
        x = x_low.astype(F32)
        grad_low = dssd_ref[:, lanes]
        grad = grad_low.astype(F32)
        through = jnp.zeros((BLOCK, LANES), F32)
        for head, keep in ((first, low_half), (first + 1, jnp.logical_not(low_half))):
            decay = spread(level, across, head)
            grad_own = jnp.where(keep, grad, 0.0).astype(BF16)
            pairs = mm(grad_own, x_low, ((1,), (1,)))
            through += mm((gram_t * decay).astype(BF16), grad_own)
            scaled = decay * pairs * step_across[head : head + 1, :]
            mixed_grads[...] += scaled
            ordered = gram * scaled * order
            left[...] = jnp.where(
                lane == head, jnp.sum(ordered, axis=1, keepdims=True), left[...]
            )
            right[head : head + 1, :] = jnp.sum(ordered, axis=0, keepdims=True)
        weight_pair = pair_of(weight, first, low_half)
        step_pair = pair_of(step, first, low_half)
        fade_pair = pair_of(fade, first, low_half)
        out_pair = pair_of(out_decay, first, low_half)
        leave = leaving[:, lanes]
        d_x = step_pair * through + weight_pair * leave + skip_ref[:, lanes] * grad
        for_step[:, lanes] = x * (through + out_pair * leave)
        weighted = weight_pair * x
        faded = fade_pair * grad
        for_level[:, lanes] = weighted * leave - faded * entering[:, lanes]
        sums[0:1, lanes] = jnp.sum(weighted * leave, axis=0, keepdims=True)
        sums[2:3, lanes] = jnp.sum(x * grad, axis=0, keepdims=True)
        faded_low = faded.astype(BF16)
        d_b += mm(weighted.astype(BF16), old_back[:, lanes], ((1,), (1,)))
        d_c += mm(faded_low, kept[:, lanes], ((1,), (1,)))
        back[:, lanes] = back[:, lanes] * pair_of(last, first, low_half) + mm(by_state, faded_low)
        d_conv = d_x * slope_x_ref[:, lanes].astype(F32)
        d_in, grads = conv_back(
            d_conv, after_x[:, lanes], px_ref[:, lanes].astype(F32), taps_x_ref[:, lanes]
        )
        after_x[:, lanes] = d_conv[0:8]
        dx_ref[:, lanes] = d_in.astype(BF16)
        v_right[pl.ds(pl.multiple_of(block * BLOCK, BLOCK), BLOCK), lanes] = d_in.astype(BF16)
        small_ref[0 : taps + 1, lanes] += grads
        if first // 2 % turns == turns - 1 and first // 2 // turns < POINTS - 1:
            serve(first // 2 // turns)

    all_pairs = mixed_grads[...]
    d_b = d_b + mm(all_pairs.T.astype(BF16), rows_c)
    d_c = d_c + mm(all_pairs.astype(BF16), rows_b)
    both = jnp.concatenate([ps_ref[0], ps_ref[1]], axis=1).astype(F32)
    d_conv = jnp.concatenate([d_b, d_c], axis=1) * slope_s_ref[...].astype(F32)
    d_in, grads = conv_back(
        d_conv, after_s[...], both, taps_s_ref[...]
    )
    after_s[...] = d_conv[0:8]
    here = pl.ds(pl.multiple_of(block * BLOCK, BLOCK), BLOCK)
    shared_parts[0, here, :] = d_in[:, :STATE].astype(BF16)
    shared_parts[1, here, :] = d_in[:, STATE:].astype(BF16)
    small_ref[0 : taps + 1, width:] += grads

    chooser = (iota2((width, LANES), 0) // HEAD == iota2((width, LANES), 1)).astype(BF16)
    d_step = head_sums(for_step[...], chooser)
    sums[1:2, :] = at_last
    total = head_sums(sums[...], chooser)
    d_level = head_sums(for_level[...], chooser) - left[...] + right[...].T
    final = -total[0:1, :] - last * total[1:2, :]
    d_level = d_level + jnp.where(iota2((BLOCK, 1), 0) == BLOCK - 1, final, 0.0)
    d_lam = mm_exact((at_row <= at_col).astype(F32), d_level)
    d_raw = (d_step + d_lam * rate) * chain_ref[...]
    head_row = taps + 2
    small_ref[head_row : head_row + 1, 0:LANES] += jnp.sum(d_raw, axis=0, keepdims=True)
    small_ref[head_row : head_row + 1, LANES : 2 * LANES] += jnp.sum(
        d_lam * lam, axis=0, keepdims=True
    )
    small_ref[head_row : head_row + 1, 2 * LANES : 3 * LANES] += total[2:3, :]
    chosen = chosen_heads(lax.axis_index("ctx"), heads, unit, n_ctx, True)
    shared_parts[2, here, :] = mm(d_raw.astype(BF16), chosen).astype(BF16)

    @pl.when(turn == pl.num_programs(0) - 1)
    def _():
        sum_shared.start()
        for way in (0, 1):
            v_right[way * piece : (way + 1) * piece, width : 2 * width] = mm(
                in_left(way, ring.at(2 * way - 1)), v_right[:, 0:width]
            ).astype(BF16)
        sum_shared.pass_row()


    serve(POINTS - 1)

    @pl.when(turn == pl.num_programs(0) - 1)
    def _():
        stores = [
            pltpu.make_async_copy(source, target, store_sem.at[i])
            for i, source, target in (
                (0, done_o, shard_o),
                (2, v_right.at[pl.ds(0, 2 * piece), pl.ds(width, width)], first_x),
                (3, v_hidden, layer_out),
                (4, shared_parts.at[ring.me], d_s),
            )
        ]
        stores[0].start()
        stores[1].start()
        share(0).wait_recv()
        share(2).start()
        total = v_hidden[...].astype(F32) + v_scale[:, 0:1] * sum_mixed.total()
        v_hidden[...] = total.astype(BF16)
        stores[2].start()
        shared_parts[ring.me] = sum_shared.total().astype(BF16)
        stores[3].start()
        share(0).wait_send()
        share(1).wait()
        share(2).wait()
        keep_z.wait()
        for copy in stores:
            copy.wait()


def scan_backward(
    n, unit, n_ctx, px, ps, kept_parts, d_ssd, gate_t, normed_t, upstream, d_z, mixed_parts, own_scale, hidden, gain_grads, par
):
    x, rows_b, rows_c, slope_x, slope_s, lam, step, chain, kept = kept_parts
    tokens, width = px.shape
    heads = width // HEAD
    count = tokens // BLOCK
    own, model = hidden.shape
    piece = width // n
    assert model == 2 * width and heads // 2 % POINTS == 0
    by_block = lambda i: (count - 1 - i, 0)
    at_block = lambda size: pl.BlockSpec((BLOCK, size), by_block)
    whole = lambda a: pl.BlockSpec(a.shape, lambda i: (0, 0))
    any_space = pl.BlockSpec(memory_space=pl.ANY)
    low = lambda *shape: jax.ShapeDtypeStruct(shape, BF16)
    v_low = lambda *shape: pltpu.VMEM(shape, BF16)
    v_full = lambda *shape: pltpu.VMEM(shape, F32)
    part = lambda a, b: pl.BlockSpec((1, a, b), lambda i: (count - 1 - i, 0, 0))
    small_shape = (8, width + 2 * STATE)
    dma = pltpu.SemaphoreType.DMA
    return pl.pallas_call(
        functools.partial(backward_kernel, heads, unit, n_ctx, n),
        grid=(count,),
        in_specs=[
            at_block(width),
            pl.BlockSpec((n_ctx, BLOCK, LANES), lambda i: (0, count - 1 - i, 0)),
            at_block(width),
            at_block(STATE),
            at_block(STATE),
            at_block(width),
            at_block(2 * STATE),
            at_block(LANES),
            at_block(LANES),
            at_block(LANES),
            part(STATE, width),
            at_block(width),
        ]
        + [any_space] * 7
        + [whole(a) for a in (gain_grads, par)],
        out_specs=[
            at_block(width),
            pl.BlockSpec(small_shape, lambda i: (0, 0)),
            any_space,
            any_space,
            any_space,
            any_space,
            any_space,
        ],
        out_shape=[
            low(tokens, width),
            jax.ShapeDtypeStruct(small_shape, F32),
            low(tokens, LANES),
            low(piece, model),
            low(n_ctx, 2, width, piece),
            low(2 * piece, width),
            low(own, model),
        ],
        scratch_shapes=[
            v_full(STATE, width),
            v_full(BLOCK, BLOCK),
            v_full(BLOCK, width),
            v_full(BLOCK, width),
            v_full(BLOCK, LANES),
            v_full(LANES, BLOCK),
            v_full(8, width),
            v_full(8, width),
            v_full(8, 2 * STATE),
            v_low(width + model, tokens),
            v_low(tokens, model + width),
            v_low(width, 2 * model),
            v_low(2, n - 1, 2, 2, piece, width // 2),
            v_low(2, 2, 2, piece, width // 2),
            v_low(piece, model),
            v_low(2, width, piece),
            v_low(2, own, model),
            v_low(2, own, model),
            v_low(own, model),
            v_low(n_ctx, tokens, LANES),
            v_low(2, tokens, LANES),
            v_low(tokens, LANES),
            v_low(own, model),
            v_full(own, LANES),
            dma((5 + 3 * n_ctx,)),
            dma((5,)),
            dma((2, 2, 2)),
            dma((2, 2, 2, n - 1)),
            dma((3,)),
            dma((3,)),
            dma((3,)),
            dma((3,)),
            dma((3,)),
            dma((3,)),
        ],
        compiler_params=pltpu.CompilerParams(
            collective_id=3, has_side_effects=True, vmem_limit_bytes=59 * 1024 * 1024
        ),
        name="scan_backward",
    )(
        px, ps, x, rows_b, rows_c, slope_x, slope_s, lam, step, chain, kept, d_ssd, gate_t, normed_t, upstream, d_z, mixed_parts, own_scale, hidden, gain_grads, par
    )


def gather_kernel(
    n,
    n_ctx,
    unit,
    taps,
    sizes,
    hidden,
    cotangent,
    in_weight_t,
    small,
    cotangent_all,
    w_x,
    w_s,
    w_z,
    par_out,
    gain_out,
    proj_x,
    proj_s,
    normed_out,
    normed_t,
    v_hidden,
    v_normed,
    v_x,
    v_s,
    own_z,
    v_small,
    raw_x,
    raw_s,
    raw_z,
    out_x,
    out_s,
    out_t,
    v_gain,
    v_par,
    conv_lines,
    gate_line,
    head_lines,
    load_sem,
    shared_sem,
    column_sem,
    local_sem,
    keep_sem,
    store_sem,
    ring_send,
    ring_recv,
    ctx_send,
    ctx_recv,
):
    ring = Ring(n)
    me, shard = ring.me, ring.shard
    width, model = v_x.shape[1], v_x.shape[0]
    inner = width * n_ctx
    r = model // n
    shared = in_weight_t.shape[0] - 2 * inner
    row = me // 2
    other_core = (me + 1 - 2 * (me % 2), shard)
    other_row = (me + 2 - 4 * row, shard)
    barrier = pltpu.get_barrier_semaphore()
    for device in (other_core, other_row, ring.neighbour(0), ring.neighbour(1)):
        pl.semaphore_signal(barrier, inc=1, device_id=device, device_id_type=MESH)

    part = unit * HEAD

    def load_columns(base, target, sems):
        return [
            pltpu.make_async_copy(
                in_weight_t.at[pl.ds(pl.multiple_of(base + (a * n_ctx + me) * part, 16), part)],
                target.at[pl.ds(a * part, part)],
                sems.at[a],
            )
            for a in range(width // part)
        ]

    loads = [
        load_columns(inner, raw_x, column_sem.at[0]),
        [],
        [pltpu.make_async_copy(small, v_small.at[shard], load_sem.at[1])],
        [pltpu.make_async_copy(hidden, v_hidden.at[me], load_sem.at[2])],
        load_columns(0, raw_z, column_sem.at[1]),
    ]
    raw_s[...] = jnp.zeros_like(raw_s)

    def load_shared(wait):
        for j in (0, 1):
            first = me * LANES + j * HEAD

            @pl.when(first < shared)
            def _():
                copy = pltpu.make_async_copy(
                    in_weight_t.at[pl.ds(pl.multiple_of(2 * inner + first, HEAD), HEAD)],
                    raw_s.at[pl.ds(j * HEAD, HEAD)],
                    shared_sem.at[j],
                )
                copy.wait() if wait else copy.start()

    load_shared(False)
    for copies in loads:
        for copy in copies:
            copy.start()

    def loaded(i):
        for copy in loads[i]:
            copy.wait()

    pl.semaphore_wait(barrier, 4)

    half = width // 2
    rows = r // 2
    both_rows = lambda index, way: pl.ds(pl.multiple_of((2 * index + way) * rows, 16), rows)
    x_part = lambda a, sub: lambda index, way: a.at[both_rows(index, way), pl.ds(sub * half, half)]
    s_part = lambda index, way: v_s.at[both_rows(index, way)]
    small_part = lambda index, way: v_small.at[index, pl.ds(way * SMALL_ROWS // 2, SMALL_ROWS // 2)]
    phases = (
        ((0, small_part), (1, s_part), (2, x_part(v_x, 0)), (3, x_part(v_x, 1))),
        ((4, x_part(w_z, 0)), (5, x_part(w_z, 1))),
    )

    def hop(stream, way, step):
        number, part = stream
        place = part(ring.at(-step if way == 0 else step), way)
        return remote(
            place, place, ring_send.at[number, way], ring_recv.at[number, way, step],
            ring.neighbour(way),
        )

    def arrives(stream, way, step):
        number, part = stream
        landed = part(ring.at(-step - 1 if way == 0 else step + 1), way)
        return remote(
            landed, landed, ring_send.at[number, way], ring_recv.at[number, way, step],
            ring.neighbour(way),
        )

    def start_stream(stream):
        for way in (0, 1):
            hop(stream, way, 0).start()

    def to_row(i, a, whole):
        return remote(a, whole.at[me], ctx_send.at[i, 0], ctx_recv.at[i, 0], other_row)

    def to_core(i, a, whole):
        return remote(a, whole.at[me], ctx_send.at[i, 1], ctx_recv.at[i, 1], other_core)

    def pass_on(i, whole):
        beyond = whole.at[other_row[0]]
        return remote(beyond, beyond, ctx_send.at[i, 2], ctx_recv.at[i, 2], other_core)

    to_row(0, hidden, v_hidden).start()
    to_core(0, hidden, v_hidden).start()
    own_rows = pl.ds(pl.multiple_of(shard * r, 16), r)
    loaded(2)
    start_stream(phases[0][0])
    loaded(0)
    v_x[own_rows, :] = raw_x[...].T
    start_stream(phases[0][2])
    start_stream(phases[0][3])
    load_shared(True)
    v_s[own_rows, :] = raw_s[...].T
    start_stream(phases[0][1])
    keep_cotangent = pltpu.make_async_copy(cotangent, cotangent_all.at[me], local_sem)
    keep_cotangent.start()
    keep_shared = pltpu.make_async_copy(out_s, proj_s.at[me], shared_sem.at[2])
    loaded(3)
    loaded(4)
    own_z[...] = raw_z[...].T
    keep_z = pltpu.make_async_copy(own_z, w_z.at[own_rows], keep_sem)
    keep_z.start()
    keep_z.wait()

    def run_phase(number, work, after):
        def body(step, carry):
            for stream in phases[number]:
                for way in (0, 1):
                    arrives(stream, way, step).wait_recv()
                    hop(stream, way, step).wait_send()
                    hop(stream, way, step + 1).start()
            if work is not None:

                @pl.when(step < n_ctx)
                def _():
                    work(step)

                @pl.when(step == n_ctx - 1)
                def _():
                    to_row(2, out_s, proj_s).start()
                    to_core(2, out_s, proj_s).start()
                    keep_shared.start()

            return carry

        lax.fori_loop(0, n - 2, body, 0)
        after()
        for stream in phases[number]:
            for way in (0, 1):
                arrives(stream, way, n - 2).wait_recv()
                hop(stream, way, n - 2).wait_send()

    tokens = v_hidden.shape[1]

    def project_first(chunk):
        at = pl.ds(pl.multiple_of(chunk * tokens, tokens), tokens)
        resid = v_hidden[chunk].astype(F32)
        scale = lax.rsqrt(jnp.mean(resid * resid, axis=1, keepdims=True) + EPS)
        normed = (resid * scale * v_gain[...]).astype(BF16)
        v_normed[at, :] = normed
        out_x[at, :] = mm(normed, v_x[...]).astype(BF16)
        out_s[at, :] = mm(normed, v_s[...]).astype(BF16)
        out_t[chunk] = normed.T

    stores = [
        pltpu.make_async_copy(source, target, store_sem.at[i])
        for i, (source, target) in enumerate(
            (
                (v_x, w_x),
                (v_s, w_s),
                (v_par, par_out),
                (v_gain, gain_out),
                (out_x, proj_x),
                (v_normed, normed_out),
                (out_t, normed_t),
            )
        )
    ]

    def after_first():
        for stream in phases[1]:
            start_stream(stream)
        to_row(0, hidden, v_hidden).wait_recv()
        pass_on(0, v_hidden).start()
        to_row(1, cotangent, cotangent_all).start()
        to_core(1, cotangent, cotangent_all).start()
        to_row(0, hidden, v_hidden).wait_send()
        to_core(0, hidden, v_hidden).wait()
        pass_on(0, v_hidden).wait()

    def after_second():
        to_row(1, cotangent, cotangent_all).wait_recv()
        pass_on(1, cotangent_all).start()
        to_row(2, out_s, proj_s).wait_recv()
        pass_on(2, proj_s).start()
        for copy in stores[4:]:
            copy.start()

    run_phase(0, None, after_first)
    gain_size, conv_size, gate_size, held = sizes
    head_lines[...] = jnp.zeros_like(head_lines)
    for f in range(n):
        v_gain[:, f * r : (f + 1) * r] = v_small[f, 0:1, 0:r].astype(F32)
        conv_lines[0 : taps + 1, f * conv_size : (f + 1) * conv_size] = v_small[
            f, 1 : taps + 2, 0:conv_size
        ].astype(F32)
        gate_line[:, f * gate_size : (f + 1) * gate_size] = v_small[
            f, taps + 2 : taps + 3, 0:gate_size
        ].astype(F32)
        for k in range(3):
            head_lines[k : k + 1, f * held : (f + 1) * held] = v_small[
                f, taps + 3 : taps + 4, k * held : (k + 1) * held
            ].astype(F32)

    def own_part(line, a):
        at = (a * n_ctx + me) * part
        span = max(part, LANES)
        found = line[:, pl.ds(pl.multiple_of(at // LANES * LANES, LANES), span)]
        if part < LANES:
            found = pltpu.roll(found, lax.rem(LANES - at % LANES, LANES), 1)
        return found[:, 0:part]

    v_par[...] = jnp.zeros_like(v_par)
    for a in range(width // part):
        v_par[0 : taps + 1, a * part : (a + 1) * part] = own_part(conv_lines, a)[0 : taps + 1]
        v_par[taps + 1 : taps + 2, a * part : (a + 1) * part] = own_part(gate_line, a)
    v_par[0 : taps + 1, width:] = conv_lines[0 : taps + 1, inner:]
    lines = mm(head_lines[...].astype(BF16), chosen_heads(me, width // HEAD, unit, n_ctx))
    heads_row = taps + 3
    v_par[heads_row : heads_row + 1, 0:LANES] = lines[0:1]
    v_par[heads_row : heads_row + 1, LANES : 2 * LANES] = jnp.exp(lines[1:2])
    wide = (iota2((LANES, width), 1) // HEAD == iota2((LANES, width), 0)).astype(BF16)
    v_par[taps + 2 : taps + 3, 0:width] = mm(lines.astype(BF16), wide)[2:3]
    for copy in stores[0:4]:
        copy.start()
    run_phase(1, project_first, after_second)
    to_row(1, cotangent, cotangent_all).wait_send()
    to_core(1, cotangent, cotangent_all).wait()
    pass_on(1, cotangent_all).wait()
    keep_cotangent.wait()
    to_row(2, out_s, proj_s).wait_send()
    to_core(2, out_s, proj_s).wait()
    pass_on(2, proj_s).wait()
    keep_shared.wait()
    for copy in stores:
        copy.wait()


def gather_all(n, n_ctx, unit, taps, sizes, width, hidden, cotangent, in_weight_t, small):
    own, model = hidden.shape
    tokens = own * n_ctx
    rows = in_weight_t.shape[1]
    any_space = pl.BlockSpec(memory_space=pl.ANY)
    par_shape = (taps + 4, width + 2 * STATE)
    inner = width * n_ctx
    low = lambda *shape: jax.ShapeDtypeStruct(shape, BF16)
    v_low = lambda *shape: pltpu.VMEM(shape, BF16)
    dma = pltpu.SemaphoreType.DMA
    return pl.pallas_call(
        functools.partial(gather_kernel, n, n_ctx, unit, taps, sizes),
        in_specs=[any_space] * 4,
        out_specs=[any_space] * 10,
        out_shape=[
            low(n_ctx, own, model),
            low(model, width),
            low(model, LANES),
            low(model, width),
            jax.ShapeDtypeStruct(par_shape, F32),
            jax.ShapeDtypeStruct((1, model), F32),
            low(tokens, width),
            low(n_ctx, tokens, LANES),
            low(tokens, model),
            low(n_ctx, model, own),
        ],
        scratch_shapes=[
            v_low(n_ctx, own, model),
            v_low(tokens, model),
            v_low(model, width),
            v_low(model, LANES),
            v_low(rows, width),
            v_low(n, small.shape[0], small.shape[1]),
            v_low(width, rows),
            v_low(LANES, rows),
            v_low(width, rows),
            v_low(tokens, width),
            v_low(tokens, LANES),
            v_low(n_ctx, model, own),
            pltpu.VMEM((1, model), F32),
            pltpu.VMEM(par_shape, F32),
            pltpu.VMEM((8, inner + 2 * STATE), F32),
            pltpu.VMEM((1, inner), F32),
            pltpu.VMEM((8, LANES), F32),
            dma((3,)),
            dma((3,)),
            dma((2, width // (unit * HEAD))),
            dma,
            dma,
            dma((7,)),
            dma((6, 2)),
            dma((6, 2, n - 1)),
            dma((3, 3)),
            dma((3, 3)),
        ],
        compiler_params=pltpu.CompilerParams(
            collective_id=0, has_side_effects=True, vmem_limit_bytes=56 * 1024 * 1024
        ),
        name="gather_all",
    )(hidden, cotangent, in_weight_t, small)


def reduce_kernel(
    n,
    n_ctx,
    direct,
    normed_t,
    d_z,
    d_x,
    d_s,
    w_z,
    w_x,
    w_s,
    shard_o,
    first_x,
    small,
    hidden,
    cotangent,
    gain,
    g_x,
    g_s,
    g_o,
    hidden_grad,
    small_out,
    norm_out,
    v_normed_t,
    v_d_z,
    v_d_x,
    v_d_s,
    v_z,
    v_x,
    v_s,
    parts,
    partials,
    slots,
    stage,
    done,
    moved,
    from_core,
    from_row,
    v_hidden,
    v_cotangent,
    v_gain,
    small_all,
    small_ctx,
    norm_all,
    norm_ctx,
    load_sem,
    store_sem,
    ring_send,
    ring_recv,
    ctx_send,
    ctx_recv,
    own_sem,
    piece_send,
    piece_recv,
    part_send,
    part_recv,
    small_send,
    small_recv,
    small_ctx_send,
    small_ctx_recv,
):
    ring = Ring(n)
    me, shard = ring.me, ring.shard
    around = Around(me, shard)
    core, row = me % 2, me // 2
    piece_peer = (shard % n_ctx, shard // n_ctx * n_ctx + me)
    moves = shard % n_ctx != me
    barrier = pltpu.get_barrier_semaphore()
    for device in around.all:
        greet(device)
    lax.fori_loop(1, n, lambda j, carry: (greet((me, lax.rem(shard + j, n))), carry)[1], 0)
    own = hidden.shape[0]
    sum_normed = TokenSum(
        around, parts, parts.at[me], parts.at[around.row_at], from_core, from_row, part_send, part_recv
    )
    sum_small, sum_norm = (
        SmallSum(
            n, around, whole, sums, small_send.at[i], small_recv.at[i], small_ctx_send.at[i], small_ctx_recv.at[i]
        )
        for i, (whole, sums) in enumerate(((small_all, small_ctx), (norm_all, norm_ctx)))
    )
    loads = [
        pltpu.make_async_copy(source, target, load_sem.at[i])
        for i, (source, target) in enumerate(
            (
                *((normed_t.at[c], v_normed_t.at[:, pl.ds(c * own, own)]) for c in range(n_ctx)),
                (d_s, v_d_s),
                (d_x, v_d_x),
                (small, small_all.at[shard]),
                (d_z, v_d_z),
                (w_z, v_z),
                (w_x, v_x),
                (w_s, v_s),
                (hidden, v_hidden),
                (cotangent, v_cotangent),
                (gain, v_gain),
            )
        )
    ]
    ring_loads = n_ctx + 2
    for copy in loads:
        copy.start()
    if direct:
        pl.semaphore_wait(barrier, n + 2)
    else:

        @pl.when(moves)
        def _():
            greet(piece_peer)
            pl.semaphore_wait(barrier, n + 3)

        @pl.when(jnp.logical_not(moves))
        def _():
            pl.semaphore_wait(barrier, n + 2)

    rows = v_normed_t.shape[0] // (2 * n)
    half, last = v_d_x.shape[1] // 2, v_d_s.shape[1]
    streams = (
        (0, v_d_s, 0, last, 2 * half),
        (1, v_d_x, 0, half, 0),
        (2, v_d_x, half, half, half),
    )

    def compute_partials(step):
        for way in (0, 1):
            index = ring.at(-step - 2 if way == 0 else step + 2)
            left = v_normed_t[pl.ds(pl.multiple_of((2 * index + way) * rows, 16), rows), :]
            partials[way, :, 2 * half :] = mm(left, v_d_s[...])
            partials[way, :, 0 : 2 * half] = mm(left, v_d_x[...])

    def slot(stream, way, step):
        return slots.at[step, way, :, pl.ds(stream[4], stream[3])]

    def hop(stream, way, step, source):
        return remote(
            source,
            slot(stream, way, step),
            ring_send.at[stream[0], way],
            ring_recv.at[stream[0], way, step],
            ring.neighbour(way),
        )

    def first_part(stream, way):
        if stream[0] == 0:
            return stage.at[way]
        return first_x.at[pl.ds(way * rows, rows), pl.ds(stream[4], stream[3])]

    def arrived(stream, way, step):
        hop(stream, way, step, first_part(stream, way)).wait()
        partial = partials[way, :, stream[4] : stream[4] + stream[3]]
        return slot(stream, way, step)[...].astype(F32) + partial

    done_of = lambda stream: done.at[pl.ds(stream[4], stream[3])]
    of_x = lambda c, first: g_x.at[c, pl.ds(first, half)]
    shares = (
        (shard_o if direct else moved, lambda c: g_o.at[c]),
        (done_of(streams[1]), lambda c: of_x(c, 0)),
        (done_of(streams[2]), lambda c: of_x(c, half)),
        (done_of(streams[0]), lambda c: g_s.at[c]),
    )

    def share(i, kind):
        source, whole = shares[i]
        at = me
        if kind == 2:
            source, at = whole(around.row_at), around.row_at
        device = around.row if kind == 0 else around.core
        return remote(source, whole(at), ctx_send.at[i, kind], ctx_recv.at[i, kind], device)

    def keep(i):
        return pltpu.make_async_copy(shares[i][0], shares[i][1](me), own_sem.at[i])

    def start_share(i):
        share(i, 0).start()
        share(i, 1).start()
        keep(i).start()

    def pass_share(i):
        share(i, 0).wait_recv()
        share(i, 2).start()

    def close_share(i):
        share(i, 0).wait_send()
        share(i, 1).wait()
        share(i, 2).wait()
        keep(i).wait()

    def move_piece(wait):
        if direct:
            return
        keep_piece = pltpu.make_async_copy(shard_o, moved, piece_send)
        send_piece = remote(shard_o, moved, piece_send, piece_recv, piece_peer)

        @pl.when(moves)
        def _():
            send_piece.wait() if wait else send_piece.start()

        @pl.when(jnp.logical_not(moves))
        def _():
            keep_piece.wait() if wait else keep_piece.start()

    def normed_part(i, carry):
        to_row = row + (1 - i % 2) * (1 - 2 * row)
        to_core = core + (1 - i // 2) * (1 - 2 * core)
        at = 2 * to_row + to_core
        tokens = pl.ds(pl.multiple_of(at * own, own), own)
        parts[at] = (
            mm(v_d_z[tokens, :], v_z[...], ((1,), (1,)))
            + mm(v_d_x[tokens, :], v_x[...], ((1,), (1,)))
            + mm(v_d_s[tokens, :], v_s[...], ((1,), (1,)))
        ).astype(BF16)
        return carry

    store_grad = pltpu.make_async_copy(v_cotangent, hidden_grad, store_sem.at[0])
    store_small = pltpu.make_async_copy(small_ctx, small_out, store_sem.at[1])
    store_norm = pltpu.make_async_copy(norm_ctx, norm_out, store_sem.at[2])

    def finish_tokens():
        resid = v_hidden[...].astype(F32)
        scale = lax.rsqrt(jnp.mean(resid * resid, axis=1, keepdims=True) + EPS)
        d_normed = sum_normed.total()
        f = v_gain[...] * d_normed
        slope = scale**3 * jnp.mean(resid * f, axis=1, keepdims=True)
        grad = v_cotangent[...].astype(F32) + scale * f - resid * slope
        v_cotangent[...] = grad.astype(BF16)
        store_grad.start()
        by_model = jnp.sum(d_normed * resid * scale, axis=0, keepdims=True)
        size = norm_all.shape[2]
        for j in range(norm_all.shape[1]):
            norm_all[shard, j : j + 1, :] = by_model[:, j * size : (j + 1) * size]
        sum_norm.start()

    for stream in streams[1:]:
        for way in (0, 1):
            hop(stream, way, 0, first_part(stream, way)).start()
    move_piece(False)
    for copy in loads[:ring_loads]:
        copy.wait()
    for way in (0, 1):
        at = (2 * ring.at(2 * way - 1) + way) * rows
        left = v_normed_t[pl.ds(pl.multiple_of(at, 16), rows), :]
        stage[way] = mm(left, v_d_s[...]).astype(BF16)
        hop(streams[0], way, 0, stage.at[way]).start()
    compute_partials(0)
    for copy in loads[ring_loads:]:
        copy.wait()
    sum_small.start()
    move_piece(True)
    start_share(0)

    def body(step, carry):
        for stream in streams:
            for way in (0, 1):
                total = arrived(stream, way, step)
                place = slot(stream, way, step)
                place[...] = total.astype(BF16)
                hop(stream, way, step + 1, place).start()
        compute_partials(step + 1)

        @pl.when(step < 2)
        def _():
            lax.fori_loop(2 * step, 2 * step + 2, normed_part, 0)

        @pl.when(step == 0)
        def _():
            sum_normed.start()

        @pl.when(step == 1)
        def _():
            sum_normed.pass_row()

        @pl.when(step == n - 3)
        def _():
            finish_tokens()

        return carry

    lax.fori_loop(0, n - 2, body, 0)
    sum_small.add()
    pass_share(0)
    for number, shared in ((0, 3), (1, 1), (2, 2)):
        place = done_of(streams[number])
        for way in (0, 1):
            total = arrived(streams[number], way, n - 2)
            place[:, way * rows : (way + 1) * rows] = total.T.astype(BF16)
        start_share(shared)
    sum_norm.add()
    sum_small.finish()
    store_small.start()
    for i in (3, 1, 2):
        pass_share(i)
    sum_norm.finish()
    store_norm.start()
    for i in range(4):
        close_share(i)
    store_grad.wait()
    store_small.wait()
    store_norm.wait()


def reduce_all(
    n, n_ctx, direct, normed_t, d_z, d_x, d_s, w_z, w_x, w_s, shard_o, first_x, small, hidden, cotangent, gain
):
    model, tokens = normed_t.shape[1], d_x.shape[0]
    width, shared_width = d_x.shape[1], d_s.shape[1]
    rows, piece, own = model // n, width // n, hidden.shape[0]
    columns = width + shared_width
    any_space = pl.BlockSpec(memory_space=pl.ANY)
    dma = pltpu.SemaphoreType.DMA
    low = lambda *shape: jax.ShapeDtypeStruct(shape, BF16)
    v_low = lambda *shape: pltpu.VMEM(shape, BF16)
    v_full = lambda *shape: pltpu.VMEM(shape, F32)
    norm_shape = (8, model // 8)
    return pl.pallas_call(
        functools.partial(reduce_kernel, n, n_ctx, direct),
        in_specs=[any_space] * 13,
        out_specs=[any_space] * 6,
        out_shape=[
            low(n_ctx, width, rows),
            low(n_ctx, shared_width, rows),
            low(n_ctx, piece, model),
            low(own, model),
            jax.ShapeDtypeStruct((n_ctx,) + small.shape, F32),
            jax.ShapeDtypeStruct((n_ctx,) + norm_shape, F32),
        ],
        scratch_shapes=[
            v_low(model, tokens),
            v_low(tokens, width),
            v_low(tokens, width),
            v_low(tokens, shared_width),
            v_low(*w_z.shape),
            v_low(*w_x.shape),
            v_low(*w_s.shape),
            v_low(n_ctx, own, model),
            v_full(2, rows // 2, columns),
            v_low(n - 1, 2, rows // 2, columns),
            v_low(2, rows // 2, shared_width),
            v_low(columns, rows),
            v_low(piece, model),
            v_low(2, own, model),
            v_low(own, model),
            v_low(own, model),
            v_low(own, model),
            v_full(1, model),
            v_full(n, *small.shape),
            v_full(n_ctx, *small.shape),
            v_full(n, *norm_shape),
            v_full(n_ctx, *norm_shape),
            dma((10 + n_ctx,)),
            dma((3,)),
            dma((3, 2)),
            dma((3, 2, n - 1)),
            dma((4, 3)),
            dma((4, 3)),
            dma((4,)),
            dma,
            dma,
            dma((3,)),
            dma((3,)),
            dma((2, n - 1)),
            dma((2, n - 1)),
            dma((2, 3)),
            dma((2, 3)),
        ],
        compiler_params=pltpu.CompilerParams(
            collective_id=1, has_side_effects=True, vmem_limit_bytes=58 * 1024 * 1024
        ),
        name="reduce_all",
    )(
        normed_t, d_z, d_x, d_s, w_z, w_x, w_s, shard_o, first_x, small, hidden, cotangent, gain
    )


def assemble_kernel(part, z_ref, x_ref, s_ref, o_ref, out_ref, rows_ref):
    place = pl.program_id(0)
    n_ctx, size, half = x_ref.shape[0], x_ref.shape[1], z_ref.shape[3]

    def interleave(write):
        for a in range(size // part):
            for c in range(n_ctx):
                write(
                    slice((a * n_ctx + c) * part, (a * n_ctx + c + 1) * part),
                    c,
                    slice(a * part, (a + 1) * part),
                )

    def write_z(target, c, source):
        for way in (0, 1):
            out_ref[target, way * half : (way + 1) * half] = z_ref[c, way, source, :].astype(F32)

    def write_x(target, c, source):
        out_ref[target, :] = x_ref[c, source, :].astype(F32)

    @pl.when(place < n_ctx)
    def _():
        interleave(write_z)

    @pl.when(jnp.logical_and(place >= n_ctx, place < 2 * n_ctx))
    def _():
        interleave(write_x)

    @pl.when(place == 2 * n_ctx)
    def _():
        for c in range(s_ref.shape[0]):
            out_ref[c * LANES : (c + 1) * LANES, :] = s_ref[c].astype(F32)

    @pl.when(place < 2 * n_ctx)
    def _():
        rows_ref[...] = o_ref[...].astype(F32)


def assemble(part, g_z, g_x, g_s, g_o, columns):
    n_ctx, width, rows = g_x.shape
    block = (n_ctx, width // n_ctx, rows)
    g_o = g_o.reshape(-1, g_o.shape[2])
    tile = max(g_o.shape[0] // (2 * n_ctx), 16)
    at_tile = lambda i: (jnp.minimum(i, g_o.shape[0] // tile - 1), 0)
    return pl.pallas_call(
        functools.partial(assemble_kernel, part),
        grid=(2 * n_ctx + 1,),
        in_specs=[
            pl.BlockSpec(
                (n_ctx, 2, width // n_ctx, rows // 2),
                lambda i: (0, 0, jnp.minimum(i, n_ctx - 1), 0),
            ),
            pl.BlockSpec(block, lambda i: (0, jnp.clip(i - n_ctx, 0, n_ctx - 1), 0)),
            pl.BlockSpec(g_s.shape, lambda i: (0, 0, 0)),
            pl.BlockSpec((tile, g_o.shape[1]), at_tile),
        ],
        out_specs=[
            pl.BlockSpec((width, rows), lambda i: (i, 0)),
            pl.BlockSpec((tile, g_o.shape[1]), at_tile),
        ],
        out_shape=[
            jax.ShapeDtypeStruct((columns, rows), F32),
            jax.ShapeDtypeStruct(g_o.shape, F32),
        ],
        compiler_params=pltpu.CompilerParams(vmem_limit_bytes=58 * 1024 * 1024),
        name="assemble",
    )(g_z, g_x, g_s, g_o)


def on_device(
    hidden,
    cotangent,
    seq_lens,
    norm_gain,
    in_weight,
    conv_weight,
    conv_bias,
    dt_bias,
    a_log,
    d_skip,
    gate_gain,
    out_weight,
):
    n_ctx, n_fsdp = lax.axis_size("ctx"), lax.axis_size("fsdp")
    me, shard = lax.axis_index("ctx"), lax.axis_index("fsdp")
    taps = conv_weight.shape[0]
    heads_all = dt_bias.shape[0] * n_fsdp
    inner = out_weight.shape[0] * n_fsdp
    heads, width = heads_all // n_ctx, inner // n_ctx
    model = hidden.shape[2]
    both = 2 * STATE
    held = dt_bias.shape[0]
    direct = held % n_ctx == 0
    unit = held // n_ctx if direct else 1
    part = unit * HEAD
    assert both + heads_all <= n_ctx * LANES and heads_all == HEAD

    per_head = jnp.concatenate([dt_bias, a_log, d_skip])
    lines = [norm_gain[None], conv_weight, conv_bias[None], gate_gain[None], per_head[None]]
    longest = -(-max(a.shape[1] for a in lines) // LANES) * LANES
    small = jnp.concatenate([jnp.pad(a, ((0, 0), (0, longest - a.shape[1]))) for a in lines])
    small = jnp.pad(small, ((0, SMALL_ROWS - small.shape[0]), (0, 0)))
    sizes = (norm_gain.shape[0], conv_bias.shape[0], gate_gain.shape[0], held)
    upstream, w_x, w_s, w_z, par, gain_norm, proj_x, proj_s, normed, normed_t = gather_all(
        n_fsdp, n_ctx, unit, taps, sizes, width, hidden[0], cotangent[0], in_weight.T, small
    )
    *kept_parts, gain_grads, gate_t, mixed_parts, d_z, d_ssd, own_scale = scan_forward(
        n_fsdp, direct, unit, n_ctx, seq_lens, proj_x, proj_s, normed, out_weight, w_z, upstream, par
    )
    d_x, small_grads, d_s, shard_o, g_z, first_x, layer_out = scan_backward(
        n_fsdp, unit, n_ctx, proj_x, proj_s, kept_parts, d_ssd, gate_t, normed_t, upstream, d_z, mixed_parts, own_scale, hidden[0], gain_grads, par
    )
    g_x, g_s, g_o, hidden_grad, sums, norm_sums = reduce_all(
        n_fsdp, n_ctx, direct, normed_t, d_z, d_x, d_s, w_z, w_x, w_s, shard_o, first_x, small_grads, hidden[0], cotangent[0], gain_norm
    )
    grad_in_weight, grad_out_weight = assemble(
        part, g_z, g_x, g_s, g_o, 2 * inner + both + heads_all
    )

    def shard_of(lines):
        size = lines.shape[1] // n_fsdp
        return lax.dynamic_slice_in_dim(lines, shard * size, size, axis=1)

    def in_order(sums_of, size):
        lines = sums_of.shape[1]
        by_part = sums_of.reshape(n_ctx, lines, -1, size)
        return jnp.transpose(by_part, (1, 2, 0, 3)).reshape(lines, -1)

    conv_sums = shard_of(
        jnp.concatenate(
            [
                in_order(sums[:, : taps + 1, :width], part),
                jnp.sum(sums[:, : taps + 1, width:], axis=0),
            ],
            axis=1,
        )
    )
    gate_sums = shard_of(in_order(sums[:, taps + 1 : taps + 2, :width], part))
    head_sums_all = sums[:, taps + 2, : 3 * LANES].reshape(n_ctx, 3, LANES)[:, :, :heads]
    head_grads = shard_of(in_order(head_sums_all, unit))
    norm_sums = jnp.sum(norm_sums, axis=0).reshape(1, -1)
    return (
        layer_out[None],
        hidden_grad[None],
        shard_of(norm_sums)[0],
        grad_in_weight.T,
        conv_sums[:taps],
        conv_sums[taps],
        head_grads[0],
        head_grads[1],
        head_grads[2],
        gate_sums[0],
        grad_out_weight,
    )


def solution(mesh):
    tokens, rows, flat = P("fsdp", "ctx", None), P("fsdp", None), P("fsdp")
    taps = P(None, "fsdp")
    return jax.shard_map(
        on_device,
        mesh=mesh,
        in_specs=(tokens, tokens, flat, flat, rows, taps, flat, flat, flat, flat, flat, rows),
        out_specs=(tokens, tokens, flat, rows, taps, flat, flat, flat, flat, flat, rows),
        check_vma=False,
    )
```

```python
import functools

import jax
import jax.numpy as jnp
from jax import lax
from jax.experimental import pallas as pl
from jax.experimental.pallas import tpu as pltpu
from jax.sharding import PartitionSpec as P

HEAD = 64
STATE = 128
BLOCK = 256
LANES = 128
POINTS = 8
EPS = 1e-05
F32 = jnp.float32
BF16 = jnp.bfloat16


def mm(a, b, contract=((1,), (0,))):
    return lax.dot_general(a, b, (contract, ((), ())), preferred_element_type=F32)


def mm_exact(a, b, contract=((1,), (0,))):
    return lax.dot_general(
        a, b, (contract, ((), ())), precision=lax.Precision.HIGHEST, preferred_element_type=F32
    )


def iota2(shape, axis):
    return lax.broadcasted_iota(jnp.int32, shape, axis)


def levels(lam, step):
    tri = (iota2((BLOCK, BLOCK), 0) >= iota2((BLOCK, BLOCK), 1)).astype(F32)
    level = mm_exact(tri, lam)
    across = level.T
    last = level[BLOCK - 1 : BLOCK, :]
    weight = jnp.exp(level - last) * step
    return level, across, jnp.exp(-last), weight, jnp.exp(-level)


def pair_of(array, first, low_half):
    return jnp.where(low_half, array[:, first : first + 1], array[:, first + 1 : first + 2])


def spread(level, across, head):
    return jnp.exp(-jnp.abs(level[:, head : head + 1] - across[head : head + 1, :]))


def silu_and_slope(v):
    s = jax.nn.sigmoid(v)
    return v * s, s * (1.0 + v * (1.0 - s))


def chosen_heads(me, heads, unit, n_ctx, turned=False):
    here, there = iota2((LANES, LANES), 1), iota2((LANES, LANES), 0)
    if turned:
        here, there = there, here
    head = (here // unit * n_ctx + me) * unit + here % unit
    return jnp.where(jnp.logical_and(there == head, here < heads), 1.0, 0.0).astype(BF16)


class Lines:
    def __init__(self, ref, first, rows, at, size):
        self.ref, self.first, self.at, self.shape = ref, first, at, (rows, size)

    def __getitem__(self, index):
        rows = slice(self.first, self.first + self.shape[0])
        lanes = slice(0, self.shape[1]) if index is Ellipsis else index[1]
        return self.ref[rows, self.at + lanes.start : self.at + lanes.stop]


def parameters(par_ref, width):
    lines = par_ref.shape[0] - 3
    head = par_ref[lines + 2 : lines + 3, 0 : 2 * LANES]
    return (
        Lines(par_ref, 0, lines, 0, width),
        Lines(par_ref, 0, lines, width, 2 * STATE),
        Lines(par_ref, lines, 1, 0, width),
        Lines(par_ref, lines + 1, 1, 0, width),
        head[:, :LANES],
        head[:, LANES:],
    )


def column_valid(length_ref, block):
    at = iota2((BLOCK, 1), 0) + block * BLOCK
    return (at < length_ref[0]).astype(F32)


MESH = pl.DeviceIdType.MESH
SMALL_ROWS = 32


def ring_place(index, half):
    a, b = index // 2, index % 2
    return a + b * (2 * half - 1 - 2 * a)


def ring_index(place, half):
    b = place // half
    return 2 * (place + b * (2 * half - 1 - 2 * place)) + b


class Ring:
    def __init__(self, n):
        self.n, self.half = n, n // 2
        self.me, self.shard = lax.axis_index("ctx"), lax.axis_index("fsdp")
        self.place = ring_place(self.shard, self.half)

    def at(self, steps):
        return ring_index(lax.rem(self.place + steps + 2 * self.n, self.n), self.half)

    def neighbour(self, way):
        return (self.me, self.at(1 if way == 0 else -1))


def remote(source, target, send, recv, device):
    return pltpu.make_async_remote_copy(
        src_ref=source,
        dst_ref=target,
        send_sem=send,
        recv_sem=recv,
        device_id=device,
        device_id_type=MESH,
    )


def greet(device):
    pl.semaphore_signal(pltpu.get_barrier_semaphore(), inc=1, device_id=device, device_id_type=MESH)


class Around:
    def __init__(self, me, shard):
        core, row = me % 2, me // 2
        self.me = me
        self.core_at = me + 1 - 2 * core
        self.row_at = me + 2 - 4 * row
        self.both_at = self.row_at + 1 - 2 * core
        self.core, self.row, self.both = (
            (at, shard) for at in (self.core_at, self.row_at, self.both_at)
        )
        self.all = (self.core, self.row, self.both)


class TokenSum:
    def __init__(self, around, parts, own_part, row_part, from_core, from_row, send, recv):
        self.around, self.parts, self.own_part, self.row_part = around, parts, own_part, row_part
        self.from_core, self.from_row, self.send, self.recv = from_core, from_row, send, recv

    def loads(self):
        at = self.around
        return (
            (self.parts.at[at.row_at], self.row_part),
            (self.parts.at[at.me], self.own_part),
        )

    def to_core(self, which):
        at = self.around
        return remote(
            self.parts.at[(at.core_at, at.both_at)[which]],
            self.from_core.at[which],
            self.send.at[which],
            self.recv.at[which],
            at.core,
        )

    def to_row(self):
        return remote(
            self.row_part, self.from_row, self.send.at[2], self.recv.at[2], self.around.row
        )

    def start(self):
        self.to_core(1).start()
        self.to_core(0).start()

    def pass_row(self):
        self.to_core(1).wait()
        total = self.row_part[...].astype(F32) + self.from_core[1].astype(F32)
        self.row_part[...] = total.astype(BF16)
        self.to_row().start()

    def total(self):
        self.to_core(0).wait()
        self.to_row().wait()
        return (
            self.own_part[...].astype(F32)
            + self.from_core[0].astype(F32)
            + self.from_row[...].astype(F32)
        )


class SmallSum:
    def __init__(self, n, around, whole, sums, send, recv, ctx_send, ctx_recv):
        self.n, self.around, self.whole, self.sums = n, around, whole, sums
        self.send, self.recv, self.ctx_send, self.ctx_recv = send, recv, ctx_send, ctx_recv
        self.shard = lax.axis_index("fsdp")

    def to_peer(self, offset):
        own = self.whole.at[self.shard]
        peer = (self.around.me, lax.rem(self.shard + offset, self.n))
        return remote(own, own, self.send.at[offset - 1], self.recv.at[offset - 1], peer)

    def to_ctx(self, i):
        own = self.sums.at[self.around.me]
        return remote(own, own, self.ctx_send.at[i], self.ctx_recv.at[i], self.around.all[i])

    def start(self):
        lax.fori_loop(1, self.n, lambda j, carry: (self.to_peer(j).start(), carry)[1], 0)

    def add(self):
        lax.fori_loop(1, self.n, lambda j, carry: (self.to_peer(j).wait(), carry)[1], 0)
        self.sums[self.around.me] = jnp.sum(self.whole[...], axis=0)
        for i in range(3):
            self.to_ctx(i).start()

    def finish(self):
        for i in range(3):
            self.to_ctx(i).wait()


def forward_kernel(
    heads,
    unit,
    n_ctx,
    n,
    direct,
    length_ref,
    px_ref,
    ps_ref,
    normed_ref,
    out_weight,
    w_z,
    upstream,
    par_ref,
    x_ref,
    b_ref,
    c_ref,
    slope_x_ref,
    slope_s_ref,
    lam_ref,
    step_ref,
    chain_ref,
    kept_ref,
    gain_ref,
    gate_t,
    mixed_parts,
    d_z,
    d_ssd,
    own_scale,
    state,
    before_x,
    before_s,
    v_o,
    v_z,
    v_up,
    all_y,
    all_z,
    all_dyn,
    all_g,
    v_yt,
    v_mixed,
    v_dz,
    v_dssd,
    v_scale,
    stat_all,
    columns,
    load_sem,
    store_sem,
    ring_send,
    ring_recv,
    piece_recv,
    stat_send,
    stat_recv,
):
    block = pl.program_id(0)
    blocks = pl.num_programs(0)
    ring = Ring(n)
    me, shard = ring.me, ring.shard
    around = Around(me, shard)
    width = px_ref.shape[1]
    taps_x_ref, taps_s_ref, gate_gain_ref, skip_ref, bias_step, rate = parameters(par_ref, width)
    channels = width * n_ctx
    piece, size = v_o.shape[0] // n, v_o.shape[1] // 4
    points = heads // 2 * n_ctx
    loads = [
        pltpu.make_async_copy(source, target, load_sem.at[i])
        for i, (source, target) in enumerate(((w_z, v_z), (upstream, v_up)))
    ]
    shard_rows = lambda index: pl.ds(pl.multiple_of(index * piece, 16), piece)
    own_piece = out_weight.at[pl.ds(pl.multiple_of(me * piece, 16), piece)]
    piece_peer = (shard % n_ctx, shard // n_ctx * n_ctx + me)
    moves = shard % n_ctx != me

    def hop(way, sub, step):
        at = pl.multiple_of((2 * way + sub) * size, LANES)
        place = v_o.at[shard_rows(ring.at(step * (2 * way - 1))), pl.ds(at, size)]
        return remote(
            place,
            place,
            ring_send.at[way, sub],
            ring_recv.at[way, sub, step],
            (me, ring.at(1 - 2 * way)),
        )

    def streams(body):
        lax.fori_loop(0, 4, lambda e, carry: (body(e // 2, e % 2), carry)[1], 0)

    def ring_step(step):
        def body(way, sub):
            hop(way, sub, step).wait()

            @pl.when(step < n - 2)
            def _():
                hop(way, sub, step + 1).start()

        streams(body)

    def serve(point):
        at = block * (heads // 2) + point
        lax.fori_loop(
            at * (n - 1) // points,
            (at + 1) * (n - 1) // points,
            lambda step, carry: (ring_step(step), carry)[1],
            0,
        )

    @pl.when(block == 0)
    def _():
        for device in around.all:
            greet(device)
        greet(ring.neighbour(0))
        greet(ring.neighbour(1))
        keep = pltpu.make_async_copy(own_piece, v_o.at[shard_rows(shard)], load_sem.at[2])
        if direct:
            keep.start()
            pl.semaphore_wait(pltpu.get_barrier_semaphore(), 5)
            keep.wait()
        else:
            send = remote(
                own_piece, v_o.at[shard_rows(piece_peer[1])], load_sem.at[2], piece_recv, piece_peer
            )

            @pl.when(moves)
            def _():
                greet(piece_peer)
                pl.semaphore_wait(pltpu.get_barrier_semaphore(), 6)
                send.start()
                send.wait()

            @pl.when(jnp.logical_not(moves))
            def _():
                pl.semaphore_wait(pltpu.get_barrier_semaphore(), 5)
                keep.start()
                keep.wait()

        streams(lambda way, sub: hop(way, sub, 0).start())
        for copy in loads:
            copy.start()
        state[...] = jnp.zeros_like(state)
        before_x[...] = jnp.zeros_like(before_x)
        before_s[...] = jnp.zeros_like(before_s)

    valid = column_valid(length_ref, block)
    low_half = iota2((1, LANES), 1) < HEAD
    taps = taps_x_ref.shape[0] - 1

    def conv(current, before, weight):
        padded = jnp.concatenate([before, current], axis=0)
        total = weight[taps : taps + 1]
        for k in range(taps):
            first = 8 - (taps - 1) + k
            total = total + weight[k : k + 1] * padded[first : first + BLOCK]
        return silu_and_slope(total)

    both = jnp.concatenate([ps_ref[0], ps_ref[1]], axis=1).astype(F32)
    active, slope = conv(both, before_s[...], taps_s_ref[...])
    before_s[...] = both[BLOCK - 8 :]
    slope_s_ref[...] = slope.astype(BF16)
    rows_b, rows_c = active[:, :STATE].astype(BF16), active[:, STATE:].astype(BF16)
    b_ref[...] = rows_b
    c_ref[...] = rows_c
    raw = mm(ps_ref[2], chosen_heads(me, heads, unit, n_ctx)) + bias_step
    own = iota2((1, LANES), 1) < heads
    step = jnp.where(own, valid * jax.nn.softplus(raw), 0.0)
    lam = step * rate
    step_ref[...] = step
    lam_ref[...] = lam
    chain_ref[...] = jnp.where(own, valid * jax.nn.sigmoid(raw), 0.0)

    gram = mm(rows_c, rows_b, ((1,), (1,)))
    level, across, last, weight, fade = levels(lam, step)
    kept_ref[0] = state[...].astype(BF16)
    entering = mm(rows_c, state[...].astype(BF16))
    by_state = rows_b.T
    for first in range(0, heads, 2):
        lanes = slice(first * HEAD, (first + 2) * HEAD)
        current = px_ref[:, lanes].astype(F32)
        active, slope = conv(current, before_x[:, lanes], taps_x_ref[:, lanes])
        before_x[:, lanes] = current[BLOCK - 8 :]
        slope_x_ref[:, lanes] = slope.astype(BF16)
        x_low = active.astype(BF16)
        x_ref[:, lanes] = x_low
        x = x_low.astype(F32)
        scaled = x * pair_of(step, first, low_half)
        total = pair_of(fade, first, low_half) * entering[:, lanes] + skip_ref[:, lanes] * x
        for head, keep in ((first, low_half), (first + 1, jnp.logical_not(low_half))):
            mixing = (gram * spread(level, across, head)).astype(BF16)
            total += mm(mixing, jnp.where(keep, scaled, 0.0).astype(BF16))
        all_y[block, :, lanes] = total
        update = mm(by_state, (x * pair_of(weight, first, low_half)).astype(BF16))
        state[:, lanes] = state[:, lanes] * pair_of(last, first, low_half) + update
        if first + 2 < heads:
            serve(first // 2)

    @pl.when(block == 0)
    def _():
        loads[0].wait()

    all_z[block] = mm(normed_ref[...], v_z[...]).astype(BF16)
    serve(heads // 2 - 1)

    @pl.when(block == blocks - 1)
    def _():
        loads[1].wait()
        lane = iota2((1, LANES), 1)

        def sums_of(chunk, carry):
            d_yn = column_valid(length_ref, chunk) * mm(v_up[chunk], v_o[...], ((1,), (1,)))
            all_dyn[chunk] = d_yn
            gated = all_y[chunk] * jax.nn.silu(all_z[chunk].astype(F32))
            square = jnp.sum(gated * gated, axis=1, keepdims=True)
            weighted = gate_gain_ref[...] * gated
            all_g[chunk] = weighted.astype(BF16)
            along = jnp.sum(weighted * d_yn, axis=1, keepdims=True)
            pair = jnp.where(lane == 0, square, 0.0) + jnp.where(lane == 1, along, 0.0)
            stat_all[me, chunk] = pair.T[0:8]
            return carry

        lax.fori_loop(0, blocks, sums_of, 0)
        own_stats = stat_all.at[me]
        copies = [
            remote(own_stats, own_stats, stat_send.at[i], stat_recv.at[i], device)
            for i, device in enumerate(around.all)
        ]
        for copy in copies:
            copy.start()
        gain_ref[...] = jnp.zeros_like(gain_ref)

        def store_mixed(chunk):
            slot = chunk % 2
            return pltpu.make_async_copy(
                v_mixed.at[slot], mixed_parts.at[chunk], store_sem.at[slot, 3]
            )

        def mixed_of(chunk, carry):
            @pl.when(chunk >= 2)
            def _():
                store_mixed(chunk - 2).wait()

            v_mixed[chunk % 2] = mm(all_g[chunk], v_o[...]).astype(BF16)
            store_mixed(chunk).start()
            return carry

        lax.fori_loop(0, blocks, mixed_of, 0)
        for copy in copies:
            copy.wait()
        total = jnp.sum(stat_all[...], axis=0)
        for i in range(n_ctx):
            columns[i] = total[i].T
        scale = lax.rsqrt(columns[me][:, 0:1] / channels + EPS) * column_valid(length_ref, me)
        v_scale[...] = jnp.broadcast_to(scale, v_scale.shape)
        store_scale = pltpu.make_async_copy(v_scale, own_scale, load_sem.at[2])
        store_scale.start()

        def stores(chunk):
            slot = chunk % 2
            rows = pl.ds(pl.multiple_of(chunk * BLOCK, BLOCK), BLOCK)
            return [
                pltpu.make_async_copy(source.at[slot], target, store_sem.at[slot, i])
                for i, (source, target) in enumerate(
                    (
                        (v_yt, gate_t.at[chunk]),
                        (v_dz, d_z.at[rows]),
                        (v_dssd, d_ssd.at[rows]),
                    )
                )
            ]

        def gate_part(chunk, carry):
            slot = chunk % 2

            @pl.when(chunk >= 2)
            def _():
                for copy in stores(chunk - 2):
                    copy.wait()

            sums = columns[chunk]
            scale = lax.rsqrt(sums[:, 0:1] / channels + EPS)
            slant = scale * scale * scale * sums[:, 1:2] / channels
            here = column_valid(length_ref, chunk)
            for first in range(0, heads, 2):
                lanes = slice(first * HEAD, (first + 2) * HEAD)
                gate, gate_slope = silu_and_slope(all_z[chunk, :, lanes].astype(F32))
                mixed = all_y[chunk, :, lanes]
                d_yn = all_dyn[chunk, :, lanes]
                gain = gate_gain_ref[:, lanes]
                gated = mixed * gate
                scaled = gated * scale
                all_z[chunk, :, lanes] = (here * (scaled * gain)).astype(BF16)
                gain_ref[0:1, lanes] += jnp.sum(d_yn * scaled, axis=0, keepdims=True)
                d_gated = scale * (gain * d_yn) - gated * slant
                v_dz[slot, :, lanes] = (d_gated * mixed * gate_slope).astype(BF16)
                v_dssd[slot, :, lanes] = (d_gated * gate).astype(BF16)
            v_yt[slot] = all_z[chunk].T
            for copy in stores(chunk):
                copy.start()
            return carry

        lax.fori_loop(0, blocks, gate_part, 0)
        for chunk in (n_ctx - 2, n_ctx - 1):
            for copy in stores(chunk):
                copy.wait()
            store_mixed(chunk).wait()
        store_scale.wait()


def scan_forward(
    n, direct, unit, n_ctx, length, px, ps, normed, out_weight, w_z, upstream, par
):
    tokens, width = px.shape
    heads = width // HEAD
    count = tokens // BLOCK
    model = out_weight.shape[1]
    assert count == n_ctx
    by_block = lambda i: (i, 0)
    at_block = lambda size: pl.BlockSpec((BLOCK, size), by_block)
    whole = lambda a: pl.BlockSpec(a.shape, lambda i: (0, 0))
    any_space = pl.BlockSpec(memory_space=pl.ANY)
    low = lambda *shape: jax.ShapeDtypeStruct(shape, BF16)
    full = lambda *shape: jax.ShapeDtypeStruct(shape, F32)
    v_low = lambda *shape: pltpu.VMEM(shape, BF16)
    v_full = lambda *shape: pltpu.VMEM(shape, F32)
    dma = pltpu.SemaphoreType.DMA
    return pl.pallas_call(
        functools.partial(forward_kernel, heads, unit, n_ctx, n, direct),
        grid=(count,),
        in_specs=[
            pl.BlockSpec(memory_space=pltpu.SMEM),
            at_block(width),
            pl.BlockSpec((n_ctx, BLOCK, LANES), lambda i: (0, i, 0)),
            at_block(model),
            any_space,
            any_space,
            any_space,
        ]
        + [whole(par)],
        out_specs=[
            at_block(width),
            at_block(STATE),
            at_block(STATE),
            at_block(width),
            at_block(2 * STATE),
            at_block(LANES),
            at_block(LANES),
            at_block(LANES),
            pl.BlockSpec((1, STATE, width), lambda i: (i, 0, 0)),
            pl.BlockSpec((8, width), lambda i: (0, 0)),
            any_space,
            any_space,
            any_space,
            any_space,
            any_space,
        ],
        out_shape=[
            low(tokens, width),
            low(tokens, STATE),
            low(tokens, STATE),
            low(tokens, width),
            low(tokens, 2 * STATE),
            full(tokens, LANES),
            full(tokens, LANES),
            full(tokens, LANES),
            low(count, STATE, width),
            full(8, width),
            low(count, width, BLOCK),
            low(count, BLOCK, model),
            low(tokens, width),
            low(tokens, width),
            full(BLOCK, LANES),
        ],
        scratch_shapes=[
            v_full(STATE, width),
            v_full(8, width),
            v_full(8, 2 * STATE),
            v_low(width, model),
            v_low(*w_z.shape),
            v_low(count, BLOCK, model),
            v_full(count, BLOCK, width),
            v_low(count, BLOCK, width),
            v_full(count, BLOCK, width),
            v_low(count, BLOCK, width),
            v_low(2, width, BLOCK),
            v_low(2, BLOCK, model),
            v_low(2, BLOCK, width),
            v_low(2, BLOCK, width),
            v_full(BLOCK, LANES),
            v_full(n_ctx, count, 8, BLOCK),
            v_full(count, BLOCK, 8),
            dma((3,)),
            dma((2, 4)),
            dma((2, 2)),
            dma((2, 2, n - 1)),
            dma,
            dma((3,)),
            dma((3,)),
        ],
        compiler_params=pltpu.CompilerParams(
            collective_id=2, has_side_effects=True, vmem_limit_bytes=58 * 1024 * 1024
        ),
        name="scan_forward",
    )(length, px, ps, normed, out_weight, w_z, upstream, par)


def head_sums(product, chooser):
    high = product.astype(BF16)
    rest = (product - high.astype(F32)).astype(BF16)
    return mm(high, chooser) + mm(rest, chooser)


def backward_kernel(
    heads,
    unit,
    n_ctx,
    n,
    px_ref,
    ps_ref,
    x_ref,
    b_ref,
    c_ref,
    slope_x_ref,
    slope_s_ref,
    lam_ref,
    step_ref,
    chain_ref,
    kept_ref,
    dssd_ref,
    gate_t,
    normed_t,
    upstream,
    d_z,
    mixed_parts,
    own_scale,
    hidden,
    gain_grads_ref,
    par_ref,
    dx_ref,
    small_ref,
    d_s,
    shard_o,
    shard_z,
    first_x,
    layer_out,
    back,
    mixed_grads,
    for_step,
    for_level,
    left,
    right,
    sums,
    after_x,
    after_s,
    v_left,
    v_right,
    products,
    slots,
    stage,
    done_o,
    done_z,
    mine,
    from_core,
    from_row,
    shared_parts,
    shared_core,
    shared_row,
    v_hidden,
    v_scale,
    load_sem,
    store_sem,
    ring_send,
    ring_recv,
    part_send,
    part_recv,
    shared_send,
    shared_recv,
):
    turn = pl.program_id(0)
    turns = heads // 2 // POINTS
    block = pl.num_programs(0) - 1 - turn
    width, model = x_ref.shape[1], v_hidden.shape[1]
    taps_x_ref, taps_s_ref, _, skip_ref, _, rate = parameters(par_ref, width)
    own = hidden.shape[0]
    ring = Ring(n)
    around = Around(ring.me, ring.shard)
    piece = slots.shape[3]
    sum_mixed = TokenSum(
        around, mixed_parts, mine.at[0], mine.at[1], from_core, from_row, part_send, part_recv
    )
    sum_shared = TokenSum(
        around,
        shared_parts,
        shared_parts.at[ring.me],
        shared_parts.at[around.row_at],
        shared_core,
        shared_row,
        shared_send,
        shared_recv,
    )
    loads = [
        pltpu.make_async_copy(source, target, load_sem.at[i])
        for i, (source, target) in enumerate(
            (
                (d_z, v_right.at[:, pl.ds(model, width)]),
                *((normed_t.at[c], v_left.at[pl.ds(width, model), pl.ds(c * own, own)]) for c in range(n_ctx)),
                *((upstream.at[c], v_right.at[pl.ds(c * own, own), pl.ds(0, model)]) for c in range(n_ctx)),
                *((gate_t.at[c], v_left.at[pl.ds(0, width), pl.ds(c * own, own)]) for c in range(n_ctx)),
                *sum_mixed.loads(),
                (hidden, v_hidden),
                (own_scale, v_scale),
            )
        )
    ]
    loads_z, loads_o = loads[: 1 + n_ctx], loads[1 + n_ctx : 1 + 3 * n_ctx]
    loads_rest = loads[1 + 3 * n_ctx :]

    def in_left(way, index):
        first = width + (2 * index + way) * piece
        return v_left[pl.ds(pl.multiple_of(first, 16), piece), :]

    def out_left(index):
        return v_left[pl.ds(pl.multiple_of(index * piece, 16), piece), :]

    def all_products():
        tile = max(2 * piece, BLOCK)
        shards = tile // (2 * piece)

        def out_rows(i, carry):
            rows = pl.ds(pl.multiple_of(i * BLOCK, BLOCK), BLOCK)
            left = v_left[rows, :]
            products[rows, 0:width] = mm(left, v_right[:, 0:width]).astype(BF16)
            products[rows, width:model] = mm(left, v_right[:, width:model]).astype(BF16)
            return carry

        def in_rows(i, carry):
            left = v_left[pl.ds(pl.multiple_of(width + i * tile, 16), tile), :]
            both = mm(left, v_right[:, model:]).astype(BF16)
            for j in range(shards):
                place = pl.ds(pl.multiple_of((i * shards + j) * piece, 16), piece)
                for way in (0, 1):
                    products[place, model + way * width : model + (way + 1) * width] = both[
                        (2 * j + way) * piece : (2 * j + way + 1) * piece
                    ]
            return carry

        lax.fori_loop(0, model // tile, in_rows, 0)
        lax.fori_loop(0, width // BLOCK, out_rows, 0)

    def product(kind, way, index):
        at = pl.multiple_of(kind * model + way * width, LANES)
        return products[pl.ds(pl.multiple_of(index * piece, 16), piece), pl.ds(at, width)]

    def hop(kind, way, step, source):
        return remote(
            source,
            slots.at[kind, step, way],
            ring_send.at[kind, way],
            ring_recv.at[kind, way, step],
            (ring.me, ring.at(1 - 2 * way)),
        )

    def start_ring(kind):
        for way in (0, 1):
            index = ring.at(2 * way - 1)
            if kind == 0:
                first = mm(out_left(index), v_right[:, way * width : (way + 1) * width])
            else:
                first = mm(in_left(way, index), v_right[:, model:])
            stage[kind, way] = first.astype(BF16)
            hop(kind, way, 0, stage.at[kind, way]).start()

    def ring_step(step):
        def body(kind, way):
            index = ring.at((step + 2) * (2 * way - 1))
            hop(kind, way, step, stage.at[kind, way]).wait()
            place = slots.at[kind, step, way]
            total = place[...] + product(kind, way, index)

            @pl.when(step < n - 2)
            def _():
                place[...] = total
                hop(kind, way, step + 1, place).start()

            @pl.when(jnp.logical_and(step == n - 2, kind == 0))
            def _():
                done_o[:, pl.ds(pl.multiple_of(way * width, LANES), width)] = total

            @pl.when(jnp.logical_and(step == n - 2, kind == 1))
            def _():
                done_z[way] = total.T

        lax.fori_loop(0, 4, lambda e, carry: (body(1 - e // 2, e % 2), carry)[1], 0)

    def serve(point):
        at = turn * POINTS + point
        points = POINTS * n_ctx
        lax.fori_loop(
            at * (n - 1) // points,
            (at + 1) * (n - 1) // points,
            lambda step, carry: (ring_step(step), carry)[1],
            0,
        )

    @pl.when(turn == 0)
    def _():
        for device in around.all:
            greet(device)
        greet(ring.neighbour(0))
        greet(ring.neighbour(1))
        for copy in loads:
            copy.start()
        for c in range(3, n_ctx):
            shared_parts[c] = jnp.zeros(shared_parts.shape[1:], BF16)
        back[...] = jnp.zeros_like(back)
        small_ref[...] = jnp.zeros_like(small_ref)
        small_ref[taps_x_ref.shape[0] : taps_x_ref.shape[0] + 1, 0:width] = gain_grads_ref[0:1, :]
        after_x[...] = jnp.zeros_like(after_x)
        after_s[...] = jnp.zeros_like(after_s)
        pl.semaphore_wait(pltpu.get_barrier_semaphore(), 5)
        for copy in loads_z:
            copy.wait()
        start_ring(1)
        for copy in loads_o:
            copy.wait()
        start_ring(0)
        sum_mixed.start()
        all_products()
        for copy in loads_rest:
            copy.wait()

    @pl.when(turn == 1)
    def _():
        sum_mixed.pass_row()

    taps = taps_x_ref.shape[0] - 1

    rows_b, rows_c = b_ref[...], c_ref[...]
    step = step_ref[...]
    lam = lam_ref[...]
    gram = mm(rows_c, rows_b, ((1,), (1,)))
    gram_t = mm(rows_b, rows_c, ((1,), (1,)))
    level, across, last, weight, fade = levels(lam, step)
    out_decay = jnp.exp(level - level[BLOCK - 1 : BLOCK, :])
    step_across = step.T
    at_row, at_col = iota2((BLOCK, BLOCK), 0), iota2((BLOCK, BLOCK), 1)
    order = (at_row > at_col).astype(F32) - (at_row < at_col).astype(F32)
    low_half = iota2((1, LANES), 1) < HEAD
    lane = iota2((1, LANES), 1)
    by_state = rows_c.T
    kept = kept_ref[0]
    old_back = back[...].astype(BF16)
    entering = mm(rows_c, kept)
    leaving = mm(rows_b, old_back)
    at_last = jnp.sum(kept.astype(F32) * back[...], axis=0, keepdims=True)
    mixed_grads[...] = jnp.zeros_like(mixed_grads)
    left[...] = jnp.zeros_like(left)
    right[...] = jnp.zeros_like(right)
    sums[...] = jnp.zeros_like(sums)
    d_b = jnp.zeros((BLOCK, STATE), F32)
    d_c = jnp.zeros((BLOCK, STATE), F32)

    def conv_back(d_conv, after, current, weight):
        padded = jnp.concatenate([d_conv, after], axis=0)
        d_in = jnp.zeros_like(d_conv)
        grads = []
        for k in range(taps):
            moved = padded[taps - 1 - k : taps - 1 - k + BLOCK]
            d_in += weight[k : k + 1] * moved
            grads.append(jnp.sum(current * moved, axis=0, keepdims=True))
        grads.append(jnp.sum(d_conv, axis=0, keepdims=True))
        return d_in, jnp.concatenate(grads, axis=0)

    for first in range(0, heads, 2):
        lanes = slice(first * HEAD, (first + 2) * HEAD)
        x_low = x_ref[:, lanes]
        x = x_low.astype(F32)
        grad_low = dssd_ref[:, lanes]
        grad = grad_low.astype(F32)
        through = jnp.zeros((BLOCK, LANES), F32)
        for head, keep in ((first, low_half), (first + 1, jnp.logical_not(low_half))):
            decay = spread(level, across, head)
            grad_own = jnp.where(keep, grad, 0.0).astype(BF16)
            pairs = mm(grad_own, x_low, ((1,), (1,)))
            through += mm((gram_t * decay).astype(BF16), grad_own)
            scaled = decay * pairs * step_across[head : head + 1, :]
            mixed_grads[...] += scaled
            ordered = gram * scaled * order
            left[...] = jnp.where(
                lane == head, jnp.sum(ordered, axis=1, keepdims=True), left[...]
            )
            right[head : head + 1, :] = jnp.sum(ordered, axis=0, keepdims=True)
        weight_pair = pair_of(weight, first, low_half)
        step_pair = pair_of(step, first, low_half)
        fade_pair = pair_of(fade, first, low_half)
        out_pair = pair_of(out_decay, first, low_half)
        leave = leaving[:, lanes]
        d_x = step_pair * through + weight_pair * leave + skip_ref[:, lanes] * grad
        for_step[:, lanes] = x * (through + out_pair * leave)
        weighted = weight_pair * x
        faded = fade_pair * grad
        for_level[:, lanes] = weighted * leave - faded * entering[:, lanes]
        sums[0:1, lanes] = jnp.sum(weighted * leave, axis=0, keepdims=True)
        sums[2:3, lanes] = jnp.sum(x * grad, axis=0, keepdims=True)
        faded_low = faded.astype(BF16)
        d_b += mm(weighted.astype(BF16), old_back[:, lanes], ((1,), (1,)))
        d_c += mm(faded_low, kept[:, lanes], ((1,), (1,)))
        back[:, lanes] = back[:, lanes] * pair_of(last, first, low_half) + mm(by_state, faded_low)
        d_conv = d_x * slope_x_ref[:, lanes].astype(F32)
        d_in, grads = conv_back(
            d_conv, after_x[:, lanes], px_ref[:, lanes].astype(F32), taps_x_ref[:, lanes]
        )
        after_x[:, lanes] = d_conv[0:8]
        dx_ref[:, lanes] = d_in.astype(BF16)
        v_right[pl.ds(pl.multiple_of(block * BLOCK, BLOCK), BLOCK), lanes] = d_in.astype(BF16)
        small_ref[0 : taps + 1, lanes] += grads
        if first // 2 % turns == turns - 1 and first // 2 // turns < POINTS - 1:
            serve(first // 2 // turns)

    all_pairs = mixed_grads[...]
    d_b = d_b + mm(all_pairs.T.astype(BF16), rows_c)
    d_c = d_c + mm(all_pairs.astype(BF16), rows_b)
    both = jnp.concatenate([ps_ref[0], ps_ref[1]], axis=1).astype(F32)
    d_conv = jnp.concatenate([d_b, d_c], axis=1) * slope_s_ref[...].astype(F32)
    d_in, grads = conv_back(
        d_conv, after_s[...], both, taps_s_ref[...]
    )
    after_s[...] = d_conv[0:8]
    here = pl.ds(pl.multiple_of(block * BLOCK, BLOCK), BLOCK)
    shared_parts[0, here, :] = d_in[:, :STATE].astype(BF16)
    shared_parts[1, here, :] = d_in[:, STATE:].astype(BF16)
    small_ref[0 : taps + 1, width:] += grads

    chooser = (iota2((width, LANES), 0) // HEAD == iota2((width, LANES), 1)).astype(BF16)
    d_step = head_sums(for_step[...], chooser)
    sums[1:2, :] = at_last
    total = head_sums(sums[...], chooser)
    d_level = head_sums(for_level[...], chooser) - left[...] + right[...].T
    final = -total[0:1, :] - last * total[1:2, :]
    d_level = d_level + jnp.where(iota2((BLOCK, 1), 0) == BLOCK - 1, final, 0.0)
    d_lam = mm_exact((at_row <= at_col).astype(F32), d_level)
    d_raw = (d_step + d_lam * rate) * chain_ref[...]
    head_row = taps + 2
    small_ref[head_row : head_row + 1, 0:LANES] += jnp.sum(d_raw, axis=0, keepdims=True)
    small_ref[head_row : head_row + 1, LANES : 2 * LANES] += jnp.sum(
        d_lam * lam, axis=0, keepdims=True
    )
    small_ref[head_row : head_row + 1, 2 * LANES : 3 * LANES] += total[2:3, :]
    chosen = chosen_heads(lax.axis_index("ctx"), heads, unit, n_ctx, True)
    shared_parts[2, here, :] = mm(d_raw.astype(BF16), chosen).astype(BF16)

    @pl.when(turn == pl.num_programs(0) - 1)
    def _():
        sum_shared.start()
        for way in (0, 1):
            v_right[way * piece : (way + 1) * piece, width : 2 * width] = mm(
                in_left(way, ring.at(2 * way - 1)), v_right[:, 0:width]
            ).astype(BF16)
        sum_shared.pass_row()


    serve(POINTS - 1)

    @pl.when(turn == pl.num_programs(0) - 1)
    def _():
        stores = [
            pltpu.make_async_copy(source, target, store_sem.at[i])
            for i, source, target in (
                (0, done_o, shard_o),
                (1, done_z, shard_z),
                (2, v_right.at[pl.ds(0, 2 * piece), pl.ds(width, width)], first_x),
                (3, v_hidden, layer_out),
                (4, shared_parts.at[ring.me], d_s),
            )
        ]
        for copy in stores[0:3]:
            copy.start()
        total = v_hidden[...].astype(F32) + v_scale[:, 0:1] * sum_mixed.total()
        v_hidden[...] = total.astype(BF16)
        stores[3].start()
        shared_parts[ring.me] = sum_shared.total().astype(BF16)
        stores[4].start()
        for copy in stores:
            copy.wait()


def scan_backward(
    n, unit, n_ctx, px, ps, kept_parts, d_ssd, gate_t, normed_t, upstream, d_z, mixed_parts, own_scale, hidden, gain_grads, par
):
    x, rows_b, rows_c, slope_x, slope_s, lam, step, chain, kept = kept_parts
    tokens, width = px.shape
    heads = width // HEAD
    count = tokens // BLOCK
    own, model = hidden.shape
    piece = width // n
    assert model == 2 * width and heads // 2 % POINTS == 0
    by_block = lambda i: (count - 1 - i, 0)
    at_block = lambda size: pl.BlockSpec((BLOCK, size), by_block)
    whole = lambda a: pl.BlockSpec(a.shape, lambda i: (0, 0))
    any_space = pl.BlockSpec(memory_space=pl.ANY)
    low = lambda *shape: jax.ShapeDtypeStruct(shape, BF16)
    v_low = lambda *shape: pltpu.VMEM(shape, BF16)
    v_full = lambda *shape: pltpu.VMEM(shape, F32)
    part = lambda a, b: pl.BlockSpec((1, a, b), lambda i: (count - 1 - i, 0, 0))
    small_shape = (8, width + 2 * STATE)
    dma = pltpu.SemaphoreType.DMA
    return pl.pallas_call(
        functools.partial(backward_kernel, heads, unit, n_ctx, n),
        grid=(count,),
        in_specs=[
            at_block(width),
            pl.BlockSpec((n_ctx, BLOCK, LANES), lambda i: (0, count - 1 - i, 0)),
            at_block(width),
            at_block(STATE),
            at_block(STATE),
            at_block(width),
            at_block(2 * STATE),
            at_block(LANES),
            at_block(LANES),
            at_block(LANES),
            part(STATE, width),
            at_block(width),
        ]
        + [any_space] * 7
        + [whole(a) for a in (gain_grads, par)],
        out_specs=[
            at_block(width),
            pl.BlockSpec(small_shape, lambda i: (0, 0)),
            any_space,
            any_space,
            any_space,
            any_space,
            any_space,
        ],
        out_shape=[
            low(tokens, width),
            jax.ShapeDtypeStruct(small_shape, F32),
            low(tokens, LANES),
            low(piece, model),
            low(2, width, piece),
            low(2 * piece, width),
            low(own, model),
        ],
        scratch_shapes=[
            v_full(STATE, width),
            v_full(BLOCK, BLOCK),
            v_full(BLOCK, width),
            v_full(BLOCK, width),
            v_full(BLOCK, LANES),
            v_full(LANES, BLOCK),
            v_full(8, width),
            v_full(8, width),
            v_full(8, 2 * STATE),
            v_low(width + model, tokens),
            v_low(tokens, model + width),
            v_low(width, 2 * model),
            v_low(2, n - 1, 2, piece, width),
            v_low(2, 2, piece, width),
            v_low(piece, model),
            v_low(2, width, piece),
            v_low(2, own, model),
            v_low(2, own, model),
            v_low(own, model),
            v_low(n_ctx, tokens, LANES),
            v_low(2, tokens, LANES),
            v_low(tokens, LANES),
            v_low(own, model),
            v_full(own, LANES),
            dma((5 + 3 * n_ctx,)),
            dma((5,)),
            dma((2, 2)),
            dma((2, 2, n - 1)),
            dma((3,)),
            dma((3,)),
            dma((3,)),
            dma((3,)),
        ],
        compiler_params=pltpu.CompilerParams(
            collective_id=3, has_side_effects=True, vmem_limit_bytes=59 * 1024 * 1024
        ),
        name="scan_backward",
    )(
        px, ps, x, rows_b, rows_c, slope_x, slope_s, lam, step, chain, kept, d_ssd, gate_t, normed_t, upstream, d_z, mixed_parts, own_scale, hidden, gain_grads, par
    )


def gather_kernel(
    n,
    n_ctx,
    unit,
    taps,
    sizes,
    hidden,
    cotangent,
    in_weight_t,
    small,
    cotangent_all,
    w_x,
    w_s,
    w_z,
    par_out,
    gain_out,
    proj_x,
    proj_s,
    normed_out,
    normed_t,
    v_hidden,
    v_normed,
    v_x,
    v_s,
    own_z,
    v_small,
    raw_x,
    raw_s,
    raw_z,
    out_x,
    out_s,
    out_t,
    v_gain,
    v_par,
    conv_lines,
    gate_line,
    head_lines,
    load_sem,
    shared_sem,
    column_sem,
    local_sem,
    keep_sem,
    store_sem,
    ring_send,
    ring_recv,
    ctx_send,
    ctx_recv,
):
    ring = Ring(n)
    me, shard = ring.me, ring.shard
    width, model = v_x.shape[1], v_x.shape[0]
    inner = width * n_ctx
    r = model // n
    shared = in_weight_t.shape[0] - 2 * inner
    row = me // 2
    other_core = (me + 1 - 2 * (me % 2), shard)
    other_row = (me + 2 - 4 * row, shard)
    barrier = pltpu.get_barrier_semaphore()
    for device in (other_core, other_row, ring.neighbour(0), ring.neighbour(1)):
        pl.semaphore_signal(barrier, inc=1, device_id=device, device_id_type=MESH)

    part = unit * HEAD

    def load_columns(base, target, sems):
        return [
            pltpu.make_async_copy(
                in_weight_t.at[pl.ds(pl.multiple_of(base + (a * n_ctx + me) * part, 16), part)],
                target.at[pl.ds(a * part, part)],
                sems.at[a],
            )
            for a in range(width // part)
        ]

    loads = [
        load_columns(inner, raw_x, column_sem.at[0]),
        [],
        [pltpu.make_async_copy(small, v_small.at[shard], load_sem.at[1])],
        [pltpu.make_async_copy(hidden, v_hidden.at[me], load_sem.at[2])],
        load_columns(0, raw_z, column_sem.at[1]),
    ]
    raw_s[...] = jnp.zeros_like(raw_s)

    def load_shared(wait):
        for j in (0, 1):
            first = me * LANES + j * HEAD

            @pl.when(first < shared)
            def _():
                copy = pltpu.make_async_copy(
                    in_weight_t.at[pl.ds(pl.multiple_of(2 * inner + first, HEAD), HEAD)],
                    raw_s.at[pl.ds(j * HEAD, HEAD)],
                    shared_sem.at[j],
                )
                copy.wait() if wait else copy.start()

    load_shared(False)
    for copies in loads:
        for copy in copies:
            copy.start()

    def loaded(i):
        for copy in loads[i]:
            copy.wait()

    pl.semaphore_wait(barrier, 4)

    half = width // 2
    rows = r // 2
    both_rows = lambda index, way: pl.ds(pl.multiple_of((2 * index + way) * rows, 16), rows)
    x_part = lambda a, sub: lambda index, way: a.at[both_rows(index, way), pl.ds(sub * half, half)]
    s_part = lambda index, way: v_s.at[both_rows(index, way)]
    small_part = lambda index, way: v_small.at[index, pl.ds(way * SMALL_ROWS // 2, SMALL_ROWS // 2)]
    phases = (
        ((0, small_part), (1, s_part), (2, x_part(v_x, 0)), (3, x_part(v_x, 1))),
        ((4, x_part(w_z, 0)), (5, x_part(w_z, 1))),
    )

    def hop(stream, way, step):
        number, part = stream
        place = part(ring.at(-step if way == 0 else step), way)
        return remote(
            place, place, ring_send.at[number, way], ring_recv.at[number, way, step],
            ring.neighbour(way),
        )

    def arrives(stream, way, step):
        number, part = stream
        landed = part(ring.at(-step - 1 if way == 0 else step + 1), way)
        return remote(
            landed, landed, ring_send.at[number, way], ring_recv.at[number, way, step],
            ring.neighbour(way),
        )

    def start_stream(stream):
        for way in (0, 1):
            hop(stream, way, 0).start()

    def to_row(i, a, whole):
        return remote(a, whole.at[me], ctx_send.at[i, 0], ctx_recv.at[i, 0], other_row)

    def to_core(i, a, whole):
        return remote(a, whole.at[me], ctx_send.at[i, 1], ctx_recv.at[i, 1], other_core)

    def pass_on(i, whole):
        beyond = whole.at[other_row[0]]
        return remote(beyond, beyond, ctx_send.at[i, 2], ctx_recv.at[i, 2], other_core)

    to_row(0, hidden, v_hidden).start()
    to_core(0, hidden, v_hidden).start()
    own_rows = pl.ds(pl.multiple_of(shard * r, 16), r)
    loaded(2)
    start_stream(phases[0][0])
    loaded(0)
    v_x[own_rows, :] = raw_x[...].T
    start_stream(phases[0][2])
    start_stream(phases[0][3])
    load_shared(True)
    v_s[own_rows, :] = raw_s[...].T
    start_stream(phases[0][1])
    keep_cotangent = pltpu.make_async_copy(cotangent, cotangent_all.at[me], local_sem)
    keep_cotangent.start()
    keep_shared = pltpu.make_async_copy(out_s, proj_s.at[me], shared_sem.at[2])
    loaded(3)
    loaded(4)
    own_z[...] = raw_z[...].T
    keep_z = pltpu.make_async_copy(own_z, w_z.at[own_rows], keep_sem)
    keep_z.start()
    keep_z.wait()

    def run_phase(number, work, after):
        def body(step, carry):
            for stream in phases[number]:
                for way in (0, 1):
                    arrives(stream, way, step).wait_recv()
                    hop(stream, way, step).wait_send()
                    hop(stream, way, step + 1).start()
            if work is not None:

                @pl.when(step < n_ctx)
                def _():
                    work(step)

                @pl.when(step == n_ctx - 1)
                def _():
                    to_row(2, out_s, proj_s).start()
                    to_core(2, out_s, proj_s).start()
                    keep_shared.start()

            return carry

        lax.fori_loop(0, n - 2, body, 0)
        after()
        for stream in phases[number]:
            for way in (0, 1):
                arrives(stream, way, n - 2).wait_recv()
                hop(stream, way, n - 2).wait_send()

    tokens = v_hidden.shape[1]

    def project_first(chunk):
        at = pl.ds(pl.multiple_of(chunk * tokens, tokens), tokens)
        resid = v_hidden[chunk].astype(F32)
        scale = lax.rsqrt(jnp.mean(resid * resid, axis=1, keepdims=True) + EPS)
        normed = (resid * scale * v_gain[...]).astype(BF16)
        v_normed[at, :] = normed
        out_x[at, :] = mm(normed, v_x[...]).astype(BF16)
        out_s[at, :] = mm(normed, v_s[...]).astype(BF16)
        out_t[chunk] = normed.T

    stores = [
        pltpu.make_async_copy(source, target, store_sem.at[i])
        for i, (source, target) in enumerate(
            (
                (v_x, w_x),
                (v_s, w_s),
                (v_par, par_out),
                (v_gain, gain_out),
                (out_x, proj_x),
                (v_normed, normed_out),
                (out_t, normed_t),
            )
        )
    ]

    def after_first():
        for stream in phases[1]:
            start_stream(stream)
        to_row(0, hidden, v_hidden).wait_recv()
        pass_on(0, v_hidden).start()
        to_row(1, cotangent, cotangent_all).start()
        to_core(1, cotangent, cotangent_all).start()
        to_row(0, hidden, v_hidden).wait_send()
        to_core(0, hidden, v_hidden).wait()
        pass_on(0, v_hidden).wait()

    def after_second():
        to_row(1, cotangent, cotangent_all).wait_recv()
        pass_on(1, cotangent_all).start()
        to_row(2, out_s, proj_s).wait_recv()
        pass_on(2, proj_s).start()
        for copy in stores[4:]:
            copy.start()

    run_phase(0, None, after_first)
    gain_size, conv_size, gate_size, held = sizes
    head_lines[...] = jnp.zeros_like(head_lines)
    for f in range(n):
        v_gain[:, f * r : (f + 1) * r] = v_small[f, 0:1, 0:r].astype(F32)
        conv_lines[0 : taps + 1, f * conv_size : (f + 1) * conv_size] = v_small[
            f, 1 : taps + 2, 0:conv_size
        ].astype(F32)
        gate_line[:, f * gate_size : (f + 1) * gate_size] = v_small[
            f, taps + 2 : taps + 3, 0:gate_size
        ].astype(F32)
        for k in range(3):
            head_lines[k : k + 1, f * held : (f + 1) * held] = v_small[
                f, taps + 3 : taps + 4, k * held : (k + 1) * held
            ].astype(F32)

    def own_part(line, a):
        at = (a * n_ctx + me) * part
        span = max(part, LANES)
        found = line[:, pl.ds(pl.multiple_of(at // LANES * LANES, LANES), span)]
        if part < LANES:
            found = pltpu.roll(found, lax.rem(LANES - at % LANES, LANES), 1)
        return found[:, 0:part]

    v_par[...] = jnp.zeros_like(v_par)
    for a in range(width // part):
        v_par[0 : taps + 1, a * part : (a + 1) * part] = own_part(conv_lines, a)[0 : taps + 1]
        v_par[taps + 1 : taps + 2, a * part : (a + 1) * part] = own_part(gate_line, a)
    v_par[0 : taps + 1, width:] = conv_lines[0 : taps + 1, inner:]
    lines = mm(head_lines[...].astype(BF16), chosen_heads(me, width // HEAD, unit, n_ctx))
    heads_row = taps + 3
    v_par[heads_row : heads_row + 1, 0:LANES] = lines[0:1]
    v_par[heads_row : heads_row + 1, LANES : 2 * LANES] = jnp.exp(lines[1:2])
    wide = (iota2((LANES, width), 1) // HEAD == iota2((LANES, width), 0)).astype(BF16)
    v_par[taps + 2 : taps + 3, 0:width] = mm(lines.astype(BF16), wide)[2:3]
    for copy in stores[0:4]:
        copy.start()
    run_phase(1, project_first, after_second)
    to_row(1, cotangent, cotangent_all).wait_send()
    to_core(1, cotangent, cotangent_all).wait()
    pass_on(1, cotangent_all).wait()
    keep_cotangent.wait()
    to_row(2, out_s, proj_s).wait_send()
    to_core(2, out_s, proj_s).wait()
    pass_on(2, proj_s).wait()
    keep_shared.wait()
    for copy in stores:
        copy.wait()


def gather_all(n, n_ctx, unit, taps, sizes, width, hidden, cotangent, in_weight_t, small):
    own, model = hidden.shape
    tokens = own * n_ctx
    rows = in_weight_t.shape[1]
    any_space = pl.BlockSpec(memory_space=pl.ANY)
    par_shape = (taps + 4, width + 2 * STATE)
    inner = width * n_ctx
    low = lambda *shape: jax.ShapeDtypeStruct(shape, BF16)
    v_low = lambda *shape: pltpu.VMEM(shape, BF16)
    dma = pltpu.SemaphoreType.DMA
    return pl.pallas_call(
        functools.partial(gather_kernel, n, n_ctx, unit, taps, sizes),
        in_specs=[any_space] * 4,
        out_specs=[any_space] * 10,
        out_shape=[
            low(n_ctx, own, model),
            low(model, width),
            low(model, LANES),
            low(model, width),
            jax.ShapeDtypeStruct(par_shape, F32),
            jax.ShapeDtypeStruct((1, model), F32),
            low(tokens, width),
            low(n_ctx, tokens, LANES),
            low(tokens, model),
            low(n_ctx, model, own),
        ],
        scratch_shapes=[
            v_low(n_ctx, own, model),
            v_low(tokens, model),
            v_low(model, width),
            v_low(model, LANES),
            v_low(rows, width),
            v_low(n, small.shape[0], small.shape[1]),
            v_low(width, rows),
            v_low(LANES, rows),
            v_low(width, rows),
            v_low(tokens, width),
            v_low(tokens, LANES),
            v_low(n_ctx, model, own),
            pltpu.VMEM((1, model), F32),
            pltpu.VMEM(par_shape, F32),
            pltpu.VMEM((8, inner + 2 * STATE), F32),
            pltpu.VMEM((1, inner), F32),
            pltpu.VMEM((8, LANES), F32),
            dma((3,)),
            dma((3,)),
            dma((2, width // (unit * HEAD))),
            dma,
            dma,
            dma((7,)),
            dma((6, 2)),
            dma((6, 2, n - 1)),
            dma((3, 3)),
            dma((3, 3)),
        ],
        compiler_params=pltpu.CompilerParams(
            collective_id=0, has_side_effects=True, vmem_limit_bytes=56 * 1024 * 1024
        ),
        name="gather_all",
    )(hidden, cotangent, in_weight_t, small)


def reduce_kernel(
    n,
    n_ctx,
    direct,
    normed_t,
    d_z,
    d_x,
    d_s,
    w_z,
    w_x,
    w_s,
    shard_o,
    shard_z,
    first_x,
    small,
    hidden,
    cotangent,
    gain,
    g_z,
    g_x,
    g_s,
    g_o,
    hidden_grad,
    small_out,
    norm_out,
    v_normed_t,
    v_d_z,
    v_d_x,
    v_d_s,
    v_z,
    v_x,
    v_s,
    parts,
    partials,
    slots,
    stage,
    done,
    moved,
    from_core,
    from_row,
    v_hidden,
    v_cotangent,
    v_gain,
    small_all,
    small_ctx,
    norm_all,
    norm_ctx,
    load_sem,
    store_sem,
    ring_send,
    ring_recv,
    ctx_send,
    ctx_recv,
    own_sem,
    piece_send,
    piece_recv,
    part_send,
    part_recv,
    small_send,
    small_recv,
    small_ctx_send,
    small_ctx_recv,
):
    ring = Ring(n)
    me, shard = ring.me, ring.shard
    around = Around(me, shard)
    core, row = me % 2, me // 2
    piece_peer = (shard % n_ctx, shard // n_ctx * n_ctx + me)
    moves = shard % n_ctx != me
    barrier = pltpu.get_barrier_semaphore()
    for device in around.all:
        greet(device)
    lax.fori_loop(1, n, lambda j, carry: (greet((me, lax.rem(shard + j, n))), carry)[1], 0)
    own = hidden.shape[0]
    sum_normed = TokenSum(
        around, parts, parts.at[me], parts.at[around.row_at], from_core, from_row, part_send, part_recv
    )
    sum_small, sum_norm = (
        SmallSum(
            n, around, whole, sums, small_send.at[i], small_recv.at[i], small_ctx_send.at[i], small_ctx_recv.at[i]
        )
        for i, (whole, sums) in enumerate(((small_all, small_ctx), (norm_all, norm_ctx)))
    )
    loads = [
        pltpu.make_async_copy(source, target, load_sem.at[i])
        for i, (source, target) in enumerate(
            (
                *((normed_t.at[c], v_normed_t.at[:, pl.ds(c * own, own)]) for c in range(n_ctx)),
                (d_s, v_d_s),
                (d_x, v_d_x),
                (small, small_all.at[shard]),
                (d_z, v_d_z),
                (w_z, v_z),
                (w_x, v_x),
                (w_s, v_s),
                (hidden, v_hidden),
                (cotangent, v_cotangent),
                (gain, v_gain),
            )
        )
    ]
    ring_loads = n_ctx + 2
    for copy in loads:
        copy.start()
    if direct:
        pl.semaphore_wait(barrier, n + 2)
    else:

        @pl.when(moves)
        def _():
            greet(piece_peer)
            pl.semaphore_wait(barrier, n + 3)

        @pl.when(jnp.logical_not(moves))
        def _():
            pl.semaphore_wait(barrier, n + 2)

    rows = v_normed_t.shape[0] // (2 * n)
    half, last = v_d_x.shape[1] // 2, v_d_s.shape[1]
    streams = (
        (0, v_d_s, 0, last, 2 * half),
        (1, v_d_x, 0, half, 0),
        (2, v_d_x, half, half, half),
    )

    def compute_partials(step):
        for way in (0, 1):
            index = ring.at(-step - 2 if way == 0 else step + 2)
            left = v_normed_t[pl.ds(pl.multiple_of((2 * index + way) * rows, 16), rows), :]
            partials[way, :, 2 * half :] = mm(left, v_d_s[...])
            partials[way, :, 0 : 2 * half] = mm(left, v_d_x[...])

    def slot(stream, way, step):
        return slots.at[step, way, :, pl.ds(stream[4], stream[3])]

    def hop(stream, way, step, source):
        return remote(
            source,
            slot(stream, way, step),
            ring_send.at[stream[0], way],
            ring_recv.at[stream[0], way, step],
            ring.neighbour(way),
        )

    def first_part(stream, way):
        if stream[0] == 0:
            return stage.at[way]
        return first_x.at[pl.ds(way * rows, rows), pl.ds(stream[4], stream[3])]

    def arrived(stream, way, step):
        hop(stream, way, step, first_part(stream, way)).wait()
        partial = partials[way, :, stream[4] : stream[4] + stream[3]]
        return slot(stream, way, step)[...].astype(F32) + partial

    done_of = lambda stream: done.at[pl.ds(stream[4], stream[3])]
    of_x = lambda c, first: g_x.at[c, pl.ds(first, half)]
    shares = (
        (shard_o if direct else moved, lambda c: g_o.at[c]),
        (shard_z, lambda c: g_z.at[c]),
        (done_of(streams[1]), lambda c: of_x(c, 0)),
        (done_of(streams[2]), lambda c: of_x(c, half)),
        (done_of(streams[0]), lambda c: g_s.at[c]),
    )

    def share(i, kind):
        source, whole = shares[i]
        at = me
        if kind == 2:
            source, at = whole(around.row_at), around.row_at
        device = around.row if kind == 0 else around.core
        return remote(source, whole(at), ctx_send.at[i, kind], ctx_recv.at[i, kind], device)

    def keep(i):
        return pltpu.make_async_copy(shares[i][0], shares[i][1](me), own_sem.at[i])

    def start_share(i):
        share(i, 0).start()
        share(i, 1).start()
        keep(i).start()

    def pass_share(i):
        share(i, 0).wait_recv()
        share(i, 2).start()

    def close_share(i):
        share(i, 0).wait_send()
        share(i, 1).wait()
        share(i, 2).wait()
        keep(i).wait()

    def move_piece(wait):
        if direct:
            return
        keep_piece = pltpu.make_async_copy(shard_o, moved, piece_send)
        send_piece = remote(shard_o, moved, piece_send, piece_recv, piece_peer)

        @pl.when(moves)
        def _():
            send_piece.wait() if wait else send_piece.start()

        @pl.when(jnp.logical_not(moves))
        def _():
            keep_piece.wait() if wait else keep_piece.start()

    def normed_part(i, carry):
        to_row = row + (1 - i % 2) * (1 - 2 * row)
        to_core = core + (1 - i // 2) * (1 - 2 * core)
        at = 2 * to_row + to_core
        tokens = pl.ds(pl.multiple_of(at * own, own), own)
        parts[at] = (
            mm(v_d_z[tokens, :], v_z[...], ((1,), (1,)))
            + mm(v_d_x[tokens, :], v_x[...], ((1,), (1,)))
            + mm(v_d_s[tokens, :], v_s[...], ((1,), (1,)))
        ).astype(BF16)
        return carry

    store_grad = pltpu.make_async_copy(v_cotangent, hidden_grad, store_sem.at[0])
    store_small = pltpu.make_async_copy(small_ctx, small_out, store_sem.at[1])
    store_norm = pltpu.make_async_copy(norm_ctx, norm_out, store_sem.at[2])

    def finish_tokens():
        resid = v_hidden[...].astype(F32)
        scale = lax.rsqrt(jnp.mean(resid * resid, axis=1, keepdims=True) + EPS)
        d_normed = sum_normed.total()
        f = v_gain[...] * d_normed
        slope = scale**3 * jnp.mean(resid * f, axis=1, keepdims=True)
        grad = v_cotangent[...].astype(F32) + scale * f - resid * slope
        v_cotangent[...] = grad.astype(BF16)
        store_grad.start()
        by_model = jnp.sum(d_normed * resid * scale, axis=0, keepdims=True)
        size = norm_all.shape[2]
        for j in range(norm_all.shape[1]):
            norm_all[shard, j : j + 1, :] = by_model[:, j * size : (j + 1) * size]
        sum_norm.start()

    for stream in streams[1:]:
        for way in (0, 1):
            hop(stream, way, 0, first_part(stream, way)).start()
    move_piece(False)
    for copy in loads[:ring_loads]:
        copy.wait()
    for way in (0, 1):
        at = (2 * ring.at(2 * way - 1) + way) * rows
        left = v_normed_t[pl.ds(pl.multiple_of(at, 16), rows), :]
        stage[way] = mm(left, v_d_s[...]).astype(BF16)
        hop(streams[0], way, 0, stage.at[way]).start()
    compute_partials(0)
    for copy in loads[ring_loads:]:
        copy.wait()
    sum_small.start()
    move_piece(True)
    start_share(0)
    start_share(1)

    def body(step, carry):
        for stream in streams:
            for way in (0, 1):
                total = arrived(stream, way, step)
                place = slot(stream, way, step)
                place[...] = total.astype(BF16)
                hop(stream, way, step + 1, place).start()
        compute_partials(step + 1)

        @pl.when(step < n_ctx)
        def _():
            normed_part(step, 0)

        @pl.when(step == 1)
        def _():
            sum_normed.start()

        @pl.when(step == 2)
        def _():
            sum_normed.pass_row()

        return carry

    lax.fori_loop(0, n - 2, body, 0)
    sum_small.add()
    pass_share(0)
    pass_share(1)
    for number, shared in ((0, 4), (1, 2), (2, 3)):
        place = done_of(streams[number])
        for way in (0, 1):
            total = arrived(streams[number], way, n - 2)
            place[:, way * rows : (way + 1) * rows] = total.T.astype(BF16)
        start_share(shared)
    finish_tokens()
    sum_norm.add()
    sum_small.finish()
    store_small.start()
    for i in (4, 2, 3):
        pass_share(i)
    sum_norm.finish()
    store_norm.start()
    for i in range(5):
        close_share(i)
    store_grad.wait()
    store_small.wait()
    store_norm.wait()


def reduce_all(
    n, n_ctx, direct, normed_t, d_z, d_x, d_s, w_z, w_x, w_s, shard_o, shard_z, first_x, small, hidden, cotangent, gain
):
    model, tokens = normed_t.shape[1], d_x.shape[0]
    width, shared_width = d_x.shape[1], d_s.shape[1]
    rows, piece, own = model // n, width // n, hidden.shape[0]
    columns = width + shared_width
    any_space = pl.BlockSpec(memory_space=pl.ANY)
    dma = pltpu.SemaphoreType.DMA
    low = lambda *shape: jax.ShapeDtypeStruct(shape, BF16)
    v_low = lambda *shape: pltpu.VMEM(shape, BF16)
    v_full = lambda *shape: pltpu.VMEM(shape, F32)
    norm_shape = (8, model // 8)
    return pl.pallas_call(
        functools.partial(reduce_kernel, n, n_ctx, direct),
        in_specs=[any_space] * 14,
        out_specs=[any_space] * 7,
        out_shape=[
            low(n_ctx, 2, width, rows // 2),
            low(n_ctx, width, rows),
            low(n_ctx, shared_width, rows),
            low(n_ctx, piece, model),
            low(own, model),
            jax.ShapeDtypeStruct((n_ctx,) + small.shape, F32),
            jax.ShapeDtypeStruct((n_ctx,) + norm_shape, F32),
        ],
        scratch_shapes=[
            v_low(model, tokens),
            v_low(tokens, width),
            v_low(tokens, width),
            v_low(tokens, shared_width),
            v_low(*w_z.shape),
            v_low(*w_x.shape),
            v_low(*w_s.shape),
            v_low(n_ctx, own, model),
            v_full(2, rows // 2, columns),
            v_low(n - 1, 2, rows // 2, columns),
            v_low(2, rows // 2, shared_width),
            v_low(columns, rows),
            v_low(piece, model),
            v_low(2, own, model),
            v_low(own, model),
            v_low(own, model),
            v_low(own, model),
            v_full(1, model),
            v_full(n, *small.shape),
            v_full(n_ctx, *small.shape),
            v_full(n, *norm_shape),
            v_full(n_ctx, *norm_shape),
            dma((10 + n_ctx,)),
            dma((3,)),
            dma((3, 2)),
            dma((3, 2, n - 1)),
            dma((5, 3)),
            dma((5, 3)),
            dma((5,)),
            dma,
            dma,
            dma((3,)),
            dma((3,)),
            dma((2, n - 1)),
            dma((2, n - 1)),
            dma((2, 3)),
            dma((2, 3)),
        ],
        compiler_params=pltpu.CompilerParams(
            collective_id=1, has_side_effects=True, vmem_limit_bytes=58 * 1024 * 1024
        ),
        name="reduce_all",
    )(
        normed_t, d_z, d_x, d_s, w_z, w_x, w_s, shard_o, shard_z, first_x, small, hidden, cotangent, gain
    )


def assemble_kernel(part, z_ref, x_ref, s_ref, o_ref, out_ref, rows_ref):
    place = pl.program_id(0)
    n_ctx, size, half = x_ref.shape[0], x_ref.shape[1], z_ref.shape[3]

    def interleave(write):
        for a in range(size // part):
            for c in range(n_ctx):
                write(
                    slice((a * n_ctx + c) * part, (a * n_ctx + c + 1) * part),
                    c,
                    slice(a * part, (a + 1) * part),
                )

    def write_z(target, c, source):
        for way in (0, 1):
            out_ref[target, way * half : (way + 1) * half] = z_ref[c, way, source, :].astype(F32)

    def write_x(target, c, source):
        out_ref[target, :] = x_ref[c, source, :].astype(F32)

    @pl.when(place < n_ctx)
    def _():
        interleave(write_z)

    @pl.when(jnp.logical_and(place >= n_ctx, place < 2 * n_ctx))
    def _():
        interleave(write_x)

    @pl.when(place == 2 * n_ctx)
    def _():
        for c in range(s_ref.shape[0]):
            out_ref[c * LANES : (c + 1) * LANES, :] = s_ref[c].astype(F32)

    @pl.when(place < 2 * n_ctx)
    def _():
        rows_ref[...] = o_ref[...].astype(F32)


def assemble(part, g_z, g_x, g_s, g_o, columns):
    n_ctx, width, rows = g_x.shape
    block = (n_ctx, width // n_ctx, rows)
    g_o = g_o.reshape(-1, g_o.shape[2])
    tile = max(g_o.shape[0] // (2 * n_ctx), 16)
    at_tile = lambda i: (jnp.minimum(i, g_o.shape[0] // tile - 1), 0)
    return pl.pallas_call(
        functools.partial(assemble_kernel, part),
        grid=(2 * n_ctx + 1,),
        in_specs=[
            pl.BlockSpec(
                (n_ctx, 2, width // n_ctx, rows // 2),
                lambda i: (0, 0, jnp.minimum(i, n_ctx - 1), 0),
            ),
            pl.BlockSpec(block, lambda i: (0, jnp.clip(i - n_ctx, 0, n_ctx - 1), 0)),
            pl.BlockSpec(g_s.shape, lambda i: (0, 0, 0)),
            pl.BlockSpec((tile, g_o.shape[1]), at_tile),
        ],
        out_specs=[
            pl.BlockSpec((width, rows), lambda i: (i, 0)),
            pl.BlockSpec((tile, g_o.shape[1]), at_tile),
        ],
        out_shape=[
            jax.ShapeDtypeStruct((columns, rows), F32),
            jax.ShapeDtypeStruct(g_o.shape, F32),
        ],
        compiler_params=pltpu.CompilerParams(vmem_limit_bytes=58 * 1024 * 1024),
        name="assemble",
    )(g_z, g_x, g_s, g_o)


def on_device(
    hidden,
    cotangent,
    seq_lens,
    norm_gain,
    in_weight,
    conv_weight,
    conv_bias,
    dt_bias,
    a_log,
    d_skip,
    gate_gain,
    out_weight,
):
    n_ctx, n_fsdp = lax.axis_size("ctx"), lax.axis_size("fsdp")
    me, shard = lax.axis_index("ctx"), lax.axis_index("fsdp")
    taps = conv_weight.shape[0]
    heads_all = dt_bias.shape[0] * n_fsdp
    inner = out_weight.shape[0] * n_fsdp
    heads, width = heads_all // n_ctx, inner // n_ctx
    model = hidden.shape[2]
    both = 2 * STATE
    held = dt_bias.shape[0]
    direct = held % n_ctx == 0
    unit = held // n_ctx if direct else 1
    part = unit * HEAD
    assert both + heads_all <= n_ctx * LANES and heads_all == HEAD

    per_head = jnp.concatenate([dt_bias, a_log, d_skip])
    lines = [norm_gain[None], conv_weight, conv_bias[None], gate_gain[None], per_head[None]]
    longest = -(-max(a.shape[1] for a in lines) // LANES) * LANES
    small = jnp.concatenate([jnp.pad(a, ((0, 0), (0, longest - a.shape[1]))) for a in lines])
    small = jnp.pad(small, ((0, SMALL_ROWS - small.shape[0]), (0, 0)))
    sizes = (norm_gain.shape[0], conv_bias.shape[0], gate_gain.shape[0], held)
    upstream, w_x, w_s, w_z, par, gain_norm, proj_x, proj_s, normed, normed_t = gather_all(
        n_fsdp, n_ctx, unit, taps, sizes, width, hidden[0], cotangent[0], in_weight.T, small
    )
    *kept_parts, gain_grads, gate_t, mixed_parts, d_z, d_ssd, own_scale = scan_forward(
        n_fsdp, direct, unit, n_ctx, seq_lens, proj_x, proj_s, normed, out_weight, w_z, upstream, par
    )
    d_x, small_grads, d_s, shard_o, shard_z, first_x, layer_out = scan_backward(
        n_fsdp, unit, n_ctx, proj_x, proj_s, kept_parts, d_ssd, gate_t, normed_t, upstream, d_z, mixed_parts, own_scale, hidden[0], gain_grads, par
    )
    g_z, g_x, g_s, g_o, hidden_grad, sums, norm_sums = reduce_all(
        n_fsdp, n_ctx, direct, normed_t, d_z, d_x, d_s, w_z, w_x, w_s, shard_o, shard_z, first_x, small_grads, hidden[0], cotangent[0], gain_norm
    )
    grad_in_weight, grad_out_weight = assemble(
        part, g_z, g_x, g_s, g_o, 2 * inner + both + heads_all
    )

    def shard_of(lines):
        size = lines.shape[1] // n_fsdp
        return lax.dynamic_slice_in_dim(lines, shard * size, size, axis=1)

    def in_order(sums_of, size):
        lines = sums_of.shape[1]
        by_part = sums_of.reshape(n_ctx, lines, -1, size)
        return jnp.transpose(by_part, (1, 2, 0, 3)).reshape(lines, -1)

    conv_sums = shard_of(
        jnp.concatenate(
            [
                in_order(sums[:, : taps + 1, :width], part),
                jnp.sum(sums[:, : taps + 1, width:], axis=0),
            ],
            axis=1,
        )
    )
    gate_sums = shard_of(in_order(sums[:, taps + 1 : taps + 2, :width], part))
    head_sums_all = sums[:, taps + 2, : 3 * LANES].reshape(n_ctx, 3, LANES)[:, :, :heads]
    head_grads = shard_of(in_order(head_sums_all, unit))
    norm_sums = jnp.sum(norm_sums, axis=0).reshape(1, -1)
    return (
        layer_out[None],
        hidden_grad[None],
        shard_of(norm_sums)[0],
        grad_in_weight.T,
        conv_sums[:taps],
        conv_sums[taps],
        head_grads[0],
        head_grads[1],
        head_grads[2],
        gate_sums[0],
        grad_out_weight,
    )


def solution(mesh):
    tokens, rows, flat = P("fsdp", "ctx", None), P("fsdp", None), P("fsdp")
    taps = P(None, "fsdp")
    return jax.shard_map(
        on_device,
        mesh=mesh,
        in_specs=(tokens, tokens, flat, flat, rows, taps, flat, flat, flat, flat, flat, rows),
        out_specs=(tokens, tokens, flat, rows, taps, flat, flat, flat, flat, flat, rows),
        check_vma=False,
    )
```

```python
import functools

import jax
import jax.numpy as jnp
from jax import lax
from jax.experimental import pallas as pl
from jax.experimental.pallas import tpu as pltpu
from jax.sharding import PartitionSpec as P

HEAD = 64
STATE = 128
BLOCK = 256
LANES = 128
POINTS = 4
EPS = 1e-05
F32 = jnp.float32
BF16 = jnp.bfloat16


def mm(a, b, contract=((1,), (0,))):
    return lax.dot_general(a, b, (contract, ((), ())), preferred_element_type=F32)


def mm_exact(a, b, contract=((1,), (0,))):
    return lax.dot_general(
        a, b, (contract, ((), ())), precision=lax.Precision.HIGHEST, preferred_element_type=F32
    )


def iota2(shape, axis):
    return lax.broadcasted_iota(jnp.int32, shape, axis)


def levels(lam, step):
    tri = (iota2((BLOCK, BLOCK), 0) >= iota2((BLOCK, BLOCK), 1)).astype(F32)
    level = mm_exact(tri, lam)
    across = level.T
    last = level[BLOCK - 1 : BLOCK, :]
    weight = jnp.exp(level - last) * step
    return level, across, jnp.exp(-last), weight, jnp.exp(-level)


def pair_of(array, first, low_half):
    return jnp.where(low_half, array[:, first : first + 1], array[:, first + 1 : first + 2])


def spread(level, across, head):
    return jnp.exp(-jnp.abs(level[:, head : head + 1] - across[head : head + 1, :]))


def silu_and_slope(v):
    s = jax.nn.sigmoid(v)
    return v * s, s * (1.0 + v * (1.0 - s))


def chosen_heads(me, heads, unit, n_ctx, turned=False):
    here, there = iota2((LANES, LANES), 1), iota2((LANES, LANES), 0)
    if turned:
        here, there = there, here
    head = (here // unit * n_ctx + me) * unit + here % unit
    return jnp.where(jnp.logical_and(there == head, here < heads), 1.0, 0.0).astype(BF16)


class Lines:
    def __init__(self, ref, first, rows, at, size):
        self.ref, self.first, self.at, self.shape = ref, first, at, (rows, size)

    def __getitem__(self, index):
        rows = slice(self.first, self.first + self.shape[0])
        lanes = slice(0, self.shape[1]) if index is Ellipsis else index[1]
        return self.ref[rows, self.at + lanes.start : self.at + lanes.stop]


def parameters(par_ref, width):
    lines = par_ref.shape[0] - 3
    head = par_ref[lines + 2 : lines + 3, 0 : 2 * LANES]
    return (
        Lines(par_ref, 0, lines, 0, width),
        Lines(par_ref, 0, lines, width, 2 * STATE),
        Lines(par_ref, lines, 1, 0, width),
        Lines(par_ref, lines + 1, 1, 0, width),
        head[:, :LANES],
        head[:, LANES:],
    )


def column_valid(length_ref, block):
    at = iota2((BLOCK, 1), 0) + block * BLOCK
    return (at < length_ref[0]).astype(F32)


MESH = pl.DeviceIdType.MESH
SMALL_ROWS = 32


def ring_place(index, half):
    a, b = index // 2, index % 2
    return a + b * (2 * half - 1 - 2 * a)


def ring_index(place, half):
    b = place // half
    return 2 * (place + b * (2 * half - 1 - 2 * place)) + b


class Ring:
    def __init__(self, n):
        self.n, self.half = n, n // 2
        self.me, self.shard = lax.axis_index("ctx"), lax.axis_index("fsdp")
        self.place = ring_place(self.shard, self.half)

    def at(self, steps):
        return ring_index(lax.rem(self.place + steps + 2 * self.n, self.n), self.half)

    def neighbour(self, way):
        return (self.me, self.at(1 if way == 0 else -1))


def remote(source, target, send, recv, device):
    return pltpu.make_async_remote_copy(
        src_ref=source,
        dst_ref=target,
        send_sem=send,
        recv_sem=recv,
        device_id=device,
        device_id_type=MESH,
    )


def greet(device):
    pl.semaphore_signal(pltpu.get_barrier_semaphore(), inc=1, device_id=device, device_id_type=MESH)


class Around:
    def __init__(self, me, shard):
        core, row = me % 2, me // 2
        self.me = me
        self.core_at = me + 1 - 2 * core
        self.row_at = me + 2 - 4 * row
        self.both_at = self.row_at + 1 - 2 * core
        self.core, self.row, self.both = (
            (at, shard) for at in (self.core_at, self.row_at, self.both_at)
        )
        self.all = (self.core, self.row, self.both)


class TokenSum:
    def __init__(self, around, parts, own_part, row_part, from_core, from_row, send, recv):
        self.around, self.parts, self.own_part, self.row_part = around, parts, own_part, row_part
        self.from_core, self.from_row, self.send, self.recv = from_core, from_row, send, recv

    def loads(self):
        at = self.around
        return (
            (self.parts.at[at.row_at], self.row_part),
            (self.parts.at[at.me], self.own_part),
        )

    def to_core(self, which):
        at = self.around
        return remote(
            self.parts.at[(at.core_at, at.both_at)[which]],
            self.from_core.at[which],
            self.send.at[which],
            self.recv.at[which],
            at.core,
        )

    def to_row(self):
        return remote(
            self.row_part, self.from_row, self.send.at[2], self.recv.at[2], self.around.row
        )

    def start(self):
        self.to_core(1).start()
        self.to_core(0).start()

    def pass_row(self):
        self.to_core(1).wait()
        total = self.row_part[...].astype(F32) + self.from_core[1].astype(F32)
        self.row_part[...] = total.astype(BF16)
        self.to_row().start()

    def total(self):
        self.to_core(0).wait()
        self.to_row().wait()
        return (
            self.own_part[...].astype(F32)
            + self.from_core[0].astype(F32)
            + self.from_row[...].astype(F32)
        )


class SmallSum:
    def __init__(self, n, around, whole, sums, send, recv, ctx_send, ctx_recv):
        self.n, self.around, self.whole, self.sums = n, around, whole, sums
        self.send, self.recv, self.ctx_send, self.ctx_recv = send, recv, ctx_send, ctx_recv
        self.shard = lax.axis_index("fsdp")

    def to_peer(self, offset):
        own = self.whole.at[self.shard]
        peer = (self.around.me, lax.rem(self.shard + offset, self.n))
        return remote(own, own, self.send.at[offset - 1], self.recv.at[offset - 1], peer)

    def to_ctx(self, i):
        own = self.sums.at[self.around.me]
        return remote(own, own, self.ctx_send.at[i], self.ctx_recv.at[i], self.around.all[i])

    def start(self):
        lax.fori_loop(1, self.n, lambda j, carry: (self.to_peer(j).start(), carry)[1], 0)

    def add(self):
        lax.fori_loop(1, self.n, lambda j, carry: (self.to_peer(j).wait(), carry)[1], 0)
        self.sums[self.around.me] = jnp.sum(self.whole[...], axis=0)
        for i in range(3):
            self.to_ctx(i).start()

    def finish(self):
        for i in range(3):
            self.to_ctx(i).wait()


def forward_kernel(
    heads,
    unit,
    n_ctx,
    n,
    direct,
    length_ref,
    px_ref,
    ps_ref,
    normed_ref,
    out_weight,
    w_z,
    upstream,
    par_ref,
    x_ref,
    b_ref,
    c_ref,
    slope_x_ref,
    slope_s_ref,
    lam_ref,
    step_ref,
    chain_ref,
    kept_ref,
    gain_ref,
    gate_t,
    mixed_parts,
    d_z,
    d_ssd,
    state,
    before_x,
    before_s,
    v_o,
    v_z,
    v_up,
    all_y,
    all_z,
    all_dyn,
    all_g,
    v_yt,
    v_mixed,
    v_dz,
    v_dssd,
    stat_all,
    columns,
    load_sem,
    store_sem,
    ring_send,
    ring_recv,
    piece_recv,
    stat_send,
    stat_recv,
):
    block = pl.program_id(0)
    blocks = pl.num_programs(0)
    ring = Ring(n)
    me, shard = ring.me, ring.shard
    around = Around(me, shard)
    width = px_ref.shape[1]
    taps_x_ref, taps_s_ref, gate_gain_ref, skip_ref, bias_step, rate = parameters(par_ref, width)
    channels = width * n_ctx
    piece, size = v_o.shape[0] // n, v_o.shape[1] // 4
    points = heads // 2 * n_ctx
    loads = [
        pltpu.make_async_copy(source, target, load_sem.at[i])
        for i, (source, target) in enumerate(((w_z, v_z), (upstream, v_up)))
    ]
    shard_rows = lambda index: pl.ds(pl.multiple_of(index * piece, 16), piece)
    own_piece = out_weight.at[pl.ds(pl.multiple_of(me * piece, 16), piece)]
    piece_peer = (shard % n_ctx, shard // n_ctx * n_ctx + me)
    moves = shard % n_ctx != me

    def hop(way, sub, step):
        at = pl.multiple_of((2 * way + sub) * size, LANES)
        place = v_o.at[shard_rows(ring.at(step * (2 * way - 1))), pl.ds(at, size)]
        return remote(
            place,
            place,
            ring_send.at[way, sub],
            ring_recv.at[way, sub, step],
            (me, ring.at(1 - 2 * way)),
        )

    def streams(body):
        lax.fori_loop(0, 4, lambda e, carry: (body(e // 2, e % 2), carry)[1], 0)

    def ring_step(step):
        def body(way, sub):
            hop(way, sub, step).wait()

            @pl.when(step < n - 2)
            def _():
                hop(way, sub, step + 1).start()

        streams(body)

    def serve(point):
        at = block * (heads // 2) + point
        lax.fori_loop(
            at * (n - 1) // points,
            (at + 1) * (n - 1) // points,
            lambda step, carry: (ring_step(step), carry)[1],
            0,
        )

    @pl.when(block == 0)
    def _():
        for device in around.all:
            greet(device)
        greet(ring.neighbour(0))
        greet(ring.neighbour(1))
        keep = pltpu.make_async_copy(own_piece, v_o.at[shard_rows(shard)], load_sem.at[2])
        if direct:
            keep.start()
            pl.semaphore_wait(pltpu.get_barrier_semaphore(), 5)
            keep.wait()
        else:
            send = remote(
                own_piece, v_o.at[shard_rows(piece_peer[1])], load_sem.at[2], piece_recv, piece_peer
            )

            @pl.when(moves)
            def _():
                greet(piece_peer)
                pl.semaphore_wait(pltpu.get_barrier_semaphore(), 6)
                send.start()
                send.wait()

            @pl.when(jnp.logical_not(moves))
            def _():
                pl.semaphore_wait(pltpu.get_barrier_semaphore(), 5)
                keep.start()
                keep.wait()

        streams(lambda way, sub: hop(way, sub, 0).start())
        for copy in loads:
            copy.start()
        state[...] = jnp.zeros_like(state)
        before_x[...] = jnp.zeros_like(before_x)
        before_s[...] = jnp.zeros_like(before_s)

    valid = column_valid(length_ref, block)
    low_half = iota2((1, LANES), 1) < HEAD
    taps = taps_x_ref.shape[0] - 1

    def conv(current, before, weight):
        padded = jnp.concatenate([before, current], axis=0)
        total = weight[taps : taps + 1]
        for k in range(taps):
            first = 8 - (taps - 1) + k
            total = total + weight[k : k + 1] * padded[first : first + BLOCK]
        return silu_and_slope(total)

    both = jnp.concatenate([ps_ref[0], ps_ref[1]], axis=1).astype(F32)
    active, slope = conv(both, before_s[...], taps_s_ref[...])
    before_s[...] = both[BLOCK - 8 :]
    slope_s_ref[...] = slope.astype(BF16)
    rows_b, rows_c = active[:, :STATE].astype(BF16), active[:, STATE:].astype(BF16)
    b_ref[...] = rows_b
    c_ref[...] = rows_c
    raw = mm(ps_ref[2], chosen_heads(me, heads, unit, n_ctx)) + bias_step
    own = iota2((1, LANES), 1) < heads
    step = jnp.where(own, valid * jax.nn.softplus(raw), 0.0)
    lam = step * rate
    step_ref[...] = step
    lam_ref[...] = lam
    chain_ref[...] = jnp.where(own, valid * jax.nn.sigmoid(raw), 0.0)

    gram = mm(rows_c, rows_b, ((1,), (1,)))
    level, across, last, weight, fade = levels(lam, step)
    kept_ref[0] = state[...].astype(BF16)
    entering = mm(rows_c, state[...].astype(BF16))
    by_state = rows_b.T
    for first in range(0, heads, 2):
        lanes = slice(first * HEAD, (first + 2) * HEAD)
        current = px_ref[:, lanes].astype(F32)
        active, slope = conv(current, before_x[:, lanes], taps_x_ref[:, lanes])
        before_x[:, lanes] = current[BLOCK - 8 :]
        slope_x_ref[:, lanes] = slope.astype(BF16)
        x_low = active.astype(BF16)
        x_ref[:, lanes] = x_low
        x = x_low.astype(F32)
        scaled = x * pair_of(step, first, low_half)
        total = pair_of(fade, first, low_half) * entering[:, lanes] + skip_ref[:, lanes] * x
        for head, keep in ((first, low_half), (first + 1, jnp.logical_not(low_half))):
            mixing = (gram * spread(level, across, head)).astype(BF16)
            total += mm(mixing, jnp.where(keep, scaled, 0.0).astype(BF16))
        all_y[block, :, lanes] = total
        update = mm(by_state, (x * pair_of(weight, first, low_half)).astype(BF16))
        state[:, lanes] = state[:, lanes] * pair_of(last, first, low_half) + update
        if first + 2 < heads:
            serve(first // 2)

    @pl.when(block == 0)
    def _():
        loads[0].wait()

    all_z[block] = mm(normed_ref[...], v_z[...]).astype(BF16)
    serve(heads // 2 - 1)

    @pl.when(block == blocks - 1)
    def _():
        loads[1].wait()
        lane = iota2((1, LANES), 1)

        def sums_of(chunk, carry):
            d_yn = column_valid(length_ref, chunk) * mm(v_up[chunk], v_o[...], ((1,), (1,)))
            all_dyn[chunk] = d_yn
            gated = all_y[chunk] * jax.nn.silu(all_z[chunk].astype(F32))
            square = jnp.sum(gated * gated, axis=1, keepdims=True)
            weighted = gate_gain_ref[...] * gated
            all_g[chunk] = weighted.astype(BF16)
            along = jnp.sum(weighted * d_yn, axis=1, keepdims=True)
            pair = jnp.where(lane == 0, square, 0.0) + jnp.where(lane == 1, along, 0.0)
            stat_all[me, chunk] = pair.T[0:8]
            return carry

        lax.fori_loop(0, blocks, sums_of, 0)
        own_stats = stat_all.at[me]
        copies = [
            remote(own_stats, own_stats, stat_send.at[i], stat_recv.at[i], device)
            for i, device in enumerate(around.all)
        ]
        for copy in copies:
            copy.start()
        gain_ref[...] = jnp.zeros_like(gain_ref)

        def store_mixed(chunk):
            slot = chunk % 2
            return pltpu.make_async_copy(
                v_mixed.at[slot], mixed_parts.at[chunk], store_sem.at[slot, 3]
            )

        def mixed_of(chunk, carry):
            @pl.when(chunk >= 2)
            def _():
                store_mixed(chunk - 2).wait()

            v_mixed[chunk % 2] = mm(all_g[chunk], v_o[...]).astype(BF16)
            store_mixed(chunk).start()
            return carry

        lax.fori_loop(0, blocks, mixed_of, 0)
        for copy in copies:
            copy.wait()
        total = jnp.sum(stat_all[...], axis=0)
        for i in range(n_ctx):
            columns[i] = total[i].T
        own_total = sum(stat_all[c, me] for c in range(n_ctx))
        own_valid = iota2((1, BLOCK), 1) + me * BLOCK < length_ref[0]
        scale_row = lax.rsqrt(own_total[0:1] / channels + EPS)
        gain_ref[1:2, 0:BLOCK] = jnp.where(own_valid, scale_row, 0.0)

        def stores(chunk):
            slot = chunk % 2
            rows = pl.ds(pl.multiple_of(chunk * BLOCK, BLOCK), BLOCK)
            return [
                pltpu.make_async_copy(source.at[slot], target, store_sem.at[slot, i])
                for i, (source, target) in enumerate(
                    (
                        (v_yt, gate_t.at[chunk]),
                        (v_dz, d_z.at[rows]),
                        (v_dssd, d_ssd.at[rows]),
                    )
                )
            ]

        def gate_part(chunk, carry):
            slot = chunk % 2

            @pl.when(chunk >= 2)
            def _():
                for copy in stores(chunk - 2):
                    copy.wait()

            sums = columns[chunk]
            scale = lax.rsqrt(sums[:, 0:1] / channels + EPS)
            slant = scale * scale * scale * sums[:, 1:2] / channels
            here = column_valid(length_ref, chunk)
            for first in range(0, heads, 2):
                lanes = slice(first * HEAD, (first + 2) * HEAD)
                gate, gate_slope = silu_and_slope(all_z[chunk, :, lanes].astype(F32))
                mixed = all_y[chunk, :, lanes]
                d_yn = all_dyn[chunk, :, lanes]
                gain = gate_gain_ref[:, lanes]
                gated = mixed * gate
                scaled = gated * scale
                all_z[chunk, :, lanes] = (here * (scaled * gain)).astype(BF16)
                gain_ref[0:1, lanes] += jnp.sum(d_yn * scaled, axis=0, keepdims=True)
                d_gated = scale * (gain * d_yn) - gated * slant
                v_dz[slot, :, lanes] = (d_gated * mixed * gate_slope).astype(BF16)
                v_dssd[slot, :, lanes] = (d_gated * gate).astype(BF16)
            v_yt[slot] = all_z[chunk].T
            for copy in stores(chunk):
                copy.start()
            return carry

        lax.fori_loop(0, blocks, gate_part, 0)
        for chunk in (n_ctx - 2, n_ctx - 1):
            for copy in stores(chunk):
                copy.wait()
            store_mixed(chunk).wait()


def scan_forward(
    n, direct, unit, n_ctx, length, px, ps, normed, out_weight, w_z, upstream, par
):
    tokens, width = px.shape
    heads = width // HEAD
    count = tokens // BLOCK
    model = out_weight.shape[1]
    assert count == n_ctx
    by_block = lambda i: (i, 0)
    at_block = lambda size: pl.BlockSpec((BLOCK, size), by_block)
    whole = lambda a: pl.BlockSpec(a.shape, lambda i: (0, 0))
    any_space = pl.BlockSpec(memory_space=pl.ANY)
    low = lambda *shape: jax.ShapeDtypeStruct(shape, BF16)
    full = lambda *shape: jax.ShapeDtypeStruct(shape, F32)
    v_low = lambda *shape: pltpu.VMEM(shape, BF16)
    v_full = lambda *shape: pltpu.VMEM(shape, F32)
    dma = pltpu.SemaphoreType.DMA
    return pl.pallas_call(
        functools.partial(forward_kernel, heads, unit, n_ctx, n, direct),
        grid=(count,),
        in_specs=[
            pl.BlockSpec(memory_space=pltpu.SMEM),
            at_block(width),
            pl.BlockSpec((n_ctx, BLOCK, LANES), lambda i: (0, i, 0)),
            at_block(model),
            any_space,
            any_space,
            any_space,
        ]
        + [whole(par)],
        out_specs=[
            at_block(width),
            at_block(STATE),
            at_block(STATE),
            at_block(width),
            at_block(2 * STATE),
            at_block(LANES),
            at_block(LANES),
            at_block(LANES),
            pl.BlockSpec((1, STATE, width), lambda i: (i, 0, 0)),
            pl.BlockSpec((8, width), lambda i: (0, 0)),
            any_space,
            any_space,
            any_space,
            any_space,
        ],
        out_shape=[
            low(tokens, width),
            low(tokens, STATE),
            low(tokens, STATE),
            low(tokens, width),
            low(tokens, 2 * STATE),
            full(tokens, LANES),
            full(tokens, LANES),
            full(tokens, LANES),
            low(count, STATE, width),
            full(8, width),
            low(count, width, BLOCK),
            low(count, BLOCK, model),
            low(tokens, width),
            low(tokens, width),
        ],
        scratch_shapes=[
            v_full(STATE, width),
            v_full(8, width),
            v_full(8, 2 * STATE),
            v_low(width, model),
            v_low(*w_z.shape),
            v_low(count, BLOCK, model),
            v_full(count, BLOCK, width),
            v_low(count, BLOCK, width),
            v_full(count, BLOCK, width),
            v_low(count, BLOCK, width),
            v_low(2, width, BLOCK),
            v_low(2, BLOCK, model),
            v_low(2, BLOCK, width),
            v_low(2, BLOCK, width),
            v_full(n_ctx, count, 8, BLOCK),
            v_full(count, BLOCK, 8),
            dma((3,)),
            dma((2, 4)),
            dma((2, 2)),
            dma((2, 2, n - 1)),
            dma,
            dma((3,)),
            dma((3,)),
        ],
        compiler_params=pltpu.CompilerParams(
            collective_id=2, has_side_effects=True, vmem_limit_bytes=58 * 1024 * 1024
        ),
        name="scan_forward",
    )(length, px, ps, normed, out_weight, w_z, upstream, par)


def head_sums(product, chooser):
    high = product.astype(BF16)
    rest = (product - high.astype(F32)).astype(BF16)
    return mm(high, chooser) + mm(rest, chooser)


def backward_kernel(
    heads,
    unit,
    n_ctx,
    n,
    px_ref,
    ps_ref,
    x_ref,
    b_ref,
    c_ref,
    slope_x_ref,
    slope_s_ref,
    lam_ref,
    step_ref,
    chain_ref,
    kept_ref,
    dssd_ref,
    gate_t,
    normed_t,
    upstream,
    d_z,
    mixed_parts,
    hidden,
    gain_grads_ref,
    par_ref,
    dx_ref,
    small_ref,
    d_s,
    shard_o,
    shard_z,
    layer_out,
    back,
    mixed_grads,
    for_step,
    for_level,
    left,
    right,
    sums,
    after_x,
    after_s,
    v_left,
    v_right,
    products,
    slots,
    stage,
    done_o,
    done_z,
    mine,
    from_core,
    from_row,
    shared_parts,
    shared_core,
    shared_row,
    v_hidden,
    load_sem,
    store_sem,
    ring_send,
    ring_recv,
    part_send,
    part_recv,
    shared_send,
    shared_recv,
):
    turn = pl.program_id(0)
    turns = heads // 2 // POINTS
    block = pl.num_programs(0) - 1 - turn
    width, model = x_ref.shape[1], v_hidden.shape[1]
    taps_x_ref, taps_s_ref, _, skip_ref, _, rate = parameters(par_ref, width)
    own = hidden.shape[0]
    ring = Ring(n)
    around = Around(ring.me, ring.shard)
    piece, size = slots.shape[4], slots.shape[5]
    sum_mixed = TokenSum(
        around, mixed_parts, mine.at[0], mine.at[1], from_core, from_row, part_send, part_recv
    )
    sum_shared = TokenSum(
        around,
        shared_parts,
        shared_parts.at[ring.me],
        shared_parts.at[around.row_at],
        shared_core,
        shared_row,
        shared_send,
        shared_recv,
    )
    loads = [
        pltpu.make_async_copy(source, target, load_sem.at[i])
        for i, (source, target) in enumerate(
            (
                *((gate_t.at[c], v_left.at[pl.ds(0, width), pl.ds(c * own, own)]) for c in range(n_ctx)),
                *((upstream.at[c], v_right.at[pl.ds(c * own, own), pl.ds(0, model)]) for c in range(n_ctx)),
                *((normed_t.at[c], v_left.at[pl.ds(width, model), pl.ds(c * own, own)]) for c in range(n_ctx)),
                (d_z, v_right.at[:, pl.ds(model, width)]),
                *sum_mixed.loads(),
                (hidden, v_hidden),
            )
        )
    ]
    ring_loads = 1 + 3 * n_ctx

    def partial_sum(kind, way, sub, index):
        first = (1 - kind) * index * piece + kind * (width + (2 * index + way) * piece)
        at = (1 - kind) * (2 * way + sub) * size + kind * (model + sub * size)
        return mm(
            v_left[pl.ds(pl.multiple_of(first, 16), piece), :],
            v_right[:, pl.ds(pl.multiple_of(at, LANES), size)],
        )

    def all_products():
        tile = max(2 * piece, BLOCK)
        shards = tile // (2 * piece)

        def out_rows(i, carry):
            rows = pl.ds(pl.multiple_of(i * BLOCK, BLOCK), BLOCK)
            left = v_left[rows, :]
            products[rows, 0:width] = mm(left, v_right[:, 0:width]).astype(BF16)
            products[rows, width:model] = mm(left, v_right[:, width:model]).astype(BF16)
            return carry

        def in_rows(i, carry):
            left = v_left[pl.ds(pl.multiple_of(width + i * tile, 16), tile), :]
            both = mm(left, v_right[:, model:]).astype(BF16)
            for j in range(shards):
                place = pl.ds(pl.multiple_of((i * shards + j) * piece, 16), piece)
                for way in (0, 1):
                    products[place, model + way * width : model + (way + 1) * width] = both[
                        (2 * j + way) * piece : (2 * j + way + 1) * piece
                    ]
            return carry

        lax.fori_loop(0, width // BLOCK, out_rows, 0)
        lax.fori_loop(0, model // tile, in_rows, 0)

    def product(kind, way, sub, index):
        at = pl.multiple_of(kind * model + way * width + sub * size, LANES)
        return products[pl.ds(pl.multiple_of(index * piece, 16), piece), pl.ds(at, size)]

    def hop(kind, way, sub, step, source):
        return remote(
            source,
            slots.at[kind, step, way, sub],
            ring_send.at[kind, way, sub],
            ring_recv.at[kind, way, sub, step],
            (ring.me, ring.at(1 - 2 * way)),
        )

    def streams(body):
        def one(e, carry):
            body(e // 4, e // 2 % 2, e % 2)
            return carry

        lax.fori_loop(0, 8, one, 0)

    def start_ring(kind, way, sub):
        place = stage.at[kind, way, sub]
        place[...] = partial_sum(kind, way, sub, ring.at(2 * way - 1)).astype(BF16)
        hop(kind, way, sub, 0, place).start()

    def ring_step(step):
        def body(kind, way, sub):
            index = ring.at((step + 2) * (2 * way - 1))
            hop(kind, way, sub, step, stage.at[kind, way, sub]).wait()
            place = slots.at[kind, step, way, sub]
            total = place[...].astype(F32) + product(kind, way, sub, index).astype(F32)

            @pl.when(step < n - 2)
            def _():
                place[...] = total.astype(BF16)
                hop(kind, way, sub, step + 1, place).start()

            @pl.when(jnp.logical_and(step == n - 2, kind == 0))
            def _():
                at = pl.multiple_of((2 * way + sub) * size, LANES)
                done_o[:, pl.ds(at, size)] = total.astype(BF16)

            @pl.when(jnp.logical_and(step == n - 2, kind == 1))
            def _():
                done_z[way, pl.ds(pl.multiple_of(sub * size, 16), size), :] = total.T.astype(BF16)

        streams(body)

    def serve(point):
        at = turn * POINTS + point
        points = POINTS * n_ctx
        lax.fori_loop(
            at * (n - 1) // points,
            (at + 1) * (n - 1) // points,
            lambda step, carry: (ring_step(step), carry)[1],
            0,
        )

    @pl.when(turn == 0)
    def _():
        for device in around.all:
            greet(device)
        greet(ring.neighbour(0))
        greet(ring.neighbour(1))
        for copy in loads:
            copy.start()
        for c in range(3, n_ctx):
            shared_parts[c] = jnp.zeros(shared_parts.shape[1:], BF16)
        back[...] = jnp.zeros_like(back)
        small_ref[...] = jnp.zeros_like(small_ref)
        small_ref[taps_x_ref.shape[0] : taps_x_ref.shape[0] + 1, 0:width] = gain_grads_ref[0:1, :]
        after_x[...] = jnp.zeros_like(after_x)
        after_s[...] = jnp.zeros_like(after_s)
        pl.semaphore_wait(pltpu.get_barrier_semaphore(), 5)
        for copy in loads[:ring_loads]:
            copy.wait()
        streams(start_ring)
        sum_mixed.start()
        all_products()
        for copy in loads[ring_loads:]:
            copy.wait()

    @pl.when(turn == 1)
    def _():
        sum_mixed.pass_row()

    taps = taps_x_ref.shape[0] - 1

    rows_b, rows_c = b_ref[...], c_ref[...]
    step = step_ref[...]
    lam = lam_ref[...]
    gram = mm(rows_c, rows_b, ((1,), (1,)))
    gram_t = mm(rows_b, rows_c, ((1,), (1,)))
    level, across, last, weight, fade = levels(lam, step)
    out_decay = jnp.exp(level - level[BLOCK - 1 : BLOCK, :])
    step_across = step.T
    at_row, at_col = iota2((BLOCK, BLOCK), 0), iota2((BLOCK, BLOCK), 1)
    order = (at_row > at_col).astype(F32) - (at_row < at_col).astype(F32)
    low_half = iota2((1, LANES), 1) < HEAD
    lane = iota2((1, LANES), 1)
    by_state = rows_c.T
    kept = kept_ref[0]
    old_back = back[...].astype(BF16)
    entering = mm(rows_c, kept)
    leaving = mm(rows_b, old_back)
    at_last = jnp.sum(kept.astype(F32) * back[...], axis=0, keepdims=True)
    mixed_grads[...] = jnp.zeros_like(mixed_grads)
    left[...] = jnp.zeros_like(left)
    right[...] = jnp.zeros_like(right)
    sums[...] = jnp.zeros_like(sums)
    d_b = jnp.zeros((BLOCK, STATE), F32)
    d_c = jnp.zeros((BLOCK, STATE), F32)

    def conv_back(d_conv, after, current, weight):
        padded = jnp.concatenate([d_conv, after], axis=0)
        d_in = jnp.zeros_like(d_conv)
        grads = []
        for k in range(taps):
            moved = padded[taps - 1 - k : taps - 1 - k + BLOCK]
            d_in += weight[k : k + 1] * moved
            grads.append(jnp.sum(current * moved, axis=0, keepdims=True))
        grads.append(jnp.sum(d_conv, axis=0, keepdims=True))
        return d_in, jnp.concatenate(grads, axis=0)

    for first in range(0, heads, 2):
        lanes = slice(first * HEAD, (first + 2) * HEAD)
        x_low = x_ref[:, lanes]
        x = x_low.astype(F32)
        grad_low = dssd_ref[:, lanes]
        grad = grad_low.astype(F32)
        through = jnp.zeros((BLOCK, LANES), F32)
        for head, keep in ((first, low_half), (first + 1, jnp.logical_not(low_half))):
            decay = spread(level, across, head)
            grad_own = jnp.where(keep, grad, 0.0).astype(BF16)
            pairs = mm(grad_own, x_low, ((1,), (1,)))
            through += mm((gram_t * decay).astype(BF16), grad_own)
            scaled = decay * pairs * step_across[head : head + 1, :]
            mixed_grads[...] += scaled
            ordered = gram * scaled * order
            left[...] = jnp.where(
                lane == head, jnp.sum(ordered, axis=1, keepdims=True), left[...]
            )
            right[head : head + 1, :] = jnp.sum(ordered, axis=0, keepdims=True)
        weight_pair = pair_of(weight, first, low_half)
        step_pair = pair_of(step, first, low_half)
        fade_pair = pair_of(fade, first, low_half)
        out_pair = pair_of(out_decay, first, low_half)
        leave = leaving[:, lanes]
        d_x = step_pair * through + weight_pair * leave + skip_ref[:, lanes] * grad
        for_step[:, lanes] = x * (through + out_pair * leave)
        weighted = weight_pair * x
        faded = fade_pair * grad
        for_level[:, lanes] = weighted * leave - faded * entering[:, lanes]
        sums[0:1, lanes] = jnp.sum(weighted * leave, axis=0, keepdims=True)
        sums[2:3, lanes] = jnp.sum(x * grad, axis=0, keepdims=True)
        faded_low = faded.astype(BF16)
        d_b += mm(weighted.astype(BF16), old_back[:, lanes], ((1,), (1,)))
        d_c += mm(faded_low, kept[:, lanes], ((1,), (1,)))
        back[:, lanes] = back[:, lanes] * pair_of(last, first, low_half) + mm(by_state, faded_low)
        d_conv = d_x * slope_x_ref[:, lanes].astype(F32)
        d_in, grads = conv_back(
            d_conv, after_x[:, lanes], px_ref[:, lanes].astype(F32), taps_x_ref[:, lanes]
        )
        after_x[:, lanes] = d_conv[0:8]
        dx_ref[:, lanes] = d_in.astype(BF16)
        small_ref[0 : taps + 1, lanes] += grads
        if first // 2 % turns == turns - 1 and first // 2 // turns < POINTS - 1:
            serve(first // 2 // turns)

    all_pairs = mixed_grads[...]
    d_b = d_b + mm(all_pairs.T.astype(BF16), rows_c)
    d_c = d_c + mm(all_pairs.astype(BF16), rows_b)
    both = jnp.concatenate([ps_ref[0], ps_ref[1]], axis=1).astype(F32)
    d_conv = jnp.concatenate([d_b, d_c], axis=1) * slope_s_ref[...].astype(F32)
    d_in, grads = conv_back(
        d_conv, after_s[...], both, taps_s_ref[...]
    )
    after_s[...] = d_conv[0:8]
    here = pl.ds(pl.multiple_of(block * BLOCK, BLOCK), BLOCK)
    shared_parts[0, here, :] = d_in[:, :STATE].astype(BF16)
    shared_parts[1, here, :] = d_in[:, STATE:].astype(BF16)
    small_ref[0 : taps + 1, width:] += grads

    chooser = (iota2((width, LANES), 0) // HEAD == iota2((width, LANES), 1)).astype(BF16)
    d_step = head_sums(for_step[...], chooser)
    sums[1:2, :] = at_last
    total = head_sums(sums[...], chooser)
    d_level = head_sums(for_level[...], chooser) - left[...] + right[...].T
    final = -total[0:1, :] - last * total[1:2, :]
    d_level = d_level + jnp.where(iota2((BLOCK, 1), 0) == BLOCK - 1, final, 0.0)
    d_lam = mm_exact((at_row <= at_col).astype(F32), d_level)
    d_raw = (d_step + d_lam * rate) * chain_ref[...]
    head_row = taps + 2
    small_ref[head_row : head_row + 1, 0:LANES] += jnp.sum(d_raw, axis=0, keepdims=True)
    small_ref[head_row : head_row + 1, LANES : 2 * LANES] += jnp.sum(
        d_lam * lam, axis=0, keepdims=True
    )
    small_ref[head_row : head_row + 1, 2 * LANES : 3 * LANES] += total[2:3, :]
    chosen = chosen_heads(lax.axis_index("ctx"), heads, unit, n_ctx, True)
    shared_parts[2, here, :] = mm(d_raw.astype(BF16), chosen).astype(BF16)

    @pl.when(turn == pl.num_programs(0) - 1)
    def _():
        sum_shared.start()
        sum_shared.pass_row()


    serve(POINTS - 1)

    @pl.when(turn == pl.num_programs(0) - 1)
    def _():
        stores = [
            pltpu.make_async_copy(source, target, store_sem.at[i])
            for i, (source, target) in enumerate(
                (
                    (done_o, shard_o),
                    (done_z, shard_z),
                    (v_hidden, layer_out),
                    (shared_parts.at[ring.me], d_s),
                )
            )
        ]
        stores[0].start()
        stores[1].start()
        scale = gain_grads_ref[:, 0:BLOCK].T[:, 1:2]
        total = v_hidden[...].astype(F32) + scale * sum_mixed.total()
        v_hidden[...] = total.astype(BF16)
        stores[2].start()
        shared_parts[ring.me] = sum_shared.total().astype(BF16)
        stores[3].start()
        for copy in stores:
            copy.wait()


def scan_backward(
    n, unit, n_ctx, px, ps, kept_parts, d_ssd, gate_t, normed_t, upstream, d_z, mixed_parts, hidden, gain_grads, par
):
    x, rows_b, rows_c, slope_x, slope_s, lam, step, chain, kept = kept_parts
    tokens, width = px.shape
    heads = width // HEAD
    count = tokens // BLOCK
    own, model = hidden.shape
    piece = width // n
    assert model == 2 * width and heads // 2 % POINTS == 0
    by_block = lambda i: (count - 1 - i, 0)
    at_block = lambda size: pl.BlockSpec((BLOCK, size), by_block)
    whole = lambda a: pl.BlockSpec(a.shape, lambda i: (0, 0))
    any_space = pl.BlockSpec(memory_space=pl.ANY)
    low = lambda *shape: jax.ShapeDtypeStruct(shape, BF16)
    v_low = lambda *shape: pltpu.VMEM(shape, BF16)
    v_full = lambda *shape: pltpu.VMEM(shape, F32)
    part = lambda a, b: pl.BlockSpec((1, a, b), lambda i: (count - 1 - i, 0, 0))
    small_shape = (8, width + 2 * STATE)
    dma = pltpu.SemaphoreType.DMA
    return pl.pallas_call(
        functools.partial(backward_kernel, heads, unit, n_ctx, n),
        grid=(count,),
        in_specs=[
            at_block(width),
            pl.BlockSpec((n_ctx, BLOCK, LANES), lambda i: (0, count - 1 - i, 0)),
            at_block(width),
            at_block(STATE),
            at_block(STATE),
            at_block(width),
            at_block(2 * STATE),
            at_block(LANES),
            at_block(LANES),
            at_block(LANES),
            part(STATE, width),
            at_block(width),
        ]
        + [any_space] * 6
        + [whole(a) for a in (gain_grads, par)],
        out_specs=[
            at_block(width),
            pl.BlockSpec(small_shape, lambda i: (0, 0)),
            any_space,
            any_space,
            any_space,
            any_space,
        ],
        out_shape=[
            low(tokens, width),
            jax.ShapeDtypeStruct(small_shape, F32),
            low(tokens, LANES),
            low(piece, model),
            low(2, width, piece),
            low(own, model),
        ],
        scratch_shapes=[
            v_full(STATE, width),
            v_full(BLOCK, BLOCK),
            v_full(BLOCK, width),
            v_full(BLOCK, width),
            v_full(BLOCK, LANES),
            v_full(LANES, BLOCK),
            v_full(8, width),
            v_full(8, width),
            v_full(8, 2 * STATE),
            v_low(width + model, tokens),
            v_low(tokens, model + width),
            v_low(width, 2 * model),
            v_low(2, n - 1, 2, 2, piece, width // 2),
            v_low(2, 2, 2, piece, width // 2),
            v_low(piece, model),
            v_low(2, width, piece),
            v_low(2, own, model),
            v_low(2, own, model),
            v_low(own, model),
            v_low(n_ctx, tokens, LANES),
            v_low(2, tokens, LANES),
            v_low(tokens, LANES),
            v_low(own, model),
            dma((4 + 3 * n_ctx,)),
            dma((4,)),
            dma((2, 2, 2)),
            dma((2, 2, 2, n - 1)),
            dma((3,)),
            dma((3,)),
            dma((3,)),
            dma((3,)),
        ],
        compiler_params=pltpu.CompilerParams(
            collective_id=3, has_side_effects=True, vmem_limit_bytes=59 * 1024 * 1024
        ),
        name="scan_backward",
    )(
        px, ps, x, rows_b, rows_c, slope_x, slope_s, lam, step, chain, kept, d_ssd, gate_t, normed_t, upstream, d_z, mixed_parts, hidden, gain_grads, par
    )


def gather_kernel(
    n,
    n_ctx,
    unit,
    taps,
    sizes,
    hidden,
    cotangent,
    in_weight_t,
    small,
    cotangent_all,
    w_x,
    w_s,
    w_z,
    par_out,
    gain_out,
    proj_x,
    proj_s,
    normed_out,
    normed_t,
    v_hidden,
    v_normed,
    v_x,
    v_s,
    own_z,
    v_small,
    raw_x,
    raw_s,
    raw_z,
    out_x,
    out_s,
    out_t,
    v_gain,
    v_par,
    conv_lines,
    gate_line,
    head_lines,
    load_sem,
    shared_sem,
    column_sem,
    local_sem,
    keep_sem,
    store_sem,
    ring_send,
    ring_recv,
    ctx_send,
    ctx_recv,
):
    ring = Ring(n)
    me, shard = ring.me, ring.shard
    width, model = v_x.shape[1], v_x.shape[0]
    inner = width * n_ctx
    r = model // n
    shared = in_weight_t.shape[0] - 2 * inner
    row = me // 2
    other_core = (me + 1 - 2 * (me % 2), shard)
    other_row = (me + 2 - 4 * row, shard)
    barrier = pltpu.get_barrier_semaphore()
    for device in (other_core, other_row, ring.neighbour(0), ring.neighbour(1)):
        pl.semaphore_signal(barrier, inc=1, device_id=device, device_id_type=MESH)

    part = unit * HEAD

    def load_columns(base, target, sems):
        return [
            pltpu.make_async_copy(
                in_weight_t.at[pl.ds(pl.multiple_of(base + (a * n_ctx + me) * part, 16), part)],
                target.at[pl.ds(a * part, part)],
                sems.at[a],
            )
            for a in range(width // part)
        ]

    loads = [
        load_columns(inner, raw_x, column_sem.at[0]),
        [],
        [pltpu.make_async_copy(small, v_small.at[shard], load_sem.at[1])],
        [pltpu.make_async_copy(hidden, v_hidden.at[me], load_sem.at[2])],
        load_columns(0, raw_z, column_sem.at[1]),
    ]
    raw_s[...] = jnp.zeros_like(raw_s)

    def load_shared(wait):
        for j in (0, 1):
            first = me * LANES + j * HEAD

            @pl.when(first < shared)
            def _():
                copy = pltpu.make_async_copy(
                    in_weight_t.at[pl.ds(pl.multiple_of(2 * inner + first, HEAD), HEAD)],
                    raw_s.at[pl.ds(j * HEAD, HEAD)],
                    shared_sem.at[j],
                )
                copy.wait() if wait else copy.start()

    load_shared(False)
    for copies in loads:
        for copy in copies:
            copy.start()

    def loaded(i):
        for copy in loads[i]:
            copy.wait()

    pl.semaphore_wait(barrier, 4)

    half = width // 2
    rows = r // 2
    both_rows = lambda index, way: pl.ds(pl.multiple_of((2 * index + way) * rows, 16), rows)
    x_part = lambda a, sub: lambda index, way: a.at[both_rows(index, way), pl.ds(sub * half, half)]
    s_part = lambda index, way: v_s.at[both_rows(index, way)]
    small_part = lambda index, way: v_small.at[index, pl.ds(way * SMALL_ROWS // 2, SMALL_ROWS // 2)]
    phases = (
        ((0, small_part), (1, s_part), (2, x_part(v_x, 0)), (3, x_part(v_x, 1))),
        ((4, x_part(w_z, 0)), (5, x_part(w_z, 1))),
    )

    def hop(stream, way, step):
        number, part = stream
        place = part(ring.at(-step if way == 0 else step), way)
        return remote(
            place, place, ring_send.at[number, way], ring_recv.at[number, way, step],
            ring.neighbour(way),
        )

    def arrives(stream, way, step):
        number, part = stream
        landed = part(ring.at(-step - 1 if way == 0 else step + 1), way)
        return remote(
            landed, landed, ring_send.at[number, way], ring_recv.at[number, way, step],
            ring.neighbour(way),
        )

    def start_stream(stream):
        for way in (0, 1):
            hop(stream, way, 0).start()

    def to_row(i, a, whole):
        return remote(a, whole.at[me], ctx_send.at[i, 0], ctx_recv.at[i, 0], other_row)

    def to_core(i, a, whole):
        return remote(a, whole.at[me], ctx_send.at[i, 1], ctx_recv.at[i, 1], other_core)

    def pass_on(i, whole):
        beyond = whole.at[other_row[0]]
        return remote(beyond, beyond, ctx_send.at[i, 2], ctx_recv.at[i, 2], other_core)

    to_row(0, hidden, v_hidden).start()
    to_core(0, hidden, v_hidden).start()
    own_rows = pl.ds(pl.multiple_of(shard * r, 16), r)
    loaded(2)
    start_stream(phases[0][0])
    loaded(0)
    v_x[own_rows, :] = raw_x[...].T
    start_stream(phases[0][2])
    start_stream(phases[0][3])
    load_shared(True)
    v_s[own_rows, :] = raw_s[...].T
    start_stream(phases[0][1])
    keep_cotangent = pltpu.make_async_copy(cotangent, cotangent_all.at[me], local_sem)
    keep_cotangent.start()
    keep_shared = pltpu.make_async_copy(out_s, proj_s.at[me], shared_sem.at[2])
    loaded(3)
    loaded(4)
    own_z[...] = raw_z[...].T
    keep_z = pltpu.make_async_copy(own_z, w_z.at[own_rows], keep_sem)
    keep_z.start()
    keep_z.wait()

    def run_phase(number, work, after):
        def body(step, carry):
            for stream in phases[number]:
                for way in (0, 1):
                    arrives(stream, way, step).wait_recv()
                    hop(stream, way, step).wait_send()
                    hop(stream, way, step + 1).start()
            if work is not None:

                @pl.when(step < n_ctx)
                def _():
                    work(step)

                @pl.when(step == n_ctx - 1)
                def _():
                    to_row(2, out_s, proj_s).start()
                    to_core(2, out_s, proj_s).start()
                    keep_shared.start()

            return carry

        lax.fori_loop(0, n - 2, body, 0)
        after()
        for stream in phases[number]:
            for way in (0, 1):
                arrives(stream, way, n - 2).wait_recv()
                hop(stream, way, n - 2).wait_send()

    tokens = v_hidden.shape[1]

    def project_first(chunk):
        at = pl.ds(pl.multiple_of(chunk * tokens, tokens), tokens)
        resid = v_hidden[chunk].astype(F32)
        scale = lax.rsqrt(jnp.mean(resid * resid, axis=1, keepdims=True) + EPS)
        normed = (resid * scale * v_gain[...]).astype(BF16)
        v_normed[at, :] = normed
        out_x[at, :] = mm(normed, v_x[...]).astype(BF16)
        out_s[at, :] = mm(normed, v_s[...]).astype(BF16)
        out_t[chunk] = normed.T

    stores = [
        pltpu.make_async_copy(source, target, store_sem.at[i])
        for i, (source, target) in enumerate(
            (
                (v_x, w_x),
                (v_s, w_s),
                (v_par, par_out),
                (v_gain, gain_out),
                (out_x, proj_x),
                (v_normed, normed_out),
                (out_t, normed_t),
            )
        )
    ]

    def after_first():
        for stream in phases[1]:
            start_stream(stream)
        to_row(0, hidden, v_hidden).wait_recv()
        pass_on(0, v_hidden).start()
        to_row(1, cotangent, cotangent_all).start()
        to_core(1, cotangent, cotangent_all).start()
        to_row(0, hidden, v_hidden).wait_send()
        to_core(0, hidden, v_hidden).wait()
        pass_on(0, v_hidden).wait()

    def after_second():
        to_row(1, cotangent, cotangent_all).wait_recv()
        pass_on(1, cotangent_all).start()
        to_row(2, out_s, proj_s).wait_recv()
        pass_on(2, proj_s).start()
        for copy in stores[4:]:
            copy.start()

    run_phase(0, None, after_first)
    gain_size, conv_size, gate_size, held = sizes
    head_lines[...] = jnp.zeros_like(head_lines)
    for f in range(n):
        v_gain[:, f * r : (f + 1) * r] = v_small[f, 0:1, 0:r].astype(F32)
        conv_lines[0 : taps + 1, f * conv_size : (f + 1) * conv_size] = v_small[
            f, 1 : taps + 2, 0:conv_size
        ].astype(F32)
        gate_line[:, f * gate_size : (f + 1) * gate_size] = v_small[
            f, taps + 2 : taps + 3, 0:gate_size
        ].astype(F32)
        for k in range(3):
            head_lines[k : k + 1, f * held : (f + 1) * held] = v_small[
                f, taps + 3 : taps + 4, k * held : (k + 1) * held
            ].astype(F32)

    def own_part(line, a):
        at = (a * n_ctx + me) * part
        span = max(part, LANES)
        found = line[:, pl.ds(pl.multiple_of(at // LANES * LANES, LANES), span)]
        if part < LANES:
            found = pltpu.roll(found, lax.rem(LANES - at % LANES, LANES), 1)
        return found[:, 0:part]

    v_par[...] = jnp.zeros_like(v_par)
    for a in range(width // part):
        v_par[0 : taps + 1, a * part : (a + 1) * part] = own_part(conv_lines, a)[0 : taps + 1]
        v_par[taps + 1 : taps + 2, a * part : (a + 1) * part] = own_part(gate_line, a)
    v_par[0 : taps + 1, width:] = conv_lines[0 : taps + 1, inner:]
    lines = mm(head_lines[...].astype(BF16), chosen_heads(me, width // HEAD, unit, n_ctx))
    heads_row = taps + 3
    v_par[heads_row : heads_row + 1, 0:LANES] = lines[0:1]
    v_par[heads_row : heads_row + 1, LANES : 2 * LANES] = jnp.exp(lines[1:2])
    wide = (iota2((LANES, width), 1) // HEAD == iota2((LANES, width), 0)).astype(BF16)
    v_par[taps + 2 : taps + 3, 0:width] = mm(lines.astype(BF16), wide)[2:3]
    for copy in stores[0:4]:
        copy.start()
    run_phase(1, project_first, after_second)
    to_row(1, cotangent, cotangent_all).wait_send()
    to_core(1, cotangent, cotangent_all).wait()
    pass_on(1, cotangent_all).wait()
    keep_cotangent.wait()
    to_row(2, out_s, proj_s).wait_send()
    to_core(2, out_s, proj_s).wait()
    pass_on(2, proj_s).wait()
    keep_shared.wait()
    for copy in stores:
        copy.wait()


def gather_all(n, n_ctx, unit, taps, sizes, width, hidden, cotangent, in_weight_t, small):
    own, model = hidden.shape
    tokens = own * n_ctx
    rows = in_weight_t.shape[1]
    any_space = pl.BlockSpec(memory_space=pl.ANY)
    par_shape = (taps + 4, width + 2 * STATE)
    inner = width * n_ctx
    low = lambda *shape: jax.ShapeDtypeStruct(shape, BF16)
    v_low = lambda *shape: pltpu.VMEM(shape, BF16)
    dma = pltpu.SemaphoreType.DMA
    return pl.pallas_call(
        functools.partial(gather_kernel, n, n_ctx, unit, taps, sizes),
        in_specs=[any_space] * 4,
        out_specs=[any_space] * 10,
        out_shape=[
            low(n_ctx, own, model),
            low(model, width),
            low(model, LANES),
            low(model, width),
            jax.ShapeDtypeStruct(par_shape, F32),
            jax.ShapeDtypeStruct((1, model), F32),
            low(tokens, width),
            low(n_ctx, tokens, LANES),
            low(tokens, model),
            low(n_ctx, model, own),
        ],
        scratch_shapes=[
            v_low(n_ctx, own, model),
            v_low(tokens, model),
            v_low(model, width),
            v_low(model, LANES),
            v_low(rows, width),
            v_low(n, small.shape[0], small.shape[1]),
            v_low(width, rows),
            v_low(LANES, rows),
            v_low(width, rows),
            v_low(tokens, width),
            v_low(tokens, LANES),
            v_low(n_ctx, model, own),
            pltpu.VMEM((1, model), F32),
            pltpu.VMEM(par_shape, F32),
            pltpu.VMEM((8, inner + 2 * STATE), F32),
            pltpu.VMEM((1, inner), F32),
            pltpu.VMEM((8, LANES), F32),
            dma((3,)),
            dma((3,)),
            dma((2, width // (unit * HEAD))),
            dma,
            dma,
            dma((7,)),
            dma((6, 2)),
            dma((6, 2, n - 1)),
            dma((3, 3)),
            dma((3, 3)),
        ],
        compiler_params=pltpu.CompilerParams(
            collective_id=0, has_side_effects=True, vmem_limit_bytes=56 * 1024 * 1024
        ),
        name="gather_all",
    )(hidden, cotangent, in_weight_t, small)


def reduce_kernel(
    n,
    n_ctx,
    direct,
    normed_t,
    d_z,
    d_x,
    d_s,
    w_z,
    w_x,
    w_s,
    shard_o,
    shard_z,
    small,
    hidden,
    cotangent,
    gain,
    g_z,
    g_x,
    g_s,
    g_o,
    hidden_grad,
    small_out,
    norm_out,
    v_normed_t,
    v_d_z,
    v_d_x,
    v_d_s,
    v_z,
    v_x,
    v_s,
    parts,
    partials,
    slots,
    stage,
    done,
    moved,
    from_core,
    from_row,
    v_hidden,
    v_cotangent,
    v_gain,
    small_all,
    small_ctx,
    norm_all,
    norm_ctx,
    load_sem,
    store_sem,
    ring_send,
    ring_recv,
    ctx_send,
    ctx_recv,
    own_sem,
    piece_send,
    piece_recv,
    part_send,
    part_recv,
    small_send,
    small_recv,
    small_ctx_send,
    small_ctx_recv,
):
    ring = Ring(n)
    me, shard = ring.me, ring.shard
    around = Around(me, shard)
    core, row = me % 2, me // 2
    piece_peer = (shard % n_ctx, shard // n_ctx * n_ctx + me)
    moves = shard % n_ctx != me
    barrier = pltpu.get_barrier_semaphore()
    for device in around.all:
        greet(device)
    lax.fori_loop(1, n, lambda j, carry: (greet((me, lax.rem(shard + j, n))), carry)[1], 0)
    own = hidden.shape[0]
    sum_normed = TokenSum(
        around, parts, parts.at[me], parts.at[around.row_at], from_core, from_row, part_send, part_recv
    )
    sum_small, sum_norm = (
        SmallSum(
            n, around, whole, sums, small_send.at[i], small_recv.at[i], small_ctx_send.at[i], small_ctx_recv.at[i]
        )
        for i, (whole, sums) in enumerate(((small_all, small_ctx), (norm_all, norm_ctx)))
    )
    loads = [
        pltpu.make_async_copy(source, target, load_sem.at[i])
        for i, (source, target) in enumerate(
            (
                *((normed_t.at[c], v_normed_t.at[:, pl.ds(c * own, own)]) for c in range(n_ctx)),
                (d_s, v_d_s),
                (d_x, v_d_x),
                (small, small_all.at[shard]),
                (d_z, v_d_z),
                (w_z, v_z),
                (w_x, v_x),
                (w_s, v_s),
                (hidden, v_hidden),
                (cotangent, v_cotangent),
                (gain, v_gain),
            )
        )
    ]
    ring_loads = n_ctx + 2
    for copy in loads:
        copy.start()
    if direct:
        pl.semaphore_wait(barrier, n + 2)
    else:

        @pl.when(moves)
        def _():
            greet(piece_peer)
            pl.semaphore_wait(barrier, n + 3)

        @pl.when(jnp.logical_not(moves))
        def _():
            pl.semaphore_wait(barrier, n + 2)

    rows = v_normed_t.shape[0] // (2 * n)
    half, last = v_d_x.shape[1] // 2, v_d_s.shape[1]
    streams = (
        (0, v_d_s, 0, last, 2 * half),
        (1, v_d_x, 0, half, 0),
        (2, v_d_x, half, half, half),
    )

    def compute_partials(step):
        for way in (0, 1):
            index = ring.at(-step - 2 if way == 0 else step + 2)
            left = v_normed_t[pl.ds(pl.multiple_of((2 * index + way) * rows, 16), rows), :]
            partials[way, :, 2 * half :] = mm(left, v_d_s[...])
            partials[way, :, 0 : 2 * half] = mm(left, v_d_x[...])

    def slot(stream, way, step):
        return slots.at[step, way, :, pl.ds(stream[4], stream[3])]

    def hop(stream, way, step, source):
        return remote(
            source,
            slot(stream, way, step),
            ring_send.at[stream[0], way],
            ring_recv.at[stream[0], way, step],
            ring.neighbour(way),
        )

    def first_part(stream, way):
        return stage.at[way, :, pl.ds(stream[4], stream[3])]

    def arrived(stream, way, step):
        hop(stream, way, step, first_part(stream, way)).wait()
        partial = partials[way, :, stream[4] : stream[4] + stream[3]]
        return slot(stream, way, step)[...].astype(F32) + partial

    done_of = lambda stream: done.at[pl.ds(stream[4], stream[3])]
    of_x = lambda c, first: g_x.at[c, pl.ds(first, half)]
    shares = (
        (shard_o if direct else moved, lambda c: g_o.at[c]),
        (shard_z, lambda c: g_z.at[c]),
        (done_of(streams[1]), lambda c: of_x(c, 0)),
        (done_of(streams[2]), lambda c: of_x(c, half)),
        (done_of(streams[0]), lambda c: g_s.at[c]),
    )

    def share(i, kind):
        source, whole = shares[i]
        at = me
        if kind == 2:
            source, at = whole(around.row_at), around.row_at
        device = around.row if kind == 0 else around.core
        return remote(source, whole(at), ctx_send.at[i, kind], ctx_recv.at[i, kind], device)

    def keep(i):
        return pltpu.make_async_copy(shares[i][0], shares[i][1](me), own_sem.at[i])

    def start_share(i):
        share(i, 0).start()
        share(i, 1).start()
        keep(i).start()

    def pass_share(i):
        share(i, 0).wait_recv()
        share(i, 2).start()

    def close_share(i):
        share(i, 0).wait_send()
        share(i, 1).wait()
        share(i, 2).wait()
        keep(i).wait()

    def move_piece(wait):
        if direct:
            return
        keep_piece = pltpu.make_async_copy(shard_o, moved, piece_send)
        send_piece = remote(shard_o, moved, piece_send, piece_recv, piece_peer)

        @pl.when(moves)
        def _():
            send_piece.wait() if wait else send_piece.start()

        @pl.when(jnp.logical_not(moves))
        def _():
            keep_piece.wait() if wait else keep_piece.start()

    def normed_part(i, carry):
        to_row = row + (1 - i % 2) * (1 - 2 * row)
        to_core = core + (1 - i // 2) * (1 - 2 * core)
        at = 2 * to_row + to_core
        tokens = pl.ds(pl.multiple_of(at * own, own), own)
        parts[at] = (
            mm(v_d_z[tokens, :], v_z[...], ((1,), (1,)))
            + mm(v_d_x[tokens, :], v_x[...], ((1,), (1,)))
            + mm(v_d_s[tokens, :], v_s[...], ((1,), (1,)))
        ).astype(BF16)
        return carry

    store_grad = pltpu.make_async_copy(v_cotangent, hidden_grad, store_sem.at[0])
    store_small = pltpu.make_async_copy(small_ctx, small_out, store_sem.at[1])
    store_norm = pltpu.make_async_copy(norm_ctx, norm_out, store_sem.at[2])

    def finish_tokens():
        resid = v_hidden[...].astype(F32)
        scale = lax.rsqrt(jnp.mean(resid * resid, axis=1, keepdims=True) + EPS)
        d_normed = sum_normed.total()
        f = v_gain[...] * d_normed
        slope = scale**3 * jnp.mean(resid * f, axis=1, keepdims=True)
        grad = v_cotangent[...].astype(F32) + scale * f - resid * slope
        v_cotangent[...] = grad.astype(BF16)
        store_grad.start()
        by_model = jnp.sum(d_normed * resid * scale, axis=0, keepdims=True)
        size = norm_all.shape[2]
        for j in range(norm_all.shape[1]):
            norm_all[shard, j : j + 1, :] = by_model[:, j * size : (j + 1) * size]
        sum_norm.start()

    move_piece(False)
    for copy in loads[:ring_loads]:
        copy.wait()
    compute_partials(-1)
    for way in (0, 1):
        stage[way] = partials[way].astype(BF16)
        for stream in streams:
            hop(stream, way, 0, first_part(stream, way)).start()
    compute_partials(0)
    for copy in loads[ring_loads:]:
        copy.wait()
    sum_small.start()
    move_piece(True)
    start_share(0)
    start_share(1)

    def body(step, carry):
        for stream in streams:
            for way in (0, 1):
                total = arrived(stream, way, step)
                place = slot(stream, way, step)
                place[...] = total.astype(BF16)
                hop(stream, way, step + 1, place).start()
        compute_partials(step + 1)

        @pl.when(step < 2)
        def _():
            lax.fori_loop(2 * step, 2 * step + 2, normed_part, 0)

        @pl.when(step == 0)
        def _():
            sum_normed.start()

        @pl.when(step == 1)
        def _():
            sum_normed.pass_row()

        @pl.when(step == n - 3)
        def _():
            finish_tokens()

        return carry

    lax.fori_loop(0, n - 2, body, 0)
    sum_small.add()
    pass_share(0)
    pass_share(1)
    for number, shared in ((0, 4), (1, 2), (2, 3)):
        place = done_of(streams[number])
        for way in (0, 1):
            total = arrived(streams[number], way, n - 2)
            place[:, way * rows : (way + 1) * rows] = total.T.astype(BF16)
        start_share(shared)
    sum_norm.add()
    sum_small.finish()
    store_small.start()
    for i in (4, 2, 3):
        pass_share(i)
    sum_norm.finish()
    store_norm.start()
    for i in range(5):
        close_share(i)
    store_grad.wait()
    store_small.wait()
    store_norm.wait()


def reduce_all(
    n, n_ctx, direct, normed_t, d_z, d_x, d_s, w_z, w_x, w_s, shard_o, shard_z, small, hidden, cotangent, gain
):
    model, tokens = normed_t.shape[1], d_x.shape[0]
    width, shared_width = d_x.shape[1], d_s.shape[1]
    rows, piece, own = model // n, width // n, hidden.shape[0]
    columns = width + shared_width
    any_space = pl.BlockSpec(memory_space=pl.ANY)
    dma = pltpu.SemaphoreType.DMA
    low = lambda *shape: jax.ShapeDtypeStruct(shape, BF16)
    v_low = lambda *shape: pltpu.VMEM(shape, BF16)
    v_full = lambda *shape: pltpu.VMEM(shape, F32)
    norm_shape = (8, model // 8)
    return pl.pallas_call(
        functools.partial(reduce_kernel, n, n_ctx, direct),
        in_specs=[any_space] * 13,
        out_specs=[any_space] * 7,
        out_shape=[
            low(n_ctx, 2, width, rows // 2),
            low(n_ctx, width, rows),
            low(n_ctx, shared_width, rows),
            low(n_ctx, piece, model),
            low(own, model),
            jax.ShapeDtypeStruct((n_ctx,) + small.shape, F32),
            jax.ShapeDtypeStruct((n_ctx,) + norm_shape, F32),
        ],
        scratch_shapes=[
            v_low(model, tokens),
            v_low(tokens, width),
            v_low(tokens, width),
            v_low(tokens, shared_width),
            v_low(*w_z.shape),
            v_low(*w_x.shape),
            v_low(*w_s.shape),
            v_low(n_ctx, own, model),
            v_full(2, rows // 2, columns),
            v_low(n - 1, 2, rows // 2, columns),
            v_low(2, rows // 2, columns),
            v_low(columns, rows),
            v_low(piece, model),
            v_low(2, own, model),
            v_low(own, model),
            v_low(own, model),
            v_low(own, model),
            v_full(1, model),
            v_full(n, *small.shape),
            v_full(n_ctx, *small.shape),
            v_full(n, *norm_shape),
            v_full(n_ctx, *norm_shape),
            dma((10 + n_ctx,)),
            dma((3,)),
            dma((3, 2)),
            dma((3, 2, n - 1)),
            dma((5, 3)),
            dma((5, 3)),
            dma((5,)),
            dma,
            dma,
            dma((3,)),
            dma((3,)),
            dma((2, n - 1)),
            dma((2, n - 1)),
            dma((2, 3)),
            dma((2, 3)),
        ],
        compiler_params=pltpu.CompilerParams(
            collective_id=1, has_side_effects=True, vmem_limit_bytes=58 * 1024 * 1024
        ),
        name="reduce_all",
    )(
        normed_t, d_z, d_x, d_s, w_z, w_x, w_s, shard_o, shard_z, small, hidden, cotangent, gain
    )


def assemble_kernel(part, z_ref, x_ref, s_ref, o_ref, out_ref, rows_ref):
    place = pl.program_id(0)
    n_ctx, size, half = x_ref.shape[0], x_ref.shape[1], z_ref.shape[3]

    def interleave(write):
        for a in range(size // part):
            for c in range(n_ctx):
                write(
                    slice((a * n_ctx + c) * part, (a * n_ctx + c + 1) * part),
                    c,
                    slice(a * part, (a + 1) * part),
                )

    def write_z(target, c, source):
        for way in (0, 1):
            out_ref[target, way * half : (way + 1) * half] = z_ref[c, way, source, :].astype(F32)

    def write_x(target, c, source):
        out_ref[target, :] = x_ref[c, source, :].astype(F32)

    @pl.when(place < n_ctx)
    def _():
        interleave(write_z)

    @pl.when(jnp.logical_and(place >= n_ctx, place < 2 * n_ctx))
    def _():
        interleave(write_x)

    @pl.when(place == 2 * n_ctx)
    def _():
        for c in range(s_ref.shape[0]):
            out_ref[c * LANES : (c + 1) * LANES, :] = s_ref[c].astype(F32)

    @pl.when(place < 2 * n_ctx)
    def _():
        rows_ref[...] = o_ref[...].astype(F32)


def assemble(part, g_z, g_x, g_s, g_o, columns):
    n_ctx, width, rows = g_x.shape
    block = (n_ctx, width // n_ctx, rows)
    g_o = g_o.reshape(-1, g_o.shape[2])
    tile = max(g_o.shape[0] // (2 * n_ctx), 16)
    at_tile = lambda i: (jnp.minimum(i, g_o.shape[0] // tile - 1), 0)
    return pl.pallas_call(
        functools.partial(assemble_kernel, part),
        grid=(2 * n_ctx + 1,),
        in_specs=[
            pl.BlockSpec(
                (n_ctx, 2, width // n_ctx, rows // 2),
                lambda i: (0, 0, jnp.minimum(i, n_ctx - 1), 0),
            ),
            pl.BlockSpec(block, lambda i: (0, jnp.clip(i - n_ctx, 0, n_ctx - 1), 0)),
            pl.BlockSpec(g_s.shape, lambda i: (0, 0, 0)),
            pl.BlockSpec((tile, g_o.shape[1]), at_tile),
        ],
        out_specs=[
            pl.BlockSpec((width, rows), lambda i: (i, 0)),
            pl.BlockSpec((tile, g_o.shape[1]), at_tile),
        ],
        out_shape=[
            jax.ShapeDtypeStruct((columns, rows), F32),
            jax.ShapeDtypeStruct(g_o.shape, F32),
        ],
        compiler_params=pltpu.CompilerParams(vmem_limit_bytes=58 * 1024 * 1024),
        name="assemble",
    )(g_z, g_x, g_s, g_o)


def on_device(
    hidden,
    cotangent,
    seq_lens,
    norm_gain,
    in_weight,
    conv_weight,
    conv_bias,
    dt_bias,
    a_log,
    d_skip,
    gate_gain,
    out_weight,
):
    n_ctx, n_fsdp = lax.axis_size("ctx"), lax.axis_size("fsdp")
    me, shard = lax.axis_index("ctx"), lax.axis_index("fsdp")
    taps = conv_weight.shape[0]
    heads_all = dt_bias.shape[0] * n_fsdp
    inner = out_weight.shape[0] * n_fsdp
    heads, width = heads_all // n_ctx, inner // n_ctx
    model = hidden.shape[2]
    both = 2 * STATE
    held = dt_bias.shape[0]
    direct = held % n_ctx == 0
    unit = held // n_ctx if direct else 1
    part = unit * HEAD
    assert both + heads_all <= n_ctx * LANES and heads_all == HEAD

    per_head = jnp.concatenate([dt_bias, a_log, d_skip])
    lines = [norm_gain[None], conv_weight, conv_bias[None], gate_gain[None], per_head[None]]
    longest = -(-max(a.shape[1] for a in lines) // LANES) * LANES
    small = jnp.concatenate([jnp.pad(a, ((0, 0), (0, longest - a.shape[1]))) for a in lines])
    small = jnp.pad(small, ((0, SMALL_ROWS - small.shape[0]), (0, 0)))
    sizes = (norm_gain.shape[0], conv_bias.shape[0], gate_gain.shape[0], held)
    upstream, w_x, w_s, w_z, par, gain_norm, proj_x, proj_s, normed, normed_t = gather_all(
        n_fsdp, n_ctx, unit, taps, sizes, width, hidden[0], cotangent[0], in_weight.T, small
    )
    *kept_parts, gain_grads, gate_t, mixed_parts, d_z, d_ssd = scan_forward(
        n_fsdp, direct, unit, n_ctx, seq_lens, proj_x, proj_s, normed, out_weight, w_z, upstream, par
    )
    d_x, small_grads, d_s, shard_o, shard_z, layer_out = scan_backward(
        n_fsdp, unit, n_ctx, proj_x, proj_s, kept_parts, d_ssd, gate_t, normed_t, upstream, d_z, mixed_parts, hidden[0], gain_grads, par
    )
    g_z, g_x, g_s, g_o, hidden_grad, sums, norm_sums = reduce_all(
        n_fsdp, n_ctx, direct, normed_t, d_z, d_x, d_s, w_z, w_x, w_s, shard_o, shard_z, small_grads, hidden[0], cotangent[0], gain_norm
    )
    grad_in_weight, grad_out_weight = assemble(
        part, g_z, g_x, g_s, g_o, 2 * inner + both + heads_all
    )

    def shard_of(lines):
        size = lines.shape[1] // n_fsdp
        return lax.dynamic_slice_in_dim(lines, shard * size, size, axis=1)

    def in_order(sums_of, size):
        lines = sums_of.shape[1]
        by_part = sums_of.reshape(n_ctx, lines, -1, size)
        return jnp.transpose(by_part, (1, 2, 0, 3)).reshape(lines, -1)

    conv_sums = shard_of(
        jnp.concatenate(
            [
                in_order(sums[:, : taps + 1, :width], part),
                jnp.sum(sums[:, : taps + 1, width:], axis=0),
            ],
            axis=1,
        )
    )
    gate_sums = shard_of(in_order(sums[:, taps + 1 : taps + 2, :width], part))
    head_sums_all = sums[:, taps + 2, : 3 * LANES].reshape(n_ctx, 3, LANES)[:, :, :heads]
    head_grads = shard_of(in_order(head_sums_all, unit))
    norm_sums = jnp.sum(norm_sums, axis=0).reshape(1, -1)
    return (
        layer_out[None],
        hidden_grad[None],
        shard_of(norm_sums)[0],
        grad_in_weight.T,
        conv_sums[:taps],
        conv_sums[taps],
        head_grads[0],
        head_grads[1],
        head_grads[2],
        gate_sums[0],
        grad_out_weight,
    )


def solution(mesh):
    tokens, rows, flat = P("fsdp", "ctx", None), P("fsdp", None), P("fsdp")
    taps = P(None, "fsdp")
    return jax.shard_map(
        on_device,
        mesh=mesh,
        in_specs=(tokens, tokens, flat, flat, rows, taps, flat, flat, flat, flat, flat, rows),
        out_specs=(tokens, tokens, flat, rows, taps, flat, flat, flat, flat, flat, rows),
        check_vma=False,
    )
```

```python
import functools

import jax
import jax.numpy as jnp
from jax import lax
from jax.experimental import pallas as pl
from jax.experimental.pallas import tpu as pltpu
from jax.sharding import PartitionSpec as P

HEAD = 64
STATE = 128
BLOCK = 256
LANES = 128
POINTS = 8
EPS = 1e-05
F32 = jnp.float32
BF16 = jnp.bfloat16


def mm(a, b, contract=((1,), (0,))):
    return lax.dot_general(a, b, (contract, ((), ())), preferred_element_type=F32)


def mm_exact(a, b, contract=((1,), (0,))):
    return lax.dot_general(
        a, b, (contract, ((), ())), precision=lax.Precision.HIGHEST, preferred_element_type=F32
    )


def iota2(shape, axis):
    return lax.broadcasted_iota(jnp.int32, shape, axis)


def levels(lam, step):
    tri = (iota2((BLOCK, BLOCK), 0) >= iota2((BLOCK, BLOCK), 1)).astype(F32)
    level = mm_exact(tri, lam)
    across = level.T
    last = level[BLOCK - 1 : BLOCK, :]
    weight = jnp.exp(level - last) * step
    return level, across, jnp.exp(-last), weight, jnp.exp(-level)


def pair_of(array, first, low_half):
    return jnp.where(low_half, array[:, first : first + 1], array[:, first + 1 : first + 2])


def spread(level, across, head):
    return jnp.exp(-jnp.abs(level[:, head : head + 1] - across[head : head + 1, :]))


def silu_and_slope(v):
    s = jax.nn.sigmoid(v)
    return v * s, s * (1.0 + v * (1.0 - s))


def chosen_heads(me, heads, unit, n_ctx, turned=False):
    here, there = iota2((LANES, LANES), 1), iota2((LANES, LANES), 0)
    if turned:
        here, there = there, here
    head = (here // unit * n_ctx + me) * unit + here % unit
    return jnp.where(jnp.logical_and(there == head, here < heads), 1.0, 0.0).astype(BF16)


class Lines:
    def __init__(self, ref, first, rows, at, size):
        self.ref, self.first, self.at, self.shape = ref, first, at, (rows, size)

    def __getitem__(self, index):
        rows = slice(self.first, self.first + self.shape[0])
        lanes = slice(0, self.shape[1]) if index is Ellipsis else index[1]
        return self.ref[rows, self.at + lanes.start : self.at + lanes.stop]


def parameters(par_ref, width):
    lines = par_ref.shape[0] - 3
    head = par_ref[lines + 2 : lines + 3, 0 : 2 * LANES]
    return (
        Lines(par_ref, 0, lines, 0, width),
        Lines(par_ref, 0, lines, width, 2 * STATE),
        Lines(par_ref, lines, 1, 0, width),
        Lines(par_ref, lines + 1, 1, 0, width),
        head[:, :LANES],
        head[:, LANES:],
    )


def column_valid(length_ref, block):
    at = iota2((BLOCK, 1), 0) + block * BLOCK
    return (at < length_ref[0]).astype(F32)


MESH = pl.DeviceIdType.MESH
SMALL_ROWS = 32


def ring_place(index, half):
    a, b = index // 2, index % 2
    return a + b * (2 * half - 1 - 2 * a)


def ring_index(place, half):
    b = place // half
    return 2 * (place + b * (2 * half - 1 - 2 * place)) + b


class Ring:
    def __init__(self, n):
        self.n, self.half = n, n // 2
        self.me, self.shard = lax.axis_index("ctx"), lax.axis_index("fsdp")
        self.place = ring_place(self.shard, self.half)

    def at(self, steps):
        return ring_index(lax.rem(self.place + steps + 2 * self.n, self.n), self.half)

    def neighbour(self, way):
        return (self.me, self.at(1 if way == 0 else -1))


def remote(source, target, send, recv, device):
    return pltpu.make_async_remote_copy(
        src_ref=source,
        dst_ref=target,
        send_sem=send,
        recv_sem=recv,
        device_id=device,
        device_id_type=MESH,
    )


def greet(device):
    pl.semaphore_signal(pltpu.get_barrier_semaphore(), inc=1, device_id=device, device_id_type=MESH)


class Around:
    def __init__(self, me, shard):
        core, row = me % 2, me // 2
        self.me = me
        self.core_at = me + 1 - 2 * core
        self.row_at = me + 2 - 4 * row
        self.both_at = self.row_at + 1 - 2 * core
        self.core, self.row, self.both = (
            (at, shard) for at in (self.core_at, self.row_at, self.both_at)
        )
        self.all = (self.core, self.row, self.both)


class TokenSum:
    def __init__(self, around, parts, own_part, row_part, from_core, from_row, send, recv):
        self.around, self.parts, self.own_part, self.row_part = around, parts, own_part, row_part
        self.from_core, self.from_row, self.send, self.recv = from_core, from_row, send, recv

    def loads(self):
        at = self.around
        return (
            (self.parts.at[at.row_at], self.row_part),
            (self.parts.at[at.me], self.own_part),
        )

    def to_core(self, which):
        at = self.around
        return remote(
            self.parts.at[(at.core_at, at.both_at)[which]],
            self.from_core.at[which],
            self.send.at[which],
            self.recv.at[which],
            at.core,
        )

    def to_row(self):
        return remote(
            self.row_part, self.from_row, self.send.at[2], self.recv.at[2], self.around.row
        )

    def start(self):
        self.to_core(1).start()
        self.to_core(0).start()

    def pass_row(self):
        self.to_core(1).wait()
        total = self.row_part[...].astype(F32) + self.from_core[1].astype(F32)
        self.row_part[...] = total.astype(BF16)
        self.to_row().start()

    def total(self):
        self.to_core(0).wait()
        self.to_row().wait()
        return (
            self.own_part[...].astype(F32)
            + self.from_core[0].astype(F32)
            + self.from_row[...].astype(F32)
        )


class SmallSum:
    def __init__(self, n, around, whole, sums, send, recv, ctx_send, ctx_recv):
        self.n, self.around, self.whole, self.sums = n, around, whole, sums
        self.send, self.recv, self.ctx_send, self.ctx_recv = send, recv, ctx_send, ctx_recv
        self.shard = lax.axis_index("fsdp")

    def to_peer(self, offset):
        own = self.whole.at[self.shard]
        peer = (self.around.me, lax.rem(self.shard + offset, self.n))
        return remote(own, own, self.send.at[offset - 1], self.recv.at[offset - 1], peer)

    def to_ctx(self, i):
        own = self.sums.at[self.around.me]
        return remote(own, own, self.ctx_send.at[i], self.ctx_recv.at[i], self.around.all[i])

    def start(self):
        lax.fori_loop(1, self.n, lambda j, carry: (self.to_peer(j).start(), carry)[1], 0)

    def add(self):
        lax.fori_loop(1, self.n, lambda j, carry: (self.to_peer(j).wait(), carry)[1], 0)
        self.sums[self.around.me] = jnp.sum(self.whole[...], axis=0)
        for i in range(3):
            self.to_ctx(i).start()

    def finish(self):
        for i in range(3):
            self.to_ctx(i).wait()


def forward_kernel(
    heads,
    unit,
    n_ctx,
    n,
    direct,
    length_ref,
    px_ref,
    ps_ref,
    normed_ref,
    out_weight,
    w_z,
    upstream,
    par_ref,
    x_ref,
    b_ref,
    c_ref,
    slope_x_ref,
    slope_s_ref,
    lam_ref,
    step_ref,
    chain_ref,
    kept_ref,
    gain_ref,
    gate_t,
    mixed_parts,
    d_z,
    d_ssd,
    state,
    before_x,
    before_s,
    v_o,
    v_z,
    v_up,
    all_y,
    all_z,
    all_dyn,
    all_g,
    v_yt,
    v_mixed,
    v_dz,
    v_dssd,
    stat_all,
    columns,
    load_sem,
    store_sem,
    ring_send,
    ring_recv,
    piece_recv,
    stat_send,
    stat_recv,
):
    block = pl.program_id(0)
    blocks = pl.num_programs(0)
    ring = Ring(n)
    me, shard = ring.me, ring.shard
    around = Around(me, shard)
    width = px_ref.shape[1]
    taps_x_ref, taps_s_ref, gate_gain_ref, skip_ref, bias_step, rate = parameters(par_ref, width)
    channels = width * n_ctx
    piece, size = v_o.shape[0] // n, v_o.shape[1] // 4
    points = heads // 2 * n_ctx
    loads = [
        pltpu.make_async_copy(source, target, load_sem.at[i])
        for i, (source, target) in enumerate(((w_z, v_z), (upstream, v_up)))
    ]
    shard_rows = lambda index: pl.ds(pl.multiple_of(index * piece, 16), piece)
    own_piece = out_weight.at[pl.ds(pl.multiple_of(me * piece, 16), piece)]
    piece_peer = (shard % n_ctx, shard // n_ctx * n_ctx + me)
    moves = shard % n_ctx != me

    def hop(way, sub, step):
        at = pl.multiple_of((2 * way + sub) * size, LANES)
        place = v_o.at[shard_rows(ring.at(step * (2 * way - 1))), pl.ds(at, size)]
        return remote(
            place,
            place,
            ring_send.at[way, sub],
            ring_recv.at[way, sub, step],
            (me, ring.at(1 - 2 * way)),
        )

    def streams(body):
        lax.fori_loop(0, 4, lambda e, carry: (body(e // 2, e % 2), carry)[1], 0)

    def ring_step(step):
        def body(way, sub):
            hop(way, sub, step).wait()

            @pl.when(step < n - 2)
            def _():
                hop(way, sub, step + 1).start()

        streams(body)

    def serve(point):
        at = block * (heads // 2) + point
        lax.fori_loop(
            at * (n - 1) // points,
            (at + 1) * (n - 1) // points,
            lambda step, carry: (ring_step(step), carry)[1],
            0,
        )

    @pl.when(block == 0)
    def _():
        for device in around.all:
            greet(device)
        greet(ring.neighbour(0))
        greet(ring.neighbour(1))
        keep = pltpu.make_async_copy(own_piece, v_o.at[shard_rows(shard)], load_sem.at[2])
        if direct:
            keep.start()
            pl.semaphore_wait(pltpu.get_barrier_semaphore(), 5)
            keep.wait()
        else:
            send = remote(
                own_piece, v_o.at[shard_rows(piece_peer[1])], load_sem.at[2], piece_recv, piece_peer
            )

            @pl.when(moves)
            def _():
                greet(piece_peer)
                pl.semaphore_wait(pltpu.get_barrier_semaphore(), 6)
                send.start()
                send.wait()

            @pl.when(jnp.logical_not(moves))
            def _():
                pl.semaphore_wait(pltpu.get_barrier_semaphore(), 5)
                keep.start()
                keep.wait()

        streams(lambda way, sub: hop(way, sub, 0).start())
        for copy in loads:
            copy.start()
        state[...] = jnp.zeros_like(state)
        before_x[...] = jnp.zeros_like(before_x)
        before_s[...] = jnp.zeros_like(before_s)

    valid = column_valid(length_ref, block)
    low_half = iota2((1, LANES), 1) < HEAD
    taps = taps_x_ref.shape[0] - 1

    def conv(current, before, weight):
        padded = jnp.concatenate([before, current], axis=0)
        total = weight[taps : taps + 1]
        for k in range(taps):
            first = 8 - (taps - 1) + k
            total = total + weight[k : k + 1] * padded[first : first + BLOCK]
        return silu_and_slope(total)

    both = jnp.concatenate([ps_ref[0], ps_ref[1]], axis=1).astype(F32)
    active, slope = conv(both, before_s[...], taps_s_ref[...])
    before_s[...] = both[BLOCK - 8 :]
    slope_s_ref[...] = slope.astype(BF16)
    rows_b, rows_c = active[:, :STATE].astype(BF16), active[:, STATE:].astype(BF16)
    b_ref[...] = rows_b
    c_ref[...] = rows_c
    raw = mm(ps_ref[2], chosen_heads(me, heads, unit, n_ctx)) + bias_step
    own = iota2((1, LANES), 1) < heads
    step = jnp.where(own, valid * jax.nn.softplus(raw), 0.0)
    lam = step * rate
    step_ref[...] = step
    lam_ref[...] = lam
    chain_ref[...] = jnp.where(own, valid * jax.nn.sigmoid(raw), 0.0)

    gram = mm(rows_c, rows_b, ((1,), (1,)))
    level, across, last, weight, fade = levels(lam, step)
    kept_ref[0] = state[...].astype(BF16)
    entering = mm(rows_c, state[...].astype(BF16))
    by_state = rows_b.T
    for first in range(0, heads, 2):
        lanes = slice(first * HEAD, (first + 2) * HEAD)
        current = px_ref[:, lanes].astype(F32)
        active, slope = conv(current, before_x[:, lanes], taps_x_ref[:, lanes])
        before_x[:, lanes] = current[BLOCK - 8 :]
        slope_x_ref[:, lanes] = slope.astype(BF16)
        x_low = active.astype(BF16)
        x_ref[:, lanes] = x_low
        x = x_low.astype(F32)
        scaled = x * pair_of(step, first, low_half)
        total = pair_of(fade, first, low_half) * entering[:, lanes] + skip_ref[:, lanes] * x
        for head, keep in ((first, low_half), (first + 1, jnp.logical_not(low_half))):
            mixing = (gram * spread(level, across, head)).astype(BF16)
            total += mm(mixing, jnp.where(keep, scaled, 0.0).astype(BF16))
        all_y[block, :, lanes] = total
        update = mm(by_state, (x * pair_of(weight, first, low_half)).astype(BF16))
        state[:, lanes] = state[:, lanes] * pair_of(last, first, low_half) + update
        if first + 2 < heads:
            serve(first // 2)

    @pl.when(block == 0)
    def _():
        loads[0].wait()

    all_z[block] = mm(normed_ref[...], v_z[...]).astype(BF16)
    serve(heads // 2 - 1)

    @pl.when(block == blocks - 1)
    def _():
        loads[1].wait()
        lane = iota2((1, LANES), 1)

        def sums_of(chunk, carry):
            d_yn = column_valid(length_ref, chunk) * mm(v_up[chunk], v_o[...], ((1,), (1,)))
            all_dyn[chunk] = d_yn
            gated = all_y[chunk] * jax.nn.silu(all_z[chunk].astype(F32))
            square = jnp.sum(gated * gated, axis=1, keepdims=True)
            weighted = gate_gain_ref[...] * gated
            all_g[chunk] = weighted.astype(BF16)
            along = jnp.sum(weighted * d_yn, axis=1, keepdims=True)
            pair = jnp.where(lane == 0, square, 0.0) + jnp.where(lane == 1, along, 0.0)
            stat_all[me, chunk] = pair.T[0:8]
            return carry

        lax.fori_loop(0, blocks, sums_of, 0)
        own_stats = stat_all.at[me]
        copies = [
            remote(own_stats, own_stats, stat_send.at[i], stat_recv.at[i], device)
            for i, device in enumerate(around.all)
        ]
        for copy in copies:
            copy.start()
        gain_ref[...] = jnp.zeros_like(gain_ref)

        def store_mixed(chunk):
            slot = chunk % 2
            return pltpu.make_async_copy(
                v_mixed.at[slot], mixed_parts.at[chunk], store_sem.at[slot, 3]
            )

        def mixed_of(chunk, carry):
            @pl.when(chunk >= 2)
            def _():
                store_mixed(chunk - 2).wait()

            v_mixed[chunk % 2] = mm(all_g[chunk], v_o[...]).astype(BF16)
            store_mixed(chunk).start()
            return carry

        lax.fori_loop(0, blocks, mixed_of, 0)
        for copy in copies:
            copy.wait()
        total = jnp.sum(stat_all[...], axis=0)
        for i in range(n_ctx):
            columns[i] = total[i].T
        own_total = sum(stat_all[c, me] for c in range(n_ctx))
        own_valid = iota2((1, BLOCK), 1) + me * BLOCK < length_ref[0]
        scale_row = lax.rsqrt(own_total[0:1] / channels + EPS)
        gain_ref[1:2, 0:BLOCK] = jnp.where(own_valid, scale_row, 0.0)

        def stores(chunk):
            slot = chunk % 2
            rows = pl.ds(pl.multiple_of(chunk * BLOCK, BLOCK), BLOCK)
            return [
                pltpu.make_async_copy(source.at[slot], target, store_sem.at[slot, i])
                for i, (source, target) in enumerate(
                    (
                        (v_yt, gate_t.at[chunk]),
                        (v_dz, d_z.at[rows]),
                        (v_dssd, d_ssd.at[rows]),
                    )
                )
            ]

        def gate_part(chunk, carry):
            slot = chunk % 2

            @pl.when(chunk >= 2)
            def _():
                for copy in stores(chunk - 2):
                    copy.wait()

            sums = columns[chunk]
            scale = lax.rsqrt(sums[:, 0:1] / channels + EPS)
            slant = scale * scale * scale * sums[:, 1:2] / channels
            here = column_valid(length_ref, chunk)
            for first in range(0, heads, 2):
                lanes = slice(first * HEAD, (first + 2) * HEAD)
                gate, gate_slope = silu_and_slope(all_z[chunk, :, lanes].astype(F32))
                mixed = all_y[chunk, :, lanes]
                d_yn = all_dyn[chunk, :, lanes]
                gain = gate_gain_ref[:, lanes]
                gated = mixed * gate
                scaled = gated * scale
                all_z[chunk, :, lanes] = (here * (scaled * gain)).astype(BF16)
                gain_ref[0:1, lanes] += jnp.sum(d_yn * scaled, axis=0, keepdims=True)
                d_gated = scale * (gain * d_yn) - gated * slant
                v_dz[slot, :, lanes] = (d_gated * mixed * gate_slope).astype(BF16)
                v_dssd[slot, :, lanes] = (d_gated * gate).astype(BF16)
            v_yt[slot] = all_z[chunk].T
            for copy in stores(chunk):
                copy.start()
            return carry

        lax.fori_loop(0, blocks, gate_part, 0)
        for chunk in (n_ctx - 2, n_ctx - 1):
            for copy in stores(chunk):
                copy.wait()
            store_mixed(chunk).wait()


def scan_forward(
    n, direct, unit, n_ctx, length, px, ps, normed, out_weight, w_z, upstream, par
):
    tokens, width = px.shape
    heads = width // HEAD
    count = tokens // BLOCK
    model = out_weight.shape[1]
    assert count == n_ctx
    by_block = lambda i: (i, 0)
    at_block = lambda size: pl.BlockSpec((BLOCK, size), by_block)
    whole = lambda a: pl.BlockSpec(a.shape, lambda i: (0, 0))
    any_space = pl.BlockSpec(memory_space=pl.ANY)
    low = lambda *shape: jax.ShapeDtypeStruct(shape, BF16)
    full = lambda *shape: jax.ShapeDtypeStruct(shape, F32)
    v_low = lambda *shape: pltpu.VMEM(shape, BF16)
    v_full = lambda *shape: pltpu.VMEM(shape, F32)
    dma = pltpu.SemaphoreType.DMA
    return pl.pallas_call(
        functools.partial(forward_kernel, heads, unit, n_ctx, n, direct),
        grid=(count,),
        in_specs=[
            pl.BlockSpec(memory_space=pltpu.SMEM),
            at_block(width),
            pl.BlockSpec((n_ctx, BLOCK, LANES), lambda i: (0, i, 0)),
            at_block(model),
            any_space,
            any_space,
            any_space,
        ]
        + [whole(par)],
        out_specs=[
            at_block(width),
            at_block(STATE),
            at_block(STATE),
            at_block(width),
            at_block(2 * STATE),
            at_block(LANES),
            at_block(LANES),
            at_block(LANES),
            pl.BlockSpec((1, STATE, width), lambda i: (i, 0, 0)),
            pl.BlockSpec((8, width), lambda i: (0, 0)),
            any_space,
            any_space,
            any_space,
            any_space,
        ],
        out_shape=[
            low(tokens, width),
            low(tokens, STATE),
            low(tokens, STATE),
            low(tokens, width),
            low(tokens, 2 * STATE),
            full(tokens, LANES),
            full(tokens, LANES),
            full(tokens, LANES),
            low(count, STATE, width),
            full(8, width),
            low(count, width, BLOCK),
            low(count, BLOCK, model),
            low(tokens, width),
            low(tokens, width),
        ],
        scratch_shapes=[
            v_full(STATE, width),
            v_full(8, width),
            v_full(8, 2 * STATE),
            v_low(width, model),
            v_low(*w_z.shape),
            v_low(count, BLOCK, model),
            v_full(count, BLOCK, width),
            v_low(count, BLOCK, width),
            v_full(count, BLOCK, width),
            v_low(count, BLOCK, width),
            v_low(2, width, BLOCK),
            v_low(2, BLOCK, model),
            v_low(2, BLOCK, width),
            v_low(2, BLOCK, width),
            v_full(n_ctx, count, 8, BLOCK),
            v_full(count, BLOCK, 8),
            dma((3,)),
            dma((2, 4)),
            dma((2, 2)),
            dma((2, 2, n - 1)),
            dma,
            dma((3,)),
            dma((3,)),
        ],
        compiler_params=pltpu.CompilerParams(
            collective_id=2, has_side_effects=True, vmem_limit_bytes=58 * 1024 * 1024
        ),
        name="scan_forward",
    )(length, px, ps, normed, out_weight, w_z, upstream, par)


def head_sums(product, chooser):
    high = product.astype(BF16)
    rest = (product - high.astype(F32)).astype(BF16)
    return mm(high, chooser) + mm(rest, chooser)


def backward_kernel(
    heads,
    unit,
    n_ctx,
    n,
    px_ref,
    ps_ref,
    x_ref,
    b_ref,
    c_ref,
    slope_x_ref,
    slope_s_ref,
    lam_ref,
    step_ref,
    chain_ref,
    kept_ref,
    dssd_ref,
    gate_t,
    normed_t,
    upstream,
    d_z,
    mixed_parts,
    hidden,
    gain_grads_ref,
    par_ref,
    dx_ref,
    small_ref,
    d_s,
    shard_o,
    shard_z,
    layer_out,
    back,
    mixed_grads,
    for_step,
    for_level,
    left,
    right,
    sums,
    after_x,
    after_s,
    v_left,
    v_right,
    products,
    slots,
    stage,
    done_o,
    done_z,
    mine,
    from_core,
    from_row,
    shared_parts,
    shared_core,
    shared_row,
    v_hidden,
    load_sem,
    store_sem,
    ring_send,
    ring_recv,
    part_send,
    part_recv,
    shared_send,
    shared_recv,
):
    turn = pl.program_id(0)
    turns = heads // 2 // POINTS
    block = pl.num_programs(0) - 1 - turn
    width, model = x_ref.shape[1], v_hidden.shape[1]
    taps_x_ref, taps_s_ref, _, skip_ref, _, rate = parameters(par_ref, width)
    own = hidden.shape[0]
    ring = Ring(n)
    around = Around(ring.me, ring.shard)
    piece, size = slots.shape[4], slots.shape[5]
    sum_mixed = TokenSum(
        around, mixed_parts, mine.at[0], mine.at[1], from_core, from_row, part_send, part_recv
    )
    sum_shared = TokenSum(
        around,
        shared_parts,
        shared_parts.at[ring.me],
        shared_parts.at[around.row_at],
        shared_core,
        shared_row,
        shared_send,
        shared_recv,
    )
    loads = [
        pltpu.make_async_copy(source, target, load_sem.at[i])
        for i, (source, target) in enumerate(
            (
                *((gate_t.at[c], v_left.at[pl.ds(0, width), pl.ds(c * own, own)]) for c in range(n_ctx)),
                *((upstream.at[c], v_right.at[pl.ds(c * own, own), pl.ds(0, model)]) for c in range(n_ctx)),
                *((normed_t.at[c], v_left.at[pl.ds(width, model), pl.ds(c * own, own)]) for c in range(n_ctx)),
                (d_z, v_right.at[:, pl.ds(model, width)]),
                *sum_mixed.loads(),
                (hidden, v_hidden),
            )
        )
    ]
    ring_loads = 1 + 3 * n_ctx

    def partial_sum(kind, way, sub, index):
        first = (1 - kind) * index * piece + kind * (width + (2 * index + way) * piece)
        at = (1 - kind) * (2 * way + sub) * size + kind * (model + sub * size)
        return mm(
            v_left[pl.ds(pl.multiple_of(first, 16), piece), :],
            v_right[:, pl.ds(pl.multiple_of(at, LANES), size)],
        )

    def all_products():
        tile = max(2 * piece, BLOCK)
        shards = tile // (2 * piece)

        def out_rows(i, carry):
            rows = pl.ds(pl.multiple_of(i * BLOCK, BLOCK), BLOCK)
            left = v_left[rows, :]
            products[rows, 0:width] = mm(left, v_right[:, 0:width]).astype(BF16)
            products[rows, width:model] = mm(left, v_right[:, width:model]).astype(BF16)
            return carry

        def in_rows(i, carry):
            left = v_left[pl.ds(pl.multiple_of(width + i * tile, 16), tile), :]
            both = mm(left, v_right[:, model:]).astype(BF16)
            for j in range(shards):
                place = pl.ds(pl.multiple_of((i * shards + j) * piece, 16), piece)
                for way in (0, 1):
                    products[place, model + way * width : model + (way + 1) * width] = both[
                        (2 * j + way) * piece : (2 * j + way + 1) * piece
                    ]
            return carry

        lax.fori_loop(0, width // BLOCK, out_rows, 0)
        lax.fori_loop(0, model // tile, in_rows, 0)

    def product(kind, way, sub, index):
        at = pl.multiple_of(kind * model + way * width + sub * size, LANES)
        return products[pl.ds(pl.multiple_of(index * piece, 16), piece), pl.ds(at, size)]

    def hop(kind, way, sub, step, source):
        return remote(
            source,
            slots.at[kind, step, way, sub],
            ring_send.at[kind, way, sub],
            ring_recv.at[kind, way, sub, step],
            (ring.me, ring.at(1 - 2 * way)),
        )

    def streams(body):
        def one(e, carry):
            body(e // 4, e // 2 % 2, e % 2)
            return carry

        lax.fori_loop(0, 8, one, 0)

    def start_ring(kind, way, sub):
        place = stage.at[kind, way, sub]
        place[...] = partial_sum(kind, way, sub, ring.at(2 * way - 1)).astype(BF16)
        hop(kind, way, sub, 0, place).start()

    def ring_step(step):
        def body(kind, way, sub):
            index = ring.at((step + 2) * (2 * way - 1))
            hop(kind, way, sub, step, stage.at[kind, way, sub]).wait()
            place = slots.at[kind, step, way, sub]
            total = place[...].astype(F32) + product(kind, way, sub, index).astype(F32)

            @pl.when(step < n - 2)
            def _():
                place[...] = total.astype(BF16)
                hop(kind, way, sub, step + 1, place).start()

            @pl.when(jnp.logical_and(step == n - 2, kind == 0))
            def _():
                at = pl.multiple_of((2 * way + sub) * size, LANES)
                done_o[:, pl.ds(at, size)] = total.astype(BF16)

            @pl.when(jnp.logical_and(step == n - 2, kind == 1))
            def _():
                done_z[way, pl.ds(pl.multiple_of(sub * size, 16), size), :] = total.T.astype(BF16)

        streams(body)

    def serve(point):
        at = turn * POINTS + point
        points = POINTS * n_ctx
        lax.fori_loop(
            at * (n - 1) // points,
            (at + 1) * (n - 1) // points,
            lambda step, carry: (ring_step(step), carry)[1],
            0,
        )

    @pl.when(turn == 0)
    def _():
        for device in around.all:
            greet(device)
        greet(ring.neighbour(0))
        greet(ring.neighbour(1))
        for copy in loads:
            copy.start()
        for c in range(3, n_ctx):
            shared_parts[c] = jnp.zeros(shared_parts.shape[1:], BF16)
        back[...] = jnp.zeros_like(back)
        small_ref[...] = jnp.zeros_like(small_ref)
        small_ref[taps_x_ref.shape[0] : taps_x_ref.shape[0] + 1, 0:width] = gain_grads_ref[0:1, :]
        after_x[...] = jnp.zeros_like(after_x)
        after_s[...] = jnp.zeros_like(after_s)
        pl.semaphore_wait(pltpu.get_barrier_semaphore(), 5)
        for copy in loads[:ring_loads]:
            copy.wait()
        streams(start_ring)
        sum_mixed.start()
        all_products()
        for copy in loads[ring_loads:]:
            copy.wait()

    @pl.when(turn == 1)
    def _():
        sum_mixed.pass_row()

    taps = taps_x_ref.shape[0] - 1

    rows_b, rows_c = b_ref[...], c_ref[...]
    step = step_ref[...]
    lam = lam_ref[...]
    gram = mm(rows_c, rows_b, ((1,), (1,)))
    gram_t = mm(rows_b, rows_c, ((1,), (1,)))
    level, across, last, weight, fade = levels(lam, step)
    out_decay = jnp.exp(level - level[BLOCK - 1 : BLOCK, :])
    step_across = step.T
    at_row, at_col = iota2((BLOCK, BLOCK), 0), iota2((BLOCK, BLOCK), 1)
    order = (at_row > at_col).astype(F32) - (at_row < at_col).astype(F32)
    low_half = iota2((1, LANES), 1) < HEAD
    lane = iota2((1, LANES), 1)
    by_state = rows_c.T
    kept = kept_ref[0]
    old_back = back[...].astype(BF16)
    entering = mm(rows_c, kept)
    leaving = mm(rows_b, old_back)
    at_last = jnp.sum(kept.astype(F32) * back[...], axis=0, keepdims=True)
    mixed_grads[...] = jnp.zeros_like(mixed_grads)
    left[...] = jnp.zeros_like(left)
    right[...] = jnp.zeros_like(right)
    sums[...] = jnp.zeros_like(sums)
    d_b = jnp.zeros((BLOCK, STATE), F32)
    d_c = jnp.zeros((BLOCK, STATE), F32)

    def conv_back(d_conv, after, current, weight):
        padded = jnp.concatenate([d_conv, after], axis=0)
        d_in = jnp.zeros_like(d_conv)
        grads = []
        for k in range(taps):
            moved = padded[taps - 1 - k : taps - 1 - k + BLOCK]
            d_in += weight[k : k + 1] * moved
            grads.append(jnp.sum(current * moved, axis=0, keepdims=True))
        grads.append(jnp.sum(d_conv, axis=0, keepdims=True))
        return d_in, jnp.concatenate(grads, axis=0)

    for first in range(0, heads, 2):
        lanes = slice(first * HEAD, (first + 2) * HEAD)
        x_low = x_ref[:, lanes]
        x = x_low.astype(F32)
        grad_low = dssd_ref[:, lanes]
        grad = grad_low.astype(F32)
        through = jnp.zeros((BLOCK, LANES), F32)
        for head, keep in ((first, low_half), (first + 1, jnp.logical_not(low_half))):
            decay = spread(level, across, head)
            grad_own = jnp.where(keep, grad, 0.0).astype(BF16)
            pairs = mm(grad_own, x_low, ((1,), (1,)))
            through += mm((gram_t * decay).astype(BF16), grad_own)
            scaled = decay * pairs * step_across[head : head + 1, :]
            mixed_grads[...] += scaled
            ordered = gram * scaled * order
            left[...] = jnp.where(
                lane == head, jnp.sum(ordered, axis=1, keepdims=True), left[...]
            )
            right[head : head + 1, :] = jnp.sum(ordered, axis=0, keepdims=True)
        weight_pair = pair_of(weight, first, low_half)
        step_pair = pair_of(step, first, low_half)
        fade_pair = pair_of(fade, first, low_half)
        out_pair = pair_of(out_decay, first, low_half)
        leave = leaving[:, lanes]
        d_x = step_pair * through + weight_pair * leave + skip_ref[:, lanes] * grad
        for_step[:, lanes] = x * (through + out_pair * leave)
        weighted = weight_pair * x
        faded = fade_pair * grad
        for_level[:, lanes] = weighted * leave - faded * entering[:, lanes]
        sums[0:1, lanes] = jnp.sum(weighted * leave, axis=0, keepdims=True)
        sums[2:3, lanes] = jnp.sum(x * grad, axis=0, keepdims=True)
        faded_low = faded.astype(BF16)
        d_b += mm(weighted.astype(BF16), old_back[:, lanes], ((1,), (1,)))
        d_c += mm(faded_low, kept[:, lanes], ((1,), (1,)))
        back[:, lanes] = back[:, lanes] * pair_of(last, first, low_half) + mm(by_state, faded_low)
        d_conv = d_x * slope_x_ref[:, lanes].astype(F32)
        d_in, grads = conv_back(
            d_conv, after_x[:, lanes], px_ref[:, lanes].astype(F32), taps_x_ref[:, lanes]
        )
        after_x[:, lanes] = d_conv[0:8]
        dx_ref[:, lanes] = d_in.astype(BF16)
        small_ref[0 : taps + 1, lanes] += grads
        if first // 2 % turns == turns - 1 and first // 2 // turns < POINTS - 1:
            serve(first // 2 // turns)

    all_pairs = mixed_grads[...]
    d_b = d_b + mm(all_pairs.T.astype(BF16), rows_c)
    d_c = d_c + mm(all_pairs.astype(BF16), rows_b)
    both = jnp.concatenate([ps_ref[0], ps_ref[1]], axis=1).astype(F32)
    d_conv = jnp.concatenate([d_b, d_c], axis=1) * slope_s_ref[...].astype(F32)
    d_in, grads = conv_back(
        d_conv, after_s[...], both, taps_s_ref[...]
    )
    after_s[...] = d_conv[0:8]
    here = pl.ds(pl.multiple_of(block * BLOCK, BLOCK), BLOCK)
    shared_parts[0, here, :] = d_in[:, :STATE].astype(BF16)
    shared_parts[1, here, :] = d_in[:, STATE:].astype(BF16)
    small_ref[0 : taps + 1, width:] += grads

    chooser = (iota2((width, LANES), 0) // HEAD == iota2((width, LANES), 1)).astype(BF16)
    d_step = head_sums(for_step[...], chooser)
    sums[1:2, :] = at_last
    total = head_sums(sums[...], chooser)
    d_level = head_sums(for_level[...], chooser) - left[...] + right[...].T
    final = -total[0:1, :] - last * total[1:2, :]
    d_level = d_level + jnp.where(iota2((BLOCK, 1), 0) == BLOCK - 1, final, 0.0)
    d_lam = mm_exact((at_row <= at_col).astype(F32), d_level)
    d_raw = (d_step + d_lam * rate) * chain_ref[...]
    head_row = taps + 2
    small_ref[head_row : head_row + 1, 0:LANES] += jnp.sum(d_raw, axis=0, keepdims=True)
    small_ref[head_row : head_row + 1, LANES : 2 * LANES] += jnp.sum(
        d_lam * lam, axis=0, keepdims=True
    )
    small_ref[head_row : head_row + 1, 2 * LANES : 3 * LANES] += total[2:3, :]
    chosen = chosen_heads(lax.axis_index("ctx"), heads, unit, n_ctx, True)
    shared_parts[2, here, :] = mm(d_raw.astype(BF16), chosen).astype(BF16)

    @pl.when(turn == pl.num_programs(0) - 1)
    def _():
        sum_shared.start()
        sum_shared.pass_row()


    serve(POINTS - 1)

    @pl.when(turn == pl.num_programs(0) - 1)
    def _():
        stores = [
            pltpu.make_async_copy(source, target, store_sem.at[i])
            for i, (source, target) in enumerate(
                (
                    (done_o, shard_o),
                    (done_z, shard_z),
                    (v_hidden, layer_out),
                    (shared_parts.at[ring.me], d_s),
                )
            )
        ]
        stores[0].start()
        stores[1].start()
        scale = gain_grads_ref[:, 0:BLOCK].T[:, 1:2]
        total = v_hidden[...].astype(F32) + scale * sum_mixed.total()
        v_hidden[...] = total.astype(BF16)
        stores[2].start()
        shared_parts[ring.me] = sum_shared.total().astype(BF16)
        stores[3].start()
        for copy in stores:
            copy.wait()


def scan_backward(
    n, unit, n_ctx, px, ps, kept_parts, d_ssd, gate_t, normed_t, upstream, d_z, mixed_parts, hidden, gain_grads, par
):
    x, rows_b, rows_c, slope_x, slope_s, lam, step, chain, kept = kept_parts
    tokens, width = px.shape
    heads = width // HEAD
    count = tokens // BLOCK
    own, model = hidden.shape
    piece = width // n
    assert model == 2 * width and heads // 2 % POINTS == 0
    by_block = lambda i: (count - 1 - i, 0)
    at_block = lambda size: pl.BlockSpec((BLOCK, size), by_block)
    whole = lambda a: pl.BlockSpec(a.shape, lambda i: (0, 0))
    any_space = pl.BlockSpec(memory_space=pl.ANY)
    low = lambda *shape: jax.ShapeDtypeStruct(shape, BF16)
    v_low = lambda *shape: pltpu.VMEM(shape, BF16)
    v_full = lambda *shape: pltpu.VMEM(shape, F32)
    part = lambda a, b: pl.BlockSpec((1, a, b), lambda i: (count - 1 - i, 0, 0))
    small_shape = (8, width + 2 * STATE)
    dma = pltpu.SemaphoreType.DMA
    return pl.pallas_call(
        functools.partial(backward_kernel, heads, unit, n_ctx, n),
        grid=(count,),
        in_specs=[
            at_block(width),
            pl.BlockSpec((n_ctx, BLOCK, LANES), lambda i: (0, count - 1 - i, 0)),
            at_block(width),
            at_block(STATE),
            at_block(STATE),
            at_block(width),
            at_block(2 * STATE),
            at_block(LANES),
            at_block(LANES),
            at_block(LANES),
            part(STATE, width),
            at_block(width),
        ]
        + [any_space] * 6
        + [whole(a) for a in (gain_grads, par)],
        out_specs=[
            at_block(width),
            pl.BlockSpec(small_shape, lambda i: (0, 0)),
            any_space,
            any_space,
            any_space,
            any_space,
        ],
        out_shape=[
            low(tokens, width),
            jax.ShapeDtypeStruct(small_shape, F32),
            low(tokens, LANES),
            low(piece, model),
            low(2, width, piece),
            low(own, model),
        ],
        scratch_shapes=[
            v_full(STATE, width),
            v_full(BLOCK, BLOCK),
            v_full(BLOCK, width),
            v_full(BLOCK, width),
            v_full(BLOCK, LANES),
            v_full(LANES, BLOCK),
            v_full(8, width),
            v_full(8, width),
            v_full(8, 2 * STATE),
            v_low(width + model, tokens),
            v_low(tokens, model + width),
            v_low(width, 2 * model),
            v_low(2, n - 1, 2, 2, piece, width // 2),
            v_low(2, 2, 2, piece, width // 2),
            v_low(piece, model),
            v_low(2, width, piece),
            v_low(2, own, model),
            v_low(2, own, model),
            v_low(own, model),
            v_low(n_ctx, tokens, LANES),
            v_low(2, tokens, LANES),
            v_low(tokens, LANES),
            v_low(own, model),
            dma((4 + 3 * n_ctx,)),
            dma((4,)),
            dma((2, 2, 2)),
            dma((2, 2, 2, n - 1)),
            dma((3,)),
            dma((3,)),
            dma((3,)),
            dma((3,)),
        ],
        compiler_params=pltpu.CompilerParams(
            collective_id=3, has_side_effects=True, vmem_limit_bytes=59 * 1024 * 1024
        ),
        name="scan_backward",
    )(
        px, ps, x, rows_b, rows_c, slope_x, slope_s, lam, step, chain, kept, d_ssd, gate_t, normed_t, upstream, d_z, mixed_parts, hidden, gain_grads, par
    )


def gather_kernel(
    n,
    n_ctx,
    unit,
    taps,
    sizes,
    hidden,
    cotangent,
    in_weight_t,
    small,
    cotangent_all,
    w_x,
    w_s,
    w_z,
    par_out,
    gain_out,
    proj_x,
    proj_s,
    normed_out,
    normed_t,
    v_hidden,
    v_normed,
    v_x,
    v_s,
    own_z,
    v_small,
    raw_x,
    raw_s,
    raw_z,
    out_x,
    out_s,
    out_t,
    v_gain,
    v_par,
    conv_lines,
    gate_line,
    head_lines,
    load_sem,
    shared_sem,
    column_sem,
    local_sem,
    keep_sem,
    store_sem,
    ring_send,
    ring_recv,
    ctx_send,
    ctx_recv,
):
    ring = Ring(n)
    me, shard = ring.me, ring.shard
    width, model = v_x.shape[1], v_x.shape[0]
    inner = width * n_ctx
    r = model // n
    shared = in_weight_t.shape[0] - 2 * inner
    row = me // 2
    other_core = (me + 1 - 2 * (me % 2), shard)
    other_row = (me + 2 - 4 * row, shard)
    barrier = pltpu.get_barrier_semaphore()
    for device in (other_core, other_row, ring.neighbour(0), ring.neighbour(1)):
        pl.semaphore_signal(barrier, inc=1, device_id=device, device_id_type=MESH)

    part = unit * HEAD

    def load_columns(base, target, sems):
        return [
            pltpu.make_async_copy(
                in_weight_t.at[pl.ds(pl.multiple_of(base + (a * n_ctx + me) * part, 16), part)],
                target.at[pl.ds(a * part, part)],
                sems.at[a],
            )
            for a in range(width // part)
        ]

    loads = [
        load_columns(inner, raw_x, column_sem.at[0]),
        [],
        [pltpu.make_async_copy(small, v_small.at[shard], load_sem.at[1])],
        [pltpu.make_async_copy(hidden, v_hidden.at[me], load_sem.at[2])],
        load_columns(0, raw_z, column_sem.at[1]),
    ]
    raw_s[...] = jnp.zeros_like(raw_s)

    def load_shared(wait):
        for j in (0, 1):
            first = me * LANES + j * HEAD

            @pl.when(first < shared)
            def _():
                copy = pltpu.make_async_copy(
                    in_weight_t.at[pl.ds(pl.multiple_of(2 * inner + first, HEAD), HEAD)],
                    raw_s.at[pl.ds(j * HEAD, HEAD)],
                    shared_sem.at[j],
                )
                copy.wait() if wait else copy.start()

    load_shared(False)
    for copies in loads:
        for copy in copies:
            copy.start()

    def loaded(i):
        for copy in loads[i]:
            copy.wait()

    pl.semaphore_wait(barrier, 4)

    half = width // 2
    rows = r // 2
    both_rows = lambda index, way: pl.ds(pl.multiple_of((2 * index + way) * rows, 16), rows)
    x_part = lambda a, sub: lambda index, way: a.at[both_rows(index, way), pl.ds(sub * half, half)]
    s_part = lambda index, way: v_s.at[both_rows(index, way)]
    small_part = lambda index, way: v_small.at[index, pl.ds(way * SMALL_ROWS // 2, SMALL_ROWS // 2)]
    phases = (
        ((0, small_part), (1, s_part), (2, x_part(v_x, 0)), (3, x_part(v_x, 1))),
        ((4, x_part(w_z, 0)), (5, x_part(w_z, 1))),
    )

    def hop(stream, way, step):
        number, part = stream
        place = part(ring.at(-step if way == 0 else step), way)
        return remote(
            place, place, ring_send.at[number, way], ring_recv.at[number, way, step],
            ring.neighbour(way),
        )

    def arrives(stream, way, step):
        number, part = stream
        landed = part(ring.at(-step - 1 if way == 0 else step + 1), way)
        return remote(
            landed, landed, ring_send.at[number, way], ring_recv.at[number, way, step],
            ring.neighbour(way),
        )

    def start_stream(stream):
        for way in (0, 1):
            hop(stream, way, 0).start()

    def to_row(i, a, whole):
        return remote(a, whole.at[me], ctx_send.at[i, 0], ctx_recv.at[i, 0], other_row)

    def to_core(i, a, whole):
        return remote(a, whole.at[me], ctx_send.at[i, 1], ctx_recv.at[i, 1], other_core)

    def pass_on(i, whole):
        beyond = whole.at[other_row[0]]
        return remote(beyond, beyond, ctx_send.at[i, 2], ctx_recv.at[i, 2], other_core)

    to_row(0, hidden, v_hidden).start()
    to_core(0, hidden, v_hidden).start()
    own_rows = pl.ds(pl.multiple_of(shard * r, 16), r)
    loaded(2)
    start_stream(phases[0][0])
    loaded(0)
    v_x[own_rows, :] = raw_x[...].T
    start_stream(phases[0][2])
    start_stream(phases[0][3])
    load_shared(True)
    v_s[own_rows, :] = raw_s[...].T
    start_stream(phases[0][1])
    keep_cotangent = pltpu.make_async_copy(cotangent, cotangent_all.at[me], local_sem)
    keep_cotangent.start()
    keep_shared = pltpu.make_async_copy(out_s, proj_s.at[me], shared_sem.at[2])
    loaded(3)
    loaded(4)
    own_z[...] = raw_z[...].T
    keep_z = pltpu.make_async_copy(own_z, w_z.at[own_rows], keep_sem)
    keep_z.start()
    keep_z.wait()

    def run_phase(number, work, after):
        def body(step, carry):
            for stream in phases[number]:
                for way in (0, 1):
                    arrives(stream, way, step).wait_recv()
                    hop(stream, way, step).wait_send()
                    hop(stream, way, step + 1).start()
            if work is not None:

                @pl.when(step < n_ctx)
                def _():
                    work(step)

                @pl.when(step == n_ctx - 1)
                def _():
                    to_row(2, out_s, proj_s).start()
                    to_core(2, out_s, proj_s).start()
                    keep_shared.start()

            return carry

        lax.fori_loop(0, n - 2, body, 0)
        after()
        for stream in phases[number]:
            for way in (0, 1):
                arrives(stream, way, n - 2).wait_recv()
                hop(stream, way, n - 2).wait_send()

    tokens = v_hidden.shape[1]

    def project_first(chunk):
        at = pl.ds(pl.multiple_of(chunk * tokens, tokens), tokens)
        resid = v_hidden[chunk].astype(F32)
        scale = lax.rsqrt(jnp.mean(resid * resid, axis=1, keepdims=True) + EPS)
        normed = (resid * scale * v_gain[...]).astype(BF16)
        v_normed[at, :] = normed
        out_x[at, :] = mm(normed, v_x[...]).astype(BF16)
        out_s[at, :] = mm(normed, v_s[...]).astype(BF16)
        out_t[chunk] = normed.T

    stores = [
        pltpu.make_async_copy(source, target, store_sem.at[i])
        for i, (source, target) in enumerate(
            (
                (v_x, w_x),
                (v_s, w_s),
                (v_par, par_out),
                (v_gain, gain_out),
                (out_x, proj_x),
                (v_normed, normed_out),
                (out_t, normed_t),
            )
        )
    ]

    def after_first():
        for stream in phases[1]:
            start_stream(stream)
        to_row(0, hidden, v_hidden).wait_recv()
        pass_on(0, v_hidden).start()
        to_row(1, cotangent, cotangent_all).start()
        to_core(1, cotangent, cotangent_all).start()
        to_row(0, hidden, v_hidden).wait_send()
        to_core(0, hidden, v_hidden).wait()
        pass_on(0, v_hidden).wait()

    def after_second():
        to_row(1, cotangent, cotangent_all).wait_recv()
        pass_on(1, cotangent_all).start()
        to_row(2, out_s, proj_s).wait_recv()
        pass_on(2, proj_s).start()
        for copy in stores[4:]:
            copy.start()

    run_phase(0, None, after_first)
    gain_size, conv_size, gate_size, held = sizes
    head_lines[...] = jnp.zeros_like(head_lines)
    for f in range(n):
        v_gain[:, f * r : (f + 1) * r] = v_small[f, 0:1, 0:r].astype(F32)
        conv_lines[0 : taps + 1, f * conv_size : (f + 1) * conv_size] = v_small[
            f, 1 : taps + 2, 0:conv_size
        ].astype(F32)
        gate_line[:, f * gate_size : (f + 1) * gate_size] = v_small[
            f, taps + 2 : taps + 3, 0:gate_size
        ].astype(F32)
        for k in range(3):
            head_lines[k : k + 1, f * held : (f + 1) * held] = v_small[
                f, taps + 3 : taps + 4, k * held : (k + 1) * held
            ].astype(F32)

    def own_part(line, a):
        at = (a * n_ctx + me) * part
        span = max(part, LANES)
        found = line[:, pl.ds(pl.multiple_of(at // LANES * LANES, LANES), span)]
        if part < LANES:
            found = pltpu.roll(found, lax.rem(LANES - at % LANES, LANES), 1)
        return found[:, 0:part]

    v_par[...] = jnp.zeros_like(v_par)
    for a in range(width // part):
        v_par[0 : taps + 1, a * part : (a + 1) * part] = own_part(conv_lines, a)[0 : taps + 1]
        v_par[taps + 1 : taps + 2, a * part : (a + 1) * part] = own_part(gate_line, a)
    v_par[0 : taps + 1, width:] = conv_lines[0 : taps + 1, inner:]
    lines = mm(head_lines[...].astype(BF16), chosen_heads(me, width // HEAD, unit, n_ctx))
    heads_row = taps + 3
    v_par[heads_row : heads_row + 1, 0:LANES] = lines[0:1]
    v_par[heads_row : heads_row + 1, LANES : 2 * LANES] = jnp.exp(lines[1:2])
    wide = (iota2((LANES, width), 1) // HEAD == iota2((LANES, width), 0)).astype(BF16)
    v_par[taps + 2 : taps + 3, 0:width] = mm(lines.astype(BF16), wide)[2:3]
    for copy in stores[0:4]:
        copy.start()
    run_phase(1, project_first, after_second)
    to_row(1, cotangent, cotangent_all).wait_send()
    to_core(1, cotangent, cotangent_all).wait()
    pass_on(1, cotangent_all).wait()
    keep_cotangent.wait()
    to_row(2, out_s, proj_s).wait_send()
    to_core(2, out_s, proj_s).wait()
    pass_on(2, proj_s).wait()
    keep_shared.wait()
    for copy in stores:
        copy.wait()


def gather_all(n, n_ctx, unit, taps, sizes, width, hidden, cotangent, in_weight_t, small):
    own, model = hidden.shape
    tokens = own * n_ctx
    rows = in_weight_t.shape[1]
    any_space = pl.BlockSpec(memory_space=pl.ANY)
    par_shape = (taps + 4, width + 2 * STATE)
    inner = width * n_ctx
    low = lambda *shape: jax.ShapeDtypeStruct(shape, BF16)
    v_low = lambda *shape: pltpu.VMEM(shape, BF16)
    dma = pltpu.SemaphoreType.DMA
    return pl.pallas_call(
        functools.partial(gather_kernel, n, n_ctx, unit, taps, sizes),
        in_specs=[any_space] * 4,
        out_specs=[any_space] * 10,
        out_shape=[
            low(n_ctx, own, model),
            low(model, width),
            low(model, LANES),
            low(model, width),
            jax.ShapeDtypeStruct(par_shape, F32),
            jax.ShapeDtypeStruct((1, model), F32),
            low(tokens, width),
            low(n_ctx, tokens, LANES),
            low(tokens, model),
            low(n_ctx, model, own),
        ],
        scratch_shapes=[
            v_low(n_ctx, own, model),
            v_low(tokens, model),
            v_low(model, width),
            v_low(model, LANES),
            v_low(rows, width),
            v_low(n, small.shape[0], small.shape[1]),
            v_low(width, rows),
            v_low(LANES, rows),
            v_low(width, rows),
            v_low(tokens, width),
            v_low(tokens, LANES),
            v_low(n_ctx, model, own),
            pltpu.VMEM((1, model), F32),
            pltpu.VMEM(par_shape, F32),
            pltpu.VMEM((8, inner + 2 * STATE), F32),
            pltpu.VMEM((1, inner), F32),
            pltpu.VMEM((8, LANES), F32),
            dma((3,)),
            dma((3,)),
            dma((2, width // (unit * HEAD))),
            dma,
            dma,
            dma((7,)),
            dma((6, 2)),
            dma((6, 2, n - 1)),
            dma((3, 3)),
            dma((3, 3)),
        ],
        compiler_params=pltpu.CompilerParams(
            collective_id=0, has_side_effects=True, vmem_limit_bytes=56 * 1024 * 1024
        ),
        name="gather_all",
    )(hidden, cotangent, in_weight_t, small)


def reduce_kernel(
    n,
    n_ctx,
    direct,
    normed_t,
    d_z,
    d_x,
    d_s,
    w_z,
    w_x,
    w_s,
    shard_o,
    shard_z,
    small,
    hidden,
    cotangent,
    gain,
    g_z,
    g_x,
    g_s,
    g_o,
    hidden_grad,
    small_out,
    norm_out,
    v_normed_t,
    v_d_z,
    v_d_x,
    v_d_s,
    v_z,
    v_x,
    v_s,
    parts,
    partials,
    slots,
    stage,
    done,
    moved,
    from_core,
    from_row,
    v_hidden,
    v_cotangent,
    v_gain,
    small_all,
    small_ctx,
    norm_all,
    norm_ctx,
    load_sem,
    store_sem,
    ring_send,
    ring_recv,
    ctx_send,
    ctx_recv,
    own_sem,
    piece_send,
    piece_recv,
    part_send,
    part_recv,
    small_send,
    small_recv,
    small_ctx_send,
    small_ctx_recv,
):
    ring = Ring(n)
    me, shard = ring.me, ring.shard
    around = Around(me, shard)
    core, row = me % 2, me // 2
    piece_peer = (shard % n_ctx, shard // n_ctx * n_ctx + me)
    moves = shard % n_ctx != me
    barrier = pltpu.get_barrier_semaphore()
    for device in around.all:
        greet(device)
    lax.fori_loop(1, n, lambda j, carry: (greet((me, lax.rem(shard + j, n))), carry)[1], 0)
    own = hidden.shape[0]
    sum_normed = TokenSum(
        around, parts, parts.at[me], parts.at[around.row_at], from_core, from_row, part_send, part_recv
    )
    sum_small, sum_norm = (
        SmallSum(
            n, around, whole, sums, small_send.at[i], small_recv.at[i], small_ctx_send.at[i], small_ctx_recv.at[i]
        )
        for i, (whole, sums) in enumerate(((small_all, small_ctx), (norm_all, norm_ctx)))
    )
    loads = [
        pltpu.make_async_copy(source, target, load_sem.at[i])
        for i, (source, target) in enumerate(
            (
                *((normed_t.at[c], v_normed_t.at[:, pl.ds(c * own, own)]) for c in range(n_ctx)),
                (d_s, v_d_s),
                (d_x, v_d_x),
                (small, small_all.at[shard]),
                (d_z, v_d_z),
                (w_z, v_z),
                (w_x, v_x),
                (w_s, v_s),
                (hidden, v_hidden),
                (cotangent, v_cotangent),
                (gain, v_gain),
            )
        )
    ]
    ring_loads = n_ctx + 2
    for copy in loads:
        copy.start()
    if direct:
        pl.semaphore_wait(barrier, n + 2)
    else:

        @pl.when(moves)
        def _():
            greet(piece_peer)
            pl.semaphore_wait(barrier, n + 3)

        @pl.when(jnp.logical_not(moves))
        def _():
            pl.semaphore_wait(barrier, n + 2)

    rows = v_normed_t.shape[0] // (2 * n)
    half, last = v_d_x.shape[1] // 2, v_d_s.shape[1]
    streams = (
        (0, v_d_s, 0, last, 2 * half),
        (1, v_d_x, 0, half, 0),
        (2, v_d_x, half, half, half),
    )

    def compute_partials(step):
        for way in (0, 1):
            index = ring.at(-step - 2 if way == 0 else step + 2)
            left = v_normed_t[pl.ds(pl.multiple_of((2 * index + way) * rows, 16), rows), :]
            partials[way, :, 2 * half :] = mm(left, v_d_s[...])
            partials[way, :, 0 : 2 * half] = mm(left, v_d_x[...])

    def slot(stream, way, step):
        return slots.at[step, way, :, pl.ds(stream[4], stream[3])]

    def hop(stream, way, step, source):
        return remote(
            source,
            slot(stream, way, step),
            ring_send.at[stream[0], way],
            ring_recv.at[stream[0], way, step],
            ring.neighbour(way),
        )

    def first_part(stream, way):
        return stage.at[way, :, pl.ds(stream[4], stream[3])]

    def arrived(stream, way, step):
        hop(stream, way, step, first_part(stream, way)).wait()
        partial = partials[way, :, stream[4] : stream[4] + stream[3]]
        return slot(stream, way, step)[...].astype(F32) + partial

    done_of = lambda stream: done.at[pl.ds(stream[4], stream[3])]
    of_x = lambda c, first: g_x.at[c, pl.ds(first, half)]
    shares = (
        (shard_o if direct else moved, lambda c: g_o.at[c]),
        (shard_z, lambda c: g_z.at[c]),
        (done_of(streams[1]), lambda c: of_x(c, 0)),
        (done_of(streams[2]), lambda c: of_x(c, half)),
        (done_of(streams[0]), lambda c: g_s.at[c]),
    )

    def share(i, kind):
        source, whole = shares[i]
        at = me
        if kind == 2:
            source, at = whole(around.row_at), around.row_at
        device = around.row if kind == 0 else around.core
        return remote(source, whole(at), ctx_send.at[i, kind], ctx_recv.at[i, kind], device)

    def keep(i):
        return pltpu.make_async_copy(shares[i][0], shares[i][1](me), own_sem.at[i])

    def start_share(i):
        share(i, 0).start()
        share(i, 1).start()
        keep(i).start()

    def pass_share(i):
        share(i, 0).wait_recv()
        share(i, 2).start()

    def close_share(i):
        share(i, 0).wait_send()
        share(i, 1).wait()
        share(i, 2).wait()
        keep(i).wait()

    def move_piece(wait):
        if direct:
            return
        keep_piece = pltpu.make_async_copy(shard_o, moved, piece_send)
        send_piece = remote(shard_o, moved, piece_send, piece_recv, piece_peer)

        @pl.when(moves)
        def _():
            send_piece.wait() if wait else send_piece.start()

        @pl.when(jnp.logical_not(moves))
        def _():
            keep_piece.wait() if wait else keep_piece.start()

    def normed_part(i, carry):
        to_row = row + (1 - i % 2) * (1 - 2 * row)
        to_core = core + (1 - i // 2) * (1 - 2 * core)
        at = 2 * to_row + to_core
        tokens = pl.ds(pl.multiple_of(at * own, own), own)
        parts[at] = (
            mm(v_d_z[tokens, :], v_z[...], ((1,), (1,)))
            + mm(v_d_x[tokens, :], v_x[...], ((1,), (1,)))
            + mm(v_d_s[tokens, :], v_s[...], ((1,), (1,)))
        ).astype(BF16)
        return carry

    store_grad = pltpu.make_async_copy(v_cotangent, hidden_grad, store_sem.at[0])
    store_small = pltpu.make_async_copy(small_ctx, small_out, store_sem.at[1])
    store_norm = pltpu.make_async_copy(norm_ctx, norm_out, store_sem.at[2])

    def finish_tokens():
        resid = v_hidden[...].astype(F32)
        scale = lax.rsqrt(jnp.mean(resid * resid, axis=1, keepdims=True) + EPS)
        d_normed = sum_normed.total()
        f = v_gain[...] * d_normed
        slope = scale**3 * jnp.mean(resid * f, axis=1, keepdims=True)
        grad = v_cotangent[...].astype(F32) + scale * f - resid * slope
        v_cotangent[...] = grad.astype(BF16)
        store_grad.start()
        by_model = jnp.sum(d_normed * resid * scale, axis=0, keepdims=True)
        size = norm_all.shape[2]
        for j in range(norm_all.shape[1]):
            norm_all[shard, j : j + 1, :] = by_model[:, j * size : (j + 1) * size]
        sum_norm.start()

    move_piece(False)
    for copy in loads[:ring_loads]:
        copy.wait()
    compute_partials(-1)
    for way in (0, 1):
        stage[way] = partials[way].astype(BF16)
        for stream in streams:
            hop(stream, way, 0, first_part(stream, way)).start()
    compute_partials(0)
    for copy in loads[ring_loads:]:
        copy.wait()
    sum_small.start()
    move_piece(True)
    start_share(0)
    start_share(1)

    def body(step, carry):
        for stream in streams:
            for way in (0, 1):
                total = arrived(stream, way, step)
                place = slot(stream, way, step)
                place[...] = total.astype(BF16)
                hop(stream, way, step + 1, place).start()
        compute_partials(step + 1)

        @pl.when(step < 2)
        def _():
            lax.fori_loop(2 * step, 2 * step + 2, normed_part, 0)

        @pl.when(step == 0)
        def _():
            sum_normed.start()

        @pl.when(step == 1)
        def _():
            sum_normed.pass_row()

        @pl.when(step == n - 3)
        def _():
            finish_tokens()

        return carry

    lax.fori_loop(0, n - 2, body, 0)
    sum_small.add()
    pass_share(0)
    pass_share(1)
    for number, shared in ((0, 4), (1, 2), (2, 3)):
        place = done_of(streams[number])
        for way in (0, 1):
            total = arrived(streams[number], way, n - 2)
            place[:, way * rows : (way + 1) * rows] = total.T.astype(BF16)
        start_share(shared)
    sum_norm.add()
    sum_small.finish()
    store_small.start()
    for i in (4, 2, 3):
        pass_share(i)
    sum_norm.finish()
    store_norm.start()
    for i in range(5):
        close_share(i)
    store_grad.wait()
    store_small.wait()
    store_norm.wait()


def reduce_all(
    n, n_ctx, direct, normed_t, d_z, d_x, d_s, w_z, w_x, w_s, shard_o, shard_z, small, hidden, cotangent, gain
):
    model, tokens = normed_t.shape[1], d_x.shape[0]
    width, shared_width = d_x.shape[1], d_s.shape[1]
    rows, piece, own = model // n, width // n, hidden.shape[0]
    columns = width + shared_width
    any_space = pl.BlockSpec(memory_space=pl.ANY)
    dma = pltpu.SemaphoreType.DMA
    low = lambda *shape: jax.ShapeDtypeStruct(shape, BF16)
    v_low = lambda *shape: pltpu.VMEM(shape, BF16)
    v_full = lambda *shape: pltpu.VMEM(shape, F32)
    norm_shape = (8, model // 8)
    return pl.pallas_call(
        functools.partial(reduce_kernel, n, n_ctx, direct),
        in_specs=[any_space] * 13,
        out_specs=[any_space] * 7,
        out_shape=[
            low(n_ctx, 2, width, rows // 2),
            low(n_ctx, width, rows),
            low(n_ctx, shared_width, rows),
            low(n_ctx, piece, model),
            low(own, model),
            jax.ShapeDtypeStruct((n_ctx,) + small.shape, F32),
            jax.ShapeDtypeStruct((n_ctx,) + norm_shape, F32),
        ],
        scratch_shapes=[
            v_low(model, tokens),
            v_low(tokens, width),
            v_low(tokens, width),
            v_low(tokens, shared_width),
            v_low(*w_z.shape),
            v_low(*w_x.shape),
            v_low(*w_s.shape),
            v_low(n_ctx, own, model),
            v_full(2, rows // 2, columns),
            v_low(n - 1, 2, rows // 2, columns),
            v_low(2, rows // 2, columns),
            v_low(columns, rows),
            v_low(piece, model),
            v_low(2, own, model),
            v_low(own, model),
            v_low(own, model),
            v_low(own, model),
            v_full(1, model),
            v_full(n, *small.shape),
            v_full(n_ctx, *small.shape),
            v_full(n, *norm_shape),
            v_full(n_ctx, *norm_shape),
            dma((10 + n_ctx,)),
            dma((3,)),
            dma((3, 2)),
            dma((3, 2, n - 1)),
            dma((5, 3)),
            dma((5, 3)),
            dma((5,)),
            dma,
            dma,
            dma((3,)),
            dma((3,)),
            dma((2, n - 1)),
            dma((2, n - 1)),
            dma((2, 3)),
            dma((2, 3)),
        ],
        compiler_params=pltpu.CompilerParams(
            collective_id=1, has_side_effects=True, vmem_limit_bytes=58 * 1024 * 1024
        ),
        name="reduce_all",
    )(
        normed_t, d_z, d_x, d_s, w_z, w_x, w_s, shard_o, shard_z, small, hidden, cotangent, gain
    )


def assemble_kernel(part, z_ref, x_ref, s_ref, o_ref, out_ref, rows_ref):
    place = pl.program_id(0)
    n_ctx, size, half = x_ref.shape[0], x_ref.shape[1], z_ref.shape[3]

    def interleave(write):
        for a in range(size // part):
            for c in range(n_ctx):
                write(
                    slice((a * n_ctx + c) * part, (a * n_ctx + c + 1) * part),
                    c,
                    slice(a * part, (a + 1) * part),
                )

    def write_z(target, c, source):
        for way in (0, 1):
            out_ref[target, way * half : (way + 1) * half] = z_ref[c, way, source, :].astype(F32)

    def write_x(target, c, source):
        out_ref[target, :] = x_ref[c, source, :].astype(F32)

    @pl.when(place < n_ctx)
    def _():
        interleave(write_z)

    @pl.when(jnp.logical_and(place >= n_ctx, place < 2 * n_ctx))
    def _():
        interleave(write_x)

    @pl.when(place == 2 * n_ctx)
    def _():
        for c in range(s_ref.shape[0]):
            out_ref[c * LANES : (c + 1) * LANES, :] = s_ref[c].astype(F32)

    @pl.when(place < 2 * n_ctx)
    def _():
        rows_ref[...] = o_ref[...].astype(F32)


def assemble(part, g_z, g_x, g_s, g_o, columns):
    n_ctx, width, rows = g_x.shape
    block = (n_ctx, width // n_ctx, rows)
    g_o = g_o.reshape(-1, g_o.shape[2])
    tile = max(g_o.shape[0] // (2 * n_ctx), 16)
    at_tile = lambda i: (jnp.minimum(i, g_o.shape[0] // tile - 1), 0)
    return pl.pallas_call(
        functools.partial(assemble_kernel, part),
        grid=(2 * n_ctx + 1,),
        in_specs=[
            pl.BlockSpec(
                (n_ctx, 2, width // n_ctx, rows // 2),
                lambda i: (0, 0, jnp.minimum(i, n_ctx - 1), 0),
            ),
            pl.BlockSpec(block, lambda i: (0, jnp.clip(i - n_ctx, 0, n_ctx - 1), 0)),
            pl.BlockSpec(g_s.shape, lambda i: (0, 0, 0)),
            pl.BlockSpec((tile, g_o.shape[1]), at_tile),
        ],
        out_specs=[
            pl.BlockSpec((width, rows), lambda i: (i, 0)),
            pl.BlockSpec((tile, g_o.shape[1]), at_tile),
        ],
        out_shape=[
            jax.ShapeDtypeStruct((columns, rows), F32),
            jax.ShapeDtypeStruct(g_o.shape, F32),
        ],
        compiler_params=pltpu.CompilerParams(vmem_limit_bytes=58 * 1024 * 1024),
        name="assemble",
    )(g_z, g_x, g_s, g_o)


def on_device(
    hidden,
    cotangent,
    seq_lens,
    norm_gain,
    in_weight,
    conv_weight,
    conv_bias,
    dt_bias,
    a_log,
    d_skip,
    gate_gain,
    out_weight,
):
    n_ctx, n_fsdp = lax.axis_size("ctx"), lax.axis_size("fsdp")
    me, shard = lax.axis_index("ctx"), lax.axis_index("fsdp")
    taps = conv_weight.shape[0]
    heads_all = dt_bias.shape[0] * n_fsdp
    inner = out_weight.shape[0] * n_fsdp
    heads, width = heads_all // n_ctx, inner // n_ctx
    model = hidden.shape[2]
    both = 2 * STATE
    held = dt_bias.shape[0]
    direct = held % n_ctx == 0
    unit = held // n_ctx if direct else 1
    part = unit * HEAD
    assert both + heads_all <= n_ctx * LANES and heads_all == HEAD

    per_head = jnp.concatenate([dt_bias, a_log, d_skip])
    lines = [norm_gain, *(conv_weight[k] for k in range(taps)), conv_bias, gate_gain, per_head]
    longest = -(-max(a.shape[0] for a in lines) // LANES) * LANES
    filler = jnp.concatenate([gate_gain, conv_bias])
    flat = []
    for line in lines:
        flat += [line, filler[: longest - line.shape[0]]]
    flat.append(jnp.zeros(((SMALL_ROWS - len(lines)) * longest,), BF16))
    small = jnp.concatenate(flat).reshape(SMALL_ROWS, longest)
    sizes = (norm_gain.shape[0], conv_bias.shape[0], gate_gain.shape[0], held)
    upstream, w_x, w_s, w_z, par, gain_norm, proj_x, proj_s, normed, normed_t = gather_all(
        n_fsdp, n_ctx, unit, taps, sizes, width, hidden[0], cotangent[0], in_weight.T, small
    )
    *kept_parts, gain_grads, gate_t, mixed_parts, d_z, d_ssd = scan_forward(
        n_fsdp, direct, unit, n_ctx, seq_lens, proj_x, proj_s, normed, out_weight, w_z, upstream, par
    )
    d_x, small_grads, d_s, shard_o, shard_z, layer_out = scan_backward(
        n_fsdp, unit, n_ctx, proj_x, proj_s, kept_parts, d_ssd, gate_t, normed_t, upstream, d_z, mixed_parts, hidden[0], gain_grads, par
    )
    g_z, g_x, g_s, g_o, hidden_grad, sums, norm_sums = reduce_all(
        n_fsdp, n_ctx, direct, normed_t, d_z, d_x, d_s, w_z, w_x, w_s, shard_o, shard_z, small_grads, hidden[0], cotangent[0], gain_norm
    )
    grad_in_weight, grad_out_weight = assemble(
        part, g_z, g_x, g_s, g_o, 2 * inner + both + heads_all
    )

    def shard_of(lines):
        size = lines.shape[1] // n_fsdp
        return lax.dynamic_slice_in_dim(lines, shard * size, size, axis=1)

    def in_order(sums_of, size):
        lines = sums_of.shape[1]
        by_part = sums_of.reshape(n_ctx, lines, -1, size)
        return jnp.transpose(by_part, (1, 2, 0, 3)).reshape(lines, -1)

    conv_sums = shard_of(
        jnp.concatenate(
            [
                in_order(sums[:, : taps + 1, :width], part),
                jnp.sum(sums[:, : taps + 1, width:], axis=0),
            ],
            axis=1,
        )
    )
    gate_sums = shard_of(in_order(sums[:, taps + 1 : taps + 2, :width], part))
    head_sums_all = sums[:, taps + 2, : 3 * LANES].reshape(n_ctx, 3, LANES)[:, :, :heads]
    head_grads = shard_of(in_order(head_sums_all, unit))
    norm_sums = jnp.sum(norm_sums, axis=0).reshape(1, -1)
    return (
        layer_out[None],
        hidden_grad[None],
        shard_of(norm_sums)[0],
        grad_in_weight.T,
        conv_sums[:taps],
        conv_sums[taps],
        head_grads[0],
        head_grads[1],
        head_grads[2],
        gate_sums[0],
        grad_out_weight,
    )


def solution(mesh):
    tokens, rows, flat = P("fsdp", "ctx", None), P("fsdp", None), P("fsdp")
    taps = P(None, "fsdp")
    return jax.shard_map(
        on_device,
        mesh=mesh,
        in_specs=(tokens, tokens, flat, flat, rows, taps, flat, flat, flat, flat, flat, rows),
        out_specs=(tokens, tokens, flat, rows, taps, flat, flat, flat, flat, flat, rows),
        check_vma=False,
    )
```

```python
import functools

import jax
import jax.numpy as jnp
from jax import lax
from jax.experimental import pallas as pl
from jax.experimental.pallas import tpu as pltpu
from jax.sharding import PartitionSpec as P

HEAD = 64
STATE = 128
BLOCK = 256
LANES = 128
POINTS = 8
EPS = 1e-05
F32 = jnp.float32
BF16 = jnp.bfloat16


def mm(a, b, contract=((1,), (0,))):
    return lax.dot_general(a, b, (contract, ((), ())), preferred_element_type=F32)


def mm_exact(a, b, contract=((1,), (0,))):
    return lax.dot_general(
        a, b, (contract, ((), ())), precision=lax.Precision.HIGHEST, preferred_element_type=F32
    )


def iota2(shape, axis):
    return lax.broadcasted_iota(jnp.int32, shape, axis)


def levels(lam, step):
    tri = (iota2((BLOCK, BLOCK), 0) >= iota2((BLOCK, BLOCK), 1)).astype(F32)
    level = mm_exact(tri, lam)
    across = level.T
    last = level[BLOCK - 1 : BLOCK, :]
    weight = jnp.exp(level - last) * step
    return level, across, jnp.exp(-last), weight, jnp.exp(-level)


def pair_of(array, first, low_half):
    return jnp.where(low_half, array[:, first : first + 1], array[:, first + 1 : first + 2])


def spread(level, across, head):
    return jnp.exp(-jnp.abs(level[:, head : head + 1] - across[head : head + 1, :]))


def silu_and_slope(v):
    s = jax.nn.sigmoid(v)
    return v * s, s * (1.0 + v * (1.0 - s))


def chosen_heads(me, heads, unit, n_ctx, turned=False):
    here, there = iota2((LANES, LANES), 1), iota2((LANES, LANES), 0)
    if turned:
        here, there = there, here
    head = (here // unit * n_ctx + me) * unit + here % unit
    return jnp.where(jnp.logical_and(there == head, here < heads), 1.0, 0.0).astype(BF16)


class Lines:
    def __init__(self, ref, first, rows, at, size):
        self.ref, self.first, self.at, self.shape = ref, first, at, (rows, size)

    def __getitem__(self, index):
        rows = slice(self.first, self.first + self.shape[0])
        lanes = slice(0, self.shape[1]) if index is Ellipsis else index[1]
        return self.ref[rows, self.at + lanes.start : self.at + lanes.stop]


def parameters(par_ref, width):
    lines = par_ref.shape[0] - 3
    head = par_ref[lines + 2 : lines + 3, 0 : 2 * LANES]
    return (
        Lines(par_ref, 0, lines, 0, width),
        Lines(par_ref, 0, lines, width, 2 * STATE),
        Lines(par_ref, lines, 1, 0, width),
        Lines(par_ref, lines + 1, 1, 0, width),
        head[:, :LANES],
        head[:, LANES:],
    )


def column_valid(length_ref, block):
    at = iota2((BLOCK, 1), 0) + block * BLOCK
    return (at < length_ref[0]).astype(F32)


MESH = pl.DeviceIdType.MESH
SMALL_ROWS = 32


def ring_place(index, half):
    a, b = index // 2, index % 2
    return a + b * (2 * half - 1 - 2 * a)


def ring_index(place, half):
    b = place // half
    return 2 * (place + b * (2 * half - 1 - 2 * place)) + b


class Ring:
    def __init__(self, n):
        self.n, self.half = n, n // 2
        self.me, self.shard = lax.axis_index("ctx"), lax.axis_index("fsdp")
        self.place = ring_place(self.shard, self.half)

    def at(self, steps):
        return ring_index(lax.rem(self.place + steps + 2 * self.n, self.n), self.half)

    def neighbour(self, way):
        return (self.me, self.at(1 if way == 0 else -1))


def remote(source, target, send, recv, device):
    return pltpu.make_async_remote_copy(
        src_ref=source,
        dst_ref=target,
        send_sem=send,
        recv_sem=recv,
        device_id=device,
        device_id_type=MESH,
    )


def greet(device):
    pl.semaphore_signal(pltpu.get_barrier_semaphore(), inc=1, device_id=device, device_id_type=MESH)


class Around:
    def __init__(self, me, shard):
        core, row = me % 2, me // 2
        self.me = me
        self.core_at = me + 1 - 2 * core
        self.row_at = me + 2 - 4 * row
        self.both_at = self.row_at + 1 - 2 * core
        self.core, self.row, self.both = (
            (at, shard) for at in (self.core_at, self.row_at, self.both_at)
        )
        self.all = (self.core, self.row, self.both)


class TokenSum:
    def __init__(self, around, parts, own_part, row_part, from_core, from_row, send, recv):
        self.around, self.parts, self.own_part, self.row_part = around, parts, own_part, row_part
        self.from_core, self.from_row, self.send, self.recv = from_core, from_row, send, recv

    def loads(self):
        at = self.around
        return (
            (self.parts.at[at.row_at], self.row_part),
            (self.parts.at[at.me], self.own_part),
        )

    def to_core(self, which):
        at = self.around
        return remote(
            self.parts.at[(at.core_at, at.both_at)[which]],
            self.from_core.at[which],
            self.send.at[which],
            self.recv.at[which],
            at.core,
        )

    def to_row(self):
        return remote(
            self.row_part, self.from_row, self.send.at[2], self.recv.at[2], self.around.row
        )

    def start(self):
        self.to_core(1).start()
        self.to_core(0).start()

    def pass_row(self):
        self.to_core(1).wait()
        total = self.row_part[...].astype(F32) + self.from_core[1].astype(F32)
        self.row_part[...] = total.astype(BF16)
        self.to_row().start()

    def total(self):
        self.to_core(0).wait()
        self.to_row().wait()
        return (
            self.own_part[...].astype(F32)
            + self.from_core[0].astype(F32)
            + self.from_row[...].astype(F32)
        )


class SmallSum:
    def __init__(self, n, around, whole, sums, send, recv, ctx_send, ctx_recv):
        self.n, self.around, self.whole, self.sums = n, around, whole, sums
        self.send, self.recv, self.ctx_send, self.ctx_recv = send, recv, ctx_send, ctx_recv
        self.shard = lax.axis_index("fsdp")

    def to_peer(self, offset):
        own = self.whole.at[self.shard]
        peer = (self.around.me, lax.rem(self.shard + offset, self.n))
        return remote(own, own, self.send.at[offset - 1], self.recv.at[offset - 1], peer)

    def to_ctx(self, i):
        own = self.sums.at[self.around.me]
        return remote(own, own, self.ctx_send.at[i], self.ctx_recv.at[i], self.around.all[i])

    def start(self):
        lax.fori_loop(1, self.n, lambda j, carry: (self.to_peer(j).start(), carry)[1], 0)

    def add(self):
        lax.fori_loop(1, self.n, lambda j, carry: (self.to_peer(j).wait(), carry)[1], 0)
        self.sums[self.around.me] = jnp.sum(self.whole[...], axis=0)
        for i in range(3):
            self.to_ctx(i).start()

    def finish(self):
        for i in range(3):
            self.to_ctx(i).wait()


def forward_kernel(
    heads,
    unit,
    n_ctx,
    n,
    direct,
    length_ref,
    px_ref,
    ps_ref,
    normed_ref,
    out_weight,
    w_z,
    upstream,
    par_ref,
    x_ref,
    b_ref,
    c_ref,
    slope_x_ref,
    slope_s_ref,
    lam_ref,
    step_ref,
    chain_ref,
    kept_ref,
    gain_ref,
    gate_t,
    mixed_parts,
    d_z,
    d_ssd,
    state,
    before_x,
    before_s,
    v_o,
    v_z,
    v_up,
    all_y,
    all_z,
    all_dyn,
    v_yt,
    v_mixed,
    v_dz,
    v_dssd,
    stat_all,
    columns,
    load_sem,
    store_sem,
    ring_send,
    ring_recv,
    piece_recv,
    stat_send,
    stat_recv,
):
    block = pl.program_id(0)
    blocks = pl.num_programs(0)
    ring = Ring(n)
    me, shard = ring.me, ring.shard
    around = Around(me, shard)
    width = px_ref.shape[1]
    taps_x_ref, taps_s_ref, gate_gain_ref, skip_ref, bias_step, rate = parameters(par_ref, width)
    channels = width * n_ctx
    piece, size = v_o.shape[0] // n, v_o.shape[1] // 4
    points = heads // 2 * n_ctx
    loads = [
        pltpu.make_async_copy(source, target, load_sem.at[i])
        for i, (source, target) in enumerate(((w_z, v_z), (upstream, v_up)))
    ]
    shard_rows = lambda index: pl.ds(pl.multiple_of(index * piece, 16), piece)
    own_piece = out_weight.at[pl.ds(pl.multiple_of(me * piece, 16), piece)]
    piece_peer = (shard % n_ctx, shard // n_ctx * n_ctx + me)
    moves = shard % n_ctx != me

    def hop(way, sub, step):
        at = pl.multiple_of((2 * way + sub) * size, LANES)
        place = v_o.at[shard_rows(ring.at(step * (2 * way - 1))), pl.ds(at, size)]
        return remote(
            place,
            place,
            ring_send.at[way, sub],
            ring_recv.at[way, sub, step],
            (me, ring.at(1 - 2 * way)),
        )

    def streams(body):
        lax.fori_loop(0, 4, lambda e, carry: (body(e // 2, e % 2), carry)[1], 0)

    def ring_step(step):
        def body(way, sub):
            hop(way, sub, step).wait()

            @pl.when(step < n - 2)
            def _():
                hop(way, sub, step + 1).start()

        streams(body)

    def serve(point):
        at = block * (heads // 2) + point
        lax.fori_loop(
            at * (n - 1) // points,
            (at + 1) * (n - 1) // points,
            lambda step, carry: (ring_step(step), carry)[1],
            0,
        )

    @pl.when(block == 0)
    def _():
        for device in around.all:
            greet(device)
        greet(ring.neighbour(0))
        greet(ring.neighbour(1))
        keep = pltpu.make_async_copy(own_piece, v_o.at[shard_rows(shard)], load_sem.at[2])
        if direct:
            keep.start()
            pl.semaphore_wait(pltpu.get_barrier_semaphore(), 5)
            keep.wait()
        else:
            send = remote(
                own_piece, v_o.at[shard_rows(piece_peer[1])], load_sem.at[2], piece_recv, piece_peer
            )

            @pl.when(moves)
            def _():
                greet(piece_peer)
                pl.semaphore_wait(pltpu.get_barrier_semaphore(), 6)
                send.start()
                send.wait()

            @pl.when(jnp.logical_not(moves))
            def _():
                pl.semaphore_wait(pltpu.get_barrier_semaphore(), 5)
                keep.start()
                keep.wait()

        streams(lambda way, sub: hop(way, sub, 0).start())
        for copy in loads:
            copy.start()
        state[...] = jnp.zeros_like(state)
        before_x[...] = jnp.zeros_like(before_x)
        before_s[...] = jnp.zeros_like(before_s)

    valid = column_valid(length_ref, block)
    low_half = iota2((1, LANES), 1) < HEAD
    taps = taps_x_ref.shape[0] - 1

    def conv(current, before, weight):
        padded = jnp.concatenate([before, current], axis=0)
        total = weight[taps : taps + 1]
        for k in range(taps):
            first = 8 - (taps - 1) + k
            total = total + weight[k : k + 1] * padded[first : first + BLOCK]
        return silu_and_slope(total)

    both = jnp.concatenate([ps_ref[0], ps_ref[1]], axis=1).astype(F32)
    active, slope = conv(both, before_s[...], taps_s_ref[...])
    before_s[...] = both[BLOCK - 8 :]
    slope_s_ref[...] = slope.astype(BF16)
    rows_b, rows_c = active[:, :STATE].astype(BF16), active[:, STATE:].astype(BF16)
    b_ref[...] = rows_b
    c_ref[...] = rows_c
    raw = mm(ps_ref[2], chosen_heads(me, heads, unit, n_ctx)) + bias_step
    own = iota2((1, LANES), 1) < heads
    step = jnp.where(own, valid * jax.nn.softplus(raw), 0.0)
    lam = step * rate
    step_ref[...] = step
    lam_ref[...] = lam
    chain_ref[...] = jnp.where(own, valid * jax.nn.sigmoid(raw), 0.0)

    gram = mm(rows_c, rows_b, ((1,), (1,)))
    level, across, last, weight, fade = levels(lam, step)
    kept_ref[0] = state[...].astype(BF16)
    entering = mm(rows_c, state[...].astype(BF16))
    by_state = rows_b.T
    for first in range(0, heads, 2):
        lanes = slice(first * HEAD, (first + 2) * HEAD)
        current = px_ref[:, lanes].astype(F32)
        active, slope = conv(current, before_x[:, lanes], taps_x_ref[:, lanes])
        before_x[:, lanes] = current[BLOCK - 8 :]
        slope_x_ref[:, lanes] = slope.astype(BF16)
        x_low = active.astype(BF16)
        x_ref[:, lanes] = x_low
        x = x_low.astype(F32)
        scaled = x * pair_of(step, first, low_half)
        total = pair_of(fade, first, low_half) * entering[:, lanes] + skip_ref[:, lanes] * x
        for head, keep in ((first, low_half), (first + 1, jnp.logical_not(low_half))):
            mixing = (gram * spread(level, across, head)).astype(BF16)
            total += mm(mixing, jnp.where(keep, scaled, 0.0).astype(BF16))
        all_y[block, :, lanes] = total
        update = mm(by_state, (x * pair_of(weight, first, low_half)).astype(BF16))
        state[:, lanes] = state[:, lanes] * pair_of(last, first, low_half) + update
        if first + 2 < heads:
            serve(first // 2)

    @pl.when(block == 0)
    def _():
        loads[0].wait()

    all_z[block] = mm(normed_ref[...], v_z[...]).astype(BF16)
    serve(heads // 2 - 1)

    @pl.when(block == blocks - 1)
    def _():
        loads[1].wait()
        lane = iota2((1, LANES), 1)

        def sums_of(chunk, carry):
            d_yn = column_valid(length_ref, chunk) * mm(v_up[chunk], v_o[...], ((1,), (1,)))
            all_dyn[chunk] = d_yn
            gated = all_y[chunk] * jax.nn.silu(all_z[chunk].astype(F32))
            square = jnp.sum(gated * gated, axis=1, keepdims=True)
            along = jnp.sum(gate_gain_ref[...] * d_yn * gated, axis=1, keepdims=True)
            pair = jnp.where(lane == 0, square, 0.0) + jnp.where(lane == 1, along, 0.0)
            stat_all[me, chunk] = pair.T[0:8]
            return carry

        lax.fori_loop(0, blocks, sums_of, 0)
        own_stats = stat_all.at[me]
        copies = [
            remote(own_stats, own_stats, stat_send.at[i], stat_recv.at[i], device)
            for i, device in enumerate(around.all)
        ]
        for copy in copies:
            copy.start()
        gain_ref[...] = jnp.zeros_like(gain_ref)
        for copy in copies:
            copy.wait()
        total = jnp.sum(stat_all[...], axis=0)
        for i in range(n_ctx):
            columns[i] = total[i].T

        def stores(chunk):
            slot = chunk % 2
            rows = pl.ds(pl.multiple_of(chunk * BLOCK, BLOCK), BLOCK)
            return [
                pltpu.make_async_copy(source.at[slot], target, store_sem.at[slot, i])
                for i, (source, target) in enumerate(
                    (
                        (v_yt, gate_t.at[chunk]),
                        (v_mixed, mixed_parts.at[chunk]),
                        (v_dz, d_z.at[rows]),
                        (v_dssd, d_ssd.at[rows]),
                    )
                )
            ]

        def gate_part(chunk, carry):
            slot = chunk % 2

            @pl.when(chunk >= 2)
            def _():
                for copy in stores(chunk - 2):
                    copy.wait()

            sums = columns[chunk]
            scale = lax.rsqrt(sums[:, 0:1] / channels + EPS)
            slant = scale * scale * scale * sums[:, 1:2] / channels
            here = column_valid(length_ref, chunk)
            for first in range(0, heads, 2):
                lanes = slice(first * HEAD, (first + 2) * HEAD)
                gate, gate_slope = silu_and_slope(all_z[chunk, :, lanes].astype(F32))
                mixed = all_y[chunk, :, lanes]
                d_yn = all_dyn[chunk, :, lanes]
                gain = gate_gain_ref[:, lanes]
                gated = mixed * gate
                scaled = gated * scale
                all_z[chunk, :, lanes] = (here * (scaled * gain)).astype(BF16)
                gain_ref[0:1, lanes] += jnp.sum(d_yn * scaled, axis=0, keepdims=True)
                d_gated = scale * (gain * d_yn) - gated * slant
                v_dz[slot, :, lanes] = (d_gated * mixed * gate_slope).astype(BF16)
                v_dssd[slot, :, lanes] = (d_gated * gate).astype(BF16)
            normed_gate = all_z[chunk]
            v_yt[slot] = normed_gate.T
            v_mixed[slot] = mm(normed_gate, v_o[...]).astype(BF16)
            for copy in stores(chunk):
                copy.start()
            return carry

        lax.fori_loop(0, blocks, gate_part, 0)
        for chunk in (n_ctx - 2, n_ctx - 1):
            for copy in stores(chunk):
                copy.wait()


def scan_forward(
    n, direct, unit, n_ctx, length, px, ps, normed, out_weight, w_z, upstream, par
):
    tokens, width = px.shape
    heads = width // HEAD
    count = tokens // BLOCK
    model = out_weight.shape[1]
    assert count == n_ctx
    by_block = lambda i: (i, 0)
    at_block = lambda size: pl.BlockSpec((BLOCK, size), by_block)
    whole = lambda a: pl.BlockSpec(a.shape, lambda i: (0, 0))
    any_space = pl.BlockSpec(memory_space=pl.ANY)
    low = lambda *shape: jax.ShapeDtypeStruct(shape, BF16)
    full = lambda *shape: jax.ShapeDtypeStruct(shape, F32)
    v_low = lambda *shape: pltpu.VMEM(shape, BF16)
    v_full = lambda *shape: pltpu.VMEM(shape, F32)
    dma = pltpu.SemaphoreType.DMA
    return pl.pallas_call(
        functools.partial(forward_kernel, heads, unit, n_ctx, n, direct),
        grid=(count,),
        in_specs=[
            pl.BlockSpec(memory_space=pltpu.SMEM),
            at_block(width),
            pl.BlockSpec((n_ctx, BLOCK, LANES), lambda i: (0, i, 0)),
            at_block(model),
            any_space,
            any_space,
            any_space,
        ]
        + [whole(par)],
        out_specs=[
            at_block(width),
            at_block(STATE),
            at_block(STATE),
            at_block(width),
            at_block(2 * STATE),
            at_block(LANES),
            at_block(LANES),
            at_block(LANES),
            pl.BlockSpec((1, STATE, width), lambda i: (i, 0, 0)),
            pl.BlockSpec((8, width), lambda i: (0, 0)),
            any_space,
            any_space,
            any_space,
            any_space,
        ],
        out_shape=[
            low(tokens, width),
            low(tokens, STATE),
            low(tokens, STATE),
            low(tokens, width),
            low(tokens, 2 * STATE),
            full(tokens, LANES),
            full(tokens, LANES),
            full(tokens, LANES),
            low(count, STATE, width),
            full(8, width),
            low(count, width, BLOCK),
            low(count, BLOCK, model),
            low(tokens, width),
            low(tokens, width),
        ],
        scratch_shapes=[
            v_full(STATE, width),
            v_full(8, width),
            v_full(8, 2 * STATE),
            v_low(width, model),
            v_low(*w_z.shape),
            v_low(count, BLOCK, model),
            v_full(count, BLOCK, width),
            v_low(count, BLOCK, width),
            v_full(count, BLOCK, width),
            v_low(2, width, BLOCK),
            v_low(2, BLOCK, model),
            v_low(2, BLOCK, width),
            v_low(2, BLOCK, width),
            v_full(n_ctx, count, 8, BLOCK),
            v_full(count, BLOCK, 8),
            dma((3,)),
            dma((2, 4)),
            dma((2, 2)),
            dma((2, 2, n - 1)),
            dma,
            dma((3,)),
            dma((3,)),
        ],
        compiler_params=pltpu.CompilerParams(
            collective_id=2, has_side_effects=True, vmem_limit_bytes=58 * 1024 * 1024
        ),
        name="scan_forward",
    )(length, px, ps, normed, out_weight, w_z, upstream, par)


def head_sums(product, chooser):
    high = product.astype(BF16)
    rest = (product - high.astype(F32)).astype(BF16)
    return mm(high, chooser) + mm(rest, chooser)


def backward_kernel(
    heads,
    unit,
    n_ctx,
    n,
    px_ref,
    ps_ref,
    x_ref,
    b_ref,
    c_ref,
    slope_x_ref,
    slope_s_ref,
    lam_ref,
    step_ref,
    chain_ref,
    kept_ref,
    dssd_ref,
    gate_t,
    normed_t,
    upstream,
    d_z,
    mixed_parts,
    hidden,
    gain_grads_ref,
    par_ref,
    dx_ref,
    small_ref,
    d_s,
    shard_o,
    shard_z,
    layer_out,
    back,
    mixed_grads,
    for_step,
    for_level,
    left,
    right,
    sums,
    after_x,
    after_s,
    v_left,
    v_right,
    products,
    slots,
    stage,
    done_o,
    done_z,
    mine,
    from_core,
    from_row,
    shared_parts,
    shared_core,
    shared_row,
    v_hidden,
    load_sem,
    store_sem,
    ring_send,
    ring_recv,
    part_send,
    part_recv,
    shared_send,
    shared_recv,
):
    turn = pl.program_id(0)
    turns = heads // 2 // POINTS
    block = pl.num_programs(0) - 1 - turn
    width, model = x_ref.shape[1], v_hidden.shape[1]
    taps_x_ref, taps_s_ref, _, skip_ref, _, rate = parameters(par_ref, width)
    own = hidden.shape[0]
    ring = Ring(n)
    around = Around(ring.me, ring.shard)
    piece, size = slots.shape[4], slots.shape[5]
    sum_mixed = TokenSum(
        around, mixed_parts, mine.at[0], mine.at[1], from_core, from_row, part_send, part_recv
    )
    sum_shared = TokenSum(
        around,
        shared_parts,
        shared_parts.at[ring.me],
        shared_parts.at[around.row_at],
        shared_core,
        shared_row,
        shared_send,
        shared_recv,
    )
    loads = [
        pltpu.make_async_copy(source, target, load_sem.at[i])
        for i, (source, target) in enumerate(
            (
                *((gate_t.at[c], v_left.at[pl.ds(0, width), pl.ds(c * own, own)]) for c in range(n_ctx)),
                *((upstream.at[c], v_right.at[pl.ds(c * own, own), pl.ds(0, model)]) for c in range(n_ctx)),
                *((normed_t.at[c], v_left.at[pl.ds(width, model), pl.ds(c * own, own)]) for c in range(n_ctx)),
                (d_z, v_right.at[:, pl.ds(model, width)]),
                *sum_mixed.loads(),
                (hidden, v_hidden),
            )
        )
    ]
    ring_loads = 1 + 3 * n_ctx

    def partial_sum(kind, way, sub, index):
        first = (1 - kind) * index * piece + kind * (width + (2 * index + way) * piece)
        at = (1 - kind) * (2 * way + sub) * size + kind * (model + sub * size)
        return mm(
            v_left[pl.ds(pl.multiple_of(first, 16), piece), :],
            v_right[:, pl.ds(pl.multiple_of(at, LANES), size)],
        )

    def all_products():
        tile = max(2 * piece, BLOCK)
        shards = tile // (2 * piece)

        def out_rows(i, carry):
            rows = pl.ds(pl.multiple_of(i * BLOCK, BLOCK), BLOCK)
            left = v_left[rows, :]
            products[rows, 0:width] = mm(left, v_right[:, 0:width]).astype(BF16)
            products[rows, width:model] = mm(left, v_right[:, width:model]).astype(BF16)
            return carry

        def in_rows(i, carry):
            left = v_left[pl.ds(pl.multiple_of(width + i * tile, 16), tile), :]
            both = mm(left, v_right[:, model:]).astype(BF16)
            for j in range(shards):
                place = pl.ds(pl.multiple_of((i * shards + j) * piece, 16), piece)
                for way in (0, 1):
                    products[place, model + way * width : model + (way + 1) * width] = both[
                        (2 * j + way) * piece : (2 * j + way + 1) * piece
                    ]
            return carry

        lax.fori_loop(0, width // BLOCK, out_rows, 0)
        lax.fori_loop(0, model // tile, in_rows, 0)

    def product(kind, way, sub, index):
        at = pl.multiple_of(kind * model + way * width + sub * size, LANES)
        return products[pl.ds(pl.multiple_of(index * piece, 16), piece), pl.ds(at, size)]

    def hop(kind, way, sub, step, source):
        return remote(
            source,
            slots.at[kind, step, way, sub],
            ring_send.at[kind, way, sub],
            ring_recv.at[kind, way, sub, step],
            (ring.me, ring.at(1 - 2 * way)),
        )

    def streams(body):
        def one(e, carry):
            body(e // 4, e // 2 % 2, e % 2)
            return carry

        lax.fori_loop(0, 8, one, 0)

    def start_ring(kind, way, sub):
        place = stage.at[kind, way, sub]
        place[...] = partial_sum(kind, way, sub, ring.at(2 * way - 1)).astype(BF16)
        hop(kind, way, sub, 0, place).start()

    def ring_step(step):
        def body(kind, way, sub):
            index = ring.at((step + 2) * (2 * way - 1))
            hop(kind, way, sub, step, stage.at[kind, way, sub]).wait()
            place = slots.at[kind, step, way, sub]
            total = place[...].astype(F32) + product(kind, way, sub, index).astype(F32)

            @pl.when(step < n - 2)
            def _():
                place[...] = total.astype(BF16)
                hop(kind, way, sub, step + 1, place).start()

            @pl.when(jnp.logical_and(step == n - 2, kind == 0))
            def _():
                at = pl.multiple_of((2 * way + sub) * size, LANES)
                done_o[:, pl.ds(at, size)] = total.astype(BF16)

            @pl.when(jnp.logical_and(step == n - 2, kind == 1))
            def _():
                done_z[way, pl.ds(pl.multiple_of(sub * size, 16), size), :] = total.T.astype(BF16)

        streams(body)

    def serve(point):
        at = turn * POINTS + point
        points = POINTS * n_ctx
        lax.fori_loop(
            at * (n - 1) // points,
            (at + 1) * (n - 1) // points,
            lambda step, carry: (ring_step(step), carry)[1],
            0,
        )

    @pl.when(turn == 0)
    def _():
        for device in around.all:
            greet(device)
        greet(ring.neighbour(0))
        greet(ring.neighbour(1))
        for copy in loads:
            copy.start()
        for c in range(3, n_ctx):
            shared_parts[c] = jnp.zeros(shared_parts.shape[1:], BF16)
        back[...] = jnp.zeros_like(back)
        small_ref[...] = jnp.zeros_like(small_ref)
        small_ref[taps_x_ref.shape[0] : taps_x_ref.shape[0] + 1, 0:width] = gain_grads_ref[0:1, :]
        after_x[...] = jnp.zeros_like(after_x)
        after_s[...] = jnp.zeros_like(after_s)
        pl.semaphore_wait(pltpu.get_barrier_semaphore(), 5)
        for copy in loads[:ring_loads]:
            copy.wait()
        streams(start_ring)
        sum_mixed.start()
        all_products()
        for copy in loads[ring_loads:]:
            copy.wait()

    @pl.when(turn == 1)
    def _():
        sum_mixed.pass_row()

    taps = taps_x_ref.shape[0] - 1

    rows_b, rows_c = b_ref[...], c_ref[...]
    step = step_ref[...]
    lam = lam_ref[...]
    gram = mm(rows_c, rows_b, ((1,), (1,)))
    gram_t = mm(rows_b, rows_c, ((1,), (1,)))
    level, across, last, weight, fade = levels(lam, step)
    out_decay = jnp.exp(level - level[BLOCK - 1 : BLOCK, :])
    step_across = step.T
    at_row, at_col = iota2((BLOCK, BLOCK), 0), iota2((BLOCK, BLOCK), 1)
    order = (at_row > at_col).astype(F32) - (at_row < at_col).astype(F32)
    low_half = iota2((1, LANES), 1) < HEAD
    lane = iota2((1, LANES), 1)
    by_state = rows_c.T
    kept = kept_ref[0]
    old_back = back[...].astype(BF16)
    entering = mm(rows_c, kept)
    leaving = mm(rows_b, old_back)
    at_last = jnp.sum(kept.astype(F32) * back[...], axis=0, keepdims=True)
    mixed_grads[...] = jnp.zeros_like(mixed_grads)
    left[...] = jnp.zeros_like(left)
    right[...] = jnp.zeros_like(right)
    sums[...] = jnp.zeros_like(sums)
    d_b = jnp.zeros((BLOCK, STATE), F32)
    d_c = jnp.zeros((BLOCK, STATE), F32)

    def conv_back(d_conv, after, current, weight):
        padded = jnp.concatenate([d_conv, after], axis=0)
        d_in = jnp.zeros_like(d_conv)
        grads = []
        for k in range(taps):
            moved = padded[taps - 1 - k : taps - 1 - k + BLOCK]
            d_in += weight[k : k + 1] * moved
            grads.append(jnp.sum(current * moved, axis=0, keepdims=True))
        grads.append(jnp.sum(d_conv, axis=0, keepdims=True))
        return d_in, jnp.concatenate(grads, axis=0)

    for first in range(0, heads, 2):
        lanes = slice(first * HEAD, (first + 2) * HEAD)
        x_low = x_ref[:, lanes]
        x = x_low.astype(F32)
        grad_low = dssd_ref[:, lanes]
        grad = grad_low.astype(F32)
        through = jnp.zeros((BLOCK, LANES), F32)
        for head, keep in ((first, low_half), (first + 1, jnp.logical_not(low_half))):
            decay = spread(level, across, head)
            grad_own = jnp.where(keep, grad, 0.0).astype(BF16)
            pairs = mm(grad_own, x_low, ((1,), (1,)))
            through += mm((gram_t * decay).astype(BF16), grad_own)
            scaled = decay * pairs * step_across[head : head + 1, :]
            mixed_grads[...] += scaled
            ordered = gram * scaled * order
            left[...] = jnp.where(
                lane == head, jnp.sum(ordered, axis=1, keepdims=True), left[...]
            )
            right[head : head + 1, :] = jnp.sum(ordered, axis=0, keepdims=True)
        weight_pair = pair_of(weight, first, low_half)
        step_pair = pair_of(step, first, low_half)
        fade_pair = pair_of(fade, first, low_half)
        out_pair = pair_of(out_decay, first, low_half)
        leave = leaving[:, lanes]
        d_x = step_pair * through + weight_pair * leave + skip_ref[:, lanes] * grad
        for_step[:, lanes] = x * (through + out_pair * leave)
        weighted = weight_pair * x
        faded = fade_pair * grad
        for_level[:, lanes] = weighted * leave - faded * entering[:, lanes]
        sums[0:1, lanes] = jnp.sum(weighted * leave, axis=0, keepdims=True)
        sums[2:3, lanes] = jnp.sum(x * grad, axis=0, keepdims=True)
        faded_low = faded.astype(BF16)
        d_b += mm(weighted.astype(BF16), old_back[:, lanes], ((1,), (1,)))
        d_c += mm(faded_low, kept[:, lanes], ((1,), (1,)))
        back[:, lanes] = back[:, lanes] * pair_of(last, first, low_half) + mm(by_state, faded_low)
        d_conv = d_x * slope_x_ref[:, lanes].astype(F32)
        d_in, grads = conv_back(
            d_conv, after_x[:, lanes], px_ref[:, lanes].astype(F32), taps_x_ref[:, lanes]
        )
        after_x[:, lanes] = d_conv[0:8]
        dx_ref[:, lanes] = d_in.astype(BF16)
        small_ref[0 : taps + 1, lanes] += grads
        if first // 2 % turns == turns - 1 and first // 2 // turns < POINTS - 1:
            serve(first // 2 // turns)

    all_pairs = mixed_grads[...]
    d_b = d_b + mm(all_pairs.T.astype(BF16), rows_c)
    d_c = d_c + mm(all_pairs.astype(BF16), rows_b)
    both = jnp.concatenate([ps_ref[0], ps_ref[1]], axis=1).astype(F32)
    d_conv = jnp.concatenate([d_b, d_c], axis=1) * slope_s_ref[...].astype(F32)
    d_in, grads = conv_back(
        d_conv, after_s[...], both, taps_s_ref[...]
    )
    after_s[...] = d_conv[0:8]
    here = pl.ds(pl.multiple_of(block * BLOCK, BLOCK), BLOCK)
    shared_parts[0, here, :] = d_in[:, :STATE].astype(BF16)
    shared_parts[1, here, :] = d_in[:, STATE:].astype(BF16)
    small_ref[0 : taps + 1, width:] += grads

    chooser = (iota2((width, LANES), 0) // HEAD == iota2((width, LANES), 1)).astype(BF16)
    d_step = head_sums(for_step[...], chooser)
    sums[1:2, :] = at_last
    total = head_sums(sums[...], chooser)
    d_level = head_sums(for_level[...], chooser) - left[...] + right[...].T
    final = -total[0:1, :] - last * total[1:2, :]
    d_level = d_level + jnp.where(iota2((BLOCK, 1), 0) == BLOCK - 1, final, 0.0)
    d_lam = mm_exact((at_row <= at_col).astype(F32), d_level)
    d_raw = (d_step + d_lam * rate) * chain_ref[...]
    head_row = taps + 2
    small_ref[head_row : head_row + 1, 0:LANES] += jnp.sum(d_raw, axis=0, keepdims=True)
    small_ref[head_row : head_row + 1, LANES : 2 * LANES] += jnp.sum(
        d_lam * lam, axis=0, keepdims=True
    )
    small_ref[head_row : head_row + 1, 2 * LANES : 3 * LANES] += total[2:3, :]
    chosen = chosen_heads(lax.axis_index("ctx"), heads, unit, n_ctx, True)
    shared_parts[2, here, :] = mm(d_raw.astype(BF16), chosen).astype(BF16)

    @pl.when(turn == pl.num_programs(0) - 1)
    def _():
        sum_shared.start()
        sum_shared.pass_row()


    serve(POINTS - 1)

    @pl.when(turn == pl.num_programs(0) - 1)
    def _():
        stores = [
            pltpu.make_async_copy(source, target, store_sem.at[i])
            for i, (source, target) in enumerate(
                (
                    (done_o, shard_o),
                    (done_z, shard_z),
                    (v_hidden, layer_out),
                    (shared_parts.at[ring.me], d_s),
                )
            )
        ]
        stores[0].start()
        stores[1].start()
        v_hidden[...] = (v_hidden[...].astype(F32) + sum_mixed.total()).astype(BF16)
        stores[2].start()
        shared_parts[ring.me] = sum_shared.total().astype(BF16)
        stores[3].start()
        for copy in stores:
            copy.wait()


def scan_backward(
    n, unit, n_ctx, px, ps, kept_parts, d_ssd, gate_t, normed_t, upstream, d_z, mixed_parts, hidden, gain_grads, par
):
    x, rows_b, rows_c, slope_x, slope_s, lam, step, chain, kept = kept_parts
    tokens, width = px.shape
    heads = width // HEAD
    count = tokens // BLOCK
    own, model = hidden.shape
    piece = width // n
    assert model == 2 * width and heads // 2 % POINTS == 0
    by_block = lambda i: (count - 1 - i, 0)
    at_block = lambda size: pl.BlockSpec((BLOCK, size), by_block)
    whole = lambda a: pl.BlockSpec(a.shape, lambda i: (0, 0))
    any_space = pl.BlockSpec(memory_space=pl.ANY)
    low = lambda *shape: jax.ShapeDtypeStruct(shape, BF16)
    v_low = lambda *shape: pltpu.VMEM(shape, BF16)
    v_full = lambda *shape: pltpu.VMEM(shape, F32)
    part = lambda a, b: pl.BlockSpec((1, a, b), lambda i: (count - 1 - i, 0, 0))
    small_shape = (8, width + 2 * STATE)
    dma = pltpu.SemaphoreType.DMA
    return pl.pallas_call(
        functools.partial(backward_kernel, heads, unit, n_ctx, n),
        grid=(count,),
        in_specs=[
            at_block(width),
            pl.BlockSpec((n_ctx, BLOCK, LANES), lambda i: (0, count - 1 - i, 0)),
            at_block(width),
            at_block(STATE),
            at_block(STATE),
            at_block(width),
            at_block(2 * STATE),
            at_block(LANES),
            at_block(LANES),
            at_block(LANES),
            part(STATE, width),
            at_block(width),
        ]
        + [any_space] * 6
        + [whole(a) for a in (gain_grads, par)],
        out_specs=[
            at_block(width),
            pl.BlockSpec(small_shape, lambda i: (0, 0)),
            any_space,
            any_space,
            any_space,
            any_space,
        ],
        out_shape=[
            low(tokens, width),
            jax.ShapeDtypeStruct(small_shape, F32),
            low(tokens, LANES),
            low(piece, model),
            low(2, width, piece),
            low(own, model),
        ],
        scratch_shapes=[
            v_full(STATE, width),
            v_full(BLOCK, BLOCK),
            v_full(BLOCK, width),
            v_full(BLOCK, width),
            v_full(BLOCK, LANES),
            v_full(LANES, BLOCK),
            v_full(8, width),
            v_full(8, width),
            v_full(8, 2 * STATE),
            v_low(width + model, tokens),
            v_low(tokens, model + width),
            v_low(width, 2 * model),
            v_low(2, n - 1, 2, 2, piece, width // 2),
            v_low(2, 2, 2, piece, width // 2),
            v_low(piece, model),
            v_low(2, width, piece),
            v_low(2, own, model),
            v_low(2, own, model),
            v_low(own, model),
            v_low(n_ctx, tokens, LANES),
            v_low(2, tokens, LANES),
            v_low(tokens, LANES),
            v_low(own, model),
            dma((4 + 3 * n_ctx,)),
            dma((4,)),
            dma((2, 2, 2)),
            dma((2, 2, 2, n - 1)),
            dma((3,)),
            dma((3,)),
            dma((3,)),
            dma((3,)),
        ],
        compiler_params=pltpu.CompilerParams(
            collective_id=3, has_side_effects=True, vmem_limit_bytes=59 * 1024 * 1024
        ),
        name="scan_backward",
    )(
        px, ps, x, rows_b, rows_c, slope_x, slope_s, lam, step, chain, kept, d_ssd, gate_t, normed_t, upstream, d_z, mixed_parts, hidden, gain_grads, par
    )


def gather_kernel(
    n,
    n_ctx,
    unit,
    taps,
    sizes,
    hidden,
    cotangent,
    in_weight_t,
    small,
    cotangent_all,
    w_x,
    w_s,
    w_z,
    par_out,
    gain_out,
    proj_x,
    proj_s,
    normed_out,
    normed_t,
    v_hidden,
    v_normed,
    v_x,
    v_s,
    own_z,
    v_small,
    raw_x,
    raw_s,
    raw_z,
    out_x,
    out_s,
    out_t,
    v_gain,
    v_par,
    conv_lines,
    gate_line,
    head_lines,
    load_sem,
    shared_sem,
    column_sem,
    local_sem,
    keep_sem,
    store_sem,
    ring_send,
    ring_recv,
    ctx_send,
    ctx_recv,
):
    ring = Ring(n)
    me, shard = ring.me, ring.shard
    width, model = v_x.shape[1], v_x.shape[0]
    inner = width * n_ctx
    r = model // n
    shared = in_weight_t.shape[0] - 2 * inner
    row = me // 2
    other_core = (me + 1 - 2 * (me % 2), shard)
    other_row = (me + 2 - 4 * row, shard)
    barrier = pltpu.get_barrier_semaphore()
    for device in (other_core, other_row, ring.neighbour(0), ring.neighbour(1)):
        pl.semaphore_signal(barrier, inc=1, device_id=device, device_id_type=MESH)

    part = unit * HEAD

    def load_columns(base, target, sems):
        return [
            pltpu.make_async_copy(
                in_weight_t.at[pl.ds(pl.multiple_of(base + (a * n_ctx + me) * part, 16), part)],
                target.at[pl.ds(a * part, part)],
                sems.at[a],
            )
            for a in range(width // part)
        ]

    loads = [
        load_columns(inner, raw_x, column_sem.at[0]),
        [],
        [pltpu.make_async_copy(small, v_small.at[shard], load_sem.at[1])],
        [pltpu.make_async_copy(hidden, v_hidden.at[me], load_sem.at[2])],
        load_columns(0, raw_z, column_sem.at[1]),
    ]
    raw_s[...] = jnp.zeros_like(raw_s)

    def load_shared(wait):
        for j in (0, 1):
            first = me * LANES + j * HEAD

            @pl.when(first < shared)
            def _():
                copy = pltpu.make_async_copy(
                    in_weight_t.at[pl.ds(pl.multiple_of(2 * inner + first, HEAD), HEAD)],
                    raw_s.at[pl.ds(j * HEAD, HEAD)],
                    shared_sem.at[j],
                )
                copy.wait() if wait else copy.start()

    load_shared(False)
    for copies in loads:
        for copy in copies:
            copy.start()

    def loaded(i):
        for copy in loads[i]:
            copy.wait()

    pl.semaphore_wait(barrier, 4)

    half = width // 2
    rows = r // 2
    both_rows = lambda index, way: pl.ds(pl.multiple_of((2 * index + way) * rows, 16), rows)
    x_part = lambda a, sub: lambda index, way: a.at[both_rows(index, way), pl.ds(sub * half, half)]
    s_part = lambda index, way: v_s.at[both_rows(index, way)]
    small_part = lambda index, way: v_small.at[index, pl.ds(way * SMALL_ROWS // 2, SMALL_ROWS // 2)]
    phases = (
        ((0, small_part), (1, s_part), (2, x_part(v_x, 0)), (3, x_part(v_x, 1))),
        ((4, x_part(w_z, 0)), (5, x_part(w_z, 1))),
    )

    def hop(stream, way, step):
        number, part = stream
        place = part(ring.at(-step if way == 0 else step), way)
        return remote(
            place, place, ring_send.at[number, way], ring_recv.at[number, way, step],
            ring.neighbour(way),
        )

    def arrives(stream, way, step):
        number, part = stream
        landed = part(ring.at(-step - 1 if way == 0 else step + 1), way)
        return remote(
            landed, landed, ring_send.at[number, way], ring_recv.at[number, way, step],
            ring.neighbour(way),
        )

    def start_stream(stream):
        for way in (0, 1):
            hop(stream, way, 0).start()

    def to_row(i, a, whole):
        return remote(a, whole.at[me], ctx_send.at[i, 0], ctx_recv.at[i, 0], other_row)

    def to_core(i, a, whole):
        return remote(a, whole.at[me], ctx_send.at[i, 1], ctx_recv.at[i, 1], other_core)

    def pass_on(i, whole):
        beyond = whole.at[other_row[0]]
        return remote(beyond, beyond, ctx_send.at[i, 2], ctx_recv.at[i, 2], other_core)

    to_row(0, hidden, v_hidden).start()
    to_core(0, hidden, v_hidden).start()
    own_rows = pl.ds(pl.multiple_of(shard * r, 16), r)
    loaded(2)
    start_stream(phases[0][0])
    loaded(0)
    v_x[own_rows, :] = raw_x[...].T
    start_stream(phases[0][2])
    start_stream(phases[0][3])
    load_shared(True)
    v_s[own_rows, :] = raw_s[...].T
    start_stream(phases[0][1])
    keep_cotangent = pltpu.make_async_copy(cotangent, cotangent_all.at[me], local_sem)
    keep_cotangent.start()
    keep_shared = pltpu.make_async_copy(out_s, proj_s.at[me], shared_sem.at[2])
    loaded(3)
    loaded(4)
    own_z[...] = raw_z[...].T
    keep_z = pltpu.make_async_copy(own_z, w_z.at[own_rows], keep_sem)
    keep_z.start()
    keep_z.wait()

    def run_phase(number, work, after):
        def body(step, carry):
            for stream in phases[number]:
                for way in (0, 1):
                    arrives(stream, way, step).wait_recv()
                    hop(stream, way, step).wait_send()
                    hop(stream, way, step + 1).start()
            if work is not None:

                @pl.when(step < n_ctx)
                def _():
                    work(step)

                @pl.when(step == n_ctx - 1)
                def _():
                    to_row(2, out_s, proj_s).start()
                    to_core(2, out_s, proj_s).start()
                    keep_shared.start()

            return carry

        lax.fori_loop(0, n - 2, body, 0)
        after()
        for stream in phases[number]:
            for way in (0, 1):
                arrives(stream, way, n - 2).wait_recv()
                hop(stream, way, n - 2).wait_send()

    tokens = v_hidden.shape[1]

    def project_first(chunk):
        at = pl.ds(pl.multiple_of(chunk * tokens, tokens), tokens)
        resid = v_hidden[chunk].astype(F32)
        scale = lax.rsqrt(jnp.mean(resid * resid, axis=1, keepdims=True) + EPS)
        normed = (resid * scale * v_gain[...]).astype(BF16)
        v_normed[at, :] = normed
        out_x[at, :] = mm(normed, v_x[...]).astype(BF16)
        out_s[at, :] = mm(normed, v_s[...]).astype(BF16)
        out_t[chunk] = normed.T

    stores = [
        pltpu.make_async_copy(source, target, store_sem.at[i])
        for i, (source, target) in enumerate(
            (
                (v_x, w_x),
                (v_s, w_s),
                (v_par, par_out),
                (v_gain, gain_out),
                (out_x, proj_x),
                (v_normed, normed_out),
                (out_t, normed_t),
            )
        )
    ]

    def after_first():
        for stream in phases[1]:
            start_stream(stream)
        to_row(0, hidden, v_hidden).wait_recv()
        pass_on(0, v_hidden).start()
        to_row(1, cotangent, cotangent_all).start()
        to_core(1, cotangent, cotangent_all).start()
        to_row(0, hidden, v_hidden).wait_send()
        to_core(0, hidden, v_hidden).wait()
        pass_on(0, v_hidden).wait()

    def after_second():
        to_row(1, cotangent, cotangent_all).wait_recv()
        pass_on(1, cotangent_all).start()
        to_row(2, out_s, proj_s).wait_recv()
        pass_on(2, proj_s).start()
        for copy in stores[4:]:
            copy.start()

    run_phase(0, None, after_first)
    gain_size, conv_size, gate_size, held = sizes
    head_lines[...] = jnp.zeros_like(head_lines)
    for f in range(n):
        v_gain[:, f * r : (f + 1) * r] = v_small[f, 0:1, 0:r].astype(F32)
        conv_lines[0 : taps + 1, f * conv_size : (f + 1) * conv_size] = v_small[
            f, 1 : taps + 2, 0:conv_size
        ].astype(F32)
        gate_line[:, f * gate_size : (f + 1) * gate_size] = v_small[
            f, taps + 2 : taps + 3, 0:gate_size
        ].astype(F32)
        for k in range(3):
            head_lines[k : k + 1, f * held : (f + 1) * held] = v_small[
                f, taps + 3 : taps + 4, k * held : (k + 1) * held
            ].astype(F32)

    def own_part(line, a):
        at = (a * n_ctx + me) * part
        span = max(part, LANES)
        found = line[:, pl.ds(pl.multiple_of(at // LANES * LANES, LANES), span)]
        if part < LANES:
            found = pltpu.roll(found, lax.rem(LANES - at % LANES, LANES), 1)
        return found[:, 0:part]

    v_par[...] = jnp.zeros_like(v_par)
    for a in range(width // part):
        v_par[0 : taps + 1, a * part : (a + 1) * part] = own_part(conv_lines, a)[0 : taps + 1]
        v_par[taps + 1 : taps + 2, a * part : (a + 1) * part] = own_part(gate_line, a)
    v_par[0 : taps + 1, width:] = conv_lines[0 : taps + 1, inner:]
    lines = mm(head_lines[...].astype(BF16), chosen_heads(me, width // HEAD, unit, n_ctx))
    heads_row = taps + 3
    v_par[heads_row : heads_row + 1, 0:LANES] = lines[0:1]
    v_par[heads_row : heads_row + 1, LANES : 2 * LANES] = jnp.exp(lines[1:2])
    wide = (iota2((LANES, width), 1) // HEAD == iota2((LANES, width), 0)).astype(BF16)
    v_par[taps + 2 : taps + 3, 0:width] = mm(lines.astype(BF16), wide)[2:3]
    for copy in stores[0:4]:
        copy.start()
    run_phase(1, project_first, after_second)
    to_row(1, cotangent, cotangent_all).wait_send()
    to_core(1, cotangent, cotangent_all).wait()
    pass_on(1, cotangent_all).wait()
    keep_cotangent.wait()
    to_row(2, out_s, proj_s).wait_send()
    to_core(2, out_s, proj_s).wait()
    pass_on(2, proj_s).wait()
    keep_shared.wait()
    for copy in stores:
        copy.wait()


def gather_all(n, n_ctx, unit, taps, sizes, width, hidden, cotangent, in_weight_t, small):
    own, model = hidden.shape
    tokens = own * n_ctx
    rows = in_weight_t.shape[1]
    any_space = pl.BlockSpec(memory_space=pl.ANY)
    par_shape = (taps + 4, width + 2 * STATE)
    inner = width * n_ctx
    low = lambda *shape: jax.ShapeDtypeStruct(shape, BF16)
    v_low = lambda *shape: pltpu.VMEM(shape, BF16)
    dma = pltpu.SemaphoreType.DMA
    return pl.pallas_call(
        functools.partial(gather_kernel, n, n_ctx, unit, taps, sizes),
        in_specs=[any_space] * 4,
        out_specs=[any_space] * 10,
        out_shape=[
            low(n_ctx, own, model),
            low(model, width),
            low(model, LANES),
            low(model, width),
            jax.ShapeDtypeStruct(par_shape, F32),
            jax.ShapeDtypeStruct((1, model), F32),
            low(tokens, width),
            low(n_ctx, tokens, LANES),
            low(tokens, model),
            low(n_ctx, model, own),
        ],
        scratch_shapes=[
            v_low(n_ctx, own, model),
            v_low(tokens, model),
            v_low(model, width),
            v_low(model, LANES),
            v_low(rows, width),
            v_low(n, small.shape[0], small.shape[1]),
            v_low(width, rows),
            v_low(LANES, rows),
            v_low(width, rows),
            v_low(tokens, width),
            v_low(tokens, LANES),
            v_low(n_ctx, model, own),
            pltpu.VMEM((1, model), F32),
            pltpu.VMEM(par_shape, F32),
            pltpu.VMEM((8, inner + 2 * STATE), F32),
            pltpu.VMEM((1, inner), F32),
            pltpu.VMEM((8, LANES), F32),
            dma((3,)),
            dma((3,)),
            dma((2, width // (unit * HEAD))),
            dma,
            dma,
            dma((7,)),
            dma((6, 2)),
            dma((6, 2, n - 1)),
            dma((3, 3)),
            dma((3, 3)),
        ],
        compiler_params=pltpu.CompilerParams(
            collective_id=0, has_side_effects=True, vmem_limit_bytes=56 * 1024 * 1024
        ),
        name="gather_all",
    )(hidden, cotangent, in_weight_t, small)


def reduce_kernel(
    n,
    n_ctx,
    direct,
    normed_t,
    d_z,
    d_x,
    d_s,
    w_z,
    w_x,
    w_s,
    shard_o,
    shard_z,
    small,
    hidden,
    cotangent,
    gain,
    g_z,
    g_x,
    g_s,
    g_o,
    hidden_grad,
    small_out,
    norm_out,
    v_normed_t,
    v_d_z,
    v_d_x,
    v_d_s,
    v_z,
    v_x,
    v_s,
    parts,
    partials,
    slots,
    stage,
    done,
    moved,
    from_core,
    from_row,
    v_hidden,
    v_cotangent,
    v_gain,
    small_all,
    small_ctx,
    norm_all,
    norm_ctx,
    load_sem,
    store_sem,
    ring_send,
    ring_recv,
    ctx_send,
    ctx_recv,
    own_sem,
    piece_send,
    piece_recv,
    part_send,
    part_recv,
    small_send,
    small_recv,
    small_ctx_send,
    small_ctx_recv,
):
    ring = Ring(n)
    me, shard = ring.me, ring.shard
    around = Around(me, shard)
    core, row = me % 2, me // 2
    piece_peer = (shard % n_ctx, shard // n_ctx * n_ctx + me)
    moves = shard % n_ctx != me
    barrier = pltpu.get_barrier_semaphore()
    for device in around.all:
        greet(device)
    lax.fori_loop(1, n, lambda j, carry: (greet((me, lax.rem(shard + j, n))), carry)[1], 0)
    own = hidden.shape[0]
    sum_normed = TokenSum(
        around, parts, parts.at[me], parts.at[around.row_at], from_core, from_row, part_send, part_recv
    )
    sum_small, sum_norm = (
        SmallSum(
            n, around, whole, sums, small_send.at[i], small_recv.at[i], small_ctx_send.at[i], small_ctx_recv.at[i]
        )
        for i, (whole, sums) in enumerate(((small_all, small_ctx), (norm_all, norm_ctx)))
    )
    loads = [
        pltpu.make_async_copy(source, target, load_sem.at[i])
        for i, (source, target) in enumerate(
            (
                *((normed_t.at[c], v_normed_t.at[:, pl.ds(c * own, own)]) for c in range(n_ctx)),
                (d_s, v_d_s),
                (d_x, v_d_x),
                (small, small_all.at[shard]),
                (d_z, v_d_z),
                (w_z, v_z),
                (w_x, v_x),
                (w_s, v_s),
                (hidden, v_hidden),
                (cotangent, v_cotangent),
                (gain, v_gain),
            )
        )
    ]
    ring_loads = n_ctx + 2
    for copy in loads:
        copy.start()
    if direct:
        pl.semaphore_wait(barrier, n + 2)
    else:

        @pl.when(moves)
        def _():
            greet(piece_peer)
            pl.semaphore_wait(barrier, n + 3)

        @pl.when(jnp.logical_not(moves))
        def _():
            pl.semaphore_wait(barrier, n + 2)

    rows = v_normed_t.shape[0] // (2 * n)
    half, last = v_d_x.shape[1] // 2, v_d_s.shape[1]
    streams = (
        (0, v_d_s, 0, last, 2 * half),
        (1, v_d_x, 0, half, 0),
        (2, v_d_x, half, half, half),
    )

    def compute_partials(step):
        for way in (0, 1):
            index = ring.at(-step - 2 if way == 0 else step + 2)
            left = v_normed_t[pl.ds(pl.multiple_of((2 * index + way) * rows, 16), rows), :]
            partials[way, :, 2 * half :] = mm(left, v_d_s[...])
            partials[way, :, 0 : 2 * half] = mm(left, v_d_x[...])

    def slot(stream, way, step):
        return slots.at[step, way, :, pl.ds(stream[4], stream[3])]

    def hop(stream, way, step, source):
        return remote(
            source,
            slot(stream, way, step),
            ring_send.at[stream[0], way],
            ring_recv.at[stream[0], way, step],
            ring.neighbour(way),
        )

    def first_part(stream, way):
        return stage.at[way, :, pl.ds(stream[4], stream[3])]

    def arrived(stream, way, step):
        hop(stream, way, step, first_part(stream, way)).wait()
        partial = partials[way, :, stream[4] : stream[4] + stream[3]]
        return slot(stream, way, step)[...].astype(F32) + partial

    done_of = lambda stream: done.at[pl.ds(stream[4], stream[3])]
    of_x = lambda c, first: g_x.at[c, pl.ds(first, half)]
    shares = (
        (shard_o if direct else moved, lambda c: g_o.at[c]),
        (shard_z, lambda c: g_z.at[c]),
        (done_of(streams[1]), lambda c: of_x(c, 0)),
        (done_of(streams[2]), lambda c: of_x(c, half)),
        (done_of(streams[0]), lambda c: g_s.at[c]),
    )

    def share(i, kind):
        source, whole = shares[i]
        at = me
        if kind == 2:
            source, at = whole(around.row_at), around.row_at
        device = around.row if kind == 0 else around.core
        return remote(source, whole(at), ctx_send.at[i, kind], ctx_recv.at[i, kind], device)

    def keep(i):
        return pltpu.make_async_copy(shares[i][0], shares[i][1](me), own_sem.at[i])

    def start_share(i):
        share(i, 0).start()
        share(i, 1).start()
        keep(i).start()

    def pass_share(i):
        share(i, 0).wait_recv()
        share(i, 2).start()

    def close_share(i):
        share(i, 0).wait_send()
        share(i, 1).wait()
        share(i, 2).wait()
        keep(i).wait()

    def move_piece(wait):
        if direct:
            return
        keep_piece = pltpu.make_async_copy(shard_o, moved, piece_send)
        send_piece = remote(shard_o, moved, piece_send, piece_recv, piece_peer)

        @pl.when(moves)
        def _():
            send_piece.wait() if wait else send_piece.start()

        @pl.when(jnp.logical_not(moves))
        def _():
            keep_piece.wait() if wait else keep_piece.start()

    def normed_part(i, carry):
        to_row = row + (1 - i % 2) * (1 - 2 * row)
        to_core = core + (1 - i // 2) * (1 - 2 * core)
        at = 2 * to_row + to_core
        tokens = pl.ds(pl.multiple_of(at * own, own), own)
        parts[at] = (
            mm(v_d_z[tokens, :], v_z[...], ((1,), (1,)))
            + mm(v_d_x[tokens, :], v_x[...], ((1,), (1,)))
            + mm(v_d_s[tokens, :], v_s[...], ((1,), (1,)))
        ).astype(BF16)
        return carry

    store_grad = pltpu.make_async_copy(v_cotangent, hidden_grad, store_sem.at[0])
    store_small = pltpu.make_async_copy(small_ctx, small_out, store_sem.at[1])
    store_norm = pltpu.make_async_copy(norm_ctx, norm_out, store_sem.at[2])

    def finish_tokens():
        resid = v_hidden[...].astype(F32)
        scale = lax.rsqrt(jnp.mean(resid * resid, axis=1, keepdims=True) + EPS)
        d_normed = sum_normed.total()
        f = v_gain[...] * d_normed
        slope = scale**3 * jnp.mean(resid * f, axis=1, keepdims=True)
        grad = v_cotangent[...].astype(F32) + scale * f - resid * slope
        v_cotangent[...] = grad.astype(BF16)
        store_grad.start()
        by_model = jnp.sum(d_normed * resid * scale, axis=0, keepdims=True)
        size = norm_all.shape[2]
        for j in range(norm_all.shape[1]):
            norm_all[shard, j : j + 1, :] = by_model[:, j * size : (j + 1) * size]
        sum_norm.start()

    move_piece(False)
    for copy in loads[:ring_loads]:
        copy.wait()
    compute_partials(-1)
    for way in (0, 1):
        stage[way] = partials[way].astype(BF16)
        for stream in streams:
            hop(stream, way, 0, first_part(stream, way)).start()
    compute_partials(0)
    for copy in loads[ring_loads:]:
        copy.wait()
    sum_small.start()
    move_piece(True)
    start_share(0)
    start_share(1)

    def body(step, carry):
        for stream in streams:
            for way in (0, 1):
                total = arrived(stream, way, step)
                place = slot(stream, way, step)
                place[...] = total.astype(BF16)
                hop(stream, way, step + 1, place).start()
        compute_partials(step + 1)

        @pl.when(step < 2)
        def _():
            lax.fori_loop(2 * step, 2 * step + 2, normed_part, 0)

        @pl.when(step == 0)
        def _():
            sum_normed.start()

        @pl.when(step == 1)
        def _():
            sum_normed.pass_row()

        @pl.when(step == n - 3)
        def _():
            finish_tokens()

        return carry

    lax.fori_loop(0, n - 2, body, 0)
    sum_small.add()
    pass_share(0)
    pass_share(1)
    for number, shared in ((0, 4), (1, 2), (2, 3)):
        place = done_of(streams[number])
        for way in (0, 1):
            total = arrived(streams[number], way, n - 2)
            place[:, way * rows : (way + 1) * rows] = total.T.astype(BF16)
        start_share(shared)
    sum_norm.add()
    sum_small.finish()
    store_small.start()
    for i in (4, 2, 3):
        pass_share(i)
    sum_norm.finish()
    store_norm.start()
    for i in range(5):
        close_share(i)
    store_grad.wait()
    store_small.wait()
    store_norm.wait()


def reduce_all(
    n, n_ctx, direct, normed_t, d_z, d_x, d_s, w_z, w_x, w_s, shard_o, shard_z, small, hidden, cotangent, gain
):
    model, tokens = normed_t.shape[1], d_x.shape[0]
    width, shared_width = d_x.shape[1], d_s.shape[1]
    rows, piece, own = model // n, width // n, hidden.shape[0]
    columns = width + shared_width
    any_space = pl.BlockSpec(memory_space=pl.ANY)
    dma = pltpu.SemaphoreType.DMA
    low = lambda *shape: jax.ShapeDtypeStruct(shape, BF16)
    v_low = lambda *shape: pltpu.VMEM(shape, BF16)
    v_full = lambda *shape: pltpu.VMEM(shape, F32)
    norm_shape = (8, model // 8)
    return pl.pallas_call(
        functools.partial(reduce_kernel, n, n_ctx, direct),
        in_specs=[any_space] * 13,
        out_specs=[any_space] * 7,
        out_shape=[
            low(n_ctx, 2, width, rows // 2),
            low(n_ctx, width, rows),
            low(n_ctx, shared_width, rows),
            low(n_ctx, piece, model),
            low(own, model),
            jax.ShapeDtypeStruct((n_ctx,) + small.shape, F32),
            jax.ShapeDtypeStruct((n_ctx,) + norm_shape, F32),
        ],
        scratch_shapes=[
            v_low(model, tokens),
            v_low(tokens, width),
            v_low(tokens, width),
            v_low(tokens, shared_width),
            v_low(*w_z.shape),
            v_low(*w_x.shape),
            v_low(*w_s.shape),
            v_low(n_ctx, own, model),
            v_full(2, rows // 2, columns),
            v_low(n - 1, 2, rows // 2, columns),
            v_low(2, rows // 2, columns),
            v_low(columns, rows),
            v_low(piece, model),
            v_low(2, own, model),
            v_low(own, model),
            v_low(own, model),
            v_low(own, model),
            v_full(1, model),
            v_full(n, *small.shape),
            v_full(n_ctx, *small.shape),
            v_full(n, *norm_shape),
            v_full(n_ctx, *norm_shape),
            dma((10 + n_ctx,)),
            dma((3,)),
            dma((3, 2)),
            dma((3, 2, n - 1)),
            dma((5, 3)),
            dma((5, 3)),
            dma((5,)),
            dma,
            dma,
            dma((3,)),
            dma((3,)),
            dma((2, n - 1)),
            dma((2, n - 1)),
            dma((2, 3)),
            dma((2, 3)),
        ],
        compiler_params=pltpu.CompilerParams(
            collective_id=1, has_side_effects=True, vmem_limit_bytes=58 * 1024 * 1024
        ),
        name="reduce_all",
    )(
        normed_t, d_z, d_x, d_s, w_z, w_x, w_s, shard_o, shard_z, small, hidden, cotangent, gain
    )


def assemble_kernel(part, z_ref, x_ref, s_ref, o_ref, out_ref, rows_ref):
    place = pl.program_id(0)
    n_ctx, size, half = x_ref.shape[0], x_ref.shape[1], z_ref.shape[3]

    def interleave(write):
        for a in range(size // part):
            for c in range(n_ctx):
                write(
                    slice((a * n_ctx + c) * part, (a * n_ctx + c + 1) * part),
                    c,
                    slice(a * part, (a + 1) * part),
                )

    def write_z(target, c, source):
        for way in (0, 1):
            out_ref[target, way * half : (way + 1) * half] = z_ref[c, way, source, :].astype(F32)

    def write_x(target, c, source):
        out_ref[target, :] = x_ref[c, source, :].astype(F32)

    @pl.when(place < n_ctx)
    def _():
        interleave(write_z)

    @pl.when(jnp.logical_and(place >= n_ctx, place < 2 * n_ctx))
    def _():
        interleave(write_x)

    @pl.when(place == 2 * n_ctx)
    def _():
        for c in range(s_ref.shape[0]):
            out_ref[c * LANES : (c + 1) * LANES, :] = s_ref[c].astype(F32)

    @pl.when(place < 2 * n_ctx)
    def _():
        rows_ref[...] = o_ref[...].astype(F32)


def assemble(part, g_z, g_x, g_s, g_o, columns):
    n_ctx, width, rows = g_x.shape
    block = (n_ctx, width // n_ctx, rows)
    g_o = g_o.reshape(-1, g_o.shape[2])
    tile = max(g_o.shape[0] // (2 * n_ctx), 16)
    at_tile = lambda i: (jnp.minimum(i, g_o.shape[0] // tile - 1), 0)
    return pl.pallas_call(
        functools.partial(assemble_kernel, part),
        grid=(2 * n_ctx + 1,),
        in_specs=[
            pl.BlockSpec(
                (n_ctx, 2, width // n_ctx, rows // 2),
                lambda i: (0, 0, jnp.minimum(i, n_ctx - 1), 0),
            ),
            pl.BlockSpec(block, lambda i: (0, jnp.clip(i - n_ctx, 0, n_ctx - 1), 0)),
            pl.BlockSpec(g_s.shape, lambda i: (0, 0, 0)),
            pl.BlockSpec((tile, g_o.shape[1]), at_tile),
        ],
        out_specs=[
            pl.BlockSpec((width, rows), lambda i: (i, 0)),
            pl.BlockSpec((tile, g_o.shape[1]), at_tile),
        ],
        out_shape=[
            jax.ShapeDtypeStruct((columns, rows), F32),
            jax.ShapeDtypeStruct(g_o.shape, F32),
        ],
        compiler_params=pltpu.CompilerParams(vmem_limit_bytes=58 * 1024 * 1024),
        name="assemble",
    )(g_z, g_x, g_s, g_o)


def on_device(
    hidden,
    cotangent,
    seq_lens,
    norm_gain,
    in_weight,
    conv_weight,
    conv_bias,
    dt_bias,
    a_log,
    d_skip,
    gate_gain,
    out_weight,
):
    n_ctx, n_fsdp = lax.axis_size("ctx"), lax.axis_size("fsdp")
    me, shard = lax.axis_index("ctx"), lax.axis_index("fsdp")
    taps = conv_weight.shape[0]
    heads_all = dt_bias.shape[0] * n_fsdp
    inner = out_weight.shape[0] * n_fsdp
    heads, width = heads_all // n_ctx, inner // n_ctx
    model = hidden.shape[2]
    both = 2 * STATE
    held = dt_bias.shape[0]
    direct = held % n_ctx == 0
    unit = held // n_ctx if direct else 1
    part = unit * HEAD
    assert both + heads_all <= n_ctx * LANES and heads_all == HEAD

    per_head = jnp.concatenate([dt_bias, a_log, d_skip])
    lines = [norm_gain[None], conv_weight, conv_bias[None], gate_gain[None], per_head[None]]
    longest = -(-max(a.shape[1] for a in lines) // LANES) * LANES
    small = jnp.concatenate([jnp.pad(a, ((0, 0), (0, longest - a.shape[1]))) for a in lines])
    small = jnp.pad(small, ((0, SMALL_ROWS - small.shape[0]), (0, 0)))
    sizes = (norm_gain.shape[0], conv_bias.shape[0], gate_gain.shape[0], held)
    upstream, w_x, w_s, w_z, par, gain_norm, proj_x, proj_s, normed, normed_t = gather_all(
        n_fsdp, n_ctx, unit, taps, sizes, width, hidden[0], cotangent[0], in_weight.T, small
    )
    *kept_parts, gain_grads, gate_t, mixed_parts, d_z, d_ssd = scan_forward(
        n_fsdp, direct, unit, n_ctx, seq_lens, proj_x, proj_s, normed, out_weight, w_z, upstream, par
    )
    d_x, small_grads, d_s, shard_o, shard_z, layer_out = scan_backward(
        n_fsdp, unit, n_ctx, proj_x, proj_s, kept_parts, d_ssd, gate_t, normed_t, upstream, d_z, mixed_parts, hidden[0], gain_grads, par
    )
    g_z, g_x, g_s, g_o, hidden_grad, sums, norm_sums = reduce_all(
        n_fsdp, n_ctx, direct, normed_t, d_z, d_x, d_s, w_z, w_x, w_s, shard_o, shard_z, small_grads, hidden[0], cotangent[0], gain_norm
    )
    grad_in_weight, grad_out_weight = assemble(
        part, g_z, g_x, g_s, g_o, 2 * inner + both + heads_all
    )

    def shard_of(lines):
        size = lines.shape[1] // n_fsdp
        return lax.dynamic_slice_in_dim(lines, shard * size, size, axis=1)

    def in_order(sums_of, size):
        lines = sums_of.shape[1]
        by_part = sums_of.reshape(n_ctx, lines, -1, size)
        return jnp.transpose(by_part, (1, 2, 0, 3)).reshape(lines, -1)

    conv_sums = shard_of(
        jnp.concatenate(
            [
                in_order(sums[:, : taps + 1, :width], part),
                jnp.sum(sums[:, : taps + 1, width:], axis=0),
            ],
            axis=1,
        )
    )
    gate_sums = shard_of(in_order(sums[:, taps + 1 : taps + 2, :width], part))
    head_sums_all = sums[:, taps + 2, : 3 * LANES].reshape(n_ctx, 3, LANES)[:, :, :heads]
    head_grads = shard_of(in_order(head_sums_all, unit))
    norm_sums = jnp.sum(norm_sums, axis=0).reshape(1, -1)
    return (
        layer_out[None],
        hidden_grad[None],
        shard_of(norm_sums)[0],
        grad_in_weight.T,
        conv_sums[:taps],
        conv_sums[taps],
        head_grads[0],
        head_grads[1],
        head_grads[2],
        gate_sums[0],
        grad_out_weight,
    )


def solution(mesh):
    tokens, rows, flat = P("fsdp", "ctx", None), P("fsdp", None), P("fsdp")
    taps = P(None, "fsdp")
    return jax.shard_map(
        on_device,
        mesh=mesh,
        in_specs=(tokens, tokens, flat, flat, rows, taps, flat, flat, flat, flat, flat, rows),
        out_specs=(tokens, tokens, flat, rows, taps, flat, flat, flat, flat, flat, rows),
        check_vma=False,
    )
```
